32 devices in a mesh: row: 4 (over y, core), kv: 8 (over z, x).
Axes of the slice: x: 2, y: 2, z: 4, core: 2. Of those that a mesh axis runs over, the one named last changes fastest.
Arguments:
- tokens: bfloat16 [4, 4096, 2048], P('row', 'kv'), may hold values from -6 to 6
- lengths: int32 [4, 8], P('row'), may hold values from 0 to 4096, as said below
- cotangent: bfloat16 [4, 4096, 2048], P('row', 'kv'), may hold values from -6 to 6
- w_query: bfloat16 [2048, 2048], P(('row', 'kv')), may hold values from -0.1875 to 0.1875
- w_key: bfloat16 [2048, 2048], P(('row', 'kv')), may hold values from -0.1875 to 0.1875
- w_value: bfloat16 [2048, 2048], P(('row', 'kv')), may hold values from -0.125 to 0.125
- w_out: bfloat16 [2048, 2048], P(('row', 'kv')), may hold values from -0.25 to 0.25
- w_gate: bfloat16 [2048, 8192], P(None, ('row', 'kv')), may hold values from -0.125 to 0.125
- w_up: bfloat16 [2048, 8192], P(None, ('row', 'kv')), may hold values from -0.125 to 0.125
- w_down: bfloat16 [8192, 2048], P(('row', 'kv')), may hold values from -0.0625 to 0.0625
- gain_attn: bfloat16 [2048], P(('row', 'kv')), may hold values from 0.099609375 to 1.8984375
- gain_mlp: bfloat16 [2048], P(('row', 'kv')), may hold values from 0.099609375 to 1.8984375
Outputs:
- mixed: bfloat16 [4, 4096, 2048], P('row', 'kv')
- grad_tokens: float32 [4, 4096, 2048], P('row', 'kv')
- grad_query: float32 [2048, 2048], P(('row', 'kv'))
- grad_key: float32 [2048, 2048], P(('row', 'kv'))
- grad_value: float32 [2048, 2048], P(('row', 'kv'))
- grad_out: float32 [2048, 2048], P(('row', 'kv'))
- grad_gate: float32 [2048, 8192], P(None, ('row', 'kv'))
- grad_up: float32 [2048, 8192], P(None, ('row', 'kv'))
- grad_down: float32 [8192, 2048], P(('row', 'kv'))
- grad_gain_attn: float32 [2048], P(('row', 'kv'))
- grad_gain_mlp: float32 [2048], P(('row', 'kv'))
The draws below stay inside these ranges and needn't reach their ends.
Inputs may be any that keep to these rules, and one draw needn't show every extreme that they name: Each row of 4096 positions holds its documents in the order of lengths, then unused positions; the lengths of a row sum to at most 4096; a length of 0 is an empty slot.
All inputs are finite; a program needn't handle non-finite values.
Results may differ from the reference program's by a relative error of at most 0.02.
Values may be sent and summed in bfloat16 or wider, within the bound.
A program may use at most 320 MiB of HBM per device.

```python
import math
import jax
import jax.numpy as jnp
from jax import lax

D = 2048
H = 16
HD = 128
FF = 8192
LEN = 4096
NDOC = 8
ROWS = 4
BLOCK = 512


def draw_lengths(key, part):
    key = jax.random.fold_in(key, 11)
    keys = jax.random.split(key, 4)
    piece = max(BLOCK // NDOC, 1)
    first = jax.random.randint(keys[0], (ROWS, 1), 0, BLOCK)
    trailing = jax.random.randint(keys[1], (ROWS, NDOC - 2), 0, piece)
    padding = jax.random.randint(keys[2], (ROWS, 1), 0, piece)
    middle = LEN - first - jnp.sum(trailing, axis=1, keepdims=True) - padding
    drawn = jnp.concatenate((first, middle, trailing), axis=1)
    whole_row = jax.random.randint(keys[3], (), 0, ROWS)
    single = jnp.zeros((ROWS, NDOC), jnp.int32).at[:, 1].set(LEN)
    picked = (jnp.arange(ROWS) == whole_row)[:, None]
    return jnp.where(picked, single, drawn).astype(jnp.int32)


def level_of(stream_key, dims, shards, smallest, top_value):
    level, own = 1.0, jax.random.fold_in(stream_key, 6)
    for position, shards_of in shards:
        draws = jnp.exp(jax.random.uniform(jax.random.fold_in(own, position), (shards_of,), jnp.float32, smallest / len(shards), top_value / len(shards)))
        level = level * jnp.repeat(draws, dims[position] // shards_of).reshape([-1 if axis == position else 1 for axis in range(len(dims))])
    return level


def normal_values(own_key, dims, scale, most, shards=(), kind=jnp.bfloat16):
    array = jax.random.normal(own_key, dims, jnp.float32) * scale
    if len(shards) > 0:
        array = level_of(own_key, dims, shards, -0.22, 0.18) * array
    return jnp.clip(array, min=-most, max=most).astype(kind)


def setup_inputs(seed: int = 0) -> dict:
    key_list = jax.random.split(jax.random.key(seed), 13)
    tokens = normal_values(key_list[0], (ROWS, LEN, D), 1.0, 6.0, ((0, 4), (1, 8)))
    lengths = draw_lengths(jax.random.fold_in(key_list[12], 71), 0)
    cotangent = normal_values(key_list[2], (ROWS, LEN, D), 1.0, 6.0, ((0, 4), (1, 8)))
    w_query = normal_values(key_list[3], (D, D), (D // 2) ** -0.5, 0.1875, ((0, 32),))
    w_key = normal_values(key_list[4], (D, D), (D // 2) ** -0.5, 0.1875, ((0, 32),))
    w_value = normal_values(key_list[5], (D, D), D ** -0.5, 0.125, ((0, 32),))
    w_out = normal_values(key_list[6], (D, D), (D // 4) ** -0.5, 0.25, ((0, 32),))
    w_gate = normal_values(key_list[7], (D, FF), D ** -0.5, 0.125, ((1, 32),))
    w_up = normal_values(key_list[8], (D, FF), D ** -0.5, 0.125, ((1, 32),))
    w_down = normal_values(key_list[9], (FF, D), FF ** -0.5, 0.0625, ((0, 32),))
    gain_attn = jnp.clip(1.0 + 0.18 * jax.random.normal(key_list[10], (D,), jnp.float32), 0.099609375, 1.8984375).astype(jnp.bfloat16)
    gain_mlp = jnp.clip(1.0 + 0.18 * jax.random.normal(key_list[11], (D,), jnp.float32), 0.099609375, 1.8984375).astype(jnp.bfloat16)
    return {"tokens": tokens, "lengths": lengths, "cotangent": cotangent, "w_query": w_query, "w_key": w_key, "w_value": w_value, "w_out": w_out, "w_gate": w_gate, "w_up": w_up, "w_down": w_down, "gain_attn": gain_attn, "gain_mlp": gain_mlp}


@jax.custom_vjp
def low(v):
    return lax.optimization_barrier(v.astype(jnp.bfloat16)).astype(jnp.float32)

@jax.custom_vjp
def low_back(v):
    return v

def low_keep(v):
    return (low(v), None)

def low_pass(kept, grad):
    return (grad,)

def back_keep(v):
    return (v, None)

def back_low(kept, grad):
    return (low(grad),)
low.defvjp(low_keep, low_pass)
low_back.defvjp(back_keep, back_low)
EPSILON = 1e-05

def norm_scale(value, gain):
    return value * lax.rsqrt(lax.optimization_barrier(jnp.mean(value * value, axis=-1, keepdims=True)) + EPSILON) * gain

def matmul(left, right):
    return jnp.dot(left, right, precision=lax.Precision.HIGHEST)

def segment_table(row_lengths):
    ends = jnp.cumsum(row_lengths).astype(jnp.int32)
    places = jnp.arange(LEN, dtype=jnp.int32)
    segment = lax.optimization_barrier(jnp.sum((ends[None, :] <= places[:, None]).astype(jnp.int32), axis=-1))
    valid = places < ends[-1]
    return (segment, valid)

def row_layer(params, x_row, row_lengths):
    w_query, w_key, w_value, w_out, w_gate, w_up, w_down, gain_attn, gain_mlp = params
    segment, valid = segment_table(row_lengths)
    normed_attn = low(norm_scale(x_row, gain_attn))
    query = low(low_back(matmul(normed_attn, w_query))).reshape(LEN, H, HD)
    key = low(low_back(matmul(normed_attn, w_key))).reshape(LEN, H, HD)
    value = low(low_back(matmul(normed_attn, w_value))).reshape(LEN, H, HD)
    places = jnp.arange(LEN, dtype=jnp.int32)
    scale = 1.0 / math.sqrt(HD)
    offset = -math.log(LEN)
    query_block = min(512, LEN)

    def attend(start):
        query_rows = lax.dynamic_slice_in_dim(query, start, query_block, 0)
        query_places = lax.dynamic_slice_in_dim(places, start, query_block, 0)
        query_segment = lax.dynamic_slice_in_dim(segment, start, query_block, 0)
        allowed = (places[None, :] <= query_places[:, None]) & (segment[None, :] == query_segment[:, None]) & valid[None, :]
        raw = jnp.einsum('qhd,khd->hqk', query_rows, key, precision=lax.Precision.HIGHEST)
        scores = low_back(raw * scale + offset)
        weight = low(jax.nn.sigmoid(scores) * allowed.astype(jnp.float32)[None])
        return jnp.einsum('hqk,khd->qhd', weight, value, precision=lax.Precision.HIGHEST).reshape(query_block, D)
    starts = jnp.arange(LEN // query_block, dtype=jnp.int32) * query_block
    attended = lax.map(jax.checkpoint(attend), starts).reshape(LEN, D)
    attended = low(low_back(attended))
    resid = x_row + low_back(matmul(attended, w_out))
    normed_mlp = low(norm_scale(resid, gain_mlp))
    gate = low_back(matmul(normed_mlp, w_gate))
    up_part = low_back(matmul(normed_mlp, w_up))
    hidden = low(jax.nn.silu(gate) * up_part)
    return resid + low_back(matmul(hidden, w_down))

def reference(tokens, lengths, cotangent, w_query, w_key, w_value, w_out, w_gate, w_up, w_down, gain_attn, gain_mlp):
    params = (w_query.astype(jnp.float32), w_key.astype(jnp.float32), w_value.astype(jnp.float32), w_out.astype(jnp.float32), w_gate.astype(jnp.float32), w_up.astype(jnp.float32), w_down.astype(jnp.float32), gain_attn.astype(jnp.float32), gain_mlp.astype(jnp.float32))
    inputs = tokens.astype(jnp.float32)

    def forward(layer_input, weights):

        def single(pair):
            return row_layer(weights, pair[0], pair[1])
        return lax.map(jax.checkpoint(single), (layer_input, lengths))
    result, pullback = jax.vjp(forward, inputs, params)
    grad_tokens, grads = pullback(cotangent.astype(jnp.float32))
    return (result.astype(jnp.bfloat16), grad_tokens, grads[0], grads[1], grads[2], grads[3], grads[4], grads[5], grads[6], grads[7], grads[8])
```

```python
import functools
import math

import jax
import jax.numpy as jnp
from jax import lax
from jax.experimental import pallas as pl
from jax.experimental.pallas import tpu as pltpu
from jax.sharding import Mesh, PartitionSpec as P

H = 16
HD = 128
LEN = 4096


EPSILON = 1e-05


def contract_rows(left, right):
    return lax.dot_general(
        left, right, (((0,), (0,)), ((), ())), preferred_element_type=jnp.float32
    )


def contract_cols(left, right):
    return lax.dot_general(
        left, right, (((1,), (1,)), ((), ())), preferred_element_type=jnp.float32
    )


def norm_forward(value, gain):
    inverse = lax.rsqrt(jnp.mean(value * value, axis=-1, keepdims=True) + EPSILON)
    return (value * inverse * gain.astype(jnp.float32), inverse)


def norm_backward(value, inverse, gain, upstream):
    scaled = upstream * gain.astype(jnp.float32)
    inner = jnp.mean(scaled * value, axis=-1, keepdims=True)
    back = inverse * scaled - value * (inverse * inverse * inverse) * inner
    gain_term = jnp.sum(upstream * value * inverse, axis=0)
    return (back, gain_term)


def segment_table(lengths):
    ends = jnp.cumsum(lengths, axis=-1)
    places = jnp.arange(LEN, dtype=jnp.int32)
    segment = jnp.sum((ends[:, None, :] <= places[None, :, None]).astype(jnp.int32), axis=-1)
    valid = places[None, :] < ends[:, -1:]
    return (segment, valid)


def score_block(
    query_rows, key_heads, query_segment, key_segment, key_valid, query_start, key_places
):
    count = query_rows.shape[0]
    query_heads = query_rows.reshape(count, H, HD)
    raw = jnp.einsum("qhd,khd->hqk", query_heads, key_heads, preferred_element_type=jnp.float32)
    scores = raw * (1.0 / math.sqrt(HD)) - math.log(LEN)
    places = query_start + jnp.arange(count, dtype=jnp.int32)
    allowed = (
        (key_places[None, :] <= places[:, None])
        & (key_segment[None, :] == query_segment[:, None])
        & key_valid[None, :]
    )
    return (jax.nn.sigmoid(scores), allowed.astype(jnp.float32)[None])


def gate_backward(d_hidden, gate, up_part, sigmoid_gate):
    d_gate = (d_hidden * up_part * sigmoid_gate * (1.0 + gate * (1.0 - sigmoid_gate))).astype(
        jnp.bfloat16
    )
    d_up = (d_hidden * gate * sigmoid_gate).astype(jnp.bfloat16)
    return (d_gate, d_up)


TILE = 512
LOW = jnp.bfloat16
VMEM_LIMIT = 60 * 1024 * 1024


def doc_start(ends, place):
    start = jnp.zeros_like(place)
    for k in range(8):
        start = jnp.where(ends[k] <= place, ends[k], start)
    return jnp.where(place < ends[7], start, LEN)


def doc_end(ends, place):
    end = ends[7]
    for k in range(6, -1, -1):
        end = jnp.where(ends[k] > place, ends[k], end)
    return end


def sigmoid_of(raw):
    return pl.reciprocal(1.0 + jnp.exp2(math.log2(LEN) - raw * (math.log2(math.e) / math.sqrt(HD))), approx=True)


def dot_nt(left, right):
    return lax.dot_general(left, right, (((1,), (1,)), ((), ())), preferred_element_type=jnp.float32)


def attend_kernel(ends, qkv, out, total):
    head, i = pl.program_id(0), pl.program_id(1)
    column = pl.multiple_of(head * HD, HD)
    width = qkv.shape[1] // 3
    first = i * TILE
    query = qkv[pl.ds(pl.multiple_of(first, TILE), TILE), pl.ds(column, HD)]
    total[...] = jnp.zeros_like(total)
    begin = jnp.minimum(doc_start(ends, first), first) // TILE
    latest = doc_start(ends, first + TILE - 1)

    def step(j, carry):
        here = pl.ds(pl.multiple_of(j * TILE, TILE), TILE)
        key = qkv[here, pl.ds(pl.multiple_of(column + width, HD), HD)]
        value = qkv[here, pl.ds(pl.multiple_of(column + 2 * width, HD), HD)]
        plain = (j < i) & (j * TILE >= latest)

        @pl.when(plain)
        def _():
            weight = sigmoid_of(dot_nt(query, key)).astype(LOW)
            total[...] += jnp.dot(weight, value, preferred_element_type=jnp.float32)

        @pl.when(jnp.logical_not(plain))
        def _():
            q_place = first + lax.broadcasted_iota(jnp.int32, (TILE, 1), 0)
            k_place = j * TILE + lax.broadcasted_iota(jnp.int32, (1, TILE), 1)
            allowed = (k_place <= q_place) & (k_place >= doc_start(ends, q_place))
            weight = jnp.where(allowed, sigmoid_of(dot_nt(query, key)), 0.0).astype(LOW)
            total[...] += jnp.dot(weight, value, preferred_element_type=jnp.float32)

        return carry

    lax.fori_loop(begin, i + 1, step, 0)
    out[pl.ds(pl.multiple_of(first, TILE), TILE), pl.ds(column, HD)] = total[...].astype(LOW)


def attend_back_kernel(ends, qkv, grads, out, query_total, key_total, value_total):
    head, j = pl.program_id(0), pl.program_id(1)
    column = pl.multiple_of(head * HD, HD)
    width = qkv.shape[1] // 3
    first = j * TILE
    here = pl.ds(pl.multiple_of(first, TILE), TILE)
    key_column = pl.multiple_of(column + width, HD)
    value_column = pl.multiple_of(column + 2 * width, HD)
    key = qkv[here, pl.ds(key_column, HD)]
    value = qkv[here, pl.ds(value_column, HD)]
    key_turned = key.T
    key_total[...] = jnp.zeros_like(key_total)
    value_total[...] = jnp.zeros_like(value_total)

    @pl.when(j == 0)
    def _():
        query_total[...] = jnp.zeros_like(query_total)

    end = pl.cdiv(doc_end(ends, first + TILE - 1), TILE)

    def step(i, carry):
        there = pl.ds(pl.multiple_of(i * TILE, TILE), TILE)
        query = qkv[there, pl.ds(column, HD)]
        grad = grads[there, pl.ds(column, HD)]
        plain = (j < i) & (first >= doc_start(ends, i * TILE + TILE - 1))

        def finish(sig):
            value_total[...] += jnp.dot(sig.astype(LOW), grad, preferred_element_type=jnp.float32)
            d_score = (dot_nt(value, grad) * (sig * (1.0 - sig))).astype(LOW)
            key_total[...] += jnp.dot(d_score, query, preferred_element_type=jnp.float32)
            query_total[:, there] += jnp.dot(key_turned, d_score, preferred_element_type=jnp.float32)

        @pl.when(plain)
        def _():
            finish(sigmoid_of(dot_nt(key, query)))

        @pl.when(jnp.logical_not(plain))
        def _():
            q_place = i * TILE + lax.broadcasted_iota(jnp.int32, (1, TILE), 1)
            k_place = first + lax.broadcasted_iota(jnp.int32, (TILE, 1), 0)
            allowed = (k_place <= q_place) & (k_place >= doc_start(ends, q_place))
            finish(jnp.where(allowed, sigmoid_of(dot_nt(key, query)), 0.0))

        return carry

    lax.fori_loop(j, end, step, 0)
    scale = 1.0 / math.sqrt(HD)
    out[here, pl.ds(key_column, HD)] = (key_total[...] * scale).astype(LOW)
    out[here, pl.ds(value_column, HD)] = value_total[...].astype(LOW)

    @pl.when(j == pl.num_programs(1) - 1)
    def _():
        for t in range(LEN // TILE):
            out[t * TILE : (t + 1) * TILE, pl.ds(column, HD)] = (
                (query_total[:, t * TILE : (t + 1) * TILE] * scale).T.astype(LOW)
            )


def attend(ends, qkv):
    places, width = qkv.shape
    heads = width // (3 * HD)
    return pl.pallas_call(
        attend_kernel,
        out_shape=jax.ShapeDtypeStruct((places, width // 3), LOW),
        grid_spec=pltpu.PrefetchScalarGridSpec(
            num_scalar_prefetch=1,
            grid=(heads, places // TILE),
            in_specs=[pl.BlockSpec((places, width), lambda h, i, ends: (0, 0))],
            out_specs=pl.BlockSpec((places, width // 3), lambda h, i, ends: (0, 0)),
            scratch_shapes=[pltpu.VMEM((TILE, HD), jnp.float32)],
        ),
        compiler_params=pltpu.CompilerParams(vmem_limit_bytes=VMEM_LIMIT),
        cost_estimate=pl.CostEstimate(
            flops=4 * heads * places * places * HD // 2, bytes_accessed=8 * places * width // 3, transcendentals=heads * places * places // 2
        ),
    )(ends, qkv)


def attend_back(ends, qkv, grads):
    places, width = qkv.shape
    heads = width // (3 * HD)
    whole = lambda columns: pl.BlockSpec((places, columns), lambda h, j, ends: (0, 0))
    return pl.pallas_call(
        attend_back_kernel,
        out_shape=jax.ShapeDtypeStruct((places, width), LOW),
        grid_spec=pltpu.PrefetchScalarGridSpec(
            num_scalar_prefetch=1,
            grid=(heads, places // TILE),
            in_specs=[whole(width), whole(width // 3)],
            out_specs=whole(width),
            scratch_shapes=[
                pltpu.VMEM((HD, places), jnp.float32),
                pltpu.VMEM((TILE, HD), jnp.float32),
                pltpu.VMEM((TILE, HD), jnp.float32),
            ],
        ),
        compiler_params=pltpu.CompilerParams(vmem_limit_bytes=VMEM_LIMIT),
        cost_estimate=pl.CostEstimate(
            flops=10 * heads * places * places * HD // 2, bytes_accessed=14 * places * width // 3, transcendentals=heads * places * places // 2
        ),
    )(ends, qkv, grads)


LAYER = ("y", "c", "x")
ALL = ("y", "c", "z", "x")


def gather_layer(part):
    return lax.all_gather(part, LAYER, axis=0, tiled=True)


def scatter_layer(whole):
    return lax.psum_scatter(whole.astype(LOW), LAYER, scatter_dimension=0, tiled=True).astype(jnp.float32)


def swap_rows(part):
    return lax.all_to_all(part.reshape(4, -1, part.shape[1]), "z", 0, 0).reshape(part.shape)


def dot_wide(left, right):
    return jnp.dot(left, right, preferred_element_type=jnp.float32)


def body_layers(
    tokens, lengths, cotangent, w_query, w_key, w_value, w_out, w_gate, w_up, w_down, gain_attn, gain_mlp
):
    rows_here, block, width = tokens.shape
    members = lax.axis_size(LAYER)
    layers = lax.axis_size("z")
    shard = w_query.shape[0]
    owned = width // members
    gains = lax.all_gather(jnp.stack((gain_attn, gain_mlp), axis=1), ALL, axis=0, tiled=True)
    full_gain_attn, full_gain_mlp = gains[:, 0], gains[:, 1]
    ends = jnp.cumsum(lax.all_gather(lengths, ("y", "c"), axis=0, tiled=True), axis=-1)
    ends = lax.dynamic_slice_in_dim(ends, lax.axis_index("z"), 1, 0)[0]

    flat = tokens.reshape(block, width).astype(jnp.float32)
    normed_attn, inverse_attn = norm_forward(flat, full_gain_attn)
    layer_normed = gather_layer(normed_attn.astype(LOW))
    qkv_shards = jnp.stack((w_query, w_key, w_value), axis=1).reshape(shard, 3, members, owned)
    qkv_shards = qkv_shards.transpose(2, 0, 1, 3).reshape(members, shard, 3 * owned)
    qkv_shards = lax.all_to_all(qkv_shards, LAYER, 0, 0)
    w_qkv = lax.all_gather(qkv_shards, "z", axis=0)
    w_qkv = w_qkv.reshape(layers, 4, 2 * shard, 3 * owned).transpose(1, 0, 2, 3).reshape(width, 3 * owned)
    out_rows = lax.all_gather(w_out, ("z", "x"), axis=0, tiled=True)
    w_out_own = lax.dynamic_slice_in_dim(out_rows, lax.axis_index("x") * owned, owned, 0)

    qkv = swap_rows(dot_wide(layer_normed, w_qkv).astype(LOW))
    attended = swap_rows(attend(ends, qkv))
    resid = flat + scatter_layer(dot_wide(attended, w_out_own))

    normed_mlp, inverse_mlp = norm_forward(resid, full_gain_mlp)
    own_gate = lax.all_gather(w_gate, "z", axis=1, tiled=True)
    own_up = lax.all_gather(w_up, "z", axis=1, tiled=True)
    own_down = lax.all_gather(w_down, "z", axis=0, tiled=True)
    upstream_low = cotangent.reshape(block, width)
    upstream = upstream_low.astype(jnp.float32)
    layer_upstream = gather_layer(upstream_low)
    layer_mlp = gather_layer(normed_mlp.astype(LOW))
    gate = dot_wide(layer_mlp, own_gate)
    up_part = dot_wide(layer_mlp, own_up)
    sigmoid_gate = jax.nn.sigmoid(gate)
    hidden = (gate * sigmoid_gate * up_part).astype(LOW)
    result = resid + scatter_layer(dot_wide(hidden, own_down))
    d_hidden = contract_cols(layer_upstream, own_down)
    d_gate, d_up = gate_backward(d_hidden, gate, up_part, sigmoid_gate)
    d_normed_mlp = scatter_layer(contract_cols(d_gate, own_gate) + contract_cols(d_up, own_up))

    def scatter_layers(whole, axis):
        return lax.psum_scatter(whole.astype(LOW), "z", scatter_dimension=axis, tiled=True).astype(jnp.float32)

    grad_gate = scatter_layers(contract_rows(layer_mlp, d_gate), 1)
    grad_up = scatter_layers(contract_rows(layer_mlp, d_up), 1)
    grad_down = scatter_layers(contract_rows(hidden, layer_upstream), 0)
    mixed = result.astype(LOW).reshape(rows_here, block, width)

    back_mlp, gain_mlp_term = norm_backward(resid, inverse_mlp, full_gain_mlp, d_normed_mlp)
    d_resid = upstream + back_mlp
    layer_d_resid = gather_layer(d_resid.astype(LOW))
    d_attended = swap_rows(contract_cols(layer_d_resid, w_out_own).astype(LOW))
    d_qkv = swap_rows(attend_back(ends, qkv, d_attended))
    d_normed_attn = scatter_layer(contract_cols(d_qkv, w_qkv))
    out_term = contract_rows(attended, layer_d_resid)
    qkv_term = contract_rows(layer_normed, d_qkv)

    back_attn, gain_attn_term = norm_backward(flat, inverse_attn, full_gain_attn, d_normed_attn)
    grad_tokens = (d_resid + back_attn).reshape(rows_here, block, width)

    out_term = lax.dynamic_update_slice_in_dim(
        jnp.zeros((2 * owned, width), LOW), out_term.astype(LOW), lax.axis_index("x") * owned, 0
    )
    grad_out = lax.psum_scatter(out_term, ("z", "x"), scatter_dimension=0, tiled=True).astype(jnp.float32)
    qkv_term = qkv_term.reshape(4, layers, 2 * shard, 3 * owned).transpose(1, 0, 2, 3)
    qkv_term = qkv_term.reshape(layers * members * shard, 3 * owned)
    qkv_term = lax.psum_scatter(qkv_term.astype(LOW), "z", scatter_dimension=0, tiled=True)
    qkv_term = lax.all_to_all(qkv_term.reshape(members, shard, 3 * owned), LAYER, 0, 0)
    qkv_term = qkv_term.reshape(members, shard, 3, owned).transpose(2, 1, 0, 3).astype(jnp.float32)
    grad_query, grad_key, grad_value = qkv_term.reshape(3, shard, width)
    gain_terms = lax.psum_scatter(
        jnp.stack((gain_attn_term, gain_mlp_term), axis=1), ALL, scatter_dimension=0, tiled=True
    )
    return (
        mixed,
        grad_tokens,
        grad_query,
        grad_key,
        grad_value,
        grad_out,
        grad_gate,
        grad_up,
        grad_down,
        gain_terms[:, 0],
        gain_terms[:, 1],
    )


def body_any(
    tokens,
    lengths,
    cotangent,
    w_query,
    w_key,
    w_value,
    w_out,
    w_gate,
    w_up,
    w_down,
    gain_attn,
    gain_mlp,
):
    rows_here, block, width = tokens.shape
    count = rows_here * block
    scale = 1.0 / math.sqrt(HD)
    kv_place = lax.axis_index("kv")
    key_places = kv_place * block + jnp.arange(block, dtype=jnp.int32)
    attn_set = (
        lax.all_gather(w_query, ("row", "kv"), axis=0, tiled=True),
        lax.all_gather(w_key, ("row", "kv"), axis=0, tiled=True),
        lax.all_gather(w_value, ("row", "kv"), axis=0, tiled=True),
        lax.all_gather(w_out, ("row", "kv"), axis=0, tiled=True),
        lax.all_gather(gain_attn, ("row", "kv"), axis=0, tiled=True),
        lax.all_gather(gain_mlp, ("row", "kv"), axis=0, tiled=True),
    )
    full_query, full_key, full_value, full_out, full_gain_attn, full_gain_mlp = attn_set
    flat = tokens.reshape(count, width).astype(jnp.float32)
    normed_attn, inverse_attn = norm_forward(flat, full_gain_attn)
    normed_attn_low = normed_attn.astype(jnp.bfloat16)
    query_low = jnp.dot(normed_attn_low, full_query, preferred_element_type=jnp.float32).astype(
        jnp.bfloat16
    )
    key_low = jnp.dot(normed_attn_low, full_key, preferred_element_type=jnp.float32).astype(
        jnp.bfloat16
    )
    value_low = jnp.dot(normed_attn_low, full_value, preferred_element_type=jnp.float32).astype(
        jnp.bfloat16
    )
    key_heads = key_low.reshape(rows_here, block, H, HD)
    value_heads = value_low.reshape(rows_here, block, H, HD)
    segment, valid = segment_table(lengths)
    key_segment = lax.dynamic_slice_in_dim(segment, kv_place * block, block, 1)
    key_valid = lax.dynamic_slice_in_dim(valid, kv_place * block, block, 1)
    queries_all = lax.all_gather(
        query_low.reshape(rows_here, block, width), "kv", axis=1, tiled=True
    )
    which = 0
    query_rows = queries_all[which]
    query_segment = segment[which]
    sigmoid_part, allowed = score_block(
        query_rows,
        key_heads[which],
        query_segment,
        key_segment[which],
        key_valid[which],
        jnp.int32(0),
        key_places,
    )
    weight = (sigmoid_part * allowed).astype(jnp.bfloat16)
    summed = jnp.einsum(
        "hqk,khd->qhd", weight, value_heads[which], preferred_element_type=jnp.float32
    )
    pieces = [
        lax.psum_scatter(
            summed.reshape(lax.axis_size("kv") * block, width).astype(jnp.bfloat16),
            "kv",
            scatter_dimension=0,
            tiled=True,
        ).astype(jnp.float32)
    ]
    attended_low = jnp.stack(pieces).reshape(count, width).astype(jnp.bfloat16)
    resid = flat + jnp.dot(attended_low, full_out, preferred_element_type=jnp.float32)
    normed_mlp, inverse_mlp = norm_forward(resid, full_gain_mlp)
    normed_mlp_low = normed_mlp.astype(jnp.bfloat16)
    upstream_low = cotangent.reshape(count, width)
    upstream = upstream_low.astype(jnp.float32)
    slice_gate, slice_up, slice_down = (
        lax.all_gather(w_gate, "row", axis=1, tiled=True),
        lax.all_gather(w_up, "row", axis=1, tiled=True),
        lax.all_gather(w_down, "row", axis=0, tiled=True),
    )
    row_normed, row_upstream = (
        lax.all_gather(normed_mlp_low.reshape(rows_here, block, width), "kv", axis=1, tiled=True),
        lax.all_gather(cotangent, "kv", axis=1, tiled=True),
    )
    normed_rows = row_normed.reshape(rows_here * LEN, width)
    upstream_rows = row_upstream.reshape(rows_here * LEN, width)
    gate = jnp.dot(normed_rows, slice_gate, preferred_element_type=jnp.float32)
    up_part = jnp.dot(normed_rows, slice_up, preferred_element_type=jnp.float32)
    sigmoid_gate = jax.nn.sigmoid(gate)
    hidden_low = (gate * sigmoid_gate * up_part).astype(jnp.bfloat16)
    hidden_rows = hidden_low.reshape(rows_here, LEN, hidden_low.shape[1])
    which = 0
    hidden_part = hidden_rows[which]
    outputs = [
        lax.psum_scatter(
            jnp.dot(hidden_part, slice_down, preferred_element_type=jnp.float32).astype(
                jnp.bfloat16
            ),
            "kv",
            scatter_dimension=0,
            tiled=True,
        ).astype(jnp.float32)
    ]
    result = resid + jnp.stack(outputs).reshape(count, width)
    d_hidden = contract_cols(upstream_rows, slice_down)
    d_gate, d_up = gate_backward(d_hidden, gate, up_part, sigmoid_gate)
    partial_normed = contract_cols(d_gate, slice_gate) + contract_cols(d_up, slice_up)
    d_normed_mlp = (
        lax.psum_scatter(
            partial_normed.reshape(rows_here, LEN, width).astype(jnp.bfloat16),
            "kv",
            scatter_dimension=1,
            tiled=True,
        )
        .astype(jnp.float32)
        .reshape(count, width)
    )
    grad_gate, grad_up, grad_down = (
        lax.psum_scatter(
            contract_rows(normed_rows, d_gate).astype(jnp.bfloat16),
            "row",
            scatter_dimension=1,
            tiled=True,
        ).astype(jnp.float32),
        lax.psum_scatter(
            contract_rows(normed_rows, d_up).astype(jnp.bfloat16),
            "row",
            scatter_dimension=1,
            tiled=True,
        ).astype(jnp.float32),
        lax.psum_scatter(
            contract_rows(hidden_low, upstream_rows).astype(jnp.bfloat16),
            "row",
            scatter_dimension=0,
            tiled=True,
        ).astype(jnp.float32),
    )
    mixed = result.astype(jnp.bfloat16).reshape(rows_here, block, width)
    back_mlp, gain_mlp_term = norm_backward(resid, inverse_mlp, full_gain_mlp, d_normed_mlp)
    d_resid = upstream + back_mlp
    d_resid_low = d_resid.astype(jnp.bfloat16)
    d_attended = contract_cols(d_resid_low, full_out).astype(jnp.bfloat16)
    grads_all = lax.all_gather(
        d_attended.reshape(rows_here, block, width), "kv", axis=1, tiled=True
    )
    query_block = min(512, LEN)
    block_count = LEN // query_block
    which = 0

    def sweep(carry, index, which=which):
        key_total, value_total = carry
        start = index * query_block
        query_rows = lax.dynamic_slice_in_dim(queries_all[which], start, query_block, 0)
        grad_rows = lax.dynamic_slice_in_dim(grads_all[which], start, query_block, 0)
        query_segment = lax.dynamic_slice_in_dim(segment[which], start, query_block, 0)
        sigmoid_part, allowed = score_block(
            query_rows,
            key_heads[which],
            query_segment,
            key_segment[which],
            key_valid[which],
            start,
            key_places,
        )
        weight = (sigmoid_part * allowed).astype(jnp.bfloat16)
        grad_heads = grad_rows.reshape(query_block, H, HD)
        value_total = value_total + jnp.einsum(
            "hqk,qhd->khd", weight, grad_heads, preferred_element_type=jnp.float32
        )
        d_weight = jnp.einsum(
            "qhd,khd->hqk", grad_heads, value_heads[which], preferred_element_type=jnp.float32
        )
        d_score = (d_weight * sigmoid_part * (1.0 - sigmoid_part) * allowed).astype(jnp.bfloat16)
        query_part = (
            jnp.einsum(
                "hqk,khd->qhd", d_score, key_heads[which], preferred_element_type=jnp.float32
            )
            * scale
        )
        key_total = (
            key_total
            + jnp.einsum(
                "hqk,qhd->khd",
                d_score,
                query_rows.reshape(query_block, H, HD),
                preferred_element_type=jnp.float32,
            )
            * scale
        )
        return ((key_total, value_total), query_part.reshape(query_block, width))

    zeros = jnp.zeros((block, H, HD), jnp.float32)
    totals, query_parts = lax.scan(sweep, (zeros, zeros), jnp.arange(block_count, dtype=jnp.int32))
    query_terms = [query_parts.reshape(LEN, width)]
    key_grads = [totals[0].reshape(block, width)]
    value_grads = [totals[1].reshape(block, width)]
    query_local = lax.psum_scatter(
        jnp.stack(query_terms).astype(jnp.bfloat16), "kv", scatter_dimension=1, tiled=True
    ).astype(jnp.float32)
    d_query_low = query_local.reshape(count, width).astype(jnp.bfloat16)
    d_key_low = jnp.stack(key_grads).reshape(count, width).astype(jnp.bfloat16)
    d_value_low = jnp.stack(value_grads).reshape(count, width).astype(jnp.bfloat16)
    d_normed_attn = (
        contract_cols(d_query_low, full_query)
        + contract_cols(d_key_low, full_key)
        + contract_cols(d_value_low, full_value)
    )
    back_attn, gain_attn_term = norm_backward(flat, inverse_attn, full_gain_attn, d_normed_attn)
    grad_tokens = (d_resid + back_attn).reshape(rows_here, block, width)
    projected_low = jnp.concatenate((d_query_low, d_key_low, d_value_low), axis=1)
    grad_projections = lax.psum_scatter(
        contract_rows(normed_attn_low, projected_low),
        ("row", "kv"),
        scatter_dimension=0,
        tiled=True,
    )
    out_term = contract_rows(attended_low, d_resid_low)
    grad_out, grad_gain_attn, grad_gain_mlp = (
        lax.psum_scatter(out_term, ("row", "kv"), scatter_dimension=0, tiled=True),
        lax.psum_scatter(gain_attn_term, ("row", "kv"), scatter_dimension=0, tiled=True),
        lax.psum_scatter(gain_mlp_term, ("row", "kv"), scatter_dimension=0, tiled=True),
    )
    grad_query = grad_projections[:, :width]
    grad_key = grad_projections[:, width : 2 * width]
    grad_value = grad_projections[:, 2 * width :]
    return (
        mixed,
        grad_tokens,
        grad_query,
        grad_key,
        grad_value,
        grad_out,
        grad_gate,
        grad_up,
        grad_down,
        grad_gain_attn,
        grad_gain_mlp,
    )


def solution(mesh):
    rows, columns = mesh.shape["row"], mesh.shape["kv"]
    if rows == 4 and columns == 2 * rows:
        mesh = Mesh(mesh.devices.reshape(2, 2, rows, 2), ("y", "c", "z", "x"))
        row, kv, run = ("y", "c"), ("z", "x"), body_layers
    else:
        row, kv, run = "row", "kv", body_any
    both = ("y", "c", "z", "x") if run is body_layers else ("row", "kv")
    tall, wide, flat = P(both, None), P(None, both), P(both)
    tokens = P(row, kv, None)
    return jax.shard_map(
        run,
        mesh=mesh,
        in_specs=(tokens, P(row, None), tokens, tall, tall, tall, tall, wide, wide, tall, flat, flat),
        out_specs=(tokens, tokens, tall, tall, tall, tall, wide, wide, tall, flat, flat),
        check_vma=False,
    )
```

```python
import functools
import math

import jax
import jax.numpy as jnp
from jax import lax
from jax.experimental import pallas as pl
from jax.experimental.pallas import tpu as pltpu
from jax.sharding import Mesh, PartitionSpec as P

H = 16
HD = 128
LEN = 4096


EPSILON = 1e-05


def contract_rows(left, right):
    return lax.dot_general(
        left, right, (((0,), (0,)), ((), ())), preferred_element_type=jnp.float32
    )


def contract_cols(left, right):
    return lax.dot_general(
        left, right, (((1,), (1,)), ((), ())), preferred_element_type=jnp.float32
    )


def norm_forward(value, gain):
    inverse = lax.rsqrt(jnp.mean(value * value, axis=-1, keepdims=True) + EPSILON)
    return (value * inverse * gain.astype(jnp.float32), inverse)


def norm_backward(value, inverse, gain, upstream):
    scaled = upstream * gain.astype(jnp.float32)
    inner = jnp.mean(scaled * value, axis=-1, keepdims=True)
    back = inverse * scaled - value * (inverse * inverse * inverse) * inner
    gain_term = jnp.sum(upstream * value * inverse, axis=0)
    return (back, gain_term)


def segment_table(lengths):
    ends = jnp.cumsum(lengths, axis=-1)
    places = jnp.arange(LEN, dtype=jnp.int32)
    segment = jnp.sum((ends[:, None, :] <= places[None, :, None]).astype(jnp.int32), axis=-1)
    valid = places[None, :] < ends[:, -1:]
    return (segment, valid)


def score_block(
    query_rows, key_heads, query_segment, key_segment, key_valid, query_start, key_places
):
    count = query_rows.shape[0]
    query_heads = query_rows.reshape(count, H, HD)
    raw = jnp.einsum("qhd,khd->hqk", query_heads, key_heads, preferred_element_type=jnp.float32)
    scores = raw * (1.0 / math.sqrt(HD)) - math.log(LEN)
    places = query_start + jnp.arange(count, dtype=jnp.int32)
    allowed = (
        (key_places[None, :] <= places[:, None])
        & (key_segment[None, :] == query_segment[:, None])
        & key_valid[None, :]
    )
    return (jax.nn.sigmoid(scores), allowed.astype(jnp.float32)[None])


def gate_backward(d_hidden, gate, up_part, sigmoid_gate):
    d_gate = (d_hidden * up_part * sigmoid_gate * (1.0 + gate * (1.0 - sigmoid_gate))).astype(
        jnp.bfloat16
    )
    d_up = (d_hidden * gate * sigmoid_gate).astype(jnp.bfloat16)
    return (d_gate, d_up)


TILE = 512
LOW = jnp.bfloat16
VMEM_LIMIT = 60 * 1024 * 1024


def doc_start(ends, place):
    start = jnp.zeros_like(place)
    for k in range(8):
        start = jnp.where(ends[k] <= place, ends[k], start)
    return jnp.where(place < ends[7], start, LEN)


def doc_end(ends, place):
    end = ends[7]
    for k in range(6, -1, -1):
        end = jnp.where(ends[k] > place, ends[k], end)
    return end


def sigmoid_of(raw):
    return pl.reciprocal(1.0 + jnp.exp2(math.log2(LEN) - raw * (math.log2(math.e) / math.sqrt(HD))), approx=True)


def dot_nt(left, right):
    return lax.dot_general(left, right, (((1,), (1,)), ((), ())), preferred_element_type=jnp.float32)


def rows_of(ends, block):
    z, x = block // 2, block % 2
    return pl.ds(pl.multiple_of((4 * ((z + ends[8]) % 2) + 2 * (z // 2) + x) * TILE, TILE), TILE)


def attend_kernel(ends, qkv, out, total):
    head, i = pl.program_id(0), pl.program_id(1)
    column = pl.multiple_of(head * HD, HD)
    width = qkv.shape[1] // 3
    first = i * TILE
    query = qkv[rows_of(ends, i), pl.ds(column, HD)]
    total[...] = jnp.zeros_like(total)
    begin = jnp.minimum(doc_start(ends, first), first) // TILE
    latest = doc_start(ends, first + TILE - 1)

    def step(j, carry):
        here = rows_of(ends, j)
        key = qkv[here, pl.ds(pl.multiple_of(column + width, HD), HD)]
        value = qkv[here, pl.ds(pl.multiple_of(column + 2 * width, HD), HD)]
        plain = (j < i) & (j * TILE >= latest)

        @pl.when(plain)
        def _():
            weight = sigmoid_of(dot_nt(query, key)).astype(LOW)
            total[...] += jnp.dot(weight, value, preferred_element_type=jnp.float32)

        @pl.when(jnp.logical_not(plain))
        def _():
            q_place = first + lax.broadcasted_iota(jnp.int32, (TILE, 1), 0)
            k_place = j * TILE + lax.broadcasted_iota(jnp.int32, (1, TILE), 1)
            allowed = (k_place <= q_place) & (k_place >= doc_start(ends, q_place))
            weight = jnp.where(allowed, sigmoid_of(dot_nt(query, key)), 0.0).astype(LOW)
            total[...] += jnp.dot(weight, value, preferred_element_type=jnp.float32)

        return carry

    lax.fori_loop(begin, i + 1, step, 0)
    out[rows_of(ends, i), pl.ds(column, HD)] = total[...].astype(LOW)


def attend_back_kernel(ends, qkv, grads, out, query_total, key_total, value_total):
    head, j = pl.program_id(0), pl.program_id(1)
    column = pl.multiple_of(head * HD, HD)
    width = qkv.shape[1] // 3
    first = j * TILE
    here = rows_of(ends, j)
    key_column = pl.multiple_of(column + width, HD)
    value_column = pl.multiple_of(column + 2 * width, HD)
    key = qkv[here, pl.ds(key_column, HD)]
    value = qkv[here, pl.ds(value_column, HD)]
    key_turned = key.T
    key_total[...] = jnp.zeros_like(key_total)
    value_total[...] = jnp.zeros_like(value_total)

    @pl.when(j == 0)
    def _():
        query_total[...] = jnp.zeros_like(query_total)

    end = pl.cdiv(doc_end(ends, first + TILE - 1), TILE)

    def step(i, carry):
        there = rows_of(ends, i)
        turned = pl.ds(pl.multiple_of(i * TILE, TILE), TILE)
        query = qkv[there, pl.ds(column, HD)]
        grad = grads[there, pl.ds(column, HD)]
        plain = (j < i) & (first >= doc_start(ends, i * TILE + TILE - 1))

        def finish(sig):
            value_total[...] += jnp.dot(sig.astype(LOW), grad, preferred_element_type=jnp.float32)
            d_score = (dot_nt(value, grad) * (sig * (1.0 - sig))).astype(LOW)
            key_total[...] += jnp.dot(d_score, query, preferred_element_type=jnp.float32)
            query_total[:, turned] += jnp.dot(key_turned, d_score, preferred_element_type=jnp.float32)

        @pl.when(plain)
        def _():
            finish(sigmoid_of(dot_nt(key, query)))

        @pl.when(jnp.logical_not(plain))
        def _():
            q_place = i * TILE + lax.broadcasted_iota(jnp.int32, (1, TILE), 1)
            k_place = first + lax.broadcasted_iota(jnp.int32, (TILE, 1), 0)
            allowed = (k_place <= q_place) & (k_place >= doc_start(ends, q_place))
            finish(jnp.where(allowed, sigmoid_of(dot_nt(key, query)), 0.0))

        return carry

    lax.fori_loop(j, end, step, 0)
    scale = 1.0 / math.sqrt(HD)
    out[here, pl.ds(key_column, HD)] = (key_total[...] * scale).astype(LOW)
    out[here, pl.ds(value_column, HD)] = value_total[...].astype(LOW)

    @pl.when(j == pl.num_programs(1) - 1)
    def _():
        for t in range(LEN // TILE):
            out[rows_of(ends, t), pl.ds(column, HD)] = (
                (query_total[:, t * TILE : (t + 1) * TILE] * scale).T.astype(LOW)
            )


def attend(ends, qkv):
    places, width = qkv.shape
    heads = width // (3 * HD)
    return pl.pallas_call(
        attend_kernel,
        out_shape=jax.ShapeDtypeStruct((places, width // 3), LOW),
        grid_spec=pltpu.PrefetchScalarGridSpec(
            num_scalar_prefetch=1,
            grid=(heads, places // TILE),
            in_specs=[pl.BlockSpec((places, width), lambda h, i, ends: (0, 0))],
            out_specs=pl.BlockSpec((places, width // 3), lambda h, i, ends: (0, 0)),
            scratch_shapes=[pltpu.VMEM((TILE, HD), jnp.float32)],
        ),
        compiler_params=pltpu.CompilerParams(vmem_limit_bytes=VMEM_LIMIT),
        cost_estimate=pl.CostEstimate(
            flops=4 * heads * places * places * HD // 2, bytes_accessed=8 * places * width // 3, transcendentals=heads * places * places // 2
        ),
    )(ends, qkv)


def attend_back(ends, qkv, grads):
    places, width = qkv.shape
    heads = width // (3 * HD)
    whole = lambda columns: pl.BlockSpec((places, columns), lambda h, j, ends: (0, 0))
    return pl.pallas_call(
        attend_back_kernel,
        out_shape=jax.ShapeDtypeStruct((places, width), LOW),
        grid_spec=pltpu.PrefetchScalarGridSpec(
            num_scalar_prefetch=1,
            grid=(heads, places // TILE),
            in_specs=[whole(width), whole(width // 3)],
            out_specs=whole(width),
            scratch_shapes=[
                pltpu.VMEM((HD, places), jnp.float32),
                pltpu.VMEM((TILE, HD), jnp.float32),
                pltpu.VMEM((TILE, HD), jnp.float32),
            ],
        ),
        compiler_params=pltpu.CompilerParams(vmem_limit_bytes=VMEM_LIMIT),
        cost_estimate=pl.CostEstimate(
            flops=10 * heads * places * places * HD // 2, bytes_accessed=14 * places * width // 3, transcendentals=heads * places * places // 2
        ),
    )(ends, qkv, grads)


LAYER = ("y", "c", "x")
ALL = ("y", "c", "z", "x")


def gather_layer(part):
    return lax.all_gather(part, LAYER, axis=0, tiled=True)


def scatter_layer(whole):
    return lax.psum_scatter(whole.astype(LOW), LAYER, scatter_dimension=0, tiled=True).astype(jnp.float32)


def trade(part, back=False):
    pairs = []
    for y in range(2):
        for c in range(2):
            for z in range(4):
                for x in range(2):
                    owner = ((y * 2 + c) * 4 + z) * 2 + x
                    worker = ((((z + c) % 2) * 2 + z // 2) * 4 + 2 * y + c) * 2 + x
                    pairs.append((worker, owner) if back else (owner, worker))
    return lax.ppermute(part, ALL, pairs)


def dot_wide(left, right):
    return jnp.dot(left, right, preferred_element_type=jnp.float32)


def body_layers(
    tokens, lengths, cotangent, w_query, w_key, w_value, w_out, w_gate, w_up, w_down, gain_attn, gain_mlp
):
    rows_here, block, width = tokens.shape
    members = lax.axis_size(LAYER)
    layers = lax.axis_size("z")
    shard = w_query.shape[0]
    owned = width // members
    gains = lax.all_gather(jnp.stack((gain_attn, gain_mlp), axis=1), ALL, axis=0, tiled=True)
    full_gain_attn, full_gain_mlp = gains[:, 0], gains[:, 1]
    parity = (lax.axis_index("z") % 2).astype(jnp.int32)
    ends = jnp.concatenate((jnp.cumsum(trade(lengths)[0]), parity[None]))
    flat = trade(tokens).reshape(block, width).astype(jnp.float32)
    normed_attn, inverse_attn = norm_forward(flat, full_gain_attn)
    layer_normed = gather_layer(normed_attn.astype(LOW))
    qkv_shards = jnp.stack((w_query, w_key, w_value), axis=1).reshape(shard, 3, members, owned)
    qkv_shards = qkv_shards.transpose(2, 0, 1, 3).reshape(members, shard, 3 * owned)
    qkv_shards = lax.all_to_all(qkv_shards, LAYER, 0, 0)
    w_qkv = lax.all_gather(qkv_shards, "z", axis=0)
    w_qkv = w_qkv.reshape(layers, 4, 2 * shard, 3 * owned).transpose(1, 0, 2, 3).reshape(width, 3 * owned)
    out_rows = lax.all_gather(w_out, ("z", "x"), axis=0, tiled=True)
    w_out_own = lax.dynamic_slice_in_dim(out_rows, lax.axis_index("x") * owned, owned, 0)

    qkv = dot_wide(layer_normed, w_qkv).astype(LOW)
    attended = attend(ends, qkv)
    resid = flat + scatter_layer(dot_wide(attended, w_out_own))

    normed_mlp, inverse_mlp = norm_forward(resid, full_gain_mlp)
    own_gate = lax.all_gather(w_gate, "z", axis=1, tiled=True)
    own_up = lax.all_gather(w_up, "z", axis=1, tiled=True)
    own_down = lax.all_gather(w_down, "z", axis=0, tiled=True)
    upstream_low = trade(cotangent).reshape(block, width)
    upstream = upstream_low.astype(jnp.float32)
    layer_upstream = gather_layer(upstream_low)
    layer_mlp = gather_layer(normed_mlp.astype(LOW))
    gate = dot_wide(layer_mlp, own_gate)
    up_part = dot_wide(layer_mlp, own_up)
    sigmoid_gate = jax.nn.sigmoid(gate)
    hidden = (gate * sigmoid_gate * up_part).astype(LOW)
    result = resid + scatter_layer(dot_wide(hidden, own_down))
    d_hidden = contract_cols(layer_upstream, own_down)
    d_gate, d_up = gate_backward(d_hidden, gate, up_part, sigmoid_gate)
    d_normed_mlp = scatter_layer(contract_cols(d_gate, own_gate) + contract_cols(d_up, own_up))

    def scatter_layers(whole, axis):
        return lax.psum_scatter(whole.astype(LOW), "z", scatter_dimension=axis, tiled=True).astype(jnp.float32)

    grad_gate = scatter_layers(contract_rows(layer_mlp, d_gate), 1)
    grad_up = scatter_layers(contract_rows(layer_mlp, d_up), 1)
    grad_down = scatter_layers(contract_rows(hidden, layer_upstream), 0)
    mixed = trade(result.astype(LOW).reshape(rows_here, block, width), back=True)

    back_mlp, gain_mlp_term = norm_backward(resid, inverse_mlp, full_gain_mlp, d_normed_mlp)
    d_resid = upstream + back_mlp
    layer_d_resid = gather_layer(d_resid.astype(LOW))
    d_attended = contract_cols(layer_d_resid, w_out_own).astype(LOW)
    d_qkv = attend_back(ends, qkv, d_attended)
    d_normed_attn = scatter_layer(contract_cols(d_qkv, w_qkv))
    out_term = contract_rows(attended, layer_d_resid)
    qkv_term = contract_rows(layer_normed, d_qkv)

    back_attn, gain_attn_term = norm_backward(flat, inverse_attn, full_gain_attn, d_normed_attn)
    grad_tokens = (d_resid + back_attn).astype(LOW).reshape(rows_here, block, width)
    grad_tokens = trade(grad_tokens, back=True).astype(jnp.float32)

    out_term = lax.dynamic_update_slice_in_dim(
        jnp.zeros((2 * owned, width), LOW), out_term.astype(LOW), lax.axis_index("x") * owned, 0
    )
    grad_out = lax.psum_scatter(out_term, ("z", "x"), scatter_dimension=0, tiled=True).astype(jnp.float32)
    qkv_term = qkv_term.reshape(4, layers, 2 * shard, 3 * owned).transpose(1, 0, 2, 3)
    qkv_term = qkv_term.reshape(layers * members * shard, 3 * owned)
    qkv_term = lax.psum_scatter(qkv_term.astype(LOW), "z", scatter_dimension=0, tiled=True)
    qkv_term = lax.all_to_all(qkv_term.reshape(members, shard, 3 * owned), LAYER, 0, 0)
    qkv_term = qkv_term.reshape(members, shard, 3, owned).transpose(2, 1, 0, 3).astype(jnp.float32)
    grad_query, grad_key, grad_value = qkv_term.reshape(3, shard, width)
    gain_terms = lax.psum_scatter(
        jnp.stack((gain_attn_term, gain_mlp_term), axis=1), ALL, scatter_dimension=0, tiled=True
    )
    return (
        mixed,
        grad_tokens,
        grad_query,
        grad_key,
        grad_value,
        grad_out,
        grad_gate,
        grad_up,
        grad_down,
        gain_terms[:, 0],
        gain_terms[:, 1],
    )


def body_any(
    tokens,
    lengths,
    cotangent,
    w_query,
    w_key,
    w_value,
    w_out,
    w_gate,
    w_up,
    w_down,
    gain_attn,
    gain_mlp,
):
    rows_here, block, width = tokens.shape
    count = rows_here * block
    scale = 1.0 / math.sqrt(HD)
    kv_place = lax.axis_index("kv")
    key_places = kv_place * block + jnp.arange(block, dtype=jnp.int32)
    attn_set = (
        lax.all_gather(w_query, ("row", "kv"), axis=0, tiled=True),
        lax.all_gather(w_key, ("row", "kv"), axis=0, tiled=True),
        lax.all_gather(w_value, ("row", "kv"), axis=0, tiled=True),
        lax.all_gather(w_out, ("row", "kv"), axis=0, tiled=True),
        lax.all_gather(gain_attn, ("row", "kv"), axis=0, tiled=True),
        lax.all_gather(gain_mlp, ("row", "kv"), axis=0, tiled=True),
    )
    full_query, full_key, full_value, full_out, full_gain_attn, full_gain_mlp = attn_set
    flat = tokens.reshape(count, width).astype(jnp.float32)
    normed_attn, inverse_attn = norm_forward(flat, full_gain_attn)
    normed_attn_low = normed_attn.astype(jnp.bfloat16)
    query_low = jnp.dot(normed_attn_low, full_query, preferred_element_type=jnp.float32).astype(
        jnp.bfloat16
    )
    key_low = jnp.dot(normed_attn_low, full_key, preferred_element_type=jnp.float32).astype(
        jnp.bfloat16
    )
    value_low = jnp.dot(normed_attn_low, full_value, preferred_element_type=jnp.float32).astype(
        jnp.bfloat16
    )
    key_heads = key_low.reshape(rows_here, block, H, HD)
    value_heads = value_low.reshape(rows_here, block, H, HD)
    segment, valid = segment_table(lengths)
    key_segment = lax.dynamic_slice_in_dim(segment, kv_place * block, block, 1)
    key_valid = lax.dynamic_slice_in_dim(valid, kv_place * block, block, 1)
    queries_all = lax.all_gather(
        query_low.reshape(rows_here, block, width), "kv", axis=1, tiled=True
    )
    which = 0
    query_rows = queries_all[which]
    query_segment = segment[which]
    sigmoid_part, allowed = score_block(
        query_rows,
        key_heads[which],
        query_segment,
        key_segment[which],
        key_valid[which],
        jnp.int32(0),
        key_places,
    )
    weight = (sigmoid_part * allowed).astype(jnp.bfloat16)
    summed = jnp.einsum(
        "hqk,khd->qhd", weight, value_heads[which], preferred_element_type=jnp.float32
    )
    pieces = [
        lax.psum_scatter(
            summed.reshape(lax.axis_size("kv") * block, width).astype(jnp.bfloat16),
            "kv",
            scatter_dimension=0,
            tiled=True,
        ).astype(jnp.float32)
    ]
    attended_low = jnp.stack(pieces).reshape(count, width).astype(jnp.bfloat16)
    resid = flat + jnp.dot(attended_low, full_out, preferred_element_type=jnp.float32)
    normed_mlp, inverse_mlp = norm_forward(resid, full_gain_mlp)
    normed_mlp_low = normed_mlp.astype(jnp.bfloat16)
    upstream_low = cotangent.reshape(count, width)
    upstream = upstream_low.astype(jnp.float32)
    slice_gate, slice_up, slice_down = (
        lax.all_gather(w_gate, "row", axis=1, tiled=True),
        lax.all_gather(w_up, "row", axis=1, tiled=True),
        lax.all_gather(w_down, "row", axis=0, tiled=True),
    )
    row_normed, row_upstream = (
        lax.all_gather(normed_mlp_low.reshape(rows_here, block, width), "kv", axis=1, tiled=True),
        lax.all_gather(cotangent, "kv", axis=1, tiled=True),
    )
    normed_rows = row_normed.reshape(rows_here * LEN, width)
    upstream_rows = row_upstream.reshape(rows_here * LEN, width)
    gate = jnp.dot(normed_rows, slice_gate, preferred_element_type=jnp.float32)
    up_part = jnp.dot(normed_rows, slice_up, preferred_element_type=jnp.float32)
    sigmoid_gate = jax.nn.sigmoid(gate)
    hidden_low = (gate * sigmoid_gate * up_part).astype(jnp.bfloat16)
    hidden_rows = hidden_low.reshape(rows_here, LEN, hidden_low.shape[1])
    which = 0
    hidden_part = hidden_rows[which]
    outputs = [
        lax.psum_scatter(
            jnp.dot(hidden_part, slice_down, preferred_element_type=jnp.float32).astype(
                jnp.bfloat16
            ),
            "kv",
            scatter_dimension=0,
            tiled=True,
        ).astype(jnp.float32)
    ]
    result = resid + jnp.stack(outputs).reshape(count, width)
    d_hidden = contract_cols(upstream_rows, slice_down)
    d_gate, d_up = gate_backward(d_hidden, gate, up_part, sigmoid_gate)
    partial_normed = contract_cols(d_gate, slice_gate) + contract_cols(d_up, slice_up)
    d_normed_mlp = (
        lax.psum_scatter(
            partial_normed.reshape(rows_here, LEN, width).astype(jnp.bfloat16),
            "kv",
            scatter_dimension=1,
            tiled=True,
        )
        .astype(jnp.float32)
        .reshape(count, width)
    )
    grad_gate, grad_up, grad_down = (
        lax.psum_scatter(
            contract_rows(normed_rows, d_gate).astype(jnp.bfloat16),
            "row",
            scatter_dimension=1,
            tiled=True,
        ).astype(jnp.float32),
        lax.psum_scatter(
            contract_rows(normed_rows, d_up).astype(jnp.bfloat16),
            "row",
            scatter_dimension=1,
            tiled=True,
        ).astype(jnp.float32),
        lax.psum_scatter(
            contract_rows(hidden_low, upstream_rows).astype(jnp.bfloat16),
            "row",
            scatter_dimension=0,
            tiled=True,
        ).astype(jnp.float32),
    )
    mixed = result.astype(jnp.bfloat16).reshape(rows_here, block, width)
    back_mlp, gain_mlp_term = norm_backward(resid, inverse_mlp, full_gain_mlp, d_normed_mlp)
    d_resid = upstream + back_mlp
    d_resid_low = d_resid.astype(jnp.bfloat16)
    d_attended = contract_cols(d_resid_low, full_out).astype(jnp.bfloat16)
    grads_all = lax.all_gather(
        d_attended.reshape(rows_here, block, width), "kv", axis=1, tiled=True
    )
    query_block = min(512, LEN)
    block_count = LEN // query_block
    which = 0

    def sweep(carry, index, which=which):
        key_total, value_total = carry
        start = index * query_block
        query_rows = lax.dynamic_slice_in_dim(queries_all[which], start, query_block, 0)
        grad_rows = lax.dynamic_slice_in_dim(grads_all[which], start, query_block, 0)
        query_segment = lax.dynamic_slice_in_dim(segment[which], start, query_block, 0)
        sigmoid_part, allowed = score_block(
            query_rows,
            key_heads[which],
            query_segment,
            key_segment[which],
            key_valid[which],
            start,
            key_places,
        )
        weight = (sigmoid_part * allowed).astype(jnp.bfloat16)
        grad_heads = grad_rows.reshape(query_block, H, HD)
        value_total = value_total + jnp.einsum(
            "hqk,qhd->khd", weight, grad_heads, preferred_element_type=jnp.float32
        )
        d_weight = jnp.einsum(
            "qhd,khd->hqk", grad_heads, value_heads[which], preferred_element_type=jnp.float32
        )
        d_score = (d_weight * sigmoid_part * (1.0 - sigmoid_part) * allowed).astype(jnp.bfloat16)
        query_part = (
            jnp.einsum(
                "hqk,khd->qhd", d_score, key_heads[which], preferred_element_type=jnp.float32
            )
            * scale
        )
        key_total = (
            key_total
            + jnp.einsum(
                "hqk,qhd->khd",
                d_score,
                query_rows.reshape(query_block, H, HD),
                preferred_element_type=jnp.float32,
            )
            * scale
        )
        return ((key_total, value_total), query_part.reshape(query_block, width))

    zeros = jnp.zeros((block, H, HD), jnp.float32)
    totals, query_parts = lax.scan(sweep, (zeros, zeros), jnp.arange(block_count, dtype=jnp.int32))
    query_terms = [query_parts.reshape(LEN, width)]
    key_grads = [totals[0].reshape(block, width)]
    value_grads = [totals[1].reshape(block, width)]
    query_local = lax.psum_scatter(
        jnp.stack(query_terms).astype(jnp.bfloat16), "kv", scatter_dimension=1, tiled=True
    ).astype(jnp.float32)
    d_query_low = query_local.reshape(count, width).astype(jnp.bfloat16)
    d_key_low = jnp.stack(key_grads).reshape(count, width).astype(jnp.bfloat16)
    d_value_low = jnp.stack(value_grads).reshape(count, width).astype(jnp.bfloat16)
    d_normed_attn = (
        contract_cols(d_query_low, full_query)
        + contract_cols(d_key_low, full_key)
        + contract_cols(d_value_low, full_value)
    )
    back_attn, gain_attn_term = norm_backward(flat, inverse_attn, full_gain_attn, d_normed_attn)
    grad_tokens = (d_resid + back_attn).reshape(rows_here, block, width)
    projected_low = jnp.concatenate((d_query_low, d_key_low, d_value_low), axis=1)
    grad_projections = lax.psum_scatter(
        contract_rows(normed_attn_low, projected_low),
        ("row", "kv"),
        scatter_dimension=0,
        tiled=True,
    )
    out_term = contract_rows(attended_low, d_resid_low)
    grad_out, grad_gain_attn, grad_gain_mlp = (
        lax.psum_scatter(out_term, ("row", "kv"), scatter_dimension=0, tiled=True),
        lax.psum_scatter(gain_attn_term, ("row", "kv"), scatter_dimension=0, tiled=True),
        lax.psum_scatter(gain_mlp_term, ("row", "kv"), scatter_dimension=0, tiled=True),
    )
    grad_query = grad_projections[:, :width]
    grad_key = grad_projections[:, width : 2 * width]
    grad_value = grad_projections[:, 2 * width :]
    return (
        mixed,
        grad_tokens,
        grad_query,
        grad_key,
        grad_value,
        grad_out,
        grad_gate,
        grad_up,
        grad_down,
        grad_gain_attn,
        grad_gain_mlp,
    )


def solution(mesh):
    rows, columns = mesh.shape["row"], mesh.shape["kv"]
    if rows == 4 and columns == 2 * rows:
        mesh = Mesh(mesh.devices.reshape(2, 2, rows, 2), ("y", "c", "z", "x"))
        row, kv, run = ("y", "c"), ("z", "x"), body_layers
    else:
        row, kv, run = "row", "kv", body_any
    both = ("y", "c", "z", "x") if run is body_layers else ("row", "kv")
    tall, wide, flat = P(both, None), P(None, both), P(both)
    tokens = P(row, kv, None)
    return jax.shard_map(
        run,
        mesh=mesh,
        in_specs=(tokens, P(row, None), tokens, tall, tall, tall, tall, wide, wide, tall, flat, flat),
        out_specs=(tokens, tokens, tall, tall, tall, tall, wide, wide, tall, flat, flat),
        check_vma=False,
    )
```

```python
import functools
import math

import jax
import jax.numpy as jnp
from jax import lax
from jax.experimental import pallas as pl
from jax.experimental.pallas import tpu as pltpu
from jax.sharding import Mesh, PartitionSpec as P

H = 16
HD = 128
LEN = 4096


EPSILON = 1e-05


def contract_rows(left, right):
    return lax.dot_general(
        left, right, (((0,), (0,)), ((), ())), preferred_element_type=jnp.float32
    )


def contract_cols(left, right):
    return lax.dot_general(
        left, right, (((1,), (1,)), ((), ())), preferred_element_type=jnp.float32
    )


def norm_forward(value, gain):
    inverse = lax.rsqrt(jnp.mean(value * value, axis=-1, keepdims=True) + EPSILON)
    return (value * inverse * gain.astype(jnp.float32), inverse)


def norm_backward(value, inverse, gain, upstream):
    scaled = upstream * gain.astype(jnp.float32)
    inner = jnp.mean(scaled * value, axis=-1, keepdims=True)
    back = inverse * scaled - value * (inverse * inverse * inverse) * inner
    gain_term = jnp.sum(upstream * value * inverse, axis=0)
    return (back, gain_term)


def segment_table(lengths):
    ends = jnp.cumsum(lengths, axis=-1)
    places = jnp.arange(LEN, dtype=jnp.int32)
    segment = jnp.sum((ends[:, None, :] <= places[None, :, None]).astype(jnp.int32), axis=-1)
    valid = places[None, :] < ends[:, -1:]
    return (segment, valid)


def score_block(
    query_rows, key_heads, query_segment, key_segment, key_valid, query_start, key_places
):
    count = query_rows.shape[0]
    query_heads = query_rows.reshape(count, H, HD)
    raw = jnp.einsum("qhd,khd->hqk", query_heads, key_heads, preferred_element_type=jnp.float32)
    scores = raw * (1.0 / math.sqrt(HD)) - math.log(LEN)
    places = query_start + jnp.arange(count, dtype=jnp.int32)
    allowed = (
        (key_places[None, :] <= places[:, None])
        & (key_segment[None, :] == query_segment[:, None])
        & key_valid[None, :]
    )
    return (jax.nn.sigmoid(scores), allowed.astype(jnp.float32)[None])


def gate_backward(d_hidden, gate, up_part, sigmoid_gate):
    d_gate = (d_hidden * up_part * sigmoid_gate * (1.0 + gate * (1.0 - sigmoid_gate))).astype(
        jnp.bfloat16
    )
    d_up = (d_hidden * gate * sigmoid_gate).astype(jnp.bfloat16)
    return (d_gate, d_up)


TILE = 512
LOW = jnp.bfloat16
VMEM_LIMIT = 60 * 1024 * 1024


def doc_start(ends, place):
    start = jnp.zeros_like(place)
    for k in range(8):
        start = jnp.where(ends[k] <= place, ends[k], start)
    return jnp.where(place < ends[7], start, LEN)


def doc_end(ends, place):
    end = ends[7]
    for k in range(6, -1, -1):
        end = jnp.where(ends[k] > place, ends[k], end)
    return end


def sigmoid_of(raw):
    return pl.reciprocal(1.0 + jnp.exp2(math.log2(LEN) - raw * (math.log2(math.e) / math.sqrt(HD))), approx=True)


def dot_nt(left, right):
    return lax.dot_general(left, right, (((1,), (1,)), ((), ())), preferred_element_type=jnp.float32)


def rows_of(ends, block):
    z, x = block // 2, block % 2
    return pl.ds(pl.multiple_of((4 * ((z + ends[8]) % 2) + 2 * (z // 2) + x) * TILE, TILE), TILE)


def attend_kernel(ends, qkv, out, total):
    head, i = pl.program_id(0), pl.program_id(1)
    column = pl.multiple_of(head * HD, HD)
    width = qkv.shape[1] // 3
    first = i * TILE
    query = qkv[rows_of(ends, i), pl.ds(column, HD)]
    total[...] = jnp.zeros_like(total)
    begin = jnp.minimum(doc_start(ends, first), first) // TILE
    latest = doc_start(ends, first + TILE - 1)

    def step(j, carry):
        here = rows_of(ends, j)
        key = qkv[here, pl.ds(pl.multiple_of(column + width, HD), HD)]
        value = qkv[here, pl.ds(pl.multiple_of(column + 2 * width, HD), HD)]
        plain = (j < i) & (j * TILE >= latest)

        @pl.when(plain)
        def _():
            weight = sigmoid_of(dot_nt(query, key)).astype(LOW)
            total[...] += jnp.dot(weight, value, preferred_element_type=jnp.float32)

        @pl.when(jnp.logical_not(plain))
        def _():
            q_place = first + lax.broadcasted_iota(jnp.int32, (TILE, 1), 0)
            k_place = j * TILE + lax.broadcasted_iota(jnp.int32, (1, TILE), 1)
            allowed = (k_place <= q_place) & (k_place >= doc_start(ends, q_place))
            weight = jnp.where(allowed, sigmoid_of(dot_nt(query, key)), 0.0).astype(LOW)
            total[...] += jnp.dot(weight, value, preferred_element_type=jnp.float32)

        return carry

    lax.fori_loop(begin, i + 1, step, 0)
    out[rows_of(ends, i), pl.ds(column, HD)] = total[...].astype(LOW)


def attend_back_kernel(ends, qkv, grads, out, query_total, key_total, value_total):
    head, j = pl.program_id(0), pl.program_id(1)
    column = pl.multiple_of(head * HD, HD)
    width = qkv.shape[1] // 3
    first = j * TILE
    here = rows_of(ends, j)
    key_column = pl.multiple_of(column + width, HD)
    value_column = pl.multiple_of(column + 2 * width, HD)
    key = qkv[here, pl.ds(key_column, HD)]
    value = qkv[here, pl.ds(value_column, HD)]
    key_turned = key.T
    key_total[...] = jnp.zeros_like(key_total)
    value_total[...] = jnp.zeros_like(value_total)

    @pl.when(j == 0)
    def _():
        query_total[...] = jnp.zeros_like(query_total)

    end = pl.cdiv(doc_end(ends, first + TILE - 1), TILE)

    def step(i, carry):
        there = rows_of(ends, i)
        turned = pl.ds(pl.multiple_of(i * TILE, TILE), TILE)
        query = qkv[there, pl.ds(column, HD)]
        grad = grads[there, pl.ds(column, HD)]
        plain = (j < i) & (first >= doc_start(ends, i * TILE + TILE - 1))

        def finish(sig):
            value_total[...] += jnp.dot(sig.astype(LOW), grad, preferred_element_type=jnp.float32)
            d_score = (dot_nt(value, grad) * (sig * (1.0 - sig))).astype(LOW)
            key_total[...] += jnp.dot(d_score, query, preferred_element_type=jnp.float32)
            query_total[:, turned] += jnp.dot(key_turned, d_score, preferred_element_type=jnp.float32)

        @pl.when(plain)
        def _():
            finish(sigmoid_of(dot_nt(key, query)))

        @pl.when(jnp.logical_not(plain))
        def _():
            q_place = i * TILE + lax.broadcasted_iota(jnp.int32, (1, TILE), 1)
            k_place = first + lax.broadcasted_iota(jnp.int32, (TILE, 1), 0)
            allowed = (k_place <= q_place) & (k_place >= doc_start(ends, q_place))
            finish(jnp.where(allowed, sigmoid_of(dot_nt(key, query)), 0.0))

        return carry

    lax.fori_loop(j, end, step, 0)
    scale = 1.0 / math.sqrt(HD)
    out[here, pl.ds(key_column, HD)] = (key_total[...] * scale).astype(LOW)
    out[here, pl.ds(value_column, HD)] = value_total[...].astype(LOW)

    @pl.when(j == pl.num_programs(1) - 1)
    def _():
        for t in range(LEN // TILE):
            out[rows_of(ends, t), pl.ds(column, HD)] = (
                (query_total[:, t * TILE : (t + 1) * TILE] * scale).T.astype(LOW)
            )


def attend(ends, qkv):
    places, width = qkv.shape
    heads = width // (3 * HD)
    return pl.pallas_call(
        attend_kernel,
        out_shape=jax.ShapeDtypeStruct((places, width // 3), LOW),
        grid_spec=pltpu.PrefetchScalarGridSpec(
            num_scalar_prefetch=1,
            grid=(heads, places // TILE),
            in_specs=[pl.BlockSpec((places, width), lambda h, i, ends: (0, 0))],
            out_specs=pl.BlockSpec((places, width // 3), lambda h, i, ends: (0, 0)),
            scratch_shapes=[pltpu.VMEM((TILE, HD), jnp.float32)],
        ),
        compiler_params=pltpu.CompilerParams(vmem_limit_bytes=VMEM_LIMIT),
        cost_estimate=pl.CostEstimate(
            flops=4 * heads * places * places * HD // 2, bytes_accessed=8 * places * width // 3, transcendentals=heads * places * places // 2
        ),
    )(ends, qkv)


def attend_back(ends, qkv, grads):
    places, width = qkv.shape
    heads = width // (3 * HD)
    whole = lambda columns: pl.BlockSpec((places, columns), lambda h, j, ends: (0, 0))
    return pl.pallas_call(
        attend_back_kernel,
        out_shape=jax.ShapeDtypeStruct((places, width), LOW),
        grid_spec=pltpu.PrefetchScalarGridSpec(
            num_scalar_prefetch=1,
            grid=(heads, places // TILE),
            in_specs=[whole(width), whole(width // 3)],
            out_specs=whole(width),
            scratch_shapes=[
                pltpu.VMEM((HD, places), jnp.float32),
                pltpu.VMEM((TILE, HD), jnp.float32),
                pltpu.VMEM((TILE, HD), jnp.float32),
            ],
        ),
        compiler_params=pltpu.CompilerParams(vmem_limit_bytes=VMEM_LIMIT),
        cost_estimate=pl.CostEstimate(
            flops=10 * heads * places * places * HD // 2, bytes_accessed=14 * places * width // 3, transcendentals=heads * places * places // 2
        ),
    )(ends, qkv, grads)


def dot_wide(left, right):
    return jnp.dot(left, right, preferred_element_type=jnp.float32)


HALF = TILE // 2
CHUNK = 32
MESH_ID = pl.DeviceIdType.MESH


def flip(bit, by):
    return bit + by - 2 * bit * by


def spot():
    return tuple(lax.axis_index(name) for name in ("y", "c", "z", "x"))


def near():
    y, c, z, x = spot()
    return (y, c, z, 1 - x), (1 - y, c, z, x), (y, 1 - c, z, x)


def worker_of(y, c, z, x):
    return lax.rem(z + c, 2), z // 2, 2 * y + c, x


def owner_of(y, c, z, x):
    row = lax.rem(z, 2)
    return z // 2, row, 2 * c + lax.rem(y + row, 2), x


def place_of(y, c, x, half=None):
    first = (4 * y + 2 * c + x) * TILE
    if half is None:
        return pl.ds(pl.multiple_of(first, TILE), TILE)
    return pl.ds(pl.multiple_of(first + half * HALF, HALF), HALF)


def remote(src, dst, send, recv, peer):
    return pltpu.make_async_remote_copy(
        src_ref=src, dst_ref=dst, send_sem=send, recv_sem=recv, device_id=peer, device_id_type=MESH_ID
    )


def greet(peers):
    barrier = pltpu.get_barrier_semaphore()
    for peer in peers:
        pl.semaphore_signal(barrier, inc=1, device_id=peer, device_id_type=MESH_ID)
    pl.semaphore_wait(barrier, len(peers))


class Gather:
    def __init__(self, own, whole, send, recv):
        y, c, z, x = spot()
        across_x, across_y, core = near()

        def from_own(k, half, peer):
            return remote(own(half), whole.at[place_of(y, c, x, half)], send.at[k], recv.at[k], peer)

        def passed(k, at, peer):
            return remote(whole.at[at], whole.at[at], send.at[k], recv.at[k], peer)

        self.mine = [
            [from_own(0, 0, across_x), from_own(1, 0, across_y), from_own(2, 0, core)],
            [from_own(3, 1, across_x), from_own(4, 1, across_y), from_own(5, 1, core)],
        ]
        held_x = [place_of(y, c, 1 - x, half) for half in (0, 1)]
        held_y = [place_of(1 - y, c, x, half) for half in (0, 1)]
        far = [place_of(1 - y, c, 1 - x, half) for half in (0, 1)]
        self.over_y, self.over_x = passed(6, held_x[0], across_y), passed(7, held_y[1], across_x)
        self.core_x = [passed(8 + half, held_x[half], core) for half in (0, 1)]
        self.core_y = [passed(10 + half, held_y[half], core) for half in (0, 1)]
        self.core_far = [passed(12 + half, far[half], core) for half in (0, 1)]

    def start(self, half):
        for copy in self.mine[half]:
            copy.start()

    def pass_first(self):
        self.mine[0][0].wait_recv()
        self.over_y.start()
        self.core_x[0].start()
        self.mine[0][1].wait_recv()
        self.core_y[0].start()

    def pass_second(self):
        self.mine[1][1].wait_recv()
        self.over_x.start()
        self.core_y[1].start()
        self.mine[1][0].wait_recv()
        self.core_x[1].start()

    def pass_far(self):
        self.over_y.wait_recv()
        self.core_far[0].start()
        self.over_x.wait_recv()
        self.core_far[1].start()

    def finish(self):
        from_core = [self.mine[0][2], self.mine[1][2]] + self.core_x + self.core_y + self.core_far
        for copy in from_core:
            copy.wait_recv()
        for copy in self.mine[0] + self.mine[1] + [self.over_y, self.over_x] + self.core_x + self.core_y + self.core_far:
            copy.wait_send()


GATHER_COPIES = 14


def run_gather(own, whole, send, recv, local):
    y, c, z, x = spot()
    keep = pltpu.make_async_copy(own, whole.at[place_of(y, c, x)], local)
    keep.start()
    gather = Gather(lambda half: own.at[pl.ds(half * HALF, HALF)], whole, send, recv)
    gather.start(0)
    gather.start(1)
    gather.pass_first()
    gather.pass_second()
    gather.pass_far()
    gather.finish()
    keep.wait()


def add_rows(total, first, term, start, count):
    def step(i, carry):
        here = pl.ds(pl.multiple_of(first + i * CHUNK, CHUNK), CHUNK)
        there = pl.ds(pl.multiple_of(start + i * CHUNK, CHUNK), CHUNK)
        total[here, :] = (total[here, :].astype(jnp.float32) + term[there, :].astype(jnp.float32)).astype(LOW)
        return carry

    lax.fori_loop(0, count // CHUNK, step, 0)


def scatter_scratch(width):
    return [
        pltpu.VMEM((2, TILE, width), LOW),
        pltpu.VMEM((4, TILE, width), LOW),
        pltpu.VMEM((4, TILE, width), LOW),
        pltpu.VMEM((2, HALF, width), LOW),
        pltpu.VMEM((2, TILE, width), LOW),
        pltpu.SemaphoreType.DMA((10,)),
        pltpu.SemaphoreType.DMA((10,)),
    ]


def run_scatter(produce, staged, core_part, total, relayed, landed, send, recv):
    y, c, z, x = spot()
    across_x, across_y, core = near()
    dests = ((1 - y, 1 - x), (y, 1 - x), (1 - y, x), (y, x))
    first, second = pl.ds(0, HALF), pl.ds(HALF, HALF)
    to_core = [
        remote(staged.at[k % 2], core_part.at[k], send.at[k], recv.at[k], core) for k in range(4)
    ]
    far_x = remote(total.at[0, first], relayed.at[0], send.at[4], recv.at[4], across_x)
    far_y = remote(total.at[0, second], relayed.at[1], send.at[5], recv.at[5], across_y)
    to_x = [
        remote(total.at[1, at], landed.at[0, at], send.at[6 + half], recv.at[6 + half], across_x)
        for half, at in enumerate((first, second))
    ]
    to_y = [
        remote(total.at[2, at], landed.at[1, at], send.at[8 + half], recv.at[8 + half], across_y)
        for half, at in enumerate((first, second))
    ]
    for k, (to_row, to_column) in enumerate(dests):
        if k >= 2:
            to_core[k - 2].wait_send()
        produce(2 * k, to_row, 1 - c, to_column, staged.at[k % 2])
        to_core[k].start()
        produce(2 * k + 1, to_row, c, to_column, total.at[k])
        to_core[k].wait_recv()
        add_rows(total.at[k], 0, core_part.at[k], 0, TILE)
        if k == 0:
            far_x.start()
            far_y.start()
        if k == 1:
            to_x[0].start()
        if k == 2:
            to_y[1].start()
    far_y.wait_recv()
    add_rows(total.at[1], HALF, relayed.at[1], 0, HALF)
    to_x[1].start()
    far_x.wait_recv()
    add_rows(total.at[2], 0, relayed.at[0], 0, HALF)
    to_y[0].start()
    for copy in to_x + to_y:
        copy.wait_recv()
    for copy in to_core[2:] + [far_x, far_y] + to_x + to_y:
        copy.wait_send()


def begin_kernel(x_own, w_query, w_key, w_value, x_whole, w_qkv, trade_send, trade_recv, gather_send, gather_recv, w_send, w_recv, up_send, up_recv, down_send, down_recv, local):
    y, c, z, x = spot()
    row = 2 * y + c
    last = lax.axis_size("z") - 1
    worker, owner = worker_of(y, c, z, x), owner_of(y, c, z, x)
    moves = jnp.logical_not((worker[0] == y) & (worker[1] == c) & (worker[2] == z))
    layer = [
        (flip(y, dy), flip(c, dc), z, flip(x, dx)) for dy in (0, 1) for dc in (0, 1) for dx in (0, 1) if dy + dc + dx
    ]
    barrier = pltpu.get_barrier_semaphore()
    for peer in layer:
        pl.semaphore_signal(barrier, inc=1, device_id=peer, device_id_type=MESH_ID)

    @pl.when(moves)
    def _():
        pl.semaphore_signal(barrier, inc=1, device_id=owner, device_id_type=MESH_ID)
        pl.semaphore_signal(barrier, inc=1, device_id=worker, device_id_type=MESH_ID)

    @pl.when(z > 0)
    def _():
        pl.semaphore_signal(barrier, inc=1, device_id=(y, c, z - 1, x), device_id_type=MESH_ID)

    @pl.when(z < last)
    def _():
        pl.semaphore_signal(barrier, inc=1, device_id=(y, c, z + 1, x), device_id_type=MESH_ID)

    pl.semaphore_wait(barrier, len(layer) + 2 * moves.astype(jnp.int32) + (z > 0).astype(jnp.int32) + (z < last).astype(jnp.int32))

    shard, width = w_query.shape
    owned = width // 8
    trades = [
        remote(
            x_own.at[half],
            x_whole.at[place_of(worker[0], worker[1], worker[3], half)],
            trade_send.at[half],
            trade_recv.at[half],
            worker,
        )
        for half in (0, 1)
    ]
    keeps = [
        pltpu.make_async_copy(x_own.at[half], x_whole.at[place_of(y, c, x, half)], trade_recv.at[half]) for half in (0, 1)
    ]

    @pl.when(moves)
    def _():
        for copy in trades:
            copy.start()

    @pl.when(jnp.logical_not(moves))
    def _():
        for copy in keeps:
            copy.start()

    spread, kept = [], []
    for m, source in enumerate((w_query, w_key, w_value)):
        dst = w_qkv.at[row, z, pl.ds(pl.multiple_of(x * shard, shard), shard), pl.ds(m * owned, owned)]
        for k, peer in enumerate(layer):
            columns = pl.ds(pl.multiple_of((4 * peer[0] + 2 * peer[1] + peer[3]) * owned, owned), owned)
            spread.append(remote(source.at[:, columns], dst, w_send.at[m, k], w_recv.at[m, k], peer))
        columns = pl.ds(pl.multiple_of((4 * y + 2 * c + x) * owned, owned), owned)
        kept.append(pltpu.make_async_copy(source.at[:, columns], dst, local.at[m]))
    for copy in spread + kept:
        copy.start()

    gather = Gather(lambda half: x_whole.at[place_of(y, c, x, half)], x_whole, gather_send, gather_recv)
    for half in (0, 1):

        @pl.when(moves)
        def _():
            trades[half].wait_recv()

        @pl.when(jnp.logical_not(moves))
        def _():
            keeps[half].wait()

        gather.start(half)

    for copy in kept:
        copy.wait()
    for copy in spread:
        copy.wait_recv()

    def up(h):
        slab = w_qkv.at[:, z - h]
        return remote(slab, slab, up_send.at[h], up_recv.at[h], (y, c, z + 1, x))

    def down(h):
        slab = w_qkv.at[:, z + h]
        return remote(slab, slab, down_send.at[h], down_recv.at[h], (y, c, z - 1, x))

    def arrive(h):
        @pl.when(z - h - 1 >= 0)
        def _():
            slab = w_qkv.at[:, z - h - 1]
            remote(slab, slab, up_send.at[h], up_recv.at[h], (y, c, z, x)).wait_recv()
            if h < 2:

                @pl.when(z < last)
                def _():
                    up(h + 1).start()

        @pl.when(z + h + 1 <= last)
        def _():
            slab = w_qkv.at[:, z + h + 1]
            remote(slab, slab, down_send.at[h], down_recv.at[h], (y, c, z, x)).wait_recv()
            if h < 2:

                @pl.when(z > 0)
                def _():
                    down(h + 1).start()

    @pl.when(z < last)
    def _():
        up(0).start()

    @pl.when(z > 0)
    def _():
        down(0).start()

    gather.pass_first()
    arrive(0)
    gather.pass_second()
    arrive(1)
    gather.pass_far()
    arrive(2)
    gather.finish()

    @pl.when(moves)
    def _():
        for copy in trades:
            copy.wait_send()

    for copy in spread:
        copy.wait_send()
    for h in range(3):

        @pl.when((z < last) & (z - h >= 0))
        def _():
            up(h).wait_send()

        @pl.when((z > 0) & (z + h <= last))
        def _():
            down(h).wait_send()


def anywhere():
    return pl.BlockSpec(memory_space=pl.ANY)


def in_vmem():
    return pl.BlockSpec(memory_space=pltpu.VMEM)


def dma(*shape):
    return pltpu.SemaphoreType.DMA(shape)


def remote_params(number):
    return pltpu.CompilerParams(collective_id=number, has_side_effects=True, vmem_limit_bytes=VMEM_LIMIT)


def begin(x_own, w_query, w_key, w_value):
    block, width = x_own.shape
    shard = w_query.shape[0]
    x_whole, w_qkv = pl.pallas_call(
        begin_kernel,
        out_shape=(
            jax.ShapeDtypeStruct((8 * block, width), LOW),
            jax.ShapeDtypeStruct((4, 4, 2 * shard, 3 * width // 8), LOW),
        ),
        in_specs=[anywhere()] * 4,
        out_specs=[anywhere()] * 2,
        scratch_shapes=[
            dma(2), dma(2), dma(GATHER_COPIES), dma(GATHER_COPIES), dma(3, 7), dma(3, 7), dma(3), dma(3), dma(3), dma(3), dma(3),
        ],
        compiler_params=remote_params(1),
        cost_estimate=pl.CostEstimate(flops=0, bytes_accessed=300_000_000, transcendentals=0),
    )(x_own.reshape(2, block // 2, width), w_query, w_key, w_value)
    return x_whole, w_qkv.reshape(width, 3 * width // 8)


def summed(total, landed, here):
    parts = (total[3, here, :], landed[0, here, :], landed[1, here, :])
    return sum(part.astype(jnp.float32) for part in parts)


def over_chunks(work):
    def step(i, carry):
        work(pl.ds(pl.multiple_of(i * CHUNK, CHUNK), CHUNK))
        return carry

    lax.fori_loop(0, TILE // CHUNK, step, 0)


def inverse_of(value):
    return lax.rsqrt(jnp.mean(value * value, axis=-1, keepdims=True) + EPSILON)


def close_attention_kernel(attended, w_out, x_own, gain, resid, normed, own, *scratch):
    scatter, (send, recv, local) = scratch[:7], scratch[7:]
    width = w_out.shape[1]
    greet(near())

    def produce(turn, y, c, x, out):
        at = place_of(y, c, x)

        def step(i, carry):
            columns = pl.ds(pl.multiple_of(i * TILE, TILE), TILE)
            out[:, columns] = dot_wide(attended[at, :], w_out[:, columns]).astype(LOW)
            return carry

        lax.fori_loop(0, width // TILE, step, 0)

    run_scatter(produce, *scatter)
    total, landed = scatter[2], scatter[4]

    def chunk(here):
        value = x_own[here, :].astype(jnp.float32) + summed(total, landed, here)
        resid[here, :] = value
        own[here, :] = (value * inverse_of(value) * gain[...]).astype(LOW)

    over_chunks(chunk)
    run_gather(own, normed, send, recv, local.at[0])


def close_attention(attended, w_out, x_own, gain):
    block, width = x_own.shape
    return pl.pallas_call(
        close_attention_kernel,
        out_shape=(
            jax.ShapeDtypeStruct((block, width), jnp.float32),
            jax.ShapeDtypeStruct((8 * block, width), LOW),
        ),
        in_specs=[in_vmem()] * 4,
        out_specs=[in_vmem(), anywhere()],
        scratch_shapes=[pltpu.VMEM((block, width), LOW)]
        + scatter_scratch(width)
        + [dma(GATHER_COPIES), dma(GATHER_COPIES), dma(1)],
        compiler_params=remote_params(2),
        cost_estimate=pl.CostEstimate(flops=0, bytes_accessed=450_000_000, transcendentals=0),
    )(attended, w_out, x_own, gain)


def norm_back(value, gain, upstream):
    inverse = inverse_of(value)
    scaled = upstream * gain
    inner = jnp.mean(scaled * value, axis=-1, keepdims=True)
    return inverse * scaled - value * (inverse * inverse * inverse) * inner, upstream * value * inverse


def fold_rows(total, terms):
    for first in range(0, CHUNK, 8):
        total[...] += terms[first : first + 8, :]


def close_mlp_kernel(d_gate, d_up, w_gate, w_up, resid, upstream, gain, d_resid, gain_term, d_resid_whole, own, blocks, *scratch):
    scatter, (send, recv, local, fetched) = scratch[:7], scratch[7:]
    y, c, z, x = spot()
    width = w_gate.shape[0]
    order = [(r, k, q) for r, q in ((1 - y, 1 - x), (y, 1 - x), (1 - y, x), (y, x)) for k in (1 - c, c)]

    def fetch(turn):
        at = place_of(*order[turn])
        slot = turn % 2
        return [
            pltpu.make_async_copy(source.at[at], blocks.at[slot, m], fetched.at[slot, m])
            for m, source in enumerate((d_gate, d_up))
        ]

    for copy in fetch(0):
        copy.start()
    greet(near())

    def produce(turn, to_y, to_c, to_x, out):
        if turn < 7:
            for copy in fetch(turn + 1):
                copy.start()
        for copy in fetch(turn):
            copy.wait()

        def step(i, carry):
            columns = pl.ds(pl.multiple_of(i * TILE, TILE), TILE)
            part = dot_nt(blocks[turn % 2, 0], w_gate[columns, :]) + dot_nt(blocks[turn % 2, 1], w_up[columns, :])
            out[:, columns] = part.astype(LOW)
            return carry

        lax.fori_loop(0, width // TILE, step, 0)

    run_scatter(produce, *scatter)
    total, landed = scatter[2], scatter[4]
    gain_term[...] = jnp.zeros_like(gain_term)

    def chunk(here):
        back, terms = norm_back(resid[here, :], gain[...], summed(total, landed, here))
        value = upstream[here, :].astype(jnp.float32) + back
        d_resid[here, :] = value
        own[here, :] = value.astype(LOW)
        fold_rows(gain_term, terms)

    over_chunks(chunk)
    run_gather(own, d_resid_whole, send, recv, local.at[0])


def close_mlp(d_gate, d_up, w_gate, w_up, resid, upstream, gain):
    block, width = resid.shape
    hidden = d_gate.shape[1]
    return pl.pallas_call(
        close_mlp_kernel,
        out_shape=(
            jax.ShapeDtypeStruct((block, width), jnp.float32),
            jax.ShapeDtypeStruct((8, width), jnp.float32),
            jax.ShapeDtypeStruct((8 * block, width), LOW),
        ),
        in_specs=[anywhere()] * 2 + [in_vmem()] * 5,
        out_specs=[in_vmem(), in_vmem(), anywhere()],
        scratch_shapes=[pltpu.VMEM((block, width), LOW), pltpu.VMEM((2, 2, block, hidden), LOW)]
        + scatter_scratch(width)
        + [dma(GATHER_COPIES), dma(GATHER_COPIES), dma(1), dma(2, 2)],
        compiler_params=remote_params(3),
        cost_estimate=pl.CostEstimate(flops=0, bytes_accessed=450_000_000, transcendentals=0),
    )(d_gate, d_up, w_gate, w_up, resid, upstream, gain)


def close_layer_kernel(d_qkv, w_qkv, x_own, d_resid, gain, grad_low, gain_term, own, *scratch):
    scatter, (send, recv) = scratch[:7], scratch[7:]
    y, c, z, x = spot()
    worker, owner = worker_of(y, c, z, x), owner_of(y, c, z, x)
    moves = jnp.logical_not((worker[0] == y) & (worker[1] == c) & (worker[2] == z))
    width = w_qkv.shape[0]
    barrier = pltpu.get_barrier_semaphore()

    @pl.when(moves)
    def _():
        pl.semaphore_signal(barrier, inc=1, device_id=owner, device_id_type=MESH_ID)
        pl.semaphore_signal(barrier, inc=1, device_id=worker, device_id_type=MESH_ID)

    for peer in near():
        pl.semaphore_signal(barrier, inc=1, device_id=peer, device_id_type=MESH_ID)
    pl.semaphore_wait(barrier, 3 + 2 * moves.astype(jnp.int32))

    def produce(turn, to_y, to_c, to_x, out):
        at = place_of(to_y, to_c, to_x)

        def step(i, carry):
            columns = pl.ds(pl.multiple_of(i * TILE, TILE), TILE)
            out[:, columns] = dot_nt(d_qkv[at, :], w_qkv[columns, :]).astype(LOW)
            return carry

        lax.fori_loop(0, width // TILE, step, 0)

    run_scatter(produce, *scatter)
    total, landed = scatter[2], scatter[4]
    gain_term[...] = jnp.zeros_like(gain_term)
    trades = [
        remote(own.at[pl.ds(half * HALF, HALF)], grad_low.at[pl.ds(half * HALF, HALF)], send.at[half], recv.at[half], owner)
        for half in (0, 1)
    ]
    keeps = [
        pltpu.make_async_copy(own.at[pl.ds(half * HALF, HALF)], grad_low.at[pl.ds(half * HALF, HALF)], recv.at[half])
        for half in (0, 1)
    ]
    for half in (0, 1):

        def step(i, carry):
            here = pl.ds(pl.multiple_of(half * HALF + i * CHUNK, CHUNK), CHUNK)
            back, terms = norm_back(x_own[here, :].astype(jnp.float32), gain[...], summed(total, landed, here))
            own[here, :] = (d_resid[here, :] + back).astype(LOW)
            fold_rows(gain_term, terms)
            return carry

        lax.fori_loop(0, HALF // CHUNK, step, 0)

        @pl.when(moves)
        def _():
            trades[half].start()

        @pl.when(jnp.logical_not(moves))
        def _():
            keeps[half].start()

    @pl.when(moves)
    def _():
        for copy in trades:
            copy.wait()

    @pl.when(jnp.logical_not(moves))
    def _():
        for copy in keeps:
            copy.wait()


def close_layer(d_qkv, w_qkv, x_own, d_resid, gain):
    block, width = x_own.shape
    return pl.pallas_call(
        close_layer_kernel,
        out_shape=(jax.ShapeDtypeStruct((block, width), LOW), jax.ShapeDtypeStruct((8, width), jnp.float32)),
        in_specs=[in_vmem()] * 5,
        out_specs=[anywhere(), in_vmem()],
        scratch_shapes=[pltpu.VMEM((block, width), LOW)] + scatter_scratch(width) + [dma(2), dma(2)],
        compiler_params=remote_params(4),
        cost_estimate=pl.CostEstimate(flops=0, bytes_accessed=350_000_000, transcendentals=0),
    )(d_qkv, w_qkv, x_own, d_resid, gain)


LAYER = ("y", "c", "x")
ALL = ("y", "c", "z", "x")


def gather_layer(part):
    return lax.all_gather(part, LAYER, axis=0, tiled=True)


def scatter_layer(whole):
    return lax.psum_scatter(whole.astype(LOW), LAYER, scatter_dimension=0, tiled=True).astype(jnp.float32)


def trade(part, back=False):
    pairs = []
    for y in range(2):
        for c in range(2):
            for z in range(4):
                for x in range(2):
                    owner = ((y * 2 + c) * 4 + z) * 2 + x
                    worker = ((((z + c) % 2) * 2 + z // 2) * 4 + 2 * y + c) * 2 + x
                    pairs.append((worker, owner) if back else (owner, worker))
    return lax.ppermute(part, ALL, pairs)


def body_layers(
    tokens, lengths, cotangent, w_query, w_key, w_value, w_out, w_gate, w_up, w_down, gain_attn, gain_mlp
):
    rows_here, block, width = tokens.shape
    members = lax.axis_size(LAYER)
    layers = lax.axis_size("z")
    shard = w_query.shape[0]
    owned = width // members
    parity = (lax.axis_index("z") % 2).astype(jnp.int32)
    ends = jnp.concatenate((jnp.cumsum(trade(lengths)[0]), parity[None]))
    layer_x, w_qkv = begin(tokens.reshape(block, width), w_query, w_key, w_value)
    place = (4 * lax.axis_index("y") + 2 * lax.axis_index("c") + lax.axis_index("x")) * block
    x_own = lax.dynamic_slice_in_dim(layer_x, place, block, 0)
    full_gain_attn, full_gain_mlp = (
        lax.all_gather(gain, ALL, axis=0, tiled=True).astype(jnp.float32)[None] for gain in (gain_attn, gain_mlp)
    )
    layer_normed = norm_forward(layer_x.astype(jnp.float32), full_gain_attn)[0].astype(LOW)
    out_rows = lax.all_gather(w_out, ("z", "x"), axis=0, tiled=True)
    w_out_own = lax.dynamic_slice_in_dim(out_rows, lax.axis_index("x") * owned, owned, 0)

    qkv = dot_wide(layer_normed, w_qkv).astype(LOW)
    attended = attend(ends, qkv)
    resid, layer_mlp = close_attention(attended, w_out_own, x_own, full_gain_mlp)

    own_gate = lax.all_gather(w_gate, "z", axis=1, tiled=True)
    own_up = lax.all_gather(w_up, "z", axis=1, tiled=True)
    own_down = lax.all_gather(w_down, "z", axis=0, tiled=True)
    upstream = trade(cotangent).reshape(block, width)
    layer_upstream = gather_layer(upstream)
    gate = dot_wide(layer_mlp, own_gate)
    up_part = dot_wide(layer_mlp, own_up)
    sigmoid_gate = jax.nn.sigmoid(gate)
    hidden = (gate * sigmoid_gate * up_part).astype(LOW)
    result = resid + scatter_layer(dot_wide(hidden, own_down))
    mixed = trade(result.astype(LOW).reshape(rows_here, block, width), back=True)
    d_hidden = contract_cols(layer_upstream, own_down)
    d_gate, d_up = gate_backward(d_hidden, gate, up_part, sigmoid_gate)
    d_resid, gain_mlp_term, layer_d_resid = close_mlp(d_gate, d_up, own_gate, own_up, resid, upstream, full_gain_mlp)

    def scatter_layers(whole, axis):
        return lax.psum_scatter(whole.astype(LOW), "z", scatter_dimension=axis, tiled=True).astype(jnp.float32)

    grad_gate = scatter_layers(contract_rows(layer_mlp, d_gate), 1)
    grad_up = scatter_layers(contract_rows(layer_mlp, d_up), 1)
    grad_down = scatter_layers(contract_rows(hidden, layer_upstream), 0)

    d_attended = contract_cols(layer_d_resid, w_out_own).astype(LOW)
    d_qkv = attend_back(ends, qkv, d_attended)
    grad_low, gain_attn_term = close_layer(d_qkv, w_qkv, x_own, d_resid, full_gain_attn)
    grad_tokens = grad_low.astype(jnp.float32).reshape(rows_here, block, width)

    out_term = contract_rows(attended, layer_d_resid)
    qkv_term = contract_rows(layer_normed, d_qkv)
    out_term = lax.dynamic_update_slice_in_dim(
        jnp.zeros((2 * owned, width), LOW), out_term.astype(LOW), lax.axis_index("x") * owned, 0
    )
    grad_out = lax.psum_scatter(out_term, ("z", "x"), scatter_dimension=0, tiled=True).astype(jnp.float32)
    qkv_term = qkv_term.reshape(4, layers, 2 * shard, 3 * owned).transpose(1, 0, 2, 3)
    qkv_term = qkv_term.reshape(layers * members * shard, 3 * owned)
    qkv_term = lax.psum_scatter(qkv_term.astype(LOW), "z", scatter_dimension=0, tiled=True)
    qkv_term = lax.all_to_all(qkv_term.reshape(members, shard, 3 * owned), LAYER, 0, 0)
    qkv_term = qkv_term.reshape(members, shard, 3, owned).transpose(2, 1, 0, 3).astype(jnp.float32)
    grad_query, grad_key, grad_value = qkv_term.reshape(3, shard, width)
    grad_gain_attn, grad_gain_mlp = (
        lax.psum_scatter(jnp.sum(term, axis=0), ALL, scatter_dimension=0, tiled=True)
        for term in (gain_attn_term, gain_mlp_term)
    )
    return (
        mixed,
        grad_tokens,
        grad_query,
        grad_key,
        grad_value,
        grad_out,
        grad_gate,
        grad_up,
        grad_down,
        grad_gain_attn,
        grad_gain_mlp,
    )


def body_any(
    tokens,
    lengths,
    cotangent,
    w_query,
    w_key,
    w_value,
    w_out,
    w_gate,
    w_up,
    w_down,
    gain_attn,
    gain_mlp,
):
    rows_here, block, width = tokens.shape
    count = rows_here * block
    scale = 1.0 / math.sqrt(HD)
    kv_place = lax.axis_index("kv")
    key_places = kv_place * block + jnp.arange(block, dtype=jnp.int32)
    attn_set = (
        lax.all_gather(w_query, ("row", "kv"), axis=0, tiled=True),
        lax.all_gather(w_key, ("row", "kv"), axis=0, tiled=True),
        lax.all_gather(w_value, ("row", "kv"), axis=0, tiled=True),
        lax.all_gather(w_out, ("row", "kv"), axis=0, tiled=True),
        lax.all_gather(gain_attn, ("row", "kv"), axis=0, tiled=True),
        lax.all_gather(gain_mlp, ("row", "kv"), axis=0, tiled=True),
    )
    full_query, full_key, full_value, full_out, full_gain_attn, full_gain_mlp = attn_set
    flat = tokens.reshape(count, width).astype(jnp.float32)
    normed_attn, inverse_attn = norm_forward(flat, full_gain_attn)
    normed_attn_low = normed_attn.astype(jnp.bfloat16)
    query_low = jnp.dot(normed_attn_low, full_query, preferred_element_type=jnp.float32).astype(
        jnp.bfloat16
    )
    key_low = jnp.dot(normed_attn_low, full_key, preferred_element_type=jnp.float32).astype(
        jnp.bfloat16
    )
    value_low = jnp.dot(normed_attn_low, full_value, preferred_element_type=jnp.float32).astype(
        jnp.bfloat16
    )
    key_heads = key_low.reshape(rows_here, block, H, HD)
    value_heads = value_low.reshape(rows_here, block, H, HD)
    segment, valid = segment_table(lengths)
    key_segment = lax.dynamic_slice_in_dim(segment, kv_place * block, block, 1)
    key_valid = lax.dynamic_slice_in_dim(valid, kv_place * block, block, 1)
    queries_all = lax.all_gather(
        query_low.reshape(rows_here, block, width), "kv", axis=1, tiled=True
    )
    which = 0
    query_rows = queries_all[which]
    query_segment = segment[which]
    sigmoid_part, allowed = score_block(
        query_rows,
        key_heads[which],
        query_segment,
        key_segment[which],
        key_valid[which],
        jnp.int32(0),
        key_places,
    )
    weight = (sigmoid_part * allowed).astype(jnp.bfloat16)
    summed = jnp.einsum(
        "hqk,khd->qhd", weight, value_heads[which], preferred_element_type=jnp.float32
    )
    pieces = [
        lax.psum_scatter(
            summed.reshape(lax.axis_size("kv") * block, width).astype(jnp.bfloat16),
            "kv",
            scatter_dimension=0,
            tiled=True,
        ).astype(jnp.float32)
    ]
    attended_low = jnp.stack(pieces).reshape(count, width).astype(jnp.bfloat16)
    resid = flat + jnp.dot(attended_low, full_out, preferred_element_type=jnp.float32)
    normed_mlp, inverse_mlp = norm_forward(resid, full_gain_mlp)
    normed_mlp_low = normed_mlp.astype(jnp.bfloat16)
    upstream_low = cotangent.reshape(count, width)
    upstream = upstream_low.astype(jnp.float32)
    slice_gate, slice_up, slice_down = (
        lax.all_gather(w_gate, "row", axis=1, tiled=True),
        lax.all_gather(w_up, "row", axis=1, tiled=True),
        lax.all_gather(w_down, "row", axis=0, tiled=True),
    )
    row_normed, row_upstream = (
        lax.all_gather(normed_mlp_low.reshape(rows_here, block, width), "kv", axis=1, tiled=True),
        lax.all_gather(cotangent, "kv", axis=1, tiled=True),
    )
    normed_rows = row_normed.reshape(rows_here * LEN, width)
    upstream_rows = row_upstream.reshape(rows_here * LEN, width)
    gate = jnp.dot(normed_rows, slice_gate, preferred_element_type=jnp.float32)
    up_part = jnp.dot(normed_rows, slice_up, preferred_element_type=jnp.float32)
    sigmoid_gate = jax.nn.sigmoid(gate)
    hidden_low = (gate * sigmoid_gate * up_part).astype(jnp.bfloat16)
    hidden_rows = hidden_low.reshape(rows_here, LEN, hidden_low.shape[1])
    which = 0
    hidden_part = hidden_rows[which]
    outputs = [
        lax.psum_scatter(
            jnp.dot(hidden_part, slice_down, preferred_element_type=jnp.float32).astype(
                jnp.bfloat16
            ),
            "kv",
            scatter_dimension=0,
            tiled=True,
        ).astype(jnp.float32)
    ]
    result = resid + jnp.stack(outputs).reshape(count, width)
    d_hidden = contract_cols(upstream_rows, slice_down)
    d_gate, d_up = gate_backward(d_hidden, gate, up_part, sigmoid_gate)
    partial_normed = contract_cols(d_gate, slice_gate) + contract_cols(d_up, slice_up)
    d_normed_mlp = (
        lax.psum_scatter(
            partial_normed.reshape(rows_here, LEN, width).astype(jnp.bfloat16),
            "kv",
            scatter_dimension=1,
            tiled=True,
        )
        .astype(jnp.float32)
        .reshape(count, width)
    )
    grad_gate, grad_up, grad_down = (
        lax.psum_scatter(
            contract_rows(normed_rows, d_gate).astype(jnp.bfloat16),
            "row",
            scatter_dimension=1,
            tiled=True,
        ).astype(jnp.float32),
        lax.psum_scatter(
            contract_rows(normed_rows, d_up).astype(jnp.bfloat16),
            "row",
            scatter_dimension=1,
            tiled=True,
        ).astype(jnp.float32),
        lax.psum_scatter(
            contract_rows(hidden_low, upstream_rows).astype(jnp.bfloat16),
            "row",
            scatter_dimension=0,
            tiled=True,
        ).astype(jnp.float32),
    )
    mixed = result.astype(jnp.bfloat16).reshape(rows_here, block, width)
    back_mlp, gain_mlp_term = norm_backward(resid, inverse_mlp, full_gain_mlp, d_normed_mlp)
    d_resid = upstream + back_mlp
    d_resid_low = d_resid.astype(jnp.bfloat16)
    d_attended = contract_cols(d_resid_low, full_out).astype(jnp.bfloat16)
    grads_all = lax.all_gather(
        d_attended.reshape(rows_here, block, width), "kv", axis=1, tiled=True
    )
    query_block = min(512, LEN)
    block_count = LEN // query_block
    which = 0

    def sweep(carry, index, which=which):
        key_total, value_total = carry
        start = index * query_block
        query_rows = lax.dynamic_slice_in_dim(queries_all[which], start, query_block, 0)
        grad_rows = lax.dynamic_slice_in_dim(grads_all[which], start, query_block, 0)
        query_segment = lax.dynamic_slice_in_dim(segment[which], start, query_block, 0)
        sigmoid_part, allowed = score_block(
            query_rows,
            key_heads[which],
            query_segment,
            key_segment[which],
            key_valid[which],
            start,
            key_places,
        )
        weight = (sigmoid_part * allowed).astype(jnp.bfloat16)
        grad_heads = grad_rows.reshape(query_block, H, HD)
        value_total = value_total + jnp.einsum(
            "hqk,qhd->khd", weight, grad_heads, preferred_element_type=jnp.float32
        )
        d_weight = jnp.einsum(
            "qhd,khd->hqk", grad_heads, value_heads[which], preferred_element_type=jnp.float32
        )
        d_score = (d_weight * sigmoid_part * (1.0 - sigmoid_part) * allowed).astype(jnp.bfloat16)
        query_part = (
            jnp.einsum(
                "hqk,khd->qhd", d_score, key_heads[which], preferred_element_type=jnp.float32
            )
            * scale
        )
        key_total = (
            key_total
            + jnp.einsum(
                "hqk,qhd->khd",
                d_score,
                query_rows.reshape(query_block, H, HD),
                preferred_element_type=jnp.float32,
            )
            * scale
        )
        return ((key_total, value_total), query_part.reshape(query_block, width))

    zeros = jnp.zeros((block, H, HD), jnp.float32)
    totals, query_parts = lax.scan(sweep, (zeros, zeros), jnp.arange(block_count, dtype=jnp.int32))
    query_terms = [query_parts.reshape(LEN, width)]
    key_grads = [totals[0].reshape(block, width)]
    value_grads = [totals[1].reshape(block, width)]
    query_local = lax.psum_scatter(
        jnp.stack(query_terms).astype(jnp.bfloat16), "kv", scatter_dimension=1, tiled=True
    ).astype(jnp.float32)
    d_query_low = query_local.reshape(count, width).astype(jnp.bfloat16)
    d_key_low = jnp.stack(key_grads).reshape(count, width).astype(jnp.bfloat16)
    d_value_low = jnp.stack(value_grads).reshape(count, width).astype(jnp.bfloat16)
    d_normed_attn = (
        contract_cols(d_query_low, full_query)
        + contract_cols(d_key_low, full_key)
        + contract_cols(d_value_low, full_value)
    )
    back_attn, gain_attn_term = norm_backward(flat, inverse_attn, full_gain_attn, d_normed_attn)
    grad_tokens = (d_resid + back_attn).reshape(rows_here, block, width)
    projected_low = jnp.concatenate((d_query_low, d_key_low, d_value_low), axis=1)
    grad_projections = lax.psum_scatter(
        contract_rows(normed_attn_low, projected_low),
        ("row", "kv"),
        scatter_dimension=0,
        tiled=True,
    )
    out_term = contract_rows(attended_low, d_resid_low)
    grad_out, grad_gain_attn, grad_gain_mlp = (
        lax.psum_scatter(out_term, ("row", "kv"), scatter_dimension=0, tiled=True),
        lax.psum_scatter(gain_attn_term, ("row", "kv"), scatter_dimension=0, tiled=True),
        lax.psum_scatter(gain_mlp_term, ("row", "kv"), scatter_dimension=0, tiled=True),
    )
    grad_query = grad_projections[:, :width]
    grad_key = grad_projections[:, width : 2 * width]
    grad_value = grad_projections[:, 2 * width :]
    return (
        mixed,
        grad_tokens,
        grad_query,
        grad_key,
        grad_value,
        grad_out,
        grad_gate,
        grad_up,
        grad_down,
        grad_gain_attn,
        grad_gain_mlp,
    )


def solution(mesh):
    rows, columns = mesh.shape["row"], mesh.shape["kv"]
    if rows == 4 and columns == 2 * rows:
        mesh = Mesh(mesh.devices.reshape(2, 2, rows, 2), ("y", "c", "z", "x"))
        row, kv, run = ("y", "c"), ("z", "x"), body_layers
    else:
        row, kv, run = "row", "kv", body_any
    both = ("y", "c", "z", "x") if run is body_layers else ("row", "kv")
    tall, wide, flat = P(both, None), P(None, both), P(both)
    tokens = P(row, kv, None)
    return jax.shard_map(
        run,
        mesh=mesh,
        in_specs=(tokens, P(row, None), tokens, tall, tall, tall, tall, wide, wide, tall, flat, flat),
        out_specs=(tokens, tokens, tall, tall, tall, tall, wide, wide, tall, flat, flat),
        check_vma=False,
    )
```

```python
import functools
import math

import jax
import jax.numpy as jnp
from jax import lax
from jax.experimental import pallas as pl
from jax.experimental.pallas import tpu as pltpu
from jax.sharding import Mesh, PartitionSpec as P

H = 16
HD = 128
LEN = 4096


EPSILON = 1e-05


def contract_rows(left, right):
    return lax.dot_general(
        left, right, (((0,), (0,)), ((), ())), preferred_element_type=jnp.float32
    )


def contract_cols(left, right):
    return lax.dot_general(
        left, right, (((1,), (1,)), ((), ())), preferred_element_type=jnp.float32
    )


def norm_forward(value, gain):
    inverse = lax.rsqrt(jnp.mean(value * value, axis=-1, keepdims=True) + EPSILON)
    return (value * inverse * gain.astype(jnp.float32), inverse)


def norm_backward(value, inverse, gain, upstream):
    scaled = upstream * gain.astype(jnp.float32)
    inner = jnp.mean(scaled * value, axis=-1, keepdims=True)
    back = inverse * scaled - value * (inverse * inverse * inverse) * inner
    gain_term = jnp.sum(upstream * value * inverse, axis=0)
    return (back, gain_term)


def segment_table(lengths):
    ends = jnp.cumsum(lengths, axis=-1)
    places = jnp.arange(LEN, dtype=jnp.int32)
    segment = jnp.sum((ends[:, None, :] <= places[None, :, None]).astype(jnp.int32), axis=-1)
    valid = places[None, :] < ends[:, -1:]
    return (segment, valid)


def score_block(
    query_rows, key_heads, query_segment, key_segment, key_valid, query_start, key_places
):
    count = query_rows.shape[0]
    query_heads = query_rows.reshape(count, H, HD)
    raw = jnp.einsum("qhd,khd->hqk", query_heads, key_heads, preferred_element_type=jnp.float32)
    scores = raw * (1.0 / math.sqrt(HD)) - math.log(LEN)
    places = query_start + jnp.arange(count, dtype=jnp.int32)
    allowed = (
        (key_places[None, :] <= places[:, None])
        & (key_segment[None, :] == query_segment[:, None])
        & key_valid[None, :]
    )
    return (jax.nn.sigmoid(scores), allowed.astype(jnp.float32)[None])


def gate_backward(d_hidden, gate, up_part, sigmoid_gate):
    d_gate = (d_hidden * up_part * sigmoid_gate * (1.0 + gate * (1.0 - sigmoid_gate))).astype(
        jnp.bfloat16
    )
    d_up = (d_hidden * gate * sigmoid_gate).astype(jnp.bfloat16)
    return (d_gate, d_up)


TILE = 512
LOW = jnp.bfloat16
VMEM_LIMIT = 60 * 1024 * 1024


def doc_start(ends, place):
    start = jnp.zeros_like(place)
    for k in range(8):
        start = jnp.where(ends[k] <= place, ends[k], start)
    return jnp.where(place < ends[7], start, LEN)


def doc_end(ends, place):
    end = ends[7]
    for k in range(6, -1, -1):
        end = jnp.where(ends[k] > place, ends[k], end)
    return end


def sigmoid_of(raw):
    return pl.reciprocal(1.0 + jnp.exp2(math.log2(LEN) - raw * (math.log2(math.e) / math.sqrt(HD))), approx=True)


def dot_nt(left, right):
    return lax.dot_general(left, right, (((1,), (1,)), ((), ())), preferred_element_type=jnp.float32)


def rows_of(ends, block):
    z, x = block // 2, block % 2
    return pl.ds(pl.multiple_of((4 * ((z + ends[8]) % 2) + 2 * (z // 2) + x) * TILE, TILE), TILE)


def attend_kernel(ends, qkv, out, total):
    head, i = pl.program_id(0), pl.program_id(1)
    column = pl.multiple_of(head * HD, HD)
    width = qkv.shape[1] // 3
    first = i * TILE
    query = qkv[rows_of(ends, i), pl.ds(column, HD)]
    total[...] = jnp.zeros_like(total)
    begin = jnp.minimum(doc_start(ends, first), first) // TILE
    latest = doc_start(ends, first + TILE - 1)

    def step(j, carry):
        here = rows_of(ends, j)
        key = qkv[here, pl.ds(pl.multiple_of(column + width, HD), HD)]
        value = qkv[here, pl.ds(pl.multiple_of(column + 2 * width, HD), HD)]
        plain = (j < i) & (j * TILE >= latest)

        @pl.when(plain)
        def _():
            weight = sigmoid_of(dot_nt(query, key)).astype(LOW)
            total[...] += jnp.dot(weight, value, preferred_element_type=jnp.float32)

        @pl.when(jnp.logical_not(plain))
        def _():
            q_place = first + lax.broadcasted_iota(jnp.int32, (TILE, 1), 0)
            k_place = j * TILE + lax.broadcasted_iota(jnp.int32, (1, TILE), 1)
            allowed = (k_place <= q_place) & (k_place >= doc_start(ends, q_place))
            weight = jnp.where(allowed, sigmoid_of(dot_nt(query, key)), 0.0).astype(LOW)
            total[...] += jnp.dot(weight, value, preferred_element_type=jnp.float32)

        return carry

    lax.fori_loop(begin, i + 1, step, 0)
    out[rows_of(ends, i), pl.ds(column, HD)] = total[...].astype(LOW)


def attend_back_kernel(ends, qkv, grads, out, query_total, key_total, value_total):
    head, j = pl.program_id(0), pl.program_id(1)
    column = pl.multiple_of(head * HD, HD)
    width = qkv.shape[1] // 3
    first = j * TILE
    here = rows_of(ends, j)
    key_column = pl.multiple_of(column + width, HD)
    value_column = pl.multiple_of(column + 2 * width, HD)
    key = qkv[here, pl.ds(key_column, HD)]
    value = qkv[here, pl.ds(value_column, HD)]
    key_turned = key.T
    key_total[...] = jnp.zeros_like(key_total)
    value_total[...] = jnp.zeros_like(value_total)

    @pl.when(j == 0)
    def _():
        query_total[...] = jnp.zeros_like(query_total)

    end = pl.cdiv(doc_end(ends, first + TILE - 1), TILE)

    def step(i, carry):
        there = rows_of(ends, i)
        turned = pl.ds(pl.multiple_of(i * TILE, TILE), TILE)
        query = qkv[there, pl.ds(column, HD)]
        grad = grads[there, pl.ds(column, HD)]
        plain = (j < i) & (first >= doc_start(ends, i * TILE + TILE - 1))

        def finish(sig):
            value_total[...] += jnp.dot(sig.astype(LOW), grad, preferred_element_type=jnp.float32)
            d_score = (dot_nt(value, grad) * (sig * (1.0 - sig))).astype(LOW)
            key_total[...] += jnp.dot(d_score, query, preferred_element_type=jnp.float32)
            query_total[:, turned] += jnp.dot(key_turned, d_score, preferred_element_type=jnp.float32)

        @pl.when(plain)
        def _():
            finish(sigmoid_of(dot_nt(key, query)))

        @pl.when(jnp.logical_not(plain))
        def _():
            q_place = i * TILE + lax.broadcasted_iota(jnp.int32, (1, TILE), 1)
            k_place = first + lax.broadcasted_iota(jnp.int32, (TILE, 1), 0)
            allowed = (k_place <= q_place) & (k_place >= doc_start(ends, q_place))
            finish(jnp.where(allowed, sigmoid_of(dot_nt(key, query)), 0.0))

        return carry

    lax.fori_loop(j, end, step, 0)
    scale = 1.0 / math.sqrt(HD)
    out[here, pl.ds(key_column, HD)] = (key_total[...] * scale).astype(LOW)
    out[here, pl.ds(value_column, HD)] = value_total[...].astype(LOW)

    @pl.when(j == pl.num_programs(1) - 1)
    def _():
        for t in range(LEN // TILE):
            out[rows_of(ends, t), pl.ds(column, HD)] = (
                (query_total[:, t * TILE : (t + 1) * TILE] * scale).T.astype(LOW)
            )


def attend(ends, qkv):
    places, width = qkv.shape
    heads = width // (3 * HD)
    return pl.pallas_call(
        attend_kernel,
        out_shape=jax.ShapeDtypeStruct((places, width // 3), LOW),
        grid_spec=pltpu.PrefetchScalarGridSpec(
            num_scalar_prefetch=1,
            grid=(heads, places // TILE),
            in_specs=[pl.BlockSpec((places, width), lambda h, i, ends: (0, 0))],
            out_specs=pl.BlockSpec((places, width // 3), lambda h, i, ends: (0, 0)),
            scratch_shapes=[pltpu.VMEM((TILE, HD), jnp.float32)],
        ),
        compiler_params=pltpu.CompilerParams(vmem_limit_bytes=VMEM_LIMIT),
        cost_estimate=pl.CostEstimate(
            flops=4 * heads * places * places * HD // 2, bytes_accessed=8 * places * width // 3, transcendentals=heads * places * places // 2
        ),
    )(ends, qkv)


def attend_back(ends, qkv, grads):
    places, width = qkv.shape
    heads = width // (3 * HD)
    whole = lambda columns: pl.BlockSpec((places, columns), lambda h, j, ends: (0, 0))
    return pl.pallas_call(
        attend_back_kernel,
        out_shape=jax.ShapeDtypeStruct((places, width), LOW),
        grid_spec=pltpu.PrefetchScalarGridSpec(
            num_scalar_prefetch=1,
            grid=(heads, places // TILE),
            in_specs=[whole(width), whole(width // 3)],
            out_specs=whole(width),
            scratch_shapes=[
                pltpu.VMEM((HD, places), jnp.float32),
                pltpu.VMEM((TILE, HD), jnp.float32),
                pltpu.VMEM((TILE, HD), jnp.float32),
            ],
        ),
        compiler_params=pltpu.CompilerParams(vmem_limit_bytes=VMEM_LIMIT),
        cost_estimate=pl.CostEstimate(
            flops=10 * heads * places * places * HD // 2, bytes_accessed=14 * places * width // 3, transcendentals=heads * places * places // 2
        ),
    )(ends, qkv, grads)


def dot_wide(left, right):
    return jnp.dot(left, right, preferred_element_type=jnp.float32)


HALF = TILE // 2
CHUNK = 32
MESH_ID = pl.DeviceIdType.MESH


def flip(bit, by):
    return bit + by - 2 * bit * by


def spot():
    return tuple(lax.axis_index(name) for name in ("y", "c", "z", "x"))


def near():
    y, c, z, x = spot()
    return (y, c, z, 1 - x), (1 - y, c, z, x), (y, 1 - c, z, x)


def worker_of(y, c, z, x):
    return lax.rem(z + c, 2), z // 2, 2 * y + c, x


def owner_of(y, c, z, x):
    row = lax.rem(z, 2)
    return z // 2, row, 2 * c + lax.rem(y + row, 2), x


def place_of(y, c, x, half=None):
    first = (4 * y + 2 * c + x) * TILE
    if half is None:
        return pl.ds(pl.multiple_of(first, TILE), TILE)
    return pl.ds(pl.multiple_of(first + half * HALF, HALF), HALF)


def remote(src, dst, send, recv, peer):
    return pltpu.make_async_remote_copy(
        src_ref=src, dst_ref=dst, send_sem=send, recv_sem=recv, device_id=peer, device_id_type=MESH_ID
    )


def greet(peers):
    barrier = pltpu.get_barrier_semaphore()
    for peer in peers:
        pl.semaphore_signal(barrier, inc=1, device_id=peer, device_id_type=MESH_ID)
    pl.semaphore_wait(barrier, len(peers))


class Gather:
    def __init__(self, own, whole, send, recv):
        y, c, z, x = spot()
        across_x, across_y, core = near()

        def from_own(k, half, peer):
            return remote(own(half), whole.at[place_of(y, c, x, half)], send.at[k], recv.at[k], peer)

        def passed(k, at, peer):
            return remote(whole.at[at], whole.at[at], send.at[k], recv.at[k], peer)

        self.mine = [
            [from_own(0, 0, across_x), from_own(1, 0, across_y), from_own(2, 0, core)],
            [from_own(3, 1, across_x), from_own(4, 1, across_y), from_own(5, 1, core)],
        ]
        held_x = [place_of(y, c, 1 - x, half) for half in (0, 1)]
        held_y = [place_of(1 - y, c, x, half) for half in (0, 1)]
        far = [place_of(1 - y, c, 1 - x, half) for half in (0, 1)]
        self.over_y, self.over_x = passed(6, held_x[0], across_y), passed(7, held_y[1], across_x)
        self.core_x = [passed(8 + half, held_x[half], core) for half in (0, 1)]
        self.core_y = [passed(10 + half, held_y[half], core) for half in (0, 1)]
        self.core_far = [passed(12 + half, far[half], core) for half in (0, 1)]

    def start(self, half):
        for copy in self.mine[half]:
            copy.start()

    def pass_first(self):
        self.mine[0][0].wait_recv()
        self.over_y.start()
        self.core_x[0].start()
        self.mine[0][1].wait_recv()
        self.core_y[0].start()

    def pass_second(self):
        self.mine[1][1].wait_recv()
        self.over_x.start()
        self.core_y[1].start()
        self.mine[1][0].wait_recv()
        self.core_x[1].start()

    def pass_far(self):
        self.over_y.wait_recv()
        self.core_far[0].start()
        self.over_x.wait_recv()
        self.core_far[1].start()

    def finish(self):
        from_core = [self.mine[0][2], self.mine[1][2]] + self.core_x + self.core_y + self.core_far
        for copy in from_core:
            copy.wait_recv()
        for copy in self.mine[0] + self.mine[1] + [self.over_y, self.over_x] + self.core_x + self.core_y + self.core_far:
            copy.wait_send()


GATHER_COPIES = 14


def run_gather(own, whole, send, recv, local, beside=lambda h: None):
    y, c, z, x = spot()
    keep = pltpu.make_async_copy(own, whole.at[place_of(y, c, x)], local)
    keep.start()
    gather = Gather(lambda half: own.at[pl.ds(half * HALF, HALF)], whole, send, recv)
    gather.start(0)
    gather.start(1)
    beside(0)
    gather.pass_first()
    gather.pass_second()
    beside(1)
    gather.pass_far()
    gather.finish()
    beside(2)
    keep.wait()


class Chain:
    def __init__(self, own, slab, sems, index):
        self.own, self.slab, self.sems, self.index = own, slab, sems, index
        self.last = lax.axis_size("z") - 1

    def move(self, which, h, source, layer, to):
        y, c, z, x = spot()
        return remote(
            source, self.slab(layer), self.sems[2 * which].at[self.index, h], self.sems[2 * which + 1].at[self.index, h], (y, c, to, x)
        )

    def up(self, h):
        z = lax.axis_index("z")
        return self.move(0, h, self.own if h == 0 else self.slab(z - h), z - h, z + 1)

    def down(self, h):
        z = lax.axis_index("z")
        return self.move(1, h, self.own if h == 0 else self.slab(z + h), z + h, z - 1)

    def start(self):
        z = lax.axis_index("z")

        @pl.when(z < self.last)
        def _():
            self.up(0).start()

        @pl.when(z > 0)
        def _():
            self.down(0).start()

    def arrive(self, h):
        z = lax.axis_index("z")

        @pl.when(z - h - 1 >= 0)
        def _():
            self.move(0, h, self.slab(z - h - 1), z - h - 1, z).wait_recv()
            if h < 2:

                @pl.when(z < self.last)
                def _():
                    self.up(h + 1).start()

        @pl.when(z + h + 1 <= self.last)
        def _():
            self.move(1, h, self.slab(z + h + 1), z + h + 1, z).wait_recv()
            if h < 2:

                @pl.when(z > 0)
                def _():
                    self.down(h + 1).start()

    def finish(self):
        z = lax.axis_index("z")
        for h in range(3):

            @pl.when((z < self.last) & (z - h >= 0))
            def _():
                self.up(h).wait_send()

            @pl.when((z > 0) & (z + h <= self.last))
            def _():
                self.down(h).wait_send()


def chain_sems(count):
    return [pltpu.SemaphoreType.DMA((count, 3)) for _ in range(4)]


def greet_neighbours(peers):
    y, c, z, x = spot()
    last = lax.axis_size("z") - 1
    barrier = pltpu.get_barrier_semaphore()
    for peer in peers:
        pl.semaphore_signal(barrier, inc=1, device_id=peer, device_id_type=MESH_ID)

    @pl.when(z > 0)
    def _():
        pl.semaphore_signal(barrier, inc=1, device_id=(y, c, z - 1, x), device_id_type=MESH_ID)

    @pl.when(z < last)
    def _():
        pl.semaphore_signal(barrier, inc=1, device_id=(y, c, z + 1, x), device_id_type=MESH_ID)

    return barrier, len(peers) + (z > 0).astype(jnp.int32) + (z < last).astype(jnp.int32)


def others():
    y, c, z, x = spot()
    return [(flip(y, dy), flip(c, dc), z, flip(x, dx)) for dy in (0, 1) for dc in (0, 1) for dx in (0, 1) if dy + dc + dx]


def add_rows(total, first, term, start, count):
    def step(i, carry):
        here = pl.ds(pl.multiple_of(first + i * CHUNK, CHUNK), CHUNK)
        there = pl.ds(pl.multiple_of(start + i * CHUNK, CHUNK), CHUNK)
        total[here, :] = (total[here, :].astype(jnp.float32) + term[there, :].astype(jnp.float32)).astype(LOW)
        return carry

    lax.fori_loop(0, count // CHUNK, step, 0)


def scatter_scratch(width):
    return [
        pltpu.VMEM((2, TILE, width), LOW),
        pltpu.VMEM((4, TILE, width), LOW),
        pltpu.VMEM((4, TILE, width), LOW),
        pltpu.VMEM((2, HALF, width), LOW),
        pltpu.VMEM((2, TILE, width), LOW),
        pltpu.SemaphoreType.DMA((10,)),
        pltpu.SemaphoreType.DMA((10,)),
    ]


def run_scatter(produce, staged, core_part, total, relayed, landed, send, recv):
    y, c, z, x = spot()
    across_x, across_y, core = near()
    dests = ((1 - y, 1 - x), (y, 1 - x), (1 - y, x), (y, x))
    first, second = pl.ds(0, HALF), pl.ds(HALF, HALF)
    to_core = [
        remote(staged.at[k % 2], core_part.at[k], send.at[k], recv.at[k], core) for k in range(4)
    ]
    far_x = remote(total.at[0, first], relayed.at[0], send.at[4], recv.at[4], across_x)
    far_y = remote(total.at[0, second], relayed.at[1], send.at[5], recv.at[5], across_y)
    to_x = [
        remote(total.at[1, at], landed.at[0, at], send.at[6 + half], recv.at[6 + half], across_x)
        for half, at in enumerate((first, second))
    ]
    to_y = [
        remote(total.at[2, at], landed.at[1, at], send.at[8 + half], recv.at[8 + half], across_y)
        for half, at in enumerate((first, second))
    ]
    for k, (to_row, to_column) in enumerate(dests):
        if k >= 2:
            to_core[k - 2].wait_send()
        produce(2 * k, to_row, 1 - c, to_column, staged.at[k % 2])
        to_core[k].start()
        produce(2 * k + 1, to_row, c, to_column, total.at[k])
        to_core[k].wait_recv()
        add_rows(total.at[k], 0, core_part.at[k], 0, TILE)
        if k == 0:
            far_x.start()
            far_y.start()
        if k == 1:
            to_x[0].start()
        if k == 2:
            to_y[1].start()
    far_y.wait_recv()
    add_rows(total.at[1], HALF, relayed.at[1], 0, HALF)
    to_x[1].start()
    far_x.wait_recv()
    add_rows(total.at[2], 0, relayed.at[0], 0, HALF)
    to_y[0].start()
    for copy in to_x + to_y:
        copy.wait_recv()
    for copy in to_core[2:] + [far_x, far_y] + to_x + to_y:
        copy.wait_send()


def begin_kernel(
    x_own, w_query, w_key, w_value, facts, x_whole, w_qkv, facts_whole,
    trade_send, trade_recv, gather_send, gather_recv, w_send, w_recv, fact_send, fact_recv, local, *sems
):
    y, c, z, x = spot()
    row = 2 * y + c
    worker, owner = worker_of(y, c, z, x), owner_of(y, c, z, x)
    moves = jnp.logical_not((worker[0] == y) & (worker[1] == c) & (worker[2] == z))
    layer = others()
    barrier, count = greet_neighbours(layer)

    @pl.when(moves)
    def _():
        pl.semaphore_signal(barrier, inc=1, device_id=owner, device_id_type=MESH_ID)
        pl.semaphore_signal(barrier, inc=1, device_id=worker, device_id_type=MESH_ID)

    pl.semaphore_wait(barrier, count + 2 * moves.astype(jnp.int32))

    shard, width = w_query.shape
    owned = width // 8
    trades = [
        remote(
            x_own.at[half],
            x_whole.at[place_of(worker[0], worker[1], worker[3], half)],
            trade_send.at[half],
            trade_recv.at[half],
            worker,
        )
        for half in (0, 1)
    ]
    keeps = [
        pltpu.make_async_copy(x_own.at[half], x_whole.at[place_of(y, c, x, half)], trade_recv.at[half]) for half in (0, 1)
    ]

    @pl.when(moves)
    def _():
        for copy in trades:
            copy.start()

    @pl.when(jnp.logical_not(moves))
    def _():
        for copy in keeps:
            copy.start()

    spread = [
        remote(facts, facts_whole.at[row, z, x], fact_send.at[k], fact_recv.at[k], peer) for k, peer in enumerate(layer)
    ]
    kept = [pltpu.make_async_copy(facts, facts_whole.at[row, z, x], local.at[3])]
    for m, source in enumerate((w_query, w_key, w_value)):
        dst = w_qkv.at[row, z, pl.ds(pl.multiple_of(x * shard, shard), shard), pl.ds(m * owned, owned)]
        for k, peer in enumerate(layer):
            columns = pl.ds(pl.multiple_of((4 * peer[0] + 2 * peer[1] + peer[3]) * owned, owned), owned)
            spread.append(remote(source.at[:, columns], dst, w_send.at[m, k], w_recv.at[m, k], peer))
        columns = pl.ds(pl.multiple_of((4 * y + 2 * c + x) * owned, owned), owned)
        kept.append(pltpu.make_async_copy(source.at[:, columns], dst, local.at[m]))
    for copy in spread + kept:
        copy.start()

    gather = Gather(lambda half: x_whole.at[place_of(y, c, x, half)], x_whole, gather_send, gather_recv)
    for half in (0, 1):

        @pl.when(moves)
        def _():
            trades[half].wait_recv()

        @pl.when(jnp.logical_not(moves))
        def _():
            keeps[half].wait()

        gather.start(half)

    for copy in kept:
        copy.wait()
    for copy in spread:
        copy.wait_recv()
    chains = [
        Chain(facts_whole.at[:, z], lambda at: facts_whole.at[:, at], sems, 0),
        Chain(w_qkv.at[:, z], lambda at: w_qkv.at[:, at], sems, 1),
    ]

    def arrive(h):
        for chain in chains:
            chain.arrive(h)

    for chain in chains:
        chain.start()
    gather.pass_first()
    arrive(0)
    gather.pass_second()
    arrive(1)
    gather.pass_far()
    arrive(2)
    gather.finish()

    @pl.when(moves)
    def _():
        for copy in trades:
            copy.wait_send()

    for copy in spread:
        copy.wait_send()
    for chain in chains:
        chain.finish()


def anywhere():
    return pl.BlockSpec(memory_space=pl.ANY)


def in_vmem():
    return pl.BlockSpec(memory_space=pltpu.VMEM)


def dma(*shape):
    return pltpu.SemaphoreType.DMA(shape)


def remote_params(number):
    return pltpu.CompilerParams(collective_id=number, has_side_effects=True, vmem_limit_bytes=VMEM_LIMIT)


def begin(x_own, w_query, w_key, w_value, facts):
    block, width = x_own.shape
    shard = w_query.shape[0]
    x_whole, w_qkv, facts_whole = pl.pallas_call(
        begin_kernel,
        out_shape=(
            jax.ShapeDtypeStruct((8 * block, width), LOW),
            jax.ShapeDtypeStruct((4, 4, 2 * shard, 3 * width // 8), LOW),
            jax.ShapeDtypeStruct((4, 4, 2, *facts.shape), jnp.float32),
        ),
        in_specs=[anywhere()] * 5,
        out_specs=[anywhere()] * 3,
        scratch_shapes=[
            dma(2), dma(2), dma(GATHER_COPIES), dma(GATHER_COPIES), dma(3, 7), dma(3, 7), dma(7), dma(7), dma(4), *chain_sems(2)
        ],
        compiler_params=remote_params(1),
        cost_estimate=pl.CostEstimate(flops=0, bytes_accessed=350_000_000, transcendentals=0),
    )(x_own.reshape(2, block // 2, width), w_query, w_key, w_value, facts)
    return x_whole, w_qkv.reshape(width, 3 * width // 8), facts_whole


def summed(total, landed, here):
    parts = (total[3, here, :], landed[0, here, :], landed[1, here, :])
    return sum(part.astype(jnp.float32) for part in parts)


def over_chunks(work):
    def step(i, carry):
        work(pl.ds(pl.multiple_of(i * CHUNK, CHUNK), CHUNK))
        return carry

    lax.fori_loop(0, TILE // CHUNK, step, 0)


def inverse_of(value):
    return lax.rsqrt(jnp.mean(value * value, axis=-1, keepdims=True) + EPSILON)


def close_attention_kernel(attended, w_out, x_own, gain, w_gate, w_up, resid, normed, own_gate, own_up, own, *scratch):
    scatter, (send, recv, local), sems = scratch[:7], scratch[7:10], scratch[10:]
    width = w_out.shape[1]
    hidden = w_gate.shape[1]
    z = lax.axis_index("z")
    barrier, count = greet_neighbours(near())
    pl.semaphore_wait(barrier, count)

    def slab_of(whole):
        return lambda at: whole.at[:, pl.ds(pl.multiple_of(at * hidden, hidden), hidden)]

    chains, kept = [], []
    for k, (part, whole) in enumerate(((w_gate, own_gate), (w_up, own_up))):
        chains.append(Chain(part, slab_of(whole), sems, k))
        chains[k].start()
        kept.append(pltpu.make_async_copy(part, slab_of(whole)(z), local.at[1 + k]))
        kept[k].start()

    def arrive(h):
        for chain in chains:
            chain.arrive(h)

    def produce(turn, y, c, x, out):
        at = place_of(y, c, x)

        def step(i, carry):
            columns = pl.ds(pl.multiple_of(i * TILE, TILE), TILE)
            out[:, columns] = dot_wide(attended[at, :], w_out[:, columns]).astype(LOW)
            return carry

        lax.fori_loop(0, width // TILE, step, 0)

    run_scatter(produce, *scatter)
    total, landed = scatter[2], scatter[4]

    def chunk(here):
        value = x_own[here, :].astype(jnp.float32) + summed(total, landed, here)
        resid[here, :] = value
        own[here, :] = (value * inverse_of(value) * gain[...]).astype(LOW)

    over_chunks(chunk)
    run_gather(own, normed, send, recv, local.at[0], arrive)
    for chain in chains:
        chain.finish()
    for copy in kept:
        copy.wait()


def close_attention(attended, w_out, x_own, gain, w_gate, w_up):
    block, width = x_own.shape
    hidden = w_gate.shape[1]
    return pl.pallas_call(
        close_attention_kernel,
        out_shape=(
            jax.ShapeDtypeStruct((block, width), jnp.float32),
            jax.ShapeDtypeStruct((8 * block, width), LOW),
            jax.ShapeDtypeStruct((width, 4 * hidden), LOW),
            jax.ShapeDtypeStruct((width, 4 * hidden), LOW),
        ),
        in_specs=[in_vmem()] * 4 + [anywhere()] * 2,
        out_specs=[in_vmem()] + [anywhere()] * 3,
        scratch_shapes=[pltpu.VMEM((block, width), LOW)]
        + scatter_scratch(width)
        + [dma(GATHER_COPIES), dma(GATHER_COPIES), dma(3), *chain_sems(2)],
        compiler_params=remote_params(2),
        cost_estimate=pl.CostEstimate(flops=0, bytes_accessed=450_000_000, transcendentals=0),
    )(attended, w_out, x_own, gain, w_gate, w_up)


def norm_back(value, gain, upstream):
    inverse = inverse_of(value)
    scaled = upstream * gain
    inner = jnp.mean(scaled * value, axis=-1, keepdims=True)
    return inverse * scaled - value * (inverse * inverse * inverse) * inner, upstream * value * inverse


def fold_rows(total, terms):
    for first in range(0, CHUNK, 8):
        total[...] += terms[first : first + 8, :]


def close_mlp_kernel(d_gate, d_up, w_gate, w_up, resid, upstream, gain, d_resid, gain_term, d_resid_whole, own, blocks, *scratch):
    scatter, (send, recv, local, fetched) = scratch[:7], scratch[7:]
    y, c, z, x = spot()
    width = w_gate.shape[0]
    order = [(r, k, q) for r, q in ((1 - y, 1 - x), (y, 1 - x), (1 - y, x), (y, x)) for k in (1 - c, c)]

    def fetch(turn):
        at = place_of(*order[turn])
        slot = turn % 2
        return [
            pltpu.make_async_copy(source.at[at], blocks.at[slot, m], fetched.at[slot, m])
            for m, source in enumerate((d_gate, d_up))
        ]

    for copy in fetch(0):
        copy.start()
    greet(near())

    def produce(turn, to_y, to_c, to_x, out):
        if turn < 7:
            for copy in fetch(turn + 1):
                copy.start()
        for copy in fetch(turn):
            copy.wait()

        def step(i, carry):
            columns = pl.ds(pl.multiple_of(i * TILE, TILE), TILE)
            part = dot_nt(blocks[turn % 2, 0], w_gate[columns, :]) + dot_nt(blocks[turn % 2, 1], w_up[columns, :])
            out[:, columns] = part.astype(LOW)
            return carry

        lax.fori_loop(0, width // TILE, step, 0)

    run_scatter(produce, *scatter)
    total, landed = scatter[2], scatter[4]
    gain_term[...] = jnp.zeros_like(gain_term)

    def chunk(here):
        back, terms = norm_back(resid[here, :], gain[...], summed(total, landed, here))
        value = upstream[here, :].astype(jnp.float32) + back
        d_resid[here, :] = value
        own[here, :] = value.astype(LOW)
        fold_rows(gain_term, terms)

    over_chunks(chunk)
    run_gather(own, d_resid_whole, send, recv, local.at[0])


def close_mlp(d_gate, d_up, w_gate, w_up, resid, upstream, gain):
    block, width = resid.shape
    hidden = d_gate.shape[1]
    return pl.pallas_call(
        close_mlp_kernel,
        out_shape=(
            jax.ShapeDtypeStruct((block, width), jnp.float32),
            jax.ShapeDtypeStruct((8, width), jnp.float32),
            jax.ShapeDtypeStruct((8 * block, width), LOW),
        ),
        in_specs=[anywhere()] * 2 + [in_vmem()] * 5,
        out_specs=[in_vmem(), in_vmem(), anywhere()],
        scratch_shapes=[pltpu.VMEM((block, width), LOW), pltpu.VMEM((2, 2, block, hidden), LOW)]
        + scatter_scratch(width)
        + [dma(GATHER_COPIES), dma(GATHER_COPIES), dma(1), dma(2, 2)],
        compiler_params=remote_params(3),
        cost_estimate=pl.CostEstimate(flops=0, bytes_accessed=450_000_000, transcendentals=0),
    )(d_gate, d_up, w_gate, w_up, resid, upstream, gain)


def close_layer_kernel(d_qkv, w_qkv, x_own, d_resid, gain, mlp_term, grad_low, gain_grads, own, terms, layer_terms, part, column_terms, *scratch):
    scatter, (send, recv, term_send, term_recv, line_send, line_recv) = scratch[:7], scratch[7:]
    y, c, z, x = spot()
    worker, owner = worker_of(y, c, z, x), owner_of(y, c, z, x)
    moves = jnp.logical_not((worker[0] == y) & (worker[1] == c) & (worker[2] == z))
    width = w_qkv.shape[0]
    barrier = pltpu.get_barrier_semaphore()

    @pl.when(moves)
    def _():
        pl.semaphore_signal(barrier, inc=1, device_id=owner, device_id_type=MESH_ID)
        pl.semaphore_signal(barrier, inc=1, device_id=worker, device_id_type=MESH_ID)

    layer = others()
    line = [(y, c, lax.rem(z + dz, 4), x) for dz in (1, 2, 3)]
    for peer in layer + line:
        pl.semaphore_signal(barrier, inc=1, device_id=peer, device_id_type=MESH_ID)
    pl.semaphore_wait(barrier, len(layer + line) + 2 * moves.astype(jnp.int32))

    def produce(turn, to_y, to_c, to_x, out):
        at = place_of(to_y, to_c, to_x)

        def step(i, carry):
            columns = pl.ds(pl.multiple_of(i * TILE, TILE), TILE)
            out[:, columns] = dot_nt(d_qkv[at, :], w_qkv[columns, :]).astype(LOW)
            return carry

        lax.fori_loop(0, width // TILE, step, 0)

    run_scatter(produce, *scatter)
    total, landed = scatter[2], scatter[4]
    terms[1] = mlp_term[...]
    terms[0] = jnp.zeros_like(mlp_term)
    trades = [
        remote(own.at[pl.ds(half * HALF, HALF)], grad_low.at[pl.ds(half * HALF, HALF)], send.at[half], recv.at[half], owner)
        for half in (0, 1)
    ]
    keeps = [
        pltpu.make_async_copy(own.at[pl.ds(half * HALF, HALF)], grad_low.at[pl.ds(half * HALF, HALF)], recv.at[half])
        for half in (0, 1)
    ]
    for half in (0, 1):

        def step(i, carry):
            here = pl.ds(pl.multiple_of(half * HALF + i * CHUNK, CHUNK), CHUNK)
            back, products = norm_back(x_own[here, :].astype(jnp.float32), gain[...], summed(total, landed, here))
            own[here, :] = (d_resid[here, :] + back).astype(LOW)
            fold_rows(terms.at[0], products)
            return carry

        lax.fori_loop(0, HALF // CHUNK, step, 0)

        @pl.when(moves)
        def _():
            trades[half].start()

        @pl.when(jnp.logical_not(moves))
        def _():
            keeps[half].start()

    def columns_of(row, layers):
        return pl.ds(pl.multiple_of((4 * row) * HD, HD), layers * HD)

    spread = [
        remote(terms.at[:, :, columns_of(2 * peer[0] + peer[1], 4)], layer_terms.at[k], term_send.at[k], term_recv.at[k], peer)
        for k, peer in enumerate(layer)
    ]
    for copy in spread:
        copy.start()
    for copy in spread:
        copy.wait_recv()
    part[...] = sum((layer_terms[k] for k in range(7)), terms[:, :, columns_of(2 * y + c, 4)])
    lines = [
        remote(
            part.at[:, :, pl.ds(pl.multiple_of(peer[2] * HD, HD), HD)], column_terms.at[k], line_send.at[k], line_recv.at[k], peer
        )
        for k, peer in enumerate(line)
    ]
    for copy in lines:
        copy.start()
    for copy in lines:
        copy.wait_recv()
    gain_grads[...] = sum((column_terms[k] for k in range(3)), part[:, :, pl.ds(pl.multiple_of(z * HD, HD), HD)])
    for copy in spread + lines:
        copy.wait_send()

    @pl.when(moves)
    def _():
        for copy in trades:
            copy.wait()

    @pl.when(jnp.logical_not(moves))
    def _():
        for copy in keeps:
            copy.wait()


def close_layer(d_qkv, w_qkv, x_own, d_resid, gain, mlp_term):
    block, width = x_own.shape
    return pl.pallas_call(
        close_layer_kernel,
        out_shape=(jax.ShapeDtypeStruct((block, width), LOW), jax.ShapeDtypeStruct((2, 8, width // 16), jnp.float32)),
        in_specs=[in_vmem()] * 6,
        out_specs=[anywhere(), in_vmem()],
        scratch_shapes=[
            pltpu.VMEM((block, width), LOW),
            pltpu.VMEM((2, 8, width), jnp.float32),
            pltpu.VMEM((7, 2, 8, width // 4), jnp.float32),
            pltpu.VMEM((2, 8, width // 4), jnp.float32),
            pltpu.VMEM((3, 2, 8, width // 16), jnp.float32),
        ]
        + scatter_scratch(width)
        + [dma(2), dma(2), dma(7), dma(7), dma(3), dma(3)],
        compiler_params=remote_params(4),
        cost_estimate=pl.CostEstimate(flops=0, bytes_accessed=350_000_000, transcendentals=0),
    )(d_qkv, w_qkv, x_own, d_resid, gain, mlp_term)


LAYER = ("y", "c", "x")
ALL = ("y", "c", "z", "x")


def gather_layer(part):
    return lax.all_gather(part, LAYER, axis=0, tiled=True)


def scatter_layer(whole):
    return lax.psum_scatter(whole.astype(LOW), LAYER, scatter_dimension=0, tiled=True).astype(jnp.float32)


def trade(part, back=False):
    pairs = []
    for y in range(2):
        for c in range(2):
            for z in range(4):
                for x in range(2):
                    owner = ((y * 2 + c) * 4 + z) * 2 + x
                    worker = ((((z + c) % 2) * 2 + z // 2) * 4 + 2 * y + c) * 2 + x
                    pairs.append((worker, owner) if back else (owner, worker))
    return lax.ppermute(part, ALL, pairs)


def after(first, then):
    return lax.optimization_barrier((first, then))[1]


def body_layers(
    tokens, lengths, cotangent, w_query, w_key, w_value, w_out, w_gate, w_up, w_down, gain_attn, gain_mlp
):
    rows_here, block, width = tokens.shape
    members = lax.axis_size(LAYER)
    layers = lax.axis_size("z")
    shard = w_query.shape[0]
    owned = width // members
    facts = jnp.zeros((8, 2 * shard), jnp.float32)
    facts = facts.at[0, :shard].set(gain_attn.astype(jnp.float32)).at[1, :shard].set(gain_mlp.astype(jnp.float32))
    facts = facts.at[2, : lengths.shape[1]].set(lengths[0].astype(jnp.float32))
    layer_x, w_qkv, facts = begin(tokens.reshape(block, width), w_query, w_key, w_value, facts)
    full_gain_attn, full_gain_mlp = facts[:, :, :, 0, :shard].reshape(1, width), facts[:, :, :, 1, :shard].reshape(1, width)
    layer = lax.axis_index("z")
    own_lengths = lax.dynamic_index_in_dim(facts[:, 0, 0, 2, : lengths.shape[1]], layer, 0, False).astype(jnp.int32)
    ends = jnp.concatenate((jnp.cumsum(own_lengths), (layer % 2).astype(jnp.int32)[None]))
    place = (4 * lax.axis_index("y") + 2 * lax.axis_index("c") + lax.axis_index("x")) * block
    x_own = lax.dynamic_slice_in_dim(layer_x, place, block, 0)
    layer_normed = norm_forward(layer_x.astype(jnp.float32), full_gain_attn)[0].astype(LOW)
    out_rows = lax.all_gather(after(facts, w_out), ("z", "x"), axis=0, tiled=True)
    w_out_own = lax.dynamic_slice_in_dim(out_rows, lax.axis_index("x") * owned, owned, 0)

    qkv = dot_wide(layer_normed, w_qkv).astype(LOW)
    attended = attend(ends, qkv)
    resid, layer_mlp, own_gate, own_up = close_attention(attended, w_out_own, x_own, full_gain_mlp, w_gate, w_up)

    own_down = lax.all_gather(after(qkv, w_down), "z", axis=0, tiled=True)
    upstream = trade(after(facts, cotangent)).reshape(block, width)
    layer_upstream = gather_layer(upstream)
    gate = dot_wide(layer_mlp, own_gate)
    up_part = dot_wide(layer_mlp, own_up)
    sigmoid_gate = jax.nn.sigmoid(gate)
    hidden = (gate * sigmoid_gate * up_part).astype(LOW)
    down_term = contract_rows(hidden, layer_upstream).astype(LOW)
    d_hidden = contract_cols(layer_upstream, own_down)
    d_gate, d_up = gate_backward(d_hidden, gate, up_part, sigmoid_gate)
    gate_term, up_term = contract_rows(layer_mlp, d_gate).astype(LOW), contract_rows(layer_mlp, d_up).astype(LOW)

    def scatter_layers(whole, axis):
        return lax.psum_scatter(whole, "z", scatter_dimension=axis, tiled=True).astype(jnp.float32)

    grad_gate, grad_up, grad_down = scatter_layers(gate_term, 1), scatter_layers(up_term, 1), scatter_layers(down_term, 0)
    d_resid, gain_mlp_term, layer_d_resid = close_mlp(
        after((gate_term, up_term, down_term), d_gate), d_up, own_gate, own_up, resid, upstream, full_gain_mlp
    )
    result = resid + scatter_layer(dot_wide(after(d_resid, hidden), own_down))
    mixed = trade(result.astype(LOW).reshape(rows_here, block, width), back=True)

    out_term = contract_rows(attended, layer_d_resid)
    out_term = lax.dynamic_update_slice_in_dim(
        jnp.zeros((2 * owned, width), LOW), out_term.astype(LOW), lax.axis_index("x") * owned, 0
    )
    grad_out = lax.psum_scatter(out_term, ("z", "x"), scatter_dimension=0, tiled=True).astype(jnp.float32)
    d_attended = contract_cols(layer_d_resid, w_out_own).astype(LOW)
    d_qkv = attend_back(ends, qkv, after(out_term, d_attended))
    qkv_term = contract_rows(layer_normed, d_qkv).astype(LOW)
    grad_low, gain_grads = close_layer(
        after(qkv_term, d_qkv), w_qkv, x_own, d_resid, full_gain_attn, gain_mlp_term
    )
    grad_tokens = grad_low.astype(jnp.float32).reshape(rows_here, block, width)

    qkv_term = qkv_term.reshape(4, layers, 2 * shard, 3 * owned).transpose(1, 0, 2, 3)
    qkv_term = qkv_term.reshape(layers * members * shard, 3 * owned)
    qkv_term = lax.psum_scatter(qkv_term, "z", scatter_dimension=0, tiled=True)
    qkv_term = lax.all_to_all(qkv_term.reshape(members, shard, 3 * owned), LAYER, 0, 0)
    qkv_term = qkv_term.reshape(members, shard, 3, owned).transpose(2, 1, 0, 3).astype(jnp.float32)
    grad_query, grad_key, grad_value = qkv_term.reshape(3, shard, width)
    gain_grads = lax.dynamic_index_in_dim(jnp.sum(gain_grads, axis=1).reshape(2, 2, shard), lax.axis_index("x"), 1, False)
    return (
        mixed,
        grad_tokens,
        grad_query,
        grad_key,
        grad_value,
        grad_out,
        grad_gate,
        grad_up,
        grad_down,
        gain_grads[0],
        gain_grads[1],
    )


def body_any(
    tokens,
    lengths,
    cotangent,
    w_query,
    w_key,
    w_value,
    w_out,
    w_gate,
    w_up,
    w_down,
    gain_attn,
    gain_mlp,
):
    rows_here, block, width = tokens.shape
    count = rows_here * block
    scale = 1.0 / math.sqrt(HD)
    kv_place = lax.axis_index("kv")
    key_places = kv_place * block + jnp.arange(block, dtype=jnp.int32)
    attn_set = (
        lax.all_gather(w_query, ("row", "kv"), axis=0, tiled=True),
        lax.all_gather(w_key, ("row", "kv"), axis=0, tiled=True),
        lax.all_gather(w_value, ("row", "kv"), axis=0, tiled=True),
        lax.all_gather(w_out, ("row", "kv"), axis=0, tiled=True),
        lax.all_gather(gain_attn, ("row", "kv"), axis=0, tiled=True),
        lax.all_gather(gain_mlp, ("row", "kv"), axis=0, tiled=True),
    )
    full_query, full_key, full_value, full_out, full_gain_attn, full_gain_mlp = attn_set
    flat = tokens.reshape(count, width).astype(jnp.float32)
    normed_attn, inverse_attn = norm_forward(flat, full_gain_attn)
    normed_attn_low = normed_attn.astype(jnp.bfloat16)
    query_low = jnp.dot(normed_attn_low, full_query, preferred_element_type=jnp.float32).astype(
        jnp.bfloat16
    )
    key_low = jnp.dot(normed_attn_low, full_key, preferred_element_type=jnp.float32).astype(
        jnp.bfloat16
    )
    value_low = jnp.dot(normed_attn_low, full_value, preferred_element_type=jnp.float32).astype(
        jnp.bfloat16
    )
    key_heads = key_low.reshape(rows_here, block, H, HD)
    value_heads = value_low.reshape(rows_here, block, H, HD)
    segment, valid = segment_table(lengths)
    key_segment = lax.dynamic_slice_in_dim(segment, kv_place * block, block, 1)
    key_valid = lax.dynamic_slice_in_dim(valid, kv_place * block, block, 1)
    queries_all = lax.all_gather(
        query_low.reshape(rows_here, block, width), "kv", axis=1, tiled=True
    )
    which = 0
    query_rows = queries_all[which]
    query_segment = segment[which]
    sigmoid_part, allowed = score_block(
        query_rows,
        key_heads[which],
        query_segment,
        key_segment[which],
        key_valid[which],
        jnp.int32(0),
        key_places,
    )
    weight = (sigmoid_part * allowed).astype(jnp.bfloat16)
    summed = jnp.einsum(
        "hqk,khd->qhd", weight, value_heads[which], preferred_element_type=jnp.float32
    )
    pieces = [
        lax.psum_scatter(
            summed.reshape(lax.axis_size("kv") * block, width).astype(jnp.bfloat16),
            "kv",
            scatter_dimension=0,
            tiled=True,
        ).astype(jnp.float32)
    ]
    attended_low = jnp.stack(pieces).reshape(count, width).astype(jnp.bfloat16)
    resid = flat + jnp.dot(attended_low, full_out, preferred_element_type=jnp.float32)
    normed_mlp, inverse_mlp = norm_forward(resid, full_gain_mlp)
    normed_mlp_low = normed_mlp.astype(jnp.bfloat16)
    upstream_low = cotangent.reshape(count, width)
    upstream = upstream_low.astype(jnp.float32)
    slice_gate, slice_up, slice_down = (
        lax.all_gather(w_gate, "row", axis=1, tiled=True),
        lax.all_gather(w_up, "row", axis=1, tiled=True),
        lax.all_gather(w_down, "row", axis=0, tiled=True),
    )
    row_normed, row_upstream = (
        lax.all_gather(normed_mlp_low.reshape(rows_here, block, width), "kv", axis=1, tiled=True),
        lax.all_gather(cotangent, "kv", axis=1, tiled=True),
    )
    normed_rows = row_normed.reshape(rows_here * LEN, width)
    upstream_rows = row_upstream.reshape(rows_here * LEN, width)
    gate = jnp.dot(normed_rows, slice_gate, preferred_element_type=jnp.float32)
    up_part = jnp.dot(normed_rows, slice_up, preferred_element_type=jnp.float32)
    sigmoid_gate = jax.nn.sigmoid(gate)
    hidden_low = (gate * sigmoid_gate * up_part).astype(jnp.bfloat16)
    hidden_rows = hidden_low.reshape(rows_here, LEN, hidden_low.shape[1])
    which = 0
    hidden_part = hidden_rows[which]
    outputs = [
        lax.psum_scatter(
            jnp.dot(hidden_part, slice_down, preferred_element_type=jnp.float32).astype(
                jnp.bfloat16
            ),
            "kv",
            scatter_dimension=0,
            tiled=True,
        ).astype(jnp.float32)
    ]
    result = resid + jnp.stack(outputs).reshape(count, width)
    d_hidden = contract_cols(upstream_rows, slice_down)
    d_gate, d_up = gate_backward(d_hidden, gate, up_part, sigmoid_gate)
    partial_normed = contract_cols(d_gate, slice_gate) + contract_cols(d_up, slice_up)
    d_normed_mlp = (
        lax.psum_scatter(
            partial_normed.reshape(rows_here, LEN, width).astype(jnp.bfloat16),
            "kv",
            scatter_dimension=1,
            tiled=True,
        )
        .astype(jnp.float32)
        .reshape(count, width)
    )
    grad_gate, grad_up, grad_down = (
        lax.psum_scatter(
            contract_rows(normed_rows, d_gate).astype(jnp.bfloat16),
            "row",
            scatter_dimension=1,
            tiled=True,
        ).astype(jnp.float32),
        lax.psum_scatter(
            contract_rows(normed_rows, d_up).astype(jnp.bfloat16),
            "row",
            scatter_dimension=1,
            tiled=True,
        ).astype(jnp.float32),
        lax.psum_scatter(
            contract_rows(hidden_low, upstream_rows).astype(jnp.bfloat16),
            "row",
            scatter_dimension=0,
            tiled=True,
        ).astype(jnp.float32),
    )
    mixed = result.astype(jnp.bfloat16).reshape(rows_here, block, width)
    back_mlp, gain_mlp_term = norm_backward(resid, inverse_mlp, full_gain_mlp, d_normed_mlp)
    d_resid = upstream + back_mlp
    d_resid_low = d_resid.astype(jnp.bfloat16)
    d_attended = contract_cols(d_resid_low, full_out).astype(jnp.bfloat16)
    grads_all = lax.all_gather(
        d_attended.reshape(rows_here, block, width), "kv", axis=1, tiled=True
    )
    query_block = min(512, LEN)
    block_count = LEN // query_block
    which = 0

    def sweep(carry, index, which=which):
        key_total, value_total = carry
        start = index * query_block
        query_rows = lax.dynamic_slice_in_dim(queries_all[which], start, query_block, 0)
        grad_rows = lax.dynamic_slice_in_dim(grads_all[which], start, query_block, 0)
        query_segment = lax.dynamic_slice_in_dim(segment[which], start, query_block, 0)
        sigmoid_part, allowed = score_block(
            query_rows,
            key_heads[which],
            query_segment,
            key_segment[which],
            key_valid[which],
            start,
            key_places,
        )
        weight = (sigmoid_part * allowed).astype(jnp.bfloat16)
        grad_heads = grad_rows.reshape(query_block, H, HD)
        value_total = value_total + jnp.einsum(
            "hqk,qhd->khd", weight, grad_heads, preferred_element_type=jnp.float32
        )
        d_weight = jnp.einsum(
            "qhd,khd->hqk", grad_heads, value_heads[which], preferred_element_type=jnp.float32
        )
        d_score = (d_weight * sigmoid_part * (1.0 - sigmoid_part) * allowed).astype(jnp.bfloat16)
        query_part = (
            jnp.einsum(
                "hqk,khd->qhd", d_score, key_heads[which], preferred_element_type=jnp.float32
            )
            * scale
        )
        key_total = (
            key_total
            + jnp.einsum(
                "hqk,qhd->khd",
                d_score,
                query_rows.reshape(query_block, H, HD),
                preferred_element_type=jnp.float32,
            )
            * scale
        )
        return ((key_total, value_total), query_part.reshape(query_block, width))

    zeros = jnp.zeros((block, H, HD), jnp.float32)
    totals, query_parts = lax.scan(sweep, (zeros, zeros), jnp.arange(block_count, dtype=jnp.int32))
    query_terms = [query_parts.reshape(LEN, width)]
    key_grads = [totals[0].reshape(block, width)]
    value_grads = [totals[1].reshape(block, width)]
    query_local = lax.psum_scatter(
        jnp.stack(query_terms).astype(jnp.bfloat16), "kv", scatter_dimension=1, tiled=True
    ).astype(jnp.float32)
    d_query_low = query_local.reshape(count, width).astype(jnp.bfloat16)
    d_key_low = jnp.stack(key_grads).reshape(count, width).astype(jnp.bfloat16)
    d_value_low = jnp.stack(value_grads).reshape(count, width).astype(jnp.bfloat16)
    d_normed_attn = (
        contract_cols(d_query_low, full_query)
        + contract_cols(d_key_low, full_key)
        + contract_cols(d_value_low, full_value)
    )
    back_attn, gain_attn_term = norm_backward(flat, inverse_attn, full_gain_attn, d_normed_attn)
    grad_tokens = (d_resid + back_attn).reshape(rows_here, block, width)
    projected_low = jnp.concatenate((d_query_low, d_key_low, d_value_low), axis=1)
    grad_projections = lax.psum_scatter(
        contract_rows(normed_attn_low, projected_low),
        ("row", "kv"),
        scatter_dimension=0,
        tiled=True,
    )
    out_term = contract_rows(attended_low, d_resid_low)
    grad_out, grad_gain_attn, grad_gain_mlp = (
        lax.psum_scatter(out_term, ("row", "kv"), scatter_dimension=0, tiled=True),
        lax.psum_scatter(gain_attn_term, ("row", "kv"), scatter_dimension=0, tiled=True),
        lax.psum_scatter(gain_mlp_term, ("row", "kv"), scatter_dimension=0, tiled=True),
    )
    grad_query = grad_projections[:, :width]
    grad_key = grad_projections[:, width : 2 * width]
    grad_value = grad_projections[:, 2 * width :]
    return (
        mixed,
        grad_tokens,
        grad_query,
        grad_key,
        grad_value,
        grad_out,
        grad_gate,
        grad_up,
        grad_down,
        grad_gain_attn,
        grad_gain_mlp,
    )


def solution(mesh):
    rows, columns = mesh.shape["row"], mesh.shape["kv"]
    if rows == 4 and columns == 2 * rows:
        mesh = Mesh(mesh.devices.reshape(2, 2, rows, 2), ("y", "c", "z", "x"))
        row, kv, run = ("y", "c"), ("z", "x"), body_layers
    else:
        row, kv, run = "row", "kv", body_any
    both = ("y", "c", "z", "x") if run is body_layers else ("row", "kv")
    tall, wide, flat = P(both, None), P(None, both), P(both)
    tokens = P(row, kv, None)
    return jax.shard_map(
        run,
        mesh=mesh,
        in_specs=(tokens, P(row, None), tokens, tall, tall, tall, tall, wide, wide, tall, flat, flat),
        out_specs=(tokens, tokens, tall, tall, tall, tall, wide, wide, tall, flat, flat),
        check_vma=False,
    )
```

```python
import functools
import math

import jax
import jax.numpy as jnp
from jax import lax
from jax.experimental import pallas as pl
from jax.experimental.pallas import tpu as pltpu
from jax.sharding import Mesh, PartitionSpec as P

H = 16
HD = 128
LEN = 4096


EPSILON = 1e-05


def contract_rows(left, right):
    return lax.dot_general(
        left, right, (((0,), (0,)), ((), ())), preferred_element_type=jnp.float32
    )


def contract_cols(left, right):
    return lax.dot_general(
        left, right, (((1,), (1,)), ((), ())), preferred_element_type=jnp.float32
    )


def norm_forward(value, gain):
    inverse = lax.rsqrt(jnp.mean(value * value, axis=-1, keepdims=True) + EPSILON)
    return (value * inverse * gain.astype(jnp.float32), inverse)


def norm_backward(value, inverse, gain, upstream):
    scaled = upstream * gain.astype(jnp.float32)
    inner = jnp.mean(scaled * value, axis=-1, keepdims=True)
    back = inverse * scaled - value * (inverse * inverse * inverse) * inner
    gain_term = jnp.sum(upstream * value * inverse, axis=0)
    return (back, gain_term)


def segment_table(lengths):
    ends = jnp.cumsum(lengths, axis=-1)
    places = jnp.arange(LEN, dtype=jnp.int32)
    segment = jnp.sum((ends[:, None, :] <= places[None, :, None]).astype(jnp.int32), axis=-1)
    valid = places[None, :] < ends[:, -1:]
    return (segment, valid)


def score_block(
    query_rows, key_heads, query_segment, key_segment, key_valid, query_start, key_places
):
    count = query_rows.shape[0]
    query_heads = query_rows.reshape(count, H, HD)
    raw = jnp.einsum("qhd,khd->hqk", query_heads, key_heads, preferred_element_type=jnp.float32)
    scores = raw * (1.0 / math.sqrt(HD)) - math.log(LEN)
    places = query_start + jnp.arange(count, dtype=jnp.int32)
    allowed = (
        (key_places[None, :] <= places[:, None])
        & (key_segment[None, :] == query_segment[:, None])
        & key_valid[None, :]
    )
    return (jax.nn.sigmoid(scores), allowed.astype(jnp.float32)[None])


def gate_backward(d_hidden, gate, up_part, sigmoid_gate):
    d_gate = (d_hidden * up_part * sigmoid_gate * (1.0 + gate * (1.0 - sigmoid_gate))).astype(
        jnp.bfloat16
    )
    d_up = (d_hidden * gate * sigmoid_gate).astype(jnp.bfloat16)
    return (d_gate, d_up)


TILE = 512
LOW = jnp.bfloat16
VMEM_LIMIT = 60 * 1024 * 1024


def dot_nt(left, right):
    return lax.dot_general(left, right, (((1,), (1,)), ((), ())), preferred_element_type=jnp.float32)


def dot_wide(left, right):
    return jnp.dot(left, right, preferred_element_type=jnp.float32)


HALF = TILE // 2
CHUNK = 32
MESH_ID = pl.DeviceIdType.MESH


def flip(bit, by):
    return bit + by - 2 * bit * by


def spot():
    return tuple(lax.axis_index(name) for name in ("y", "c", "z", "x"))


def near():
    y, c, z, x = spot()
    return (y, c, z, 1 - x), (1 - y, c, z, x), (y, 1 - c, z, x)


def partner_of(y, c, z, x):
    return lax.rem(z, 2), z // 2, 2 * c + y, x


def place_of(y, c, x, half=None):
    first = (4 * c + 2 * y + x) * TILE
    if half is None:
        return pl.ds(pl.multiple_of(first, TILE), TILE)
    return pl.ds(pl.multiple_of(first + half * HALF, HALF), HALF)


def remote(src, dst, send, recv, peer):
    return pltpu.make_async_remote_copy(
        src_ref=src, dst_ref=dst, send_sem=send, recv_sem=recv, device_id=peer, device_id_type=MESH_ID
    )


def greet(peers):
    barrier = pltpu.get_barrier_semaphore()
    for peer in peers:
        pl.semaphore_signal(barrier, inc=1, device_id=peer, device_id_type=MESH_ID)
    pl.semaphore_wait(barrier, len(peers))


class Gather:
    def __init__(self, own, whole, send, recv):
        y, c, z, x = spot()
        across_x, across_y, core = near()

        def from_own(k, half, peer):
            return remote(own(half), whole.at[place_of(y, c, x, half)], send.at[k], recv.at[k], peer)

        def passed(k, at, peer):
            return remote(whole.at[at], whole.at[at], send.at[k], recv.at[k], peer)

        self.mine = [
            [from_own(0, 0, across_x), from_own(1, 0, across_y), from_own(2, 0, core)],
            [from_own(3, 1, across_x), from_own(4, 1, across_y), from_own(5, 1, core)],
        ]
        held_x = [place_of(y, c, 1 - x, half) for half in (0, 1)]
        held_y = [place_of(1 - y, c, x, half) for half in (0, 1)]
        far = [place_of(1 - y, c, 1 - x, half) for half in (0, 1)]
        self.over_y, self.over_x = passed(6, held_x[0], across_y), passed(7, held_y[1], across_x)
        self.core_x = [passed(8 + half, held_x[half], core) for half in (0, 1)]
        self.core_y = [passed(10 + half, held_y[half], core) for half in (0, 1)]
        self.core_far = [passed(12 + half, far[half], core) for half in (0, 1)]

    def start(self, half):
        for copy in self.mine[half]:
            copy.start()

    def pass_first(self):
        self.mine[0][0].wait_recv()
        self.over_y.start()
        self.core_x[0].start()
        self.mine[0][1].wait_recv()
        self.core_y[0].start()

    def pass_second(self):
        self.mine[1][1].wait_recv()
        self.over_x.start()
        self.core_y[1].start()
        self.mine[1][0].wait_recv()
        self.core_x[1].start()

    def pass_far(self):
        self.over_y.wait_recv()
        self.core_far[0].start()
        self.over_x.wait_recv()
        self.core_far[1].start()

    def finish(self):
        from_core = [self.mine[0][2], self.mine[1][2]] + self.core_x + self.core_y + self.core_far
        for copy in from_core:
            copy.wait_recv()
        for copy in self.mine[0] + self.mine[1] + [self.over_y, self.over_x] + self.core_x + self.core_y + self.core_far:
            copy.wait_send()


GATHER_COPIES = 14


def run_gather(own, whole, send, recv, local, beside=lambda h: None):
    y, c, z, x = spot()
    keep = pltpu.make_async_copy(own, whole.at[place_of(y, c, x)], local)
    keep.start()
    gather = Gather(lambda half: own.at[pl.ds(half * HALF, HALF)], whole, send, recv)
    gather.start(0)
    gather.start(1)
    gather.pass_first()
    beside(1)
    gather.pass_second()
    gather.pass_far()
    gather.finish()
    beside(2)
    keep.wait()


class Chain:
    def __init__(self, own, slab, sems, index):
        self.own, self.slab, self.sems, self.index = own, slab, sems, index
        self.last = lax.axis_size("z") - 1

    def move(self, which, h, source, layer, to):
        y, c, z, x = spot()
        return remote(
            source, self.slab(layer), self.sems[2 * which].at[self.index, h], self.sems[2 * which + 1].at[self.index, h], (y, c, to, x)
        )

    def up(self, h):
        z = lax.axis_index("z")
        return self.move(0, h, self.own if h == 0 else self.slab(z - h), z - h, z + 1)

    def down(self, h):
        z = lax.axis_index("z")
        return self.move(1, h, self.own if h == 0 else self.slab(z + h), z + h, z - 1)

    def start(self):
        z = lax.axis_index("z")

        @pl.when(z < self.last)
        def _():
            self.up(0).start()

        @pl.when(z > 0)
        def _():
            self.down(0).start()

    def arrive(self, h):
        z = lax.axis_index("z")

        @pl.when(z - h - 1 >= 0)
        def _():
            self.move(0, h, self.slab(z - h - 1), z - h - 1, z).wait_recv()
            if h < 2:

                @pl.when(z < self.last)
                def _():
                    self.up(h + 1).start()

        @pl.when(z + h + 1 <= self.last)
        def _():
            self.move(1, h, self.slab(z + h + 1), z + h + 1, z).wait_recv()
            if h < 2:

                @pl.when(z > 0)
                def _():
                    self.down(h + 1).start()

    def finish(self):
        z = lax.axis_index("z")
        for h in range(3):

            @pl.when((z < self.last) & (z - h >= 0))
            def _():
                self.up(h).wait_send()

            @pl.when((z > 0) & (z + h <= self.last))
            def _():
                self.down(h).wait_send()


def chain_sems(count):
    return [pltpu.SemaphoreType.DMA((count, 3)) for _ in range(4)]


def greet_neighbours(peers):
    y, c, z, x = spot()
    last = lax.axis_size("z") - 1
    barrier = pltpu.get_barrier_semaphore()
    for peer in peers:
        pl.semaphore_signal(barrier, inc=1, device_id=peer, device_id_type=MESH_ID)

    @pl.when(z > 0)
    def _():
        pl.semaphore_signal(barrier, inc=1, device_id=(y, c, z - 1, x), device_id_type=MESH_ID)

    @pl.when(z < last)
    def _():
        pl.semaphore_signal(barrier, inc=1, device_id=(y, c, z + 1, x), device_id_type=MESH_ID)

    return barrier, len(peers) + (z > 0).astype(jnp.int32) + (z < last).astype(jnp.int32)


def others():
    y, c, z, x = spot()
    return [(flip(y, dy), flip(c, dc), z, flip(x, dx)) for dy in (0, 1) for dc in (0, 1) for dx in (0, 1) if dy + dc + dx]


def line_of():
    y, c, z, x = spot()
    return [(y, c, lax.rem(z + dz, 4), x) for dz in (1, 2, 3)]


def spread_columns(whole, parts, send, recv):
    size = whole.shape[1] // 4
    return [
        remote(
            whole.at[:, pl.ds(pl.multiple_of(peer[2] * size, size), size)], parts.at[k], send.at[k], recv.at[k], peer
        )
        for k, peer in enumerate(line_of())
    ]


def add_rows(total, first, term, start, count):
    def step(i, carry):
        here = pl.ds(pl.multiple_of(first + i * CHUNK, CHUNK), CHUNK)
        there = pl.ds(pl.multiple_of(start + i * CHUNK, CHUNK), CHUNK)
        total[here, :] = (total[here, :].astype(jnp.float32) + term[there, :].astype(jnp.float32)).astype(LOW)
        return carry

    lax.fori_loop(0, count // CHUNK, step, 0)


def scatter_scratch(width):
    return [
        pltpu.VMEM((2, TILE, width), LOW),
        pltpu.VMEM((4, TILE, width), LOW),
        pltpu.VMEM((4, TILE, width), LOW),
        pltpu.VMEM((2, HALF, width), LOW),
        pltpu.VMEM((2, TILE, width), LOW),
        pltpu.SemaphoreType.DMA((10,)),
        pltpu.SemaphoreType.DMA((10,)),
    ]


def run_scatter(produce, staged, core_part, total, relayed, landed, send, recv, beside=lambda: None):
    y, c, z, x = spot()
    across_x, across_y, core = near()
    dests = ((1 - y, 1 - x), (y, 1 - x), (1 - y, x), (y, x))
    first, second = pl.ds(0, HALF), pl.ds(HALF, HALF)
    to_core = [
        remote(staged.at[k % 2], core_part.at[k], send.at[k], recv.at[k], core) for k in range(4)
    ]
    far_x = remote(total.at[0, first], relayed.at[0], send.at[4], recv.at[4], across_x)
    far_y = remote(total.at[0, second], relayed.at[1], send.at[5], recv.at[5], across_y)
    to_x = [
        remote(total.at[1, at], landed.at[0, at], send.at[6 + half], recv.at[6 + half], across_x)
        for half, at in enumerate((first, second))
    ]
    to_y = [
        remote(total.at[2, at], landed.at[1, at], send.at[8 + half], recv.at[8 + half], across_y)
        for half, at in enumerate((first, second))
    ]
    for k, (to_row, to_column) in enumerate(dests):
        if k >= 2:
            to_core[k - 2].wait_send()
        produce(2 * k, to_row, 1 - c, to_column, staged.at[k % 2])
        to_core[k].start()
        produce(2 * k + 1, to_row, c, to_column, total.at[k])
        to_core[k].wait_recv()
        add_rows(total.at[k], 0, core_part.at[k], 0, TILE)
        if k == 0:
            far_x.start()
            far_y.start()
        if k == 1:
            to_x[0].start()
        if k == 2:
            to_y[1].start()
    far_y.wait_recv()
    add_rows(total.at[1], HALF, relayed.at[1], 0, HALF)
    to_x[1].start()
    far_x.wait_recv()
    add_rows(total.at[2], 0, relayed.at[0], 0, HALF)
    to_y[0].start()
    beside()
    for copy in to_x + to_y:
        copy.wait_recv()
    for copy in to_core[2:] + [far_x, far_y] + to_x + to_y:
        copy.wait_send()


def begin_kernel(
    x_own, w_query, w_key, w_value, facts, x_whole, w_qkv, facts_whole,
    trade_send, trade_recv, gather_send, gather_recv, w_send, w_recv, fact_send, fact_recv, local, *sems
):
    y, c, z, x = spot()
    row = 2 * y + c
    partner = partner_of(y, c, z, x)
    moves = z != 2 * c + y
    layer = others()
    barrier, count = greet_neighbours(layer)

    @pl.when(moves)
    def _():
        pl.semaphore_signal(barrier, inc=1, device_id=partner, device_id_type=MESH_ID)

    pl.semaphore_wait(barrier, count + moves.astype(jnp.int32))

    shard, width = w_query.shape
    owned = width // 8
    trades = [
        remote(
            x_own.at[half],
            x_whole.at[place_of(partner[0], partner[1], partner[3], half)],
            trade_send.at[half],
            trade_recv.at[half],
            partner,
        )
        for half in (0, 1)
    ]
    keeps = [
        pltpu.make_async_copy(x_own.at[half], x_whole.at[place_of(y, c, x, half)], trade_recv.at[half]) for half in (0, 1)
    ]

    @pl.when(moves)
    def _():
        for copy in trades:
            copy.start()

    @pl.when(jnp.logical_not(moves))
    def _():
        for copy in keeps:
            copy.start()

    spread = [
        remote(facts, facts_whole.at[row, z, x], fact_send.at[k], fact_recv.at[k], peer) for k, peer in enumerate(layer)
    ]
    kept = [pltpu.make_async_copy(facts, facts_whole.at[row, z, x], local.at[3])]
    for m, source in enumerate((w_query, w_key, w_value)):
        dst = w_qkv.at[row, z, pl.ds(pl.multiple_of(x * shard, shard), shard), pl.ds(m * owned, owned)]
        for k, peer in enumerate(layer):
            columns = pl.ds(pl.multiple_of((4 * peer[0] + 2 * peer[1] + peer[3]) * owned, owned), owned)
            spread.append(remote(source.at[:, columns], dst, w_send.at[m, k], w_recv.at[m, k], peer))
        columns = pl.ds(pl.multiple_of((4 * y + 2 * c + x) * owned, owned), owned)
        kept.append(pltpu.make_async_copy(source.at[:, columns], dst, local.at[m]))
    for copy in spread + kept:
        copy.start()

    gather = Gather(lambda half: x_whole.at[place_of(y, c, x, half)], x_whole, gather_send, gather_recv)
    for half in (0, 1):

        @pl.when(moves)
        def _():
            trades[half].wait_recv()

        @pl.when(jnp.logical_not(moves))
        def _():
            keeps[half].wait()

        gather.start(half)

    for copy in kept:
        copy.wait()
    for copy in spread:
        copy.wait_recv()
    chains = [
        Chain(facts_whole.at[:, z], lambda at: facts_whole.at[:, at], sems, 0),
        Chain(w_qkv.at[:, z], lambda at: w_qkv.at[:, at], sems, 1),
    ]

    def arrive(h):
        for chain in chains:
            chain.arrive(h)

    for chain in chains:
        chain.start()
    gather.pass_first()
    arrive(0)
    gather.pass_second()
    arrive(1)
    gather.pass_far()
    arrive(2)
    gather.finish()

    @pl.when(moves)
    def _():
        for copy in trades:
            copy.wait_send()

    for copy in spread:
        copy.wait_send()
    for chain in chains:
        chain.finish()


def anywhere():
    return pl.BlockSpec(memory_space=pl.ANY)


def in_vmem():
    return pl.BlockSpec(memory_space=pltpu.VMEM)


def dma(*shape):
    return pltpu.SemaphoreType.DMA(shape)


def remote_params(number):
    return pltpu.CompilerParams(collective_id=number, has_side_effects=True, vmem_limit_bytes=VMEM_LIMIT)


def begin(x_own, w_query, w_key, w_value, facts):
    block, width = x_own.shape
    shard = w_query.shape[0]
    x_whole, w_qkv, facts_whole = pl.pallas_call(
        begin_kernel,
        out_shape=(
            jax.ShapeDtypeStruct((8 * block, width), LOW),
            jax.ShapeDtypeStruct((4, 4, 2 * shard, 3 * width // 8), LOW),
            jax.ShapeDtypeStruct((4, 4, 2, *facts.shape), jnp.float32),
        ),
        in_specs=[in_vmem()] + [anywhere()] * 4,
        out_specs=[anywhere()] * 3,
        scratch_shapes=[
            dma(2), dma(2), dma(GATHER_COPIES), dma(GATHER_COPIES), dma(3, 7), dma(3, 7), dma(7), dma(7), dma(4), *chain_sems(2)
        ],
        compiler_params=remote_params(1),
        cost_estimate=pl.CostEstimate(flops=0, bytes_accessed=350_000_000, transcendentals=0),
    )(x_own.reshape(2, block // 2, width), w_query, w_key, w_value, facts)
    return x_whole, w_qkv.reshape(width, 3 * width // 8), facts_whole


def summed(total, landed, here):
    parts = (total[3, here, :], landed[0, here, :], landed[1, here, :])
    return sum(part.astype(jnp.float32) for part in parts)


def over_chunks(work):
    def step(i, carry):
        work(pl.ds(pl.multiple_of(i * CHUNK, CHUNK), CHUNK))
        return carry

    lax.fori_loop(0, TILE // CHUNK, step, 0)


def inverse_of(value):
    return lax.rsqrt(jnp.mean(value * value, axis=-1, keepdims=True) + EPSILON)


def close_attention_kernel(attended, w_out, x_own, gain, w_gate, w_up, resid, normed, own_gate, own_up, own, *scratch):
    scatter, (send, recv, local), sems = scratch[:7], scratch[7:10], scratch[10:]
    width = w_out.shape[1]
    hidden = w_gate.shape[1]
    z = lax.axis_index("z")
    barrier, count = greet_neighbours(near())
    pl.semaphore_wait(barrier, count)

    def slab_of(whole):
        return lambda at: whole.at[:, pl.ds(pl.multiple_of(at * hidden, hidden), hidden)]

    chains, kept = [], []
    for k, (part, whole) in enumerate(((w_gate, own_gate), (w_up, own_up))):
        chains.append(Chain(part, slab_of(whole), sems, k))
        chains[k].start()
        kept.append(pltpu.make_async_copy(part, slab_of(whole)(z), local.at[1 + k]))
        kept[k].start()

    def arrive(h):
        for chain in chains:
            chain.arrive(h)

    def produce(turn, y, c, x, out):
        at = place_of(y, c, x)

        def step(i, carry):
            columns = pl.ds(pl.multiple_of(i * TILE, TILE), TILE)
            out[:, columns] = dot_wide(attended[at, :], w_out[:, columns]).astype(LOW)
            return carry

        lax.fori_loop(0, width // TILE, step, 0)

    run_scatter(produce, *scatter, beside=lambda: arrive(0))
    total, landed = scatter[2], scatter[4]

    def chunk(here):
        value = x_own[here, :].astype(jnp.float32) + summed(total, landed, here)
        resid[here, :] = value
        own[here, :] = (value * inverse_of(value) * gain[...]).astype(LOW)

    over_chunks(chunk)
    run_gather(own, normed, send, recv, local.at[0], arrive)
    for chain in chains:
        chain.finish()
    for copy in kept:
        copy.wait()


def close_attention(attended, w_out, x_own, gain, w_gate, w_up):
    block, width = x_own.shape
    hidden = w_gate.shape[1]
    return pl.pallas_call(
        close_attention_kernel,
        out_shape=(
            jax.ShapeDtypeStruct((block, width), jnp.float32),
            jax.ShapeDtypeStruct((8 * block, width), LOW),
            jax.ShapeDtypeStruct((width, 4 * hidden), LOW),
            jax.ShapeDtypeStruct((width, 4 * hidden), LOW),
        ),
        in_specs=[in_vmem()] * 6,
        out_specs=[in_vmem()] + [anywhere()] * 3,
        scratch_shapes=[pltpu.VMEM((block, width), LOW)]
        + scatter_scratch(width)
        + [dma(GATHER_COPIES), dma(GATHER_COPIES), dma(3), *chain_sems(2)],
        compiler_params=remote_params(2),
        cost_estimate=pl.CostEstimate(flops=0, bytes_accessed=450_000_000, transcendentals=0),
    )(attended, w_out, x_own, gain, w_gate, w_up)


def norm_back(value, gain, upstream):
    inverse = inverse_of(value)
    scaled = upstream * gain
    inner = jnp.mean(scaled * value, axis=-1, keepdims=True)
    return inverse * scaled - value * (inverse * inverse * inverse) * inner, upstream * value * inverse


def fold_rows(total, terms):
    for first in range(0, CHUNK, 8):
        total[...] += terms[first : first + 8, :]


def close_mlp_kernel(
    d_gate, d_up, w_gate, w_up, resid, upstream, gain, grad, d_resid, gain_term, d_resid_whole, grad_parts, own, blocks, *scratch
):
    scatter, (send, recv, local, fetched, line_send, line_recv) = scratch[:7], scratch[7:]
    y, c, z, x = spot()
    width = w_gate.shape[0]
    order = [(r, k, q) for r, q in ((1 - y, 1 - x), (y, 1 - x), (1 - y, x), (y, x)) for k in (1 - c, c)]

    def fetch(turn):
        at = place_of(*order[turn])
        slot = turn % 2
        return [
            pltpu.make_async_copy(source.at[at], blocks.at[slot, m], fetched.at[slot, m])
            for m, source in enumerate((d_gate, d_up))
        ]

    for copy in fetch(0):
        copy.start()
    greet(near() + tuple(line_of()))
    to_layers = spread_columns(grad, grad_parts, line_send, line_recv)
    for copy in to_layers:
        copy.start()

    def produce(turn, to_y, to_c, to_x, out):
        if turn < 7:
            for copy in fetch(turn + 1):
                copy.start()
        for copy in fetch(turn):
            copy.wait()

        def step(i, carry):
            columns = pl.ds(pl.multiple_of(i * TILE, TILE), TILE)
            part = dot_nt(blocks[turn % 2, 0], w_gate[columns, :]) + dot_nt(blocks[turn % 2, 1], w_up[columns, :])
            out[:, columns] = part.astype(LOW)
            return carry

        lax.fori_loop(0, width // TILE, step, 0)

    run_scatter(produce, *scatter)
    total, landed = scatter[2], scatter[4]
    gain_term[...] = jnp.zeros_like(gain_term)

    def chunk(here):
        back, terms = norm_back(resid[here, :], gain[...], summed(total, landed, here))
        value = upstream[here, :].astype(jnp.float32) + back
        d_resid[here, :] = value
        own[here, :] = value.astype(LOW)
        fold_rows(gain_term, terms)

    over_chunks(chunk)
    run_gather(own, d_resid_whole, send, recv, local.at[0])
    for copy in to_layers:
        copy.wait()


def close_mlp(d_gate, d_up, w_gate, w_up, resid, upstream, gain, grad):
    block, width = resid.shape
    hidden = d_gate.shape[1]
    return pl.pallas_call(
        close_mlp_kernel,
        out_shape=(
            jax.ShapeDtypeStruct((block, width), jnp.float32),
            jax.ShapeDtypeStruct((8, width), jnp.float32),
            jax.ShapeDtypeStruct((8 * block, width), LOW),
            jax.ShapeDtypeStruct((3, width, hidden // 4), LOW),
        ),
        in_specs=[anywhere()] * 2 + [in_vmem()] * 5 + [anywhere()],
        out_specs=[in_vmem(), in_vmem(), anywhere(), anywhere()],
        scratch_shapes=[pltpu.VMEM((block, width), LOW), pltpu.VMEM((2, 2, block, hidden), LOW)]
        + scatter_scratch(width)
        + [dma(GATHER_COPIES), dma(GATHER_COPIES), dma(1), dma(2, 2), dma(3), dma(3)],
        compiler_params=remote_params(3),
        cost_estimate=pl.CostEstimate(flops=0, bytes_accessed=450_000_000, transcendentals=0),
    )(d_gate, d_up, w_gate, w_up, resid, upstream, gain, grad)


def close_layer_kernel(d_qkv, w_qkv, x_own, d_resid, gain, mlp_term, grad_low, gain_grads, own, terms, layer_terms, part, column_terms, *scratch):
    scatter, (send, recv, term_send, term_recv, line_send, line_recv) = scratch[:7], scratch[7:]
    y, c, z, x = spot()
    partner = partner_of(y, c, z, x)
    moves = z != 2 * c + y
    width = w_qkv.shape[0]
    barrier = pltpu.get_barrier_semaphore()

    @pl.when(moves)
    def _():
        pl.semaphore_signal(barrier, inc=1, device_id=partner, device_id_type=MESH_ID)

    layer = others()
    line = line_of()
    for peer in layer + line:
        pl.semaphore_signal(barrier, inc=1, device_id=peer, device_id_type=MESH_ID)
    pl.semaphore_wait(barrier, len(layer + line) + moves.astype(jnp.int32))

    def produce(turn, to_y, to_c, to_x, out):
        at = place_of(to_y, to_c, to_x)

        def step(i, carry):
            columns = pl.ds(pl.multiple_of(i * TILE, TILE), TILE)
            out[:, columns] = dot_nt(d_qkv[at, :], w_qkv[columns, :]).astype(LOW)
            return carry

        lax.fori_loop(0, width // TILE, step, 0)

    run_scatter(produce, *scatter)
    total, landed = scatter[2], scatter[4]
    terms[1] = mlp_term[...]
    terms[0] = jnp.zeros_like(mlp_term)
    trades = [
        remote(own.at[pl.ds(half * HALF, HALF)], grad_low.at[pl.ds(half * HALF, HALF)], send.at[half], recv.at[half], partner)
        for half in (0, 1)
    ]
    keeps = [
        pltpu.make_async_copy(own.at[pl.ds(half * HALF, HALF)], grad_low.at[pl.ds(half * HALF, HALF)], recv.at[half])
        for half in (0, 1)
    ]
    for half in (0, 1):

        def step(i, carry):
            here = pl.ds(pl.multiple_of(half * HALF + i * CHUNK, CHUNK), CHUNK)
            back, products = norm_back(x_own[here, :].astype(jnp.float32), gain[...], summed(total, landed, here))
            own[here, :] = (d_resid[here, :] + back).astype(LOW)
            fold_rows(terms.at[0], products)
            return carry

        lax.fori_loop(0, HALF // CHUNK, step, 0)

        @pl.when(moves)
        def _():
            trades[half].start()

        @pl.when(jnp.logical_not(moves))
        def _():
            keeps[half].start()

    def columns_of(row, layers):
        return pl.ds(pl.multiple_of((4 * row) * HD, HD), layers * HD)

    spread = [
        remote(terms.at[:, :, columns_of(2 * peer[0] + peer[1], 4)], layer_terms.at[k], term_send.at[k], term_recv.at[k], peer)
        for k, peer in enumerate(layer)
    ]
    for copy in spread:
        copy.start()
    for copy in spread:
        copy.wait_recv()
    part[...] = sum((layer_terms[k] for k in range(7)), terms[:, :, columns_of(2 * y + c, 4)])
    lines = [
        remote(
            part.at[:, :, pl.ds(pl.multiple_of(peer[2] * HD, HD), HD)], column_terms.at[k], line_send.at[k], line_recv.at[k], peer
        )
        for k, peer in enumerate(line)
    ]
    for copy in lines:
        copy.start()
    for copy in lines:
        copy.wait_recv()
    gain_grads[...] = sum((column_terms[k] for k in range(3)), part[:, :, pl.ds(pl.multiple_of(z * HD, HD), HD)])
    for copy in spread + lines:
        copy.wait_send()

    @pl.when(moves)
    def _():
        for copy in trades:
            copy.wait()

    @pl.when(jnp.logical_not(moves))
    def _():
        for copy in keeps:
            copy.wait()


def close_layer(d_qkv, w_qkv, x_own, d_resid, gain, mlp_term):
    block, width = x_own.shape
    return pl.pallas_call(
        close_layer_kernel,
        out_shape=(jax.ShapeDtypeStruct((block, width), LOW), jax.ShapeDtypeStruct((2, 8, width // 16), jnp.float32)),
        in_specs=[in_vmem()] * 6,
        out_specs=[anywhere(), in_vmem()],
        scratch_shapes=[
            pltpu.VMEM((block, width), LOW),
            pltpu.VMEM((2, 8, width), jnp.float32),
            pltpu.VMEM((7, 2, 8, width // 4), jnp.float32),
            pltpu.VMEM((2, 8, width // 4), jnp.float32),
            pltpu.VMEM((3, 2, 8, width // 16), jnp.float32),
        ]
        + scatter_scratch(width)
        + [dma(2), dma(2), dma(7), dma(7), dma(3), dma(3)],
        compiler_params=remote_params(4),
        cost_estimate=pl.CostEstimate(flops=0, bytes_accessed=350_000_000, transcendentals=0),
    )(d_qkv, w_qkv, x_own, d_resid, gain, mlp_term)


def doc_start(ends, place):
    start = jnp.zeros_like(place)
    for k in range(8):
        start = jnp.where(ends[k] <= place, ends[k], start)
    return jnp.where(place < ends[7], start, LEN)


def sigmoid_of(raw):
    return pl.reciprocal(1.0 + jnp.exp2(math.log2(LEN) - raw * (math.log2(math.e) / math.sqrt(HD))), approx=True)


def tile_at(index):
    return pl.ds(pl.multiple_of(index * TILE, TILE), TILE)


def head_of(array, rows, part, head):
    first = (part * (array.shape[1] // 3) // HD + head) * HD
    return array[rows, first : first + HD]


def attend_kernel(ends, qkv, upstream, out, upstream_whole, total, send, recv, local):
    i = pl.program_id(0)
    y, c, z, x = spot()
    heads = qkv.shape[1] // (3 * HD)
    gather = Gather(lambda half: upstream.at[pl.ds(half * HALF, HALF)], upstream_whole, send, recv)
    keep = pltpu.make_async_copy(upstream, upstream_whole.at[place_of(y, c, x)], local.at[0])

    @pl.when(i == 0)
    def _():
        greet(near())
        gather.start(0)
        gather.start(1)
        keep.start()

    @pl.when(i == 6)
    def _():
        gather.pass_first()

    total[...] = jnp.zeros_like(total)
    q_place = i * TILE + lax.broadcasted_iota(jnp.int32, (TILE, 1), 0)
    q_start = doc_start(ends, q_place)

    def tile(j, diagonal):
        k_place = j * TILE + lax.broadcasted_iota(jnp.int32, (1, TILE), 1)
        allowed = k_place >= q_start
        if diagonal:
            allowed = allowed & (k_place <= q_place)
        for head in range(heads):
            raw = dot_nt(head_of(qkv, tile_at(i), 0, head), head_of(qkv, tile_at(j), 1, head))
            weight = jnp.where(allowed, sigmoid_of(raw), 0.0).astype(LOW)
            total[head] += dot_wide(weight, head_of(qkv, tile_at(j), 2, head))

    def step(j, carry):
        tile(j, False)
        return carry

    lax.fori_loop(0, i, step, 0)
    tile(i, True)
    for head in range(heads):
        out[tile_at(i), head * HD : (head + 1) * HD] = total[head].astype(LOW)

    @pl.when(i == LEN // TILE - 1)
    def _():
        gather.pass_second()
        gather.pass_far()
        gather.finish()
        keep.wait()


def out_turns():
    y, c, z, x = spot()
    owners = [((y, c, 2 * x + j // 2, j % 2), (z == 2 * x + j // 2) & (x == j % 2)) for j in range(4)]
    holders = [((y, c, j, z // 2), (z == j) & (x == z // 2)) for j in range(4)]
    return owners, holders


def attend_back_kernel(
    ends, qkv, grads, up_grad, out_grad, out, up_parts, out_parts, query_total, key_total, value_total, line_send, line_recv, send, recv
):
    j = pl.program_id(0)
    y, c, z, x = spot()
    heads = qkv.shape[1] // (3 * HD)
    shard = out_grad.shape[0] // 4
    owners, holders = out_turns()
    to_layers = spread_columns(up_grad, up_parts, line_send, line_recv)

    def to_owner(turn):
        return remote(out_grad.at[pl.ds(turn * shard, shard)], out_parts.at[z], send.at[turn], recv.at[z], owners[turn][0])

    def to_self(turn):
        return pltpu.make_async_copy(out_grad.at[pl.ds(turn * shard, shard)], out_parts.at[z], recv.at[z])

    @pl.when(j == 0)
    def _():
        query_total[...] = jnp.zeros_like(query_total)
        barrier = pltpu.get_barrier_semaphore()
        for peer in line_of():
            pl.semaphore_signal(barrier, inc=1, device_id=peer, device_id_type=MESH_ID)
        for peer, here in holders:

            @pl.when(jnp.logical_not(here))
            def _():
                pl.semaphore_signal(barrier, inc=1, device_id=peer, device_id_type=MESH_ID)

        pl.semaphore_wait(barrier, 7 - (x == z // 2).astype(jnp.int32))
        for copy in to_layers:
            copy.start()
        for turn in range(4):

            @pl.when(jnp.logical_not(owners[turn][1]))
            def _():
                to_owner(turn).start()

            @pl.when(owners[turn][1])
            def _():
                to_self(turn).start()

    key_total[...] = jnp.zeros_like(key_total)
    value_total[...] = jnp.zeros_like(value_total)
    here = tile_at(j)
    k_place = j * TILE + lax.broadcasted_iota(jnp.int32, (TILE, 1), 0)
    turned = [head_of(qkv, here, 1, head).T for head in range(heads)]

    def tile(i, diagonal):
        q_place = i * TILE + lax.broadcasted_iota(jnp.int32, (1, TILE), 1)
        allowed = k_place >= doc_start(ends, q_place)
        if diagonal:
            allowed = allowed & (k_place <= q_place)
        for head in range(heads):
            query, grad = head_of(qkv, tile_at(i), 0, head), grads[tile_at(i), head * HD : (head + 1) * HD]
            sig = jnp.where(allowed, sigmoid_of(dot_nt(head_of(qkv, here, 1, head), query)), 0.0)
            value_total[head] += dot_wide(sig.astype(LOW), grad)
            d_score = (dot_nt(head_of(qkv, here, 2, head), grad) * (sig * (1.0 - sig))).astype(LOW)
            key_total[head] += dot_wide(d_score, query)
            query_total[head, :, tile_at(i)] += dot_wide(turned[head], d_score)

    def step(i, carry):
        tile(i, False)
        return carry

    tile(j, True)
    lax.fori_loop(j + 1, LEN // TILE, step, 0)
    scale = 1.0 / math.sqrt(HD)
    for head in range(heads):
        first = head * HD
        out[here, heads * HD + first : (heads + 1) * HD + first] = (key_total[head] * scale).astype(LOW)
        out[here, 2 * heads * HD + first : (2 * heads + 1) * HD + first] = value_total[head].astype(LOW)
        out[here, first : first + HD] = (query_total[head, :, here] * scale).T.astype(LOW)

    @pl.when(j == LEN // TILE - 1)
    def _():
        for copy in to_layers:
            copy.wait()
        for turn in range(4):

            @pl.when(jnp.logical_not(owners[turn][1]))
            def _():
                to_owner(turn).wait_send()

            @pl.when(jnp.logical_not(holders[turn][1]))
            def _():
                landed = out_parts.at[turn]
                remote(landed, landed, send.at[turn], recv.at[turn], holders[turn][0]).wait_recv()

            @pl.when(owners[turn][1])
            def _():
                to_self(turn).wait()


def attend(ends, qkv, upstream):
    places, width = qkv.shape
    heads = width // (3 * HD)
    whole = lambda columns: pl.BlockSpec((places, columns), lambda i: (0, 0))
    return pl.pallas_call(
        attend_kernel,
        out_shape=(
            jax.ShapeDtypeStruct((places, width // 3), LOW),
            jax.ShapeDtypeStruct((places, upstream.shape[1]), LOW),
        ),
        grid=(places // TILE,),
        in_specs=[
            pl.BlockSpec(memory_space=pltpu.SMEM),
            whole(width),
            pl.BlockSpec(upstream.shape, lambda i: (0, 0)),
        ],
        out_specs=[whole(width // 3), anywhere()],
        scratch_shapes=[pltpu.VMEM((heads, TILE, HD), jnp.float32), dma(GATHER_COPIES), dma(GATHER_COPIES), dma(1)],
        compiler_params=remote_params(5),
        cost_estimate=pl.CostEstimate(flops=0, bytes_accessed=200_000_000, transcendentals=0),
    )(ends, qkv, upstream)


def attend_back(ends, qkv, grads, up_grad, out_grad):
    places, width = qkv.shape
    heads = width // (3 * HD)
    whole = lambda columns: pl.BlockSpec((places, columns), lambda j: (0, 0))
    return pl.pallas_call(
        attend_back_kernel,
        out_shape=(
            jax.ShapeDtypeStruct((places, width), LOW),
            jax.ShapeDtypeStruct((3, up_grad.shape[0], up_grad.shape[1] // 4), LOW),
            jax.ShapeDtypeStruct((4, out_grad.shape[0] // 4, out_grad.shape[1]), LOW),
        ),
        grid=(places // TILE,),
        in_specs=[pl.BlockSpec(memory_space=pltpu.SMEM), whole(width), whole(width // 3), anywhere(), anywhere()],
        out_specs=[whole(width), anywhere(), anywhere()],
        scratch_shapes=[
            pltpu.VMEM((heads, HD, places), jnp.float32),
            pltpu.VMEM((heads, TILE, HD), jnp.float32),
            pltpu.VMEM((heads, TILE, HD), jnp.float32),
            dma(3),
            dma(3),
            dma(4),
            dma(4),
        ],
        compiler_params=remote_params(6),
        cost_estimate=pl.CostEstimate(flops=0, bytes_accessed=300_000_000, transcendentals=0),
    )(ends, qkv, grads, up_grad, out_grad)


LAYER = ("y", "c", "x")
PLACES = ("c", "y", "x")
ALL = ("y", "c", "z", "x")


def scatter_layer(whole):
    return lax.psum_scatter(whole.astype(LOW), PLACES, scatter_dimension=0, tiled=True).astype(jnp.float32)


def trade(part):
    pairs = []
    for y in range(2):
        for c in range(2):
            for z in range(4):
                for x in range(2):
                    pairs.append((((y * 2 + c) * 4 + z) * 2 + x, (((z % 2) * 2 + z // 2) * 4 + 2 * c + y) * 2 + x))
    return lax.ppermute(part, ALL, pairs)


def after(first, then):
    return lax.optimization_barrier((first, then))[1]


def body_layers(
    tokens, lengths, cotangent, w_query, w_key, w_value, w_out, w_gate, w_up, w_down, gain_attn, gain_mlp
):
    rows_here, block, width = tokens.shape
    members = lax.axis_size(LAYER)
    layers = lax.axis_size("z")
    shard = w_query.shape[0]
    owned = width // members
    facts = jnp.zeros((8, 2 * shard), jnp.float32)
    facts = facts.at[0, :shard].set(gain_attn.astype(jnp.float32)).at[1, :shard].set(gain_mlp.astype(jnp.float32))
    facts = facts.at[2, : lengths.shape[1]].set(lengths[0].astype(jnp.float32))
    layer_x, w_qkv, facts = begin(tokens.reshape(block, width), w_query, w_key, w_value, facts)
    full_gain_attn, full_gain_mlp = facts[:, :, :, 0, :shard].reshape(1, width), facts[:, :, :, 1, :shard].reshape(1, width)
    layer = lax.axis_index("z")
    own_lengths = facts[:, 0, 0, 2, : lengths.shape[1]].reshape(2, 2, -1)
    own_lengths = lax.dynamic_slice(own_lengths, (layer % 2, layer // 2, 0), (1, 1, own_lengths.shape[2]))[0, 0]
    ends = jnp.cumsum(own_lengths.astype(jnp.int32))
    place = (4 * lax.axis_index("c") + 2 * lax.axis_index("y") + lax.axis_index("x")) * block
    x_own = lax.dynamic_slice_in_dim(layer_x, place, block, 0)
    layer_normed = norm_forward(layer_x.astype(jnp.float32), full_gain_attn)[0].astype(LOW)
    out_rows = lax.all_gather(after(facts, w_out), ("z", "x"), axis=0, tiled=True)
    w_out_own = lax.dynamic_slice_in_dim(out_rows, lax.axis_index("x") * owned, owned, 0)

    qkv = dot_wide(layer_normed, w_qkv).astype(LOW)
    upstream = trade(after(facts, cotangent)).reshape(block, width)
    attended, layer_upstream = attend(ends, qkv, upstream)
    resid, layer_mlp, own_gate, own_up = close_attention(attended, w_out_own, x_own, full_gain_mlp, w_gate, w_up)

    own_down = lax.all_gather(after(resid, w_down), "z", axis=0, tiled=True)
    gate = dot_wide(layer_mlp, own_gate)
    up_part = dot_wide(layer_mlp, own_up)
    sigmoid_gate = jax.nn.sigmoid(gate)
    hidden = (gate * sigmoid_gate * up_part).astype(LOW)
    down_term = contract_rows(hidden, layer_upstream).astype(LOW)
    d_hidden = contract_cols(layer_upstream, own_down)
    d_gate, d_up = gate_backward(d_hidden, gate, up_part, sigmoid_gate)
    gate_term, up_term = contract_rows(layer_mlp, d_gate).astype(LOW), contract_rows(layer_mlp, d_up).astype(LOW)

    grad_down = lax.psum_scatter(down_term, "z", scatter_dimension=0, tiled=True)
    d_resid, gain_mlp_term, layer_d_resid, gate_parts = close_mlp(
        after((up_term, grad_down), d_gate), d_up, own_gate, own_up, resid, upstream, full_gain_mlp, gate_term
    )

    def own_part(whole, parts):
        own = lax.dynamic_slice_in_dim(whole, layer * parts.shape[2], parts.shape[2], 1)
        return own.astype(jnp.float32) + jnp.sum(parts.astype(jnp.float32), axis=0)

    result = resid + scatter_layer(dot_wide(after(d_resid, hidden), own_down))
    mixed = trade(result.astype(LOW).reshape(rows_here, block, width))

    out_term = contract_rows(attended, layer_d_resid).astype(LOW)
    d_attended = contract_cols(layer_d_resid, w_out_own).astype(LOW)
    d_qkv, up_parts, out_parts = attend_back(ends, qkv, d_attended, up_term, out_term)
    grad_gate, grad_up = own_part(gate_term, gate_parts), own_part(up_term, up_parts)
    grad_out = jnp.sum(out_parts.astype(jnp.float32), axis=0)
    qkv_term = contract_rows(layer_normed, d_qkv).astype(LOW)
    grad_low, gain_grads = close_layer(
        after(qkv_term, d_qkv), w_qkv, x_own, d_resid, full_gain_attn, gain_mlp_term
    )
    grad_tokens = grad_low.astype(jnp.float32).reshape(rows_here, block, width)

    qkv_term = qkv_term.reshape(4, layers, 2 * shard, 3 * owned).transpose(1, 0, 2, 3)
    qkv_term = qkv_term.reshape(layers * members * shard, 3 * owned)
    qkv_term = lax.psum_scatter(qkv_term, "z", scatter_dimension=0, tiled=True)
    qkv_term = lax.all_to_all(qkv_term.reshape(members, shard, 3 * owned), LAYER, 0, 0)
    qkv_term = qkv_term.reshape(members, shard, 3, owned).transpose(2, 1, 0, 3).astype(jnp.float32)
    grad_query, grad_key, grad_value = qkv_term.reshape(3, shard, width)
    gain_grads = lax.dynamic_index_in_dim(jnp.sum(gain_grads, axis=1).reshape(2, 2, shard), lax.axis_index("x"), 1, False)
    return (
        mixed,
        grad_tokens,
        grad_query,
        grad_key,
        grad_value,
        grad_out,
        grad_gate,
        grad_up,
        grad_down.astype(jnp.float32),
        gain_grads[0],
        gain_grads[1],
    )


def body_any(
    tokens,
    lengths,
    cotangent,
    w_query,
    w_key,
    w_value,
    w_out,
    w_gate,
    w_up,
    w_down,
    gain_attn,
    gain_mlp,
):
    rows_here, block, width = tokens.shape
    count = rows_here * block
    scale = 1.0 / math.sqrt(HD)
    kv_place = lax.axis_index("kv")
    key_places = kv_place * block + jnp.arange(block, dtype=jnp.int32)
    attn_set = (
        lax.all_gather(w_query, ("row", "kv"), axis=0, tiled=True),
        lax.all_gather(w_key, ("row", "kv"), axis=0, tiled=True),
        lax.all_gather(w_value, ("row", "kv"), axis=0, tiled=True),
        lax.all_gather(w_out, ("row", "kv"), axis=0, tiled=True),
        lax.all_gather(gain_attn, ("row", "kv"), axis=0, tiled=True),
        lax.all_gather(gain_mlp, ("row", "kv"), axis=0, tiled=True),
    )
    full_query, full_key, full_value, full_out, full_gain_attn, full_gain_mlp = attn_set
    flat = tokens.reshape(count, width).astype(jnp.float32)
    normed_attn, inverse_attn = norm_forward(flat, full_gain_attn)
    normed_attn_low = normed_attn.astype(jnp.bfloat16)
    query_low = jnp.dot(normed_attn_low, full_query, preferred_element_type=jnp.float32).astype(
        jnp.bfloat16
    )
    key_low = jnp.dot(normed_attn_low, full_key, preferred_element_type=jnp.float32).astype(
        jnp.bfloat16
    )
    value_low = jnp.dot(normed_attn_low, full_value, preferred_element_type=jnp.float32).astype(
        jnp.bfloat16
    )
    key_heads = key_low.reshape(rows_here, block, H, HD)
    value_heads = value_low.reshape(rows_here, block, H, HD)
    segment, valid = segment_table(lengths)
    key_segment = lax.dynamic_slice_in_dim(segment, kv_place * block, block, 1)
    key_valid = lax.dynamic_slice_in_dim(valid, kv_place * block, block, 1)
    queries_all = lax.all_gather(
        query_low.reshape(rows_here, block, width), "kv", axis=1, tiled=True
    )
    which = 0
    query_rows = queries_all[which]
    query_segment = segment[which]
    sigmoid_part, allowed = score_block(
        query_rows,
        key_heads[which],
        query_segment,
        key_segment[which],
        key_valid[which],
        jnp.int32(0),
        key_places,
    )
    weight = (sigmoid_part * allowed).astype(jnp.bfloat16)
    summed = jnp.einsum(
        "hqk,khd->qhd", weight, value_heads[which], preferred_element_type=jnp.float32
    )
    pieces = [
        lax.psum_scatter(
            summed.reshape(lax.axis_size("kv") * block, width).astype(jnp.bfloat16),
            "kv",
            scatter_dimension=0,
            tiled=True,
        ).astype(jnp.float32)
    ]
    attended_low = jnp.stack(pieces).reshape(count, width).astype(jnp.bfloat16)
    resid = flat + jnp.dot(attended_low, full_out, preferred_element_type=jnp.float32)
    normed_mlp, inverse_mlp = norm_forward(resid, full_gain_mlp)
    normed_mlp_low = normed_mlp.astype(jnp.bfloat16)
    upstream_low = cotangent.reshape(count, width)
    upstream = upstream_low.astype(jnp.float32)
    slice_gate, slice_up, slice_down = (
        lax.all_gather(w_gate, "row", axis=1, tiled=True),
        lax.all_gather(w_up, "row", axis=1, tiled=True),
        lax.all_gather(w_down, "row", axis=0, tiled=True),
    )
    row_normed, row_upstream = (
        lax.all_gather(normed_mlp_low.reshape(rows_here, block, width), "kv", axis=1, tiled=True),
        lax.all_gather(cotangent, "kv", axis=1, tiled=True),
    )
    normed_rows = row_normed.reshape(rows_here * LEN, width)
    upstream_rows = row_upstream.reshape(rows_here * LEN, width)
    gate = jnp.dot(normed_rows, slice_gate, preferred_element_type=jnp.float32)
    up_part = jnp.dot(normed_rows, slice_up, preferred_element_type=jnp.float32)
    sigmoid_gate = jax.nn.sigmoid(gate)
    hidden_low = (gate * sigmoid_gate * up_part).astype(jnp.bfloat16)
    hidden_rows = hidden_low.reshape(rows_here, LEN, hidden_low.shape[1])
    which = 0
    hidden_part = hidden_rows[which]
    outputs = [
        lax.psum_scatter(
            jnp.dot(hidden_part, slice_down, preferred_element_type=jnp.float32).astype(
                jnp.bfloat16
            ),
            "kv",
            scatter_dimension=0,
            tiled=True,
        ).astype(jnp.float32)
    ]
    result = resid + jnp.stack(outputs).reshape(count, width)
    d_hidden = contract_cols(upstream_rows, slice_down)
    d_gate, d_up = gate_backward(d_hidden, gate, up_part, sigmoid_gate)
    partial_normed = contract_cols(d_gate, slice_gate) + contract_cols(d_up, slice_up)
    d_normed_mlp = (
        lax.psum_scatter(
            partial_normed.reshape(rows_here, LEN, width).astype(jnp.bfloat16),
            "kv",
            scatter_dimension=1,
            tiled=True,
        )
        .astype(jnp.float32)
        .reshape(count, width)
    )
    grad_gate, grad_up, grad_down = (
        lax.psum_scatter(
            contract_rows(normed_rows, d_gate).astype(jnp.bfloat16),
            "row",
            scatter_dimension=1,
            tiled=True,
        ).astype(jnp.float32),
        lax.psum_scatter(
            contract_rows(normed_rows, d_up).astype(jnp.bfloat16),
            "row",
            scatter_dimension=1,
            tiled=True,
        ).astype(jnp.float32),
        lax.psum_scatter(
            contract_rows(hidden_low, upstream_rows).astype(jnp.bfloat16),
            "row",
            scatter_dimension=0,
            tiled=True,
        ).astype(jnp.float32),
    )
    mixed = result.astype(jnp.bfloat16).reshape(rows_here, block, width)
    back_mlp, gain_mlp_term = norm_backward(resid, inverse_mlp, full_gain_mlp, d_normed_mlp)
    d_resid = upstream + back_mlp
    d_resid_low = d_resid.astype(jnp.bfloat16)
    d_attended = contract_cols(d_resid_low, full_out).astype(jnp.bfloat16)
    grads_all = lax.all_gather(
        d_attended.reshape(rows_here, block, width), "kv", axis=1, tiled=True
    )
    query_block = min(512, LEN)
    block_count = LEN // query_block
    which = 0

    def sweep(carry, index, which=which):
        key_total, value_total = carry
        start = index * query_block
        query_rows = lax.dynamic_slice_in_dim(queries_all[which], start, query_block, 0)
        grad_rows = lax.dynamic_slice_in_dim(grads_all[which], start, query_block, 0)
        query_segment = lax.dynamic_slice_in_dim(segment[which], start, query_block, 0)
        sigmoid_part, allowed = score_block(
            query_rows,
            key_heads[which],
            query_segment,
            key_segment[which],
            key_valid[which],
            start,
            key_places,
        )
        weight = (sigmoid_part * allowed).astype(jnp.bfloat16)
        grad_heads = grad_rows.reshape(query_block, H, HD)
        value_total = value_total + jnp.einsum(
            "hqk,qhd->khd", weight, grad_heads, preferred_element_type=jnp.float32
        )
        d_weight = jnp.einsum(
            "qhd,khd->hqk", grad_heads, value_heads[which], preferred_element_type=jnp.float32
        )
        d_score = (d_weight * sigmoid_part * (1.0 - sigmoid_part) * allowed).astype(jnp.bfloat16)
        query_part = (
            jnp.einsum(
                "hqk,khd->qhd", d_score, key_heads[which], preferred_element_type=jnp.float32
            )
            * scale
        )
        key_total = (
            key_total
            + jnp.einsum(
                "hqk,qhd->khd",
                d_score,
                query_rows.reshape(query_block, H, HD),
                preferred_element_type=jnp.float32,
            )
            * scale
        )
        return ((key_total, value_total), query_part.reshape(query_block, width))

    zeros = jnp.zeros((block, H, HD), jnp.float32)
    totals, query_parts = lax.scan(sweep, (zeros, zeros), jnp.arange(block_count, dtype=jnp.int32))
    query_terms = [query_parts.reshape(LEN, width)]
    key_grads = [totals[0].reshape(block, width)]
    value_grads = [totals[1].reshape(block, width)]
    query_local = lax.psum_scatter(
        jnp.stack(query_terms).astype(jnp.bfloat16), "kv", scatter_dimension=1, tiled=True
    ).astype(jnp.float32)
    d_query_low = query_local.reshape(count, width).astype(jnp.bfloat16)
    d_key_low = jnp.stack(key_grads).reshape(count, width).astype(jnp.bfloat16)
    d_value_low = jnp.stack(value_grads).reshape(count, width).astype(jnp.bfloat16)
    d_normed_attn = (
        contract_cols(d_query_low, full_query)
        + contract_cols(d_key_low, full_key)
        + contract_cols(d_value_low, full_value)
    )
    back_attn, gain_attn_term = norm_backward(flat, inverse_attn, full_gain_attn, d_normed_attn)
    grad_tokens = (d_resid + back_attn).reshape(rows_here, block, width)
    projected_low = jnp.concatenate((d_query_low, d_key_low, d_value_low), axis=1)
    grad_projections = lax.psum_scatter(
        contract_rows(normed_attn_low, projected_low),
        ("row", "kv"),
        scatter_dimension=0,
        tiled=True,
    )
    out_term = contract_rows(attended_low, d_resid_low)
    grad_out, grad_gain_attn, grad_gain_mlp = (
        lax.psum_scatter(out_term, ("row", "kv"), scatter_dimension=0, tiled=True),
        lax.psum_scatter(gain_attn_term, ("row", "kv"), scatter_dimension=0, tiled=True),
        lax.psum_scatter(gain_mlp_term, ("row", "kv"), scatter_dimension=0, tiled=True),
    )
    grad_query = grad_projections[:, :width]
    grad_key = grad_projections[:, width : 2 * width]
    grad_value = grad_projections[:, 2 * width :]
    return (
        mixed,
        grad_tokens,
        grad_query,
        grad_key,
        grad_value,
        grad_out,
        grad_gate,
        grad_up,
        grad_down,
        grad_gain_attn,
        grad_gain_mlp,
    )


def solution(mesh):
    rows, columns = mesh.shape["row"], mesh.shape["kv"]
    if rows == 4 and columns == 2 * rows:
        mesh = Mesh(mesh.devices.reshape(2, 2, rows, 2), ("y", "c", "z", "x"))
        row, kv, run = ("y", "c"), ("z", "x"), body_layers
    else:
        row, kv, run = "row", "kv", body_any
    both = ("y", "c", "z", "x") if run is body_layers else ("row", "kv")
    tall, wide, flat = P(both, None), P(None, both), P(both)
    tokens = P(row, kv, None)
    return jax.shard_map(
        run,
        mesh=mesh,
        in_specs=(tokens, P(row, None), tokens, tall, tall, tall, tall, wide, wide, tall, flat, flat),
        out_specs=(tokens, tokens, tall, tall, tall, tall, wide, wide, tall, flat, flat),
        check_vma=False,
    )
```

```python
import functools
import math

import jax
import jax.numpy as jnp
from jax import lax
from jax.experimental import pallas as pl
from jax.experimental.pallas import tpu as pltpu
from jax.sharding import Mesh, PartitionSpec as P

H = 16
HD = 128
LEN = 4096


EPSILON = 1e-05


def contract_rows(left, right):
    return lax.dot_general(
        left, right, (((0,), (0,)), ((), ())), preferred_element_type=jnp.float32
    )


def contract_cols(left, right):
    return lax.dot_general(
        left, right, (((1,), (1,)), ((), ())), preferred_element_type=jnp.float32
    )


def norm_forward(value, gain):
    inverse = lax.rsqrt(jnp.mean(value * value, axis=-1, keepdims=True) + EPSILON)
    return (value * inverse * gain.astype(jnp.float32), inverse)


def norm_backward(value, inverse, gain, upstream):
    scaled = upstream * gain.astype(jnp.float32)
    inner = jnp.mean(scaled * value, axis=-1, keepdims=True)
    back = inverse * scaled - value * (inverse * inverse * inverse) * inner
    gain_term = jnp.sum(upstream * value * inverse, axis=0)
    return (back, gain_term)


def segment_table(lengths):
    ends = jnp.cumsum(lengths, axis=-1)
    places = jnp.arange(LEN, dtype=jnp.int32)
    segment = jnp.sum((ends[:, None, :] <= places[None, :, None]).astype(jnp.int32), axis=-1)
    valid = places[None, :] < ends[:, -1:]
    return (segment, valid)


def score_block(
    query_rows, key_heads, query_segment, key_segment, key_valid, query_start, key_places
):
    count = query_rows.shape[0]
    query_heads = query_rows.reshape(count, H, HD)
    raw = jnp.einsum("qhd,khd->hqk", query_heads, key_heads, preferred_element_type=jnp.float32)
    scores = raw * (1.0 / math.sqrt(HD)) - math.log(LEN)
    places = query_start + jnp.arange(count, dtype=jnp.int32)
    allowed = (
        (key_places[None, :] <= places[:, None])
        & (key_segment[None, :] == query_segment[:, None])
        & key_valid[None, :]
    )
    return (jax.nn.sigmoid(scores), allowed.astype(jnp.float32)[None])


def gate_backward(d_hidden, gate, up_part, sigmoid_gate):
    d_gate = (d_hidden * up_part * sigmoid_gate * (1.0 + gate * (1.0 - sigmoid_gate))).astype(
        jnp.bfloat16
    )
    d_up = (d_hidden * gate * sigmoid_gate).astype(jnp.bfloat16)
    return (d_gate, d_up)


TILE = 512
LOW = jnp.bfloat16
VMEM_LIMIT = 60 * 1024 * 1024


def dot_nt(left, right):
    return lax.dot_general(left, right, (((1,), (1,)), ((), ())), preferred_element_type=jnp.float32)


def dot_wide(left, right):
    return jnp.dot(left, right, preferred_element_type=jnp.float32)


HALF = TILE // 2
CHUNK = 32
MESH_ID = pl.DeviceIdType.MESH


def flip(bit, by):
    return bit + by - 2 * bit * by


def spot():
    return tuple(lax.axis_index(name) for name in ("y", "c", "z", "x"))


def near():
    y, c, z, x = spot()
    return (y, c, z, 1 - x), (1 - y, c, z, x), (y, 1 - c, z, x)


def partner_of(y, c, z, x):
    return lax.rem(z, 2), z // 2, 2 * c + y, x


def place_of(y, c, x, half=None):
    first = (4 * c + 2 * y + x) * TILE
    if half is None:
        return pl.ds(pl.multiple_of(first, TILE), TILE)
    return pl.ds(pl.multiple_of(first + half * HALF, HALF), HALF)


def remote(src, dst, send, recv, peer):
    return pltpu.make_async_remote_copy(
        src_ref=src, dst_ref=dst, send_sem=send, recv_sem=recv, device_id=peer, device_id_type=MESH_ID
    )


def greet(peers):
    barrier = pltpu.get_barrier_semaphore()
    for peer in peers:
        pl.semaphore_signal(barrier, inc=1, device_id=peer, device_id_type=MESH_ID)
    pl.semaphore_wait(barrier, len(peers))


class Gather:
    def __init__(self, own, whole, send, recv):
        y, c, z, x = spot()
        across_x, across_y, core = near()

        def from_own(k, half, peer):
            return remote(own(half), whole.at[place_of(y, c, x, half)], send.at[k], recv.at[k], peer)

        def passed(k, at, peer):
            return remote(whole.at[at], whole.at[at], send.at[k], recv.at[k], peer)

        self.mine = [
            [from_own(0, 0, across_x), from_own(1, 0, across_y), from_own(2, 0, core)],
            [from_own(3, 1, across_x), from_own(4, 1, across_y), from_own(5, 1, core)],
        ]
        held_x = [place_of(y, c, 1 - x, half) for half in (0, 1)]
        held_y = [place_of(1 - y, c, x, half) for half in (0, 1)]
        far = [place_of(1 - y, c, 1 - x, half) for half in (0, 1)]
        self.over_y, self.over_x = passed(6, held_x[0], across_y), passed(7, held_y[1], across_x)
        self.core_x = [passed(8 + half, held_x[half], core) for half in (0, 1)]
        self.core_y = [passed(10 + half, held_y[half], core) for half in (0, 1)]
        self.core_far = [passed(12 + half, far[half], core) for half in (0, 1)]

    def start(self, half):
        for copy in self.mine[half]:
            copy.start()

    def pass_first(self):
        self.mine[0][0].wait_recv()
        self.over_y.start()
        self.core_x[0].start()
        self.mine[0][1].wait_recv()
        self.core_y[0].start()

    def pass_second(self):
        self.mine[1][1].wait_recv()
        self.over_x.start()
        self.core_y[1].start()
        self.mine[1][0].wait_recv()
        self.core_x[1].start()

    def pass_far(self):
        self.over_y.wait_recv()
        self.core_far[0].start()
        self.over_x.wait_recv()
        self.core_far[1].start()

    def finish(self):
        from_core = [self.mine[0][2], self.mine[1][2]] + self.core_x + self.core_y + self.core_far
        for copy in from_core:
            copy.wait_recv()
        for copy in self.mine[0] + self.mine[1] + [self.over_y, self.over_x] + self.core_x + self.core_y + self.core_far:
            copy.wait_send()


GATHER_COPIES = 14


def run_gather(own, whole, send, recv, local, beside=lambda h: None):
    y, c, z, x = spot()
    keep = pltpu.make_async_copy(own, whole.at[place_of(y, c, x)], local)
    keep.start()
    gather = Gather(lambda half: own.at[pl.ds(half * HALF, HALF)], whole, send, recv)
    gather.start(0)
    gather.start(1)
    gather.pass_first()
    beside(1)
    gather.pass_second()
    gather.pass_far()
    gather.finish()
    beside(2)
    keep.wait()


class Chain:
    def __init__(self, own, slab, sems, index):
        self.own, self.slab, self.sems, self.index = own, slab, sems, index
        self.last = lax.axis_size("z") - 1

    def move(self, which, h, source, layer, to):
        y, c, z, x = spot()
        return remote(
            source, self.slab(layer), self.sems[2 * which].at[self.index, h], self.sems[2 * which + 1].at[self.index, h], (y, c, to, x)
        )

    def up(self, h):
        z = lax.axis_index("z")
        return self.move(0, h, self.own if h == 0 else self.slab(z - h), z - h, z + 1)

    def down(self, h):
        z = lax.axis_index("z")
        return self.move(1, h, self.own if h == 0 else self.slab(z + h), z + h, z - 1)

    def start(self):
        z = lax.axis_index("z")

        @pl.when(z < self.last)
        def _():
            self.up(0).start()

        @pl.when(z > 0)
        def _():
            self.down(0).start()

    def arrive(self, h):
        z = lax.axis_index("z")

        @pl.when(z - h - 1 >= 0)
        def _():
            self.move(0, h, self.slab(z - h - 1), z - h - 1, z).wait_recv()
            if h < 2:

                @pl.when(z < self.last)
                def _():
                    self.up(h + 1).start()

        @pl.when(z + h + 1 <= self.last)
        def _():
            self.move(1, h, self.slab(z + h + 1), z + h + 1, z).wait_recv()
            if h < 2:

                @pl.when(z > 0)
                def _():
                    self.down(h + 1).start()

    def finish(self):
        z = lax.axis_index("z")
        for h in range(3):

            @pl.when((z < self.last) & (z - h >= 0))
            def _():
                self.up(h).wait_send()

            @pl.when((z > 0) & (z + h <= self.last))
            def _():
                self.down(h).wait_send()


def chain_sems(count):
    return [pltpu.SemaphoreType.DMA((count, 3)) for _ in range(4)]


def greet_neighbours(peers):
    y, c, z, x = spot()
    last = lax.axis_size("z") - 1
    barrier = pltpu.get_barrier_semaphore()
    for peer in peers:
        pl.semaphore_signal(barrier, inc=1, device_id=peer, device_id_type=MESH_ID)

    @pl.when(z > 0)
    def _():
        pl.semaphore_signal(barrier, inc=1, device_id=(y, c, z - 1, x), device_id_type=MESH_ID)

    @pl.when(z < last)
    def _():
        pl.semaphore_signal(barrier, inc=1, device_id=(y, c, z + 1, x), device_id_type=MESH_ID)

    return barrier, len(peers) + (z > 0).astype(jnp.int32) + (z < last).astype(jnp.int32)


def others():
    y, c, z, x = spot()
    return [(flip(y, dy), flip(c, dc), z, flip(x, dx)) for dy in (0, 1) for dc in (0, 1) for dx in (0, 1) if dy + dc + dx]


def line_of():
    y, c, z, x = spot()
    return [(y, c, lax.rem(z + dz, 4), x) for dz in (1, 2, 3)]


def spread_columns(whole, parts, send, recv):
    size = whole.shape[1] // 4
    return [
        remote(
            whole.at[:, pl.ds(pl.multiple_of(peer[2] * size, size), size)], parts.at[k], send.at[k], recv.at[k], peer
        )
        for k, peer in enumerate(line_of())
    ]


def add_rows(total, first, term, start, count):
    def step(i, carry):
        here = pl.ds(pl.multiple_of(first + i * CHUNK, CHUNK), CHUNK)
        there = pl.ds(pl.multiple_of(start + i * CHUNK, CHUNK), CHUNK)
        total[here, :] = (total[here, :].astype(jnp.float32) + term[there, :].astype(jnp.float32)).astype(LOW)
        return carry

    lax.fori_loop(0, count // CHUNK, step, 0)


def scatter_scratch(width):
    return [
        pltpu.VMEM((2, TILE, width), LOW),
        pltpu.VMEM((4, TILE, width), LOW),
        pltpu.VMEM((4, TILE, width), LOW),
        pltpu.VMEM((2, HALF, width), LOW),
        pltpu.VMEM((2, TILE, width), LOW),
        pltpu.SemaphoreType.DMA((10,)),
        pltpu.SemaphoreType.DMA((10,)),
    ]


def run_scatter(produce, staged, core_part, total, relayed, landed, send, recv, beside=lambda: None):
    y, c, z, x = spot()
    across_x, across_y, core = near()
    dests = ((1 - y, 1 - x), (y, 1 - x), (1 - y, x), (y, x))
    first, second = pl.ds(0, HALF), pl.ds(HALF, HALF)
    to_core = [
        remote(staged.at[k % 2], core_part.at[k], send.at[k], recv.at[k], core) for k in range(4)
    ]
    far_x = remote(total.at[0, first], relayed.at[0], send.at[4], recv.at[4], across_x)
    far_y = remote(total.at[0, second], relayed.at[1], send.at[5], recv.at[5], across_y)
    to_x = [
        remote(total.at[1, at], landed.at[0, at], send.at[6 + half], recv.at[6 + half], across_x)
        for half, at in enumerate((first, second))
    ]
    to_y = [
        remote(total.at[2, at], landed.at[1, at], send.at[8 + half], recv.at[8 + half], across_y)
        for half, at in enumerate((first, second))
    ]
    for k, (to_row, to_column) in enumerate(dests):
        if k >= 2:
            to_core[k - 2].wait_send()
        produce(2 * k, to_row, 1 - c, to_column, staged.at[k % 2])
        to_core[k].start()
        produce(2 * k + 1, to_row, c, to_column, total.at[k])
        to_core[k].wait_recv()
        add_rows(total.at[k], 0, core_part.at[k], 0, TILE)
        if k == 0:
            far_x.start()
            far_y.start()
        if k == 1:
            to_x[0].start()
        if k == 2:
            to_y[1].start()
    far_y.wait_recv()
    add_rows(total.at[1], HALF, relayed.at[1], 0, HALF)
    to_x[1].start()
    far_x.wait_recv()
    add_rows(total.at[2], 0, relayed.at[0], 0, HALF)
    to_y[0].start()
    beside()
    for copy in to_x + to_y:
        copy.wait_recv()
    for copy in to_core[2:] + [far_x, far_y] + to_x + to_y:
        copy.wait_send()


def begin_kernel(
    x_own, w_query, w_key, w_value, facts, x_whole, w_qkv, facts_whole,
    trade_send, trade_recv, gather_send, gather_recv, w_send, w_recv, fact_send, fact_recv, local, *sems
):
    y, c, z, x = spot()
    row = 2 * y + c
    partner = partner_of(y, c, z, x)
    moves = z != 2 * c + y
    layer = others()
    barrier, count = greet_neighbours(layer)

    @pl.when(moves)
    def _():
        pl.semaphore_signal(barrier, inc=1, device_id=partner, device_id_type=MESH_ID)

    pl.semaphore_wait(barrier, count + moves.astype(jnp.int32))

    shard, width = w_query.shape
    owned = width // 8
    trades = [
        remote(
            x_own.at[half],
            x_whole.at[place_of(partner[0], partner[1], partner[3], half)],
            trade_send.at[half],
            trade_recv.at[half],
            partner,
        )
        for half in (0, 1)
    ]
    keeps = [
        pltpu.make_async_copy(x_own.at[half], x_whole.at[place_of(y, c, x, half)], trade_recv.at[half]) for half in (0, 1)
    ]

    @pl.when(moves)
    def _():
        for copy in trades:
            copy.start()

    @pl.when(jnp.logical_not(moves))
    def _():
        for copy in keeps:
            copy.start()

    spread = [
        remote(facts, facts_whole.at[row, z, x], fact_send.at[k], fact_recv.at[k], peer) for k, peer in enumerate(layer)
    ]
    kept = [pltpu.make_async_copy(facts, facts_whole.at[row, z, x], local.at[3])]
    for m, source in enumerate((w_query, w_key, w_value)):
        dst = w_qkv.at[row, z, pl.ds(pl.multiple_of(x * shard, shard), shard), pl.ds(m * owned, owned)]
        for k, peer in enumerate(layer):
            columns = pl.ds(pl.multiple_of((4 * peer[0] + 2 * peer[1] + peer[3]) * owned, owned), owned)
            spread.append(remote(source.at[:, columns], dst, w_send.at[m, k], w_recv.at[m, k], peer))
        columns = pl.ds(pl.multiple_of((4 * y + 2 * c + x) * owned, owned), owned)
        kept.append(pltpu.make_async_copy(source.at[:, columns], dst, local.at[m]))
    for copy in spread + kept:
        copy.start()

    gather = Gather(lambda half: x_whole.at[place_of(y, c, x, half)], x_whole, gather_send, gather_recv)
    for half in (0, 1):

        @pl.when(moves)
        def _():
            trades[half].wait_recv()

        @pl.when(jnp.logical_not(moves))
        def _():
            keeps[half].wait()

        gather.start(half)

    for copy in kept:
        copy.wait()
    for copy in spread:
        copy.wait_recv()
    chains = [
        Chain(facts_whole.at[:, z], lambda at: facts_whole.at[:, at], sems, 0),
        Chain(w_qkv.at[:, z], lambda at: w_qkv.at[:, at], sems, 1),
    ]

    def arrive(h):
        for chain in chains:
            chain.arrive(h)

    for chain in chains:
        chain.start()
    gather.pass_first()
    arrive(0)
    gather.pass_second()
    arrive(1)
    gather.pass_far()
    arrive(2)
    gather.finish()

    @pl.when(moves)
    def _():
        for copy in trades:
            copy.wait_send()

    for copy in spread:
        copy.wait_send()
    for chain in chains:
        chain.finish()


def anywhere():
    return pl.BlockSpec(memory_space=pl.ANY)


def in_vmem():
    return pl.BlockSpec(memory_space=pltpu.VMEM)


def dma(*shape):
    return pltpu.SemaphoreType.DMA(shape)


def remote_params(number):
    return pltpu.CompilerParams(collective_id=number, has_side_effects=True, vmem_limit_bytes=VMEM_LIMIT)


def begin(x_own, w_query, w_key, w_value, facts):
    block, width = x_own.shape
    shard = w_query.shape[0]
    x_whole, w_qkv, facts_whole = pl.pallas_call(
        begin_kernel,
        out_shape=(
            jax.ShapeDtypeStruct((8 * block, width), LOW),
            jax.ShapeDtypeStruct((4, 4, 2 * shard, 3 * width // 8), LOW),
            jax.ShapeDtypeStruct((4, 4, 2, *facts.shape), jnp.float32),
        ),
        in_specs=[in_vmem()] + [anywhere()] * 4,
        out_specs=[anywhere()] * 3,
        scratch_shapes=[
            dma(2), dma(2), dma(GATHER_COPIES), dma(GATHER_COPIES), dma(3, 7), dma(3, 7), dma(7), dma(7), dma(4), *chain_sems(2)
        ],
        compiler_params=remote_params(1),
        cost_estimate=pl.CostEstimate(flops=0, bytes_accessed=350_000_000, transcendentals=0),
    )(x_own.reshape(2, block // 2, width), w_query, w_key, w_value, facts)
    return x_whole, w_qkv.reshape(width, 3 * width // 8), facts_whole


def summed(total, landed, here):
    parts = (total[3, here, :], landed[0, here, :], landed[1, here, :])
    return sum(part.astype(jnp.float32) for part in parts)


def over_chunks(work):
    def step(i, carry):
        work(pl.ds(pl.multiple_of(i * CHUNK, CHUNK), CHUNK))
        return carry

    lax.fori_loop(0, TILE // CHUNK, step, 0)


def inverse_of(value):
    return lax.rsqrt(jnp.mean(value * value, axis=-1, keepdims=True) + EPSILON)


def close_attention_kernel(attended, w_out, x_own, gain, w_gate, w_up, resid, normed, own_gate, own_up, own, *scratch):
    scatter, (send, recv, local), sems = scratch[:7], scratch[7:10], scratch[10:]
    width = w_out.shape[1]
    hidden = w_gate.shape[1]
    z = lax.axis_index("z")
    barrier, count = greet_neighbours(near())
    pl.semaphore_wait(barrier, count)

    def slab_of(whole):
        return lambda at: whole.at[:, pl.ds(pl.multiple_of(at * hidden, hidden), hidden)]

    chains, kept = [], []
    for k, (part, whole) in enumerate(((w_gate, own_gate), (w_up, own_up))):
        chains.append(Chain(part, slab_of(whole), sems, k))
        chains[k].start()
        kept.append(pltpu.make_async_copy(part, slab_of(whole)(z), local.at[1 + k]))
        kept[k].start()

    def arrive(h):
        for chain in chains:
            chain.arrive(h)

    def produce(turn, y, c, x, out):
        at = place_of(y, c, x)

        def step(i, carry):
            columns = pl.ds(pl.multiple_of(i * TILE, TILE), TILE)
            out[:, columns] = dot_wide(attended[at, :], w_out[:, columns]).astype(LOW)
            return carry

        lax.fori_loop(0, width // TILE, step, 0)

    run_scatter(produce, *scatter, beside=lambda: arrive(0))
    total, landed = scatter[2], scatter[4]

    def chunk(here):
        value = x_own[here, :].astype(jnp.float32) + summed(total, landed, here)
        resid[here, :] = value
        own[here, :] = (value * inverse_of(value) * gain[...]).astype(LOW)

    over_chunks(chunk)
    run_gather(own, normed, send, recv, local.at[0], arrive)
    for chain in chains:
        chain.finish()
    for copy in kept:
        copy.wait()


def close_attention(attended, w_out, x_own, gain, w_gate, w_up):
    block, width = x_own.shape
    hidden = w_gate.shape[1]
    return pl.pallas_call(
        close_attention_kernel,
        out_shape=(
            jax.ShapeDtypeStruct((block, width), jnp.float32),
            jax.ShapeDtypeStruct((8 * block, width), LOW),
            jax.ShapeDtypeStruct((width, 4 * hidden), LOW),
            jax.ShapeDtypeStruct((width, 4 * hidden), LOW),
        ),
        in_specs=[in_vmem()] * 6,
        out_specs=[in_vmem()] + [anywhere()] * 3,
        scratch_shapes=[pltpu.VMEM((block, width), LOW)]
        + scatter_scratch(width)
        + [dma(GATHER_COPIES), dma(GATHER_COPIES), dma(3), *chain_sems(2)],
        compiler_params=remote_params(2),
        cost_estimate=pl.CostEstimate(flops=0, bytes_accessed=450_000_000, transcendentals=0),
    )(attended, w_out, x_own, gain, w_gate, w_up)


def norm_back(value, gain, upstream):
    inverse = inverse_of(value)
    scaled = upstream * gain
    inner = jnp.mean(scaled * value, axis=-1, keepdims=True)
    return inverse * scaled - value * (inverse * inverse * inverse) * inner, upstream * value * inverse


def fold_rows(total, terms):
    for first in range(0, CHUNK, 8):
        total[...] += terms[first : first + 8, :]


def close_mlp_kernel(
    d_gate, d_up, w_gate, w_up, resid, upstream, gain, grad_a, grad_b, d_resid, gain_term, d_resid_whole, parts_a, parts_b, own, blocks, *scratch
):
    scatter, (send, recv, local, fetched, line_send, line_recv) = scratch[:7], scratch[7:]
    y, c, z, x = spot()
    width = w_gate.shape[0]
    order = [(r, k, q) for r, q in ((1 - y, 1 - x), (y, 1 - x), (1 - y, x), (y, x)) for k in (1 - c, c)]

    def fetch(turn):
        at = place_of(*order[turn])
        slot = turn % 2
        return [
            pltpu.make_async_copy(source.at[at], blocks.at[slot, m], fetched.at[slot, m])
            for m, source in enumerate((d_gate, d_up))
        ]

    for copy in fetch(0):
        copy.start()
    greet(near() + tuple(line_of()))
    to_layers = [
        copy
        for k, (grad, parts) in enumerate(((grad_a, parts_a), (grad_b, parts_b)))
        for copy in spread_columns(grad, parts, line_send.at[k], line_recv.at[k])
    ]
    for copy in to_layers:
        copy.start()

    def produce(turn, to_y, to_c, to_x, out):
        if turn < 7:
            for copy in fetch(turn + 1):
                copy.start()
        for copy in fetch(turn):
            copy.wait()

        def step(i, carry):
            columns = pl.ds(pl.multiple_of(i * TILE, TILE), TILE)
            part = dot_nt(blocks[turn % 2, 0], w_gate[columns, :]) + dot_nt(blocks[turn % 2, 1], w_up[columns, :])
            out[:, columns] = part.astype(LOW)
            return carry

        lax.fori_loop(0, width // TILE, step, 0)

    run_scatter(produce, *scatter)
    total, landed = scatter[2], scatter[4]
    gain_term[...] = jnp.zeros_like(gain_term)

    def chunk(here):
        back, terms = norm_back(resid[here, :], gain[...], summed(total, landed, here))
        value = upstream[here, :].astype(jnp.float32) + back
        d_resid[here, :] = value
        own[here, :] = value.astype(LOW)
        fold_rows(gain_term, terms)

    over_chunks(chunk)
    run_gather(own, d_resid_whole, send, recv, local.at[0])
    for copy in to_layers:
        copy.wait()


def close_mlp(d_gate, d_up, w_gate, w_up, resid, upstream, gain, *grads):
    block, width = resid.shape
    hidden = d_gate.shape[1]
    return pl.pallas_call(
        close_mlp_kernel,
        out_shape=(
            jax.ShapeDtypeStruct((block, width), jnp.float32),
            jax.ShapeDtypeStruct((8, width), jnp.float32),
            jax.ShapeDtypeStruct((8 * block, width), LOW),
            jax.ShapeDtypeStruct((3, width, hidden // 4), LOW),
            jax.ShapeDtypeStruct((3, width, hidden // 4), LOW),
        ),
        in_specs=[anywhere()] * 2 + [in_vmem()] * 5 + [anywhere()] * 2,
        out_specs=[in_vmem(), in_vmem()] + [anywhere()] * 3,
        scratch_shapes=[pltpu.VMEM((block, width), LOW), pltpu.VMEM((2, 2, block, hidden), LOW)]
        + scatter_scratch(width)
        + [dma(GATHER_COPIES), dma(GATHER_COPIES), dma(1), dma(2, 2), dma(2, 3), dma(2, 3)],
        compiler_params=remote_params(3),
        cost_estimate=pl.CostEstimate(flops=0, bytes_accessed=450_000_000, transcendentals=0),
    )(d_gate, d_up, w_gate, w_up, resid, upstream, gain, *grads)


def close_layer_kernel(d_qkv, w_qkv, x_own, d_resid, gain, mlp_term, grad_low, gain_grads, own, terms, layer_terms, part, column_terms, *scratch):
    scatter, (send, recv, term_send, term_recv, line_send, line_recv) = scratch[:7], scratch[7:]
    y, c, z, x = spot()
    partner = partner_of(y, c, z, x)
    moves = z != 2 * c + y
    width = w_qkv.shape[0]
    barrier = pltpu.get_barrier_semaphore()

    @pl.when(moves)
    def _():
        pl.semaphore_signal(barrier, inc=1, device_id=partner, device_id_type=MESH_ID)

    layer = others()
    line = line_of()
    for peer in layer + line:
        pl.semaphore_signal(barrier, inc=1, device_id=peer, device_id_type=MESH_ID)
    pl.semaphore_wait(barrier, len(layer + line) + moves.astype(jnp.int32))

    def produce(turn, to_y, to_c, to_x, out):
        at = place_of(to_y, to_c, to_x)

        def step(i, carry):
            columns = pl.ds(pl.multiple_of(i * TILE, TILE), TILE)
            out[:, columns] = dot_nt(d_qkv[at, :], w_qkv[columns, :]).astype(LOW)
            return carry

        lax.fori_loop(0, width // TILE, step, 0)

    run_scatter(produce, *scatter)
    total, landed = scatter[2], scatter[4]
    terms[1] = mlp_term[...]
    terms[0] = jnp.zeros_like(mlp_term)
    trades = [
        remote(own.at[pl.ds(half * HALF, HALF)], grad_low.at[pl.ds(half * HALF, HALF)], send.at[half], recv.at[half], partner)
        for half in (0, 1)
    ]
    keeps = [
        pltpu.make_async_copy(own.at[pl.ds(half * HALF, HALF)], grad_low.at[pl.ds(half * HALF, HALF)], recv.at[half])
        for half in (0, 1)
    ]
    for half in (0, 1):

        def step(i, carry):
            here = pl.ds(pl.multiple_of(half * HALF + i * CHUNK, CHUNK), CHUNK)
            back, products = norm_back(x_own[here, :].astype(jnp.float32), gain[...], summed(total, landed, here))
            own[here, :] = (d_resid[here, :] + back).astype(LOW)
            fold_rows(terms.at[0], products)
            return carry

        lax.fori_loop(0, HALF // CHUNK, step, 0)

        @pl.when(moves)
        def _():
            trades[half].start()

        @pl.when(jnp.logical_not(moves))
        def _():
            keeps[half].start()

    def columns_of(row, layers):
        return pl.ds(pl.multiple_of((4 * row) * HD, HD), layers * HD)

    spread = [
        remote(terms.at[:, :, columns_of(2 * peer[0] + peer[1], 4)], layer_terms.at[k], term_send.at[k], term_recv.at[k], peer)
        for k, peer in enumerate(layer)
    ]
    for copy in spread:
        copy.start()
    for copy in spread:
        copy.wait_recv()
    part[...] = sum((layer_terms[k] for k in range(7)), terms[:, :, columns_of(2 * y + c, 4)])
    lines = [
        remote(
            part.at[:, :, pl.ds(pl.multiple_of(peer[2] * HD, HD), HD)], column_terms.at[k], line_send.at[k], line_recv.at[k], peer
        )
        for k, peer in enumerate(line)
    ]
    for copy in lines:
        copy.start()
    for copy in lines:
        copy.wait_recv()
    gain_grads[...] = sum((column_terms[k] for k in range(3)), part[:, :, pl.ds(pl.multiple_of(z * HD, HD), HD)])
    for copy in spread + lines:
        copy.wait_send()

    @pl.when(moves)
    def _():
        for copy in trades:
            copy.wait()

    @pl.when(jnp.logical_not(moves))
    def _():
        for copy in keeps:
            copy.wait()


def close_layer(d_qkv, w_qkv, x_own, d_resid, gain, mlp_term):
    block, width = x_own.shape
    return pl.pallas_call(
        close_layer_kernel,
        out_shape=(jax.ShapeDtypeStruct((block, width), LOW), jax.ShapeDtypeStruct((2, 8, width // 16), jnp.float32)),
        in_specs=[in_vmem()] * 6,
        out_specs=[anywhere(), in_vmem()],
        scratch_shapes=[
            pltpu.VMEM((block, width), LOW),
            pltpu.VMEM((2, 8, width), jnp.float32),
            pltpu.VMEM((7, 2, 8, width // 4), jnp.float32),
            pltpu.VMEM((2, 8, width // 4), jnp.float32),
            pltpu.VMEM((3, 2, 8, width // 16), jnp.float32),
        ]
        + scatter_scratch(width)
        + [dma(2), dma(2), dma(7), dma(7), dma(3), dma(3)],
        compiler_params=remote_params(4),
        cost_estimate=pl.CostEstimate(flops=0, bytes_accessed=350_000_000, transcendentals=0),
    )(d_qkv, w_qkv, x_own, d_resid, gain, mlp_term)


def doc_start(ends, place):
    start = jnp.zeros_like(place)
    for k in range(8):
        start = jnp.where(ends[k] <= place, ends[k], start)
    return jnp.where(place < ends[7], start, LEN)


def sigmoid_of(raw):
    return pl.reciprocal(1.0 + jnp.exp2(math.log2(LEN) - raw * (math.log2(math.e) / math.sqrt(HD))), approx=True)


def tile_at(index):
    return pl.ds(pl.multiple_of(index * TILE, TILE), TILE)


def head_of(array, rows, part, head):
    first = (part * (array.shape[1] // 3) // HD + head) * HD
    return array[rows, first : first + HD]


def attend_kernel(ends, qkv, out, total):
    i = pl.program_id(0)
    heads = qkv.shape[1] // (3 * HD)
    total[...] = jnp.zeros_like(total)
    q_place = i * TILE + lax.broadcasted_iota(jnp.int32, (TILE, 1), 0)
    q_start = doc_start(ends, q_place)

    def tile(j, diagonal):
        k_place = j * TILE + lax.broadcasted_iota(jnp.int32, (1, TILE), 1)
        allowed = k_place >= q_start
        if diagonal:
            allowed = allowed & (k_place <= q_place)
        for head in range(heads):
            raw = dot_nt(head_of(qkv, tile_at(i), 0, head), head_of(qkv, tile_at(j), 1, head))
            weight = jnp.where(allowed, sigmoid_of(raw), 0.0).astype(LOW)
            total[head] += dot_wide(weight, head_of(qkv, tile_at(j), 2, head))

    def step(j, carry):
        tile(j, False)
        return carry

    lax.fori_loop(0, i, step, 0)
    tile(i, True)
    for head in range(heads):
        out[tile_at(i), head * HD : (head + 1) * HD] = total[head].astype(LOW)


def open_mlp_kernel(normed, w_gate, w_up, upstream, gate, up, hidden, upstream_whole, send, recv, local):
    i = pl.program_id(0)
    y, c, z, x = spot()
    steps = pl.num_programs(0)
    gather = Gather(lambda half: upstream.at[pl.ds(half * HALF, HALF)], upstream_whole, send, recv)
    keep = pltpu.make_async_copy(upstream, upstream_whole.at[place_of(y, c, x)], local.at[0])

    @pl.when(i == 0)
    def _():
        greet(near())
        gather.start(0)
        gather.start(1)
        keep.start()

    @pl.when(i == steps - 3)
    def _():
        gather.pass_first()

    def step(n, carry):
        columns = pl.ds(pl.multiple_of(n * HALF, HALF), HALF)
        gate_part, up_part = dot_wide(normed[...], w_gate[:, columns]), dot_wide(normed[...], w_up[:, columns])
        gate[:, columns] = gate_part
        up[:, columns] = up_part
        hidden[:, columns] = (gate_part * jax.nn.sigmoid(gate_part) * up_part).astype(LOW)
        return carry

    lax.fori_loop(0, w_gate.shape[1] // HALF, step, 0)

    @pl.when(i == steps - 1)
    def _():
        gather.pass_second()
        gather.pass_far()
        gather.finish()
        keep.wait()


def open_mlp(normed, w_gate, w_up, upstream):
    places, width = normed.shape
    hidden = w_gate.shape[1]
    rows = lambda columns: pl.BlockSpec((TILE, columns), lambda i: (i, 0))
    whole = lambda array: pl.BlockSpec(array.shape, lambda i: (0, 0))
    return pl.pallas_call(
        open_mlp_kernel,
        out_shape=(
            jax.ShapeDtypeStruct((places, hidden), jnp.float32),
            jax.ShapeDtypeStruct((places, hidden), jnp.float32),
            jax.ShapeDtypeStruct((places, hidden), LOW),
            jax.ShapeDtypeStruct((places, width), LOW),
        ),
        grid=(places // TILE,),
        in_specs=[rows(width), whole(w_gate), whole(w_up), whole(upstream)],
        out_specs=[rows(hidden), rows(hidden), rows(hidden), anywhere()],
        scratch_shapes=[dma(GATHER_COPIES), dma(GATHER_COPIES), dma(1)],
        compiler_params=remote_params(5),
        cost_estimate=pl.CostEstimate(flops=0, bytes_accessed=250_000_000, transcendentals=0),
    )(normed, w_gate, w_up, upstream)


def out_turns():
    y, c, z, x = spot()
    owners = [((y, c, 2 * x + j // 2, j % 2), (z == 2 * x + j // 2) & (x == j % 2)) for j in range(4)]
    holders = [((y, c, j, z // 2), (z == j) & (x == z // 2)) for j in range(4)]
    return owners, holders


def attend_back_kernel(
    ends, qkv, grads, out_grad, out, out_parts, query_total, key_total, value_total, send, recv
):
    j = pl.program_id(0)
    y, c, z, x = spot()
    heads = qkv.shape[1] // (3 * HD)
    shard = out_grad.shape[0] // 4
    owners, holders = out_turns()

    def to_owner(turn):
        return remote(out_grad.at[pl.ds(turn * shard, shard)], out_parts.at[z], send.at[turn], recv.at[z], owners[turn][0])

    def to_self(turn):
        return pltpu.make_async_copy(out_grad.at[pl.ds(turn * shard, shard)], out_parts.at[z], recv.at[z])

    @pl.when(j == 0)
    def _():
        query_total[...] = jnp.zeros_like(query_total)
        barrier = pltpu.get_barrier_semaphore()
        for peer, here in holders:

            @pl.when(jnp.logical_not(here))
            def _():
                pl.semaphore_signal(barrier, inc=1, device_id=peer, device_id_type=MESH_ID)

        pl.semaphore_wait(barrier, 4 - (x == z // 2).astype(jnp.int32))
        for turn in range(4):

            @pl.when(jnp.logical_not(owners[turn][1]))
            def _():
                to_owner(turn).start()

            @pl.when(owners[turn][1])
            def _():
                to_self(turn).start()

    key_total[...] = jnp.zeros_like(key_total)
    value_total[...] = jnp.zeros_like(value_total)
    here = tile_at(j)
    k_place = j * TILE + lax.broadcasted_iota(jnp.int32, (TILE, 1), 0)
    turned = [head_of(qkv, here, 1, head).T for head in range(heads)]

    def tile(i, diagonal):
        q_place = i * TILE + lax.broadcasted_iota(jnp.int32, (1, TILE), 1)
        allowed = k_place >= doc_start(ends, q_place)
        if diagonal:
            allowed = allowed & (k_place <= q_place)
        for head in range(heads):
            query, grad = head_of(qkv, tile_at(i), 0, head), grads[tile_at(i), head * HD : (head + 1) * HD]
            sig = jnp.where(allowed, sigmoid_of(dot_nt(head_of(qkv, here, 1, head), query)), 0.0)
            value_total[head] += dot_wide(sig.astype(LOW), grad)
            d_score = (dot_nt(head_of(qkv, here, 2, head), grad) * (sig * (1.0 - sig))).astype(LOW)
            key_total[head] += dot_wide(d_score, query)
            query_total[head, :, tile_at(i)] += dot_wide(turned[head], d_score)

    def step(i, carry):
        tile(i, False)
        return carry

    tile(j, True)
    lax.fori_loop(j + 1, LEN // TILE, step, 0)
    scale = 1.0 / math.sqrt(HD)
    for head in range(heads):
        first = head * HD
        out[here, heads * HD + first : (heads + 1) * HD + first] = (key_total[head] * scale).astype(LOW)
        out[here, 2 * heads * HD + first : (2 * heads + 1) * HD + first] = value_total[head].astype(LOW)
        out[here, first : first + HD] = (query_total[head, :, here] * scale).T.astype(LOW)

    @pl.when(j == LEN // TILE - 1)
    def _():
        for turn in range(4):

            @pl.when(jnp.logical_not(owners[turn][1]))
            def _():
                to_owner(turn).wait_send()

            @pl.when(jnp.logical_not(holders[turn][1]))
            def _():
                landed = out_parts.at[turn]
                remote(landed, landed, send.at[turn], recv.at[turn], holders[turn][0]).wait_recv()

            @pl.when(owners[turn][1])
            def _():
                to_self(turn).wait()


def attend(ends, qkv):
    places, width = qkv.shape
    heads = width // (3 * HD)
    whole = lambda columns: pl.BlockSpec((places, columns), lambda i: (0, 0))
    return pl.pallas_call(
        attend_kernel,
        out_shape=jax.ShapeDtypeStruct((places, width // 3), LOW),
        grid=(places // TILE,),
        in_specs=[pl.BlockSpec(memory_space=pltpu.SMEM), whole(width)],
        out_specs=whole(width // 3),
        scratch_shapes=[pltpu.VMEM((heads, TILE, HD), jnp.float32)],
        compiler_params=pltpu.CompilerParams(vmem_limit_bytes=VMEM_LIMIT),
        cost_estimate=pl.CostEstimate(flops=0, bytes_accessed=150_000_000, transcendentals=0),
    )(ends, qkv)


def attend_back(ends, qkv, grads, out_grad):
    places, width = qkv.shape
    heads = width // (3 * HD)
    whole = lambda columns: pl.BlockSpec((places, columns), lambda j: (0, 0))
    return pl.pallas_call(
        attend_back_kernel,
        out_shape=(
            jax.ShapeDtypeStruct((places, width), LOW),
            jax.ShapeDtypeStruct((4, out_grad.shape[0] // 4, out_grad.shape[1]), LOW),
        ),
        grid=(places // TILE,),
        in_specs=[pl.BlockSpec(memory_space=pltpu.SMEM), whole(width), whole(width // 3), anywhere()],
        out_specs=[whole(width), anywhere()],
        scratch_shapes=[
            pltpu.VMEM((heads, HD, places), jnp.float32),
            pltpu.VMEM((heads, TILE, HD), jnp.float32),
            pltpu.VMEM((heads, TILE, HD), jnp.float32),
            dma(4),
            dma(4),
        ],
        compiler_params=remote_params(6),
        cost_estimate=pl.CostEstimate(flops=0, bytes_accessed=300_000_000, transcendentals=0),
    )(ends, qkv, grads, out_grad)


LAYER = ("y", "c", "x")
PLACES = ("c", "y", "x")
ALL = ("y", "c", "z", "x")


def scatter_layer(whole):
    return lax.psum_scatter(whole.astype(LOW), PLACES, scatter_dimension=0, tiled=True).astype(jnp.float32)


def trade(part):
    pairs = []
    for y in range(2):
        for c in range(2):
            for z in range(4):
                for x in range(2):
                    pairs.append((((y * 2 + c) * 4 + z) * 2 + x, (((z % 2) * 2 + z // 2) * 4 + 2 * c + y) * 2 + x))
    return lax.ppermute(part, ALL, pairs)


def after(first, then):
    return lax.optimization_barrier((first, then))[1]


def body_layers(
    tokens, lengths, cotangent, w_query, w_key, w_value, w_out, w_gate, w_up, w_down, gain_attn, gain_mlp
):
    rows_here, block, width = tokens.shape
    members = lax.axis_size(LAYER)
    layers = lax.axis_size("z")
    shard = w_query.shape[0]
    owned = width // members
    facts = jnp.zeros((8, 2 * shard), jnp.float32)
    facts = facts.at[0, :shard].set(gain_attn.astype(jnp.float32)).at[1, :shard].set(gain_mlp.astype(jnp.float32))
    facts = facts.at[2, : lengths.shape[1]].set(lengths[0].astype(jnp.float32))
    layer_x, w_qkv, facts = begin(tokens.reshape(block, width), w_query, w_key, w_value, facts)
    full_gain_attn, full_gain_mlp = facts[:, :, :, 0, :shard].reshape(1, width), facts[:, :, :, 1, :shard].reshape(1, width)
    layer = lax.axis_index("z")
    own_lengths = facts[:, 0, 0, 2, : lengths.shape[1]].reshape(2, 2, -1)
    own_lengths = lax.dynamic_slice(own_lengths, (layer % 2, layer // 2, 0), (1, 1, own_lengths.shape[2]))[0, 0]
    ends = jnp.cumsum(own_lengths.astype(jnp.int32))
    place = (4 * lax.axis_index("c") + 2 * lax.axis_index("y") + lax.axis_index("x")) * block
    x_own = lax.dynamic_slice_in_dim(layer_x, place, block, 0)
    layer_normed = norm_forward(layer_x.astype(jnp.float32), full_gain_attn)[0].astype(LOW)
    out_rows = lax.all_gather(after(facts, w_out), ("z", "x"), axis=0, tiled=True)
    w_out_own = lax.dynamic_slice_in_dim(out_rows, lax.axis_index("x") * owned, owned, 0)

    qkv = dot_wide(layer_normed, w_qkv).astype(LOW)
    upstream = trade(after(facts, cotangent)).reshape(block, width)
    attended = attend(ends, qkv)
    resid, layer_mlp, own_gate, own_up = close_attention(attended, w_out_own, x_own, full_gain_mlp, w_gate, w_up)

    own_down = lax.all_gather(after(resid, w_down), "z", axis=0, tiled=True)
    gate, up_part, hidden, layer_upstream = open_mlp(layer_mlp, own_gate, own_up, upstream)
    down_term = contract_rows(hidden, layer_upstream).astype(LOW)
    d_hidden = contract_cols(after(down_term, layer_upstream), own_down)
    d_gate, d_up = gate_backward(d_hidden, gate, up_part, jax.nn.sigmoid(gate))
    gate_term, up_term = contract_rows(layer_mlp, d_gate).astype(LOW), contract_rows(layer_mlp, d_up).astype(LOW)
    grad_down = lax.psum_scatter(down_term, "z", scatter_dimension=0, tiled=True)
    d_resid, gain_mlp_term, layer_d_resid, gate_parts, up_parts = close_mlp(
        after(grad_down, d_gate), d_up, own_gate, own_up, resid, upstream, full_gain_mlp, gate_term, up_term
    )

    def own_part(whole, parts):
        own = lax.dynamic_slice_in_dim(whole, layer * parts.shape[2], parts.shape[2], 1)
        return own.astype(jnp.float32) + jnp.sum(parts.astype(jnp.float32), axis=0)

    result = resid + scatter_layer(dot_wide(after(d_resid, hidden), own_down))
    mixed = trade(result.astype(LOW).reshape(rows_here, block, width))

    out_term = contract_rows(attended, layer_d_resid).astype(LOW)
    d_attended = contract_cols(layer_d_resid, w_out_own).astype(LOW)
    d_qkv, out_parts = attend_back(ends, qkv, d_attended, out_term)
    grad_gate, grad_up = own_part(gate_term, gate_parts), own_part(up_term, up_parts)
    grad_out = jnp.sum(out_parts.astype(jnp.float32), axis=0)
    qkv_term = contract_rows(layer_normed, d_qkv).astype(LOW)
    grad_low, gain_grads = close_layer(
        after(qkv_term, d_qkv), w_qkv, x_own, d_resid, full_gain_attn, gain_mlp_term
    )
    grad_tokens = grad_low.astype(jnp.float32).reshape(rows_here, block, width)

    qkv_term = qkv_term.reshape(4, layers, 2 * shard, 3 * owned).transpose(1, 0, 2, 3)
    qkv_term = qkv_term.reshape(layers * members * shard, 3 * owned)
    qkv_term = lax.psum_scatter(qkv_term, "z", scatter_dimension=0, tiled=True)
    qkv_term = lax.all_to_all(qkv_term.reshape(members, shard, 3 * owned), LAYER, 0, 0)
    qkv_term = qkv_term.reshape(members, shard, 3, owned).transpose(2, 1, 0, 3).astype(jnp.float32)
    grad_query, grad_key, grad_value = qkv_term.reshape(3, shard, width)
    gain_grads = lax.dynamic_index_in_dim(jnp.sum(gain_grads, axis=1).reshape(2, 2, shard), lax.axis_index("x"), 1, False)
    return (
        mixed,
        grad_tokens,
        grad_query,
        grad_key,
        grad_value,
        grad_out,
        grad_gate,
        grad_up,
        grad_down.astype(jnp.float32),
        gain_grads[0],
        gain_grads[1],
    )


def body_any(
    tokens,
    lengths,
    cotangent,
    w_query,
    w_key,
    w_value,
    w_out,
    w_gate,
    w_up,
    w_down,
    gain_attn,
    gain_mlp,
):
    rows_here, block, width = tokens.shape
    count = rows_here * block
    scale = 1.0 / math.sqrt(HD)
    kv_place = lax.axis_index("kv")
    key_places = kv_place * block + jnp.arange(block, dtype=jnp.int32)
    attn_set = (
        lax.all_gather(w_query, ("row", "kv"), axis=0, tiled=True),
        lax.all_gather(w_key, ("row", "kv"), axis=0, tiled=True),
        lax.all_gather(w_value, ("row", "kv"), axis=0, tiled=True),
        lax.all_gather(w_out, ("row", "kv"), axis=0, tiled=True),
        lax.all_gather(gain_attn, ("row", "kv"), axis=0, tiled=True),
        lax.all_gather(gain_mlp, ("row", "kv"), axis=0, tiled=True),
    )
    full_query, full_key, full_value, full_out, full_gain_attn, full_gain_mlp = attn_set
    flat = tokens.reshape(count, width).astype(jnp.float32)
    normed_attn, inverse_attn = norm_forward(flat, full_gain_attn)
    normed_attn_low = normed_attn.astype(jnp.bfloat16)
    query_low = jnp.dot(normed_attn_low, full_query, preferred_element_type=jnp.float32).astype(
        jnp.bfloat16
    )
    key_low = jnp.dot(normed_attn_low, full_key, preferred_element_type=jnp.float32).astype(
        jnp.bfloat16
    )
    value_low = jnp.dot(normed_attn_low, full_value, preferred_element_type=jnp.float32).astype(
        jnp.bfloat16
    )
    key_heads = key_low.reshape(rows_here, block, H, HD)
    value_heads = value_low.reshape(rows_here, block, H, HD)
    segment, valid = segment_table(lengths)
    key_segment = lax.dynamic_slice_in_dim(segment, kv_place * block, block, 1)
    key_valid = lax.dynamic_slice_in_dim(valid, kv_place * block, block, 1)
    queries_all = lax.all_gather(
        query_low.reshape(rows_here, block, width), "kv", axis=1, tiled=True
    )
    which = 0
    query_rows = queries_all[which]
    query_segment = segment[which]
    sigmoid_part, allowed = score_block(
        query_rows,
        key_heads[which],
        query_segment,
        key_segment[which],
        key_valid[which],
        jnp.int32(0),
        key_places,
    )
    weight = (sigmoid_part * allowed).astype(jnp.bfloat16)
    summed = jnp.einsum(
        "hqk,khd->qhd", weight, value_heads[which], preferred_element_type=jnp.float32
    )
    pieces = [
        lax.psum_scatter(
            summed.reshape(lax.axis_size("kv") * block, width).astype(jnp.bfloat16),
            "kv",
            scatter_dimension=0,
            tiled=True,
        ).astype(jnp.float32)
    ]
    attended_low = jnp.stack(pieces).reshape(count, width).astype(jnp.bfloat16)
    resid = flat + jnp.dot(attended_low, full_out, preferred_element_type=jnp.float32)
    normed_mlp, inverse_mlp = norm_forward(resid, full_gain_mlp)
    normed_mlp_low = normed_mlp.astype(jnp.bfloat16)
    upstream_low = cotangent.reshape(count, width)
    upstream = upstream_low.astype(jnp.float32)
    slice_gate, slice_up, slice_down = (
        lax.all_gather(w_gate, "row", axis=1, tiled=True),
        lax.all_gather(w_up, "row", axis=1, tiled=True),
        lax.all_gather(w_down, "row", axis=0, tiled=True),
    )
    row_normed, row_upstream = (
        lax.all_gather(normed_mlp_low.reshape(rows_here, block, width), "kv", axis=1, tiled=True),
        lax.all_gather(cotangent, "kv", axis=1, tiled=True),
    )
    normed_rows = row_normed.reshape(rows_here * LEN, width)
    upstream_rows = row_upstream.reshape(rows_here * LEN, width)
    gate = jnp.dot(normed_rows, slice_gate, preferred_element_type=jnp.float32)
    up_part = jnp.dot(normed_rows, slice_up, preferred_element_type=jnp.float32)
    sigmoid_gate = jax.nn.sigmoid(gate)
    hidden_low = (gate * sigmoid_gate * up_part).astype(jnp.bfloat16)
    hidden_rows = hidden_low.reshape(rows_here, LEN, hidden_low.shape[1])
    which = 0
    hidden_part = hidden_rows[which]
    outputs = [
        lax.psum_scatter(
            jnp.dot(hidden_part, slice_down, preferred_element_type=jnp.float32).astype(
                jnp.bfloat16
            ),
            "kv",
            scatter_dimension=0,
            tiled=True,
        ).astype(jnp.float32)
    ]
    result = resid + jnp.stack(outputs).reshape(count, width)
    d_hidden = contract_cols(upstream_rows, slice_down)
    d_gate, d_up = gate_backward(d_hidden, gate, up_part, sigmoid_gate)
    partial_normed = contract_cols(d_gate, slice_gate) + contract_cols(d_up, slice_up)
    d_normed_mlp = (
        lax.psum_scatter(
            partial_normed.reshape(rows_here, LEN, width).astype(jnp.bfloat16),
            "kv",
            scatter_dimension=1,
            tiled=True,
        )
        .astype(jnp.float32)
        .reshape(count, width)
    )
    grad_gate, grad_up, grad_down = (
        lax.psum_scatter(
            contract_rows(normed_rows, d_gate).astype(jnp.bfloat16),
            "row",
            scatter_dimension=1,
            tiled=True,
        ).astype(jnp.float32),
        lax.psum_scatter(
            contract_rows(normed_rows, d_up).astype(jnp.bfloat16),
            "row",
            scatter_dimension=1,
            tiled=True,
        ).astype(jnp.float32),
        lax.psum_scatter(
            contract_rows(hidden_low, upstream_rows).astype(jnp.bfloat16),
            "row",
            scatter_dimension=0,
            tiled=True,
        ).astype(jnp.float32),
    )
    mixed = result.astype(jnp.bfloat16).reshape(rows_here, block, width)
    back_mlp, gain_mlp_term = norm_backward(resid, inverse_mlp, full_gain_mlp, d_normed_mlp)
    d_resid = upstream + back_mlp
    d_resid_low = d_resid.astype(jnp.bfloat16)
    d_attended = contract_cols(d_resid_low, full_out).astype(jnp.bfloat16)
    grads_all = lax.all_gather(
        d_attended.reshape(rows_here, block, width), "kv", axis=1, tiled=True
    )
    query_block = min(512, LEN)
    block_count = LEN // query_block
    which = 0

    def sweep(carry, index, which=which):
        key_total, value_total = carry
        start = index * query_block
        query_rows = lax.dynamic_slice_in_dim(queries_all[which], start, query_block, 0)
        grad_rows = lax.dynamic_slice_in_dim(grads_all[which], start, query_block, 0)
        query_segment = lax.dynamic_slice_in_dim(segment[which], start, query_block, 0)
        sigmoid_part, allowed = score_block(
            query_rows,
            key_heads[which],
            query_segment,
            key_segment[which],
            key_valid[which],
            start,
            key_places,
        )
        weight = (sigmoid_part * allowed).astype(jnp.bfloat16)
        grad_heads = grad_rows.reshape(query_block, H, HD)
        value_total = value_total + jnp.einsum(
            "hqk,qhd->khd", weight, grad_heads, preferred_element_type=jnp.float32
        )
        d_weight = jnp.einsum(
            "qhd,khd->hqk", grad_heads, value_heads[which], preferred_element_type=jnp.float32
        )
        d_score = (d_weight * sigmoid_part * (1.0 - sigmoid_part) * allowed).astype(jnp.bfloat16)
        query_part = (
            jnp.einsum(
                "hqk,khd->qhd", d_score, key_heads[which], preferred_element_type=jnp.float32
            )
            * scale
        )
        key_total = (
            key_total
            + jnp.einsum(
                "hqk,qhd->khd",
                d_score,
                query_rows.reshape(query_block, H, HD),
                preferred_element_type=jnp.float32,
            )
            * scale
        )
        return ((key_total, value_total), query_part.reshape(query_block, width))

    zeros = jnp.zeros((block, H, HD), jnp.float32)
    totals, query_parts = lax.scan(sweep, (zeros, zeros), jnp.arange(block_count, dtype=jnp.int32))
    query_terms = [query_parts.reshape(LEN, width)]
    key_grads = [totals[0].reshape(block, width)]
    value_grads = [totals[1].reshape(block, width)]
    query_local = lax.psum_scatter(
        jnp.stack(query_terms).astype(jnp.bfloat16), "kv", scatter_dimension=1, tiled=True
    ).astype(jnp.float32)
    d_query_low = query_local.reshape(count, width).astype(jnp.bfloat16)
    d_key_low = jnp.stack(key_grads).reshape(count, width).astype(jnp.bfloat16)
    d_value_low = jnp.stack(value_grads).reshape(count, width).astype(jnp.bfloat16)
    d_normed_attn = (
        contract_cols(d_query_low, full_query)
        + contract_cols(d_key_low, full_key)
        + contract_cols(d_value_low, full_value)
    )
    back_attn, gain_attn_term = norm_backward(flat, inverse_attn, full_gain_attn, d_normed_attn)
    grad_tokens = (d_resid + back_attn).reshape(rows_here, block, width)
    projected_low = jnp.concatenate((d_query_low, d_key_low, d_value_low), axis=1)
    grad_projections = lax.psum_scatter(
        contract_rows(normed_attn_low, projected_low),
        ("row", "kv"),
        scatter_dimension=0,
        tiled=True,
    )
    out_term = contract_rows(attended_low, d_resid_low)
    grad_out, grad_gain_attn, grad_gain_mlp = (
        lax.psum_scatter(out_term, ("row", "kv"), scatter_dimension=0, tiled=True),
        lax.psum_scatter(gain_attn_term, ("row", "kv"), scatter_dimension=0, tiled=True),
        lax.psum_scatter(gain_mlp_term, ("row", "kv"), scatter_dimension=0, tiled=True),
    )
    grad_query = grad_projections[:, :width]
    grad_key = grad_projections[:, width : 2 * width]
    grad_value = grad_projections[:, 2 * width :]
    return (
        mixed,
        grad_tokens,
        grad_query,
        grad_key,
        grad_value,
        grad_out,
        grad_gate,
        grad_up,
        grad_down,
        grad_gain_attn,
        grad_gain_mlp,
    )


def solution(mesh):
    rows, columns = mesh.shape["row"], mesh.shape["kv"]
    if rows == 4 and columns == 2 * rows:
        mesh = Mesh(mesh.devices.reshape(2, 2, rows, 2), ("y", "c", "z", "x"))
        row, kv, run = ("y", "c"), ("z", "x"), body_layers
    else:
        row, kv, run = "row", "kv", body_any
    both = ("y", "c", "z", "x") if run is body_layers else ("row", "kv")
    tall, wide, flat = P(both, None), P(None, both), P(both)
    tokens = P(row, kv, None)
    return jax.shard_map(
        run,
        mesh=mesh,
        in_specs=(tokens, P(row, None), tokens, tall, tall, tall, tall, wide, wide, tall, flat, flat),
        out_specs=(tokens, tokens, tall, tall, tall, tall, wide, wide, tall, flat, flat),
        check_vma=False,
    )
```

```python
import functools
import math

import jax
import jax.numpy as jnp
from jax import lax
from jax.experimental import pallas as pl
from jax.experimental.pallas import tpu as pltpu
from jax.sharding import Mesh, PartitionSpec as P

H = 16
HD = 128
LEN = 4096


EPSILON = 1e-05


def contract_rows(left, right):
    return lax.dot_general(
        left, right, (((0,), (0,)), ((), ())), preferred_element_type=jnp.float32
    )


def contract_cols(left, right):
    return lax.dot_general(
        left, right, (((1,), (1,)), ((), ())), preferred_element_type=jnp.float32
    )


def norm_forward(value, gain):
    inverse = lax.rsqrt(jnp.mean(value * value, axis=-1, keepdims=True) + EPSILON)
    return (value * inverse * gain.astype(jnp.float32), inverse)


def norm_backward(value, inverse, gain, upstream):
    scaled = upstream * gain.astype(jnp.float32)
    inner = jnp.mean(scaled * value, axis=-1, keepdims=True)
    back = inverse * scaled - value * (inverse * inverse * inverse) * inner
    gain_term = jnp.sum(upstream * value * inverse, axis=0)
    return (back, gain_term)


def segment_table(lengths):
    ends = jnp.cumsum(lengths, axis=-1)
    places = jnp.arange(LEN, dtype=jnp.int32)
    segment = jnp.sum((ends[:, None, :] <= places[None, :, None]).astype(jnp.int32), axis=-1)
    valid = places[None, :] < ends[:, -1:]
    return (segment, valid)


def score_block(
    query_rows, key_heads, query_segment, key_segment, key_valid, query_start, key_places
):
    count = query_rows.shape[0]
    query_heads = query_rows.reshape(count, H, HD)
    raw = jnp.einsum("qhd,khd->hqk", query_heads, key_heads, preferred_element_type=jnp.float32)
    scores = raw * (1.0 / math.sqrt(HD)) - math.log(LEN)
    places = query_start + jnp.arange(count, dtype=jnp.int32)
    allowed = (
        (key_places[None, :] <= places[:, None])
        & (key_segment[None, :] == query_segment[:, None])
        & key_valid[None, :]
    )
    return (jax.nn.sigmoid(scores), allowed.astype(jnp.float32)[None])


def gate_backward(d_hidden, gate, up_part, sigmoid_gate):
    d_gate = (d_hidden * up_part * sigmoid_gate * (1.0 + gate * (1.0 - sigmoid_gate))).astype(
        jnp.bfloat16
    )
    d_up = (d_hidden * gate * sigmoid_gate).astype(jnp.bfloat16)
    return (d_gate, d_up)


TILE = 512
LOW = jnp.bfloat16
VMEM_LIMIT = 60 * 1024 * 1024


def dot_nt(left, right):
    return lax.dot_general(left, right, (((1,), (1,)), ((), ())), preferred_element_type=jnp.float32)


def dot_wide(left, right):
    return jnp.dot(left, right, preferred_element_type=jnp.float32)


HALF = TILE // 2
CHUNK = 32
MESH_ID = pl.DeviceIdType.MESH


def flip(bit, by):
    return bit + by - 2 * bit * by


def spot():
    return tuple(lax.axis_index(name) for name in ("y", "c", "z", "x"))


def near():
    y, c, z, x = spot()
    return (y, c, z, 1 - x), (1 - y, c, z, x), (y, 1 - c, z, x)


def partner_of(y, c, z, x):
    return lax.rem(z, 2), z // 2, 2 * c + y, x


def place_of(y, c, x, half=None):
    first = (4 * c + 2 * y + x) * TILE
    if half is None:
        return pl.ds(pl.multiple_of(first, TILE), TILE)
    return pl.ds(pl.multiple_of(first + half * HALF, HALF), HALF)


def remote(src, dst, send, recv, peer):
    return pltpu.make_async_remote_copy(
        src_ref=src, dst_ref=dst, send_sem=send, recv_sem=recv, device_id=peer, device_id_type=MESH_ID
    )


def greet(peers):
    barrier = pltpu.get_barrier_semaphore()
    for peer in peers:
        pl.semaphore_signal(barrier, inc=1, device_id=peer, device_id_type=MESH_ID)
    pl.semaphore_wait(barrier, len(peers))


class Gather:
    def __init__(self, own, whole, send, recv):
        y, c, z, x = spot()
        across_x, across_y, core = near()

        def from_own(k, half, peer):
            return remote(own(half), whole.at[place_of(y, c, x, half)], send.at[k], recv.at[k], peer)

        def passed(k, at, peer):
            return remote(whole.at[at], whole.at[at], send.at[k], recv.at[k], peer)

        self.mine = [
            [from_own(0, 0, across_x), from_own(1, 0, across_y), from_own(2, 0, core)],
            [from_own(3, 1, across_x), from_own(4, 1, across_y), from_own(5, 1, core)],
        ]
        held_x = [place_of(y, c, 1 - x, half) for half in (0, 1)]
        held_y = [place_of(1 - y, c, x, half) for half in (0, 1)]
        far = [place_of(1 - y, c, 1 - x, half) for half in (0, 1)]
        self.over_y, self.over_x = passed(6, held_x[0], across_y), passed(7, held_y[1], across_x)
        self.core_x = [passed(8 + half, held_x[half], core) for half in (0, 1)]
        self.core_y = [passed(10 + half, held_y[half], core) for half in (0, 1)]
        self.core_far = [passed(12 + half, far[half], core) for half in (0, 1)]

    def start(self, half):
        for copy in self.mine[half]:
            copy.start()

    def pass_first(self):
        self.mine[0][0].wait_recv()
        self.over_y.start()
        self.core_x[0].start()
        self.mine[0][1].wait_recv()
        self.core_y[0].start()

    def pass_second(self):
        self.mine[1][1].wait_recv()
        self.over_x.start()
        self.core_y[1].start()
        self.mine[1][0].wait_recv()
        self.core_x[1].start()

    def pass_far(self):
        self.over_y.wait_recv()
        self.core_far[0].start()
        self.over_x.wait_recv()
        self.core_far[1].start()

    def finish(self):
        from_core = [self.mine[0][2], self.mine[1][2]] + self.core_x + self.core_y + self.core_far
        for copy in from_core:
            copy.wait_recv()
        for copy in self.mine[0] + self.mine[1] + [self.over_y, self.over_x] + self.core_x + self.core_y + self.core_far:
            copy.wait_send()


GATHER_COPIES = 14


def run_gather(own, whole, send, recv, local, beside=lambda h: None):
    y, c, z, x = spot()
    keep = pltpu.make_async_copy(own, whole.at[place_of(y, c, x)], local)
    keep.start()
    gather = Gather(lambda half: own.at[pl.ds(half * HALF, HALF)], whole, send, recv)
    gather.start(0)
    gather.start(1)
    gather.pass_first()
    beside(1)
    gather.pass_second()
    gather.pass_far()
    gather.finish()
    beside(2)
    keep.wait()


class Chain:
    def __init__(self, own, slab, sems, index):
        self.own, self.slab, self.sems, self.index = own, slab, sems, index
        self.last = lax.axis_size("z") - 1

    def move(self, which, h, source, layer, to):
        y, c, z, x = spot()
        return remote(
            source, self.slab(layer), self.sems[2 * which].at[self.index, h], self.sems[2 * which + 1].at[self.index, h], (y, c, to, x)
        )

    def up(self, h):
        z = lax.axis_index("z")
        return self.move(0, h, self.own if h == 0 else self.slab(z - h), z - h, z + 1)

    def down(self, h):
        z = lax.axis_index("z")
        return self.move(1, h, self.own if h == 0 else self.slab(z + h), z + h, z - 1)

    def start(self):
        z = lax.axis_index("z")

        @pl.when(z < self.last)
        def _():
            self.up(0).start()

        @pl.when(z > 0)
        def _():
            self.down(0).start()

    def arrive(self, h):
        z = lax.axis_index("z")

        @pl.when(z - h - 1 >= 0)
        def _():
            self.move(0, h, self.slab(z - h - 1), z - h - 1, z).wait_recv()
            if h < 2:

                @pl.when(z < self.last)
                def _():
                    self.up(h + 1).start()

        @pl.when(z + h + 1 <= self.last)
        def _():
            self.move(1, h, self.slab(z + h + 1), z + h + 1, z).wait_recv()
            if h < 2:

                @pl.when(z > 0)
                def _():
                    self.down(h + 1).start()

    def finish(self):
        z = lax.axis_index("z")
        for h in range(3):

            @pl.when((z < self.last) & (z - h >= 0))
            def _():
                self.up(h).wait_send()

            @pl.when((z > 0) & (z + h <= self.last))
            def _():
                self.down(h).wait_send()


def chain_sems(count):
    return [pltpu.SemaphoreType.DMA((count, 3)) for _ in range(4)]


def greet_neighbours(peers):
    y, c, z, x = spot()
    last = lax.axis_size("z") - 1
    barrier = pltpu.get_barrier_semaphore()
    for peer in peers:
        pl.semaphore_signal(barrier, inc=1, device_id=peer, device_id_type=MESH_ID)

    @pl.when(z > 0)
    def _():
        pl.semaphore_signal(barrier, inc=1, device_id=(y, c, z - 1, x), device_id_type=MESH_ID)

    @pl.when(z < last)
    def _():
        pl.semaphore_signal(barrier, inc=1, device_id=(y, c, z + 1, x), device_id_type=MESH_ID)

    return barrier, len(peers) + (z > 0).astype(jnp.int32) + (z < last).astype(jnp.int32)


def others():
    y, c, z, x = spot()
    return [(flip(y, dy), flip(c, dc), z, flip(x, dx)) for dy in (0, 1) for dc in (0, 1) for dx in (0, 1) if dy + dc + dx]


def line_of():
    y, c, z, x = spot()
    return [(y, c, lax.rem(z + dz, 4), x) for dz in (1, 2, 3)]


def spread_columns(whole, parts, send, recv):
    size = whole.shape[1] // 4
    return [
        remote(
            whole.at[:, pl.ds(pl.multiple_of(peer[2] * size, size), size)], parts.at[k], send.at[k], recv.at[k], peer
        )
        for k, peer in enumerate(line_of())
    ]


def add_rows(total, first, term, start, count):
    def step(i, carry):
        here = pl.ds(pl.multiple_of(first + i * CHUNK, CHUNK), CHUNK)
        there = pl.ds(pl.multiple_of(start + i * CHUNK, CHUNK), CHUNK)
        total[here, :] = (total[here, :].astype(jnp.float32) + term[there, :].astype(jnp.float32)).astype(LOW)
        return carry

    lax.fori_loop(0, count // CHUNK, step, 0)


def scatter_scratch(width, parts=1):
    return [
        pltpu.VMEM((2, TILE, width), LOW),
        pltpu.VMEM((4, TILE, width), LOW),
        pltpu.VMEM((4, TILE, width), LOW),
        pltpu.VMEM((2, HALF, width), LOW),
        pltpu.VMEM((2, TILE, width), LOW),
        pltpu.SemaphoreType.DMA((parts, 10)),
        pltpu.SemaphoreType.DMA((parts, 10)),
    ]


class Scatter:
    def __init__(self, produce, staged, core_part, total, relayed, landed, send, recv, part=0, start=0, size=TILE):
        across_x, across_y, core = near()
        self.produce, self.staged, self.core_part, self.total, self.relayed = produce, staged, core_part, total, relayed
        self.start, self.size, self.half = start, size, size // 2
        send, recv = send.at[part], recv.at[part]
        rows = pl.ds(start, size)
        halves = (pl.ds(start, self.half), pl.ds(start + self.half, self.half))
        self.relay_row = start // 2
        passing = pl.ds(self.relay_row, self.half)
        self.to_core = [
            remote(staged.at[k % 2, rows], core_part.at[k, rows], send.at[k], recv.at[k], core) for k in range(4)
        ]
        self.far_x = remote(total.at[0, halves[0]], relayed.at[0, passing], send.at[4], recv.at[4], across_x)
        self.far_y = remote(total.at[0, halves[1]], relayed.at[1, passing], send.at[5], recv.at[5], across_y)
        self.to_x = [
            remote(total.at[1, at], landed.at[0, at], send.at[6 + half], recv.at[6 + half], across_x)
            for half, at in enumerate(halves)
        ]
        self.to_y = [
            remote(total.at[2, at], landed.at[1, at], send.at[8 + half], recv.at[8 + half], across_y)
            for half, at in enumerate(halves)
        ]

    def begin(self):
        y, c, z, x = spot()
        rows = pl.ds(self.start, self.size)
        for k, (to_row, to_column) in enumerate(((1 - y, 1 - x), (y, 1 - x), (1 - y, x), (y, x))):
            if k >= 2:
                self.to_core[k - 2].wait_send()
            self.produce(2 * k, to_row, 1 - c, to_column, self.staged.at[k % 2, rows])
            self.to_core[k].start()
            self.produce(2 * k + 1, to_row, c, to_column, self.total.at[k, rows])
            self.to_core[k].wait_recv()
            add_rows(self.total.at[k], self.start, self.core_part.at[k], self.start, self.size)
            if k == 0:
                self.far_x.start()
                self.far_y.start()
            if k == 1:
                self.to_x[0].start()
            if k == 2:
                self.to_y[1].start()

    def relay(self):
        self.far_y.wait_recv()
        add_rows(self.total.at[1], self.start + self.half, self.relayed.at[1], self.relay_row, self.half)
        self.to_x[1].start()
        self.far_x.wait_recv()
        add_rows(self.total.at[2], self.start, self.relayed.at[0], self.relay_row, self.half)
        self.to_y[0].start()

    def arrive(self):
        for copy in self.to_x + self.to_y:
            copy.wait_recv()

    def finish(self):
        for copy in self.to_core[2:] + [self.far_x, self.far_y] + self.to_x + self.to_y:
            copy.wait_send()


def run_scatter(produce, *scratch, beside=lambda: None):
    scatter = Scatter(produce, *scratch)
    scatter.begin()
    scatter.relay()
    beside()
    scatter.arrive()
    scatter.finish()


def begin_kernel(
    x_own, w_query, w_key, w_value, facts, x_whole, w_qkv, facts_whole,
    trade_send, trade_recv, gather_send, gather_recv, w_send, w_recv, fact_send, fact_recv, local, *sems
):
    y, c, z, x = spot()
    row = 2 * y + c
    partner = partner_of(y, c, z, x)
    moves = z != 2 * c + y
    layer = others()
    barrier, count = greet_neighbours(layer)

    @pl.when(moves)
    def _():
        pl.semaphore_signal(barrier, inc=1, device_id=partner, device_id_type=MESH_ID)

    pl.semaphore_wait(barrier, count + moves.astype(jnp.int32))

    shard, width = w_query.shape
    owned = width // 8
    trades = [
        remote(
            x_own.at[half],
            x_whole.at[place_of(partner[0], partner[1], partner[3], half)],
            trade_send.at[half],
            trade_recv.at[half],
            partner,
        )
        for half in (0, 1)
    ]
    keeps = [
        pltpu.make_async_copy(x_own.at[half], x_whole.at[place_of(y, c, x, half)], trade_recv.at[half]) for half in (0, 1)
    ]

    @pl.when(moves)
    def _():
        for copy in trades:
            copy.start()

    @pl.when(jnp.logical_not(moves))
    def _():
        for copy in keeps:
            copy.start()

    spread = [
        remote(facts, facts_whole.at[row, z, x], fact_send.at[k], fact_recv.at[k], peer) for k, peer in enumerate(layer)
    ]
    kept = [pltpu.make_async_copy(facts, facts_whole.at[row, z, x], local.at[3])]
    for m, source in enumerate((w_query, w_key, w_value)):
        dst = w_qkv.at[row, z, pl.ds(pl.multiple_of(x * shard, shard), shard), pl.ds(m * owned, owned)]
        for k, peer in enumerate(layer):
            columns = pl.ds(pl.multiple_of((4 * peer[0] + 2 * peer[1] + peer[3]) * owned, owned), owned)
            spread.append(remote(source.at[:, columns], dst, w_send.at[m, k], w_recv.at[m, k], peer))
        columns = pl.ds(pl.multiple_of((4 * y + 2 * c + x) * owned, owned), owned)
        kept.append(pltpu.make_async_copy(source.at[:, columns], dst, local.at[m]))
    for copy in spread + kept:
        copy.start()

    gather = Gather(lambda half: x_whole.at[place_of(y, c, x, half)], x_whole, gather_send, gather_recv)
    for half in (0, 1):

        @pl.when(moves)
        def _():
            trades[half].wait_recv()

        @pl.when(jnp.logical_not(moves))
        def _():
            keeps[half].wait()

        gather.start(half)

    for copy in kept:
        copy.wait()
    for copy in spread:
        copy.wait_recv()
    chains = [
        Chain(facts_whole.at[:, z], lambda at: facts_whole.at[:, at], sems, 0),
        Chain(w_qkv.at[:, z], lambda at: w_qkv.at[:, at], sems, 1),
    ]

    def arrive(h):
        for chain in chains:
            chain.arrive(h)

    for chain in chains:
        chain.start()
    gather.pass_first()
    arrive(0)
    gather.pass_second()
    arrive(1)
    gather.pass_far()
    arrive(2)
    gather.finish()

    @pl.when(moves)
    def _():
        for copy in trades:
            copy.wait_send()

    for copy in spread:
        copy.wait_send()
    for chain in chains:
        chain.finish()


def anywhere():
    return pl.BlockSpec(memory_space=pl.ANY)


def in_vmem():
    return pl.BlockSpec(memory_space=pltpu.VMEM)


def dma(*shape):
    return pltpu.SemaphoreType.DMA(shape)


def remote_params(number):
    return pltpu.CompilerParams(collective_id=number, has_side_effects=True, vmem_limit_bytes=VMEM_LIMIT)


def begin(x_own, w_query, w_key, w_value, facts):
    block, width = x_own.shape
    shard = w_query.shape[0]
    x_whole, w_qkv, facts_whole = pl.pallas_call(
        begin_kernel,
        out_shape=(
            jax.ShapeDtypeStruct((8 * block, width), LOW),
            jax.ShapeDtypeStruct((4, 4, 2 * shard, 3 * width // 8), LOW),
            jax.ShapeDtypeStruct((4, 4, 2, *facts.shape), jnp.float32),
        ),
        in_specs=[in_vmem()] + [anywhere()] * 4,
        out_specs=[anywhere()] * 3,
        scratch_shapes=[
            dma(2), dma(2), dma(GATHER_COPIES), dma(GATHER_COPIES), dma(3, 7), dma(3, 7), dma(7), dma(7), dma(4), *chain_sems(2)
        ],
        compiler_params=remote_params(1),
        cost_estimate=pl.CostEstimate(flops=0, bytes_accessed=350_000_000, transcendentals=0),
    )(x_own.reshape(2, block // 2, width), w_query, w_key, w_value, facts)
    return x_whole, w_qkv.reshape(width, 3 * width // 8), facts_whole


def summed(total, landed, here):
    parts = (total[3, here, :], landed[0, here, :], landed[1, here, :])
    return sum(part.astype(jnp.float32) for part in parts)


def over_chunks(work):
    def step(i, carry):
        work(pl.ds(pl.multiple_of(i * CHUNK, CHUNK), CHUNK))
        return carry

    lax.fori_loop(0, TILE // CHUNK, step, 0)


def inverse_of(value):
    return lax.rsqrt(jnp.mean(value * value, axis=-1, keepdims=True) + EPSILON)


def close_attention_kernel(attended, w_out, x_own, gain, w_gate, w_up, resid, normed, own_gate, own_up, own, *scratch):
    scatter, (send, recv, local), sems = scratch[:7], scratch[7:10], scratch[10:]
    width = w_out.shape[1]
    hidden = w_gate.shape[1]
    z = lax.axis_index("z")
    barrier, count = greet_neighbours(near())
    pl.semaphore_wait(barrier, count)

    def slab_of(whole):
        return lambda at: whole.at[:, pl.ds(pl.multiple_of(at * hidden, hidden), hidden)]

    chains, kept = [], []
    for k, (part, whole) in enumerate(((w_gate, own_gate), (w_up, own_up))):
        chains.append(Chain(part, slab_of(whole), sems, k))
        chains[k].start()
        kept.append(pltpu.make_async_copy(part, slab_of(whole)(z), local.at[1 + k]))
        kept[k].start()

    def arrive(h):
        for chain in chains:
            chain.arrive(h)

    def produce(turn, y, c, x, out):
        at = place_of(y, c, x)

        def step(i, carry):
            columns = pl.ds(pl.multiple_of(i * TILE, TILE), TILE)
            out[:, columns] = dot_wide(attended[at, :], w_out[:, columns]).astype(LOW)
            return carry

        lax.fori_loop(0, width // TILE, step, 0)

    run_scatter(produce, *scatter, beside=lambda: arrive(0))
    total, landed = scatter[2], scatter[4]

    def chunk(here):
        value = x_own[here, :].astype(jnp.float32) + summed(total, landed, here)
        resid[here, :] = value
        own[here, :] = (value * inverse_of(value) * gain[...]).astype(LOW)

    over_chunks(chunk)
    run_gather(own, normed, send, recv, local.at[0], arrive)
    for chain in chains:
        chain.finish()
    for copy in kept:
        copy.wait()


def close_attention(attended, w_out, x_own, gain, w_gate, w_up):
    block, width = x_own.shape
    hidden = w_gate.shape[1]
    return pl.pallas_call(
        close_attention_kernel,
        out_shape=(
            jax.ShapeDtypeStruct((block, width), jnp.float32),
            jax.ShapeDtypeStruct((8 * block, width), LOW),
            jax.ShapeDtypeStruct((width, 4 * hidden), LOW),
            jax.ShapeDtypeStruct((width, 4 * hidden), LOW),
        ),
        in_specs=[in_vmem()] * 6,
        out_specs=[in_vmem()] + [anywhere()] * 3,
        scratch_shapes=[pltpu.VMEM((block, width), LOW)]
        + scatter_scratch(width)
        + [dma(GATHER_COPIES), dma(GATHER_COPIES), dma(3), *chain_sems(2)],
        compiler_params=remote_params(2),
        cost_estimate=pl.CostEstimate(flops=0, bytes_accessed=450_000_000, transcendentals=0),
    )(attended, w_out, x_own, gain, w_gate, w_up)


def norm_back(value, gain, upstream):
    inverse = inverse_of(value)
    scaled = upstream * gain
    inner = jnp.mean(scaled * value, axis=-1, keepdims=True)
    return inverse * scaled - value * (inverse * inverse * inverse) * inner, upstream * value * inverse


def fold_rows(total, terms):
    for first in range(0, CHUNK, 8):
        total[...] += terms[first : first + 8, :]


def close_mlp_kernel(
    d_gate, d_up, w_gate, w_up, resid, upstream, gain, grad_a, grad_b, d_resid, gain_term, d_resid_whole, parts_a, parts_b, own, blocks, *scratch
):
    scatter, (send, recv, local, fetched, line_send, line_recv) = scratch[:7], scratch[7:]
    y, c, z, x = spot()
    width = w_gate.shape[0]
    order = [(r, k, q) for r, q in ((1 - y, 1 - x), (y, 1 - x), (1 - y, x), (y, x)) for k in (1 - c, c)]

    def fetch(turn):
        at = place_of(*order[turn])
        slot = turn % 2
        return [
            pltpu.make_async_copy(source.at[at], blocks.at[slot, m], fetched.at[slot, m])
            for m, source in enumerate((d_gate, d_up))
        ]

    for copy in fetch(0):
        copy.start()
    greet(near() + tuple(line_of()))
    to_layers = [
        copy
        for k, (grad, parts) in enumerate(((grad_a, parts_a), (grad_b, parts_b)))
        for copy in spread_columns(grad, parts, line_send.at[k], line_recv.at[k])
    ]
    for copy in to_layers:
        copy.start()

    def produce(turn, to_y, to_c, to_x, out):
        if turn < 7:
            for copy in fetch(turn + 1):
                copy.start()
        for copy in fetch(turn):
            copy.wait()

        def step(i, carry):
            columns = pl.ds(pl.multiple_of(i * TILE, TILE), TILE)
            part = dot_nt(blocks[turn % 2, 0], w_gate[columns, :]) + dot_nt(blocks[turn % 2, 1], w_up[columns, :])
            out[:, columns] = part.astype(LOW)
            return carry

        lax.fori_loop(0, width // TILE, step, 0)

    run_scatter(produce, *scatter)
    total, landed = scatter[2], scatter[4]
    gain_term[...] = jnp.zeros_like(gain_term)

    def chunk(here):
        back, terms = norm_back(resid[here, :], gain[...], summed(total, landed, here))
        value = upstream[here, :].astype(jnp.float32) + back
        d_resid[here, :] = value
        own[here, :] = value.astype(LOW)
        fold_rows(gain_term, terms)

    over_chunks(chunk)
    run_gather(own, d_resid_whole, send, recv, local.at[0])
    for copy in to_layers:
        copy.wait()


def close_mlp(d_gate, d_up, w_gate, w_up, resid, upstream, gain, *grads):
    block, width = resid.shape
    hidden = d_gate.shape[1]
    return pl.pallas_call(
        close_mlp_kernel,
        out_shape=(
            jax.ShapeDtypeStruct((block, width), jnp.float32),
            jax.ShapeDtypeStruct((8, width), jnp.float32),
            jax.ShapeDtypeStruct((8 * block, width), LOW),
            jax.ShapeDtypeStruct((3, width, hidden // 4), LOW),
            jax.ShapeDtypeStruct((3, width, hidden // 4), LOW),
        ),
        in_specs=[anywhere()] * 2 + [in_vmem()] * 5 + [anywhere()] * 2,
        out_specs=[in_vmem(), in_vmem()] + [anywhere()] * 3,
        scratch_shapes=[pltpu.VMEM((block, width), LOW), pltpu.VMEM((2, 2, block, hidden), LOW)]
        + scatter_scratch(width)
        + [dma(GATHER_COPIES), dma(GATHER_COPIES), dma(1), dma(2, 2), dma(2, 3), dma(2, 3)],
        compiler_params=remote_params(3),
        cost_estimate=pl.CostEstimate(flops=0, bytes_accessed=450_000_000, transcendentals=0),
    )(d_gate, d_up, w_gate, w_up, resid, upstream, gain, *grads)


def close_layer_kernel(d_qkv, w_qkv, x_own, d_resid, gain, mlp_term, grad_low, gain_grads, own, terms, layer_terms, part, column_terms, *scratch):
    scatter, (send, recv, term_send, term_recv, line_send, line_recv) = scratch[:7], scratch[7:]
    y, c, z, x = spot()
    partner = partner_of(y, c, z, x)
    moves = z != 2 * c + y
    width = w_qkv.shape[0]
    barrier = pltpu.get_barrier_semaphore()

    @pl.when(moves)
    def _():
        pl.semaphore_signal(barrier, inc=1, device_id=partner, device_id_type=MESH_ID)

    layer = others()
    line = line_of()
    for peer in layer + line:
        pl.semaphore_signal(barrier, inc=1, device_id=peer, device_id_type=MESH_ID)
    pl.semaphore_wait(barrier, len(layer + line) + moves.astype(jnp.int32))

    def part_of(half):
        def produce(turn, to_y, to_c, to_x, out):
            at = place_of(to_y, to_c, to_x, half)

            def step(i, carry):
                columns = pl.ds(pl.multiple_of(i * TILE, TILE), TILE)
                out[:, columns] = dot_nt(d_qkv[at, :], w_qkv[columns, :]).astype(LOW)
                return carry

            lax.fori_loop(0, width // TILE, step, 0)

        return Scatter(produce, *scatter, part=half, start=half * HALF, size=HALF)

    sums = [part_of(half) for half in (0, 1)]
    sums[0].begin()
    sums[0].relay()
    sums[1].begin()
    total, landed = scatter[2], scatter[4]
    terms[1] = mlp_term[...]
    terms[0] = jnp.zeros_like(mlp_term)
    trades = [
        remote(own.at[pl.ds(half * HALF, HALF)], grad_low.at[pl.ds(half * HALF, HALF)], send.at[half], recv.at[half], partner)
        for half in (0, 1)
    ]
    keeps = [
        pltpu.make_async_copy(own.at[pl.ds(half * HALF, HALF)], grad_low.at[pl.ds(half * HALF, HALF)], recv.at[half])
        for half in (0, 1)
    ]
    for half in (0, 1):
        if half == 1:
            sums[1].relay()
        sums[half].arrive()

        def step(i, carry):
            here = pl.ds(pl.multiple_of(half * HALF + i * CHUNK, CHUNK), CHUNK)
            back, products = norm_back(x_own[here, :].astype(jnp.float32), gain[...], summed(total, landed, here))
            own[here, :] = (d_resid[here, :] + back).astype(LOW)
            fold_rows(terms.at[0], products)
            return carry

        lax.fori_loop(0, HALF // CHUNK, step, 0)

        @pl.when(moves)
        def _():
            trades[half].start()

        @pl.when(jnp.logical_not(moves))
        def _():
            keeps[half].start()

    def columns_of(row, layers):
        return pl.ds(pl.multiple_of((4 * row) * HD, HD), layers * HD)

    spread = [
        remote(terms.at[:, :, columns_of(2 * peer[0] + peer[1], 4)], layer_terms.at[k], term_send.at[k], term_recv.at[k], peer)
        for k, peer in enumerate(layer)
    ]
    for copy in spread:
        copy.start()
    for copy in spread:
        copy.wait_recv()
    part[...] = sum((layer_terms[k] for k in range(7)), terms[:, :, columns_of(2 * y + c, 4)])
    lines = [
        remote(
            part.at[:, :, pl.ds(pl.multiple_of(peer[2] * HD, HD), HD)], column_terms.at[k], line_send.at[k], line_recv.at[k], peer
        )
        for k, peer in enumerate(line)
    ]
    for copy in lines:
        copy.start()
    for copy in lines:
        copy.wait_recv()
    gain_grads[...] = sum((column_terms[k] for k in range(3)), part[:, :, pl.ds(pl.multiple_of(z * HD, HD), HD)])
    for copy in spread + lines:
        copy.wait_send()
    for half in (0, 1):
        sums[half].finish()

    @pl.when(moves)
    def _():
        for copy in trades:
            copy.wait()

    @pl.when(jnp.logical_not(moves))
    def _():
        for copy in keeps:
            copy.wait()


def close_layer(d_qkv, w_qkv, x_own, d_resid, gain, mlp_term):
    block, width = x_own.shape
    return pl.pallas_call(
        close_layer_kernel,
        out_shape=(jax.ShapeDtypeStruct((block, width), LOW), jax.ShapeDtypeStruct((2, 8, width // 16), jnp.float32)),
        in_specs=[in_vmem()] * 6,
        out_specs=[anywhere(), in_vmem()],
        scratch_shapes=[
            pltpu.VMEM((block, width), LOW),
            pltpu.VMEM((2, 8, width), jnp.float32),
            pltpu.VMEM((7, 2, 8, width // 4), jnp.float32),
            pltpu.VMEM((2, 8, width // 4), jnp.float32),
            pltpu.VMEM((3, 2, 8, width // 16), jnp.float32),
        ]
        + scatter_scratch(width, 2)
        + [dma(2), dma(2), dma(7), dma(7), dma(3), dma(3)],
        compiler_params=remote_params(4),
        cost_estimate=pl.CostEstimate(flops=0, bytes_accessed=350_000_000, transcendentals=0),
    )(d_qkv, w_qkv, x_own, d_resid, gain, mlp_term)


def doc_start(ends, place):
    start = jnp.zeros_like(place)
    for k in range(8):
        start = jnp.where(ends[k] <= place, ends[k], start)
    return jnp.where(place < ends[7], start, LEN)


def sigmoid_of(raw):
    return pl.reciprocal(1.0 + jnp.exp2(math.log2(LEN) - raw * (math.log2(math.e) / math.sqrt(HD))), approx=True)


def tile_at(index):
    return pl.ds(pl.multiple_of(index * TILE, TILE), TILE)


def head_of(array, rows, part, head):
    first = (part * (array.shape[1] // 3) // HD + head) * HD
    return array[rows, first : first + HD]


def attend_kernel(ends, qkv, out, total):
    i = pl.program_id(0)
    heads = qkv.shape[1] // (3 * HD)
    total[...] = jnp.zeros_like(total)
    q_place = i * TILE + lax.broadcasted_iota(jnp.int32, (TILE, 1), 0)
    q_start = doc_start(ends, q_place)

    def tile(j, diagonal):
        k_place = j * TILE + lax.broadcasted_iota(jnp.int32, (1, TILE), 1)
        allowed = k_place >= q_start
        if diagonal:
            allowed = allowed & (k_place <= q_place)
        for head in range(heads):
            raw = dot_nt(head_of(qkv, tile_at(i), 0, head), head_of(qkv, tile_at(j), 1, head))
            weight = jnp.where(allowed, sigmoid_of(raw), 0.0).astype(LOW)
            total[head] += dot_wide(weight, head_of(qkv, tile_at(j), 2, head))

    def step(j, carry):
        tile(j, False)
        return carry

    lax.fori_loop(0, i, step, 0)
    tile(i, True)
    for head in range(heads):
        out[tile_at(i), head * HD : (head + 1) * HD] = total[head].astype(LOW)


def open_mlp_kernel(normed, w_gate, w_up, upstream, gate, up, hidden, upstream_whole, send, recv, local):
    i = pl.program_id(0)
    y, c, z, x = spot()
    steps = pl.num_programs(0)
    gather = Gather(lambda half: upstream.at[pl.ds(half * HALF, HALF)], upstream_whole, send, recv)
    keep = pltpu.make_async_copy(upstream, upstream_whole.at[place_of(y, c, x)], local.at[0])

    @pl.when(i == 0)
    def _():
        greet(near())
        gather.start(0)
        gather.start(1)
        keep.start()

    @pl.when(i == steps - 3)
    def _():
        gather.pass_first()

    def step(n, carry):
        columns = pl.ds(pl.multiple_of(n * HALF, HALF), HALF)
        gate_part, up_part = dot_wide(normed[...], w_gate[:, columns]), dot_wide(normed[...], w_up[:, columns])
        gate[:, columns] = gate_part
        up[:, columns] = up_part
        hidden[:, columns] = (gate_part * jax.nn.sigmoid(gate_part) * up_part).astype(LOW)
        return carry

    lax.fori_loop(0, w_gate.shape[1] // HALF, step, 0)

    @pl.when(i == steps - 1)
    def _():
        gather.pass_second()
        gather.pass_far()
        gather.finish()
        keep.wait()


def open_mlp(normed, w_gate, w_up, upstream):
    places, width = normed.shape
    hidden = w_gate.shape[1]
    rows = lambda columns: pl.BlockSpec((TILE, columns), lambda i: (i, 0))
    whole = lambda array: pl.BlockSpec(array.shape, lambda i: (0, 0))
    return pl.pallas_call(
        open_mlp_kernel,
        out_shape=(
            jax.ShapeDtypeStruct((places, hidden), jnp.float32),
            jax.ShapeDtypeStruct((places, hidden), jnp.float32),
            jax.ShapeDtypeStruct((places, hidden), LOW),
            jax.ShapeDtypeStruct((places, width), LOW),
        ),
        grid=(places // TILE,),
        in_specs=[rows(width), whole(w_gate), whole(w_up), whole(upstream)],
        out_specs=[rows(hidden), rows(hidden), rows(hidden), anywhere()],
        scratch_shapes=[dma(GATHER_COPIES), dma(GATHER_COPIES), dma(1)],
        compiler_params=remote_params(5),
        cost_estimate=pl.CostEstimate(flops=0, bytes_accessed=250_000_000, transcendentals=0),
    )(normed, w_gate, w_up, upstream)


def out_turns():
    y, c, z, x = spot()
    owners = [((y, c, 2 * x + j // 2, j % 2), (z == 2 * x + j // 2) & (x == j % 2)) for j in range(4)]
    holders = [((y, c, j, z // 2), (z == j) & (x == z // 2)) for j in range(4)]
    return owners, holders


def attend_back_kernel(
    ends, qkv, grads, out_grad, mixed, out, out_parts, mixed_home, query_total, key_total, value_total, send, recv, trade_send, trade_recv
):
    j = pl.program_id(0)
    y, c, z, x = spot()
    heads = qkv.shape[1] // (3 * HD)
    shard = out_grad.shape[0] // 4
    owners, holders = out_turns()
    partner = partner_of(y, c, z, x)
    moves = z != 2 * c + y
    trade_copy = remote(mixed, mixed_home, trade_send.at[0], trade_recv.at[0], partner)
    keep = pltpu.make_async_copy(mixed, mixed_home, trade_recv.at[0])

    def to_owner(turn):
        return remote(out_grad.at[pl.ds(turn * shard, shard)], out_parts.at[z], send.at[turn], recv.at[z], owners[turn][0])

    def to_self(turn):
        return pltpu.make_async_copy(out_grad.at[pl.ds(turn * shard, shard)], out_parts.at[z], recv.at[z])

    @pl.when(j == 0)
    def _():
        query_total[...] = jnp.zeros_like(query_total)
        barrier = pltpu.get_barrier_semaphore()
        for peer, here in holders:

            @pl.when(jnp.logical_not(here))
            def _():
                pl.semaphore_signal(barrier, inc=1, device_id=peer, device_id_type=MESH_ID)

        @pl.when(moves)
        def _():
            pl.semaphore_signal(barrier, inc=1, device_id=partner, device_id_type=MESH_ID)

        pl.semaphore_wait(barrier, 4 - (x == z // 2).astype(jnp.int32) + moves.astype(jnp.int32))

        @pl.when(moves)
        def _():
            trade_copy.start()

        @pl.when(jnp.logical_not(moves))
        def _():
            keep.start()

        for turn in range(4):

            @pl.when(jnp.logical_not(owners[turn][1]))
            def _():
                to_owner(turn).start()

            @pl.when(owners[turn][1])
            def _():
                to_self(turn).start()

    key_total[...] = jnp.zeros_like(key_total)
    value_total[...] = jnp.zeros_like(value_total)
    here = tile_at(j)
    k_place = j * TILE + lax.broadcasted_iota(jnp.int32, (TILE, 1), 0)
    turned = [head_of(qkv, here, 1, head).T for head in range(heads)]

    def tile(i, diagonal):
        q_place = i * TILE + lax.broadcasted_iota(jnp.int32, (1, TILE), 1)
        allowed = k_place >= doc_start(ends, q_place)
        if diagonal:
            allowed = allowed & (k_place <= q_place)
        for head in range(heads):
            query, grad = head_of(qkv, tile_at(i), 0, head), grads[tile_at(i), head * HD : (head + 1) * HD]
            sig = jnp.where(allowed, sigmoid_of(dot_nt(head_of(qkv, here, 1, head), query)), 0.0)
            value_total[head] += dot_wide(sig.astype(LOW), grad)
            d_score = (dot_nt(head_of(qkv, here, 2, head), grad) * (sig * (1.0 - sig))).astype(LOW)
            key_total[head] += dot_wide(d_score, query)
            query_total[head, :, tile_at(i)] += dot_wide(turned[head], d_score)

    def step(i, carry):
        tile(i, False)
        return carry

    tile(j, True)
    lax.fori_loop(j + 1, LEN // TILE, step, 0)
    scale = 1.0 / math.sqrt(HD)
    for head in range(heads):
        first = head * HD
        out[here, heads * HD + first : (heads + 1) * HD + first] = (key_total[head] * scale).astype(LOW)
        out[here, 2 * heads * HD + first : (2 * heads + 1) * HD + first] = value_total[head].astype(LOW)
        out[here, first : first + HD] = (query_total[head, :, here] * scale).T.astype(LOW)

    @pl.when(j == LEN // TILE - 1)
    def _():
        for turn in range(4):

            @pl.when(jnp.logical_not(owners[turn][1]))
            def _():
                to_owner(turn).wait_send()

            @pl.when(jnp.logical_not(holders[turn][1]))
            def _():
                landed = out_parts.at[turn]
                remote(landed, landed, send.at[turn], recv.at[turn], holders[turn][0]).wait_recv()

            @pl.when(owners[turn][1])
            def _():
                to_self(turn).wait()

        @pl.when(moves)
        def _():
            trade_copy.wait()

        @pl.when(jnp.logical_not(moves))
        def _():
            keep.wait()


def attend(ends, qkv):
    places, width = qkv.shape
    heads = width // (3 * HD)
    whole = lambda columns: pl.BlockSpec((places, columns), lambda i: (0, 0))
    return pl.pallas_call(
        attend_kernel,
        out_shape=jax.ShapeDtypeStruct((places, width // 3), LOW),
        grid=(places // TILE,),
        in_specs=[pl.BlockSpec(memory_space=pltpu.SMEM), whole(width)],
        out_specs=whole(width // 3),
        scratch_shapes=[pltpu.VMEM((heads, TILE, HD), jnp.float32)],
        compiler_params=pltpu.CompilerParams(vmem_limit_bytes=VMEM_LIMIT),
        cost_estimate=pl.CostEstimate(flops=0, bytes_accessed=150_000_000, transcendentals=0),
    )(ends, qkv)


def attend_back(ends, qkv, grads, out_grad, mixed):
    places, width = qkv.shape
    heads = width // (3 * HD)
    whole = lambda columns: pl.BlockSpec((places, columns), lambda j: (0, 0))
    return pl.pallas_call(
        attend_back_kernel,
        out_shape=(
            jax.ShapeDtypeStruct((places, width), LOW),
            jax.ShapeDtypeStruct((4, out_grad.shape[0] // 4, out_grad.shape[1]), LOW),
            jax.ShapeDtypeStruct(mixed.shape, LOW),
        ),
        grid=(places // TILE,),
        in_specs=[pl.BlockSpec(memory_space=pltpu.SMEM), whole(width), whole(width // 3), anywhere(), pl.BlockSpec(mixed.shape, lambda j: (0, 0))],
        out_specs=[whole(width), anywhere(), anywhere()],
        scratch_shapes=[
            pltpu.VMEM((heads, HD, places), jnp.float32),
            pltpu.VMEM((heads, TILE, HD), jnp.float32),
            pltpu.VMEM((heads, TILE, HD), jnp.float32),
            dma(4),
            dma(4),
            dma(1),
            dma(1),
        ],
        compiler_params=remote_params(6),
        cost_estimate=pl.CostEstimate(flops=0, bytes_accessed=300_000_000, transcendentals=0),
    )(ends, qkv, grads, out_grad, mixed)


LAYER = ("y", "c", "x")
PLACES = ("c", "y", "x")
ALL = ("y", "c", "z", "x")


def trade(part):
    pairs = []
    for y in range(2):
        for c in range(2):
            for z in range(4):
                for x in range(2):
                    pairs.append((((y * 2 + c) * 4 + z) * 2 + x, (((z % 2) * 2 + z // 2) * 4 + 2 * c + y) * 2 + x))
    return lax.ppermute(part, ALL, pairs)


def after(first, then):
    return lax.optimization_barrier((first, then))[1]


def body_layers(
    tokens, lengths, cotangent, w_query, w_key, w_value, w_out, w_gate, w_up, w_down, gain_attn, gain_mlp
):
    rows_here, block, width = tokens.shape
    members = lax.axis_size(LAYER)
    layers = lax.axis_size("z")
    shard = w_query.shape[0]
    owned = width // members
    facts = jnp.zeros((8, 2 * shard), jnp.float32)
    facts = facts.at[0, :shard].set(gain_attn.astype(jnp.float32)).at[1, :shard].set(gain_mlp.astype(jnp.float32))
    facts = facts.at[2, : lengths.shape[1]].set(lengths[0].astype(jnp.float32))
    layer_x, w_qkv, facts = begin(tokens.reshape(block, width), w_query, w_key, w_value, facts)
    full_gain_attn, full_gain_mlp = facts[:, :, :, 0, :shard].reshape(1, width), facts[:, :, :, 1, :shard].reshape(1, width)
    layer = lax.axis_index("z")
    own_lengths = facts[:, 0, 0, 2, : lengths.shape[1]].reshape(2, 2, -1)
    own_lengths = lax.dynamic_slice(own_lengths, (layer % 2, layer // 2, 0), (1, 1, own_lengths.shape[2]))[0, 0]
    ends = jnp.cumsum(own_lengths.astype(jnp.int32))
    place = (4 * lax.axis_index("c") + 2 * lax.axis_index("y") + lax.axis_index("x")) * block
    x_own = lax.dynamic_slice_in_dim(layer_x, place, block, 0)
    layer_normed = norm_forward(layer_x.astype(jnp.float32), full_gain_attn)[0].astype(LOW)
    out_rows = lax.all_gather(after(facts, w_out), ("z", "x"), axis=0, tiled=True)
    w_out_own = lax.dynamic_slice_in_dim(out_rows, lax.axis_index("x") * owned, owned, 0)

    qkv = dot_wide(layer_normed, w_qkv).astype(LOW)
    upstream = trade(after(facts, cotangent)).reshape(block, width)
    attended = attend(ends, qkv)
    resid, layer_mlp, own_gate, own_up = close_attention(after(upstream, attended), w_out_own, x_own, full_gain_mlp, w_gate, w_up)

    own_down = lax.all_gather(after(resid, w_down), "z", axis=0, tiled=True)
    gate, up_part, hidden, layer_upstream = open_mlp(layer_mlp, own_gate, own_up, upstream)
    part = dot_wide(hidden, own_down).astype(LOW)
    mixed_sum = lax.psum_scatter(part, PLACES, scatter_dimension=0, tiled=True)
    down_term = contract_rows(after(part, hidden), layer_upstream).astype(LOW)
    down_rows = w_down.shape[0]
    down_parts = []
    for up in range(1, 4):
        layers_pairs = [(at, (at + up) % 4) for at in range(4)]
        slab = lax.dynamic_slice_in_dim(down_term, (layer + up) % 4 * down_rows, down_rows, 0)
        down_parts.append(lax.ppermute(slab, "z", layers_pairs))
    d_hidden = contract_cols(after(down_term, layer_upstream), own_down)
    d_gate, d_up = gate_backward(d_hidden, gate, up_part, jax.nn.sigmoid(gate))
    gate_term, up_term = contract_rows(layer_mlp, d_gate).astype(LOW), contract_rows(layer_mlp, d_up).astype(LOW)
    d_resid, gain_mlp_term, layer_d_resid, gate_parts, up_parts = close_mlp(
        after((mixed_sum, *down_parts), d_gate), d_up, own_gate, own_up, resid, upstream, full_gain_mlp, gate_term, up_term
    )

    def own_part(whole, parts):
        own = lax.dynamic_slice_in_dim(whole, layer * parts.shape[2], parts.shape[2], 1)
        return own.astype(jnp.float32) + jnp.sum(parts.astype(jnp.float32), axis=0)

    mixed = (resid + after(layer_d_resid, mixed_sum).astype(jnp.float32)).astype(LOW)
    grad_down = lax.dynamic_slice_in_dim(down_term, layer * down_rows, down_rows, 0).astype(jnp.float32)
    grad_down = grad_down + sum(slab.astype(jnp.float32) for slab in down_parts)

    out_term = contract_rows(attended, layer_d_resid).astype(LOW)
    d_attended = contract_cols(layer_d_resid, w_out_own).astype(LOW)
    d_qkv, out_parts, mixed = attend_back(ends, qkv, d_attended, out_term, mixed)
    mixed = mixed.reshape(rows_here, block, width)
    grad_gate, grad_up = own_part(gate_term, gate_parts), own_part(up_term, up_parts)
    grad_out = jnp.sum(out_parts.astype(jnp.float32), axis=0)
    qkv_term = contract_rows(layer_normed, d_qkv).astype(LOW)
    grad_low, gain_grads = close_layer(
        after(qkv_term, d_qkv), w_qkv, x_own, d_resid, full_gain_attn, gain_mlp_term
    )
    grad_tokens = grad_low.astype(jnp.float32).reshape(rows_here, block, width)

    qkv_term = qkv_term.reshape(4, layers, 2 * shard, 3 * owned).transpose(1, 0, 2, 3)
    qkv_term = qkv_term.reshape(layers * members * shard, 3 * owned)
    qkv_term = lax.psum_scatter(qkv_term, "z", scatter_dimension=0, tiled=True)
    qkv_term = lax.all_to_all(qkv_term.reshape(members, shard, 3 * owned), LAYER, 0, 0)
    qkv_term = qkv_term.reshape(members, shard, 3, owned).transpose(2, 1, 0, 3).astype(jnp.float32)
    grad_query, grad_key, grad_value = qkv_term.reshape(3, shard, width)
    gain_grads = lax.dynamic_index_in_dim(jnp.sum(gain_grads, axis=1).reshape(2, 2, shard), lax.axis_index("x"), 1, False)
    return (
        mixed,
        grad_tokens,
        grad_query,
        grad_key,
        grad_value,
        grad_out,
        grad_gate,
        grad_up,
        grad_down,
        gain_grads[0],
        gain_grads[1],
    )


def body_any(
    tokens,
    lengths,
    cotangent,
    w_query,
    w_key,
    w_value,
    w_out,
    w_gate,
    w_up,
    w_down,
    gain_attn,
    gain_mlp,
):
    rows_here, block, width = tokens.shape
    count = rows_here * block
    scale = 1.0 / math.sqrt(HD)
    kv_place = lax.axis_index("kv")
    key_places = kv_place * block + jnp.arange(block, dtype=jnp.int32)
    attn_set = (
        lax.all_gather(w_query, ("row", "kv"), axis=0, tiled=True),
        lax.all_gather(w_key, ("row", "kv"), axis=0, tiled=True),
        lax.all_gather(w_value, ("row", "kv"), axis=0, tiled=True),
        lax.all_gather(w_out, ("row", "kv"), axis=0, tiled=True),
        lax.all_gather(gain_attn, ("row", "kv"), axis=0, tiled=True),
        lax.all_gather(gain_mlp, ("row", "kv"), axis=0, tiled=True),
    )
    full_query, full_key, full_value, full_out, full_gain_attn, full_gain_mlp = attn_set
    flat = tokens.reshape(count, width).astype(jnp.float32)
    normed_attn, inverse_attn = norm_forward(flat, full_gain_attn)
    normed_attn_low = normed_attn.astype(jnp.bfloat16)
    query_low = jnp.dot(normed_attn_low, full_query, preferred_element_type=jnp.float32).astype(
        jnp.bfloat16
    )
    key_low = jnp.dot(normed_attn_low, full_key, preferred_element_type=jnp.float32).astype(
        jnp.bfloat16
    )
    value_low = jnp.dot(normed_attn_low, full_value, preferred_element_type=jnp.float32).astype(
        jnp.bfloat16
    )
    key_heads = key_low.reshape(rows_here, block, H, HD)
    value_heads = value_low.reshape(rows_here, block, H, HD)
    segment, valid = segment_table(lengths)
    key_segment = lax.dynamic_slice_in_dim(segment, kv_place * block, block, 1)
    key_valid = lax.dynamic_slice_in_dim(valid, kv_place * block, block, 1)
    queries_all = lax.all_gather(
        query_low.reshape(rows_here, block, width), "kv", axis=1, tiled=True
    )
    which = 0
    query_rows = queries_all[which]
    query_segment = segment[which]
    sigmoid_part, allowed = score_block(
        query_rows,
        key_heads[which],
        query_segment,
        key_segment[which],
        key_valid[which],
        jnp.int32(0),
        key_places,
    )
    weight = (sigmoid_part * allowed).astype(jnp.bfloat16)
    summed = jnp.einsum(
        "hqk,khd->qhd", weight, value_heads[which], preferred_element_type=jnp.float32
    )
    pieces = [
        lax.psum_scatter(
            summed.reshape(lax.axis_size("kv") * block, width).astype(jnp.bfloat16),
            "kv",
            scatter_dimension=0,
            tiled=True,
        ).astype(jnp.float32)
    ]
    attended_low = jnp.stack(pieces).reshape(count, width).astype(jnp.bfloat16)
    resid = flat + jnp.dot(attended_low, full_out, preferred_element_type=jnp.float32)
    normed_mlp, inverse_mlp = norm_forward(resid, full_gain_mlp)
    normed_mlp_low = normed_mlp.astype(jnp.bfloat16)
    upstream_low = cotangent.reshape(count, width)
    upstream = upstream_low.astype(jnp.float32)
    slice_gate, slice_up, slice_down = (
        lax.all_gather(w_gate, "row", axis=1, tiled=True),
        lax.all_gather(w_up, "row", axis=1, tiled=True),
        lax.all_gather(w_down, "row", axis=0, tiled=True),
    )
    row_normed, row_upstream = (
        lax.all_gather(normed_mlp_low.reshape(rows_here, block, width), "kv", axis=1, tiled=True),
        lax.all_gather(cotangent, "kv", axis=1, tiled=True),
    )
    normed_rows = row_normed.reshape(rows_here * LEN, width)
    upstream_rows = row_upstream.reshape(rows_here * LEN, width)
    gate = jnp.dot(normed_rows, slice_gate, preferred_element_type=jnp.float32)
    up_part = jnp.dot(normed_rows, slice_up, preferred_element_type=jnp.float32)
    sigmoid_gate = jax.nn.sigmoid(gate)
    hidden_low = (gate * sigmoid_gate * up_part).astype(jnp.bfloat16)
    hidden_rows = hidden_low.reshape(rows_here, LEN, hidden_low.shape[1])
    which = 0
    hidden_part = hidden_rows[which]
    outputs = [
        lax.psum_scatter(
            jnp.dot(hidden_part, slice_down, preferred_element_type=jnp.float32).astype(
                jnp.bfloat16
            ),
            "kv",
            scatter_dimension=0,
            tiled=True,
        ).astype(jnp.float32)
    ]
    result = resid + jnp.stack(outputs).reshape(count, width)
    d_hidden = contract_cols(upstream_rows, slice_down)
    d_gate, d_up = gate_backward(d_hidden, gate, up_part, sigmoid_gate)
    partial_normed = contract_cols(d_gate, slice_gate) + contract_cols(d_up, slice_up)
    d_normed_mlp = (
        lax.psum_scatter(
            partial_normed.reshape(rows_here, LEN, width).astype(jnp.bfloat16),
            "kv",
            scatter_dimension=1,
            tiled=True,
        )
        .astype(jnp.float32)
        .reshape(count, width)
    )
    grad_gate, grad_up, grad_down = (
        lax.psum_scatter(
            contract_rows(normed_rows, d_gate).astype(jnp.bfloat16),
            "row",
            scatter_dimension=1,
            tiled=True,
        ).astype(jnp.float32),
        lax.psum_scatter(
            contract_rows(normed_rows, d_up).astype(jnp.bfloat16),
            "row",
            scatter_dimension=1,
            tiled=True,
        ).astype(jnp.float32),
        lax.psum_scatter(
            contract_rows(hidden_low, upstream_rows).astype(jnp.bfloat16),
            "row",
            scatter_dimension=0,
            tiled=True,
        ).astype(jnp.float32),
    )
    mixed = result.astype(jnp.bfloat16).reshape(rows_here, block, width)
    back_mlp, gain_mlp_term = norm_backward(resid, inverse_mlp, full_gain_mlp, d_normed_mlp)
    d_resid = upstream + back_mlp
    d_resid_low = d_resid.astype(jnp.bfloat16)
    d_attended = contract_cols(d_resid_low, full_out).astype(jnp.bfloat16)
    grads_all = lax.all_gather(
        d_attended.reshape(rows_here, block, width), "kv", axis=1, tiled=True
    )
    query_block = min(512, LEN)
    block_count = LEN // query_block
    which = 0

    def sweep(carry, index, which=which):
        key_total, value_total = carry
        start = index * query_block
        query_rows = lax.dynamic_slice_in_dim(queries_all[which], start, query_block, 0)
        grad_rows = lax.dynamic_slice_in_dim(grads_all[which], start, query_block, 0)
        query_segment = lax.dynamic_slice_in_dim(segment[which], start, query_block, 0)
        sigmoid_part, allowed = score_block(
            query_rows,
            key_heads[which],
            query_segment,
            key_segment[which],
            key_valid[which],
            start,
            key_places,
        )
        weight = (sigmoid_part * allowed).astype(jnp.bfloat16)
        grad_heads = grad_rows.reshape(query_block, H, HD)
        value_total = value_total + jnp.einsum(
            "hqk,qhd->khd", weight, grad_heads, preferred_element_type=jnp.float32
        )
        d_weight = jnp.einsum(
            "qhd,khd->hqk", grad_heads, value_heads[which], preferred_element_type=jnp.float32
        )
        d_score = (d_weight * sigmoid_part * (1.0 - sigmoid_part) * allowed).astype(jnp.bfloat16)
        query_part = (
            jnp.einsum(
                "hqk,khd->qhd", d_score, key_heads[which], preferred_element_type=jnp.float32
            )
            * scale
        )
        key_total = (
            key_total
            + jnp.einsum(
                "hqk,qhd->khd",
                d_score,
                query_rows.reshape(query_block, H, HD),
                preferred_element_type=jnp.float32,
            )
            * scale
        )
        return ((key_total, value_total), query_part.reshape(query_block, width))

    zeros = jnp.zeros((block, H, HD), jnp.float32)
    totals, query_parts = lax.scan(sweep, (zeros, zeros), jnp.arange(block_count, dtype=jnp.int32))
    query_terms = [query_parts.reshape(LEN, width)]
    key_grads = [totals[0].reshape(block, width)]
    value_grads = [totals[1].reshape(block, width)]
    query_local = lax.psum_scatter(
        jnp.stack(query_terms).astype(jnp.bfloat16), "kv", scatter_dimension=1, tiled=True
    ).astype(jnp.float32)
    d_query_low = query_local.reshape(count, width).astype(jnp.bfloat16)
    d_key_low = jnp.stack(key_grads).reshape(count, width).astype(jnp.bfloat16)
    d_value_low = jnp.stack(value_grads).reshape(count, width).astype(jnp.bfloat16)
    d_normed_attn = (
        contract_cols(d_query_low, full_query)
        + contract_cols(d_key_low, full_key)
        + contract_cols(d_value_low, full_value)
    )
    back_attn, gain_attn_term = norm_backward(flat, inverse_attn, full_gain_attn, d_normed_attn)
    grad_tokens = (d_resid + back_attn).reshape(rows_here, block, width)
    projected_low = jnp.concatenate((d_query_low, d_key_low, d_value_low), axis=1)
    grad_projections = lax.psum_scatter(
        contract_rows(normed_attn_low, projected_low),
        ("row", "kv"),
        scatter_dimension=0,
        tiled=True,
    )
    out_term = contract_rows(attended_low, d_resid_low)
    grad_out, grad_gain_attn, grad_gain_mlp = (
        lax.psum_scatter(out_term, ("row", "kv"), scatter_dimension=0, tiled=True),
        lax.psum_scatter(gain_attn_term, ("row", "kv"), scatter_dimension=0, tiled=True),
        lax.psum_scatter(gain_mlp_term, ("row", "kv"), scatter_dimension=0, tiled=True),
    )
    grad_query = grad_projections[:, :width]
    grad_key = grad_projections[:, width : 2 * width]
    grad_value = grad_projections[:, 2 * width :]
    return (
        mixed,
        grad_tokens,
        grad_query,
        grad_key,
        grad_value,
        grad_out,
        grad_gate,
        grad_up,
        grad_down,
        grad_gain_attn,
        grad_gain_mlp,
    )


def solution(mesh):
    rows, columns = mesh.shape["row"], mesh.shape["kv"]
    if rows == 4 and columns == 2 * rows:
        mesh = Mesh(mesh.devices.reshape(2, 2, rows, 2), ("y", "c", "z", "x"))
        row, kv, run = ("y", "c"), ("z", "x"), body_layers
    else:
        row, kv, run = "row", "kv", body_any
    both = ("y", "c", "z", "x") if run is body_layers else ("row", "kv")
    tall, wide, flat = P(both, None), P(None, both), P(both)
    tokens = P(row, kv, None)
    return jax.shard_map(
        run,
        mesh=mesh,
        in_specs=(tokens, P(row, None), tokens, tall, tall, tall, tall, wide, wide, tall, flat, flat),
        out_specs=(tokens, tokens, tall, tall, tall, tall, wide, wide, tall, flat, flat),
        check_vma=False,
    )
```

```python
import functools
import math

import jax
import jax.numpy as jnp
from jax import lax
from jax.experimental import pallas as pl
from jax.experimental.pallas import tpu as pltpu
from jax.sharding import Mesh, PartitionSpec as P

H = 16
HD = 128
LEN = 4096


EPSILON = 1e-05


def contract_rows(left, right):
    return lax.dot_general(
        left, right, (((0,), (0,)), ((), ())), preferred_element_type=jnp.float32
    )


def contract_cols(left, right):
    return lax.dot_general(
        left, right, (((1,), (1,)), ((), ())), preferred_element_type=jnp.float32
    )


def norm_forward(value, gain):
    inverse = lax.rsqrt(jnp.mean(value * value, axis=-1, keepdims=True) + EPSILON)
    return (value * inverse * gain.astype(jnp.float32), inverse)


def norm_backward(value, inverse, gain, upstream):
    scaled = upstream * gain.astype(jnp.float32)
    inner = jnp.mean(scaled * value, axis=-1, keepdims=True)
    back = inverse * scaled - value * (inverse * inverse * inverse) * inner
    gain_term = jnp.sum(upstream * value * inverse, axis=0)
    return (back, gain_term)


def segment_table(lengths):
    ends = jnp.cumsum(lengths, axis=-1)
    places = jnp.arange(LEN, dtype=jnp.int32)
    segment = jnp.sum((ends[:, None, :] <= places[None, :, None]).astype(jnp.int32), axis=-1)
    valid = places[None, :] < ends[:, -1:]
    return (segment, valid)


def score_block(
    query_rows, key_heads, query_segment, key_segment, key_valid, query_start, key_places
):
    count = query_rows.shape[0]
    query_heads = query_rows.reshape(count, H, HD)
    raw = jnp.einsum("qhd,khd->hqk", query_heads, key_heads, preferred_element_type=jnp.float32)
    scores = raw * (1.0 / math.sqrt(HD)) - math.log(LEN)
    places = query_start + jnp.arange(count, dtype=jnp.int32)
    allowed = (
        (key_places[None, :] <= places[:, None])
        & (key_segment[None, :] == query_segment[:, None])
        & key_valid[None, :]
    )
    return (jax.nn.sigmoid(scores), allowed.astype(jnp.float32)[None])


def gate_backward(d_hidden, gate, up_part, sigmoid_gate):
    d_gate = (d_hidden * up_part * sigmoid_gate * (1.0 + gate * (1.0 - sigmoid_gate))).astype(
        jnp.bfloat16
    )
    d_up = (d_hidden * gate * sigmoid_gate).astype(jnp.bfloat16)
    return (d_gate, d_up)


TILE = 512
LOW = jnp.bfloat16
VMEM_LIMIT = 60 * 1024 * 1024


def dot_nt(left, right):
    return lax.dot_general(left, right, (((1,), (1,)), ((), ())), preferred_element_type=jnp.float32)


def dot_wide(left, right):
    return jnp.dot(left, right, preferred_element_type=jnp.float32)


HALF = TILE // 2
CHUNK = 32
MESH_ID = pl.DeviceIdType.MESH


def flip(bit, by):
    return bit + by - 2 * bit * by


def spot():
    return tuple(lax.axis_index(name) for name in ("y", "c", "z", "x"))


def near():
    y, c, z, x = spot()
    return (y, c, z, 1 - x), (1 - y, c, z, x), (y, 1 - c, z, x)


def partner_of(y, c, z, x):
    return lax.rem(z, 2), z // 2, 2 * c + y, x


def place_of(y, c, x, half=None):
    first = (4 * c + 2 * y + x) * TILE
    if half is None:
        return pl.ds(pl.multiple_of(first, TILE), TILE)
    return pl.ds(pl.multiple_of(first + half * HALF, HALF), HALF)


def quarter_of(y, c, x, half, quarter):
    return pl.ds(pl.multiple_of((4 * c + 2 * y + x) * TILE + half * HALF + quarter * (HALF // 2), HALF // 2), HALF // 2)


def remote(src, dst, send, recv, peer):
    return pltpu.make_async_remote_copy(
        src_ref=src, dst_ref=dst, send_sem=send, recv_sem=recv, device_id=peer, device_id_type=MESH_ID
    )


def greet(peers):
    barrier = pltpu.get_barrier_semaphore()
    for peer in peers:
        pl.semaphore_signal(barrier, inc=1, device_id=peer, device_id_type=MESH_ID)
    pl.semaphore_wait(barrier, len(peers))


class Gather:
    def __init__(self, own, whole, send, recv):
        y, c, z, x = spot()
        across_x, across_y, core = near()

        def passed(k, at, peer):
            return remote(whole.at[at], whole.at[at], send.at[k], recv.at[k], peer)

        self.halves = []
        for half in (0, 1):
            k, at = 9 * half, place_of(y, c, x, half)
            mine = [
                remote(own(half), whole.at[at], send.at[k + m], recv.at[k + m], peer)
                for m, peer in enumerate((across_x, across_y, core))
            ]
            held_x, held_y = (y, c, 1 - x), (1 - y, c, x)
            far = (1 - y, c, 1 - x)
            self.halves.append(
                (
                    mine,
                    passed(k + 3, quarter_of(*held_x, half, 0), across_y),
                    passed(k + 4, quarter_of(*held_y, half, 1), across_x),
                    [passed(k + 5, place_of(*held_x, half), core), passed(k + 6, place_of(*held_y, half), core)],
                    [passed(k + 7 + q, quarter_of(*far, half, q), core) for q in (0, 1)],
                )
            )

    def start(self, half):
        for copy in self.halves[half][0]:
            copy.start()

    def pass_near(self, half):
        mine, over_y, over_x, from_near, from_far = self.halves[half]
        mine[0].wait_recv()
        over_y.start()
        from_near[0].start()
        mine[1].wait_recv()
        over_x.start()
        from_near[1].start()

    def pass_far(self, half):
        mine, over_y, over_x, from_near, from_far = self.halves[half]
        over_y.wait_recv()
        from_far[0].start()
        over_x.wait_recv()
        from_far[1].start()

    def finish(self):
        for mine, over_y, over_x, from_near, from_far in self.halves:
            for copy in [mine[2]] + from_near + from_far:
                copy.wait_recv()
            for copy in mine + [over_y, over_x] + from_near + from_far:
                copy.wait_send()


GATHER_COPIES = 18


class GatherWhole:
    def __init__(self, own, whole, send, recv):
        y, c, z, x = spot()
        across_x, across_y, core = near()

        def from_own(k, half, peer):
            return remote(own(half), whole.at[place_of(y, c, x, half)], send.at[k], recv.at[k], peer)

        def passed(k, at, peer):
            return remote(whole.at[at], whole.at[at], send.at[k], recv.at[k], peer)

        self.mine = [
            [from_own(0, 0, across_x), from_own(1, 0, across_y), from_own(2, 0, core)],
            [from_own(3, 1, across_x), from_own(4, 1, across_y), from_own(5, 1, core)],
        ]
        held_x = [place_of(y, c, 1 - x, half) for half in (0, 1)]
        held_y = [place_of(1 - y, c, x, half) for half in (0, 1)]
        far = [place_of(1 - y, c, 1 - x, half) for half in (0, 1)]
        self.over_y, self.over_x = passed(6, held_x[0], across_y), passed(7, held_y[1], across_x)
        self.core_x = [passed(8 + half, held_x[half], core) for half in (0, 1)]
        self.core_y = [passed(10 + half, held_y[half], core) for half in (0, 1)]
        self.core_far = [passed(12 + half, far[half], core) for half in (0, 1)]

    def start(self, half):
        for copy in self.mine[half]:
            copy.start()

    def pass_first(self):
        self.mine[0][0].wait_recv()
        self.over_y.start()
        self.core_x[0].start()
        self.mine[0][1].wait_recv()
        self.core_y[0].start()

    def pass_second(self):
        self.mine[1][1].wait_recv()
        self.over_x.start()
        self.core_y[1].start()
        self.mine[1][0].wait_recv()
        self.core_x[1].start()

    def pass_far(self):
        self.over_y.wait_recv()
        self.core_far[0].start()
        self.over_x.wait_recv()
        self.core_far[1].start()

    def finish(self):
        from_core = [self.mine[0][2], self.mine[1][2]] + self.core_x + self.core_y + self.core_far
        for copy in from_core:
            copy.wait_recv()
        for copy in self.mine[0] + self.mine[1] + [self.over_y, self.over_x] + self.core_x + self.core_y + self.core_far:
            copy.wait_send()


class Trade:
    def __init__(self, sources, dst, held, send, recv, held_recv, pass_send, detour=True):
        y, c, z, x = spot()
        self.detour = detour
        across_y = (1 - y, c, z, x)
        self.moves = z != 2 * c + y
        self.away = (y == c) & (z == 1 + y)
        self.straight = self.moves & jnp.logical_not(self.away) if detour else self.moves
        self.passes = (1 - y == c) & (z == 2 - y)
        partner = partner_of(y, c, z, x)
        comes_by = ((partner[0] == partner[1]) & (partner[2] == 1 + partner[0])).astype(jnp.int32)
        self.sender = (flip(partner[0], comes_by), partner[1], partner[2], x) if detour else partner
        self.across_y = across_y
        target = partner_of(*across_y)
        self.direct, self.keep, self.out, self.onward = [], [], [], []
        for h, source in enumerate(sources):
            self.direct.append(remote(source, dst(h, partner), send.at[h], recv.at[h], partner))
            self.keep.append(pltpu.make_async_copy(source, dst(h, (y, c, z, x)), recv.at[h]))
            self.out.append(remote(source, held.at[h], send.at[h], held_recv.at[h], across_y))
            self.onward.append(remote(held.at[h], dst(h, target), pass_send.at[h], recv.at[h], target))

    def greet(self, barrier, neighbours_greet):
        @pl.when(self.moves)
        def _():
            pl.semaphore_signal(barrier, inc=1, device_id=self.sender, device_id_type=MESH_ID)

        count = self.straight.astype(jnp.int32)
        if not self.detour:
            return count
        count = count + self.passes.astype(jnp.int32)
        if not neighbours_greet:

            @pl.when(self.passes)
            def _():
                pl.semaphore_signal(barrier, inc=1, device_id=self.across_y, device_id_type=MESH_ID)

            count = count + self.away.astype(jnp.int32)
        return count

    def start(self, h):
        @pl.when(self.straight)
        def _():
            self.direct[h].start()

        if self.detour:

            @pl.when(self.away)
            def _():
                self.out[h].start()

        @pl.when(jnp.logical_not(self.moves))
        def _():
            self.keep[h].start()

    def wait_sent(self, h):
        @pl.when(self.straight)
        def _():
            self.direct[h].wait_send()

        if self.detour:

            @pl.when(self.away)
            def _():
                self.out[h].wait_send()

    def forward(self, h):
        if self.detour:

            @pl.when(self.passes)
            def _():
                self.out[h].wait_recv()
                self.onward[h].start()

    def arrive(self, h):
        @pl.when(self.moves)
        def _():
            self.direct[h].wait_recv()

        @pl.when(jnp.logical_not(self.moves))
        def _():
            self.keep[h].wait()

    def finish(self, first=0):
        for h in range(len(self.direct)):
            if h >= first:
                self.wait_sent(h)

            if self.detour:

                @pl.when(self.passes)
                def _():
                    self.onward[h].wait_send()


def trade_scratch(pieces, rows, width):
    return [pltpu.VMEM((pieces, rows, width), LOW)] + [pltpu.SemaphoreType.DMA((pieces,)) for _ in range(4)]


class Chain:
    def __init__(self, own, slab, sems, index):
        self.own, self.slab, self.sems, self.index = own, slab, sems, index
        self.last = lax.axis_size("z") - 1

    def move(self, which, h, source, layer, to):
        y, c, z, x = spot()
        return remote(
            source, self.slab(layer), self.sems[2 * which].at[self.index, h], self.sems[2 * which + 1].at[self.index, h], (y, c, to, x)
        )

    def up(self, h):
        z = lax.axis_index("z")
        return self.move(0, h, self.own if h == 0 else self.slab(z - h), z - h, z + 1)

    def down(self, h):
        z = lax.axis_index("z")
        return self.move(1, h, self.own if h == 0 else self.slab(z + h), z + h, z - 1)

    def start(self):
        z = lax.axis_index("z")

        @pl.when(z < self.last)
        def _():
            self.up(0).start()

        @pl.when(z > 0)
        def _():
            self.down(0).start()

    def arrive(self, h):
        z = lax.axis_index("z")

        @pl.when(z - h - 1 >= 0)
        def _():
            self.move(0, h, self.slab(z - h - 1), z - h - 1, z).wait_recv()
            if h < 2:

                @pl.when(z < self.last)
                def _():
                    self.up(h + 1).start()

        @pl.when(z + h + 1 <= self.last)
        def _():
            self.move(1, h, self.slab(z + h + 1), z + h + 1, z).wait_recv()
            if h < 2:

                @pl.when(z > 0)
                def _():
                    self.down(h + 1).start()

    def finish(self):
        z = lax.axis_index("z")
        for h in range(3):

            @pl.when((z < self.last) & (z - h >= 0))
            def _():
                self.up(h).wait_send()

            @pl.when((z > 0) & (z + h <= self.last))
            def _():
                self.down(h).wait_send()


def chain_sems(count):
    return [pltpu.SemaphoreType.DMA((count, 3)) for _ in range(4)]


def greet_neighbours(peers):
    y, c, z, x = spot()
    last = lax.axis_size("z") - 1
    barrier = pltpu.get_barrier_semaphore()
    for peer in peers:
        pl.semaphore_signal(barrier, inc=1, device_id=peer, device_id_type=MESH_ID)

    @pl.when(z > 0)
    def _():
        pl.semaphore_signal(barrier, inc=1, device_id=(y, c, z - 1, x), device_id_type=MESH_ID)

    @pl.when(z < last)
    def _():
        pl.semaphore_signal(barrier, inc=1, device_id=(y, c, z + 1, x), device_id_type=MESH_ID)

    return barrier, len(peers) + (z > 0).astype(jnp.int32) + (z < last).astype(jnp.int32)


def others():
    y, c, z, x = spot()
    return [(flip(y, dy), flip(c, dc), z, flip(x, dx)) for dy in (0, 1) for dc in (0, 1) for dx in (0, 1) if dy + dc + dx]


def line_of():
    y, c, z, x = spot()
    return [(y, c, lax.rem(z + dz, 4), x) for dz in (1, 2, 3)]


class Fold:
    def __init__(self, whole, far, near_part, cross, mine, theirs, send, recv, local):
        y, c, z, x = spot()
        a, b = z // 2, lax.rem(z, 2)
        size = whole.shape[1] // 4

        def slab(at):
            return whole.at[:, pl.ds(pl.multiple_of(at * size, size), size)]

        pair, middle = (y, c, 2 * a + 1 - b, x), (y, c, 2 * (1 - a) + b, x)
        self.far = remote(slab(2 * (1 - a) + 1 - b), far, send.at[0], recv.at[0], pair)
        self.near = remote(slab(2 * a + 1 - b), near_part, send.at[1], recv.at[1], pair)
        self.cross = remote(mine, cross, send.at[2], recv.at[2], middle)
        self.fetches = [
            pltpu.make_async_copy(slab(2 * (1 - a) + b), mine, local.at[0]),
            pltpu.make_async_copy(far, theirs, local.at[1]),
        ]
        self.mine, self.theirs = mine, theirs

    def start(self):
        self.far.start()
        self.fetches[0].start()

    def fold(self):
        self.far.wait_recv()
        self.fetches[1].start()
        for copy in self.fetches:
            copy.wait()
        add_rows(self.mine, 0, self.theirs, 0, self.mine.shape[0])
        self.cross.start()
        self.near.start()

    def finish(self):
        for copy in (self.near, self.cross):
            copy.wait_recv()
        for copy in (self.far, self.near, self.cross):
            copy.wait_send()


def fold_peers():
    y, c, z, x = spot()
    a, b = z // 2, lax.rem(z, 2)
    return ((y, c, 2 * a + 1 - b, x), (y, c, 2 * (1 - a) + b, x))


def add_rows(total, first, term, start, count):
    def step(i, carry):
        here = pl.ds(pl.multiple_of(first + i * CHUNK, CHUNK), CHUNK)
        there = pl.ds(pl.multiple_of(start + i * CHUNK, CHUNK), CHUNK)
        total[here, :] = (total[here, :].astype(jnp.float32) + term[there, :].astype(jnp.float32)).astype(LOW)
        return carry

    lax.fori_loop(0, count // CHUNK, step, 0)


def scatter_scratch(width, parts=1):
    return [
        pltpu.VMEM((2, TILE, width), LOW),
        pltpu.VMEM((4, TILE, width), LOW),
        pltpu.VMEM((4, TILE, width), LOW),
        pltpu.VMEM((2, HALF, width), LOW),
        pltpu.VMEM((2, TILE, width), LOW),
        pltpu.SemaphoreType.DMA((parts, 10)),
        pltpu.SemaphoreType.DMA((parts, 10)),
    ]


class Scatter:
    def __init__(self, produce, staged, core_part, total, relayed, landed, send, recv, part=0, start=0, size=TILE):
        across_x, across_y, core = near()
        self.produce, self.staged, self.core_part, self.total, self.relayed = produce, staged, core_part, total, relayed
        self.start, self.size, self.half = start, size, size // 2
        send, recv = send.at[part], recv.at[part]
        rows = pl.ds(start, size)
        halves = (pl.ds(start, self.half), pl.ds(start + self.half, self.half))
        self.relay_row = start // 2
        passing = pl.ds(self.relay_row, self.half)
        self.to_core = [
            remote(staged.at[k % 2, rows], core_part.at[k, rows], send.at[k], recv.at[k], core) for k in range(4)
        ]
        self.far_x = remote(total.at[0, halves[0]], relayed.at[0, passing], send.at[4], recv.at[4], across_x)
        self.far_y = remote(total.at[0, halves[1]], relayed.at[1, passing], send.at[5], recv.at[5], across_y)
        self.to_x = [
            remote(total.at[1, at], landed.at[0, at], send.at[6 + half], recv.at[6 + half], across_x)
            for half, at in enumerate(halves)
        ]
        self.to_y = [
            remote(total.at[2, at], landed.at[1, at], send.at[8 + half], recv.at[8 + half], across_y)
            for half, at in enumerate(halves)
        ]

    def begin(self):
        y, c, z, x = spot()
        rows = pl.ds(self.start, self.size)
        for k, (to_row, to_column) in enumerate(((1 - y, 1 - x), (y, 1 - x), (1 - y, x), (y, x))):
            if k >= 2:
                self.to_core[k - 2].wait_send()
            self.produce(2 * k, to_row, 1 - c, to_column, self.staged.at[k % 2, rows])
            self.to_core[k].start()
            self.produce(2 * k + 1, to_row, c, to_column, self.total.at[k, rows])
            self.to_core[k].wait_recv()
            add_rows(self.total.at[k], self.start, self.core_part.at[k], self.start, self.size)
            if k == 0:
                self.far_x.start()
                self.far_y.start()
            if k == 1:
                self.to_x[0].start()
            if k == 2:
                self.to_y[1].start()

    def relay(self):
        self.far_y.wait_recv()
        add_rows(self.total.at[1], self.start + self.half, self.relayed.at[1], self.relay_row, self.half)
        self.to_x[1].start()
        self.far_x.wait_recv()
        add_rows(self.total.at[2], self.start, self.relayed.at[0], self.relay_row, self.half)
        self.to_y[0].start()

    def arrive(self):
        for copy in self.to_x + self.to_y:
            copy.wait_recv()

    def finish(self):
        for copy in self.to_core[2:] + [self.far_x, self.far_y] + self.to_x + self.to_y:
            copy.wait_send()


def sum_and_gather(part_of, rows_of_half, gather, beside):
    sums = [part_of(half) for half in (0, 1)]
    sums[0].begin()
    sums[0].relay()
    sums[1].begin()
    sums[0].arrive()
    rows_of_half(0)
    gather.start(0)
    beside(0)
    sums[1].relay()
    beside(1)
    sums[1].arrive()
    rows_of_half(1)
    gather.start(1)
    gather.pass_near(0)
    beside(2)
    gather.pass_near(1)
    gather.pass_far(0)
    gather.pass_far(1)
    gather.finish()
    beside(3)
    for half in (0, 1):
        sums[half].finish()


def begin_kernel(
    x_own, w_query, w_key, w_value, facts, x_whole, w_qkv, facts_whole,
    gather_send, gather_recv, w_send, w_recv, fact_send, fact_recv, local, *scratch
):
    y, c, z, x = spot()
    row = 2 * y + c
    layer = others()
    trade_parts, sems = scratch[:5], scratch[5:]
    trade = Trade(
        [x_own.at[half] for half in (0, 1)], lambda half, at: x_whole.at[place_of(at[0], at[1], at[3], half)], *trade_parts, detour=False
    )
    barrier, count = greet_neighbours(layer)
    pl.semaphore_wait(barrier, count + trade.greet(barrier, True))

    shard, width = w_query.shape
    owned = width // 8
    for half in (0, 1):
        trade.start(half)
    spread = [
        remote(facts, facts_whole.at[row, z, x], fact_send.at[k], fact_recv.at[k], peer) for k, peer in enumerate(layer)
    ]
    kept = [pltpu.make_async_copy(facts, facts_whole.at[row, z, x], local.at[3])]
    for m, source in enumerate((w_query, w_key, w_value)):
        dst = w_qkv.at[row, z, pl.ds(pl.multiple_of(x * shard, shard), shard), pl.ds(m * owned, owned)]
        for k, peer in enumerate(layer):
            columns = pl.ds(pl.multiple_of((4 * peer[0] + 2 * peer[1] + peer[3]) * owned, owned), owned)
            spread.append(remote(source.at[:, columns], dst, w_send.at[m, k], w_recv.at[m, k], peer))
        columns = pl.ds(pl.multiple_of((4 * y + 2 * c + x) * owned, owned), owned)
        kept.append(pltpu.make_async_copy(source.at[:, columns], dst, local.at[m]))
    for copy in spread + kept:
        copy.start()

    gather = GatherWhole(lambda half: x_whole.at[place_of(y, c, x, half)], x_whole, gather_send, gather_recv)
    for half in (0, 1):
        trade.forward(half)
        trade.arrive(half)
        gather.start(half)

    for copy in kept:
        copy.wait()
    for copy in spread:
        copy.wait_recv()
    chains = [
        Chain(facts_whole.at[:, z], lambda at: facts_whole.at[:, at], sems, 0),
        Chain(w_qkv.at[:, z], lambda at: w_qkv.at[:, at], sems, 1),
    ]

    def arrive(h):
        for chain in chains:
            chain.arrive(h)

    for chain in chains:
        chain.start()
    gather.pass_first()
    arrive(0)
    gather.pass_second()
    arrive(1)
    gather.pass_far()
    arrive(2)
    gather.finish()
    trade.finish()
    for copy in spread:
        copy.wait_send()
    for chain in chains:
        chain.finish()


def anywhere():
    return pl.BlockSpec(memory_space=pl.ANY)


def in_vmem():
    return pl.BlockSpec(memory_space=pltpu.VMEM)


def dma(*shape):
    return pltpu.SemaphoreType.DMA(shape)


def remote_params(number):
    return pltpu.CompilerParams(collective_id=number, has_side_effects=True, vmem_limit_bytes=VMEM_LIMIT)


def begin(x_own, w_query, w_key, w_value, facts):
    block, width = x_own.shape
    shard = w_query.shape[0]
    x_whole, w_qkv, facts_whole = pl.pallas_call(
        begin_kernel,
        out_shape=(
            jax.ShapeDtypeStruct((8 * block, width), LOW),
            jax.ShapeDtypeStruct((4, 4, 2 * shard, 3 * width // 8), LOW),
            jax.ShapeDtypeStruct((4, 4, 2, *facts.shape), jnp.float32),
        ),
        in_specs=[in_vmem()] + [anywhere()] * 4,
        out_specs=[anywhere()] * 3,
        scratch_shapes=[
            dma(GATHER_COPIES), dma(GATHER_COPIES), dma(3, 7), dma(3, 7), dma(7), dma(7), dma(4),
            *trade_scratch(2, block // 2, width), *chain_sems(2),
        ],
        compiler_params=remote_params(1),
        cost_estimate=pl.CostEstimate(flops=0, bytes_accessed=350_000_000, transcendentals=0),
    )(x_own.reshape(2, block // 2, width), w_query, w_key, w_value, facts)
    return x_whole, w_qkv.reshape(width, 3 * width // 8), facts_whole


def summed(total, landed, here):
    parts = (total[3, here, :], landed[0, here, :], landed[1, here, :])
    return sum(part.astype(jnp.float32) for part in parts)


def over_chunks(work, half):
    def step(i, carry):
        work(pl.ds(pl.multiple_of(half * HALF + i * CHUNK, CHUNK), CHUNK))
        return carry

    lax.fori_loop(0, HALF // CHUNK, step, 0)


def own_halves(own):
    return lambda half: own.at[pl.ds(half * HALF, HALF)]


def inverse_of(value):
    return lax.rsqrt(jnp.mean(value * value, axis=-1, keepdims=True) + EPSILON)


def close_attention_kernel(attended, w_out, x_own, gain, w_gate, w_up, resid, normed, own_gate, own_up, own, *scratch):
    scatter, (send, recv, local), sems = scratch[:7], scratch[7:10], scratch[10:]
    width = w_out.shape[1]
    hidden = w_gate.shape[1]
    z = lax.axis_index("z")
    barrier, count = greet_neighbours(near())
    pl.semaphore_wait(barrier, count)

    def slab_of(whole):
        return lambda at: whole.at[:, pl.ds(pl.multiple_of(at * hidden, hidden), hidden)]

    chains, kept = [], []
    for k, (part, whole) in enumerate(((w_gate, own_gate), (w_up, own_up))):
        chains.append(Chain(part, slab_of(whole), sems, k))
        chains[k].start()
        kept.append(pltpu.make_async_copy(part, slab_of(whole)(z), local.at[1 + k]))
        kept[k].start()

    def arrive(h):
        for chain in chains:
            chain.arrive(h)

    def part_of(half):
        def produce(turn, y, c, x, out):
            at = place_of(y, c, x, half)

            def step(i, carry):
                columns = pl.ds(pl.multiple_of(i * TILE, TILE), TILE)
                out[:, columns] = dot_wide(attended[at, :], w_out[:, columns]).astype(LOW)
                return carry

            lax.fori_loop(0, width // TILE, step, 0)

        return Scatter(produce, *scatter, part=half, start=half * HALF, size=HALF)

    total, landed = scatter[2], scatter[4]

    def chunk(here):
        value = x_own[here, :].astype(jnp.float32) + summed(total, landed, here)
        resid[here, :] = value
        own[here, :] = (value * inverse_of(value) * gain[...]).astype(LOW)

    def rows_of_half(half):
        over_chunks(chunk, half)

    y, c, z, x = spot()
    gather = Gather(own_halves(own), normed, send, recv)
    sum_and_gather(part_of, rows_of_half, gather, lambda turn: arrive(turn - 1) if turn > 0 else None)
    keep = pltpu.make_async_copy(own, normed.at[place_of(y, c, x)], local.at[0])
    keep.start()
    for chain in chains:
        chain.finish()
    for copy in kept + [keep]:
        copy.wait()


def close_attention(attended, w_out, x_own, gain, w_gate, w_up):
    block, width = x_own.shape
    hidden = w_gate.shape[1]
    return pl.pallas_call(
        close_attention_kernel,
        out_shape=(
            jax.ShapeDtypeStruct((block, width), jnp.float32),
            jax.ShapeDtypeStruct((8 * block, width), LOW),
            jax.ShapeDtypeStruct((width, 4 * hidden), LOW),
            jax.ShapeDtypeStruct((width, 4 * hidden), LOW),
        ),
        in_specs=[in_vmem()] * 6,
        out_specs=[in_vmem()] + [anywhere()] * 3,
        scratch_shapes=[pltpu.VMEM((block, width), LOW)]
        + scatter_scratch(width, 2)
        + [dma(GATHER_COPIES), dma(GATHER_COPIES), dma(3), *chain_sems(2)],
        compiler_params=remote_params(2),
        cost_estimate=pl.CostEstimate(flops=0, bytes_accessed=450_000_000, transcendentals=0),
    )(attended, w_out, x_own, gain, w_gate, w_up)


def norm_back(value, gain, upstream):
    inverse = inverse_of(value)
    scaled = upstream * gain
    inner = jnp.mean(scaled * value, axis=-1, keepdims=True)
    return inverse * scaled - value * (inverse * inverse * inverse) * inner, upstream * value * inverse


def fold_rows(total, terms):
    for first in range(0, CHUNK, 8):
        total[...] += terms[first : first + 8, :]


def close_mlp_kernel(
    d_gate, d_up, w_gate, w_up, resid, upstream, gain, grad_a, grad_b, d_resid, gain_term, d_resid_whole,
    far_a, near_a, cross_a, far_b, near_b, cross_b, own, blocks, *scratch
):
    scatter, (send, recv, local, fetched, fold_send, fold_recv, fold_local, mine, theirs) = scratch[:7], scratch[7:]
    y, c, z, x = spot()
    width = w_gate.shape[0]
    order = [
        place_of(r, k, q, half)
        for half in (0, 1)
        for r, q in ((1 - y, 1 - x), (y, 1 - x), (1 - y, x), (y, x))
        for k in (1 - c, c)
    ]

    def fetch(turn):
        slot = turn % 2
        return [
            pltpu.make_async_copy(source.at[order[turn]], blocks.at[slot, m], fetched.at[slot, m])
            for m, source in enumerate((d_gate, d_up))
        ]

    for copy in fetch(0):
        copy.start()
    greet(near() + fold_peers())
    folds = [
        Fold(*refs, mine.at[k], theirs, fold_send.at[k], fold_recv.at[k], fold_local.at[k])
        for k, refs in enumerate(((grad_a, far_a, near_a, cross_a), (grad_b, far_b, near_b, cross_b)))
    ]
    for fold in folds:
        fold.start()

    def part_of(half):
        def produce(turn, to_y, to_c, to_x, out):
            turn = turn + 8 * half
            if turn < 15:
                for copy in fetch(turn + 1):
                    copy.start()
            for copy in fetch(turn):
                copy.wait()

            def step(i, carry):
                columns = pl.ds(pl.multiple_of(i * TILE, TILE), TILE)
                part = dot_nt(blocks[turn % 2, 0], w_gate[columns, :]) + dot_nt(blocks[turn % 2, 1], w_up[columns, :])
                out[:, columns] = part.astype(LOW)
                return carry

            lax.fori_loop(0, width // TILE, step, 0)

        return Scatter(produce, *scatter, part=half, start=half * HALF, size=HALF)

    total, landed = scatter[2], scatter[4]
    gain_term[...] = jnp.zeros_like(gain_term)

    def chunk(here):
        back, terms = norm_back(resid[here, :], gain[...], summed(total, landed, here))
        value = upstream[here, :].astype(jnp.float32) + back
        d_resid[here, :] = value
        own[here, :] = value.astype(LOW)
        fold_rows(gain_term, terms)

    def rows_of_half(half):
        over_chunks(chunk, half)

    gather = Gather(own_halves(own), d_resid_whole, send, recv)
    sum_and_gather(part_of, rows_of_half, gather, lambda turn: folds[turn].fold() if turn < 2 else None)
    keep = pltpu.make_async_copy(own, d_resid_whole.at[place_of(y, c, x)], local.at[0])
    keep.start()
    for fold in folds:
        fold.finish()
    keep.wait()


def close_mlp(d_gate, d_up, w_gate, w_up, resid, upstream, gain, *grads):
    block, width = resid.shape
    hidden = d_gate.shape[1]
    return pl.pallas_call(
        close_mlp_kernel,
        out_shape=(
            jax.ShapeDtypeStruct((block, width), jnp.float32),
            jax.ShapeDtypeStruct((8, width), jnp.float32),
            jax.ShapeDtypeStruct((8 * block, width), LOW),
            *[jax.ShapeDtypeStruct((width, hidden // 4), LOW)] * 6,
        ),
        in_specs=[anywhere()] * 2 + [in_vmem()] * 5 + [anywhere()] * 2,
        out_specs=[in_vmem(), in_vmem()] + [anywhere()] * 7,
        scratch_shapes=[pltpu.VMEM((block, width), LOW), pltpu.VMEM((2, 2, block // 2, hidden), LOW)]
        + scatter_scratch(width, 2)
        + [dma(GATHER_COPIES), dma(GATHER_COPIES), dma(1), dma(2, 2), dma(2, 3), dma(2, 3), dma(2, 2)]
        + [pltpu.VMEM((2, width, hidden // 4), LOW), pltpu.VMEM((width, hidden // 4), LOW)],
        compiler_params=remote_params(3),
        cost_estimate=pl.CostEstimate(flops=0, bytes_accessed=450_000_000, transcendentals=0),
    )(d_gate, d_up, w_gate, w_up, resid, upstream, gain, *grads)


def close_layer_kernel(d_qkv, w_qkv, x_own, d_resid, gain, mlp_term, grad_low, gain_grads, own, terms, layer_terms, part, column_terms, *scratch):
    scatter, (send, recv, term_send, term_recv, line_send, line_recv) = scratch[:7], scratch[7:]
    y, c, z, x = spot()
    partner = partner_of(y, c, z, x)
    moves = z != 2 * c + y
    width = w_qkv.shape[0]
    barrier = pltpu.get_barrier_semaphore()

    @pl.when(moves)
    def _():
        pl.semaphore_signal(barrier, inc=1, device_id=partner, device_id_type=MESH_ID)

    layer = others()
    line = line_of()
    for peer in layer + line:
        pl.semaphore_signal(barrier, inc=1, device_id=peer, device_id_type=MESH_ID)
    pl.semaphore_wait(barrier, len(layer + line) + moves.astype(jnp.int32))

    def part_of(half):
        def produce(turn, to_y, to_c, to_x, out):
            at = place_of(to_y, to_c, to_x, half)

            def step(i, carry):
                columns = pl.ds(pl.multiple_of(i * TILE, TILE), TILE)
                out[:, columns] = dot_nt(d_qkv[at, :], w_qkv[columns, :]).astype(LOW)
                return carry

            lax.fori_loop(0, width // TILE, step, 0)

        return Scatter(produce, *scatter, part=half, start=half * HALF, size=HALF)

    sums = [part_of(half) for half in (0, 1)]
    sums[0].begin()
    sums[0].relay()
    sums[1].begin()
    total, landed = scatter[2], scatter[4]
    terms[1] = mlp_term[...]
    terms[0] = jnp.zeros_like(mlp_term)
    trades = [
        remote(own.at[pl.ds(half * HALF, HALF)], grad_low.at[pl.ds(half * HALF, HALF)], send.at[half], recv.at[half], partner)
        for half in (0, 1)
    ]
    keeps = [
        pltpu.make_async_copy(own.at[pl.ds(half * HALF, HALF)], grad_low.at[pl.ds(half * HALF, HALF)], recv.at[half])
        for half in (0, 1)
    ]
    for half in (0, 1):
        if half == 1:
            sums[1].relay()
        sums[half].arrive()

        def step(i, carry):
            here = pl.ds(pl.multiple_of(half * HALF + i * CHUNK, CHUNK), CHUNK)
            back, products = norm_back(x_own[here, :].astype(jnp.float32), gain[...], summed(total, landed, here))
            own[here, :] = (d_resid[here, :] + back).astype(LOW)
            fold_rows(terms.at[0], products)
            return carry

        lax.fori_loop(0, HALF // CHUNK, step, 0)

        @pl.when(moves)
        def _():
            trades[half].start()

        @pl.when(jnp.logical_not(moves))
        def _():
            keeps[half].start()

    def columns_of(row, layers):
        return pl.ds(pl.multiple_of((4 * row) * HD, HD), layers * HD)

    spread = [
        remote(terms.at[:, :, columns_of(2 * peer[0] + peer[1], 4)], layer_terms.at[k], term_send.at[k], term_recv.at[k], peer)
        for k, peer in enumerate(layer)
    ]
    for copy in spread:
        copy.start()
    for copy in spread:
        copy.wait_recv()
    part[...] = sum((layer_terms[k] for k in range(7)), terms[:, :, columns_of(2 * y + c, 4)])
    lines = [
        remote(
            part.at[:, :, pl.ds(pl.multiple_of(peer[2] * HD, HD), HD)], column_terms.at[k], line_send.at[k], line_recv.at[k], peer
        )
        for k, peer in enumerate(line)
    ]
    for copy in lines:
        copy.start()
    for copy in lines:
        copy.wait_recv()
    gain_grads[...] = sum((column_terms[k] for k in range(3)), part[:, :, pl.ds(pl.multiple_of(z * HD, HD), HD)])
    for copy in spread + lines:
        copy.wait_send()
    for half in (0, 1):
        sums[half].finish()

    @pl.when(moves)
    def _():
        for copy in trades:
            copy.wait()

    @pl.when(jnp.logical_not(moves))
    def _():
        for copy in keeps:
            copy.wait()


def close_layer(d_qkv, w_qkv, x_own, d_resid, gain, mlp_term):
    block, width = x_own.shape
    return pl.pallas_call(
        close_layer_kernel,
        out_shape=(jax.ShapeDtypeStruct((block, width), LOW), jax.ShapeDtypeStruct((2, 8, width // 16), jnp.float32)),
        in_specs=[in_vmem()] * 6,
        out_specs=[anywhere(), in_vmem()],
        scratch_shapes=[
            pltpu.VMEM((block, width), LOW),
            pltpu.VMEM((2, 8, width), jnp.float32),
            pltpu.VMEM((7, 2, 8, width // 4), jnp.float32),
            pltpu.VMEM((2, 8, width // 4), jnp.float32),
            pltpu.VMEM((3, 2, 8, width // 16), jnp.float32),
        ]
        + scatter_scratch(width, 2)
        + [dma(2), dma(2), dma(7), dma(7), dma(3), dma(3)],
        compiler_params=remote_params(4),
        cost_estimate=pl.CostEstimate(flops=0, bytes_accessed=350_000_000, transcendentals=0),
    )(d_qkv, w_qkv, x_own, d_resid, gain, mlp_term)


def doc_start(ends, place):
    start = jnp.zeros_like(place)
    for k in range(8):
        start = jnp.where(ends[k] <= place, ends[k], start)
    return jnp.where(place < ends[7], start, LEN)


def sigmoid_of(raw):
    return pl.reciprocal(1.0 + jnp.exp2(math.log2(LEN) - raw * (math.log2(math.e) / math.sqrt(HD))), approx=True)


def tile_at(index):
    return pl.ds(pl.multiple_of(index * TILE, TILE), TILE)


def head_of(array, rows, part, head):
    first = (part * (array.shape[1] // 3) // HD + head) * HD
    return array[rows, first : first + HD]


def attend_kernel(ends, qkv, out, total):
    i = pl.program_id(0)
    heads = qkv.shape[1] // (3 * HD)
    total[...] = jnp.zeros_like(total)
    q_place = i * TILE + lax.broadcasted_iota(jnp.int32, (TILE, 1), 0)
    q_start = doc_start(ends, q_place)

    def tile(j, diagonal):
        k_place = j * TILE + lax.broadcasted_iota(jnp.int32, (1, TILE), 1)
        allowed = k_place >= q_start
        if diagonal:
            allowed = allowed & (k_place <= q_place)
        for head in range(heads):
            raw = dot_nt(head_of(qkv, tile_at(i), 0, head), head_of(qkv, tile_at(j), 1, head))
            weight = jnp.where(allowed, sigmoid_of(raw), 0.0).astype(LOW)
            total[head] += dot_wide(weight, head_of(qkv, tile_at(j), 2, head))

    def step(j, carry):
        tile(j, False)
        return carry

    lax.fori_loop(0, i, step, 0)
    tile(i, True)
    for head in range(heads):
        out[tile_at(i), head * HD : (head + 1) * HD] = total[head].astype(LOW)


def open_mlp_kernel(normed, w_gate, w_up, upstream, gate, up, hidden, upstream_whole, send, recv, local):
    i = pl.program_id(0)
    y, c, z, x = spot()
    steps = pl.num_programs(0)
    gather = Gather(lambda half: upstream.at[pl.ds(half * HALF, HALF)], upstream_whole, send, recv)
    keep = pltpu.make_async_copy(upstream, upstream_whole.at[place_of(y, c, x)], local.at[0])

    @pl.when(i == 0)
    def _():
        greet(near())
        gather.start(0)
        gather.start(1)
        keep.start()

    def step(n, carry):
        columns = pl.ds(pl.multiple_of(n * HALF, HALF), HALF)
        gate_part, up_part = dot_wide(normed[...], w_gate[:, columns]), dot_wide(normed[...], w_up[:, columns])
        gate[:, columns] = gate_part
        up[:, columns] = up_part
        hidden[:, columns] = (gate_part * jax.nn.sigmoid(gate_part) * up_part).astype(LOW)
        return carry

    lax.fori_loop(0, w_gate.shape[1] // HALF, step, 0)

    @pl.when(i == steps - 1)
    def _():
        for half in (0, 1):
            gather.pass_near(half)
        for half in (0, 1):
            gather.pass_far(half)
        gather.finish()
        keep.wait()


def open_mlp(normed, w_gate, w_up, upstream):
    places, width = normed.shape
    hidden = w_gate.shape[1]
    rows = lambda columns: pl.BlockSpec((TILE, columns), lambda i: (i, 0))
    whole = lambda array: pl.BlockSpec(array.shape, lambda i: (0, 0))
    return pl.pallas_call(
        open_mlp_kernel,
        out_shape=(
            jax.ShapeDtypeStruct((places, hidden), jnp.float32),
            jax.ShapeDtypeStruct((places, hidden), jnp.float32),
            jax.ShapeDtypeStruct((places, hidden), LOW),
            jax.ShapeDtypeStruct((places, width), LOW),
        ),
        grid=(places // TILE,),
        in_specs=[rows(width), whole(w_gate), whole(w_up), whole(upstream)],
        out_specs=[rows(hidden), rows(hidden), rows(hidden), anywhere()],
        scratch_shapes=[dma(GATHER_COPIES), dma(GATHER_COPIES), dma(1)],
        compiler_params=remote_params(5),
        cost_estimate=pl.CostEstimate(flops=0, bytes_accessed=250_000_000, transcendentals=0),
    )(normed, w_gate, w_up, upstream)


def out_turns():
    y, c, z, x = spot()
    owners = [((y, c, 2 * x + j // 2, j % 2), (z == 2 * x + j // 2) & (x == j % 2)) for j in range(4)]
    holders = [((y, c, j, z // 2), (z == j) & (x == z // 2)) for j in range(4)]
    return owners, holders


def attend_back_kernel(
    ends, qkv, grads, out_grad, mixed, out, out_parts, mixed_home, query_total, key_total, value_total, send, recv, *trade_parts
):
    j = pl.program_id(0)
    y, c, z, x = spot()
    heads = qkv.shape[1] // (3 * HD)
    shard = out_grad.shape[0] // 4
    owners, holders = out_turns()
    trade = Trade(
        [mixed.at[pl.ds(half * HALF, HALF)] for half in (0, 1)], lambda half, at: mixed_home.at[pl.ds(half * HALF, HALF)], *trade_parts
    )

    def to_owner(turn):
        return remote(out_grad.at[pl.ds(turn * shard, shard)], out_parts.at[z], send.at[turn], recv.at[z], owners[turn][0])

    def to_self(turn):
        return pltpu.make_async_copy(out_grad.at[pl.ds(turn * shard, shard)], out_parts.at[z], recv.at[z])

    @pl.when(j == 0)
    def _():
        query_total[...] = jnp.zeros_like(query_total)
        barrier = pltpu.get_barrier_semaphore()
        for peer, here in holders:

            @pl.when(jnp.logical_not(here))
            def _():
                pl.semaphore_signal(barrier, inc=1, device_id=peer, device_id_type=MESH_ID)

        pl.semaphore_wait(barrier, 4 - (x == z // 2).astype(jnp.int32) + trade.greet(barrier, False))
        for half in (0, 1):
            trade.start(half)
        for turn in range(4):

            @pl.when(jnp.logical_not(owners[turn][1]))
            def _():
                to_owner(turn).start()

            @pl.when(owners[turn][1])
            def _():
                to_self(turn).start()

    key_total[...] = jnp.zeros_like(key_total)
    value_total[...] = jnp.zeros_like(value_total)
    here = tile_at(j)
    k_place = j * TILE + lax.broadcasted_iota(jnp.int32, (TILE, 1), 0)
    turned = [head_of(qkv, here, 1, head).T for head in range(heads)]

    def tile(i, diagonal):
        q_place = i * TILE + lax.broadcasted_iota(jnp.int32, (1, TILE), 1)
        allowed = k_place >= doc_start(ends, q_place)
        if diagonal:
            allowed = allowed & (k_place <= q_place)
        for head in range(heads):
            query, grad = head_of(qkv, tile_at(i), 0, head), grads[tile_at(i), head * HD : (head + 1) * HD]
            sig = jnp.where(allowed, sigmoid_of(dot_nt(head_of(qkv, here, 1, head), query)), 0.0)
            value_total[head] += dot_wide(sig.astype(LOW), grad)
            d_score = (dot_nt(head_of(qkv, here, 2, head), grad) * (sig * (1.0 - sig))).astype(LOW)
            key_total[head] += dot_wide(d_score, query)
            query_total[head, :, tile_at(i)] += dot_wide(turned[head], d_score)

    def step(i, carry):
        tile(i, False)
        return carry

    tile(j, True)
    lax.fori_loop(j + 1, LEN // TILE, step, 0)
    scale = 1.0 / math.sqrt(HD)
    for head in range(heads):
        first = head * HD
        out[here, heads * HD + first : (heads + 1) * HD + first] = (key_total[head] * scale).astype(LOW)
        out[here, 2 * heads * HD + first : (2 * heads + 1) * HD + first] = value_total[head].astype(LOW)
        out[here, first : first + HD] = (query_total[head, :, here] * scale).T.astype(LOW)

    @pl.when(j == LEN // TILE - 1)
    def _():
        for turn in range(4):

            @pl.when(jnp.logical_not(owners[turn][1]))
            def _():
                to_owner(turn).wait_send()

            @pl.when(jnp.logical_not(holders[turn][1]))
            def _():
                landed = out_parts.at[turn]
                remote(landed, landed, send.at[turn], recv.at[turn], holders[turn][0]).wait_recv()

            @pl.when(owners[turn][1])
            def _():
                to_self(turn).wait()

        for half in (0, 1):
            trade.arrive(half)
        trade.finish()

    @pl.when(j == 1)
    def _():
        for half in (0, 1):
            trade.forward(half)


def back_mlp_kernel(upstream, w_down, gate, up, d_gate, d_up):
    def step(n, carry):
        columns = pl.ds(pl.multiple_of(n * HALF, HALF), HALF)
        d_hidden = dot_nt(upstream[...], w_down[columns, :])
        d_gate[:, columns], d_up[:, columns] = gate_backward(
            d_hidden, gate[:, columns], up[:, columns], jax.nn.sigmoid(gate[:, columns])
        )
        return carry

    lax.fori_loop(0, gate.shape[1] // HALF, step, 0)


def back_mlp(upstream, w_down, gate, up):
    places, width = upstream.shape
    hidden = gate.shape[1]
    rows = lambda size: pl.BlockSpec((TILE, size), lambda i: (i, 0))
    return pl.pallas_call(
        back_mlp_kernel,
        out_shape=(jax.ShapeDtypeStruct((places, hidden), LOW), jax.ShapeDtypeStruct((places, hidden), LOW)),
        grid=(places // TILE,),
        in_specs=[rows(width), pl.BlockSpec(w_down.shape, lambda i: (0, 0)), rows(hidden), rows(hidden)],
        out_specs=[rows(hidden), rows(hidden)],
        compiler_params=pltpu.CompilerParams(vmem_limit_bytes=VMEM_LIMIT),
        cost_estimate=pl.CostEstimate(flops=0, bytes_accessed=90_000_000, transcendentals=0),
    )(upstream, w_down, gate, up)


def attend(ends, qkv):
    places, width = qkv.shape
    heads = width // (3 * HD)
    whole = lambda columns: pl.BlockSpec((places, columns), lambda i: (0, 0))
    return pl.pallas_call(
        attend_kernel,
        out_shape=jax.ShapeDtypeStruct((places, width // 3), LOW),
        grid=(places // TILE,),
        in_specs=[pl.BlockSpec(memory_space=pltpu.SMEM), whole(width)],
        out_specs=whole(width // 3),
        scratch_shapes=[pltpu.VMEM((heads, TILE, HD), jnp.float32)],
        compiler_params=pltpu.CompilerParams(vmem_limit_bytes=VMEM_LIMIT),
        cost_estimate=pl.CostEstimate(flops=0, bytes_accessed=150_000_000, transcendentals=0),
    )(ends, qkv)


def attend_back(ends, qkv, grads, out_grad, mixed):
    places, width = qkv.shape
    heads = width // (3 * HD)
    whole = lambda columns: pl.BlockSpec((places, columns), lambda j: (0, 0))
    return pl.pallas_call(
        attend_back_kernel,
        out_shape=(
            jax.ShapeDtypeStruct((places, width), LOW),
            jax.ShapeDtypeStruct((4, out_grad.shape[0] // 4, out_grad.shape[1]), LOW),
            jax.ShapeDtypeStruct(mixed.shape, LOW),
        ),
        grid=(places // TILE,),
        in_specs=[pl.BlockSpec(memory_space=pltpu.SMEM), whole(width), whole(width // 3), anywhere(), pl.BlockSpec(mixed.shape, lambda j: (0, 0))],
        out_specs=[whole(width), anywhere(), anywhere()],
        scratch_shapes=[
            pltpu.VMEM((heads, HD, places), jnp.float32),
            pltpu.VMEM((heads, TILE, HD), jnp.float32),
            pltpu.VMEM((heads, TILE, HD), jnp.float32),
            dma(4),
            dma(4),
            *trade_scratch(2, HALF, mixed.shape[1]),
        ],
        compiler_params=remote_params(6),
        cost_estimate=pl.CostEstimate(flops=0, bytes_accessed=300_000_000, transcendentals=0),
    )(ends, qkv, grads, out_grad, mixed)


LAYER = ("y", "c", "x")
PLACES = ("c", "y", "x")
ALL = ("y", "c", "z", "x")


def trade(part):
    pairs = []
    for y in range(2):
        for c in range(2):
            for z in range(4):
                for x in range(2):
                    pairs.append((((y * 2 + c) * 4 + z) * 2 + x, (((z % 2) * 2 + z // 2) * 4 + 2 * c + y) * 2 + x))
    return lax.ppermute(part, ALL, pairs)


def after(first, then):
    return lax.optimization_barrier((first, then))[1]


def body_layers(
    tokens, lengths, cotangent, w_query, w_key, w_value, w_out, w_gate, w_up, w_down, gain_attn, gain_mlp
):
    rows_here, block, width = tokens.shape
    members = lax.axis_size(LAYER)
    layers = lax.axis_size("z")
    shard = w_query.shape[0]
    owned = width // members
    facts = jnp.zeros((8, 2 * shard), jnp.float32)
    facts = facts.at[0, :shard].set(gain_attn.astype(jnp.float32)).at[1, :shard].set(gain_mlp.astype(jnp.float32))
    facts = facts.at[2, : lengths.shape[1]].set(lengths[0].astype(jnp.float32))
    layer_x, w_qkv, facts = begin(tokens.reshape(block, width), w_query, w_key, w_value, facts)
    full_gain_attn, full_gain_mlp = facts[:, :, :, 0, :shard].reshape(1, width), facts[:, :, :, 1, :shard].reshape(1, width)
    layer = lax.axis_index("z")
    own_lengths = facts[:, 0, 0, 2, : lengths.shape[1]].reshape(2, 2, -1)
    own_lengths = lax.dynamic_slice(own_lengths, (layer % 2, layer // 2, 0), (1, 1, own_lengths.shape[2]))[0, 0]
    ends = jnp.cumsum(own_lengths.astype(jnp.int32))
    place = (4 * lax.axis_index("c") + 2 * lax.axis_index("y") + lax.axis_index("x")) * block
    x_own = lax.dynamic_slice_in_dim(layer_x, place, block, 0)
    layer_normed = norm_forward(layer_x.astype(jnp.float32), full_gain_attn)[0].astype(LOW)
    out_rows = lax.all_gather(after(facts, w_out), ("z", "x"), axis=0, tiled=True)
    w_out_own = lax.dynamic_slice_in_dim(out_rows, lax.axis_index("x") * owned, owned, 0)

    upstream = trade(after(facts, cotangent)).reshape(block, width)
    qkv = dot_wide(layer_normed, w_qkv).astype(LOW)
    attended = attend(ends, qkv)
    resid, layer_mlp, own_gate, own_up = close_attention(after(upstream, attended), w_out_own, x_own, full_gain_mlp, w_gate, w_up)

    own_down = lax.all_gather(after(resid, w_down), "z", axis=0, tiled=True)
    gate, up_part, hidden, layer_upstream = open_mlp(layer_mlp, own_gate, own_up, upstream)
    part = dot_wide(hidden, own_down).astype(LOW)
    mixed_sum = lax.psum_scatter(part, PLACES, scatter_dimension=0, tiled=True)
    down_term = contract_rows(after(part, hidden), layer_upstream).astype(LOW)
    down_rows = w_down.shape[0]
    down_parts = []
    for up in range(1, 4):
        layers_pairs = [(at, (at + up) % 4) for at in range(4)]
        slab = lax.dynamic_slice_in_dim(down_term, (layer + up) % 4 * down_rows, down_rows, 0)
        down_parts.append(lax.ppermute(slab, "z", layers_pairs))
    d_gate, d_up = back_mlp(after(down_term, layer_upstream), own_down, gate, up_part)
    gate_term, up_term = contract_rows(layer_mlp, d_gate).astype(LOW), contract_rows(layer_mlp, d_up).astype(LOW)
    d_resid, gain_mlp_term, layer_d_resid, *parts = close_mlp(
        after((mixed_sum, *down_parts), d_gate), d_up, own_gate, own_up, resid, upstream, full_gain_mlp, gate_term, up_term
    )

    def own_part(whole, near_part, cross):
        own = lax.dynamic_slice_in_dim(whole, layer * cross.shape[1], cross.shape[1], 1)
        return own.astype(jnp.float32) + near_part.astype(jnp.float32) + cross.astype(jnp.float32)

    mixed = (resid + after(layer_d_resid, mixed_sum).astype(jnp.float32)).astype(LOW)
    grad_down = lax.dynamic_slice_in_dim(down_term, layer * down_rows, down_rows, 0).astype(jnp.float32)
    grad_down = grad_down + sum(slab.astype(jnp.float32) for slab in down_parts)

    out_term = contract_rows(attended, layer_d_resid).astype(LOW)
    d_attended = contract_cols(layer_d_resid, w_out_own).astype(LOW)
    d_qkv, out_parts, mixed = attend_back(ends, qkv, d_attended, out_term, mixed)
    mixed = mixed.reshape(rows_here, block, width)
    grad_gate, grad_up = own_part(gate_term, *parts[1:3]), own_part(up_term, *parts[4:6])
    grad_out = jnp.sum(out_parts.astype(jnp.float32), axis=0)
    qkv_term = contract_rows(layer_normed, d_qkv).astype(LOW)
    grad_low, gain_grads = close_layer(
        after(qkv_term, d_qkv), w_qkv, x_own, d_resid, full_gain_attn, gain_mlp_term
    )
    grad_tokens = grad_low.astype(jnp.float32).reshape(rows_here, block, width)

    qkv_term = qkv_term.reshape(4, layers, 2 * shard, 3 * owned).transpose(1, 0, 2, 3)
    qkv_term = qkv_term.reshape(layers * members * shard, 3 * owned)
    qkv_term = lax.psum_scatter(qkv_term, "z", scatter_dimension=0, tiled=True)
    qkv_term = lax.all_to_all(qkv_term.reshape(members, shard, 3 * owned), LAYER, 0, 0)
    qkv_term = qkv_term.reshape(members, shard, 3, owned).transpose(2, 1, 0, 3).astype(jnp.float32)
    grad_query, grad_key, grad_value = qkv_term.reshape(3, shard, width)
    gain_grads = lax.dynamic_index_in_dim(jnp.sum(gain_grads, axis=1).reshape(2, 2, shard), lax.axis_index("x"), 1, False)
    return (
        mixed,
        grad_tokens,
        grad_query,
        grad_key,
        grad_value,
        grad_out,
        grad_gate,
        grad_up,
        grad_down,
        gain_grads[0],
        gain_grads[1],
    )


def body_any(
    tokens,
    lengths,
    cotangent,
    w_query,
    w_key,
    w_value,
    w_out,
    w_gate,
    w_up,
    w_down,
    gain_attn,
    gain_mlp,
):
    rows_here, block, width = tokens.shape
    count = rows_here * block
    scale = 1.0 / math.sqrt(HD)
    kv_place = lax.axis_index("kv")
    key_places = kv_place * block + jnp.arange(block, dtype=jnp.int32)
    attn_set = (
        lax.all_gather(w_query, ("row", "kv"), axis=0, tiled=True),
        lax.all_gather(w_key, ("row", "kv"), axis=0, tiled=True),
        lax.all_gather(w_value, ("row", "kv"), axis=0, tiled=True),
        lax.all_gather(w_out, ("row", "kv"), axis=0, tiled=True),
        lax.all_gather(gain_attn, ("row", "kv"), axis=0, tiled=True),
        lax.all_gather(gain_mlp, ("row", "kv"), axis=0, tiled=True),
    )
    full_query, full_key, full_value, full_out, full_gain_attn, full_gain_mlp = attn_set
    flat = tokens.reshape(count, width).astype(jnp.float32)
    normed_attn, inverse_attn = norm_forward(flat, full_gain_attn)
    normed_attn_low = normed_attn.astype(jnp.bfloat16)
    query_low = jnp.dot(normed_attn_low, full_query, preferred_element_type=jnp.float32).astype(
        jnp.bfloat16
    )
    key_low = jnp.dot(normed_attn_low, full_key, preferred_element_type=jnp.float32).astype(
        jnp.bfloat16
    )
    value_low = jnp.dot(normed_attn_low, full_value, preferred_element_type=jnp.float32).astype(
        jnp.bfloat16
    )
    key_heads = key_low.reshape(rows_here, block, H, HD)
    value_heads = value_low.reshape(rows_here, block, H, HD)
    segment, valid = segment_table(lengths)
    key_segment = lax.dynamic_slice_in_dim(segment, kv_place * block, block, 1)
    key_valid = lax.dynamic_slice_in_dim(valid, kv_place * block, block, 1)
    queries_all = lax.all_gather(
        query_low.reshape(rows_here, block, width), "kv", axis=1, tiled=True
    )
    which = 0
    query_rows = queries_all[which]
    query_segment = segment[which]
    sigmoid_part, allowed = score_block(
        query_rows,
        key_heads[which],
        query_segment,
        key_segment[which],
        key_valid[which],
        jnp.int32(0),
        key_places,
    )
    weight = (sigmoid_part * allowed).astype(jnp.bfloat16)
    summed = jnp.einsum(
        "hqk,khd->qhd", weight, value_heads[which], preferred_element_type=jnp.float32
    )
    pieces = [
        lax.psum_scatter(
            summed.reshape(lax.axis_size("kv") * block, width).astype(jnp.bfloat16),
            "kv",
            scatter_dimension=0,
            tiled=True,
        ).astype(jnp.float32)
    ]
    attended_low = jnp.stack(pieces).reshape(count, width).astype(jnp.bfloat16)
    resid = flat + jnp.dot(attended_low, full_out, preferred_element_type=jnp.float32)
    normed_mlp, inverse_mlp = norm_forward(resid, full_gain_mlp)
    normed_mlp_low = normed_mlp.astype(jnp.bfloat16)
    upstream_low = cotangent.reshape(count, width)
    upstream = upstream_low.astype(jnp.float32)
    slice_gate, slice_up, slice_down = (
        lax.all_gather(w_gate, "row", axis=1, tiled=True),
        lax.all_gather(w_up, "row", axis=1, tiled=True),
        lax.all_gather(w_down, "row", axis=0, tiled=True),
    )
    row_normed, row_upstream = (
        lax.all_gather(normed_mlp_low.reshape(rows_here, block, width), "kv", axis=1, tiled=True),
        lax.all_gather(cotangent, "kv", axis=1, tiled=True),
    )
    normed_rows = row_normed.reshape(rows_here * LEN, width)
    upstream_rows = row_upstream.reshape(rows_here * LEN, width)
    gate = jnp.dot(normed_rows, slice_gate, preferred_element_type=jnp.float32)
    up_part = jnp.dot(normed_rows, slice_up, preferred_element_type=jnp.float32)
    sigmoid_gate = jax.nn.sigmoid(gate)
    hidden_low = (gate * sigmoid_gate * up_part).astype(jnp.bfloat16)
    hidden_rows = hidden_low.reshape(rows_here, LEN, hidden_low.shape[1])
    which = 0
    hidden_part = hidden_rows[which]
    outputs = [
        lax.psum_scatter(
            jnp.dot(hidden_part, slice_down, preferred_element_type=jnp.float32).astype(
                jnp.bfloat16
            ),
            "kv",
            scatter_dimension=0,
            tiled=True,
        ).astype(jnp.float32)
    ]
    result = resid + jnp.stack(outputs).reshape(count, width)
    d_hidden = contract_cols(upstream_rows, slice_down)
    d_gate, d_up = gate_backward(d_hidden, gate, up_part, sigmoid_gate)
    partial_normed = contract_cols(d_gate, slice_gate) + contract_cols(d_up, slice_up)
    d_normed_mlp = (
        lax.psum_scatter(
            partial_normed.reshape(rows_here, LEN, width).astype(jnp.bfloat16),
            "kv",
            scatter_dimension=1,
            tiled=True,
        )
        .astype(jnp.float32)
        .reshape(count, width)
    )
    grad_gate, grad_up, grad_down = (
        lax.psum_scatter(
            contract_rows(normed_rows, d_gate).astype(jnp.bfloat16),
            "row",
            scatter_dimension=1,
            tiled=True,
        ).astype(jnp.float32),
        lax.psum_scatter(
            contract_rows(normed_rows, d_up).astype(jnp.bfloat16),
            "row",
            scatter_dimension=1,
            tiled=True,
        ).astype(jnp.float32),
        lax.psum_scatter(
            contract_rows(hidden_low, upstream_rows).astype(jnp.bfloat16),
            "row",
            scatter_dimension=0,
            tiled=True,
        ).astype(jnp.float32),
    )
    mixed = result.astype(jnp.bfloat16).reshape(rows_here, block, width)
    back_mlp, gain_mlp_term = norm_backward(resid, inverse_mlp, full_gain_mlp, d_normed_mlp)
    d_resid = upstream + back_mlp
    d_resid_low = d_resid.astype(jnp.bfloat16)
    d_attended = contract_cols(d_resid_low, full_out).astype(jnp.bfloat16)
    grads_all = lax.all_gather(
        d_attended.reshape(rows_here, block, width), "kv", axis=1, tiled=True
    )
    query_block = min(512, LEN)
    block_count = LEN // query_block
    which = 0

    def sweep(carry, index, which=which):
        key_total, value_total = carry
        start = index * query_block
        query_rows = lax.dynamic_slice_in_dim(queries_all[which], start, query_block, 0)
        grad_rows = lax.dynamic_slice_in_dim(grads_all[which], start, query_block, 0)
        query_segment = lax.dynamic_slice_in_dim(segment[which], start, query_block, 0)
        sigmoid_part, allowed = score_block(
            query_rows,
            key_heads[which],
            query_segment,
            key_segment[which],
            key_valid[which],
            start,
            key_places,
        )
        weight = (sigmoid_part * allowed).astype(jnp.bfloat16)
        grad_heads = grad_rows.reshape(query_block, H, HD)
        value_total = value_total + jnp.einsum(
            "hqk,qhd->khd", weight, grad_heads, preferred_element_type=jnp.float32
        )
        d_weight = jnp.einsum(
            "qhd,khd->hqk", grad_heads, value_heads[which], preferred_element_type=jnp.float32
        )
        d_score = (d_weight * sigmoid_part * (1.0 - sigmoid_part) * allowed).astype(jnp.bfloat16)
        query_part = (
            jnp.einsum(
                "hqk,khd->qhd", d_score, key_heads[which], preferred_element_type=jnp.float32
            )
            * scale
        )
        key_total = (
            key_total
            + jnp.einsum(
                "hqk,qhd->khd",
                d_score,
                query_rows.reshape(query_block, H, HD),
                preferred_element_type=jnp.float32,
            )
            * scale
        )
        return ((key_total, value_total), query_part.reshape(query_block, width))

    zeros = jnp.zeros((block, H, HD), jnp.float32)
    totals, query_parts = lax.scan(sweep, (zeros, zeros), jnp.arange(block_count, dtype=jnp.int32))
    query_terms = [query_parts.reshape(LEN, width)]
    key_grads = [totals[0].reshape(block, width)]
    value_grads = [totals[1].reshape(block, width)]
    query_local = lax.psum_scatter(
        jnp.stack(query_terms).astype(jnp.bfloat16), "kv", scatter_dimension=1, tiled=True
    ).astype(jnp.float32)
    d_query_low = query_local.reshape(count, width).astype(jnp.bfloat16)
    d_key_low = jnp.stack(key_grads).reshape(count, width).astype(jnp.bfloat16)
    d_value_low = jnp.stack(value_grads).reshape(count, width).astype(jnp.bfloat16)
    d_normed_attn = (
        contract_cols(d_query_low, full_query)
        + contract_cols(d_key_low, full_key)
        + contract_cols(d_value_low, full_value)
    )
    back_attn, gain_attn_term = norm_backward(flat, inverse_attn, full_gain_attn, d_normed_attn)
    grad_tokens = (d_resid + back_attn).reshape(rows_here, block, width)
    projected_low = jnp.concatenate((d_query_low, d_key_low, d_value_low), axis=1)
    grad_projections = lax.psum_scatter(
        contract_rows(normed_attn_low, projected_low),
        ("row", "kv"),
        scatter_dimension=0,
        tiled=True,
    )
    out_term = contract_rows(attended_low, d_resid_low)
    grad_out, grad_gain_attn, grad_gain_mlp = (
        lax.psum_scatter(out_term, ("row", "kv"), scatter_dimension=0, tiled=True),
        lax.psum_scatter(gain_attn_term, ("row", "kv"), scatter_dimension=0, tiled=True),
        lax.psum_scatter(gain_mlp_term, ("row", "kv"), scatter_dimension=0, tiled=True),
    )
    grad_query = grad_projections[:, :width]
    grad_key = grad_projections[:, width : 2 * width]
    grad_value = grad_projections[:, 2 * width :]
    return (
        mixed,
        grad_tokens,
        grad_query,
        grad_key,
        grad_value,
        grad_out,
        grad_gate,
        grad_up,
        grad_down,
        grad_gain_attn,
        grad_gain_mlp,
    )


def solution(mesh):
    rows, columns = mesh.shape["row"], mesh.shape["kv"]
    if rows == 4 and columns == 2 * rows:
        mesh = Mesh(mesh.devices.reshape(2, 2, rows, 2), ("y", "c", "z", "x"))
        row, kv, run = ("y", "c"), ("z", "x"), body_layers
    else:
        row, kv, run = "row", "kv", body_any
    both = ("y", "c", "z", "x") if run is body_layers else ("row", "kv")
    tall, wide, flat = P(both, None), P(None, both), P(both)
    tokens = P(row, kv, None)
    return jax.shard_map(
        run,
        mesh=mesh,
        in_specs=(tokens, P(row, None), tokens, tall, tall, tall, tall, wide, wide, tall, flat, flat),
        out_specs=(tokens, tokens, tall, tall, tall, tall, wide, wide, tall, flat, flat),
        check_vma=False,
    )
```

```python
import functools
import math

import jax
import jax.numpy as jnp
from jax import lax
from jax.experimental import pallas as pl
from jax.experimental.pallas import tpu as pltpu
from jax.sharding import Mesh, PartitionSpec as P

H = 16
HD = 128
LEN = 4096


EPSILON = 1e-05


def contract_rows(left, right):
    return lax.dot_general(
        left, right, (((0,), (0,)), ((), ())), preferred_element_type=jnp.float32
    )


def contract_cols(left, right):
    return lax.dot_general(
        left, right, (((1,), (1,)), ((), ())), preferred_element_type=jnp.float32
    )


def norm_forward(value, gain):
    inverse = lax.rsqrt(jnp.mean(value * value, axis=-1, keepdims=True) + EPSILON)
    return (value * inverse * gain.astype(jnp.float32), inverse)


def norm_backward(value, inverse, gain, upstream):
    scaled = upstream * gain.astype(jnp.float32)
    inner = jnp.mean(scaled * value, axis=-1, keepdims=True)
    back = inverse * scaled - value * (inverse * inverse * inverse) * inner
    gain_term = jnp.sum(upstream * value * inverse, axis=0)
    return (back, gain_term)


def segment_table(lengths):
    ends = jnp.cumsum(lengths, axis=-1)
    places = jnp.arange(LEN, dtype=jnp.int32)
    segment = jnp.sum((ends[:, None, :] <= places[None, :, None]).astype(jnp.int32), axis=-1)
    valid = places[None, :] < ends[:, -1:]
    return (segment, valid)


def score_block(
    query_rows, key_heads, query_segment, key_segment, key_valid, query_start, key_places
):
    count = query_rows.shape[0]
    query_heads = query_rows.reshape(count, H, HD)
    raw = jnp.einsum("qhd,khd->hqk", query_heads, key_heads, preferred_element_type=jnp.float32)
    scores = raw * (1.0 / math.sqrt(HD)) - math.log(LEN)
    places = query_start + jnp.arange(count, dtype=jnp.int32)
    allowed = (
        (key_places[None, :] <= places[:, None])
        & (key_segment[None, :] == query_segment[:, None])
        & key_valid[None, :]
    )
    return (jax.nn.sigmoid(scores), allowed.astype(jnp.float32)[None])


def gate_backward(d_hidden, gate, up_part, sigmoid_gate):
    d_gate = (d_hidden * up_part * sigmoid_gate * (1.0 + gate * (1.0 - sigmoid_gate))).astype(
        jnp.bfloat16
    )
    d_up = (d_hidden * gate * sigmoid_gate).astype(jnp.bfloat16)
    return (d_gate, d_up)


TILE = 512
LOW = jnp.bfloat16
VMEM_LIMIT = 60 * 1024 * 1024


def dot_nt(left, right):
    return lax.dot_general(left, right, (((1,), (1,)), ((), ())), preferred_element_type=jnp.float32)


def dot_wide(left, right):
    return jnp.dot(left, right, preferred_element_type=jnp.float32)


HALF = TILE // 2
PIECES = 4
CHUNK = 32
MESH_ID = pl.DeviceIdType.MESH


def flip(bit, by):
    return bit + by - 2 * bit * by


def spot():
    return tuple(lax.axis_index(name) for name in ("y", "c", "z", "x"))


def near():
    y, c, z, x = spot()
    return (y, c, z, 1 - x), (1 - y, c, z, x), (y, 1 - c, z, x)


def partner_of(y, c, z, x):
    return lax.rem(z, 2), z // 2, 2 * c + y, x


def place_of(y, c, x, half=None):
    first = (4 * c + 2 * y + x) * TILE
    if half is None:
        return pl.ds(pl.multiple_of(first, TILE), TILE)
    return pl.ds(pl.multiple_of(first + half * HALF, HALF), HALF)


def quarter_of(y, c, x, half, quarter):
    return pl.ds(pl.multiple_of((4 * c + 2 * y + x) * TILE + half * HALF + quarter * (HALF // 2), HALF // 2), HALF // 2)


def remote(src, dst, send, recv, peer):
    return pltpu.make_async_remote_copy(
        src_ref=src, dst_ref=dst, send_sem=send, recv_sem=recv, device_id=peer, device_id_type=MESH_ID
    )


def greet(peers):
    barrier = pltpu.get_barrier_semaphore()
    for peer in peers:
        pl.semaphore_signal(barrier, inc=1, device_id=peer, device_id_type=MESH_ID)
    pl.semaphore_wait(barrier, len(peers))


class Gather:
    def __init__(self, own, whole, send, recv):
        y, c, z, x = spot()
        across_x, across_y, core = near()

        def passed(k, at, peer):
            return remote(whole.at[at], whole.at[at], send.at[k], recv.at[k], peer)

        self.halves = []
        for half in (0, 1):
            k, at = 9 * half, place_of(y, c, x, half)
            mine = [
                remote(own(half), whole.at[at], send.at[k + m], recv.at[k + m], peer)
                for m, peer in enumerate((across_x, across_y, core))
            ]
            held_x, held_y = (y, c, 1 - x), (1 - y, c, x)
            far = (1 - y, c, 1 - x)
            self.halves.append(
                (
                    mine,
                    passed(k + 3, quarter_of(*held_x, half, 0), across_y),
                    passed(k + 4, quarter_of(*held_y, half, 1), across_x),
                    [passed(k + 5, place_of(*held_x, half), core), passed(k + 6, place_of(*held_y, half), core)],
                    [passed(k + 7 + q, quarter_of(*far, half, q), core) for q in (0, 1)],
                )
            )

    def start(self, half):
        for copy in self.halves[half][0]:
            copy.start()

    def pass_near(self, half):
        mine, over_y, over_x, from_near, from_far = self.halves[half]
        mine[0].wait_recv()
        over_y.start()
        from_near[0].start()
        mine[1].wait_recv()
        over_x.start()
        from_near[1].start()

    def pass_far(self, half):
        mine, over_y, over_x, from_near, from_far = self.halves[half]
        over_y.wait_recv()
        from_far[0].start()
        over_x.wait_recv()
        from_far[1].start()

    def finish(self):
        for mine, over_y, over_x, from_near, from_far in self.halves:
            for copy in [mine[2]] + from_near + from_far:
                copy.wait_recv()
            for copy in mine + [over_y, over_x] + from_near + from_far:
                copy.wait_send()


GATHER_COPIES = 18


class GatherWhole:
    def __init__(self, own, whole, send, recv):
        y, c, z, x = spot()
        across_x, across_y, core = near()

        def from_own(k, half, peer):
            return remote(own(half), whole.at[place_of(y, c, x, half)], send.at[k], recv.at[k], peer)

        def passed(k, at, peer):
            return remote(whole.at[at], whole.at[at], send.at[k], recv.at[k], peer)

        self.mine = [
            [from_own(0, 0, across_x), from_own(1, 0, across_y), from_own(2, 0, core)],
            [from_own(3, 1, across_x), from_own(4, 1, across_y), from_own(5, 1, core)],
        ]
        held_x = [place_of(y, c, 1 - x, half) for half in (0, 1)]
        held_y = [place_of(1 - y, c, x, half) for half in (0, 1)]
        far = [place_of(1 - y, c, 1 - x, half) for half in (0, 1)]
        self.over_y, self.over_x = passed(6, held_x[0], across_y), passed(7, held_y[1], across_x)
        self.core_x = [passed(8 + half, held_x[half], core) for half in (0, 1)]
        self.core_y = [passed(10 + half, held_y[half], core) for half in (0, 1)]
        self.core_far = [passed(12 + half, far[half], core) for half in (0, 1)]

    def start(self, half):
        for copy in self.mine[half]:
            copy.start()

    def pass_first(self):
        self.mine[0][0].wait_recv()
        self.over_y.start()
        self.core_x[0].start()
        self.mine[0][1].wait_recv()
        self.core_y[0].start()

    def pass_second(self):
        self.mine[1][1].wait_recv()
        self.over_x.start()
        self.core_y[1].start()
        self.mine[1][0].wait_recv()
        self.core_x[1].start()

    def pass_far(self):
        self.over_y.wait_recv()
        self.core_far[0].start()
        self.over_x.wait_recv()
        self.core_far[1].start()

    def finish(self):
        from_core = [self.mine[0][2], self.mine[1][2]] + self.core_x + self.core_y + self.core_far
        for copy in from_core:
            copy.wait_recv()
        for copy in self.mine[0] + self.mine[1] + [self.over_y, self.over_x] + self.core_x + self.core_y + self.core_far:
            copy.wait_send()


class Trade:
    def __init__(self, sources, dst, held, send, recv, held_recv, pass_send, detour=True):
        y, c, z, x = spot()
        self.detour = detour
        across_y = (1 - y, c, z, x)
        self.moves = z != 2 * c + y
        self.away = (y == c) & (z == 1 + y)
        self.straight = self.moves & jnp.logical_not(self.away) if detour else self.moves
        self.passes = (1 - y == c) & (z == 2 - y)
        partner = partner_of(y, c, z, x)
        comes_by = ((partner[0] == partner[1]) & (partner[2] == 1 + partner[0])).astype(jnp.int32)
        self.sender = (flip(partner[0], comes_by), partner[1], partner[2], x) if detour else partner
        self.across_y = across_y
        target = partner_of(*across_y)
        self.direct, self.keep, self.out, self.onward = [], [], [], []
        for h, source in enumerate(sources):
            self.direct.append(remote(source, dst(h, partner), send.at[h], recv.at[h], partner))
            self.keep.append(pltpu.make_async_copy(source, dst(h, (y, c, z, x)), recv.at[h]))
            self.out.append(remote(source, held.at[h], send.at[h], held_recv.at[h], across_y))
            self.onward.append(remote(held.at[h], dst(h, target), pass_send.at[h], recv.at[h], target))

    def greet(self, barrier, neighbours_greet):
        @pl.when(self.moves)
        def _():
            pl.semaphore_signal(barrier, inc=1, device_id=self.sender, device_id_type=MESH_ID)

        count = self.straight.astype(jnp.int32)
        if not self.detour:
            return count
        count = count + self.passes.astype(jnp.int32)
        if not neighbours_greet:

            @pl.when(self.passes)
            def _():
                pl.semaphore_signal(barrier, inc=1, device_id=self.across_y, device_id_type=MESH_ID)

            count = count + self.away.astype(jnp.int32)
        return count

    def start(self, h):
        @pl.when(self.straight)
        def _():
            self.direct[h].start()

        if self.detour:

            @pl.when(self.away)
            def _():
                self.out[h].start()

        @pl.when(jnp.logical_not(self.moves))
        def _():
            self.keep[h].start()

    def wait_sent(self, h):
        @pl.when(self.straight)
        def _():
            self.direct[h].wait_send()

        if self.detour:

            @pl.when(self.away)
            def _():
                self.out[h].wait_send()

    def forward(self, h):
        if self.detour:

            @pl.when(self.passes)
            def _():
                self.out[h].wait_recv()
                self.onward[h].start()

    def arrive(self, h):
        @pl.when(self.moves)
        def _():
            self.direct[h].wait_recv()

        @pl.when(jnp.logical_not(self.moves))
        def _():
            self.keep[h].wait()

    def finish(self, first=0):
        for h in range(len(self.direct)):
            if h >= first:
                self.wait_sent(h)

            if self.detour:

                @pl.when(self.passes)
                def _():
                    self.onward[h].wait_send()


def trade_scratch(pieces, rows, width):
    return [pltpu.VMEM((pieces, rows, width), LOW)] + [pltpu.SemaphoreType.DMA((pieces,)) for _ in range(4)]


class Chain:
    def __init__(self, own, slab, sems, index):
        self.own, self.slab, self.sems, self.index = own, slab, sems, index
        self.last = lax.axis_size("z") - 1

    def move(self, which, h, source, layer, to):
        y, c, z, x = spot()
        return remote(
            source, self.slab(layer), self.sems[2 * which].at[self.index, h], self.sems[2 * which + 1].at[self.index, h], (y, c, to, x)
        )

    def up(self, h):
        z = lax.axis_index("z")
        return self.move(0, h, self.own if h == 0 else self.slab(z - h), z - h, z + 1)

    def down(self, h):
        z = lax.axis_index("z")
        return self.move(1, h, self.own if h == 0 else self.slab(z + h), z + h, z - 1)

    def start(self):
        z = lax.axis_index("z")

        @pl.when(z < self.last)
        def _():
            self.up(0).start()

        @pl.when(z > 0)
        def _():
            self.down(0).start()

    def arrive(self, h):
        z = lax.axis_index("z")

        @pl.when(z - h - 1 >= 0)
        def _():
            self.move(0, h, self.slab(z - h - 1), z - h - 1, z).wait_recv()
            if h < 2:

                @pl.when(z < self.last)
                def _():
                    self.up(h + 1).start()

        @pl.when(z + h + 1 <= self.last)
        def _():
            self.move(1, h, self.slab(z + h + 1), z + h + 1, z).wait_recv()
            if h < 2:

                @pl.when(z > 0)
                def _():
                    self.down(h + 1).start()

    def finish(self):
        z = lax.axis_index("z")
        for h in range(3):

            @pl.when((z < self.last) & (z - h >= 0))
            def _():
                self.up(h).wait_send()

            @pl.when((z > 0) & (z + h <= self.last))
            def _():
                self.down(h).wait_send()


def chain_sems(count):
    return [pltpu.SemaphoreType.DMA((count, 3)) for _ in range(4)]


def greet_neighbours(peers):
    y, c, z, x = spot()
    last = lax.axis_size("z") - 1
    barrier = pltpu.get_barrier_semaphore()
    for peer in peers:
        pl.semaphore_signal(barrier, inc=1, device_id=peer, device_id_type=MESH_ID)

    @pl.when(z > 0)
    def _():
        pl.semaphore_signal(barrier, inc=1, device_id=(y, c, z - 1, x), device_id_type=MESH_ID)

    @pl.when(z < last)
    def _():
        pl.semaphore_signal(barrier, inc=1, device_id=(y, c, z + 1, x), device_id_type=MESH_ID)

    return barrier, len(peers) + (z > 0).astype(jnp.int32) + (z < last).astype(jnp.int32)


def others():
    y, c, z, x = spot()
    return [(flip(y, dy), flip(c, dc), z, flip(x, dx)) for dy in (0, 1) for dc in (0, 1) for dx in (0, 1) if dy + dc + dx]


def line_of():
    y, c, z, x = spot()
    return [(y, c, lax.rem(z + dz, 4), x) for dz in (1, 2, 3)]


class Fold:
    def __init__(self, whole, far, near_part, cross, mine, theirs, send, recv, local):
        y, c, z, x = spot()
        a, b = z // 2, lax.rem(z, 2)
        size = whole.shape[1] // 4

        def slab(at):
            return whole.at[:, pl.ds(pl.multiple_of(at * size, size), size)]

        pair, middle = (y, c, 2 * a + 1 - b, x), (y, c, 2 * (1 - a) + b, x)
        self.far = remote(slab(2 * (1 - a) + 1 - b), far, send.at[0], recv.at[0], pair)
        self.near = remote(slab(2 * a + 1 - b), near_part, send.at[1], recv.at[1], pair)
        self.cross = remote(mine, cross, send.at[2], recv.at[2], middle)
        self.fetches = [
            pltpu.make_async_copy(slab(2 * (1 - a) + b), mine, local.at[0]),
            pltpu.make_async_copy(far, theirs, local.at[1]),
        ]
        self.mine, self.theirs = mine, theirs

    def start(self):
        self.far.start()
        self.fetches[0].start()

    def fold(self):
        self.far.wait_recv()
        self.fetches[1].start()
        for copy in self.fetches:
            copy.wait()
        add_rows(self.mine, 0, self.theirs, 0, self.mine.shape[0])
        self.cross.start()
        self.near.start()

    def finish(self):
        for copy in (self.near, self.cross):
            copy.wait_recv()
        for copy in (self.far, self.near, self.cross):
            copy.wait_send()


def fold_peers():
    y, c, z, x = spot()
    a, b = z // 2, lax.rem(z, 2)
    return ((y, c, 2 * a + 1 - b, x), (y, c, 2 * (1 - a) + b, x))


def add_rows(total, first, term, start, count):
    def step(i, carry):
        here = pl.ds(pl.multiple_of(first + i * CHUNK, CHUNK), CHUNK)
        there = pl.ds(pl.multiple_of(start + i * CHUNK, CHUNK), CHUNK)
        total[here, :] = (total[here, :].astype(jnp.float32) + term[there, :].astype(jnp.float32)).astype(LOW)
        return carry

    lax.fori_loop(0, count // CHUNK, step, 0)


def scatter_scratch(width, parts=1):
    return [
        pltpu.VMEM((2, TILE, width), LOW),
        pltpu.VMEM((4, TILE, width), LOW),
        pltpu.VMEM((4, TILE, width), LOW),
        pltpu.VMEM((2, HALF, width), LOW),
        pltpu.VMEM((2, TILE, width), LOW),
        pltpu.SemaphoreType.DMA((parts, 10)),
        pltpu.SemaphoreType.DMA((parts, 10)),
    ]


class Scatter:
    def __init__(self, produce, staged, core_part, total, relayed, landed, send, recv, part=0, start=0, size=TILE):
        across_x, across_y, core = near()
        self.produce, self.staged, self.core_part, self.total, self.relayed = produce, staged, core_part, total, relayed
        self.start, self.size, self.half = start, size, size // 2
        send, recv = send.at[part], recv.at[part]
        rows = pl.ds(start, size)
        halves = (pl.ds(start, self.half), pl.ds(start + self.half, self.half))
        self.relay_row = start // 2
        passing = pl.ds(self.relay_row, self.half)
        self.to_core = [
            remote(staged.at[k % 2, rows], core_part.at[k, rows], send.at[k], recv.at[k], core) for k in range(4)
        ]
        self.far_x = remote(total.at[0, halves[0]], relayed.at[0, passing], send.at[4], recv.at[4], across_x)
        self.far_y = remote(total.at[0, halves[1]], relayed.at[1, passing], send.at[5], recv.at[5], across_y)
        self.to_x = [
            remote(total.at[1, at], landed.at[0, at], send.at[6 + half], recv.at[6 + half], across_x)
            for half, at in enumerate(halves)
        ]
        self.to_y = [
            remote(total.at[2, at], landed.at[1, at], send.at[8 + half], recv.at[8 + half], across_y)
            for half, at in enumerate(halves)
        ]

    def begin(self):
        y, c, z, x = spot()
        rows = pl.ds(self.start, self.size)
        for k, (to_row, to_column) in enumerate(((1 - y, 1 - x), (y, 1 - x), (1 - y, x), (y, x))):
            if k >= 2:
                self.to_core[k - 2].wait_send()
            self.produce(2 * k, to_row, 1 - c, to_column, self.staged.at[k % 2, rows])
            self.to_core[k].start()
            self.produce(2 * k + 1, to_row, c, to_column, self.total.at[k, rows])
            self.to_core[k].wait_recv()
            add_rows(self.total.at[k], self.start, self.core_part.at[k], self.start, self.size)
            if k == 0:
                self.far_x.start()
                self.far_y.start()
            if k == 1:
                self.to_x[0].start()
            if k == 2:
                self.to_y[1].start()

    def relay(self):
        self.far_y.wait_recv()
        add_rows(self.total.at[1], self.start + self.half, self.relayed.at[1], self.relay_row, self.half)
        self.to_x[1].start()
        self.far_x.wait_recv()
        add_rows(self.total.at[2], self.start, self.relayed.at[0], self.relay_row, self.half)
        self.to_y[0].start()

    def arrive(self):
        for copy in self.to_x + self.to_y:
            copy.wait_recv()

    def finish(self):
        for copy in self.to_core[2:] + [self.far_x, self.far_y] + self.to_x + self.to_y:
            copy.wait_send()


def sum_and_gather(part_of, rows_of_half, gather, beside):
    sums = [part_of(half) for half in (0, 1)]
    sums[0].begin()
    sums[0].relay()
    sums[1].begin()
    sums[0].arrive()
    rows_of_half(0)
    gather.start(0)
    beside(0)
    sums[1].relay()
    beside(1)
    sums[1].arrive()
    rows_of_half(1)
    gather.start(1)
    gather.pass_near(0)
    beside(2)
    gather.pass_near(1)
    gather.pass_far(0)
    gather.pass_far(1)
    gather.finish()
    beside(3)
    for half in (0, 1):
        sums[half].finish()


def begin_kernel(
    x_own, w_query, w_key, w_value, facts, x_whole, w_qkv, facts_whole,
    gather_send, gather_recv, w_send, w_recv, fact_send, fact_recv, local, *scratch
):
    y, c, z, x = spot()
    row = 2 * y + c
    layer = others()
    trade_parts, sems = scratch[:5], scratch[5:]
    trade = Trade(
        [x_own.at[half] for half in (0, 1)], lambda half, at: x_whole.at[place_of(at[0], at[1], at[3], half)], *trade_parts, detour=False
    )
    barrier, count = greet_neighbours(layer)
    pl.semaphore_wait(barrier, count + trade.greet(barrier, True))

    shard, width = w_query.shape
    owned = width // 8
    for half in (0, 1):
        trade.start(half)
    spread = [
        remote(facts, facts_whole.at[row, z, x], fact_send.at[k], fact_recv.at[k], peer) for k, peer in enumerate(layer)
    ]
    kept = [pltpu.make_async_copy(facts, facts_whole.at[row, z, x], local.at[3])]
    for m, source in enumerate((w_query, w_key, w_value)):
        dst = w_qkv.at[row, z, pl.ds(pl.multiple_of(x * shard, shard), shard), pl.ds(m * owned, owned)]
        for k, peer in enumerate(layer):
            columns = pl.ds(pl.multiple_of((4 * peer[0] + 2 * peer[1] + peer[3]) * owned, owned), owned)
            spread.append(remote(source.at[:, columns], dst, w_send.at[m, k], w_recv.at[m, k], peer))
        columns = pl.ds(pl.multiple_of((4 * y + 2 * c + x) * owned, owned), owned)
        kept.append(pltpu.make_async_copy(source.at[:, columns], dst, local.at[m]))
    for copy in spread + kept:
        copy.start()

    gather = GatherWhole(lambda half: x_whole.at[place_of(y, c, x, half)], x_whole, gather_send, gather_recv)
    for half in (0, 1):
        trade.forward(half)
        trade.arrive(half)
        gather.start(half)

    for copy in kept:
        copy.wait()
    for copy in spread:
        copy.wait_recv()
    chains = [
        Chain(facts_whole.at[:, z], lambda at: facts_whole.at[:, at], sems, 0),
        Chain(w_qkv.at[:, z], lambda at: w_qkv.at[:, at], sems, 1),
    ]

    def arrive(h):
        for chain in chains:
            chain.arrive(h)

    for chain in chains:
        chain.start()
    gather.pass_first()
    arrive(0)
    gather.pass_second()
    arrive(1)
    gather.pass_far()
    arrive(2)
    gather.finish()
    trade.finish()
    for copy in spread:
        copy.wait_send()
    for chain in chains:
        chain.finish()


def anywhere():
    return pl.BlockSpec(memory_space=pl.ANY)


def in_vmem():
    return pl.BlockSpec(memory_space=pltpu.VMEM)


def dma(*shape):
    return pltpu.SemaphoreType.DMA(shape)


def remote_params(number):
    return pltpu.CompilerParams(collective_id=number, has_side_effects=True, vmem_limit_bytes=VMEM_LIMIT)


def begin(x_own, w_query, w_key, w_value, facts):
    block, width = x_own.shape
    shard = w_query.shape[0]
    x_whole, w_qkv, facts_whole = pl.pallas_call(
        begin_kernel,
        out_shape=(
            jax.ShapeDtypeStruct((8 * block, width), LOW),
            jax.ShapeDtypeStruct((4, 4, 2 * shard, 3 * width // 8), LOW),
            jax.ShapeDtypeStruct((4, 4, 2, *facts.shape), jnp.float32),
        ),
        in_specs=[in_vmem()] + [anywhere()] * 4,
        out_specs=[anywhere()] * 3,
        scratch_shapes=[
            dma(GATHER_COPIES), dma(GATHER_COPIES), dma(3, 7), dma(3, 7), dma(7), dma(7), dma(4),
            *trade_scratch(2, block // 2, width), *chain_sems(2),
        ],
        compiler_params=remote_params(1),
        cost_estimate=pl.CostEstimate(flops=0, bytes_accessed=350_000_000, transcendentals=0),
    )(x_own.reshape(2, block // 2, width), w_query, w_key, w_value, facts)
    return x_whole, w_qkv.reshape(width, 3 * width // 8), facts_whole


def summed(total, landed, here):
    parts = (total[3, here, :], landed[0, here, :], landed[1, here, :])
    return sum(part.astype(jnp.float32) for part in parts)


def over_chunks(work, half):
    def step(i, carry):
        work(pl.ds(pl.multiple_of(half * HALF + i * CHUNK, CHUNK), CHUNK))
        return carry

    lax.fori_loop(0, HALF // CHUNK, step, 0)


def own_halves(own):
    return lambda half: own.at[pl.ds(half * HALF, HALF)]


def inverse_of(value):
    return lax.rsqrt(jnp.mean(value * value, axis=-1, keepdims=True) + EPSILON)


def close_attention_kernel(attended, w_out, x_whole, gain, w_gate, w_up, resid, normed, own_gate, own_up, own, x_own, *scratch):
    scatter, (send, recv, local), sems = scratch[:7], scratch[7:10], scratch[10:]
    y, c, z, x = spot()
    fetch_x = pltpu.make_async_copy(x_whole.at[place_of(y, c, x)], x_own, local.at[0])
    fetch_x.start()
    width = w_out.shape[1]
    hidden = w_gate.shape[1]
    z = lax.axis_index("z")
    barrier, count = greet_neighbours(near())
    pl.semaphore_wait(barrier, count)

    def slab_of(whole):
        return lambda at: whole.at[:, pl.ds(pl.multiple_of(at * hidden, hidden), hidden)]

    chains, kept = [], []
    for k, (part, whole) in enumerate(((w_gate, own_gate), (w_up, own_up))):
        chains.append(Chain(part, slab_of(whole), sems, k))
        chains[k].start()
        kept.append(pltpu.make_async_copy(part, slab_of(whole)(z), local.at[1 + k]))
        kept[k].start()

    def arrive(h):
        for chain in chains:
            chain.arrive(h)

    def part_of(half):
        def produce(turn, y, c, x, out):
            at = place_of(y, c, x, half)

            def step(i, carry):
                columns = pl.ds(pl.multiple_of(i * TILE, TILE), TILE)
                out[:, columns] = dot_wide(attended[at, :], w_out[:, columns]).astype(LOW)
                return carry

            lax.fori_loop(0, width // TILE, step, 0)

        return Scatter(produce, *scatter, part=half, start=half * HALF, size=HALF)

    total, landed = scatter[2], scatter[4]

    def chunk(here):
        value = x_own[here, :].astype(jnp.float32) + summed(total, landed, here)
        resid[here, :] = value
        own[here, :] = (value * inverse_of(value) * gain[...]).astype(LOW)

    def rows_of_half(half):
        if half == 0:
            fetch_x.wait()
        over_chunks(chunk, half)

    gather = Gather(own_halves(own), normed, send, recv)
    sum_and_gather(part_of, rows_of_half, gather, lambda turn: arrive(turn - 1) if turn > 0 else None)
    keep = pltpu.make_async_copy(own, normed.at[place_of(y, c, x)], local.at[0])
    keep.start()
    for chain in chains:
        chain.finish()
    for copy in kept + [keep]:
        copy.wait()


def close_attention(attended, w_out, x_whole, gain, w_gate, w_up):
    block, width = x_whole.shape[0] // 8, x_whole.shape[1]
    hidden = w_gate.shape[1]
    return pl.pallas_call(
        close_attention_kernel,
        out_shape=(
            jax.ShapeDtypeStruct((block, width), jnp.float32),
            jax.ShapeDtypeStruct((8 * block, width), LOW),
            jax.ShapeDtypeStruct((width, 4 * hidden), LOW),
            jax.ShapeDtypeStruct((width, 4 * hidden), LOW),
        ),
        in_specs=[in_vmem(), in_vmem(), anywhere()] + [in_vmem()] * 3,
        out_specs=[in_vmem()] + [anywhere()] * 3,
        scratch_shapes=[pltpu.VMEM((block, width), LOW)] * 2
        + scatter_scratch(width, 2)
        + [dma(GATHER_COPIES), dma(GATHER_COPIES), dma(3), *chain_sems(2)],
        compiler_params=remote_params(2),
        cost_estimate=pl.CostEstimate(flops=0, bytes_accessed=450_000_000, transcendentals=0),
    )(attended, w_out, x_whole, gain, w_gate, w_up)


def norm_back(value, gain, upstream):
    inverse = inverse_of(value)
    scaled = upstream * gain
    inner = jnp.mean(scaled * value, axis=-1, keepdims=True)
    return inverse * scaled - value * (inverse * inverse * inverse) * inner, upstream * value * inverse


def fold_rows(total, terms):
    for first in range(0, CHUNK, 8):
        total[...] += terms[first : first + 8, :]


def close_mlp_kernel(
    d_gate, d_up, w_gate, w_up, resid, upstream, gain, grad_a, grad_b, d_resid, gain_term, d_resid_whole,
    far_a, near_a, cross_a, far_b, near_b, cross_b, own, blocks, *scratch
):
    scatter, (send, recv, local, fetched, fold_send, fold_recv, fold_local, mine, theirs) = scratch[:7], scratch[7:]
    y, c, z, x = spot()
    width = w_gate.shape[0]
    order = [
        place_of(r, k, q, half)
        for half in (0, 1)
        for r, q in ((1 - y, 1 - x), (y, 1 - x), (1 - y, x), (y, x))
        for k in (1 - c, c)
    ]

    def fetch(turn):
        slot = turn % 2
        return [
            pltpu.make_async_copy(source.at[order[turn]], blocks.at[slot, m], fetched.at[slot, m])
            for m, source in enumerate((d_gate, d_up))
        ]

    for copy in fetch(0):
        copy.start()
    greet(near() + fold_peers())
    folds = [
        Fold(*refs, mine.at[k], theirs, fold_send.at[k], fold_recv.at[k], fold_local.at[k])
        for k, refs in enumerate(((grad_a, far_a, near_a, cross_a), (grad_b, far_b, near_b, cross_b)))
    ]
    for fold in folds:
        fold.start()

    def part_of(half):
        def produce(turn, to_y, to_c, to_x, out):
            turn = turn + 8 * half
            if turn < 15:
                for copy in fetch(turn + 1):
                    copy.start()
            for copy in fetch(turn):
                copy.wait()

            def step(i, carry):
                columns = pl.ds(pl.multiple_of(i * TILE, TILE), TILE)
                part = dot_nt(blocks[turn % 2, 0], w_gate[columns, :]) + dot_nt(blocks[turn % 2, 1], w_up[columns, :])
                out[:, columns] = part.astype(LOW)
                return carry

            lax.fori_loop(0, width // TILE, step, 0)

        return Scatter(produce, *scatter, part=half, start=half * HALF, size=HALF)

    total, landed = scatter[2], scatter[4]
    gain_term[...] = jnp.zeros_like(gain_term)

    def chunk(here):
        back, terms = norm_back(resid[here, :], gain[...], summed(total, landed, here))
        value = upstream[here, :].astype(jnp.float32) + back
        d_resid[here, :] = value
        own[here, :] = value.astype(LOW)
        fold_rows(gain_term, terms)

    def rows_of_half(half):
        over_chunks(chunk, half)

    gather = Gather(own_halves(own), d_resid_whole, send, recv)
    sum_and_gather(part_of, rows_of_half, gather, lambda turn: folds[turn].fold() if turn < 2 else None)
    keep = pltpu.make_async_copy(own, d_resid_whole.at[place_of(y, c, x)], local.at[0])
    keep.start()
    for fold in folds:
        fold.finish()
    keep.wait()


def close_mlp(d_gate, d_up, w_gate, w_up, resid, upstream, gain, *grads):
    block, width = resid.shape
    hidden = d_gate.shape[1]
    return pl.pallas_call(
        close_mlp_kernel,
        out_shape=(
            jax.ShapeDtypeStruct((block, width), jnp.float32),
            jax.ShapeDtypeStruct((8, width), jnp.float32),
            jax.ShapeDtypeStruct((8 * block, width), LOW),
            *[jax.ShapeDtypeStruct((width, hidden // 4), LOW)] * 6,
        ),
        in_specs=[anywhere()] * 2 + [in_vmem()] * 5 + [anywhere()] * 2,
        out_specs=[in_vmem(), in_vmem()] + [anywhere()] * 7,
        scratch_shapes=[pltpu.VMEM((block, width), LOW), pltpu.VMEM((2, 2, block // 2, hidden), LOW)]
        + scatter_scratch(width, 2)
        + [dma(GATHER_COPIES), dma(GATHER_COPIES), dma(1), dma(2, 2), dma(2, 3), dma(2, 3), dma(2, 2)]
        + [pltpu.VMEM((2, width, hidden // 4), LOW), pltpu.VMEM((width, hidden // 4), LOW)],
        compiler_params=remote_params(3),
        cost_estimate=pl.CostEstimate(flops=0, bytes_accessed=450_000_000, transcendentals=0),
    )(d_gate, d_up, w_gate, w_up, resid, upstream, gain, *grads)


def close_layer_kernel(d_qkv, w_qkv, x_whole, d_resid, gain, mlp_term, grad_low, gain_grads, own, terms, layer_terms, part, column_terms, *scratch):
    scatter, (send, recv, term_send, term_recv, line_send, line_recv, x_own, x_sem) = scratch[:7], scratch[7:]
    y, c, z, x = spot()
    fetch_x = pltpu.make_async_copy(x_whole.at[place_of(y, c, x)], x_own, x_sem.at[0])
    fetch_x.start()
    partner = partner_of(y, c, z, x)
    moves = z != 2 * c + y
    width = w_qkv.shape[0]
    barrier = pltpu.get_barrier_semaphore()

    @pl.when(moves)
    def _():
        pl.semaphore_signal(barrier, inc=1, device_id=partner, device_id_type=MESH_ID)

    layer = others()
    line = line_of()
    for peer in layer + line:
        pl.semaphore_signal(barrier, inc=1, device_id=peer, device_id_type=MESH_ID)
    pl.semaphore_wait(barrier, len(layer + line) + moves.astype(jnp.int32))

    size = TILE // PIECES

    def part_of(piece):
        def produce(turn, to_y, to_c, to_x, out):
            at = quarter_of(to_y, to_c, to_x, piece // 2, piece % 2)

            def step(i, carry):
                columns = pl.ds(pl.multiple_of(i * TILE, TILE), TILE)
                out[:, columns] = dot_nt(d_qkv[at, :], w_qkv[columns, :]).astype(LOW)
                return carry

            lax.fori_loop(0, width // TILE, step, 0)

        return Scatter(produce, *scatter, part=piece, start=piece * size, size=size)

    sums = [part_of(piece) for piece in range(PIECES)]
    sums[0].begin()
    sums[0].relay()
    sums[1].begin()
    total, landed = scatter[2], scatter[4]
    terms[1] = mlp_term[...]
    terms[0] = jnp.zeros_like(mlp_term)
    pieces = [pl.ds(piece * size, size) for piece in range(PIECES)]
    trades = [remote(own.at[at], grad_low.at[at], send.at[k], recv.at[k], partner) for k, at in enumerate(pieces)]
    keeps = [pltpu.make_async_copy(own.at[at], grad_low.at[at], recv.at[k]) for k, at in enumerate(pieces)]
    fetch_x.wait()
    for piece in range(PIECES):
        sums[piece].arrive()

        def step(i, carry):
            here = pl.ds(pl.multiple_of(piece * size + i * CHUNK, CHUNK), CHUNK)
            back, products = norm_back(x_own[here, :].astype(jnp.float32), gain[...], summed(total, landed, here))
            own[here, :] = (d_resid[here, :] + back).astype(LOW)
            fold_rows(terms.at[0], products)
            return carry

        lax.fori_loop(0, size // CHUNK, step, 0)

        @pl.when(moves)
        def _():
            trades[piece].start()

        @pl.when(jnp.logical_not(moves))
        def _():
            keeps[piece].start()

        if piece + 1 < PIECES:
            sums[piece + 1].relay()
        if piece + 2 < PIECES:
            sums[piece + 2].begin()

    def columns_of(row, layers):
        return pl.ds(pl.multiple_of((4 * row) * HD, HD), layers * HD)

    spread = [
        remote(terms.at[:, :, columns_of(2 * peer[0] + peer[1], 4)], layer_terms.at[k], term_send.at[k], term_recv.at[k], peer)
        for k, peer in enumerate(layer)
    ]
    for copy in spread:
        copy.start()
    for copy in spread:
        copy.wait_recv()
    part[...] = sum((layer_terms[k] for k in range(7)), terms[:, :, columns_of(2 * y + c, 4)])
    lines = [
        remote(
            part.at[:, :, pl.ds(pl.multiple_of(peer[2] * HD, HD), HD)], column_terms.at[k], line_send.at[k], line_recv.at[k], peer
        )
        for k, peer in enumerate(line)
    ]
    for copy in lines:
        copy.start()
    for copy in lines:
        copy.wait_recv()
    gain_grads[...] = sum((column_terms[k] for k in range(3)), part[:, :, pl.ds(pl.multiple_of(z * HD, HD), HD)])
    for copy in spread + lines:
        copy.wait_send()
    for part_sum in sums:
        part_sum.finish()

    @pl.when(moves)
    def _():
        for copy in trades:
            copy.wait()

    @pl.when(jnp.logical_not(moves))
    def _():
        for copy in keeps:
            copy.wait()


def close_layer(d_qkv, w_qkv, x_whole, d_resid, gain, mlp_term):
    block, width = d_resid.shape
    return pl.pallas_call(
        close_layer_kernel,
        out_shape=(jax.ShapeDtypeStruct((block, width), LOW), jax.ShapeDtypeStruct((2, 8, width // 16), jnp.float32)),
        in_specs=[in_vmem(), in_vmem(), anywhere()] + [in_vmem()] * 3,
        out_specs=[anywhere(), in_vmem()],
        scratch_shapes=[
            pltpu.VMEM((block, width), LOW),
            pltpu.VMEM((2, 8, width), jnp.float32),
            pltpu.VMEM((7, 2, 8, width // 4), jnp.float32),
            pltpu.VMEM((2, 8, width // 4), jnp.float32),
            pltpu.VMEM((3, 2, 8, width // 16), jnp.float32),
        ]
        + scatter_scratch(width, PIECES)
        + [dma(PIECES), dma(PIECES), dma(7), dma(7), dma(3), dma(3), pltpu.VMEM((block, width), LOW), dma(1)],
        compiler_params=remote_params(4),
        cost_estimate=pl.CostEstimate(flops=0, bytes_accessed=350_000_000, transcendentals=0),
    )(d_qkv, w_qkv, x_whole, d_resid, gain, mlp_term)


def doc_start(ends, place):
    start = jnp.zeros_like(place)
    for k in range(8):
        start = jnp.where(ends[k] <= place, ends[k], start)
    return jnp.where(place < ends[7], start, LEN)


def sigmoid_of(raw):
    return pl.reciprocal(1.0 + jnp.exp2(math.log2(LEN) - raw * (math.log2(math.e) / math.sqrt(HD))), approx=True)


def tile_at(index):
    return pl.ds(pl.multiple_of(index * TILE, TILE), TILE)


def head_of(array, rows, part, head):
    first = (part * (array.shape[1] // 3) // HD + head) * HD
    return array[rows, first : first + HD]


def attend_kernel(ends, qkv, out, total):
    i = pl.program_id(0)
    heads = qkv.shape[1] // (3 * HD)
    total[...] = jnp.zeros_like(total)
    q_place = i * TILE + lax.broadcasted_iota(jnp.int32, (TILE, 1), 0)
    q_start = doc_start(ends, q_place)

    def tile(j, diagonal):
        k_place = j * TILE + lax.broadcasted_iota(jnp.int32, (1, TILE), 1)
        allowed = k_place >= q_start
        if diagonal:
            allowed = allowed & (k_place <= q_place)
        for head in range(heads):
            raw = dot_nt(head_of(qkv, tile_at(i), 0, head), head_of(qkv, tile_at(j), 1, head))
            weight = jnp.where(allowed, sigmoid_of(raw), 0.0).astype(LOW)
            total[head] += dot_wide(weight, head_of(qkv, tile_at(j), 2, head))

    def step(j, carry):
        tile(j, False)
        return carry

    lax.fori_loop(0, i, step, 0)
    tile(i, True)
    for head in range(heads):
        out[tile_at(i), head * HD : (head + 1) * HD] = total[head].astype(LOW)


def open_mlp_kernel(normed, w_gate, w_up, upstream, gate, up, hidden, upstream_whole, send, recv, local):
    i = pl.program_id(0)
    y, c, z, x = spot()
    steps = pl.num_programs(0)
    gather = Gather(lambda half: upstream.at[pl.ds(half * HALF, HALF)], upstream_whole, send, recv)
    keep = pltpu.make_async_copy(upstream, upstream_whole.at[place_of(y, c, x)], local.at[0])

    @pl.when(i == 0)
    def _():
        greet(near())
        gather.start(0)
        gather.start(1)
        keep.start()

    def step(n, carry):
        columns = pl.ds(pl.multiple_of(n * TILE, TILE), TILE)
        gate_part, up_part = dot_wide(normed[...], w_gate[:, columns]), dot_wide(normed[...], w_up[:, columns])
        gate[:, columns] = gate_part
        up[:, columns] = up_part
        hidden[:, columns] = (gate_part * jax.nn.sigmoid(gate_part) * up_part).astype(LOW)
        return carry

    lax.fori_loop(0, w_gate.shape[1] // TILE, step, 0)

    @pl.when(i == steps - 1)
    def _():
        for half in (0, 1):
            gather.pass_near(half)
        for half in (0, 1):
            gather.pass_far(half)
        gather.finish()
        keep.wait()


def open_mlp(normed, w_gate, w_up, upstream):
    places, width = normed.shape
    hidden = w_gate.shape[1]
    rows = lambda columns: pl.BlockSpec((TILE, columns), lambda i: (i, 0))
    whole = lambda array: pl.BlockSpec(array.shape, lambda i: (0, 0))
    return pl.pallas_call(
        open_mlp_kernel,
        out_shape=(
            jax.ShapeDtypeStruct((places, hidden), jnp.float32),
            jax.ShapeDtypeStruct((places, hidden), jnp.float32),
            jax.ShapeDtypeStruct((places, hidden), LOW),
            jax.ShapeDtypeStruct((places, width), LOW),
        ),
        grid=(places // TILE,),
        in_specs=[rows(width), whole(w_gate), whole(w_up), whole(upstream)],
        out_specs=[rows(hidden), rows(hidden), rows(hidden), anywhere()],
        scratch_shapes=[dma(GATHER_COPIES), dma(GATHER_COPIES), dma(1)],
        compiler_params=remote_params(5),
        cost_estimate=pl.CostEstimate(flops=0, bytes_accessed=250_000_000, transcendentals=0),
    )(normed, w_gate, w_up, upstream)


def out_turns():
    y, c, z, x = spot()
    owners = [((y, c, 2 * x + j // 2, j % 2), (z == 2 * x + j // 2) & (x == j % 2)) for j in range(4)]
    holders = [((y, c, j, z // 2), (z == j) & (x == z // 2)) for j in range(4)]
    return owners, holders


def attend_back_kernel(
    ends, qkv, grads, out_grad, mixed, out, out_parts, mixed_home, query_total, key_total, value_total, send, recv, *trade_parts
):
    j = pl.program_id(0)
    y, c, z, x = spot()
    heads = qkv.shape[1] // (3 * HD)
    shard = out_grad.shape[0] // 4
    owners, holders = out_turns()
    trade = Trade(
        [mixed.at[pl.ds(half * HALF, HALF)] for half in (0, 1)], lambda half, at: mixed_home.at[pl.ds(half * HALF, HALF)], *trade_parts
    )

    def to_owner(turn):
        return remote(out_grad.at[pl.ds(turn * shard, shard)], out_parts.at[z], send.at[turn], recv.at[z], owners[turn][0])

    def to_self(turn):
        return pltpu.make_async_copy(out_grad.at[pl.ds(turn * shard, shard)], out_parts.at[z], recv.at[z])

    @pl.when(j == 0)
    def _():
        query_total[...] = jnp.zeros_like(query_total)
        barrier = pltpu.get_barrier_semaphore()
        for peer, here in holders:

            @pl.when(jnp.logical_not(here))
            def _():
                pl.semaphore_signal(barrier, inc=1, device_id=peer, device_id_type=MESH_ID)

        pl.semaphore_wait(barrier, 4 - (x == z // 2).astype(jnp.int32) + trade.greet(barrier, False))
        for half in (0, 1):
            trade.start(half)
        for turn in range(4):

            @pl.when(jnp.logical_not(owners[turn][1]))
            def _():
                to_owner(turn).start()

            @pl.when(owners[turn][1])
            def _():
                to_self(turn).start()

    key_total[...] = jnp.zeros_like(key_total)
    value_total[...] = jnp.zeros_like(value_total)
    here = tile_at(j)
    k_place = j * TILE + lax.broadcasted_iota(jnp.int32, (TILE, 1), 0)
    turned = [head_of(qkv, here, 1, head).T for head in range(heads)]

    def tile(i, diagonal):
        q_place = i * TILE + lax.broadcasted_iota(jnp.int32, (1, TILE), 1)
        allowed = k_place >= doc_start(ends, q_place)
        if diagonal:
            allowed = allowed & (k_place <= q_place)
        for head in range(heads):
            query, grad = head_of(qkv, tile_at(i), 0, head), grads[tile_at(i), head * HD : (head + 1) * HD]
            sig = jnp.where(allowed, sigmoid_of(dot_nt(head_of(qkv, here, 1, head), query)), 0.0)
            value_total[head] += dot_wide(sig.astype(LOW), grad)
            d_score = (dot_nt(head_of(qkv, here, 2, head), grad) * (sig * (1.0 - sig))).astype(LOW)
            key_total[head] += dot_wide(d_score, query)
            query_total[head, :, tile_at(i)] += dot_wide(turned[head], d_score)

    def step(i, carry):
        tile(i, False)
        return carry

    tile(j, True)
    lax.fori_loop(j + 1, LEN // TILE, step, 0)
    scale = 1.0 / math.sqrt(HD)
    for head in range(heads):
        first = head * HD
        out[here, heads * HD + first : (heads + 1) * HD + first] = (key_total[head] * scale).astype(LOW)
        out[here, 2 * heads * HD + first : (2 * heads + 1) * HD + first] = value_total[head].astype(LOW)
        out[here, first : first + HD] = (query_total[head, :, here] * scale).T.astype(LOW)

    @pl.when(j == LEN // TILE - 1)
    def _():
        for turn in range(4):

            @pl.when(jnp.logical_not(owners[turn][1]))
            def _():
                to_owner(turn).wait_send()

            @pl.when(jnp.logical_not(holders[turn][1]))
            def _():
                landed = out_parts.at[turn]
                remote(landed, landed, send.at[turn], recv.at[turn], holders[turn][0]).wait_recv()

            @pl.when(owners[turn][1])
            def _():
                to_self(turn).wait()

        for half in (0, 1):
            trade.arrive(half)
        trade.finish()

    @pl.when(j == 1)
    def _():
        for half in (0, 1):
            trade.forward(half)


def back_mlp_kernel(upstream, w_down, gate, up, d_gate, d_up):
    def step(n, carry):
        columns = pl.ds(pl.multiple_of(n * TILE, TILE), TILE)
        d_hidden = dot_nt(upstream[...], w_down[columns, :])
        d_gate[:, columns], d_up[:, columns] = gate_backward(
            d_hidden, gate[:, columns], up[:, columns], jax.nn.sigmoid(gate[:, columns])
        )
        return carry

    lax.fori_loop(0, gate.shape[1] // TILE, step, 0, unroll=2)


def back_mlp(upstream, w_down, gate, up):
    places, width = upstream.shape
    hidden = gate.shape[1]
    rows = lambda size: pl.BlockSpec((TILE, size), lambda i: (i, 0))
    return pl.pallas_call(
        back_mlp_kernel,
        out_shape=(jax.ShapeDtypeStruct((places, hidden), LOW), jax.ShapeDtypeStruct((places, hidden), LOW)),
        grid=(places // TILE,),
        in_specs=[rows(width), pl.BlockSpec(w_down.shape, lambda i: (0, 0)), rows(hidden), rows(hidden)],
        out_specs=[rows(hidden), rows(hidden)],
        compiler_params=pltpu.CompilerParams(vmem_limit_bytes=VMEM_LIMIT),
        cost_estimate=pl.CostEstimate(flops=0, bytes_accessed=90_000_000, transcendentals=0),
    )(upstream, w_down, gate, up)


def attend(ends, qkv):
    places, width = qkv.shape
    heads = width // (3 * HD)
    whole = lambda columns: pl.BlockSpec((places, columns), lambda i: (0, 0))
    return pl.pallas_call(
        attend_kernel,
        out_shape=jax.ShapeDtypeStruct((places, width // 3), LOW),
        grid=(places // TILE,),
        in_specs=[pl.BlockSpec(memory_space=pltpu.SMEM), whole(width)],
        out_specs=whole(width // 3),
        scratch_shapes=[pltpu.VMEM((heads, TILE, HD), jnp.float32)],
        compiler_params=pltpu.CompilerParams(vmem_limit_bytes=VMEM_LIMIT),
        cost_estimate=pl.CostEstimate(flops=0, bytes_accessed=150_000_000, transcendentals=0),
    )(ends, qkv)


def attend_back(ends, qkv, grads, out_grad, mixed):
    places, width = qkv.shape
    heads = width // (3 * HD)
    whole = lambda columns: pl.BlockSpec((places, columns), lambda j: (0, 0))
    return pl.pallas_call(
        attend_back_kernel,
        out_shape=(
            jax.ShapeDtypeStruct((places, width), LOW),
            jax.ShapeDtypeStruct((4, out_grad.shape[0] // 4, out_grad.shape[1]), LOW),
            jax.ShapeDtypeStruct(mixed.shape, LOW),
        ),
        grid=(places // TILE,),
        in_specs=[pl.BlockSpec(memory_space=pltpu.SMEM), whole(width), whole(width // 3), anywhere(), pl.BlockSpec(mixed.shape, lambda j: (0, 0))],
        out_specs=[whole(width), anywhere(), anywhere()],
        scratch_shapes=[
            pltpu.VMEM((heads, HD, places), jnp.float32),
            pltpu.VMEM((heads, TILE, HD), jnp.float32),
            pltpu.VMEM((heads, TILE, HD), jnp.float32),
            dma(4),
            dma(4),
            *trade_scratch(2, HALF, mixed.shape[1]),
        ],
        compiler_params=remote_params(6),
        cost_estimate=pl.CostEstimate(flops=0, bytes_accessed=300_000_000, transcendentals=0),
    )(ends, qkv, grads, out_grad, mixed)


LAYER = ("y", "c", "x")
PLACES = ("c", "y", "x")
ALL = ("y", "c", "z", "x")


def trade(part):
    pairs = []
    for y in range(2):
        for c in range(2):
            for z in range(4):
                for x in range(2):
                    pairs.append((((y * 2 + c) * 4 + z) * 2 + x, (((z % 2) * 2 + z // 2) * 4 + 2 * c + y) * 2 + x))
    return lax.ppermute(part, ALL, pairs)


def after(first, then):
    return lax.optimization_barrier((first, then))[1]


def body_layers(
    tokens, lengths, cotangent, w_query, w_key, w_value, w_out, w_gate, w_up, w_down, gain_attn, gain_mlp
):
    rows_here, block, width = tokens.shape
    members = lax.axis_size(LAYER)
    layers = lax.axis_size("z")
    shard = w_query.shape[0]
    owned = width // members
    facts = jnp.zeros((8, 2 * shard), jnp.float32)
    facts = facts.at[0, :shard].set(gain_attn.astype(jnp.float32)).at[1, :shard].set(gain_mlp.astype(jnp.float32))
    facts = facts.at[2, : lengths.shape[1]].set(lengths[0].astype(jnp.float32))
    layer_x, w_qkv, facts = begin(tokens.reshape(block, width), w_query, w_key, w_value, facts)
    full_gain_attn, full_gain_mlp = facts[:, :, :, 0, :shard].reshape(1, width), facts[:, :, :, 1, :shard].reshape(1, width)
    layer = lax.axis_index("z")
    own_lengths = facts[:, 0, 0, 2, : lengths.shape[1]].reshape(2, 2, -1)
    own_lengths = lax.dynamic_slice(own_lengths, (layer % 2, layer // 2, 0), (1, 1, own_lengths.shape[2]))[0, 0]
    ends = jnp.cumsum(own_lengths.astype(jnp.int32))
    layer_normed = norm_forward(layer_x.astype(jnp.float32), full_gain_attn)[0].astype(LOW)
    line = lax.all_gather(after(facts, w_out), "z", axis=0)
    qkv = dot_wide(layer_normed, w_qkv).astype(LOW)
    here = lax.axis_index("x")
    line = after(qkv, line)
    to_neighbour = lax.dynamic_slice_in_dim(line, 2 * (1 - here), 2, 0)
    mine, theirs = lax.dynamic_slice_in_dim(line, 2 * here, 2, 0), lax.ppermute(to_neighbour, "x", [(0, 1), (1, 0)])
    w_out_own = jnp.stack((jnp.where(here == 0, mine, theirs), jnp.where(here == 0, theirs, mine)), axis=1)
    w_out_own = w_out_own.reshape(owned, width)
    upstream = trade(after(facts, cotangent)).reshape(block, width)
    attended = attend(ends, after(to_neighbour, qkv))
    resid, layer_mlp, own_gate, own_up = close_attention(after(upstream, attended), w_out_own, layer_x, full_gain_mlp, w_gate, w_up)

    own_down = lax.all_gather(after(resid, w_down), "z", axis=0, tiled=True)
    gate, up_part, hidden, layer_upstream = open_mlp(layer_mlp, own_gate, own_up, upstream)
    part = dot_wide(hidden, own_down).astype(LOW)
    mixed_sum = lax.psum_scatter(part, PLACES, scatter_dimension=0, tiled=True)
    down_term = contract_rows(after(part, hidden), layer_upstream).astype(LOW)
    down_rows = w_down.shape[0]
    down_parts = []
    for up in range(1, 4):
        layers_pairs = [(at, (at + up) % 4) for at in range(4)]
        slab = lax.dynamic_slice_in_dim(down_term, (layer + up) % 4 * down_rows, down_rows, 0)
        down_parts.append(lax.ppermute(slab, "z", layers_pairs))
    d_gate, d_up = back_mlp(after(down_term, layer_upstream), own_down, gate, up_part)
    gate_term, up_term = contract_rows(layer_mlp, d_gate).astype(LOW), contract_rows(layer_mlp, d_up).astype(LOW)
    d_resid, gain_mlp_term, layer_d_resid, *parts = close_mlp(
        after((mixed_sum, *down_parts), d_gate), d_up, own_gate, own_up, resid, upstream, full_gain_mlp, gate_term, up_term
    )

    def own_part(whole, near_part, cross):
        own = lax.dynamic_slice_in_dim(whole, layer * cross.shape[1], cross.shape[1], 1)
        return own.astype(jnp.float32) + near_part.astype(jnp.float32) + cross.astype(jnp.float32)

    mixed = (resid + after(layer_d_resid, mixed_sum).astype(jnp.float32)).astype(LOW)
    grad_down = lax.dynamic_slice_in_dim(down_term, layer * down_rows, down_rows, 0).astype(jnp.float32)
    grad_down = grad_down + sum(slab.astype(jnp.float32) for slab in down_parts)

    out_term = contract_rows(attended, layer_d_resid).astype(LOW)
    d_attended = contract_cols(layer_d_resid, w_out_own).astype(LOW)
    d_qkv, out_parts, mixed = attend_back(ends, qkv, d_attended, out_term, mixed)
    mixed = mixed.reshape(rows_here, block, width)
    grad_gate, grad_up = own_part(gate_term, *parts[1:3]), own_part(up_term, *parts[4:6])
    grad_out = jnp.sum(out_parts.astype(jnp.float32), axis=0)
    qkv_term = contract_rows(layer_normed, d_qkv).astype(LOW)
    grad_low, gain_grads = close_layer(
        after(qkv_term, d_qkv), w_qkv, layer_x, d_resid, full_gain_attn, gain_mlp_term
    )
    grad_tokens = grad_low.astype(jnp.float32).reshape(rows_here, block, width)

    qkv_term = qkv_term.reshape(4, layers, 2 * shard, 3 * owned).transpose(1, 0, 2, 3)
    qkv_term = qkv_term.reshape(layers * members * shard, 3 * owned)
    qkv_term = lax.psum_scatter(qkv_term, "z", scatter_dimension=0, tiled=True)
    qkv_term = lax.all_to_all(qkv_term.reshape(members, shard, 3 * owned), LAYER, 0, 0)
    qkv_term = qkv_term.reshape(members, shard, 3, owned).transpose(2, 1, 0, 3).astype(jnp.float32)
    grad_query, grad_key, grad_value = qkv_term.reshape(3, shard, width)
    gain_grads = lax.dynamic_index_in_dim(jnp.sum(gain_grads, axis=1).reshape(2, 2, shard), lax.axis_index("x"), 1, False)
    return (
        mixed,
        grad_tokens,
        grad_query,
        grad_key,
        grad_value,
        grad_out,
        grad_gate,
        grad_up,
        grad_down,
        gain_grads[0],
        gain_grads[1],
    )


def body_any(
    tokens,
    lengths,
    cotangent,
    w_query,
    w_key,
    w_value,
    w_out,
    w_gate,
    w_up,
    w_down,
    gain_attn,
    gain_mlp,
):
    rows_here, block, width = tokens.shape
    count = rows_here * block
    scale = 1.0 / math.sqrt(HD)
    kv_place = lax.axis_index("kv")
    key_places = kv_place * block + jnp.arange(block, dtype=jnp.int32)
    attn_set = (
        lax.all_gather(w_query, ("row", "kv"), axis=0, tiled=True),
        lax.all_gather(w_key, ("row", "kv"), axis=0, tiled=True),
        lax.all_gather(w_value, ("row", "kv"), axis=0, tiled=True),
        lax.all_gather(w_out, ("row", "kv"), axis=0, tiled=True),
        lax.all_gather(gain_attn, ("row", "kv"), axis=0, tiled=True),
        lax.all_gather(gain_mlp, ("row", "kv"), axis=0, tiled=True),
    )
    full_query, full_key, full_value, full_out, full_gain_attn, full_gain_mlp = attn_set
    flat = tokens.reshape(count, width).astype(jnp.float32)
    normed_attn, inverse_attn = norm_forward(flat, full_gain_attn)
    normed_attn_low = normed_attn.astype(jnp.bfloat16)
    query_low = jnp.dot(normed_attn_low, full_query, preferred_element_type=jnp.float32).astype(
        jnp.bfloat16
    )
    key_low = jnp.dot(normed_attn_low, full_key, preferred_element_type=jnp.float32).astype(
        jnp.bfloat16
    )
    value_low = jnp.dot(normed_attn_low, full_value, preferred_element_type=jnp.float32).astype(
        jnp.bfloat16
    )
    key_heads = key_low.reshape(rows_here, block, H, HD)
    value_heads = value_low.reshape(rows_here, block, H, HD)
    segment, valid = segment_table(lengths)
    key_segment = lax.dynamic_slice_in_dim(segment, kv_place * block, block, 1)
    key_valid = lax.dynamic_slice_in_dim(valid, kv_place * block, block, 1)
    queries_all = lax.all_gather(
        query_low.reshape(rows_here, block, width), "kv", axis=1, tiled=True
    )
    which = 0
    query_rows = queries_all[which]
    query_segment = segment[which]
    sigmoid_part, allowed = score_block(
        query_rows,
        key_heads[which],
        query_segment,
        key_segment[which],
        key_valid[which],
        jnp.int32(0),
        key_places,
    )
    weight = (sigmoid_part * allowed).astype(jnp.bfloat16)
    summed = jnp.einsum(
        "hqk,khd->qhd", weight, value_heads[which], preferred_element_type=jnp.float32
    )
    pieces = [
        lax.psum_scatter(
            summed.reshape(lax.axis_size("kv") * block, width).astype(jnp.bfloat16),
            "kv",
            scatter_dimension=0,
            tiled=True,
        ).astype(jnp.float32)
    ]
    attended_low = jnp.stack(pieces).reshape(count, width).astype(jnp.bfloat16)
    resid = flat + jnp.dot(attended_low, full_out, preferred_element_type=jnp.float32)
    normed_mlp, inverse_mlp = norm_forward(resid, full_gain_mlp)
    normed_mlp_low = normed_mlp.astype(jnp.bfloat16)
    upstream_low = cotangent.reshape(count, width)
    upstream = upstream_low.astype(jnp.float32)
    slice_gate, slice_up, slice_down = (
        lax.all_gather(w_gate, "row", axis=1, tiled=True),
        lax.all_gather(w_up, "row", axis=1, tiled=True),
        lax.all_gather(w_down, "row", axis=0, tiled=True),
    )
    row_normed, row_upstream = (
        lax.all_gather(normed_mlp_low.reshape(rows_here, block, width), "kv", axis=1, tiled=True),
        lax.all_gather(cotangent, "kv", axis=1, tiled=True),
    )
    normed_rows = row_normed.reshape(rows_here * LEN, width)
    upstream_rows = row_upstream.reshape(rows_here * LEN, width)
    gate = jnp.dot(normed_rows, slice_gate, preferred_element_type=jnp.float32)
    up_part = jnp.dot(normed_rows, slice_up, preferred_element_type=jnp.float32)
    sigmoid_gate = jax.nn.sigmoid(gate)
    hidden_low = (gate * sigmoid_gate * up_part).astype(jnp.bfloat16)
    hidden_rows = hidden_low.reshape(rows_here, LEN, hidden_low.shape[1])
    which = 0
    hidden_part = hidden_rows[which]
    outputs = [
        lax.psum_scatter(
            jnp.dot(hidden_part, slice_down, preferred_element_type=jnp.float32).astype(
                jnp.bfloat16
            ),
            "kv",
            scatter_dimension=0,
            tiled=True,
        ).astype(jnp.float32)
    ]
    result = resid + jnp.stack(outputs).reshape(count, width)
    d_hidden = contract_cols(upstream_rows, slice_down)
    d_gate, d_up = gate_backward(d_hidden, gate, up_part, sigmoid_gate)
    partial_normed = contract_cols(d_gate, slice_gate) + contract_cols(d_up, slice_up)
    d_normed_mlp = (
        lax.psum_scatter(
            partial_normed.reshape(rows_here, LEN, width).astype(jnp.bfloat16),
            "kv",
            scatter_dimension=1,
            tiled=True,
        )
        .astype(jnp.float32)
        .reshape(count, width)
    )
    grad_gate, grad_up, grad_down = (
        lax.psum_scatter(
            contract_rows(normed_rows, d_gate).astype(jnp.bfloat16),
            "row",
            scatter_dimension=1,
            tiled=True,
        ).astype(jnp.float32),
        lax.psum_scatter(
            contract_rows(normed_rows, d_up).astype(jnp.bfloat16),
            "row",
            scatter_dimension=1,
            tiled=True,
        ).astype(jnp.float32),
        lax.psum_scatter(
            contract_rows(hidden_low, upstream_rows).astype(jnp.bfloat16),
            "row",
            scatter_dimension=0,
            tiled=True,
        ).astype(jnp.float32),
    )
    mixed = result.astype(jnp.bfloat16).reshape(rows_here, block, width)
    back_mlp, gain_mlp_term = norm_backward(resid, inverse_mlp, full_gain_mlp, d_normed_mlp)
    d_resid = upstream + back_mlp
    d_resid_low = d_resid.astype(jnp.bfloat16)
    d_attended = contract_cols(d_resid_low, full_out).astype(jnp.bfloat16)
    grads_all = lax.all_gather(
        d_attended.reshape(rows_here, block, width), "kv", axis=1, tiled=True
    )
    query_block = min(512, LEN)
    block_count = LEN // query_block
    which = 0

    def sweep(carry, index, which=which):
        key_total, value_total = carry
        start = index * query_block
        query_rows = lax.dynamic_slice_in_dim(queries_all[which], start, query_block, 0)
        grad_rows = lax.dynamic_slice_in_dim(grads_all[which], start, query_block, 0)
        query_segment = lax.dynamic_slice_in_dim(segment[which], start, query_block, 0)
        sigmoid_part, allowed = score_block(
            query_rows,
            key_heads[which],
            query_segment,
            key_segment[which],
            key_valid[which],
            start,
            key_places,
        )
        weight = (sigmoid_part * allowed).astype(jnp.bfloat16)
        grad_heads = grad_rows.reshape(query_block, H, HD)
        value_total = value_total + jnp.einsum(
            "hqk,qhd->khd", weight, grad_heads, preferred_element_type=jnp.float32
        )
        d_weight = jnp.einsum(
            "qhd,khd->hqk", grad_heads, value_heads[which], preferred_element_type=jnp.float32
        )
        d_score = (d_weight * sigmoid_part * (1.0 - sigmoid_part) * allowed).astype(jnp.bfloat16)
        query_part = (
            jnp.einsum(
                "hqk,khd->qhd", d_score, key_heads[which], preferred_element_type=jnp.float32
            )
            * scale
        )
        key_total = (
            key_total
            + jnp.einsum(
                "hqk,qhd->khd",
                d_score,
                query_rows.reshape(query_block, H, HD),
                preferred_element_type=jnp.float32,
            )
            * scale
        )
        return ((key_total, value_total), query_part.reshape(query_block, width))

    zeros = jnp.zeros((block, H, HD), jnp.float32)
    totals, query_parts = lax.scan(sweep, (zeros, zeros), jnp.arange(block_count, dtype=jnp.int32))
    query_terms = [query_parts.reshape(LEN, width)]
    key_grads = [totals[0].reshape(block, width)]
    value_grads = [totals[1].reshape(block, width)]
    query_local = lax.psum_scatter(
        jnp.stack(query_terms).astype(jnp.bfloat16), "kv", scatter_dimension=1, tiled=True
    ).astype(jnp.float32)
    d_query_low = query_local.reshape(count, width).astype(jnp.bfloat16)
    d_key_low = jnp.stack(key_grads).reshape(count, width).astype(jnp.bfloat16)
    d_value_low = jnp.stack(value_grads).reshape(count, width).astype(jnp.bfloat16)
    d_normed_attn = (
        contract_cols(d_query_low, full_query)
        + contract_cols(d_key_low, full_key)
        + contract_cols(d_value_low, full_value)
    )
    back_attn, gain_attn_term = norm_backward(flat, inverse_attn, full_gain_attn, d_normed_attn)
    grad_tokens = (d_resid + back_attn).reshape(rows_here, block, width)
    projected_low = jnp.concatenate((d_query_low, d_key_low, d_value_low), axis=1)
    grad_projections = lax.psum_scatter(
        contract_rows(normed_attn_low, projected_low),
        ("row", "kv"),
        scatter_dimension=0,
        tiled=True,
    )
    out_term = contract_rows(attended_low, d_resid_low)
    grad_out, grad_gain_attn, grad_gain_mlp = (
        lax.psum_scatter(out_term, ("row", "kv"), scatter_dimension=0, tiled=True),
        lax.psum_scatter(gain_attn_term, ("row", "kv"), scatter_dimension=0, tiled=True),
        lax.psum_scatter(gain_mlp_term, ("row", "kv"), scatter_dimension=0, tiled=True),
    )
    grad_query = grad_projections[:, :width]
    grad_key = grad_projections[:, width : 2 * width]
    grad_value = grad_projections[:, 2 * width :]
    return (
        mixed,
        grad_tokens,
        grad_query,
        grad_key,
        grad_value,
        grad_out,
        grad_gate,
        grad_up,
        grad_down,
        grad_gain_attn,
        grad_gain_mlp,
    )


def solution(mesh):
    rows, columns = mesh.shape["row"], mesh.shape["kv"]
    if rows == 4 and columns == 2 * rows:
        mesh = Mesh(mesh.devices.reshape(2, 2, rows, 2), ("y", "c", "z", "x"))
        row, kv, run = ("y", "c"), ("z", "x"), body_layers
    else:
        row, kv, run = "row", "kv", body_any
    both = ("y", "c", "z", "x") if run is body_layers else ("row", "kv")
    tall, wide, flat = P(both, None), P(None, both), P(both)
    tokens = P(row, kv, None)
    return jax.shard_map(
        run,
        mesh=mesh,
        in_specs=(tokens, P(row, None), tokens, tall, tall, tall, tall, wide, wide, tall, flat, flat),
        out_specs=(tokens, tokens, tall, tall, tall, tall, wide, wide, tall, flat, flat),
        check_vma=False,
    )
```

```python
import functools
import math

import jax
import jax.numpy as jnp
from jax import lax
from jax.experimental import pallas as pl
from jax.experimental.pallas import tpu as pltpu
from jax.sharding import Mesh, PartitionSpec as P

H = 16
HD = 128
LEN = 4096


EPSILON = 1e-05


def contract_rows(left, right):
    return lax.dot_general(
        left, right, (((0,), (0,)), ((), ())), preferred_element_type=jnp.float32
    )


def contract_cols(left, right):
    return lax.dot_general(
        left, right, (((1,), (1,)), ((), ())), preferred_element_type=jnp.float32
    )


def norm_forward(value, gain):
    inverse = lax.rsqrt(jnp.mean(value * value, axis=-1, keepdims=True) + EPSILON)
    return (value * inverse * gain.astype(jnp.float32), inverse)


def norm_backward(value, inverse, gain, upstream):
    scaled = upstream * gain.astype(jnp.float32)
    inner = jnp.mean(scaled * value, axis=-1, keepdims=True)
    back = inverse * scaled - value * (inverse * inverse * inverse) * inner
    gain_term = jnp.sum(upstream * value * inverse, axis=0)
    return (back, gain_term)


def segment_table(lengths):
    ends = jnp.cumsum(lengths, axis=-1)
    places = jnp.arange(LEN, dtype=jnp.int32)
    segment = jnp.sum((ends[:, None, :] <= places[None, :, None]).astype(jnp.int32), axis=-1)
    valid = places[None, :] < ends[:, -1:]
    return (segment, valid)


def score_block(
    query_rows, key_heads, query_segment, key_segment, key_valid, query_start, key_places
):
    count = query_rows.shape[0]
    query_heads = query_rows.reshape(count, H, HD)
    raw = jnp.einsum("qhd,khd->hqk", query_heads, key_heads, preferred_element_type=jnp.float32)
    scores = raw * (1.0 / math.sqrt(HD)) - math.log(LEN)
    places = query_start + jnp.arange(count, dtype=jnp.int32)
    allowed = (
        (key_places[None, :] <= places[:, None])
        & (key_segment[None, :] == query_segment[:, None])
        & key_valid[None, :]
    )
    return (jax.nn.sigmoid(scores), allowed.astype(jnp.float32)[None])


def gate_backward(d_hidden, gate, up_part, sigmoid_gate):
    d_gate = (d_hidden * up_part * sigmoid_gate * (1.0 + gate * (1.0 - sigmoid_gate))).astype(
        jnp.bfloat16
    )
    d_up = (d_hidden * gate * sigmoid_gate).astype(jnp.bfloat16)
    return (d_gate, d_up)


TILE = 512
LOW = jnp.bfloat16
VMEM_LIMIT = 60 * 1024 * 1024


def dot_nt(left, right):
    return lax.dot_general(left, right, (((1,), (1,)), ((), ())), preferred_element_type=jnp.float32)


def dot_wide(left, right):
    return jnp.dot(left, right, preferred_element_type=jnp.float32)


HALF = TILE // 2
PIECES = 4
CHUNK = 32
MESH_ID = pl.DeviceIdType.MESH


def flip(bit, by):
    return bit + by - 2 * bit * by


def spot():
    return tuple(lax.axis_index(name) for name in ("y", "c", "z", "x"))


def near():
    y, c, z, x = spot()
    return (y, c, z, 1 - x), (1 - y, c, z, x), (y, 1 - c, z, x)


def partner_of(y, c, z, x):
    return lax.rem(z, 2), z // 2, 2 * c + y, x


def place_of(y, c, x, half=None):
    first = (4 * c + 2 * y + x) * TILE
    if half is None:
        return pl.ds(pl.multiple_of(first, TILE), TILE)
    return pl.ds(pl.multiple_of(first + half * HALF, HALF), HALF)


def quarter_of(y, c, x, half, quarter):
    return pl.ds(pl.multiple_of((4 * c + 2 * y + x) * TILE + half * HALF + quarter * (HALF // 2), HALF // 2), HALF // 2)


def remote(src, dst, send, recv, peer):
    return pltpu.make_async_remote_copy(
        src_ref=src, dst_ref=dst, send_sem=send, recv_sem=recv, device_id=peer, device_id_type=MESH_ID
    )


def greet(peers):
    barrier = pltpu.get_barrier_semaphore()
    for peer in peers:
        pl.semaphore_signal(barrier, inc=1, device_id=peer, device_id_type=MESH_ID)
    pl.semaphore_wait(barrier, len(peers))


class Gather:
    def __init__(self, own, whole, send, recv):
        y, c, z, x = spot()
        across_x, across_y, core = near()

        def passed(k, at, peer):
            return remote(whole.at[at], whole.at[at], send.at[k], recv.at[k], peer)

        self.halves = []
        for half in (0, 1):
            k, at = 9 * half, place_of(y, c, x, half)
            mine = [
                remote(own(half), whole.at[at], send.at[k + m], recv.at[k + m], peer)
                for m, peer in enumerate((across_x, across_y, core))
            ]
            held_x, held_y = (y, c, 1 - x), (1 - y, c, x)
            far = (1 - y, c, 1 - x)
            self.halves.append(
                (
                    mine,
                    passed(k + 3, quarter_of(*held_x, half, 0), across_y),
                    passed(k + 4, quarter_of(*held_y, half, 1), across_x),
                    [passed(k + 5, place_of(*held_x, half), core), passed(k + 6, place_of(*held_y, half), core)],
                    [passed(k + 7 + q, quarter_of(*far, half, q), core) for q in (0, 1)],
                )
            )

    def start(self, half):
        for copy in self.halves[half][0]:
            copy.start()

    def pass_near(self, half):
        mine, over_y, over_x, from_near, from_far = self.halves[half]
        mine[0].wait_recv()
        over_y.start()
        from_near[0].start()
        mine[1].wait_recv()
        over_x.start()
        from_near[1].start()

    def pass_far(self, half):
        mine, over_y, over_x, from_near, from_far = self.halves[half]
        over_y.wait_recv()
        from_far[0].start()
        over_x.wait_recv()
        from_far[1].start()

    def finish(self):
        for mine, over_y, over_x, from_near, from_far in self.halves:
            for copy in [mine[2]] + from_near + from_far:
                copy.wait_recv()
            for copy in mine + [over_y, over_x] + from_near + from_far:
                copy.wait_send()


GATHER_COPIES = 18


class GatherWhole:
    def __init__(self, own, whole, send, recv):
        y, c, z, x = spot()
        across_x, across_y, core = near()

        def from_own(k, half, peer):
            return remote(own(half), whole.at[place_of(y, c, x, half)], send.at[k], recv.at[k], peer)

        def passed(k, at, peer):
            return remote(whole.at[at], whole.at[at], send.at[k], recv.at[k], peer)

        self.mine = [
            [from_own(0, 0, across_x), from_own(1, 0, across_y), from_own(2, 0, core)],
            [from_own(3, 1, across_x), from_own(4, 1, across_y), from_own(5, 1, core)],
        ]
        held_x = [place_of(y, c, 1 - x, half) for half in (0, 1)]
        held_y = [place_of(1 - y, c, x, half) for half in (0, 1)]
        far = [place_of(1 - y, c, 1 - x, half) for half in (0, 1)]
        self.over_y, self.over_x = passed(6, held_x[0], across_y), passed(7, held_y[1], across_x)
        self.core_x = [passed(8 + half, held_x[half], core) for half in (0, 1)]
        self.core_y = [passed(10 + half, held_y[half], core) for half in (0, 1)]
        self.core_far = [passed(12 + half, far[half], core) for half in (0, 1)]

    def start(self, half):
        for copy in self.mine[half]:
            copy.start()

    def pass_first(self):
        self.mine[0][0].wait_recv()
        self.over_y.start()
        self.core_x[0].start()
        self.mine[0][1].wait_recv()
        self.core_y[0].start()

    def pass_second(self):
        self.mine[1][1].wait_recv()
        self.over_x.start()
        self.core_y[1].start()
        self.mine[1][0].wait_recv()
        self.core_x[1].start()

    def pass_far(self):
        self.over_y.wait_recv()
        self.core_far[0].start()
        self.over_x.wait_recv()
        self.core_far[1].start()

    def finish(self):
        from_core = [self.mine[0][2], self.mine[1][2]] + self.core_x + self.core_y + self.core_far
        for copy in from_core:
            copy.wait_recv()
        for copy in self.mine[0] + self.mine[1] + [self.over_y, self.over_x] + self.core_x + self.core_y + self.core_far:
            copy.wait_send()


class Trade:
    def __init__(self, sources, dst, held, send, recv, held_recv, pass_send, detour=True):
        y, c, z, x = spot()
        self.detour = detour
        across_y = (1 - y, c, z, x)
        self.moves = z != 2 * c + y
        self.away = (y == c) & (z == 1 + y)
        self.straight = self.moves & jnp.logical_not(self.away) if detour else self.moves
        self.passes = (1 - y == c) & (z == 2 - y)
        partner = partner_of(y, c, z, x)
        comes_by = ((partner[0] == partner[1]) & (partner[2] == 1 + partner[0])).astype(jnp.int32)
        self.sender = (flip(partner[0], comes_by), partner[1], partner[2], x) if detour else partner
        self.across_y = across_y
        target = partner_of(*across_y)
        self.direct, self.keep, self.out, self.onward = [], [], [], []
        for h, source in enumerate(sources):
            self.direct.append(remote(source, dst(h, partner), send.at[h], recv.at[h], partner))
            self.keep.append(pltpu.make_async_copy(source, dst(h, (y, c, z, x)), recv.at[h]))
            self.out.append(remote(source, held.at[h], send.at[h], held_recv.at[h], across_y))
            self.onward.append(remote(held.at[h], dst(h, target), pass_send.at[h], recv.at[h], target))

    def greet(self, barrier, neighbours_greet):
        @pl.when(self.moves)
        def _():
            pl.semaphore_signal(barrier, inc=1, device_id=self.sender, device_id_type=MESH_ID)

        count = self.straight.astype(jnp.int32)
        if not self.detour:
            return count
        count = count + self.passes.astype(jnp.int32)
        if not neighbours_greet:

            @pl.when(self.passes)
            def _():
                pl.semaphore_signal(barrier, inc=1, device_id=self.across_y, device_id_type=MESH_ID)

            count = count + self.away.astype(jnp.int32)
        return count

    def start(self, h):
        @pl.when(self.straight)
        def _():
            self.direct[h].start()

        if self.detour:

            @pl.when(self.away)
            def _():
                self.out[h].start()

        @pl.when(jnp.logical_not(self.moves))
        def _():
            self.keep[h].start()

    def wait_sent(self, h):
        @pl.when(self.straight)
        def _():
            self.direct[h].wait_send()

        if self.detour:

            @pl.when(self.away)
            def _():
                self.out[h].wait_send()

    def forward(self, h):
        if self.detour:

            @pl.when(self.passes)
            def _():
                self.out[h].wait_recv()
                self.onward[h].start()

    def arrive(self, h):
        @pl.when(self.moves)
        def _():
            self.direct[h].wait_recv()

        @pl.when(jnp.logical_not(self.moves))
        def _():
            self.keep[h].wait()

    def finish(self, first=0):
        for h in range(len(self.direct)):
            if h >= first:
                self.wait_sent(h)

            if self.detour:

                @pl.when(self.passes)
                def _():
                    self.onward[h].wait_send()


def trade_scratch(pieces, rows, width):
    return [pltpu.VMEM((pieces, rows, width), LOW)] + [pltpu.SemaphoreType.DMA((pieces,)) for _ in range(4)]


class Chain:
    def __init__(self, own, slab, sems, index):
        self.own, self.slab, self.sems, self.index = own, slab, sems, index
        self.last = lax.axis_size("z") - 1

    def move(self, which, h, source, layer, to):
        y, c, z, x = spot()
        return remote(
            source, self.slab(layer), self.sems[2 * which].at[self.index, h], self.sems[2 * which + 1].at[self.index, h], (y, c, to, x)
        )

    def up(self, h):
        z = lax.axis_index("z")
        return self.move(0, h, self.own if h == 0 else self.slab(z - h), z - h, z + 1)

    def down(self, h):
        z = lax.axis_index("z")
        return self.move(1, h, self.own if h == 0 else self.slab(z + h), z + h, z - 1)

    def start(self):
        z = lax.axis_index("z")

        @pl.when(z < self.last)
        def _():
            self.up(0).start()

        @pl.when(z > 0)
        def _():
            self.down(0).start()

    def arrive(self, h):
        z = lax.axis_index("z")

        @pl.when(z - h - 1 >= 0)
        def _():
            self.move(0, h, self.slab(z - h - 1), z - h - 1, z).wait_recv()
            if h < 2:

                @pl.when(z < self.last)
                def _():
                    self.up(h + 1).start()

        @pl.when(z + h + 1 <= self.last)
        def _():
            self.move(1, h, self.slab(z + h + 1), z + h + 1, z).wait_recv()
            if h < 2:

                @pl.when(z > 0)
                def _():
                    self.down(h + 1).start()

    def finish(self):
        z = lax.axis_index("z")
        for h in range(3):

            @pl.when((z < self.last) & (z - h >= 0))
            def _():
                self.up(h).wait_send()

            @pl.when((z > 0) & (z + h <= self.last))
            def _():
                self.down(h).wait_send()


def chain_sems(count):
    return [pltpu.SemaphoreType.DMA((count, 3)) for _ in range(4)]


def greet_neighbours(peers):
    y, c, z, x = spot()
    last = lax.axis_size("z") - 1
    barrier = pltpu.get_barrier_semaphore()
    for peer in peers:
        pl.semaphore_signal(barrier, inc=1, device_id=peer, device_id_type=MESH_ID)

    @pl.when(z > 0)
    def _():
        pl.semaphore_signal(barrier, inc=1, device_id=(y, c, z - 1, x), device_id_type=MESH_ID)

    @pl.when(z < last)
    def _():
        pl.semaphore_signal(barrier, inc=1, device_id=(y, c, z + 1, x), device_id_type=MESH_ID)

    return barrier, len(peers) + (z > 0).astype(jnp.int32) + (z < last).astype(jnp.int32)


def others():
    y, c, z, x = spot()
    return [(flip(y, dy), flip(c, dc), z, flip(x, dx)) for dy in (0, 1) for dc in (0, 1) for dx in (0, 1) if dy + dc + dx]


def line_of():
    y, c, z, x = spot()
    return [(y, c, lax.rem(z + dz, 4), x) for dz in (1, 2, 3)]


class Fold:
    def __init__(self, slab, far, near_part, cross, mine, theirs, send, recv, local):
        y, c, z, x = spot()
        a, b = z // 2, lax.rem(z, 2)
        pair, middle = (y, c, 2 * a + 1 - b, x), (y, c, 2 * (1 - a) + b, x)
        self.far = remote(slab(2 * (1 - a) + 1 - b), far, send.at[0], recv.at[0], pair)
        self.near = remote(slab(2 * a + 1 - b), near_part, send.at[1], recv.at[1], pair)
        self.cross = remote(mine, cross, send.at[2], recv.at[2], middle)
        self.fetches = [
            pltpu.make_async_copy(slab(2 * (1 - a) + b), mine, local.at[0]),
            pltpu.make_async_copy(far, theirs, local.at[1]),
        ]
        self.mine, self.theirs = mine, theirs

    def start(self):
        self.far.start()
        self.fetches[0].start()

    def fold(self):
        self.far.wait_recv()
        self.fetches[1].start()
        for copy in self.fetches:
            copy.wait()
        add_rows(self.mine, 0, self.theirs, 0, self.mine.shape[0])
        self.cross.start()
        self.near.start()

    def finish(self):
        for copy in (self.near, self.cross):
            copy.wait_recv()
        for copy in (self.far, self.near, self.cross):
            copy.wait_send()


def columns_of_layer(whole):
    size = whole.shape[1] // 4
    return lambda at: whole.at[:, pl.ds(pl.multiple_of(at * size, size), size)]


def fold_peers():
    y, c, z, x = spot()
    a, b = z // 2, lax.rem(z, 2)
    return ((y, c, 2 * a + 1 - b, x), (y, c, 2 * (1 - a) + b, x))


def add_rows(total, first, term, start, count):
    def step(i, carry):
        here = pl.ds(pl.multiple_of(first + i * CHUNK, CHUNK), CHUNK)
        there = pl.ds(pl.multiple_of(start + i * CHUNK, CHUNK), CHUNK)
        total[here, :] = (total[here, :].astype(jnp.float32) + term[there, :].astype(jnp.float32)).astype(LOW)
        return carry

    lax.fori_loop(0, count // CHUNK, step, 0)


def scatter_scratch(width, parts=1):
    return [
        pltpu.VMEM((2, TILE, width), LOW),
        pltpu.VMEM((4, TILE, width), LOW),
        pltpu.VMEM((4, TILE, width), LOW),
        pltpu.VMEM((2, HALF, width), LOW),
        pltpu.VMEM((2, TILE, width), LOW),
        pltpu.SemaphoreType.DMA((parts, 10)),
        pltpu.SemaphoreType.DMA((parts, 10)),
    ]


class Scatter:
    def __init__(self, produce, staged, core_part, total, relayed, landed, send, recv, part=0, start=0, size=TILE):
        across_x, across_y, core = near()
        self.produce, self.staged, self.core_part, self.total, self.relayed = produce, staged, core_part, total, relayed
        self.start, self.size, self.half = start, size, size // 2
        send, recv = send.at[part], recv.at[part]
        rows = pl.ds(start, size)
        halves = (pl.ds(start, self.half), pl.ds(start + self.half, self.half))
        self.relay_row = start // 2
        passing = pl.ds(self.relay_row, self.half)
        self.to_core = [
            remote(staged.at[k % 2, rows], core_part.at[k, rows], send.at[k], recv.at[k], core) for k in range(4)
        ]
        self.far_x = remote(total.at[0, halves[0]], relayed.at[0, passing], send.at[4], recv.at[4], across_x)
        self.far_y = remote(total.at[0, halves[1]], relayed.at[1, passing], send.at[5], recv.at[5], across_y)
        self.to_x = [
            remote(total.at[1, at], landed.at[0, at], send.at[6 + half], recv.at[6 + half], across_x)
            for half, at in enumerate(halves)
        ]
        self.to_y = [
            remote(total.at[2, at], landed.at[1, at], send.at[8 + half], recv.at[8 + half], across_y)
            for half, at in enumerate(halves)
        ]

    def begin(self):
        y, c, z, x = spot()
        rows = pl.ds(self.start, self.size)
        for k, (to_row, to_column) in enumerate(((1 - y, 1 - x), (y, 1 - x), (1 - y, x), (y, x))):
            if k >= 2:
                self.to_core[k - 2].wait_send()
            self.produce(2 * k, to_row, 1 - c, to_column, self.staged.at[k % 2, rows])
            self.to_core[k].start()
            self.produce(2 * k + 1, to_row, c, to_column, self.total.at[k, rows])
            self.to_core[k].wait_recv()
            add_rows(self.total.at[k], self.start, self.core_part.at[k], self.start, self.size)
            if k == 0:
                self.far_x.start()
                self.far_y.start()
            if k == 1:
                self.to_x[0].start()
            if k == 2:
                self.to_y[1].start()

    def relay(self):
        self.far_y.wait_recv()
        add_rows(self.total.at[1], self.start + self.half, self.relayed.at[1], self.relay_row, self.half)
        self.to_x[1].start()
        self.far_x.wait_recv()
        add_rows(self.total.at[2], self.start, self.relayed.at[0], self.relay_row, self.half)
        self.to_y[0].start()

    def arrive(self):
        for copy in self.to_x + self.to_y:
            copy.wait_recv()

    def finish(self):
        for copy in self.to_core[2:] + [self.far_x, self.far_y] + self.to_x + self.to_y:
            copy.wait_send()


def sum_and_gather(part_of, rows_of_half, gather, beside):
    sums = [part_of(half) for half in (0, 1)]
    sums[0].begin()
    sums[0].relay()
    sums[1].begin()
    sums[0].arrive()
    rows_of_half(0)
    gather.start(0)
    beside(0)
    sums[1].relay()
    beside(1)
    sums[1].arrive()
    rows_of_half(1)
    gather.start(1)
    gather.pass_near(0)
    beside(2)
    gather.pass_near(1)
    gather.pass_far(0)
    gather.pass_far(1)
    gather.finish()
    beside(3)
    for half in (0, 1):
        sums[half].finish()


def begin_kernel(
    x_own, w_query, w_key, w_value, facts, x_whole, w_qkv, facts_whole,
    gather_send, gather_recv, w_send, w_recv, fact_send, fact_recv, local, *scratch
):
    y, c, z, x = spot()
    row = 2 * y + c
    layer = others()
    trade_parts, sems = scratch[:5], scratch[5:]
    trade = Trade(
        [x_own.at[half] for half in (0, 1)], lambda half, at: x_whole.at[place_of(at[0], at[1], at[3], half)], *trade_parts, detour=False
    )
    barrier, count = greet_neighbours(layer)
    pl.semaphore_wait(barrier, count + trade.greet(barrier, True))

    shard = w_query.shape[0]
    for half in (0, 1):
        trade.start(half)
    spread = [
        remote(facts, facts_whole.at[row, z, x], fact_send.at[k], fact_recv.at[k], peer) for k, peer in enumerate(layer)
    ]
    kept = [pltpu.make_async_copy(facts, facts_whole.at[row, z, x], local.at[6])]
    for m in range(6):
        source, slot = (w_query, w_key, w_value)[m // 2], m % 2

        def columns_of(at):
            head = 4 * (2 * at[0] + at[1]) + (3 - at[3] if slot else at[3])
            return source.at[:, pl.ds(pl.multiple_of(head * HD, HD), HD)]

        dst = w_qkv.at[row, z, pl.ds(pl.multiple_of(x * shard, shard), shard), pl.ds(m * HD, HD)]
        for k, peer in enumerate(layer):
            spread.append(remote(columns_of(peer), dst, w_send.at[m, k], w_recv.at[m, k], peer))
        kept.append(pltpu.make_async_copy(columns_of((y, c, z, x)), dst, local.at[m]))
    for copy in spread + kept:
        copy.start()

    gather = GatherWhole(lambda half: x_whole.at[place_of(y, c, x, half)], x_whole, gather_send, gather_recv)
    for half in (0, 1):
        trade.forward(half)
        trade.arrive(half)
        gather.start(half)

    for copy in kept:
        copy.wait()
    for copy in spread:
        copy.wait_recv()
    chains = [
        Chain(facts_whole.at[:, z], lambda at: facts_whole.at[:, at], sems, 0),
        Chain(w_qkv.at[:, z], lambda at: w_qkv.at[:, at], sems, 1),
    ]

    def arrive(h):
        for chain in chains:
            chain.arrive(h)

    for chain in chains:
        chain.start()
    gather.pass_first()
    arrive(0)
    gather.pass_second()
    arrive(1)
    gather.pass_far()
    arrive(2)
    gather.finish()
    trade.finish()
    for copy in spread:
        copy.wait_send()
    for chain in chains:
        chain.finish()


def anywhere():
    return pl.BlockSpec(memory_space=pl.ANY)


def in_vmem():
    return pl.BlockSpec(memory_space=pltpu.VMEM)


def dma(*shape):
    return pltpu.SemaphoreType.DMA(shape)


def remote_params(number):
    return pltpu.CompilerParams(collective_id=number, has_side_effects=True, vmem_limit_bytes=VMEM_LIMIT)


def begin(x_own, w_query, w_key, w_value, facts):
    block, width = x_own.shape
    shard = w_query.shape[0]
    x_whole, w_qkv, facts_whole = pl.pallas_call(
        begin_kernel,
        out_shape=(
            jax.ShapeDtypeStruct((8 * block, width), LOW),
            jax.ShapeDtypeStruct((4, 4, 2 * shard, 3 * width // 8), LOW),
            jax.ShapeDtypeStruct((4, 4, 2, *facts.shape), jnp.float32),
        ),
        in_specs=[in_vmem()] + [anywhere()] * 4,
        out_specs=[anywhere()] * 3,
        scratch_shapes=[
            dma(GATHER_COPIES), dma(GATHER_COPIES), dma(6, 7), dma(6, 7), dma(7), dma(7), dma(7),
            *trade_scratch(2, block // 2, width), *chain_sems(2),
        ],
        compiler_params=remote_params(1),
        cost_estimate=pl.CostEstimate(flops=0, bytes_accessed=350_000_000, transcendentals=0),
    )(x_own.reshape(2, block // 2, width), w_query, w_key, w_value, facts)
    return x_whole, w_qkv.reshape(width, 3 * width // 8), facts_whole


def summed(total, landed, here):
    parts = (total[3, here, :], landed[0, here, :], landed[1, here, :])
    return sum(part.astype(jnp.float32) for part in parts)


def over_chunks(work, half):
    def step(i, carry):
        work(pl.ds(pl.multiple_of(half * HALF + i * CHUNK, CHUNK), CHUNK))
        return carry

    lax.fori_loop(0, HALF // CHUNK, step, 0)


def own_halves(own):
    return lambda half: own.at[pl.ds(half * HALF, HALF)]


def inverse_of(value):
    return lax.rsqrt(jnp.mean(value * value, axis=-1, keepdims=True) + EPSILON)


def close_attention_kernel(attended, w_out, x_whole, gain, w_gate, w_up, resid, normed, own_gate, own_up, own, x_own, *scratch):
    scatter, (send, recv, local), sems = scratch[:7], scratch[7:10], scratch[10:]
    y, c, z, x = spot()
    fetch_x = pltpu.make_async_copy(x_whole.at[place_of(y, c, x)], x_own, local.at[0])
    fetch_x.start()
    width = w_out.shape[1]
    hidden = w_gate.shape[1]
    z = lax.axis_index("z")
    barrier, count = greet_neighbours(near())
    pl.semaphore_wait(barrier, count)

    def slab_of(whole):
        return lambda at: whole.at[:, pl.ds(pl.multiple_of(at * hidden, hidden), hidden)]

    chains, kept = [], []
    for k, (part, whole) in enumerate(((w_gate, own_gate), (w_up, own_up))):
        chains.append(Chain(part, slab_of(whole), sems, k))
        chains[k].start()
        kept.append(pltpu.make_async_copy(part, slab_of(whole)(z), local.at[1 + k]))
        kept[k].start()

    def arrive(h):
        for chain in chains:
            chain.arrive(h)

    def part_of(half):
        def produce(turn, y, c, x, out):
            at = place_of(y, c, x, half)

            def step(i, carry):
                columns = pl.ds(pl.multiple_of(i * TILE, TILE), TILE)
                out[:, columns] = dot_wide(attended[at, :], w_out[:, columns]).astype(LOW)
                return carry

            lax.fori_loop(0, width // TILE, step, 0)

        return Scatter(produce, *scatter, part=half, start=half * HALF, size=HALF)

    total, landed = scatter[2], scatter[4]

    def chunk(here):
        value = x_own[here, :].astype(jnp.float32) + summed(total, landed, here)
        resid[here, :] = value
        own[here, :] = (value * inverse_of(value) * gain[...]).astype(LOW)

    def rows_of_half(half):
        if half == 0:
            fetch_x.wait()
        over_chunks(chunk, half)

    gather = Gather(own_halves(own), normed, send, recv)
    sum_and_gather(part_of, rows_of_half, gather, lambda turn: arrive(turn - 1) if turn > 0 else None)
    keep = pltpu.make_async_copy(own, normed.at[place_of(y, c, x)], local.at[0])
    keep.start()
    for chain in chains:
        chain.finish()
    for copy in kept + [keep]:
        copy.wait()


def close_attention(attended, w_out, x_whole, gain, w_gate, w_up):
    block, width = x_whole.shape[0] // 8, x_whole.shape[1]
    hidden = w_gate.shape[1]
    return pl.pallas_call(
        close_attention_kernel,
        out_shape=(
            jax.ShapeDtypeStruct((block, width), jnp.float32),
            jax.ShapeDtypeStruct((8 * block, width), LOW),
            jax.ShapeDtypeStruct((width, 4 * hidden), LOW),
            jax.ShapeDtypeStruct((width, 4 * hidden), LOW),
        ),
        in_specs=[in_vmem(), in_vmem(), anywhere()] + [in_vmem()] * 3,
        out_specs=[in_vmem()] + [anywhere()] * 3,
        scratch_shapes=[pltpu.VMEM((block, width), LOW)] * 2
        + scatter_scratch(width, 2)
        + [dma(GATHER_COPIES), dma(GATHER_COPIES), dma(3), *chain_sems(2)],
        compiler_params=remote_params(2),
        cost_estimate=pl.CostEstimate(flops=0, bytes_accessed=450_000_000, transcendentals=0),
    )(attended, w_out, x_whole, gain, w_gate, w_up)


def norm_back(value, gain, upstream):
    inverse = inverse_of(value)
    scaled = upstream * gain
    inner = jnp.mean(scaled * value, axis=-1, keepdims=True)
    return inverse * scaled - value * (inverse * inverse * inverse) * inner, upstream * value * inverse


def fold_rows(total, terms):
    for first in range(0, CHUNK, 8):
        total[...] += terms[first : first + 8, :]


def close_mlp_kernel(
    d_gate, d_up, w_gate, w_up, resid, upstream, gain, grad_a, grad_b, d_resid, gain_term, d_resid_whole,
    far_a, near_a, cross_a, far_b, near_b, cross_b, own, blocks, *scratch
):
    scatter, (send, recv, local, fetched, fold_send, fold_recv, fold_local, mine, theirs) = scratch[:7], scratch[7:]
    y, c, z, x = spot()
    width = w_gate.shape[0]
    order = [
        place_of(r, k, q, half)
        for half in (0, 1)
        for r, q in ((1 - y, 1 - x), (y, 1 - x), (1 - y, x), (y, x))
        for k in (1 - c, c)
    ]

    def fetch(turn):
        slot = turn % 2
        return [
            pltpu.make_async_copy(source.at[order[turn]], blocks.at[slot, m], fetched.at[slot, m])
            for m, source in enumerate((d_gate, d_up))
        ]

    for copy in fetch(0):
        copy.start()
    greet(near() + fold_peers())
    folds = [
        Fold(columns_of_layer(grad), *refs, mine.at[k], theirs, fold_send.at[k], fold_recv.at[k], fold_local.at[k])
        for k, (grad, *refs) in enumerate(((grad_a, far_a, near_a, cross_a), (grad_b, far_b, near_b, cross_b)))
    ]
    for fold in folds:
        fold.start()

    def part_of(half):
        def produce(turn, to_y, to_c, to_x, out):
            turn = turn + 8 * half
            if turn < 15:
                for copy in fetch(turn + 1):
                    copy.start()
            for copy in fetch(turn):
                copy.wait()

            def step(i, carry):
                columns = pl.ds(pl.multiple_of(i * TILE, TILE), TILE)
                part = dot_nt(blocks[turn % 2, 0], w_gate[columns, :]) + dot_nt(blocks[turn % 2, 1], w_up[columns, :])
                out[:, columns] = part.astype(LOW)
                return carry

            lax.fori_loop(0, width // TILE, step, 0)

        return Scatter(produce, *scatter, part=half, start=half * HALF, size=HALF)

    total, landed = scatter[2], scatter[4]
    gain_term[...] = jnp.zeros_like(gain_term)

    def chunk(here):
        back, terms = norm_back(resid[here, :], gain[...], summed(total, landed, here))
        value = upstream[here, :].astype(jnp.float32) + back
        d_resid[here, :] = value
        own[here, :] = value.astype(LOW)
        fold_rows(gain_term, terms)

    def rows_of_half(half):
        over_chunks(chunk, half)

    gather = Gather(own_halves(own), d_resid_whole, send, recv)
    sum_and_gather(part_of, rows_of_half, gather, lambda turn: folds[turn].fold() if turn < 2 else None)
    keep = pltpu.make_async_copy(own, d_resid_whole.at[place_of(y, c, x)], local.at[0])
    keep.start()
    for fold in folds:
        fold.finish()
    keep.wait()


def close_mlp(d_gate, d_up, w_gate, w_up, resid, upstream, gain, *grads):
    block, width = resid.shape
    hidden = d_gate.shape[1]
    return pl.pallas_call(
        close_mlp_kernel,
        out_shape=(
            jax.ShapeDtypeStruct((block, width), jnp.float32),
            jax.ShapeDtypeStruct((8, width), jnp.float32),
            jax.ShapeDtypeStruct((8 * block, width), LOW),
            *[jax.ShapeDtypeStruct((width, hidden // 4), LOW)] * 6,
        ),
        in_specs=[anywhere()] * 2 + [in_vmem()] * 5 + [anywhere()] * 2,
        out_specs=[in_vmem(), in_vmem()] + [anywhere()] * 7,
        scratch_shapes=[pltpu.VMEM((block, width), LOW), pltpu.VMEM((2, 2, block // 2, hidden), LOW)]
        + scatter_scratch(width, 2)
        + [dma(GATHER_COPIES), dma(GATHER_COPIES), dma(1), dma(2, 2), dma(2, 3), dma(2, 3), dma(2, 2)]
        + [pltpu.VMEM((2, width, hidden // 4), LOW), pltpu.VMEM((width, hidden // 4), LOW)],
        compiler_params=remote_params(3),
        cost_estimate=pl.CostEstimate(flops=0, bytes_accessed=450_000_000, transcendentals=0),
    )(d_gate, d_up, w_gate, w_up, resid, upstream, gain, *grads)


def close_layer_kernel(
    d_qkv, w_qkv, x_whole, d_resid, gain, mlp_term, grad, grad_low, gain_grads, far, near_part, cross, grad_parts, own, terms, layer_terms, part, column_terms, *scratch
):
    scatter, (send, recv, term_send, term_recv, line_send, line_recv, x_own, x_sem, *rest) = scratch[:7], scratch[7:]
    mine, theirs, fold_send, fold_recv, fold_local, part_send, part_recv = rest
    y, c, z, x = spot()
    fetch_x = pltpu.make_async_copy(x_whole.at[place_of(y, c, x)], x_own, x_sem.at[0])
    fetch_x.start()
    partner = partner_of(y, c, z, x)
    moves = z != 2 * c + y
    width = w_qkv.shape[0]
    barrier = pltpu.get_barrier_semaphore()

    @pl.when(moves)
    def _():
        pl.semaphore_signal(barrier, inc=1, device_id=partner, device_id_type=MESH_ID)

    layer = others()
    line = line_of()
    for peer in layer + line:
        pl.semaphore_signal(barrier, inc=1, device_id=peer, device_id_type=MESH_ID)
    pl.semaphore_wait(barrier, len(layer + line) + moves.astype(jnp.int32))

    size = TILE // PIECES

    def part_of(piece):
        def produce(turn, to_y, to_c, to_x, out):
            at = quarter_of(to_y, to_c, to_x, piece // 2, piece % 2)

            def step(i, carry):
                columns = pl.ds(pl.multiple_of(i * TILE, TILE), TILE)
                out[:, columns] = dot_nt(d_qkv[at, :], w_qkv[columns, :]).astype(LOW)
                return carry

            lax.fori_loop(0, width // TILE, step, 0)

        return Scatter(produce, *scatter, part=piece, start=piece * size, size=size)

    fold = Fold(lambda at: grad.at[at], far, near_part, cross, mine, theirs, fold_send, fold_recv, fold_local)
    fold.start()
    sums = [part_of(piece) for piece in range(PIECES)]
    sums[0].begin()
    sums[0].relay()
    sums[1].begin()
    fold.fold()
    total, landed = scatter[2], scatter[4]
    terms[1] = mlp_term[...]
    terms[0] = jnp.zeros_like(mlp_term)
    pieces = [pl.ds(piece * size, size) for piece in range(PIECES)]
    trades = [remote(own.at[at], grad_low.at[at], send.at[k], recv.at[k], partner) for k, at in enumerate(pieces)]
    keeps = [pltpu.make_async_copy(own.at[at], grad_low.at[at], recv.at[k]) for k, at in enumerate(pieces)]
    fetch_x.wait()
    for piece in range(PIECES):
        sums[piece].arrive()

        def step(i, carry):
            here = pl.ds(pl.multiple_of(piece * size + i * CHUNK, CHUNK), CHUNK)
            back, products = norm_back(x_own[here, :].astype(jnp.float32), gain[...], summed(total, landed, here))
            own[here, :] = (d_resid[here, :] + back).astype(LOW)
            fold_rows(terms.at[0], products)
            return carry

        lax.fori_loop(0, size // CHUNK, step, 0)

        @pl.when(moves)
        def _():
            trades[piece].start()

        @pl.when(jnp.logical_not(moves))
        def _():
            keeps[piece].start()

        if piece + 1 < PIECES:
            sums[piece + 1].relay()
        if piece + 2 < PIECES:
            sums[piece + 2].begin()

    fold.finish()
    for source, target, k in ((grad.at[z], mine, 0), (near_part, theirs, 1)):
        pltpu.make_async_copy(source, target, fold_local.at[k]).start()
    for source, target, k in ((grad.at[z], mine, 0), (near_part, theirs, 1)):
        pltpu.make_async_copy(source, target, fold_local.at[k]).wait()
    add_rows(mine, 0, theirs, 0, mine.shape[0])
    last = pltpu.make_async_copy(cross, theirs, fold_local.at[1])
    last.start()
    last.wait()
    add_rows(mine, 0, theirs, 0, mine.shape[0])
    shard = mine.shape[0] // 8
    index = 4 * y + 2 * c + x
    parts = [
        remote(
            mine.at[pl.ds(pl.multiple_of((4 * peer[0] + 2 * peer[1] + peer[3]) * shard, shard), shard)],
            grad_parts.at[index],
            part_send.at[k],
            part_recv.at[k],
            peer,
        )
        for k, peer in enumerate(layer)
    ]
    kept = pltpu.make_async_copy(mine.at[pl.ds(pl.multiple_of(index * shard, shard), shard)], grad_parts.at[index], fold_local.at[0])
    for copy in parts + [kept]:
        copy.start()

    def columns_of(row, layers):
        return pl.ds(pl.multiple_of((4 * row) * HD, HD), layers * HD)

    spread = [
        remote(terms.at[:, :, columns_of(2 * peer[0] + peer[1], 4)], layer_terms.at[k], term_send.at[k], term_recv.at[k], peer)
        for k, peer in enumerate(layer)
    ]
    for copy in spread:
        copy.start()
    for copy in spread:
        copy.wait_recv()
    part[...] = sum((layer_terms[k] for k in range(7)), terms[:, :, columns_of(2 * y + c, 4)])
    lines = [
        remote(
            part.at[:, :, pl.ds(pl.multiple_of(peer[2] * HD, HD), HD)], column_terms.at[k], line_send.at[k], line_recv.at[k], peer
        )
        for k, peer in enumerate(line)
    ]
    for copy in lines:
        copy.start()
    for copy in lines:
        copy.wait_recv()
    gain_grads[...] = sum((column_terms[k] for k in range(3)), part[:, :, pl.ds(pl.multiple_of(z * HD, HD), HD)])
    for copy in spread + lines:
        copy.wait_send()
    for part_sum in sums:
        part_sum.finish()
    for copy in parts + [kept]:
        copy.wait()

    @pl.when(moves)
    def _():
        for copy in trades:
            copy.wait()

    @pl.when(jnp.logical_not(moves))
    def _():
        for copy in keeps:
            copy.wait()


def close_layer(d_qkv, w_qkv, x_whole, d_resid, gain, mlp_term, grad):
    block, width = d_resid.shape
    return pl.pallas_call(
        close_layer_kernel,
        out_shape=(
            jax.ShapeDtypeStruct((block, width), LOW),
            jax.ShapeDtypeStruct((2, 8, width // 16), jnp.float32),
            *[jax.ShapeDtypeStruct(grad.shape[1:], LOW)] * 3,
            jax.ShapeDtypeStruct((8, grad.shape[1] // 8, grad.shape[2]), LOW),
        ),
        in_specs=[in_vmem(), in_vmem(), anywhere()] + [in_vmem()] * 3 + [anywhere()],
        out_specs=[anywhere(), in_vmem()] + [anywhere()] * 4,
        scratch_shapes=[
            pltpu.VMEM((block, width), LOW),
            pltpu.VMEM((2, 8, width), jnp.float32),
            pltpu.VMEM((7, 2, 8, width // 4), jnp.float32),
            pltpu.VMEM((2, 8, width // 4), jnp.float32),
            pltpu.VMEM((3, 2, 8, width // 16), jnp.float32),
        ]
        + scatter_scratch(width, PIECES)
        + [dma(PIECES), dma(PIECES), dma(7), dma(7), dma(3), dma(3), pltpu.VMEM((block, width), LOW), dma(1)]
        + [pltpu.VMEM(grad.shape[1:], LOW)] * 2
        + [dma(3), dma(3), dma(2), dma(7), dma(7)],
        compiler_params=remote_params(4),
        cost_estimate=pl.CostEstimate(flops=0, bytes_accessed=350_000_000, transcendentals=0),
    )(d_qkv, w_qkv, x_whole, d_resid, gain, mlp_term, grad)


def doc_start(ends, place):
    start = jnp.zeros_like(place)
    for k in range(8):
        start = jnp.where(ends[k] <= place, ends[k], start)
    return jnp.where(place < ends[7], start, LEN)


def sigmoid_of(raw):
    return pl.reciprocal(1.0 + jnp.exp2(math.log2(LEN) - raw * (math.log2(math.e) / math.sqrt(HD))), approx=True)


def tile_at(index):
    return pl.ds(pl.multiple_of(index * TILE, TILE), TILE)


def head_of(array, rows, part, head):
    first = (part * (array.shape[1] // 3) // HD + head) * HD
    return array[rows, first : first + HD]


def attend_kernel(ends, qkv, out, total):
    i = pl.program_id(0)
    heads = qkv.shape[1] // (3 * HD)
    total[...] = jnp.zeros_like(total)
    q_place = i * TILE + lax.broadcasted_iota(jnp.int32, (TILE, 1), 0)
    q_start = doc_start(ends, q_place)

    def tile(j, diagonal):
        k_place = j * TILE + lax.broadcasted_iota(jnp.int32, (1, TILE), 1)
        allowed = k_place >= q_start
        if diagonal:
            allowed = allowed & (k_place <= q_place)
        for head in range(heads):
            raw = dot_nt(head_of(qkv, tile_at(i), 0, head), head_of(qkv, tile_at(j), 1, head))
            weight = jnp.where(allowed, sigmoid_of(raw), 0.0).astype(LOW)
            total[head] += dot_wide(weight, head_of(qkv, tile_at(j), 2, head))

    def step(j, carry):
        tile(j, False)
        return carry

    lax.fori_loop(0, i, step, 0)
    tile(i, True)
    for head in range(heads):
        out[tile_at(i), head * HD : (head + 1) * HD] = total[head].astype(LOW)


def open_mlp_kernel(normed, w_gate, w_up, upstream, gate, up, hidden, upstream_whole, send, recv, local):
    i = pl.program_id(0)
    y, c, z, x = spot()
    steps = pl.num_programs(0)
    gather = Gather(lambda half: upstream.at[pl.ds(half * HALF, HALF)], upstream_whole, send, recv)
    keep = pltpu.make_async_copy(upstream, upstream_whole.at[place_of(y, c, x)], local.at[0])

    @pl.when(i == 0)
    def _():
        greet(near())
        gather.start(0)
        gather.start(1)
        keep.start()

    def step(n, carry):
        columns = pl.ds(pl.multiple_of(n * TILE, TILE), TILE)
        gate_part, up_part = dot_wide(normed[...], w_gate[:, columns]), dot_wide(normed[...], w_up[:, columns])
        gate[:, columns] = gate_part
        up[:, columns] = up_part
        hidden[:, columns] = (gate_part * jax.nn.sigmoid(gate_part) * up_part).astype(LOW)
        return carry

    lax.fori_loop(0, w_gate.shape[1] // TILE, step, 0)

    @pl.when(i == steps - 1)
    def _():
        for half in (0, 1):
            gather.pass_near(half)
        for half in (0, 1):
            gather.pass_far(half)
        gather.finish()
        keep.wait()


def open_mlp(normed, w_gate, w_up, upstream):
    places, width = normed.shape
    hidden = w_gate.shape[1]
    rows = lambda columns: pl.BlockSpec((TILE, columns), lambda i: (i, 0))
    whole = lambda array: pl.BlockSpec(array.shape, lambda i: (0, 0))
    return pl.pallas_call(
        open_mlp_kernel,
        out_shape=(
            jax.ShapeDtypeStruct((places, hidden), jnp.float32),
            jax.ShapeDtypeStruct((places, hidden), jnp.float32),
            jax.ShapeDtypeStruct((places, hidden), LOW),
            jax.ShapeDtypeStruct((places, width), LOW),
        ),
        grid=(places // TILE,),
        in_specs=[rows(width), whole(w_gate), whole(w_up), whole(upstream)],
        out_specs=[rows(hidden), rows(hidden), rows(hidden), anywhere()],
        scratch_shapes=[dma(GATHER_COPIES), dma(GATHER_COPIES), dma(1)],
        compiler_params=remote_params(5),
        cost_estimate=pl.CostEstimate(flops=0, bytes_accessed=250_000_000, transcendentals=0),
    )(normed, w_gate, w_up, upstream)


def out_turns():
    y, c, z, x = spot()
    layers = (x, x, 3 - x, 3 - x)
    owners = [((y, c, layers[j], j % 2), (z == layers[j]) & (x == j % 2)) for j in range(4)]
    side = lax.rem((z + 1) // 2, 2)
    holders = [((y, c, j, side), (z == j) & (x == side)) for j in range(4)]
    return owners, holders


def attend_back_kernel(
    ends, qkv, grads, out_grad, mixed, out, out_parts, mixed_home, query_total, key_total, value_total, send, recv, *trade_parts
):
    j = pl.program_id(0)
    y, c, z, x = spot()
    heads = qkv.shape[1] // (3 * HD)
    shard = out_grad.shape[0] // 4
    owners, holders = out_turns()
    trade = Trade(
        [mixed.at[pl.ds(half * HALF, HALF)] for half in (0, 1)], lambda half, at: mixed_home.at[pl.ds(half * HALF, HALF)], *trade_parts
    )

    def to_owner(turn):
        return remote(out_grad.at[pl.ds(turn * shard, shard)], out_parts.at[z], send.at[turn], recv.at[z], owners[turn][0])

    def to_self(turn):
        return pltpu.make_async_copy(out_grad.at[pl.ds(turn * shard, shard)], out_parts.at[z], recv.at[z])

    @pl.when(j == 0)
    def _():
        query_total[...] = jnp.zeros_like(query_total)
        barrier = pltpu.get_barrier_semaphore()
        for peer, here in holders:

            @pl.when(jnp.logical_not(here))
            def _():
                pl.semaphore_signal(barrier, inc=1, device_id=peer, device_id_type=MESH_ID)

        pl.semaphore_wait(barrier, 4 - (x == lax.rem((z + 1) // 2, 2)).astype(jnp.int32) + trade.greet(barrier, False))
        for half in (0, 1):
            trade.start(half)
        for turn in range(4):

            @pl.when(jnp.logical_not(owners[turn][1]))
            def _():
                to_owner(turn).start()

            @pl.when(owners[turn][1])
            def _():
                to_self(turn).start()

    key_total[...] = jnp.zeros_like(key_total)
    value_total[...] = jnp.zeros_like(value_total)
    here = tile_at(j)
    k_place = j * TILE + lax.broadcasted_iota(jnp.int32, (TILE, 1), 0)
    turned = [head_of(qkv, here, 1, head).T for head in range(heads)]

    def tile(i, diagonal):
        q_place = i * TILE + lax.broadcasted_iota(jnp.int32, (1, TILE), 1)
        allowed = k_place >= doc_start(ends, q_place)
        if diagonal:
            allowed = allowed & (k_place <= q_place)
        for head in range(heads):
            query, grad = head_of(qkv, tile_at(i), 0, head), grads[tile_at(i), head * HD : (head + 1) * HD]
            sig = jnp.where(allowed, sigmoid_of(dot_nt(head_of(qkv, here, 1, head), query)), 0.0)
            value_total[head] += dot_wide(sig.astype(LOW), grad)
            d_score = (dot_nt(head_of(qkv, here, 2, head), grad) * (sig * (1.0 - sig))).astype(LOW)
            key_total[head] += dot_wide(d_score, query)
            query_total[head, :, tile_at(i)] += dot_wide(turned[head], d_score)

    def step(i, carry):
        tile(i, False)
        return carry

    tile(j, True)
    lax.fori_loop(j + 1, LEN // TILE, step, 0)
    scale = 1.0 / math.sqrt(HD)
    for head in range(heads):
        first = head * HD
        out[here, heads * HD + first : (heads + 1) * HD + first] = (key_total[head] * scale).astype(LOW)
        out[here, 2 * heads * HD + first : (2 * heads + 1) * HD + first] = value_total[head].astype(LOW)
        out[here, first : first + HD] = (query_total[head, :, here] * scale).T.astype(LOW)

    @pl.when(j == LEN // TILE - 1)
    def _():
        for turn in range(4):

            @pl.when(jnp.logical_not(owners[turn][1]))
            def _():
                to_owner(turn).wait_send()

            @pl.when(jnp.logical_not(holders[turn][1]))
            def _():
                landed = out_parts.at[turn]
                remote(landed, landed, send.at[turn], recv.at[turn], holders[turn][0]).wait_recv()

            @pl.when(owners[turn][1])
            def _():
                to_self(turn).wait()

        for half in (0, 1):
            trade.arrive(half)
        trade.finish()

    @pl.when(j == 1)
    def _():
        for half in (0, 1):
            trade.forward(half)


def back_mlp_kernel(upstream, w_down, gate, up, d_gate, d_up):
    def step(n, carry):
        columns = pl.ds(pl.multiple_of(n * TILE, TILE), TILE)
        d_hidden = dot_nt(upstream[...], w_down[columns, :])
        d_gate[:, columns], d_up[:, columns] = gate_backward(
            d_hidden, gate[:, columns], up[:, columns], jax.nn.sigmoid(gate[:, columns])
        )
        return carry

    lax.fori_loop(0, gate.shape[1] // TILE, step, 0, unroll=2)


def back_mlp(upstream, w_down, gate, up):
    places, width = upstream.shape
    hidden = gate.shape[1]
    rows = lambda size: pl.BlockSpec((TILE, size), lambda i: (i, 0))
    return pl.pallas_call(
        back_mlp_kernel,
        out_shape=(jax.ShapeDtypeStruct((places, hidden), LOW), jax.ShapeDtypeStruct((places, hidden), LOW)),
        grid=(places // TILE,),
        in_specs=[rows(width), pl.BlockSpec(w_down.shape, lambda i: (0, 0)), rows(hidden), rows(hidden)],
        out_specs=[rows(hidden), rows(hidden)],
        compiler_params=pltpu.CompilerParams(vmem_limit_bytes=VMEM_LIMIT),
        cost_estimate=pl.CostEstimate(flops=0, bytes_accessed=90_000_000, transcendentals=0),
    )(upstream, w_down, gate, up)


def attend(ends, qkv):
    places, width = qkv.shape
    heads = width // (3 * HD)
    whole = lambda columns: pl.BlockSpec((places, columns), lambda i: (0, 0))
    return pl.pallas_call(
        attend_kernel,
        out_shape=jax.ShapeDtypeStruct((places, width // 3), LOW),
        grid=(places // TILE,),
        in_specs=[pl.BlockSpec(memory_space=pltpu.SMEM), whole(width)],
        out_specs=whole(width // 3),
        scratch_shapes=[pltpu.VMEM((heads, TILE, HD), jnp.float32)],
        compiler_params=pltpu.CompilerParams(vmem_limit_bytes=VMEM_LIMIT),
        cost_estimate=pl.CostEstimate(flops=0, bytes_accessed=150_000_000, transcendentals=0),
    )(ends, qkv)


def attend_back(ends, qkv, grads, out_grad, mixed):
    places, width = qkv.shape
    heads = width // (3 * HD)
    whole = lambda columns: pl.BlockSpec((places, columns), lambda j: (0, 0))
    return pl.pallas_call(
        attend_back_kernel,
        out_shape=(
            jax.ShapeDtypeStruct((places, width), LOW),
            jax.ShapeDtypeStruct((4, out_grad.shape[0] // 4, out_grad.shape[1]), LOW),
            jax.ShapeDtypeStruct(mixed.shape, LOW),
        ),
        grid=(places // TILE,),
        in_specs=[pl.BlockSpec(memory_space=pltpu.SMEM), whole(width), whole(width // 3), anywhere(), pl.BlockSpec(mixed.shape, lambda j: (0, 0))],
        out_specs=[whole(width), anywhere(), anywhere()],
        scratch_shapes=[
            pltpu.VMEM((heads, HD, places), jnp.float32),
            pltpu.VMEM((heads, TILE, HD), jnp.float32),
            pltpu.VMEM((heads, TILE, HD), jnp.float32),
            dma(4),
            dma(4),
            *trade_scratch(2, HALF, mixed.shape[1]),
        ],
        compiler_params=remote_params(6),
        cost_estimate=pl.CostEstimate(flops=0, bytes_accessed=300_000_000, transcendentals=0),
    )(ends, qkv, grads, out_grad, mixed)


LAYER = ("y", "c", "x")
PLACES = ("c", "y", "x")
ALL = ("y", "c", "z", "x")


def trade(part):
    pairs = []
    for y in range(2):
        for c in range(2):
            for z in range(4):
                for x in range(2):
                    pairs.append((((y * 2 + c) * 4 + z) * 2 + x, (((z % 2) * 2 + z // 2) * 4 + 2 * c + y) * 2 + x))
    return lax.ppermute(part, ALL, pairs)


def after(first, then):
    return lax.optimization_barrier((first, then))[1]


def body_layers(
    tokens, lengths, cotangent, w_query, w_key, w_value, w_out, w_gate, w_up, w_down, gain_attn, gain_mlp
):
    rows_here, block, width = tokens.shape
    members = lax.axis_size(LAYER)
    layers = lax.axis_size("z")
    shard = w_query.shape[0]
    owned = width // members
    facts = jnp.zeros((8, 2 * shard), jnp.float32)
    facts = facts.at[0, :shard].set(gain_attn.astype(jnp.float32)).at[1, :shard].set(gain_mlp.astype(jnp.float32))
    facts = facts.at[2, : lengths.shape[1]].set(lengths[0].astype(jnp.float32))
    layer_x, w_qkv, facts = begin(tokens.reshape(block, width), w_query, w_key, w_value, facts)
    full_gain_attn, full_gain_mlp = facts[:, :, :, 0, :shard].reshape(1, width), facts[:, :, :, 1, :shard].reshape(1, width)
    layer = lax.axis_index("z")
    own_lengths = facts[:, 0, 0, 2, : lengths.shape[1]].reshape(2, 2, -1)
    own_lengths = lax.dynamic_slice(own_lengths, (layer % 2, layer // 2, 0), (1, 1, own_lengths.shape[2]))[0, 0]
    ends = jnp.cumsum(own_lengths.astype(jnp.int32))
    layer_normed = norm_forward(layer_x.astype(jnp.float32), full_gain_attn)[0].astype(LOW)
    here = lax.axis_index("x")
    out_rows = lax.all_gather(after(facts, w_out), ("z", "x"), axis=0, tiled=True)
    w_out_own = [lax.dynamic_slice_in_dim(out_rows, head * HD, HD, 0) for head in (here, 3 - here)]
    w_out_own = jnp.concatenate(w_out_own, axis=0)

    qkv = dot_wide(layer_normed, w_qkv).astype(LOW)
    upstream = trade(after(facts, cotangent)).reshape(block, width)
    attended = attend(ends, qkv)
    resid, layer_mlp, own_gate, own_up = close_attention(after(upstream, attended), w_out_own, layer_x, full_gain_mlp, w_gate, w_up)

    own_down = lax.all_gather(after(resid, w_down), "z", axis=0, tiled=True)
    gate, up_part, hidden, layer_upstream = open_mlp(layer_mlp, own_gate, own_up, upstream)
    part = dot_wide(hidden, own_down).astype(LOW)
    mixed_sum = lax.psum_scatter(part, PLACES, scatter_dimension=0, tiled=True)
    down_term = contract_rows(after(part, hidden), layer_upstream).astype(LOW)
    down_rows = w_down.shape[0]
    down_parts = []
    for up in range(1, 4):
        layers_pairs = [(at, (at + up) % 4) for at in range(4)]
        slab = lax.dynamic_slice_in_dim(down_term, (layer + up) % 4 * down_rows, down_rows, 0)
        down_parts.append(lax.ppermute(slab, "z", layers_pairs))
    d_gate, d_up = back_mlp(after(down_term, layer_upstream), own_down, gate, up_part)
    gate_term, up_term = contract_rows(layer_mlp, d_gate).astype(LOW), contract_rows(layer_mlp, d_up).astype(LOW)
    d_resid, gain_mlp_term, layer_d_resid, *parts = close_mlp(
        after((mixed_sum, *down_parts), d_gate), d_up, own_gate, own_up, resid, upstream, full_gain_mlp, gate_term, up_term
    )

    def own_part(whole, near_part, cross):
        own = lax.dynamic_slice_in_dim(whole, layer * cross.shape[1], cross.shape[1], 1)
        return own.astype(jnp.float32) + near_part.astype(jnp.float32) + cross.astype(jnp.float32)

    mixed = (resid + after(layer_d_resid, mixed_sum).astype(jnp.float32)).astype(LOW)
    grad_down = lax.dynamic_slice_in_dim(down_term, layer * down_rows, down_rows, 0).astype(jnp.float32)
    grad_down = grad_down + sum(slab.astype(jnp.float32) for slab in down_parts)

    out_term = contract_rows(attended, layer_d_resid).astype(LOW)
    d_attended = contract_cols(layer_d_resid, w_out_own).astype(LOW)
    d_qkv, out_parts, mixed = attend_back(ends, qkv, d_attended, out_term, mixed)
    mixed = mixed.reshape(rows_here, block, width)
    grad_gate, grad_up = own_part(gate_term, *parts[1:3]), own_part(up_term, *parts[4:6])
    grad_out = jnp.sum(out_parts.astype(jnp.float32), axis=0)
    qkv_term = contract_rows(layer_normed, d_qkv).astype(LOW)
    qkv_term = qkv_term.reshape(4, layers, 2 * shard, 3 * owned).transpose(1, 0, 2, 3)
    qkv_term = qkv_term.reshape(layers, members * shard, 3 * owned)
    grad_low, gain_grads, *_, parts = close_layer(
        d_qkv, w_qkv, layer_x, d_resid, full_gain_attn, gain_mlp_term, qkv_term
    )
    grad_tokens = grad_low.astype(jnp.float32).reshape(rows_here, block, width)
    parts = parts.reshape(4, 2, shard, 3, 2, HD)
    parts = jnp.stack((parts[:, 0, :, :, 0], parts[:, 1, :, :, 0], parts[:, 1, :, :, 1], parts[:, 0, :, :, 1]), axis=1)
    grad_query, grad_key, grad_value = parts.transpose(3, 2, 0, 1, 4).astype(jnp.float32).reshape(3, shard, width)
    gain_grads = lax.dynamic_index_in_dim(jnp.sum(gain_grads, axis=1).reshape(2, 2, shard), lax.axis_index("x"), 1, False)
    return (
        mixed,
        grad_tokens,
        grad_query,
        grad_key,
        grad_value,
        grad_out,
        grad_gate,
        grad_up,
        grad_down,
        gain_grads[0],
        gain_grads[1],
    )


def body_any(
    tokens,
    lengths,
    cotangent,
    w_query,
    w_key,
    w_value,
    w_out,
    w_gate,
    w_up,
    w_down,
    gain_attn,
    gain_mlp,
):
    rows_here, block, width = tokens.shape
    count = rows_here * block
    scale = 1.0 / math.sqrt(HD)
    kv_place = lax.axis_index("kv")
    key_places = kv_place * block + jnp.arange(block, dtype=jnp.int32)
    attn_set = (
        lax.all_gather(w_query, ("row", "kv"), axis=0, tiled=True),
        lax.all_gather(w_key, ("row", "kv"), axis=0, tiled=True),
        lax.all_gather(w_value, ("row", "kv"), axis=0, tiled=True),
        lax.all_gather(w_out, ("row", "kv"), axis=0, tiled=True),
        lax.all_gather(gain_attn, ("row", "kv"), axis=0, tiled=True),
        lax.all_gather(gain_mlp, ("row", "kv"), axis=0, tiled=True),
    )
    full_query, full_key, full_value, full_out, full_gain_attn, full_gain_mlp = attn_set
    flat = tokens.reshape(count, width).astype(jnp.float32)
    normed_attn, inverse_attn = norm_forward(flat, full_gain_attn)
    normed_attn_low = normed_attn.astype(jnp.bfloat16)
    query_low = jnp.dot(normed_attn_low, full_query, preferred_element_type=jnp.float32).astype(
        jnp.bfloat16
    )
    key_low = jnp.dot(normed_attn_low, full_key, preferred_element_type=jnp.float32).astype(
        jnp.bfloat16
    )
    value_low = jnp.dot(normed_attn_low, full_value, preferred_element_type=jnp.float32).astype(
        jnp.bfloat16
    )
    key_heads = key_low.reshape(rows_here, block, H, HD)
    value_heads = value_low.reshape(rows_here, block, H, HD)
    segment, valid = segment_table(lengths)
    key_segment = lax.dynamic_slice_in_dim(segment, kv_place * block, block, 1)
    key_valid = lax.dynamic_slice_in_dim(valid, kv_place * block, block, 1)
    queries_all = lax.all_gather(
        query_low.reshape(rows_here, block, width), "kv", axis=1, tiled=True
    )
    which = 0
    query_rows = queries_all[which]
    query_segment = segment[which]
    sigmoid_part, allowed = score_block(
        query_rows,
        key_heads[which],
        query_segment,
        key_segment[which],
        key_valid[which],
        jnp.int32(0),
        key_places,
    )
    weight = (sigmoid_part * allowed).astype(jnp.bfloat16)
    summed = jnp.einsum(
        "hqk,khd->qhd", weight, value_heads[which], preferred_element_type=jnp.float32
    )
    pieces = [
        lax.psum_scatter(
            summed.reshape(lax.axis_size("kv") * block, width).astype(jnp.bfloat16),
            "kv",
            scatter_dimension=0,
            tiled=True,
        ).astype(jnp.float32)
    ]
    attended_low = jnp.stack(pieces).reshape(count, width).astype(jnp.bfloat16)
    resid = flat + jnp.dot(attended_low, full_out, preferred_element_type=jnp.float32)
    normed_mlp, inverse_mlp = norm_forward(resid, full_gain_mlp)
    normed_mlp_low = normed_mlp.astype(jnp.bfloat16)
    upstream_low = cotangent.reshape(count, width)
    upstream = upstream_low.astype(jnp.float32)
    slice_gate, slice_up, slice_down = (
        lax.all_gather(w_gate, "row", axis=1, tiled=True),
        lax.all_gather(w_up, "row", axis=1, tiled=True),
        lax.all_gather(w_down, "row", axis=0, tiled=True),
    )
    row_normed, row_upstream = (
        lax.all_gather(normed_mlp_low.reshape(rows_here, block, width), "kv", axis=1, tiled=True),
        lax.all_gather(cotangent, "kv", axis=1, tiled=True),
    )
    normed_rows = row_normed.reshape(rows_here * LEN, width)
    upstream_rows = row_upstream.reshape(rows_here * LEN, width)
    gate = jnp.dot(normed_rows, slice_gate, preferred_element_type=jnp.float32)
    up_part = jnp.dot(normed_rows, slice_up, preferred_element_type=jnp.float32)
    sigmoid_gate = jax.nn.sigmoid(gate)
    hidden_low = (gate * sigmoid_gate * up_part).astype(jnp.bfloat16)
    hidden_rows = hidden_low.reshape(rows_here, LEN, hidden_low.shape[1])
    which = 0
    hidden_part = hidden_rows[which]
    outputs = [
        lax.psum_scatter(
            jnp.dot(hidden_part, slice_down, preferred_element_type=jnp.float32).astype(
                jnp.bfloat16
            ),
            "kv",
            scatter_dimension=0,
            tiled=True,
        ).astype(jnp.float32)
    ]
    result = resid + jnp.stack(outputs).reshape(count, width)
    d_hidden = contract_cols(upstream_rows, slice_down)
    d_gate, d_up = gate_backward(d_hidden, gate, up_part, sigmoid_gate)
    partial_normed = contract_cols(d_gate, slice_gate) + contract_cols(d_up, slice_up)
    d_normed_mlp = (
        lax.psum_scatter(
            partial_normed.reshape(rows_here, LEN, width).astype(jnp.bfloat16),
            "kv",
            scatter_dimension=1,
            tiled=True,
        )
        .astype(jnp.float32)
        .reshape(count, width)
    )
    grad_gate, grad_up, grad_down = (
        lax.psum_scatter(
            contract_rows(normed_rows, d_gate).astype(jnp.bfloat16),
            "row",
            scatter_dimension=1,
            tiled=True,
        ).astype(jnp.float32),
        lax.psum_scatter(
            contract_rows(normed_rows, d_up).astype(jnp.bfloat16),
            "row",
            scatter_dimension=1,
            tiled=True,
        ).astype(jnp.float32),
        lax.psum_scatter(
            contract_rows(hidden_low, upstream_rows).astype(jnp.bfloat16),
            "row",
            scatter_dimension=0,
            tiled=True,
        ).astype(jnp.float32),
    )
    mixed = result.astype(jnp.bfloat16).reshape(rows_here, block, width)
    back_mlp, gain_mlp_term = norm_backward(resid, inverse_mlp, full_gain_mlp, d_normed_mlp)
    d_resid = upstream + back_mlp
    d_resid_low = d_resid.astype(jnp.bfloat16)
    d_attended = contract_cols(d_resid_low, full_out).astype(jnp.bfloat16)
    grads_all = lax.all_gather(
        d_attended.reshape(rows_here, block, width), "kv", axis=1, tiled=True
    )
    query_block = min(512, LEN)
    block_count = LEN // query_block
    which = 0

    def sweep(carry, index, which=which):
        key_total, value_total = carry
        start = index * query_block
        query_rows = lax.dynamic_slice_in_dim(queries_all[which], start, query_block, 0)
        grad_rows = lax.dynamic_slice_in_dim(grads_all[which], start, query_block, 0)
        query_segment = lax.dynamic_slice_in_dim(segment[which], start, query_block, 0)
        sigmoid_part, allowed = score_block(
            query_rows,
            key_heads[which],
            query_segment,
            key_segment[which],
            key_valid[which],
            start,
            key_places,
        )
        weight = (sigmoid_part * allowed).astype(jnp.bfloat16)
        grad_heads = grad_rows.reshape(query_block, H, HD)
        value_total = value_total + jnp.einsum(
            "hqk,qhd->khd", weight, grad_heads, preferred_element_type=jnp.float32
        )
        d_weight = jnp.einsum(
            "qhd,khd->hqk", grad_heads, value_heads[which], preferred_element_type=jnp.float32
        )
        d_score = (d_weight * sigmoid_part * (1.0 - sigmoid_part) * allowed).astype(jnp.bfloat16)
        query_part = (
            jnp.einsum(
                "hqk,khd->qhd", d_score, key_heads[which], preferred_element_type=jnp.float32
            )
            * scale
        )
        key_total = (
            key_total
            + jnp.einsum(
                "hqk,qhd->khd",
                d_score,
                query_rows.reshape(query_block, H, HD),
                preferred_element_type=jnp.float32,
            )
            * scale
        )
        return ((key_total, value_total), query_part.reshape(query_block, width))

    zeros = jnp.zeros((block, H, HD), jnp.float32)
    totals, query_parts = lax.scan(sweep, (zeros, zeros), jnp.arange(block_count, dtype=jnp.int32))
    query_terms = [query_parts.reshape(LEN, width)]
    key_grads = [totals[0].reshape(block, width)]
    value_grads = [totals[1].reshape(block, width)]
    query_local = lax.psum_scatter(
        jnp.stack(query_terms).astype(jnp.bfloat16), "kv", scatter_dimension=1, tiled=True
    ).astype(jnp.float32)
    d_query_low = query_local.reshape(count, width).astype(jnp.bfloat16)
    d_key_low = jnp.stack(key_grads).reshape(count, width).astype(jnp.bfloat16)
    d_value_low = jnp.stack(value_grads).reshape(count, width).astype(jnp.bfloat16)
    d_normed_attn = (
        contract_cols(d_query_low, full_query)
        + contract_cols(d_key_low, full_key)
        + contract_cols(d_value_low, full_value)
    )
    back_attn, gain_attn_term = norm_backward(flat, inverse_attn, full_gain_attn, d_normed_attn)
    grad_tokens = (d_resid + back_attn).reshape(rows_here, block, width)
    projected_low = jnp.concatenate((d_query_low, d_key_low, d_value_low), axis=1)
    grad_projections = lax.psum_scatter(
        contract_rows(normed_attn_low, projected_low),
        ("row", "kv"),
        scatter_dimension=0,
        tiled=True,
    )
    out_term = contract_rows(attended_low, d_resid_low)
    grad_out, grad_gain_attn, grad_gain_mlp = (
        lax.psum_scatter(out_term, ("row", "kv"), scatter_dimension=0, tiled=True),
        lax.psum_scatter(gain_attn_term, ("row", "kv"), scatter_dimension=0, tiled=True),
        lax.psum_scatter(gain_mlp_term, ("row", "kv"), scatter_dimension=0, tiled=True),
    )
    grad_query = grad_projections[:, :width]
    grad_key = grad_projections[:, width : 2 * width]
    grad_value = grad_projections[:, 2 * width :]
    return (
        mixed,
        grad_tokens,
        grad_query,
        grad_key,
        grad_value,
        grad_out,
        grad_gate,
        grad_up,
        grad_down,
        grad_gain_attn,
        grad_gain_mlp,
    )


def solution(mesh):
    rows, columns = mesh.shape["row"], mesh.shape["kv"]
    if rows == 4 and columns == 2 * rows:
        mesh = Mesh(mesh.devices.reshape(2, 2, rows, 2), ("y", "c", "z", "x"))
        row, kv, run = ("y", "c"), ("z", "x"), body_layers
    else:
        row, kv, run = "row", "kv", body_any
    both = ("y", "c", "z", "x") if run is body_layers else ("row", "kv")
    tall, wide, flat = P(both, None), P(None, both), P(both)
    tokens = P(row, kv, None)
    return jax.shard_map(
        run,
        mesh=mesh,
        in_specs=(tokens, P(row, None), tokens, tall, tall, tall, tall, wide, wide, tall, flat, flat),
        out_specs=(tokens, tokens, tall, tall, tall, tall, wide, wide, tall, flat, flat),
        check_vma=False,
    )
```

```python
import functools
import math

import jax
import jax.numpy as jnp
from jax import lax
from jax.experimental import pallas as pl
from jax.experimental.pallas import tpu as pltpu
from jax.sharding import Mesh, PartitionSpec as P

H = 16
HD = 128
LEN = 4096


EPSILON = 1e-05


def contract_rows(left, right):
    return lax.dot_general(
        left, right, (((0,), (0,)), ((), ())), preferred_element_type=jnp.float32
    )


def contract_cols(left, right):
    return lax.dot_general(
        left, right, (((1,), (1,)), ((), ())), preferred_element_type=jnp.float32
    )


def norm_forward(value, gain):
    inverse = lax.rsqrt(jnp.mean(value * value, axis=-1, keepdims=True) + EPSILON)
    return (value * inverse * gain.astype(jnp.float32), inverse)


def norm_backward(value, inverse, gain, upstream):
    scaled = upstream * gain.astype(jnp.float32)
    inner = jnp.mean(scaled * value, axis=-1, keepdims=True)
    back = inverse * scaled - value * (inverse * inverse * inverse) * inner
    gain_term = jnp.sum(upstream * value * inverse, axis=0)
    return (back, gain_term)


def segment_table(lengths):
    ends = jnp.cumsum(lengths, axis=-1)
    places = jnp.arange(LEN, dtype=jnp.int32)
    segment = jnp.sum((ends[:, None, :] <= places[None, :, None]).astype(jnp.int32), axis=-1)
    valid = places[None, :] < ends[:, -1:]
    return (segment, valid)


def score_block(
    query_rows, key_heads, query_segment, key_segment, key_valid, query_start, key_places
):
    count = query_rows.shape[0]
    query_heads = query_rows.reshape(count, H, HD)
    raw = jnp.einsum("qhd,khd->hqk", query_heads, key_heads, preferred_element_type=jnp.float32)
    scores = raw * (1.0 / math.sqrt(HD)) - math.log(LEN)
    places = query_start + jnp.arange(count, dtype=jnp.int32)
    allowed = (
        (key_places[None, :] <= places[:, None])
        & (key_segment[None, :] == query_segment[:, None])
        & key_valid[None, :]
    )
    return (jax.nn.sigmoid(scores), allowed.astype(jnp.float32)[None])


def gate_backward(d_hidden, gate, up_part, sigmoid_gate):
    d_gate = (d_hidden * up_part * sigmoid_gate * (1.0 + gate * (1.0 - sigmoid_gate))).astype(
        jnp.bfloat16
    )
    d_up = (d_hidden * gate * sigmoid_gate).astype(jnp.bfloat16)
    return (d_gate, d_up)


TILE = 512
LOW = jnp.bfloat16
VMEM_LIMIT = 60 * 1024 * 1024


def dot_nt(left, right):
    return lax.dot_general(left, right, (((1,), (1,)), ((), ())), preferred_element_type=jnp.float32)


def dot_wide(left, right):
    return jnp.dot(left, right, preferred_element_type=jnp.float32)


HALF = TILE // 2
PIECES = 4
CHUNK = 32
MESH_ID = pl.DeviceIdType.MESH


def flip(bit, by):
    return bit + by - 2 * bit * by


def spot():
    return tuple(lax.axis_index(name) for name in ("y", "c", "z", "x"))


def near():
    y, c, z, x = spot()
    return (y, c, z, 1 - x), (1 - y, c, z, x), (y, 1 - c, z, x)


def partner_of(y, c, z, x):
    return lax.rem(z, 2), z // 2, 2 * c + y, x


def place_of(y, c, x, half=None):
    first = (4 * c + 2 * y + x) * TILE
    if half is None:
        return pl.ds(pl.multiple_of(first, TILE), TILE)
    return pl.ds(pl.multiple_of(first + half * HALF, HALF), HALF)


def quarter_of(y, c, x, half, quarter):
    return pl.ds(pl.multiple_of((4 * c + 2 * y + x) * TILE + half * HALF + quarter * (HALF // 2), HALF // 2), HALF // 2)


def remote(src, dst, send, recv, peer):
    return pltpu.make_async_remote_copy(
        src_ref=src, dst_ref=dst, send_sem=send, recv_sem=recv, device_id=peer, device_id_type=MESH_ID
    )


def greet(peers):
    barrier = pltpu.get_barrier_semaphore()
    for peer in peers:
        pl.semaphore_signal(barrier, inc=1, device_id=peer, device_id_type=MESH_ID)
    pl.semaphore_wait(barrier, len(peers))


class Gather:
    def __init__(self, own, whole, send, recv):
        y, c, z, x = spot()
        across_x, across_y, core = near()

        def passed(k, at, peer):
            return remote(whole.at[at], whole.at[at], send.at[k], recv.at[k], peer)

        self.halves = []
        for half in (0, 1):
            k, at = 9 * half, place_of(y, c, x, half)
            mine = [
                remote(own(half), whole.at[at], send.at[k + m], recv.at[k + m], peer)
                for m, peer in enumerate((across_x, across_y, core))
            ]
            held_x, held_y = (y, c, 1 - x), (1 - y, c, x)
            far = (1 - y, c, 1 - x)
            self.halves.append(
                (
                    mine,
                    passed(k + 3, quarter_of(*held_x, half, 0), across_y),
                    passed(k + 4, quarter_of(*held_y, half, 1), across_x),
                    [passed(k + 5, place_of(*held_x, half), core), passed(k + 6, place_of(*held_y, half), core)],
                    [passed(k + 7 + q, quarter_of(*far, half, q), core) for q in (0, 1)],
                )
            )

    def start(self, half):
        for copy in self.halves[half][0]:
            copy.start()

    def pass_near(self, half):
        mine, over_y, over_x, from_near, from_far = self.halves[half]
        mine[0].wait_recv()
        over_y.start()
        from_near[0].start()
        mine[1].wait_recv()
        over_x.start()
        from_near[1].start()

    def pass_far(self, half):
        mine, over_y, over_x, from_near, from_far = self.halves[half]
        over_y.wait_recv()
        from_far[0].start()
        over_x.wait_recv()
        from_far[1].start()

    def finish(self):
        for mine, over_y, over_x, from_near, from_far in self.halves:
            for copy in [mine[2]] + from_near + from_far:
                copy.wait_recv()
            for copy in mine + [over_y, over_x] + from_near + from_far:
                copy.wait_send()


GATHER_COPIES = 18


class GatherWhole:
    def __init__(self, own, whole, send, recv):
        y, c, z, x = spot()
        across_x, across_y, core = near()

        def from_own(k, half, peer):
            return remote(own(half), whole.at[place_of(y, c, x, half)], send.at[k], recv.at[k], peer)

        def passed(k, at, peer):
            return remote(whole.at[at], whole.at[at], send.at[k], recv.at[k], peer)

        self.mine = [
            [from_own(0, 0, across_x), from_own(1, 0, across_y), from_own(2, 0, core)],
            [from_own(3, 1, across_x), from_own(4, 1, across_y), from_own(5, 1, core)],
        ]
        held_x = [place_of(y, c, 1 - x, half) for half in (0, 1)]
        held_y = [place_of(1 - y, c, x, half) for half in (0, 1)]
        far = [place_of(1 - y, c, 1 - x, half) for half in (0, 1)]
        self.over_y, self.over_x = passed(6, held_x[0], across_y), passed(7, held_y[1], across_x)
        self.core_x = [passed(8 + half, held_x[half], core) for half in (0, 1)]
        self.core_y = [passed(10 + half, held_y[half], core) for half in (0, 1)]
        self.core_far = [passed(12 + half, far[half], core) for half in (0, 1)]

    def start(self, half):
        for copy in self.mine[half]:
            copy.start()

    def pass_first(self):
        self.mine[0][0].wait_recv()
        self.over_y.start()
        self.core_x[0].start()
        self.mine[0][1].wait_recv()
        self.core_y[0].start()

    def pass_second(self):
        self.mine[1][1].wait_recv()
        self.over_x.start()
        self.core_y[1].start()
        self.mine[1][0].wait_recv()
        self.core_x[1].start()

    def pass_far(self):
        self.over_y.wait_recv()
        self.core_far[0].start()
        self.over_x.wait_recv()
        self.core_far[1].start()

    def finish(self):
        from_core = [self.mine[0][2], self.mine[1][2]] + self.core_x + self.core_y + self.core_far
        for copy in from_core:
            copy.wait_recv()
        for copy in self.mine[0] + self.mine[1] + [self.over_y, self.over_x] + self.core_x + self.core_y + self.core_far:
            copy.wait_send()


class Trade:
    def __init__(self, sources, dst, held, send, recv, held_recv, pass_send, detour=True):
        y, c, z, x = spot()
        self.detour = detour
        across_y = (1 - y, c, z, x)
        self.moves = z != 2 * c + y
        self.away = (y == c) & (z == 1 + y)
        self.straight = self.moves & jnp.logical_not(self.away) if detour else self.moves
        self.passes = (1 - y == c) & (z == 2 - y)
        partner = partner_of(y, c, z, x)
        comes_by = ((partner[0] == partner[1]) & (partner[2] == 1 + partner[0])).astype(jnp.int32)
        self.sender = (flip(partner[0], comes_by), partner[1], partner[2], x) if detour else partner
        self.across_y = across_y
        target = partner_of(*across_y)
        self.direct, self.keep, self.out, self.onward = [], [], [], []
        for h, source in enumerate(sources):
            self.direct.append(remote(source, dst(h, partner), send.at[h], recv.at[h], partner))
            self.keep.append(pltpu.make_async_copy(source, dst(h, (y, c, z, x)), recv.at[h]))
            self.out.append(remote(source, held.at[h], send.at[h], held_recv.at[h], across_y))
            self.onward.append(remote(held.at[h], dst(h, target), pass_send.at[h], recv.at[h], target))

    def greet(self, barrier, neighbours_greet):
        @pl.when(self.moves)
        def _():
            pl.semaphore_signal(barrier, inc=1, device_id=self.sender, device_id_type=MESH_ID)

        count = self.straight.astype(jnp.int32)
        if not self.detour:
            return count
        count = count + self.passes.astype(jnp.int32)
        if not neighbours_greet:

            @pl.when(self.passes)
            def _():
                pl.semaphore_signal(barrier, inc=1, device_id=self.across_y, device_id_type=MESH_ID)

            count = count + self.away.astype(jnp.int32)
        return count

    def start(self, h):
        @pl.when(self.straight)
        def _():
            self.direct[h].start()

        if self.detour:

            @pl.when(self.away)
            def _():
                self.out[h].start()

        @pl.when(jnp.logical_not(self.moves))
        def _():
            self.keep[h].start()

    def wait_sent(self, h):
        @pl.when(self.straight)
        def _():
            self.direct[h].wait_send()

        if self.detour:

            @pl.when(self.away)
            def _():
                self.out[h].wait_send()

    def forward(self, h):
        if self.detour:

            @pl.when(self.passes)
            def _():
                self.out[h].wait_recv()
                self.onward[h].start()

    def arrive(self, h):
        @pl.when(self.moves)
        def _():
            self.direct[h].wait_recv()

        @pl.when(jnp.logical_not(self.moves))
        def _():
            self.keep[h].wait()

    def finish(self, first=0):
        for h in range(len(self.direct)):
            if h >= first:
                self.wait_sent(h)

            if self.detour:

                @pl.when(self.passes)
                def _():
                    self.onward[h].wait_send()


def trade_scratch(pieces, rows, width):
    return [pltpu.VMEM((pieces, rows, width), LOW)] + [pltpu.SemaphoreType.DMA((pieces,)) for _ in range(4)]


class Chain:
    def __init__(self, own, slab, sems, index):
        self.own, self.slab, self.sems, self.index = own, slab, sems, index
        self.last = lax.axis_size("z") - 1

    def move(self, which, h, source, layer, to):
        y, c, z, x = spot()
        return remote(
            source, self.slab(layer), self.sems[2 * which].at[self.index, h], self.sems[2 * which + 1].at[self.index, h], (y, c, to, x)
        )

    def up(self, h):
        z = lax.axis_index("z")
        return self.move(0, h, self.own if h == 0 else self.slab(z - h), z - h, z + 1)

    def down(self, h):
        z = lax.axis_index("z")
        return self.move(1, h, self.own if h == 0 else self.slab(z + h), z + h, z - 1)

    def start(self):
        z = lax.axis_index("z")

        @pl.when(z < self.last)
        def _():
            self.up(0).start()

        @pl.when(z > 0)
        def _():
            self.down(0).start()

    def arrive(self, h):
        z = lax.axis_index("z")

        @pl.when(z - h - 1 >= 0)
        def _():
            self.move(0, h, self.slab(z - h - 1), z - h - 1, z).wait_recv()
            if h < 2:

                @pl.when(z < self.last)
                def _():
                    self.up(h + 1).start()

        @pl.when(z + h + 1 <= self.last)
        def _():
            self.move(1, h, self.slab(z + h + 1), z + h + 1, z).wait_recv()
            if h < 2:

                @pl.when(z > 0)
                def _():
                    self.down(h + 1).start()

    def finish(self):
        z = lax.axis_index("z")
        for h in range(3):

            @pl.when((z < self.last) & (z - h >= 0))
            def _():
                self.up(h).wait_send()

            @pl.when((z > 0) & (z + h <= self.last))
            def _():
                self.down(h).wait_send()


def chain_sems(count):
    return [pltpu.SemaphoreType.DMA((count, 3)) for _ in range(4)]


def greet_neighbours(peers):
    y, c, z, x = spot()
    last = lax.axis_size("z") - 1
    barrier = pltpu.get_barrier_semaphore()
    for peer in peers:
        pl.semaphore_signal(barrier, inc=1, device_id=peer, device_id_type=MESH_ID)

    @pl.when(z > 0)
    def _():
        pl.semaphore_signal(barrier, inc=1, device_id=(y, c, z - 1, x), device_id_type=MESH_ID)

    @pl.when(z < last)
    def _():
        pl.semaphore_signal(barrier, inc=1, device_id=(y, c, z + 1, x), device_id_type=MESH_ID)

    return barrier, len(peers) + (z > 0).astype(jnp.int32) + (z < last).astype(jnp.int32)


def others():
    y, c, z, x = spot()
    return [(flip(y, dy), flip(c, dc), z, flip(x, dx)) for dy in (0, 1) for dc in (0, 1) for dx in (0, 1) if dy + dc + dx]


def line_of():
    y, c, z, x = spot()
    return [(y, c, lax.rem(z + dz, 4), x) for dz in (1, 2, 3)]


class Fold:
    def __init__(self, slab, far, near_part, cross, mine, theirs, send, recv, local):
        y, c, z, x = spot()
        a, b = z // 2, lax.rem(z, 2)
        pair, middle = (y, c, 2 * a + 1 - b, x), (y, c, 2 * (1 - a) + b, x)
        self.far = remote(slab(2 * (1 - a) + 1 - b), far, send.at[0], recv.at[0], pair)
        self.near = remote(slab(2 * a + 1 - b), near_part, send.at[1], recv.at[1], pair)
        self.cross = remote(mine, cross, send.at[2], recv.at[2], middle)
        self.fetches = [
            pltpu.make_async_copy(slab(2 * (1 - a) + b), mine, local.at[0]),
            pltpu.make_async_copy(far, theirs, local.at[1]),
        ]
        self.mine, self.theirs = mine, theirs

    def start(self):
        self.far.start()
        self.fetches[0].start()

    def fold(self):
        self.far.wait_recv()
        self.fetches[1].start()
        for copy in self.fetches:
            copy.wait()
        add_rows(self.mine, 0, self.theirs, 0, self.mine.shape[0])
        self.cross.start()
        self.near.start()

    def finish(self):
        for copy in (self.near, self.cross):
            copy.wait_recv()
        for copy in (self.far, self.near, self.cross):
            copy.wait_send()


def columns_of_layer(whole):
    size = whole.shape[1] // 4
    return lambda at: whole.at[:, pl.ds(pl.multiple_of(at * size, size), size)]


def fold_peers():
    y, c, z, x = spot()
    a, b = z // 2, lax.rem(z, 2)
    return ((y, c, 2 * a + 1 - b, x), (y, c, 2 * (1 - a) + b, x))


def add_rows(total, first, term, start, count):
    def step(i, carry):
        here = pl.ds(pl.multiple_of(first + i * CHUNK, CHUNK), CHUNK)
        there = pl.ds(pl.multiple_of(start + i * CHUNK, CHUNK), CHUNK)
        total[here, :] = (total[here, :].astype(jnp.float32) + term[there, :].astype(jnp.float32)).astype(LOW)
        return carry

    lax.fori_loop(0, count // CHUNK, step, 0)


def scatter_scratch(width, parts=1):
    return [
        pltpu.VMEM((2, TILE, width), LOW),
        pltpu.VMEM((4, TILE, width), LOW),
        pltpu.VMEM((4, TILE, width), LOW),
        pltpu.VMEM((2, HALF, width), LOW),
        pltpu.VMEM((2, TILE, width), LOW),
        pltpu.SemaphoreType.DMA((parts, 10)),
        pltpu.SemaphoreType.DMA((parts, 10)),
    ]


class Scatter:
    def __init__(self, produce, staged, core_part, total, relayed, landed, send, recv, part=0, start=0, size=TILE):
        across_x, across_y, core = near()
        self.produce, self.staged, self.core_part, self.total, self.relayed = produce, staged, core_part, total, relayed
        self.start, self.size, self.half = start, size, size // 2
        send, recv = send.at[part], recv.at[part]
        rows = pl.ds(start, size)
        halves = (pl.ds(start, self.half), pl.ds(start + self.half, self.half))
        self.relay_row = start // 2
        passing = pl.ds(self.relay_row, self.half)
        self.to_core = [
            remote(staged.at[k % 2, rows], core_part.at[k, rows], send.at[k], recv.at[k], core) for k in range(4)
        ]
        self.far_x = remote(total.at[0, halves[0]], relayed.at[0, passing], send.at[4], recv.at[4], across_x)
        self.far_y = remote(total.at[0, halves[1]], relayed.at[1, passing], send.at[5], recv.at[5], across_y)
        self.to_x = [
            remote(total.at[1, at], landed.at[0, at], send.at[6 + half], recv.at[6 + half], across_x)
            for half, at in enumerate(halves)
        ]
        self.to_y = [
            remote(total.at[2, at], landed.at[1, at], send.at[8 + half], recv.at[8 + half], across_y)
            for half, at in enumerate(halves)
        ]

    def begin(self):
        y, c, z, x = spot()
        rows = pl.ds(self.start, self.size)
        for k, (to_row, to_column) in enumerate(((1 - y, 1 - x), (y, 1 - x), (1 - y, x), (y, x))):
            if k >= 2:
                self.to_core[k - 2].wait_send()
            self.produce(2 * k, to_row, 1 - c, to_column, self.staged.at[k % 2, rows])
            self.to_core[k].start()
            self.produce(2 * k + 1, to_row, c, to_column, self.total.at[k, rows])
            self.to_core[k].wait_recv()
            add_rows(self.total.at[k], self.start, self.core_part.at[k], self.start, self.size)
            if k == 0:
                self.far_x.start()
                self.far_y.start()
            if k == 1:
                self.to_x[0].start()
            if k == 2:
                self.to_y[1].start()

    def relay(self):
        self.far_y.wait_recv()
        add_rows(self.total.at[1], self.start + self.half, self.relayed.at[1], self.relay_row, self.half)
        self.to_x[1].start()
        self.far_x.wait_recv()
        add_rows(self.total.at[2], self.start, self.relayed.at[0], self.relay_row, self.half)
        self.to_y[0].start()

    def arrive(self):
        for copy in self.to_x + self.to_y:
            copy.wait_recv()

    def finish(self):
        for copy in self.to_core[2:] + [self.far_x, self.far_y] + self.to_x + self.to_y:
            copy.wait_send()


def sum_and_gather(part_of, rows_of_half, gather, beside):
    sums = [part_of(half) for half in (0, 1)]
    sums[0].begin()
    sums[0].relay()
    sums[1].begin()
    sums[0].arrive()
    rows_of_half(0)
    gather.start(0)
    beside(0)
    sums[1].relay()
    beside(1)
    sums[1].arrive()
    rows_of_half(1)
    gather.start(1)
    gather.pass_near(0)
    beside(2)
    gather.pass_near(1)
    gather.pass_far(0)
    gather.pass_far(1)
    gather.finish()
    beside(3)
    for half in (0, 1):
        sums[half].finish()


def begin_kernel(
    x_source, w_query, w_key, w_value, facts, normed_whole, x_own, w_qkv, facts_whole,
    held, normed, gather_send, gather_recv, w_send, w_recv, fact_send, fact_recv, local, *scratch
):
    y, c, z, x = spot()
    row = 2 * y + c
    layer = others()
    trade_parts, sems = scratch[:5], scratch[5:]
    trade = Trade([x_source.at[half] for half in (0, 1)], lambda half, at: held.at[half], *trade_parts, detour=False)
    barrier, count = greet_neighbours(layer)
    pl.semaphore_wait(barrier, count + trade.greet(barrier, True))

    shard = w_query.shape[0]
    for half in (0, 1):
        trade.start(half)
    spread = [
        remote(facts, facts_whole.at[row, z, x], fact_send.at[k], fact_recv.at[k], peer) for k, peer in enumerate(layer)
    ]
    kept = [pltpu.make_async_copy(facts, facts_whole.at[row, z, x], local.at[6])]
    for m in range(6):
        source, slot = (w_query, w_key, w_value)[m // 2], m % 2

        def columns_of(at):
            head = 4 * (2 * at[0] + at[1]) + (3 - at[3] if slot else at[3])
            return source.at[:, pl.ds(pl.multiple_of(head * HD, HD), HD)]

        dst = w_qkv.at[row, z, pl.ds(pl.multiple_of(x * shard, shard), shard), pl.ds(m * HD, HD)]
        for k, peer in enumerate(layer):
            spread.append(remote(columns_of(peer), dst, w_send.at[m, k], w_recv.at[m, k], peer))
        kept.append(pltpu.make_async_copy(columns_of((y, c, z, x)), dst, local.at[m]))
    for copy in spread + kept:
        copy.start()

    gather = GatherWhole(lambda half: normed.at[half], normed_whole, gather_send, gather_recv)
    outs = []
    for half in (0, 1):
        trade.arrive(half)

        def step(i, carry):
            here = pl.ds(pl.multiple_of(i * CHUNK, CHUNK), CHUNK)
            value = held[half, here, :].astype(jnp.float32)
            normed[half, here, :] = (value * inverse_of(value)).astype(LOW)
            return carry

        lax.fori_loop(0, HALF // CHUNK, step, 0)
        gather.start(half)
        outs.append(pltpu.make_async_copy(held.at[half], x_own.at[pl.ds(half * HALF, HALF)], local.at[7 + half]))
        outs.append(pltpu.make_async_copy(normed.at[half], normed_whole.at[place_of(y, c, x, half)], local.at[9 + half]))
        outs[-2].start()
        outs[-1].start()

    for copy in kept:
        copy.wait()
    for copy in spread:
        copy.wait_recv()
    chains = [
        Chain(facts_whole.at[:, z], lambda at: facts_whole.at[:, at], sems, 0),
        Chain(w_qkv.at[:, z], lambda at: w_qkv.at[:, at], sems, 1),
    ]

    def arrive(h):
        for chain in chains:
            chain.arrive(h)

    for chain in chains:
        chain.start()
    gather.pass_first()
    arrive(0)
    gather.pass_second()
    arrive(1)
    gather.pass_far()
    arrive(2)
    gather.finish()
    trade.finish()
    for copy in spread:
        copy.wait_send()
    for chain in chains:
        chain.finish()
    for copy in outs:
        copy.wait()


def anywhere():
    return pl.BlockSpec(memory_space=pl.ANY)


def in_vmem():
    return pl.BlockSpec(memory_space=pltpu.VMEM)


def dma(*shape):
    return pltpu.SemaphoreType.DMA(shape)


def remote_params(number):
    return pltpu.CompilerParams(collective_id=number, has_side_effects=True, vmem_limit_bytes=VMEM_LIMIT)


def begin(x_source, w_query, w_key, w_value, facts):
    block, width = x_source.shape
    shard = w_query.shape[0]
    whole_facts = (4, 4, 2, *facts.shape)
    normed_whole, x_own, w_qkv, facts_whole = pl.pallas_call(
        begin_kernel,
        out_shape=(
            jax.ShapeDtypeStruct((8 * block, width), LOW),
            jax.ShapeDtypeStruct((block, width), LOW),
            jax.ShapeDtypeStruct((4, 4, 2 * shard, 3 * width // 8), LOW),
            jax.ShapeDtypeStruct(whole_facts, jnp.float32),
        ),
        in_specs=[in_vmem()] + [anywhere()] * 4,
        out_specs=[anywhere()] * 4,
        scratch_shapes=[
            pltpu.VMEM((2, block // 2, width), LOW),
            pltpu.VMEM((2, block // 2, width), LOW),
            dma(14), dma(14), dma(6, 7), dma(6, 7), dma(7), dma(7), dma(11),
            *trade_scratch(2, block // 2, width), *chain_sems(2),
        ],
        compiler_params=remote_params(1),
        cost_estimate=pl.CostEstimate(flops=0, bytes_accessed=350_000_000, transcendentals=0),
    )(x_source.reshape(2, block // 2, width), w_query, w_key, w_value, facts)
    return normed_whole, x_own, w_qkv.reshape(width, 3 * width // 8), facts_whole


def summed(total, landed, here):
    parts = (total[3, here, :], landed[0, here, :], landed[1, here, :])
    return sum(part.astype(jnp.float32) for part in parts)


def over_chunks(work, half):
    def step(i, carry):
        work(pl.ds(pl.multiple_of(half * HALF + i * CHUNK, CHUNK), CHUNK))
        return carry

    lax.fori_loop(0, HALF // CHUNK, step, 0)


def own_halves(own):
    return lambda half: own.at[pl.ds(half * HALF, HALF)]


def inverse_of(value):
    return lax.rsqrt(jnp.mean(value * value, axis=-1, keepdims=True) + EPSILON)


def close_attention_kernel(attended, w_out, x_home, gain, w_gate, w_up, resid, normed, own_gate, own_up, own, x_own, *scratch):
    scatter, (send, recv, local), sems = scratch[:7], scratch[7:10], scratch[10:]
    y, c, z, x = spot()
    fetch_x = pltpu.make_async_copy(x_home, x_own, local.at[0])
    fetch_x.start()
    width = w_out.shape[1]
    hidden = w_gate.shape[1]
    z = lax.axis_index("z")
    barrier, count = greet_neighbours(near())
    pl.semaphore_wait(barrier, count)

    def slab_of(whole):
        return lambda at: whole.at[:, pl.ds(pl.multiple_of(at * hidden, hidden), hidden)]

    chains, kept = [], []
    for k, (part, whole) in enumerate(((w_gate, own_gate), (w_up, own_up))):
        chains.append(Chain(part, slab_of(whole), sems, k))
        chains[k].start()
        kept.append(pltpu.make_async_copy(part, slab_of(whole)(z), local.at[1 + k]))
        kept[k].start()

    def arrive(h):
        for chain in chains:
            chain.arrive(h)

    def part_of(half):
        def produce(turn, y, c, x, out):
            at = place_of(y, c, x, half)

            def step(i, carry):
                columns = pl.ds(pl.multiple_of(i * TILE, TILE), TILE)
                out[:, columns] = dot_wide(attended[at, :], w_out[:, columns]).astype(LOW)
                return carry

            lax.fori_loop(0, width // TILE, step, 0)

        return Scatter(produce, *scatter, part=half, start=half * HALF, size=HALF)

    total, landed = scatter[2], scatter[4]

    def chunk(here):
        value = x_own[here, :].astype(jnp.float32) + summed(total, landed, here)
        resid[here, :] = value
        own[here, :] = (value * inverse_of(value) * gain[...]).astype(LOW)

    def rows_of_half(half):
        if half == 0:
            fetch_x.wait()
        over_chunks(chunk, half)

    gather = Gather(own_halves(own), normed, send, recv)
    sum_and_gather(part_of, rows_of_half, gather, lambda turn: arrive(turn - 1) if turn > 0 else None)
    keep = pltpu.make_async_copy(own, normed.at[place_of(y, c, x)], local.at[0])
    keep.start()
    for chain in chains:
        chain.finish()
    for copy in kept + [keep]:
        copy.wait()


def close_attention(attended, w_out, x_home, gain, w_gate, w_up):
    block, width = x_home.shape
    hidden = w_gate.shape[1]
    return pl.pallas_call(
        close_attention_kernel,
        out_shape=(
            jax.ShapeDtypeStruct((block, width), jnp.float32),
            jax.ShapeDtypeStruct((8 * block, width), LOW),
            jax.ShapeDtypeStruct((width, 4 * hidden), LOW),
            jax.ShapeDtypeStruct((width, 4 * hidden), LOW),
        ),
        in_specs=[in_vmem(), in_vmem(), anywhere()] + [in_vmem()] * 3,
        out_specs=[in_vmem()] + [anywhere()] * 3,
        scratch_shapes=[pltpu.VMEM((block, width), LOW)] * 2
        + scatter_scratch(width, 2)
        + [dma(GATHER_COPIES), dma(GATHER_COPIES), dma(3), *chain_sems(2)],
        compiler_params=remote_params(2),
        cost_estimate=pl.CostEstimate(flops=0, bytes_accessed=450_000_000, transcendentals=0),
    )(attended, w_out, x_home, gain, w_gate, w_up)


def norm_back(value, gain, upstream):
    inverse = inverse_of(value)
    scaled = upstream * gain
    inner = jnp.mean(scaled * value, axis=-1, keepdims=True)
    return inverse * scaled - value * (inverse * inverse * inverse) * inner, upstream * value * inverse


def fold_rows(total, terms):
    for first in range(0, CHUNK, 8):
        total[...] += terms[first : first + 8, :]


def close_mlp_kernel(
    d_gate, d_up, w_gate, w_up, resid, upstream, gain, grad_a, grad_b, d_resid, gain_term, d_resid_whole,
    far_a, near_a, cross_a, far_b, near_b, cross_b, own, blocks, *scratch
):
    scatter, (send, recv, local, fetched, fold_send, fold_recv, fold_local, mine, theirs) = scratch[:7], scratch[7:]
    y, c, z, x = spot()
    width = w_gate.shape[0]
    order = [
        place_of(r, k, q, half)
        for half in (0, 1)
        for r, q in ((1 - y, 1 - x), (y, 1 - x), (1 - y, x), (y, x))
        for k in (1 - c, c)
    ]

    def fetch(turn):
        slot = turn % 2
        return [
            pltpu.make_async_copy(source.at[order[turn]], blocks.at[slot, m], fetched.at[slot, m])
            for m, source in enumerate((d_gate, d_up))
        ]

    for copy in fetch(0):
        copy.start()
    greet(near() + fold_peers())
    folds = [
        Fold(columns_of_layer(grad), *refs, mine.at[k], theirs, fold_send.at[k], fold_recv.at[k], fold_local.at[k])
        for k, (grad, *refs) in enumerate(((grad_a, far_a, near_a, cross_a), (grad_b, far_b, near_b, cross_b)))
    ]
    for fold in folds:
        fold.start()

    def part_of(half):
        def produce(turn, to_y, to_c, to_x, out):
            turn = turn + 8 * half
            if turn < 15:
                for copy in fetch(turn + 1):
                    copy.start()
            for copy in fetch(turn):
                copy.wait()

            def step(i, carry):
                columns = pl.ds(pl.multiple_of(i * TILE, TILE), TILE)
                part = dot_nt(blocks[turn % 2, 0], w_gate[columns, :]) + dot_nt(blocks[turn % 2, 1], w_up[columns, :])
                out[:, columns] = part.astype(LOW)
                return carry

            lax.fori_loop(0, width // TILE, step, 0)

        return Scatter(produce, *scatter, part=half, start=half * HALF, size=HALF)

    total, landed = scatter[2], scatter[4]
    gain_term[...] = jnp.zeros_like(gain_term)

    def chunk(here):
        back, terms = norm_back(resid[here, :], gain[...], summed(total, landed, here))
        value = upstream[here, :].astype(jnp.float32) + back
        d_resid[here, :] = value
        own[here, :] = value.astype(LOW)
        fold_rows(gain_term, terms)

    def rows_of_half(half):
        over_chunks(chunk, half)

    gather = Gather(own_halves(own), d_resid_whole, send, recv)
    sum_and_gather(part_of, rows_of_half, gather, lambda turn: folds[turn].fold() if turn < 2 else None)
    keep = pltpu.make_async_copy(own, d_resid_whole.at[place_of(y, c, x)], local.at[0])
    keep.start()
    for fold in folds:
        fold.finish()
    keep.wait()


def close_mlp(d_gate, d_up, w_gate, w_up, resid, upstream, gain, *grads):
    block, width = resid.shape
    hidden = d_gate.shape[1]
    return pl.pallas_call(
        close_mlp_kernel,
        out_shape=(
            jax.ShapeDtypeStruct((block, width), jnp.float32),
            jax.ShapeDtypeStruct((8, width), jnp.float32),
            jax.ShapeDtypeStruct((8 * block, width), LOW),
            *[jax.ShapeDtypeStruct((width, hidden // 4), LOW)] * 6,
        ),
        in_specs=[anywhere()] * 2 + [in_vmem()] * 5 + [anywhere()] * 2,
        out_specs=[in_vmem(), in_vmem()] + [anywhere()] * 7,
        scratch_shapes=[pltpu.VMEM((block, width), LOW), pltpu.VMEM((2, 2, block // 2, hidden), LOW)]
        + scatter_scratch(width, 2)
        + [dma(GATHER_COPIES), dma(GATHER_COPIES), dma(1), dma(2, 2), dma(2, 3), dma(2, 3), dma(2, 2)]
        + [pltpu.VMEM((2, width, hidden // 4), LOW), pltpu.VMEM((width, hidden // 4), LOW)],
        compiler_params=remote_params(3),
        cost_estimate=pl.CostEstimate(flops=0, bytes_accessed=450_000_000, transcendentals=0),
    )(d_gate, d_up, w_gate, w_up, resid, upstream, gain, *grads)


def close_layer_kernel(
    d_qkv, w_qkv, x_home, d_resid, gain, mlp_term, grad, grad_low, gain_grads, far, near_part, cross, grad_parts, own, terms, layer_terms, part, column_terms, *scratch
):
    scatter, (send, recv, term_send, term_recv, line_send, line_recv, x_own, x_sem, *rest) = scratch[:7], scratch[7:]
    mine, theirs, fold_send, fold_recv, fold_local, part_send, part_recv = rest
    y, c, z, x = spot()
    fetch_x = pltpu.make_async_copy(x_home, x_own, x_sem.at[0])
    fetch_x.start()
    partner = partner_of(y, c, z, x)
    moves = z != 2 * c + y
    width = w_qkv.shape[0]
    barrier = pltpu.get_barrier_semaphore()

    @pl.when(moves)
    def _():
        pl.semaphore_signal(barrier, inc=1, device_id=partner, device_id_type=MESH_ID)

    layer = others()
    line = line_of()
    for peer in layer + line:
        pl.semaphore_signal(barrier, inc=1, device_id=peer, device_id_type=MESH_ID)
    pl.semaphore_wait(barrier, len(layer + line) + moves.astype(jnp.int32))

    size = TILE // PIECES

    def part_of(piece):
        def produce(turn, to_y, to_c, to_x, out):
            at = quarter_of(to_y, to_c, to_x, piece // 2, piece % 2)

            def step(i, carry):
                columns = pl.ds(pl.multiple_of(i * TILE, TILE), TILE)
                out[:, columns] = dot_nt(d_qkv[at, :], w_qkv[columns, :]).astype(LOW)
                return carry

            lax.fori_loop(0, width // TILE, step, 0)

        return Scatter(produce, *scatter, part=piece, start=piece * size, size=size)

    fold = Fold(lambda at: grad.at[at], far, near_part, cross, mine, theirs, fold_send, fold_recv, fold_local)
    fold.start()
    def end_fold():
        fold.finish()
        for source, target, k in ((grad.at[z], mine, 0), (near_part, theirs, 1)):
            pltpu.make_async_copy(source, target, fold_local.at[k]).start()
        for source, target, k in ((grad.at[z], mine, 0), (near_part, theirs, 1)):
            pltpu.make_async_copy(source, target, fold_local.at[k]).wait()
        add_rows(mine, 0, theirs, 0, mine.shape[0])
        last = pltpu.make_async_copy(cross, theirs, fold_local.at[1])
        last.start()
        last.wait()
        add_rows(mine, 0, theirs, 0, mine.shape[0])
        shard = mine.shape[0] // 8
        index = 4 * y + 2 * c + x
        parts = [
            remote(
                mine.at[pl.ds(pl.multiple_of((4 * peer[0] + 2 * peer[1] + peer[3]) * shard, shard), shard)],
                grad_parts.at[index],
                part_send.at[k],
                part_recv.at[k],
                peer,
            )
            for k, peer in enumerate(layer)
        ]
        kept = pltpu.make_async_copy(mine.at[pl.ds(pl.multiple_of(index * shard, shard), shard)], grad_parts.at[index], fold_local.at[0])
        for copy in parts + [kept]:
            copy.start()
        return parts + [kept]

    sums = [part_of(piece) for piece in range(PIECES)]
    sums[0].begin()
    sums[0].relay()
    sums[1].begin()
    fold.fold()
    total, landed = scatter[2], scatter[4]
    terms[1] = mlp_term[...]
    terms[0] = jnp.zeros_like(mlp_term)
    pieces = [pl.ds(piece * size, size) for piece in range(PIECES)]
    trades = [remote(own.at[at], grad_low.at[at], send.at[k], recv.at[k], partner) for k, at in enumerate(pieces)]
    keeps = [pltpu.make_async_copy(own.at[at], grad_low.at[at], recv.at[k]) for k, at in enumerate(pieces)]
    fetch_x.wait()
    to_peers = []
    for piece in range(PIECES):
        if piece == PIECES - 1:
            to_peers = end_fold()
        sums[piece].arrive()

        def step(i, carry):
            here = pl.ds(pl.multiple_of(piece * size + i * CHUNK, CHUNK), CHUNK)
            back, products = norm_back(x_own[here, :].astype(jnp.float32), gain[...], summed(total, landed, here))
            own[here, :] = (d_resid[here, :] + back).astype(LOW)
            fold_rows(terms.at[0], products)
            return carry

        lax.fori_loop(0, size // CHUNK, step, 0)

        @pl.when(moves)
        def _():
            trades[piece].start()

        @pl.when(jnp.logical_not(moves))
        def _():
            keeps[piece].start()

        if piece + 1 < PIECES:
            sums[piece + 1].relay()
        if piece + 2 < PIECES:
            sums[piece + 2].begin()

    def columns_of(row, layers):
        return pl.ds(pl.multiple_of((4 * row) * HD, HD), layers * HD)

    spread = [
        remote(terms.at[:, :, columns_of(2 * peer[0] + peer[1], 4)], layer_terms.at[k], term_send.at[k], term_recv.at[k], peer)
        for k, peer in enumerate(layer)
    ]
    for copy in spread:
        copy.start()
    for copy in spread:
        copy.wait_recv()
    part[...] = sum((layer_terms[k] for k in range(7)), terms[:, :, columns_of(2 * y + c, 4)])
    lines = [
        remote(
            part.at[:, :, pl.ds(pl.multiple_of(peer[2] * HD, HD), HD)], column_terms.at[k], line_send.at[k], line_recv.at[k], peer
        )
        for k, peer in enumerate(line)
    ]
    for copy in lines:
        copy.start()
    for copy in lines:
        copy.wait_recv()
    gain_grads[...] = sum((column_terms[k] for k in range(3)), part[:, :, pl.ds(pl.multiple_of(z * HD, HD), HD)])
    for copy in spread + lines:
        copy.wait_send()
    for part_sum in sums:
        part_sum.finish()
    for copy in to_peers:
        copy.wait()

    @pl.when(moves)
    def _():
        for copy in trades:
            copy.wait()

    @pl.when(jnp.logical_not(moves))
    def _():
        for copy in keeps:
            copy.wait()


def close_layer(d_qkv, w_qkv, x_home, d_resid, gain, mlp_term, grad):
    block, width = d_resid.shape
    return pl.pallas_call(
        close_layer_kernel,
        out_shape=(
            jax.ShapeDtypeStruct((block, width), LOW),
            jax.ShapeDtypeStruct((2, 8, width // 16), jnp.float32),
            *[jax.ShapeDtypeStruct(grad.shape[1:], LOW)] * 3,
            jax.ShapeDtypeStruct((8, grad.shape[1] // 8, grad.shape[2]), LOW),
        ),
        in_specs=[in_vmem(), in_vmem(), anywhere()] + [in_vmem()] * 3 + [anywhere()],
        out_specs=[anywhere(), in_vmem()] + [anywhere()] * 4,
        scratch_shapes=[
            pltpu.VMEM((block, width), LOW),
            pltpu.VMEM((2, 8, width), jnp.float32),
            pltpu.VMEM((7, 2, 8, width // 4), jnp.float32),
            pltpu.VMEM((2, 8, width // 4), jnp.float32),
            pltpu.VMEM((3, 2, 8, width // 16), jnp.float32),
        ]
        + scatter_scratch(width, PIECES)
        + [dma(PIECES), dma(PIECES), dma(7), dma(7), dma(3), dma(3), pltpu.VMEM((block, width), LOW), dma(1)]
        + [pltpu.VMEM(grad.shape[1:], LOW)] * 2
        + [dma(3), dma(3), dma(2), dma(7), dma(7)],
        compiler_params=remote_params(4),
        cost_estimate=pl.CostEstimate(flops=0, bytes_accessed=350_000_000, transcendentals=0),
    )(d_qkv, w_qkv, x_home, d_resid, gain, mlp_term, grad)


def doc_start(ends, place):
    start = jnp.zeros_like(place)
    for k in range(8):
        start = jnp.where(ends[k] <= place, ends[k], start)
    return jnp.where(place < ends[7], start, LEN)


def sigmoid_of(raw):
    return pl.reciprocal(1.0 + jnp.exp2(math.log2(LEN) - raw * (math.log2(math.e) / math.sqrt(HD))), approx=True)


def tile_at(index):
    return pl.ds(pl.multiple_of(index * TILE, TILE), TILE)


def head_of(array, rows, part, head):
    first = (part * (array.shape[1] // 3) // HD + head) * HD
    return array[rows, first : first + HD]


def attend_kernel(ends, qkv, out, total):
    i = pl.program_id(0)
    heads = qkv.shape[1] // (3 * HD)
    total[...] = jnp.zeros_like(total)
    q_place = i * TILE + lax.broadcasted_iota(jnp.int32, (TILE, 1), 0)
    q_start = doc_start(ends, q_place)

    def tile(j, diagonal):
        k_place = j * TILE + lax.broadcasted_iota(jnp.int32, (1, TILE), 1)
        allowed = k_place >= q_start
        if diagonal:
            allowed = allowed & (k_place <= q_place)
        for head in range(heads):
            raw = dot_nt(head_of(qkv, tile_at(i), 0, head), head_of(qkv, tile_at(j), 1, head))
            weight = jnp.where(allowed, sigmoid_of(raw), 0.0).astype(LOW)
            total[head] += dot_wide(weight, head_of(qkv, tile_at(j), 2, head))

    def step(j, carry):
        tile(j, False)
        return carry

    lax.fori_loop(0, i, step, 0)
    tile(i, True)
    for head in range(heads):
        out[tile_at(i), head * HD : (head + 1) * HD] = total[head].astype(LOW)


def open_mlp_kernel(normed, w_gate, w_up, upstream, gate, up, hidden, upstream_whole, send, recv, local):
    i = pl.program_id(0)
    y, c, z, x = spot()
    steps = pl.num_programs(0)
    gather = Gather(lambda half: upstream.at[pl.ds(half * HALF, HALF)], upstream_whole, send, recv)
    keep = pltpu.make_async_copy(upstream, upstream_whole.at[place_of(y, c, x)], local.at[0])

    @pl.when(i == 0)
    def _():
        greet(near())
        gather.start(0)
        gather.start(1)
        keep.start()

    def step(n, carry):
        columns = pl.ds(pl.multiple_of(n * TILE, TILE), TILE)
        gate_part, up_part = dot_wide(normed[...], w_gate[:, columns]), dot_wide(normed[...], w_up[:, columns])
        gate[:, columns] = gate_part
        up[:, columns] = up_part
        hidden[:, columns] = (gate_part * jax.nn.sigmoid(gate_part) * up_part).astype(LOW)
        return carry

    lax.fori_loop(0, w_gate.shape[1] // TILE, step, 0)

    @pl.when(i == steps - 1)
    def _():
        for half in (0, 1):
            gather.pass_near(half)
        for half in (0, 1):
            gather.pass_far(half)
        gather.finish()
        keep.wait()


def open_mlp(normed, w_gate, w_up, upstream):
    places, width = normed.shape
    hidden = w_gate.shape[1]
    rows = lambda columns: pl.BlockSpec((TILE, columns), lambda i: (i, 0))
    whole = lambda array: pl.BlockSpec(array.shape, lambda i: (0, 0))
    return pl.pallas_call(
        open_mlp_kernel,
        out_shape=(
            jax.ShapeDtypeStruct((places, hidden), jnp.float32),
            jax.ShapeDtypeStruct((places, hidden), jnp.float32),
            jax.ShapeDtypeStruct((places, hidden), LOW),
            jax.ShapeDtypeStruct((places, width), LOW),
        ),
        grid=(places // TILE,),
        in_specs=[rows(width), whole(w_gate), whole(w_up), whole(upstream)],
        out_specs=[rows(hidden), rows(hidden), rows(hidden), anywhere()],
        scratch_shapes=[dma(GATHER_COPIES), dma(GATHER_COPIES), dma(1)],
        compiler_params=remote_params(5),
        cost_estimate=pl.CostEstimate(flops=0, bytes_accessed=250_000_000, transcendentals=0),
    )(normed, w_gate, w_up, upstream)


def out_turns():
    y, c, z, x = spot()
    layers = (x, x, 3 - x, 3 - x)
    owners = [((y, c, layers[j], j % 2), (z == layers[j]) & (x == j % 2)) for j in range(4)]
    side = lax.rem((z + 1) // 2, 2)
    holders = [((y, c, j, side), (z == j) & (x == side)) for j in range(4)]
    return owners, holders


def attend_back_kernel(
    ends, qkv, grads, out_grad, mixed, out, out_parts, mixed_home, query_total, key_total, value_total, send, recv, *trade_parts
):
    j = pl.program_id(0)
    y, c, z, x = spot()
    heads = qkv.shape[1] // (3 * HD)
    shard = out_grad.shape[0] // 4
    owners, holders = out_turns()
    trade = Trade(
        [mixed.at[pl.ds(half * HALF, HALF)] for half in (0, 1)], lambda half, at: mixed_home.at[pl.ds(half * HALF, HALF)], *trade_parts
    )

    def to_owner(turn):
        return remote(out_grad.at[pl.ds(turn * shard, shard)], out_parts.at[z], send.at[turn], recv.at[z], owners[turn][0])

    def to_self(turn):
        return pltpu.make_async_copy(out_grad.at[pl.ds(turn * shard, shard)], out_parts.at[z], recv.at[z])

    @pl.when(j == 0)
    def _():
        query_total[...] = jnp.zeros_like(query_total)
        barrier = pltpu.get_barrier_semaphore()
        for peer, here in holders:

            @pl.when(jnp.logical_not(here))
            def _():
                pl.semaphore_signal(barrier, inc=1, device_id=peer, device_id_type=MESH_ID)

        pl.semaphore_wait(barrier, 4 - (x == lax.rem((z + 1) // 2, 2)).astype(jnp.int32) + trade.greet(barrier, False))
        for half in (0, 1):
            trade.start(half)
        for turn in range(4):

            @pl.when(jnp.logical_not(owners[turn][1]))
            def _():
                to_owner(turn).start()

            @pl.when(owners[turn][1])
            def _():
                to_self(turn).start()

    key_total[...] = jnp.zeros_like(key_total)
    value_total[...] = jnp.zeros_like(value_total)
    here = tile_at(j)
    k_place = j * TILE + lax.broadcasted_iota(jnp.int32, (TILE, 1), 0)
    turned = [head_of(qkv, here, 1, head).T for head in range(heads)]

    def tile(i, diagonal):
        q_place = i * TILE + lax.broadcasted_iota(jnp.int32, (1, TILE), 1)
        allowed = k_place >= doc_start(ends, q_place)
        if diagonal:
            allowed = allowed & (k_place <= q_place)
        for head in range(heads):
            query, grad = head_of(qkv, tile_at(i), 0, head), grads[tile_at(i), head * HD : (head + 1) * HD]
            sig = jnp.where(allowed, sigmoid_of(dot_nt(head_of(qkv, here, 1, head), query)), 0.0)
            value_total[head] += dot_wide(sig.astype(LOW), grad)
            d_score = (dot_nt(head_of(qkv, here, 2, head), grad) * (sig * (1.0 - sig))).astype(LOW)
            key_total[head] += dot_wide(d_score, query)
            query_total[head, :, tile_at(i)] += dot_wide(turned[head], d_score)

    def step(i, carry):
        tile(i, False)
        return carry

    tile(j, True)
    lax.fori_loop(j + 1, LEN // TILE, step, 0)
    scale = 1.0 / math.sqrt(HD)
    for head in range(heads):
        first = head * HD
        out[here, heads * HD + first : (heads + 1) * HD + first] = (key_total[head] * scale).astype(LOW)
        out[here, 2 * heads * HD + first : (2 * heads + 1) * HD + first] = value_total[head].astype(LOW)
        out[here, first : first + HD] = (query_total[head, :, here] * scale).T.astype(LOW)

    @pl.when(j == LEN // TILE - 1)
    def _():
        for turn in range(4):

            @pl.when(jnp.logical_not(owners[turn][1]))
            def _():
                to_owner(turn).wait_send()

            @pl.when(jnp.logical_not(holders[turn][1]))
            def _():
                landed = out_parts.at[turn]
                remote(landed, landed, send.at[turn], recv.at[turn], holders[turn][0]).wait_recv()

            @pl.when(owners[turn][1])
            def _():
                to_self(turn).wait()

        for half in (0, 1):
            trade.arrive(half)
        trade.finish()

    @pl.when(j == 1)
    def _():
        for half in (0, 1):
            trade.forward(half)


def back_mlp_kernel(upstream, w_down, gate, up, d_gate, d_up):
    def step(n, carry):
        columns = pl.ds(pl.multiple_of(n * TILE, TILE), TILE)
        d_hidden = dot_nt(upstream[...], w_down[columns, :])
        d_gate[:, columns], d_up[:, columns] = gate_backward(
            d_hidden, gate[:, columns], up[:, columns], jax.nn.sigmoid(gate[:, columns])
        )
        return carry

    lax.fori_loop(0, gate.shape[1] // TILE, step, 0, unroll=2)


def back_mlp(upstream, w_down, gate, up):
    places, width = upstream.shape
    hidden = gate.shape[1]
    rows = lambda size: pl.BlockSpec((TILE, size), lambda i: (i, 0))
    return pl.pallas_call(
        back_mlp_kernel,
        out_shape=(jax.ShapeDtypeStruct((places, hidden), LOW), jax.ShapeDtypeStruct((places, hidden), LOW)),
        grid=(places // TILE,),
        in_specs=[rows(width), pl.BlockSpec(w_down.shape, lambda i: (0, 0)), rows(hidden), rows(hidden)],
        out_specs=[rows(hidden), rows(hidden)],
        compiler_params=pltpu.CompilerParams(vmem_limit_bytes=VMEM_LIMIT),
        cost_estimate=pl.CostEstimate(flops=0, bytes_accessed=90_000_000, transcendentals=0),
    )(upstream, w_down, gate, up)


def attend(ends, qkv):
    places, width = qkv.shape
    heads = width // (3 * HD)
    whole = lambda columns: pl.BlockSpec((places, columns), lambda i: (0, 0))
    return pl.pallas_call(
        attend_kernel,
        out_shape=jax.ShapeDtypeStruct((places, width // 3), LOW),
        grid=(places // TILE,),
        in_specs=[pl.BlockSpec(memory_space=pltpu.SMEM), whole(width)],
        out_specs=whole(width // 3),
        scratch_shapes=[pltpu.VMEM((heads, TILE, HD), jnp.float32)],
        compiler_params=pltpu.CompilerParams(vmem_limit_bytes=VMEM_LIMIT),
        cost_estimate=pl.CostEstimate(flops=0, bytes_accessed=150_000_000, transcendentals=0),
    )(ends, qkv)


def attend_back(ends, qkv, grads, out_grad, mixed):
    places, width = qkv.shape
    heads = width // (3 * HD)
    whole = lambda columns: pl.BlockSpec((places, columns), lambda j: (0, 0))
    return pl.pallas_call(
        attend_back_kernel,
        out_shape=(
            jax.ShapeDtypeStruct((places, width), LOW),
            jax.ShapeDtypeStruct((4, out_grad.shape[0] // 4, out_grad.shape[1]), LOW),
            jax.ShapeDtypeStruct(mixed.shape, LOW),
        ),
        grid=(places // TILE,),
        in_specs=[pl.BlockSpec(memory_space=pltpu.SMEM), whole(width), whole(width // 3), anywhere(), pl.BlockSpec(mixed.shape, lambda j: (0, 0))],
        out_specs=[whole(width), anywhere(), anywhere()],
        scratch_shapes=[
            pltpu.VMEM((heads, HD, places), jnp.float32),
            pltpu.VMEM((heads, TILE, HD), jnp.float32),
            pltpu.VMEM((heads, TILE, HD), jnp.float32),
            dma(4),
            dma(4),
            *trade_scratch(2, HALF, mixed.shape[1]),
        ],
        compiler_params=remote_params(6),
        cost_estimate=pl.CostEstimate(flops=0, bytes_accessed=300_000_000, transcendentals=0),
    )(ends, qkv, grads, out_grad, mixed)


LAYER = ("y", "c", "x")
PLACES = ("c", "y", "x")
ALL = ("y", "c", "z", "x")


def trade(part):
    pairs = []
    for y in range(2):
        for c in range(2):
            for z in range(4):
                for x in range(2):
                    pairs.append((((y * 2 + c) * 4 + z) * 2 + x, (((z % 2) * 2 + z // 2) * 4 + 2 * c + y) * 2 + x))
    return lax.ppermute(part, ALL, pairs)


def after(first, then):
    return lax.optimization_barrier((first, then))[1]


def body_layers(
    tokens, lengths, cotangent, w_query, w_key, w_value, w_out, w_gate, w_up, w_down, gain_attn, gain_mlp
):
    rows_here, block, width = tokens.shape
    members = lax.axis_size(LAYER)
    layers = lax.axis_size("z")
    shard = w_query.shape[0]
    owned = width // members
    here = lax.axis_index("x")
    gains = jnp.stack((gain_attn, gain_mlp)).astype(jnp.float32)
    gains = jnp.concatenate((jnp.where(here == 0, gains, 0.0), jnp.where(here == 1, gains, 0.0)), axis=1)
    lengths_row = jnp.pad(lengths.astype(jnp.float32), ((0, 0), (0, 2 * shard - lengths.shape[1])))
    facts = jnp.concatenate((gains, lengths_row, jnp.zeros((5, 2 * shard), jnp.float32)), axis=0)
    layer_scaled, x_own, w_qkv, facts = begin(tokens.reshape(block, width), w_query, w_key, w_value, facts)
    gains = facts[:, :, 0] + facts[:, :, 1]
    full_gain_attn, full_gain_mlp = gains[:, :, 0].reshape(1, width), gains[:, :, 1].reshape(1, width)
    layer_normed = (layer_scaled.astype(jnp.float32) * full_gain_attn).astype(LOW)
    layer = lax.axis_index("z")
    own_lengths = facts[:, 0, 0, 2, : lengths.shape[1]].reshape(2, 2, -1)
    own_lengths = lax.dynamic_slice(own_lengths, (layer % 2, layer // 2, 0), (1, 1, own_lengths.shape[2]))[0, 0]
    ends = jnp.cumsum(own_lengths.astype(jnp.int32))
    out_rows = lax.all_gather(after(facts, w_out), ("z", "x"), axis=0, tiled=True)
    w_out_own = [lax.dynamic_slice_in_dim(out_rows, head * HD, HD, 0) for head in (here, 3 - here)]
    w_out_own = jnp.concatenate(w_out_own, axis=0)

    qkv = dot_wide(layer_normed, w_qkv).astype(LOW)
    upstream = trade(after(facts, cotangent)).reshape(block, width)
    attended = attend(ends, qkv)
    resid, layer_mlp, own_gate, own_up = close_attention(after(upstream, attended), w_out_own, x_own, full_gain_mlp, w_gate, w_up)

    own_down = lax.all_gather(after(resid, w_down), "z", axis=0, tiled=True)
    gate, up_part, hidden, layer_upstream = open_mlp(layer_mlp, own_gate, own_up, upstream)
    part = dot_wide(hidden, own_down).astype(LOW)
    mixed_sum = lax.psum_scatter(part, PLACES, scatter_dimension=0, tiled=True)
    down_term = contract_rows(after(part, hidden), layer_upstream).astype(LOW)
    down_rows = w_down.shape[0]
    down_parts = []
    for up in range(1, 4):
        layers_pairs = [(at, (at + up) % 4) for at in range(4)]
        slab = lax.dynamic_slice_in_dim(down_term, (layer + up) % 4 * down_rows, down_rows, 0)
        down_parts.append(lax.ppermute(slab, "z", layers_pairs))
    d_gate, d_up = back_mlp(after(down_term, layer_upstream), own_down, gate, up_part)
    gate_term, up_term = contract_rows(layer_mlp, d_gate).astype(LOW), contract_rows(layer_mlp, d_up).astype(LOW)
    d_resid, gain_mlp_term, layer_d_resid, *parts = close_mlp(
        after((mixed_sum, *down_parts), d_gate), d_up, own_gate, own_up, resid, upstream, full_gain_mlp, gate_term, up_term
    )

    def own_part(whole, near_part, cross):
        own = lax.dynamic_slice_in_dim(whole, layer * cross.shape[1], cross.shape[1], 1)
        return own.astype(jnp.float32) + near_part.astype(jnp.float32) + cross.astype(jnp.float32)

    mixed = (resid + after(layer_d_resid, mixed_sum).astype(jnp.float32)).astype(LOW)
    grad_down = lax.dynamic_slice_in_dim(down_term, layer * down_rows, down_rows, 0).astype(jnp.float32)
    grad_down = grad_down + sum(slab.astype(jnp.float32) for slab in down_parts)

    out_term = contract_rows(attended, layer_d_resid).astype(LOW)
    d_attended = contract_cols(layer_d_resid, w_out_own).astype(LOW)
    d_qkv, out_parts, mixed = attend_back(ends, qkv, d_attended, out_term, mixed)
    mixed = mixed.reshape(rows_here, block, width)
    grad_gate, grad_up = own_part(gate_term, *parts[1:3]), own_part(up_term, *parts[4:6])
    grad_out = jnp.sum(out_parts.astype(jnp.float32), axis=0)
    qkv_term = contract_rows(layer_normed, d_qkv).astype(LOW)
    qkv_term = qkv_term.reshape(4, layers, 2 * shard, 3 * owned).transpose(1, 0, 2, 3)
    qkv_term = qkv_term.reshape(layers, members * shard, 3 * owned)
    grad_low, gain_grads, *_, parts = close_layer(
        d_qkv, w_qkv, x_own, d_resid, full_gain_attn, gain_mlp_term, qkv_term
    )
    grad_tokens = grad_low.astype(jnp.float32).reshape(rows_here, block, width)
    parts = parts.reshape(4, 2, shard, 3, 2, HD)
    parts = jnp.stack((parts[:, 0, :, :, 0], parts[:, 1, :, :, 0], parts[:, 1, :, :, 1], parts[:, 0, :, :, 1]), axis=1)
    grad_query, grad_key, grad_value = parts.transpose(3, 2, 0, 1, 4).astype(jnp.float32).reshape(3, shard, width)
    gain_grads = lax.dynamic_index_in_dim(jnp.sum(gain_grads, axis=1).reshape(2, 2, shard), lax.axis_index("x"), 1, False)
    return (
        mixed,
        grad_tokens,
        grad_query,
        grad_key,
        grad_value,
        grad_out,
        grad_gate,
        grad_up,
        grad_down,
        gain_grads[0],
        gain_grads[1],
    )


def body_any(
    tokens,
    lengths,
    cotangent,
    w_query,
    w_key,
    w_value,
    w_out,
    w_gate,
    w_up,
    w_down,
    gain_attn,
    gain_mlp,
):
    rows_here, block, width = tokens.shape
    count = rows_here * block
    scale = 1.0 / math.sqrt(HD)
    kv_place = lax.axis_index("kv")
    key_places = kv_place * block + jnp.arange(block, dtype=jnp.int32)
    attn_set = (
        lax.all_gather(w_query, ("row", "kv"), axis=0, tiled=True),
        lax.all_gather(w_key, ("row", "kv"), axis=0, tiled=True),
        lax.all_gather(w_value, ("row", "kv"), axis=0, tiled=True),
        lax.all_gather(w_out, ("row", "kv"), axis=0, tiled=True),
        lax.all_gather(gain_attn, ("row", "kv"), axis=0, tiled=True),
        lax.all_gather(gain_mlp, ("row", "kv"), axis=0, tiled=True),
    )
    full_query, full_key, full_value, full_out, full_gain_attn, full_gain_mlp = attn_set
    flat = tokens.reshape(count, width).astype(jnp.float32)
    normed_attn, inverse_attn = norm_forward(flat, full_gain_attn)
    normed_attn_low = normed_attn.astype(jnp.bfloat16)
    query_low = jnp.dot(normed_attn_low, full_query, preferred_element_type=jnp.float32).astype(
        jnp.bfloat16
    )
    key_low = jnp.dot(normed_attn_low, full_key, preferred_element_type=jnp.float32).astype(
        jnp.bfloat16
    )
    value_low = jnp.dot(normed_attn_low, full_value, preferred_element_type=jnp.float32).astype(
        jnp.bfloat16
    )
    key_heads = key_low.reshape(rows_here, block, H, HD)
    value_heads = value_low.reshape(rows_here, block, H, HD)
    segment, valid = segment_table(lengths)
    key_segment = lax.dynamic_slice_in_dim(segment, kv_place * block, block, 1)
    key_valid = lax.dynamic_slice_in_dim(valid, kv_place * block, block, 1)
    queries_all = lax.all_gather(
        query_low.reshape(rows_here, block, width), "kv", axis=1, tiled=True
    )
    which = 0
    query_rows = queries_all[which]
    query_segment = segment[which]
    sigmoid_part, allowed = score_block(
        query_rows,
        key_heads[which],
        query_segment,
        key_segment[which],
        key_valid[which],
        jnp.int32(0),
        key_places,
    )
    weight = (sigmoid_part * allowed).astype(jnp.bfloat16)
    summed = jnp.einsum(
        "hqk,khd->qhd", weight, value_heads[which], preferred_element_type=jnp.float32
    )
    pieces = [
        lax.psum_scatter(
            summed.reshape(lax.axis_size("kv") * block, width).astype(jnp.bfloat16),
            "kv",
            scatter_dimension=0,
            tiled=True,
        ).astype(jnp.float32)
    ]
    attended_low = jnp.stack(pieces).reshape(count, width).astype(jnp.bfloat16)
    resid = flat + jnp.dot(attended_low, full_out, preferred_element_type=jnp.float32)
    normed_mlp, inverse_mlp = norm_forward(resid, full_gain_mlp)
    normed_mlp_low = normed_mlp.astype(jnp.bfloat16)
    upstream_low = cotangent.reshape(count, width)
    upstream = upstream_low.astype(jnp.float32)
    slice_gate, slice_up, slice_down = (
        lax.all_gather(w_gate, "row", axis=1, tiled=True),
        lax.all_gather(w_up, "row", axis=1, tiled=True),
        lax.all_gather(w_down, "row", axis=0, tiled=True),
    )
    row_normed, row_upstream = (
        lax.all_gather(normed_mlp_low.reshape(rows_here, block, width), "kv", axis=1, tiled=True),
        lax.all_gather(cotangent, "kv", axis=1, tiled=True),
    )
    normed_rows = row_normed.reshape(rows_here * LEN, width)
    upstream_rows = row_upstream.reshape(rows_here * LEN, width)
    gate = jnp.dot(normed_rows, slice_gate, preferred_element_type=jnp.float32)
    up_part = jnp.dot(normed_rows, slice_up, preferred_element_type=jnp.float32)
    sigmoid_gate = jax.nn.sigmoid(gate)
    hidden_low = (gate * sigmoid_gate * up_part).astype(jnp.bfloat16)
    hidden_rows = hidden_low.reshape(rows_here, LEN, hidden_low.shape[1])
    which = 0
    hidden_part = hidden_rows[which]
    outputs = [
        lax.psum_scatter(
            jnp.dot(hidden_part, slice_down, preferred_element_type=jnp.float32).astype(
                jnp.bfloat16
            ),
            "kv",
            scatter_dimension=0,
            tiled=True,
        ).astype(jnp.float32)
    ]
    result = resid + jnp.stack(outputs).reshape(count, width)
    d_hidden = contract_cols(upstream_rows, slice_down)
    d_gate, d_up = gate_backward(d_hidden, gate, up_part, sigmoid_gate)
    partial_normed = contract_cols(d_gate, slice_gate) + contract_cols(d_up, slice_up)
    d_normed_mlp = (
        lax.psum_scatter(
            partial_normed.reshape(rows_here, LEN, width).astype(jnp.bfloat16),
            "kv",
            scatter_dimension=1,
            tiled=True,
        )
        .astype(jnp.float32)
        .reshape(count, width)
    )
    grad_gate, grad_up, grad_down = (
        lax.psum_scatter(
            contract_rows(normed_rows, d_gate).astype(jnp.bfloat16),
            "row",
            scatter_dimension=1,
            tiled=True,
        ).astype(jnp.float32),
        lax.psum_scatter(
            contract_rows(normed_rows, d_up).astype(jnp.bfloat16),
            "row",
            scatter_dimension=1,
            tiled=True,
        ).astype(jnp.float32),
        lax.psum_scatter(
            contract_rows(hidden_low, upstream_rows).astype(jnp.bfloat16),
            "row",
            scatter_dimension=0,
            tiled=True,
        ).astype(jnp.float32),
    )
    mixed = result.astype(jnp.bfloat16).reshape(rows_here, block, width)
    back_mlp, gain_mlp_term = norm_backward(resid, inverse_mlp, full_gain_mlp, d_normed_mlp)
    d_resid = upstream + back_mlp
    d_resid_low = d_resid.astype(jnp.bfloat16)
    d_attended = contract_cols(d_resid_low, full_out).astype(jnp.bfloat16)
    grads_all = lax.all_gather(
        d_attended.reshape(rows_here, block, width), "kv", axis=1, tiled=True
    )
    query_block = min(512, LEN)
    block_count = LEN // query_block
    which = 0

    def sweep(carry, index, which=which):
        key_total, value_total = carry
        start = index * query_block
        query_rows = lax.dynamic_slice_in_dim(queries_all[which], start, query_block, 0)
        grad_rows = lax.dynamic_slice_in_dim(grads_all[which], start, query_block, 0)
        query_segment = lax.dynamic_slice_in_dim(segment[which], start, query_block, 0)
        sigmoid_part, allowed = score_block(
            query_rows,
            key_heads[which],
            query_segment,
            key_segment[which],
            key_valid[which],
            start,
            key_places,
        )
        weight = (sigmoid_part * allowed).astype(jnp.bfloat16)
        grad_heads = grad_rows.reshape(query_block, H, HD)
        value_total = value_total + jnp.einsum(
            "hqk,qhd->khd", weight, grad_heads, preferred_element_type=jnp.float32
        )
        d_weight = jnp.einsum(
            "qhd,khd->hqk", grad_heads, value_heads[which], preferred_element_type=jnp.float32
        )
        d_score = (d_weight * sigmoid_part * (1.0 - sigmoid_part) * allowed).astype(jnp.bfloat16)
        query_part = (
            jnp.einsum(
                "hqk,khd->qhd", d_score, key_heads[which], preferred_element_type=jnp.float32
            )
            * scale
        )
        key_total = (
            key_total
            + jnp.einsum(
                "hqk,qhd->khd",
                d_score,
                query_rows.reshape(query_block, H, HD),
                preferred_element_type=jnp.float32,
            )
            * scale
        )
        return ((key_total, value_total), query_part.reshape(query_block, width))

    zeros = jnp.zeros((block, H, HD), jnp.float32)
    totals, query_parts = lax.scan(sweep, (zeros, zeros), jnp.arange(block_count, dtype=jnp.int32))
    query_terms = [query_parts.reshape(LEN, width)]
    key_grads = [totals[0].reshape(block, width)]
    value_grads = [totals[1].reshape(block, width)]
    query_local = lax.psum_scatter(
        jnp.stack(query_terms).astype(jnp.bfloat16), "kv", scatter_dimension=1, tiled=True
    ).astype(jnp.float32)
    d_query_low = query_local.reshape(count, width).astype(jnp.bfloat16)
    d_key_low = jnp.stack(key_grads).reshape(count, width).astype(jnp.bfloat16)
    d_value_low = jnp.stack(value_grads).reshape(count, width).astype(jnp.bfloat16)
    d_normed_attn = (
        contract_cols(d_query_low, full_query)
        + contract_cols(d_key_low, full_key)
        + contract_cols(d_value_low, full_value)
    )
    back_attn, gain_attn_term = norm_backward(flat, inverse_attn, full_gain_attn, d_normed_attn)
    grad_tokens = (d_resid + back_attn).reshape(rows_here, block, width)
    projected_low = jnp.concatenate((d_query_low, d_key_low, d_value_low), axis=1)
    grad_projections = lax.psum_scatter(
        contract_rows(normed_attn_low, projected_low),
        ("row", "kv"),
        scatter_dimension=0,
        tiled=True,
    )
    out_term = contract_rows(attended_low, d_resid_low)
    grad_out, grad_gain_attn, grad_gain_mlp = (
        lax.psum_scatter(out_term, ("row", "kv"), scatter_dimension=0, tiled=True),
        lax.psum_scatter(gain_attn_term, ("row", "kv"), scatter_dimension=0, tiled=True),
        lax.psum_scatter(gain_mlp_term, ("row", "kv"), scatter_dimension=0, tiled=True),
    )
    grad_query = grad_projections[:, :width]
    grad_key = grad_projections[:, width : 2 * width]
    grad_value = grad_projections[:, 2 * width :]
    return (
        mixed,
        grad_tokens,
        grad_query,
        grad_key,
        grad_value,
        grad_out,
        grad_gate,
        grad_up,
        grad_down,
        grad_gain_attn,
        grad_gain_mlp,
    )


def solution(mesh):
    rows, columns = mesh.shape["row"], mesh.shape["kv"]
    if rows == 4 and columns == 2 * rows:
        mesh = Mesh(mesh.devices.reshape(2, 2, rows, 2), ("y", "c", "z", "x"))
        row, kv, run = ("y", "c"), ("z", "x"), body_layers
    else:
        row, kv, run = "row", "kv", body_any
    both = ("y", "c", "z", "x") if run is body_layers else ("row", "kv")
    tall, wide, flat = P(both, None), P(None, both), P(both)
    tokens = P(row, kv, None)
    return jax.shard_map(
        run,
        mesh=mesh,
        in_specs=(tokens, P(row, None), tokens, tall, tall, tall, tall, wide, wide, tall, flat, flat),
        out_specs=(tokens, tokens, tall, tall, tall, tall, wide, wide, tall, flat, flat),
        check_vma=False,
    )
```

```python
import functools
import math

import jax
import jax.numpy as jnp
from jax import lax
from jax.experimental import pallas as pl
from jax.experimental.pallas import tpu as pltpu
from jax.sharding import Mesh, PartitionSpec as P

H = 16
HD = 128
LEN = 4096


EPSILON = 1e-05


def contract_rows(left, right):
    return lax.dot_general(
        left, right, (((0,), (0,)), ((), ())), preferred_element_type=jnp.float32
    )


def contract_cols(left, right):
    return lax.dot_general(
        left, right, (((1,), (1,)), ((), ())), preferred_element_type=jnp.float32
    )


def norm_forward(value, gain):
    inverse = lax.rsqrt(jnp.mean(value * value, axis=-1, keepdims=True) + EPSILON)
    return (value * inverse * gain.astype(jnp.float32), inverse)


def norm_backward(value, inverse, gain, upstream):
    scaled = upstream * gain.astype(jnp.float32)
    inner = jnp.mean(scaled * value, axis=-1, keepdims=True)
    back = inverse * scaled - value * (inverse * inverse * inverse) * inner
    gain_term = jnp.sum(upstream * value * inverse, axis=0)
    return (back, gain_term)


def segment_table(lengths):
    ends = jnp.cumsum(lengths, axis=-1)
    places = jnp.arange(LEN, dtype=jnp.int32)
    segment = jnp.sum((ends[:, None, :] <= places[None, :, None]).astype(jnp.int32), axis=-1)
    valid = places[None, :] < ends[:, -1:]
    return (segment, valid)


def score_block(
    query_rows, key_heads, query_segment, key_segment, key_valid, query_start, key_places
):
    count = query_rows.shape[0]
    query_heads = query_rows.reshape(count, H, HD)
    raw = jnp.einsum("qhd,khd->hqk", query_heads, key_heads, preferred_element_type=jnp.float32)
    scores = raw * (1.0 / math.sqrt(HD)) - math.log(LEN)
    places = query_start + jnp.arange(count, dtype=jnp.int32)
    allowed = (
        (key_places[None, :] <= places[:, None])
        & (key_segment[None, :] == query_segment[:, None])
        & key_valid[None, :]
    )
    return (jax.nn.sigmoid(scores), allowed.astype(jnp.float32)[None])


def gate_backward(d_hidden, gate, up_part, sigmoid_gate):
    d_gate = (d_hidden * up_part * sigmoid_gate * (1.0 + gate * (1.0 - sigmoid_gate))).astype(
        jnp.bfloat16
    )
    d_up = (d_hidden * gate * sigmoid_gate).astype(jnp.bfloat16)
    return (d_gate, d_up)


TILE = 512
LOW = jnp.bfloat16
VMEM_LIMIT = 60 * 1024 * 1024


def dot_nt(left, right):
    return lax.dot_general(left, right, (((1,), (1,)), ((), ())), preferred_element_type=jnp.float32)


def dot_wide(left, right):
    return jnp.dot(left, right, preferred_element_type=jnp.float32)


HALF = TILE // 2
PIECES = 4
CHUNK = 32
MESH_ID = pl.DeviceIdType.MESH


def flip(bit, by):
    return bit + by - 2 * bit * by


def spot():
    return tuple(lax.axis_index(name) for name in ("y", "c", "z", "x"))


def near():
    y, c, z, x = spot()
    return (y, c, z, 1 - x), (1 - y, c, z, x), (y, 1 - c, z, x)


def partner_of(y, c, z, x):
    return lax.rem(z, 2), z // 2, 2 * c + y, x


def place_of(y, c, x, half=None):
    first = (4 * c + 2 * y + x) * TILE
    if half is None:
        return pl.ds(pl.multiple_of(first, TILE), TILE)
    return pl.ds(pl.multiple_of(first + half * HALF, HALF), HALF)


def quarter_of(y, c, x, half, quarter):
    return pl.ds(pl.multiple_of((4 * c + 2 * y + x) * TILE + half * HALF + quarter * (HALF // 2), HALF // 2), HALF // 2)


def remote(src, dst, send, recv, peer):
    return pltpu.make_async_remote_copy(
        src_ref=src, dst_ref=dst, send_sem=send, recv_sem=recv, device_id=peer, device_id_type=MESH_ID
    )


def greet(peers):
    barrier = pltpu.get_barrier_semaphore()
    for peer in peers:
        pl.semaphore_signal(barrier, inc=1, device_id=peer, device_id_type=MESH_ID)
    pl.semaphore_wait(barrier, len(peers))


class Gather:
    def __init__(self, own, whole, send, recv):
        y, c, z, x = spot()
        across_x, across_y, core = near()

        def passed(k, at, peer):
            return remote(whole.at[at], whole.at[at], send.at[k], recv.at[k], peer)

        self.halves = []
        for half in (0, 1):
            k, at = 9 * half, place_of(y, c, x, half)
            mine = [
                remote(own(half), whole.at[at], send.at[k + m], recv.at[k + m], peer)
                for m, peer in enumerate((across_x, across_y, core))
            ]
            held_x, held_y = (y, c, 1 - x), (1 - y, c, x)
            far = (1 - y, c, 1 - x)
            self.halves.append(
                (
                    mine,
                    passed(k + 3, quarter_of(*held_x, half, 0), across_y),
                    passed(k + 4, quarter_of(*held_y, half, 1), across_x),
                    [passed(k + 5, place_of(*held_x, half), core), passed(k + 6, place_of(*held_y, half), core)],
                    [passed(k + 7 + q, quarter_of(*far, half, q), core) for q in (0, 1)],
                )
            )

    def start(self, half):
        for copy in self.halves[half][0]:
            copy.start()

    def pass_near(self, half):
        mine, over_y, over_x, from_near, from_far = self.halves[half]
        mine[0].wait_recv()
        over_y.start()
        from_near[0].start()
        mine[1].wait_recv()
        over_x.start()
        from_near[1].start()

    def pass_far(self, half):
        mine, over_y, over_x, from_near, from_far = self.halves[half]
        over_y.wait_recv()
        from_far[0].start()
        over_x.wait_recv()
        from_far[1].start()

    def finish(self):
        for mine, over_y, over_x, from_near, from_far in self.halves:
            for copy in [mine[2]] + from_near + from_far:
                copy.wait_recv()
            for copy in mine + [over_y, over_x] + from_near + from_far:
                copy.wait_send()


GATHER_COPIES = 18


class GatherWhole:
    def __init__(self, own, whole, send, recv):
        y, c, z, x = spot()
        across_x, across_y, core = near()

        def from_own(k, half, peer):
            return remote(own(half), whole.at[place_of(y, c, x, half)], send.at[k], recv.at[k], peer)

        def passed(k, at, peer):
            return remote(whole.at[at], whole.at[at], send.at[k], recv.at[k], peer)

        self.mine = [
            [from_own(0, 0, across_x), from_own(1, 0, across_y), from_own(2, 0, core)],
            [from_own(3, 1, across_x), from_own(4, 1, across_y), from_own(5, 1, core)],
        ]
        held_x = [place_of(y, c, 1 - x, half) for half in (0, 1)]
        held_y = [place_of(1 - y, c, x, half) for half in (0, 1)]
        far = [place_of(1 - y, c, 1 - x, half) for half in (0, 1)]
        self.over_y, self.over_x = passed(6, held_x[0], across_y), passed(7, held_y[1], across_x)
        self.core_x = [passed(8 + half, held_x[half], core) for half in (0, 1)]
        self.core_y = [passed(10 + half, held_y[half], core) for half in (0, 1)]
        self.core_far = [passed(12 + half, far[half], core) for half in (0, 1)]

    def start(self, half):
        for copy in self.mine[half]:
            copy.start()

    def pass_first(self):
        self.mine[0][0].wait_recv()
        self.over_y.start()
        self.core_x[0].start()
        self.mine[0][1].wait_recv()
        self.core_y[0].start()

    def pass_second(self):
        self.mine[1][1].wait_recv()
        self.over_x.start()
        self.core_y[1].start()
        self.mine[1][0].wait_recv()
        self.core_x[1].start()

    def pass_far(self):
        self.over_y.wait_recv()
        self.core_far[0].start()
        self.over_x.wait_recv()
        self.core_far[1].start()

    def finish(self):
        from_core = [self.mine[0][2], self.mine[1][2]] + self.core_x + self.core_y + self.core_far
        for copy in from_core:
            copy.wait_recv()
        for copy in self.mine[0] + self.mine[1] + [self.over_y, self.over_x] + self.core_x + self.core_y + self.core_far:
            copy.wait_send()


class Trade:
    def __init__(self, sources, dst, held, send, recv, held_recv, pass_send, detour=True):
        y, c, z, x = spot()
        self.detour = detour
        across_y = (1 - y, c, z, x)
        self.moves = z != 2 * c + y
        self.away = (y == c) & (z == 1 + y)
        self.straight = self.moves & jnp.logical_not(self.away) if detour else self.moves
        self.passes = (1 - y == c) & (z == 2 - y)
        partner = partner_of(y, c, z, x)
        comes_by = ((partner[0] == partner[1]) & (partner[2] == 1 + partner[0])).astype(jnp.int32)
        self.sender = (flip(partner[0], comes_by), partner[1], partner[2], x) if detour else partner
        self.across_y = across_y
        target = partner_of(*across_y)
        self.direct, self.keep, self.out, self.onward = [], [], [], []
        for h, source in enumerate(sources):
            self.direct.append(remote(source, dst(h, partner), send.at[h], recv.at[h], partner))
            self.keep.append(pltpu.make_async_copy(source, dst(h, (y, c, z, x)), recv.at[h]))
            self.out.append(remote(source, held.at[h], send.at[h], held_recv.at[h], across_y))
            self.onward.append(remote(held.at[h], dst(h, target), pass_send.at[h], recv.at[h], target))

    def greet(self, barrier, neighbours_greet):
        @pl.when(self.moves)
        def _():
            pl.semaphore_signal(barrier, inc=1, device_id=self.sender, device_id_type=MESH_ID)

        count = self.straight.astype(jnp.int32)
        if not self.detour:
            return count
        count = count + self.passes.astype(jnp.int32)
        if not neighbours_greet:

            @pl.when(self.passes)
            def _():
                pl.semaphore_signal(barrier, inc=1, device_id=self.across_y, device_id_type=MESH_ID)

            count = count + self.away.astype(jnp.int32)
        return count

    def start(self, h):
        @pl.when(self.straight)
        def _():
            self.direct[h].start()

        if self.detour:

            @pl.when(self.away)
            def _():
                self.out[h].start()

        @pl.when(jnp.logical_not(self.moves))
        def _():
            self.keep[h].start()

    def wait_sent(self, h):
        @pl.when(self.straight)
        def _():
            self.direct[h].wait_send()

        if self.detour:

            @pl.when(self.away)
            def _():
                self.out[h].wait_send()

    def forward(self, h):
        if self.detour:

            @pl.when(self.passes)
            def _():
                self.out[h].wait_recv()
                self.onward[h].start()

    def arrive(self, h):
        @pl.when(self.moves)
        def _():
            self.direct[h].wait_recv()

        @pl.when(jnp.logical_not(self.moves))
        def _():
            self.keep[h].wait()

    def finish(self, first=0):
        for h in range(len(self.direct)):
            if h >= first:
                self.wait_sent(h)

            if self.detour:

                @pl.when(self.passes)
                def _():
                    self.onward[h].wait_send()


def trade_scratch(pieces, rows, width):
    return [pltpu.VMEM((pieces, rows, width), LOW)] + [pltpu.SemaphoreType.DMA((pieces,)) for _ in range(4)]


class Chain:
    def __init__(self, own, slab, sems, index):
        self.own, self.slab, self.sems, self.index = own, slab, sems, index
        self.last = lax.axis_size("z") - 1

    def move(self, which, h, source, layer, to):
        y, c, z, x = spot()
        return remote(
            source, self.slab(layer), self.sems[2 * which].at[self.index, h], self.sems[2 * which + 1].at[self.index, h], (y, c, to, x)
        )

    def up(self, h):
        z = lax.axis_index("z")
        return self.move(0, h, self.own if h == 0 else self.slab(z - h), z - h, z + 1)

    def down(self, h):
        z = lax.axis_index("z")
        return self.move(1, h, self.own if h == 0 else self.slab(z + h), z + h, z - 1)

    def start(self):
        z = lax.axis_index("z")

        @pl.when(z < self.last)
        def _():
            self.up(0).start()

        @pl.when(z > 0)
        def _():
            self.down(0).start()

    def arrive(self, h):
        z = lax.axis_index("z")

        @pl.when(z - h - 1 >= 0)
        def _():
            self.move(0, h, self.slab(z - h - 1), z - h - 1, z).wait_recv()
            if h < 2:

                @pl.when(z < self.last)
                def _():
                    self.up(h + 1).start()

        @pl.when(z + h + 1 <= self.last)
        def _():
            self.move(1, h, self.slab(z + h + 1), z + h + 1, z).wait_recv()
            if h < 2:

                @pl.when(z > 0)
                def _():
                    self.down(h + 1).start()

    def finish(self):
        z = lax.axis_index("z")
        for h in range(3):

            @pl.when((z < self.last) & (z - h >= 0))
            def _():
                self.up(h).wait_send()

            @pl.when((z > 0) & (z + h <= self.last))
            def _():
                self.down(h).wait_send()


def chain_sems(count):
    return [pltpu.SemaphoreType.DMA((count, 3)) for _ in range(4)]


def greet_neighbours(peers):
    y, c, z, x = spot()
    last = lax.axis_size("z") - 1
    barrier = pltpu.get_barrier_semaphore()
    for peer in peers:
        pl.semaphore_signal(barrier, inc=1, device_id=peer, device_id_type=MESH_ID)

    @pl.when(z > 0)
    def _():
        pl.semaphore_signal(barrier, inc=1, device_id=(y, c, z - 1, x), device_id_type=MESH_ID)

    @pl.when(z < last)
    def _():
        pl.semaphore_signal(barrier, inc=1, device_id=(y, c, z + 1, x), device_id_type=MESH_ID)

    return barrier, len(peers) + (z > 0).astype(jnp.int32) + (z < last).astype(jnp.int32)


def others():
    y, c, z, x = spot()
    return [(flip(y, dy), flip(c, dc), z, flip(x, dx)) for dy in (0, 1) for dc in (0, 1) for dx in (0, 1) if dy + dc + dx]


def line_of():
    y, c, z, x = spot()
    return [(y, c, lax.rem(z + dz, 4), x) for dz in (1, 2, 3)]


class Fold:
    def __init__(self, slab, far, near_part, cross, mine, theirs, send, recv, local):
        y, c, z, x = spot()
        a, b = z // 2, lax.rem(z, 2)
        pair, middle = (y, c, 2 * a + 1 - b, x), (y, c, 2 * (1 - a) + b, x)
        self.far = remote(slab(2 * (1 - a) + 1 - b), far, send.at[0], recv.at[0], pair)
        self.near = remote(slab(2 * a + 1 - b), near_part, send.at[1], recv.at[1], pair)
        self.cross = remote(mine, cross, send.at[2], recv.at[2], middle)
        self.fetches = [
            pltpu.make_async_copy(slab(2 * (1 - a) + b), mine, local.at[0]),
            pltpu.make_async_copy(far, theirs, local.at[1]),
        ]
        self.mine, self.theirs = mine, theirs

    def start(self):
        self.far.start()
        self.fetches[0].start()

    def fold(self):
        self.far.wait_recv()
        self.fetches[1].start()
        for copy in self.fetches:
            copy.wait()
        add_rows(self.mine, 0, self.theirs, 0, self.mine.shape[0])
        self.cross.start()
        self.near.start()

    def finish(self):
        for copy in (self.near, self.cross):
            copy.wait_recv()
        for copy in (self.far, self.near, self.cross):
            copy.wait_send()


def columns_of_layer(whole):
    size = whole.shape[1] // 4
    return lambda at: whole.at[:, pl.ds(pl.multiple_of(at * size, size), size)]


def fold_peers():
    y, c, z, x = spot()
    a, b = z // 2, lax.rem(z, 2)
    return ((y, c, 2 * a + 1 - b, x), (y, c, 2 * (1 - a) + b, x))


def add_rows(total, first, term, start, count):
    def step(i, carry):
        here = pl.ds(pl.multiple_of(first + i * CHUNK, CHUNK), CHUNK)
        there = pl.ds(pl.multiple_of(start + i * CHUNK, CHUNK), CHUNK)
        total[here, :] = (total[here, :].astype(jnp.float32) + term[there, :].astype(jnp.float32)).astype(LOW)
        return carry

    lax.fori_loop(0, count // CHUNK, step, 0)


def scatter_scratch(width, parts=1):
    return [
        pltpu.VMEM((2, TILE, width), LOW),
        pltpu.VMEM((4, TILE, width), LOW),
        pltpu.VMEM((4, TILE, width), LOW),
        pltpu.VMEM((2, HALF, width), LOW),
        pltpu.VMEM((2, TILE, width), LOW),
        pltpu.SemaphoreType.DMA((parts, 10)),
        pltpu.SemaphoreType.DMA((parts, 10)),
    ]


class Scatter:
    def __init__(self, produce, staged, core_part, total, relayed, landed, send, recv, part=0, start=0, size=TILE):
        across_x, across_y, core = near()
        self.produce, self.staged, self.core_part, self.total, self.relayed = produce, staged, core_part, total, relayed
        self.start, self.size, self.half = start, size, size // 2
        send, recv = send.at[part], recv.at[part]
        rows = pl.ds(start, size)
        halves = (pl.ds(start, self.half), pl.ds(start + self.half, self.half))
        self.relay_row = start // 2
        passing = pl.ds(self.relay_row, self.half)
        self.to_core = [
            remote(staged.at[k % 2, rows], core_part.at[k, rows], send.at[k], recv.at[k], core) for k in range(4)
        ]
        self.far_x = remote(total.at[0, halves[0]], relayed.at[0, passing], send.at[4], recv.at[4], across_x)
        self.far_y = remote(total.at[0, halves[1]], relayed.at[1, passing], send.at[5], recv.at[5], across_y)
        self.to_x = [
            remote(total.at[1, at], landed.at[0, at], send.at[6 + half], recv.at[6 + half], across_x)
            for half, at in enumerate(halves)
        ]
        self.to_y = [
            remote(total.at[2, at], landed.at[1, at], send.at[8 + half], recv.at[8 + half], across_y)
            for half, at in enumerate(halves)
        ]

    def begin(self):
        y, c, z, x = spot()
        rows = pl.ds(self.start, self.size)
        for k, (to_row, to_column) in enumerate(((1 - y, 1 - x), (y, 1 - x), (1 - y, x), (y, x))):
            if k >= 2:
                self.to_core[k - 2].wait_send()
            self.produce(2 * k, to_row, 1 - c, to_column, self.staged.at[k % 2, rows])
            self.to_core[k].start()
            self.produce(2 * k + 1, to_row, c, to_column, self.total.at[k, rows])
            self.to_core[k].wait_recv()
            add_rows(self.total.at[k], self.start, self.core_part.at[k], self.start, self.size)
            if k == 0:
                self.far_x.start()
                self.far_y.start()
            if k == 1:
                self.to_x[0].start()
            if k == 2:
                self.to_y[1].start()

    def relay(self):
        self.far_y.wait_recv()
        add_rows(self.total.at[1], self.start + self.half, self.relayed.at[1], self.relay_row, self.half)
        self.to_x[1].start()
        self.far_x.wait_recv()
        add_rows(self.total.at[2], self.start, self.relayed.at[0], self.relay_row, self.half)
        self.to_y[0].start()

    def arrive(self):
        for copy in self.to_x + self.to_y:
            copy.wait_recv()

    def finish(self):
        for copy in self.to_core[2:] + [self.far_x, self.far_y] + self.to_x + self.to_y:
            copy.wait_send()


def sum_and_gather(part_of, rows_of_half, gather, beside):
    sums = [part_of(half) for half in (0, 1)]
    sums[0].begin()
    sums[0].relay()
    sums[1].begin()
    sums[0].arrive()
    rows_of_half(0)
    gather.start(0)
    beside(0)
    sums[1].relay()
    beside(1)
    sums[1].arrive()
    rows_of_half(1)
    gather.start(1)
    gather.pass_near(0)
    beside(2)
    gather.pass_near(1)
    gather.pass_far(0)
    gather.pass_far(1)
    gather.finish()
    beside(3)
    for half in (0, 1):
        sums[half].finish()


def begin_kernel(
    x_own, w_query, w_key, w_value, facts, x_whole, w_qkv, facts_whole,
    gather_send, gather_recv, w_send, w_recv, fact_send, fact_recv, local, *scratch
):
    y, c, z, x = spot()
    row = 2 * y + c
    layer = others()
    trade_parts, sems = scratch[:5], scratch[5:]
    trade = Trade(
        [x_own.at[half] for half in (0, 1)], lambda half, at: x_whole.at[place_of(at[0], at[1], at[3], half)], *trade_parts, detour=False
    )
    barrier, count = greet_neighbours(layer)
    pl.semaphore_wait(barrier, count + trade.greet(barrier, True))

    shard = w_query.shape[0]
    for half in (0, 1):
        trade.start(half)
    spread = [
        remote(facts, facts_whole.at[row, z, x], fact_send.at[k], fact_recv.at[k], peer) for k, peer in enumerate(layer)
    ]
    kept = [pltpu.make_async_copy(facts, facts_whole.at[row, z, x], local.at[6])]
    for m in range(6):
        source, slot = (w_query, w_key, w_value)[m // 2], m % 2

        def columns_of(at):
            head = 4 * (2 * at[0] + at[1]) + (3 - at[3] if slot else at[3])
            return source.at[:, pl.ds(pl.multiple_of(head * HD, HD), HD)]

        dst = w_qkv.at[row, z, pl.ds(pl.multiple_of(x * shard, shard), shard), pl.ds(m * HD, HD)]
        for k, peer in enumerate(layer):
            spread.append(remote(columns_of(peer), dst, w_send.at[m, k], w_recv.at[m, k], peer))
        kept.append(pltpu.make_async_copy(columns_of((y, c, z, x)), dst, local.at[m]))
    for copy in spread + kept:
        copy.start()

    gather = GatherWhole(lambda half: x_whole.at[place_of(y, c, x, half)], x_whole, gather_send, gather_recv)
    for half in (0, 1):
        trade.forward(half)
        trade.arrive(half)
        gather.start(half)

    for copy in kept:
        copy.wait()
    for copy in spread:
        copy.wait_recv()
    chains = [
        Chain(facts_whole.at[:, z], lambda at: facts_whole.at[:, at], sems, 0),
        Chain(w_qkv.at[:, z], lambda at: w_qkv.at[:, at], sems, 1),
    ]

    def arrive(h):
        for chain in chains:
            chain.arrive(h)

    for chain in chains:
        chain.start()
    gather.pass_first()
    arrive(0)
    gather.pass_second()
    arrive(1)
    gather.pass_far()
    arrive(2)
    gather.finish()
    trade.finish()
    for copy in spread:
        copy.wait_send()
    for chain in chains:
        chain.finish()


def anywhere():
    return pl.BlockSpec(memory_space=pl.ANY)


def in_vmem():
    return pl.BlockSpec(memory_space=pltpu.VMEM)


def dma(*shape):
    return pltpu.SemaphoreType.DMA(shape)


def remote_params(number):
    return pltpu.CompilerParams(collective_id=number, has_side_effects=True, vmem_limit_bytes=VMEM_LIMIT)


def begin(x_own, w_query, w_key, w_value, facts):
    block, width = x_own.shape
    shard = w_query.shape[0]
    x_whole, w_qkv, facts_whole = pl.pallas_call(
        begin_kernel,
        out_shape=(
            jax.ShapeDtypeStruct((8 * block, width), LOW),
            jax.ShapeDtypeStruct((4, 4, 2 * shard, 3 * width // 8), LOW),
            jax.ShapeDtypeStruct((4, 4, 2, *facts.shape), jnp.float32),
        ),
        in_specs=[in_vmem()] + [anywhere()] * 4,
        out_specs=[anywhere()] * 3,
        scratch_shapes=[
            dma(GATHER_COPIES), dma(GATHER_COPIES), dma(6, 7), dma(6, 7), dma(7), dma(7), dma(7),
            *trade_scratch(2, block // 2, width), *chain_sems(2),
        ],
        compiler_params=remote_params(1),
        cost_estimate=pl.CostEstimate(flops=0, bytes_accessed=350_000_000, transcendentals=0),
    )(x_own.reshape(2, block // 2, width), w_query, w_key, w_value, facts)
    return x_whole, w_qkv.reshape(width, 3 * width // 8), facts_whole


def summed(total, landed, here):
    parts = (total[3, here, :], landed[0, here, :], landed[1, here, :])
    return sum(part.astype(jnp.float32) for part in parts)


def over_chunks(work, half):
    def step(i, carry):
        work(pl.ds(pl.multiple_of(half * HALF + i * CHUNK, CHUNK), CHUNK))
        return carry

    lax.fori_loop(0, HALF // CHUNK, step, 0)


def own_halves(own):
    return lambda half: own.at[pl.ds(half * HALF, HALF)]


def inverse_of(value):
    return lax.rsqrt(jnp.mean(value * value, axis=-1, keepdims=True) + EPSILON)


def close_attention_kernel(attended, w_out, x_whole, gain, w_gate, w_up, resid, normed, own_gate, own_up, own, x_own, *scratch):
    scatter, (send, recv, local), sems = scratch[:7], scratch[7:10], scratch[10:]
    y, c, z, x = spot()
    fetch_x = pltpu.make_async_copy(x_whole.at[place_of(y, c, x)], x_own, local.at[0])
    fetch_x.start()
    width = w_out.shape[1]
    hidden = w_gate.shape[1]
    z = lax.axis_index("z")
    barrier, count = greet_neighbours(near())
    pl.semaphore_wait(barrier, count)

    def slab_of(whole):
        return lambda at: whole.at[:, pl.ds(pl.multiple_of(at * hidden, hidden), hidden)]

    chains, kept = [], []
    for k, (part, whole) in enumerate(((w_gate, own_gate), (w_up, own_up))):
        chains.append(Chain(part, slab_of(whole), sems, k))
        chains[k].start()
        kept.append(pltpu.make_async_copy(part, slab_of(whole)(z), local.at[1 + k]))
        kept[k].start()

    def arrive(h):
        for chain in chains:
            chain.arrive(h)

    def part_of(half):
        def produce(turn, y, c, x, out):
            at = place_of(y, c, x, half)

            def step(i, carry):
                columns = pl.ds(pl.multiple_of(i * TILE, TILE), TILE)
                out[:, columns] = dot_wide(attended[at, :], w_out[:, columns]).astype(LOW)
                return carry

            lax.fori_loop(0, width // TILE, step, 0)

        return Scatter(produce, *scatter, part=half, start=half * HALF, size=HALF)

    total, landed = scatter[2], scatter[4]

    def chunk(here):
        value = x_own[here, :].astype(jnp.float32) + summed(total, landed, here)
        resid[here, :] = value
        own[here, :] = (value * inverse_of(value) * gain[...]).astype(LOW)

    def rows_of_half(half):
        if half == 0:
            fetch_x.wait()
        over_chunks(chunk, half)

    gather = Gather(own_halves(own), normed, send, recv)
    sum_and_gather(part_of, rows_of_half, gather, lambda turn: arrive(turn - 1) if turn > 0 else None)
    keep = pltpu.make_async_copy(own, normed.at[place_of(y, c, x)], local.at[0])
    keep.start()
    for chain in chains:
        chain.finish()
    for copy in kept + [keep]:
        copy.wait()


def close_attention(attended, w_out, x_whole, gain, w_gate, w_up):
    block, width = x_whole.shape[0] // 8, x_whole.shape[1]
    hidden = w_gate.shape[1]
    return pl.pallas_call(
        close_attention_kernel,
        out_shape=(
            jax.ShapeDtypeStruct((block, width), jnp.float32),
            jax.ShapeDtypeStruct((8 * block, width), LOW),
            jax.ShapeDtypeStruct((width, 4 * hidden), LOW),
            jax.ShapeDtypeStruct((width, 4 * hidden), LOW),
        ),
        in_specs=[in_vmem(), in_vmem(), anywhere()] + [in_vmem()] * 3,
        out_specs=[in_vmem()] + [anywhere()] * 3,
        scratch_shapes=[pltpu.VMEM((block, width), LOW)] * 2
        + scatter_scratch(width, 2)
        + [dma(GATHER_COPIES), dma(GATHER_COPIES), dma(3), *chain_sems(2)],
        compiler_params=remote_params(2),
        cost_estimate=pl.CostEstimate(flops=0, bytes_accessed=450_000_000, transcendentals=0),
    )(attended, w_out, x_whole, gain, w_gate, w_up)


def norm_back(value, gain, upstream):
    inverse = inverse_of(value)
    scaled = upstream * gain
    inner = jnp.mean(scaled * value, axis=-1, keepdims=True)
    return inverse * scaled - value * (inverse * inverse * inverse) * inner, upstream * value * inverse


def fold_rows(total, terms):
    for first in range(0, CHUNK, 8):
        total[...] += terms[first : first + 8, :]


def close_mlp_kernel(
    d_gate, d_up, w_gate, w_up, resid_home, upstream_home, gain, grad_a, grad_b, d_resid, gain_term, d_resid_whole,
    far_a, near_a, cross_a, far_b, near_b, cross_b, own, blocks, *scratch
):
    scatter, (send, recv, local, fetched, fold_send, fold_recv, fold_local, mine, theirs, resid, upstream, row_sems) = scratch[:7], scratch[7:]
    rows_fetched = [
        pltpu.make_async_copy(source, target, row_sems.at[k])
        for k, (source, target) in enumerate(((resid_home, resid), (upstream_home, upstream)))
    ]
    y, c, z, x = spot()
    width = w_gate.shape[0]
    order = [
        place_of(r, k, q, half)
        for half in (0, 1)
        for r, q in ((1 - y, 1 - x), (y, 1 - x), (1 - y, x), (y, x))
        for k in (1 - c, c)
    ]

    def fetch(turn):
        slot = turn % 2
        return [
            pltpu.make_async_copy(source.at[order[turn]], blocks.at[slot, m], fetched.at[slot, m])
            for m, source in enumerate((d_gate, d_up))
        ]

    for copy in fetch(0) + rows_fetched:
        copy.start()
    greet(near() + fold_peers())
    folds = [
        Fold(columns_of_layer(grad), *refs, mine.at[k], theirs, fold_send.at[k], fold_recv.at[k], fold_local.at[k])
        for k, (grad, *refs) in enumerate(((grad_a, far_a, near_a, cross_a), (grad_b, far_b, near_b, cross_b)))
    ]
    for fold in folds:
        fold.start()

    def part_of(half):
        def produce(turn, to_y, to_c, to_x, out):
            turn = turn + 8 * half
            if turn < 15:
                for copy in fetch(turn + 1):
                    copy.start()
            for copy in fetch(turn):
                copy.wait()

            def step(i, carry):
                columns = pl.ds(pl.multiple_of(i * TILE, TILE), TILE)
                part = dot_nt(blocks[turn % 2, 0], w_gate[columns, :]) + dot_nt(blocks[turn % 2, 1], w_up[columns, :])
                out[:, columns] = part.astype(LOW)
                return carry

            lax.fori_loop(0, width // TILE, step, 0)

        return Scatter(produce, *scatter, part=half, start=half * HALF, size=HALF)

    total, landed = scatter[2], scatter[4]
    gain_term[...] = jnp.zeros_like(gain_term)

    def chunk(here):
        back, terms = norm_back(resid[here, :], gain[...], summed(total, landed, here))
        value = upstream[here, :].astype(jnp.float32) + back
        d_resid[here, :] = value
        own[here, :] = value.astype(LOW)
        fold_rows(gain_term, terms)

    def rows_of_half(half):
        if half == 0:
            for copy in rows_fetched:
                copy.wait()
        over_chunks(chunk, half)

    gather = Gather(own_halves(own), d_resid_whole, send, recv)
    sum_and_gather(part_of, rows_of_half, gather, lambda turn: folds[turn].fold() if turn < 2 else None)
    keep = pltpu.make_async_copy(own, d_resid_whole.at[place_of(y, c, x)], local.at[0])
    keep.start()
    for fold in folds:
        fold.finish()
    keep.wait()


def close_mlp(d_gate, d_up, w_gate, w_up, resid, upstream, gain, *grads):
    block, width = resid.shape
    hidden = d_gate.shape[1]
    return pl.pallas_call(
        close_mlp_kernel,
        out_shape=(
            jax.ShapeDtypeStruct((block, width), jnp.float32),
            jax.ShapeDtypeStruct((8, width), jnp.float32),
            jax.ShapeDtypeStruct((8 * block, width), LOW),
            *[jax.ShapeDtypeStruct((width, hidden // 4), LOW)] * 6,
        ),
        in_specs=[anywhere()] * 2 + [in_vmem()] * 2 + [anywhere()] * 2 + [in_vmem()] + [anywhere()] * 2,
        out_specs=[in_vmem(), in_vmem()] + [anywhere()] * 7,
        scratch_shapes=[pltpu.VMEM((block, width), LOW), pltpu.VMEM((2, 2, block // 2, hidden), LOW)]
        + scatter_scratch(width, 2)
        + [dma(GATHER_COPIES), dma(GATHER_COPIES), dma(1), dma(2, 2), dma(2, 3), dma(2, 3), dma(2, 2)]
        + [pltpu.VMEM((2, width, hidden // 4), LOW), pltpu.VMEM((width, hidden // 4), LOW)]
        + [pltpu.VMEM((block, width), jnp.float32), pltpu.VMEM((block, width), LOW), dma(2)],
        compiler_params=remote_params(3),
        cost_estimate=pl.CostEstimate(flops=0, bytes_accessed=450_000_000, transcendentals=0),
    )(d_gate, d_up, w_gate, w_up, resid, upstream, gain, *grads)


def close_layer_kernel(
    d_qkv, w_qkv, x_whole, d_resid, gain, mlp_term, grad, grad_low, gain_grads, far, near_part, cross, grad_parts, own, terms, layer_terms, part, column_terms, *scratch
):
    scatter, (send, recv, term_send, term_recv, line_send, line_recv, x_own, x_sem, *rest) = scratch[:7], scratch[7:]
    mine, theirs, fold_send, fold_recv, fold_local, part_send, part_recv = rest
    y, c, z, x = spot()
    fetch_x = pltpu.make_async_copy(x_whole.at[place_of(y, c, x)], x_own, x_sem.at[0])
    fetch_x.start()
    partner = partner_of(y, c, z, x)
    moves = z != 2 * c + y
    width = w_qkv.shape[0]
    barrier = pltpu.get_barrier_semaphore()

    @pl.when(moves)
    def _():
        pl.semaphore_signal(barrier, inc=1, device_id=partner, device_id_type=MESH_ID)

    layer = others()
    line = line_of()
    for peer in layer + line:
        pl.semaphore_signal(barrier, inc=1, device_id=peer, device_id_type=MESH_ID)
    pl.semaphore_wait(barrier, len(layer + line) + moves.astype(jnp.int32))

    size = TILE // PIECES

    def part_of(piece):
        def produce(turn, to_y, to_c, to_x, out):
            at = quarter_of(to_y, to_c, to_x, piece // 2, piece % 2)

            def step(i, carry):
                columns = pl.ds(pl.multiple_of(i * TILE, TILE), TILE)
                out[:, columns] = dot_nt(d_qkv[at, :], w_qkv[columns, :]).astype(LOW)
                return carry

            lax.fori_loop(0, width // TILE, step, 0)

        return Scatter(produce, *scatter, part=piece, start=piece * size, size=size)

    fold = Fold(lambda at: grad.at[at], far, near_part, cross, mine, theirs, fold_send, fold_recv, fold_local)
    fold.start()
    def end_fold():
        fold.finish()
        for source, target, k in ((grad.at[z], mine, 0), (near_part, theirs, 1)):
            pltpu.make_async_copy(source, target, fold_local.at[k]).start()
        for source, target, k in ((grad.at[z], mine, 0), (near_part, theirs, 1)):
            pltpu.make_async_copy(source, target, fold_local.at[k]).wait()
        add_rows(mine, 0, theirs, 0, mine.shape[0])
        last = pltpu.make_async_copy(cross, theirs, fold_local.at[1])
        last.start()
        last.wait()
        add_rows(mine, 0, theirs, 0, mine.shape[0])
        shard = mine.shape[0] // 8
        index = 4 * y + 2 * c + x
        parts = [
            remote(
                mine.at[pl.ds(pl.multiple_of((4 * peer[0] + 2 * peer[1] + peer[3]) * shard, shard), shard)],
                grad_parts.at[index],
                part_send.at[k],
                part_recv.at[k],
                peer,
            )
            for k, peer in enumerate(layer)
        ]
        kept = pltpu.make_async_copy(mine.at[pl.ds(pl.multiple_of(index * shard, shard), shard)], grad_parts.at[index], fold_local.at[0])
        for copy in parts + [kept]:
            copy.start()
        return parts + [kept]

    sums = [part_of(piece) for piece in range(PIECES)]
    sums[0].begin()
    sums[0].relay()
    sums[1].begin()
    fold.fold()
    total, landed = scatter[2], scatter[4]
    terms[1] = mlp_term[...]
    terms[0] = jnp.zeros_like(mlp_term)
    pieces = [pl.ds(piece * size, size) for piece in range(PIECES)]
    trades = [remote(own.at[at], grad_low.at[at], send.at[k], recv.at[k], partner) for k, at in enumerate(pieces)]
    keeps = [pltpu.make_async_copy(own.at[at], grad_low.at[at], recv.at[k]) for k, at in enumerate(pieces)]
    fetch_x.wait()
    to_peers = []
    for piece in range(PIECES):
        if piece == PIECES - 1:
            to_peers = end_fold()
        sums[piece].arrive()

        def step(i, carry):
            here = pl.ds(pl.multiple_of(piece * size + i * CHUNK, CHUNK), CHUNK)
            back, products = norm_back(x_own[here, :].astype(jnp.float32), gain[...], summed(total, landed, here))
            own[here, :] = (d_resid[here, :] + back).astype(LOW)
            fold_rows(terms.at[0], products)
            return carry

        lax.fori_loop(0, size // CHUNK, step, 0)

        @pl.when(moves)
        def _():
            trades[piece].start()

        @pl.when(jnp.logical_not(moves))
        def _():
            keeps[piece].start()

        if piece + 1 < PIECES:
            sums[piece + 1].relay()
        if piece + 2 < PIECES:
            sums[piece + 2].begin()

    def columns_of(row, layers):
        return pl.ds(pl.multiple_of((4 * row) * HD, HD), layers * HD)

    spread = [
        remote(terms.at[:, :, columns_of(2 * peer[0] + peer[1], 4)], layer_terms.at[k], term_send.at[k], term_recv.at[k], peer)
        for k, peer in enumerate(layer)
    ]
    for copy in spread:
        copy.start()
    for copy in spread:
        copy.wait_recv()
    part[...] = sum((layer_terms[k] for k in range(7)), terms[:, :, columns_of(2 * y + c, 4)])
    lines = [
        remote(
            part.at[:, :, pl.ds(pl.multiple_of(peer[2] * HD, HD), HD)], column_terms.at[k], line_send.at[k], line_recv.at[k], peer
        )
        for k, peer in enumerate(line)
    ]
    for copy in lines:
        copy.start()
    for copy in lines:
        copy.wait_recv()
    gain_grads[...] = sum((column_terms[k] for k in range(3)), part[:, :, pl.ds(pl.multiple_of(z * HD, HD), HD)])
    for copy in spread + lines:
        copy.wait_send()
    for part_sum in sums:
        part_sum.finish()
    for copy in to_peers:
        copy.wait()

    @pl.when(moves)
    def _():
        for copy in trades:
            copy.wait()

    @pl.when(jnp.logical_not(moves))
    def _():
        for copy in keeps:
            copy.wait()


def close_layer(d_qkv, w_qkv, x_whole, d_resid, gain, mlp_term, grad):
    block, width = d_resid.shape
    return pl.pallas_call(
        close_layer_kernel,
        out_shape=(
            jax.ShapeDtypeStruct((block, width), LOW),
            jax.ShapeDtypeStruct((2, 8, width // 16), jnp.float32),
            *[jax.ShapeDtypeStruct(grad.shape[1:], LOW)] * 3,
            jax.ShapeDtypeStruct((8, grad.shape[1] // 8, grad.shape[2]), LOW),
        ),
        in_specs=[in_vmem(), in_vmem(), anywhere()] + [in_vmem()] * 3 + [anywhere()],
        out_specs=[anywhere(), in_vmem()] + [anywhere()] * 4,
        scratch_shapes=[
            pltpu.VMEM((block, width), LOW),
            pltpu.VMEM((2, 8, width), jnp.float32),
            pltpu.VMEM((7, 2, 8, width // 4), jnp.float32),
            pltpu.VMEM((2, 8, width // 4), jnp.float32),
            pltpu.VMEM((3, 2, 8, width // 16), jnp.float32),
        ]
        + scatter_scratch(width, PIECES)
        + [dma(PIECES), dma(PIECES), dma(7), dma(7), dma(3), dma(3), pltpu.VMEM((block, width), LOW), dma(1)]
        + [pltpu.VMEM(grad.shape[1:], LOW)] * 2
        + [dma(3), dma(3), dma(2), dma(7), dma(7)],
        compiler_params=remote_params(4),
        cost_estimate=pl.CostEstimate(flops=0, bytes_accessed=350_000_000, transcendentals=0),
    )(d_qkv, w_qkv, x_whole, d_resid, gain, mlp_term, grad)


def doc_start(ends, place):
    start = jnp.zeros_like(place)
    for k in range(8):
        start = jnp.where(ends[k] <= place, ends[k], start)
    return jnp.where(place < ends[7], start, LEN)


def sigmoid_of(raw):
    return pl.reciprocal(1.0 + jnp.exp2(math.log2(LEN) - raw * (math.log2(math.e) / math.sqrt(HD))), approx=True)


def tile_at(index):
    return pl.ds(pl.multiple_of(index * TILE, TILE), TILE)


def head_of(array, rows, part, head):
    first = (part * (array.shape[1] // 3) // HD + head) * HD
    return array[rows, first : first + HD]


def attend_kernel(ends, qkv, out, total):
    i = pl.program_id(0)
    heads = qkv.shape[1] // (3 * HD)
    total[...] = jnp.zeros_like(total)
    q_place = i * TILE + lax.broadcasted_iota(jnp.int32, (TILE, 1), 0)
    q_start = doc_start(ends, q_place)

    def tile(j, diagonal):
        k_place = j * TILE + lax.broadcasted_iota(jnp.int32, (1, TILE), 1)
        allowed = k_place >= q_start
        if diagonal:
            allowed = allowed & (k_place <= q_place)
        for head in range(heads):
            raw = dot_nt(head_of(qkv, tile_at(i), 0, head), head_of(qkv, tile_at(j), 1, head))
            weight = jnp.where(allowed, sigmoid_of(raw), 0.0).astype(LOW)
            total[head] += dot_wide(weight, head_of(qkv, tile_at(j), 2, head))

    def step(j, carry):
        tile(j, False)
        return carry

    lax.fori_loop(0, i, step, 0)
    tile(i, True)
    for head in range(heads):
        out[tile_at(i), head * HD : (head + 1) * HD] = total[head].astype(LOW)


def open_mlp_kernel(normed, w_gate, w_up, upstream, gate, up, hidden, upstream_whole, send, recv, local):
    i = pl.program_id(0)
    y, c, z, x = spot()
    steps = pl.num_programs(0)
    gather = Gather(lambda half: upstream.at[pl.ds(half * HALF, HALF)], upstream_whole, send, recv)
    keep = pltpu.make_async_copy(upstream, upstream_whole.at[place_of(y, c, x)], local.at[0])

    @pl.when(i == 0)
    def _():
        greet(near())
        gather.start(0)
        gather.start(1)
        keep.start()

    def step(n, carry):
        columns = pl.ds(pl.multiple_of(n * TILE, TILE), TILE)
        gate_part, up_part = dot_wide(normed[...], w_gate[:, columns]), dot_wide(normed[...], w_up[:, columns])
        gate[:, columns] = gate_part
        up[:, columns] = up_part
        hidden[:, columns] = (gate_part * jax.nn.sigmoid(gate_part) * up_part).astype(LOW)
        return carry

    lax.fori_loop(0, w_gate.shape[1] // TILE, step, 0)

    @pl.when(i == steps - 1)
    def _():
        for half in (0, 1):
            gather.pass_near(half)
        for half in (0, 1):
            gather.pass_far(half)
        gather.finish()
        keep.wait()


def open_mlp(normed, w_gate, w_up, upstream):
    places, width = normed.shape
    hidden = w_gate.shape[1]
    rows = lambda columns: pl.BlockSpec((TILE, columns), lambda i: (i, 0))
    whole = lambda array: pl.BlockSpec(array.shape, lambda i: (0, 0))
    return pl.pallas_call(
        open_mlp_kernel,
        out_shape=(
            jax.ShapeDtypeStruct((places, hidden), jnp.float32),
            jax.ShapeDtypeStruct((places, hidden), jnp.float32),
            jax.ShapeDtypeStruct((places, hidden), LOW),
            jax.ShapeDtypeStruct((places, width), LOW),
        ),
        grid=(places // TILE,),
        in_specs=[rows(width), whole(w_gate), whole(w_up), whole(upstream)],
        out_specs=[rows(hidden), rows(hidden), rows(hidden), anywhere()],
        scratch_shapes=[dma(GATHER_COPIES), dma(GATHER_COPIES), dma(1)],
        compiler_params=remote_params(5),
        cost_estimate=pl.CostEstimate(flops=0, bytes_accessed=250_000_000, transcendentals=0),
    )(normed, w_gate, w_up, upstream)


def out_turns():
    y, c, z, x = spot()
    layers = (x, x, 3 - x, 3 - x)
    owners = [((y, c, layers[j], j % 2), (z == layers[j]) & (x == j % 2)) for j in range(4)]
    side = lax.rem((z + 1) // 2, 2)
    holders = [((y, c, j, side), (z == j) & (x == side)) for j in range(4)]
    return owners, holders


def attend_back_kernel(
    ends, qkv, grads, out_grad, mixed, out, out_parts, mixed_home, query_total, key_total, value_total, send, recv, *trade_parts
):
    j = pl.program_id(0)
    y, c, z, x = spot()
    heads = qkv.shape[1] // (3 * HD)
    shard = out_grad.shape[0] // 4
    owners, holders = out_turns()
    trade = Trade(
        [mixed.at[pl.ds(half * HALF, HALF)] for half in (0, 1)], lambda half, at: mixed_home.at[pl.ds(half * HALF, HALF)], *trade_parts
    )

    def to_owner(turn):
        return remote(out_grad.at[pl.ds(turn * shard, shard)], out_parts.at[z], send.at[turn], recv.at[z], owners[turn][0])

    def to_self(turn):
        return pltpu.make_async_copy(out_grad.at[pl.ds(turn * shard, shard)], out_parts.at[z], recv.at[z])

    @pl.when(j == 0)
    def _():
        query_total[...] = jnp.zeros_like(query_total)
        barrier = pltpu.get_barrier_semaphore()
        for peer, here in holders:

            @pl.when(jnp.logical_not(here))
            def _():
                pl.semaphore_signal(barrier, inc=1, device_id=peer, device_id_type=MESH_ID)

        pl.semaphore_wait(barrier, 4 - (x == lax.rem((z + 1) // 2, 2)).astype(jnp.int32) + trade.greet(barrier, False))
        for half in (0, 1):
            trade.start(half)
        for turn in range(4):

            @pl.when(jnp.logical_not(owners[turn][1]))
            def _():
                to_owner(turn).start()

            @pl.when(owners[turn][1])
            def _():
                to_self(turn).start()

    key_total[...] = jnp.zeros_like(key_total)
    value_total[...] = jnp.zeros_like(value_total)
    here = tile_at(j)
    k_place = j * TILE + lax.broadcasted_iota(jnp.int32, (TILE, 1), 0)
    turned = [head_of(qkv, here, 1, head).T for head in range(heads)]

    def tile(i, diagonal):
        q_place = i * TILE + lax.broadcasted_iota(jnp.int32, (1, TILE), 1)
        allowed = k_place >= doc_start(ends, q_place)
        if diagonal:
            allowed = allowed & (k_place <= q_place)
        for head in range(heads):
            query, grad = head_of(qkv, tile_at(i), 0, head), grads[tile_at(i), head * HD : (head + 1) * HD]
            sig = jnp.where(allowed, sigmoid_of(dot_nt(head_of(qkv, here, 1, head), query)), 0.0)
            value_total[head] += dot_wide(sig.astype(LOW), grad)
            d_score = (dot_nt(head_of(qkv, here, 2, head), grad) * (sig * (1.0 - sig))).astype(LOW)
            key_total[head] += dot_wide(d_score, query)
            query_total[head, :, tile_at(i)] += dot_wide(turned[head], d_score)

    def step(i, carry):
        tile(i, False)
        return carry

    tile(j, True)
    lax.fori_loop(j + 1, LEN // TILE, step, 0)
    scale = 1.0 / math.sqrt(HD)
    for head in range(heads):
        first = head * HD
        out[here, heads * HD + first : (heads + 1) * HD + first] = (key_total[head] * scale).astype(LOW)
        out[here, 2 * heads * HD + first : (2 * heads + 1) * HD + first] = value_total[head].astype(LOW)
        out[here, first : first + HD] = (query_total[head, :, here] * scale).T.astype(LOW)

    @pl.when(j == LEN // TILE - 1)
    def _():
        for turn in range(4):

            @pl.when(jnp.logical_not(owners[turn][1]))
            def _():
                to_owner(turn).wait_send()

            @pl.when(jnp.logical_not(holders[turn][1]))
            def _():
                landed = out_parts.at[turn]
                remote(landed, landed, send.at[turn], recv.at[turn], holders[turn][0]).wait_recv()

            @pl.when(owners[turn][1])
            def _():
                to_self(turn).wait()

        for half in (0, 1):
            trade.arrive(half)
        trade.finish()

    @pl.when(j == 1)
    def _():
        for half in (0, 1):
            trade.forward(half)


def back_mlp_kernel(upstream, w_down, gate, up, d_gate, d_up):
    def step(n, carry):
        columns = pl.ds(pl.multiple_of(n * TILE, TILE), TILE)
        d_hidden = dot_nt(upstream[...], w_down[columns, :])
        d_gate[:, columns], d_up[:, columns] = gate_backward(
            d_hidden, gate[:, columns], up[:, columns], jax.nn.sigmoid(gate[:, columns])
        )
        return carry

    lax.fori_loop(0, gate.shape[1] // TILE, step, 0, unroll=2)


def back_mlp(upstream, w_down, gate, up):
    places, width = upstream.shape
    hidden = gate.shape[1]
    rows = lambda size: pl.BlockSpec((TILE, size), lambda i: (i, 0))
    return pl.pallas_call(
        back_mlp_kernel,
        out_shape=(jax.ShapeDtypeStruct((places, hidden), LOW), jax.ShapeDtypeStruct((places, hidden), LOW)),
        grid=(places // TILE,),
        in_specs=[rows(width), pl.BlockSpec(w_down.shape, lambda i: (0, 0)), rows(hidden), rows(hidden)],
        out_specs=[rows(hidden), rows(hidden)],
        compiler_params=pltpu.CompilerParams(vmem_limit_bytes=VMEM_LIMIT),
        cost_estimate=pl.CostEstimate(flops=0, bytes_accessed=90_000_000, transcendentals=0),
    )(upstream, w_down, gate, up)


def attend(ends, qkv):
    places, width = qkv.shape
    heads = width // (3 * HD)
    whole = lambda columns: pl.BlockSpec((places, columns), lambda i: (0, 0))
    return pl.pallas_call(
        attend_kernel,
        out_shape=jax.ShapeDtypeStruct((places, width // 3), LOW),
        grid=(places // TILE,),
        in_specs=[pl.BlockSpec(memory_space=pltpu.SMEM), whole(width)],
        out_specs=whole(width // 3),
        scratch_shapes=[pltpu.VMEM((heads, TILE, HD), jnp.float32)],
        compiler_params=pltpu.CompilerParams(vmem_limit_bytes=VMEM_LIMIT),
        cost_estimate=pl.CostEstimate(flops=0, bytes_accessed=150_000_000, transcendentals=0),
    )(ends, qkv)


def attend_back(ends, qkv, grads, out_grad, mixed):
    places, width = qkv.shape
    heads = width // (3 * HD)
    whole = lambda columns: pl.BlockSpec((places, columns), lambda j: (0, 0))
    return pl.pallas_call(
        attend_back_kernel,
        out_shape=(
            jax.ShapeDtypeStruct((places, width), LOW),
            jax.ShapeDtypeStruct((4, out_grad.shape[0] // 4, out_grad.shape[1]), LOW),
            jax.ShapeDtypeStruct(mixed.shape, LOW),
        ),
        grid=(places // TILE,),
        in_specs=[pl.BlockSpec(memory_space=pltpu.SMEM), whole(width), whole(width // 3), anywhere(), pl.BlockSpec(mixed.shape, lambda j: (0, 0))],
        out_specs=[whole(width), anywhere(), anywhere()],
        scratch_shapes=[
            pltpu.VMEM((heads, HD, places), jnp.float32),
            pltpu.VMEM((heads, TILE, HD), jnp.float32),
            pltpu.VMEM((heads, TILE, HD), jnp.float32),
            dma(4),
            dma(4),
            *trade_scratch(2, HALF, mixed.shape[1]),
        ],
        compiler_params=remote_params(6),
        cost_estimate=pl.CostEstimate(flops=0, bytes_accessed=300_000_000, transcendentals=0),
    )(ends, qkv, grads, out_grad, mixed)


LAYER = ("y", "c", "x")
PLACES = ("c", "y", "x")
ALL = ("y", "c", "z", "x")


def trade(part):
    pairs = []
    for y in range(2):
        for c in range(2):
            for z in range(4):
                for x in range(2):
                    pairs.append((((y * 2 + c) * 4 + z) * 2 + x, (((z % 2) * 2 + z // 2) * 4 + 2 * c + y) * 2 + x))
    return lax.ppermute(part, ALL, pairs)


def after(first, then):
    return lax.optimization_barrier((first, then))[1]


def body_layers(
    tokens, lengths, cotangent, w_query, w_key, w_value, w_out, w_gate, w_up, w_down, gain_attn, gain_mlp
):
    rows_here, block, width = tokens.shape
    members = lax.axis_size(LAYER)
    layers = lax.axis_size("z")
    shard = w_query.shape[0]
    owned = width // members
    facts = jnp.zeros((8, 2 * shard), jnp.float32)
    facts = facts.at[0, :shard].set(gain_attn.astype(jnp.float32)).at[1, :shard].set(gain_mlp.astype(jnp.float32))
    facts = facts.at[2, : lengths.shape[1]].set(lengths[0].astype(jnp.float32))
    layer_x, w_qkv, facts = begin(tokens.reshape(block, width), w_query, w_key, w_value, facts)
    full_gain_attn, full_gain_mlp = facts[:, :, :, 0, :shard].reshape(1, width), facts[:, :, :, 1, :shard].reshape(1, width)
    layer = lax.axis_index("z")
    own_lengths = facts[:, 0, 0, 2, : lengths.shape[1]].reshape(2, 2, -1)
    own_lengths = lax.dynamic_slice(own_lengths, (layer % 2, layer // 2, 0), (1, 1, own_lengths.shape[2]))[0, 0]
    ends = jnp.cumsum(own_lengths.astype(jnp.int32))
    layer_normed = norm_forward(layer_x.astype(jnp.float32), full_gain_attn)[0].astype(LOW)
    here = lax.axis_index("x")
    out_rows = lax.all_gather(after(facts, w_out), ("z", "x"), axis=0, tiled=True)
    w_out_own = [lax.dynamic_slice_in_dim(out_rows, head * HD, HD, 0) for head in (here, 3 - here)]
    w_out_own = jnp.concatenate(w_out_own, axis=0)

    qkv = dot_wide(layer_normed, w_qkv).astype(LOW)
    upstream = trade(after(facts, cotangent)).reshape(block, width)
    attended = attend(ends, qkv)
    resid, layer_mlp, own_gate, own_up = close_attention(after(upstream, attended), w_out_own, layer_x, full_gain_mlp, w_gate, w_up)

    own_down = lax.all_gather(after(resid, w_down), "z", axis=0, tiled=True)
    gate, up_part, hidden, layer_upstream = open_mlp(layer_mlp, own_gate, own_up, upstream)
    part = dot_wide(hidden, own_down).astype(LOW)
    mixed_sum = lax.psum_scatter(part, PLACES, scatter_dimension=0, tiled=True)
    down_term = contract_rows(after(part, hidden), layer_upstream).astype(LOW)
    down_rows = w_down.shape[0]
    down_parts = []
    for up in range(1, 4):
        layers_pairs = [(at, (at + up) % 4) for at in range(4)]
        slab = lax.dynamic_slice_in_dim(down_term, (layer + up) % 4 * down_rows, down_rows, 0)
        down_parts.append(lax.ppermute(slab, "z", layers_pairs))
    d_gate, d_up = back_mlp(after(down_term, layer_upstream), own_down, gate, up_part)
    gate_term, up_term = contract_rows(layer_mlp, d_gate).astype(LOW), contract_rows(layer_mlp, d_up).astype(LOW)
    d_resid, gain_mlp_term, layer_d_resid, *parts = close_mlp(
        after(mixed_sum, d_gate), d_up, own_gate, own_up, resid, upstream, full_gain_mlp, gate_term, up_term
    )

    def own_part(whole, near_part, cross):
        own = lax.dynamic_slice_in_dim(whole, layer * cross.shape[1], cross.shape[1], 1)
        return own.astype(jnp.float32) + near_part.astype(jnp.float32) + cross.astype(jnp.float32)

    mixed = (resid + after(layer_d_resid, mixed_sum).astype(jnp.float32)).astype(LOW)
    grad_down = lax.dynamic_slice_in_dim(down_term, layer * down_rows, down_rows, 0).astype(jnp.float32)
    grad_down = grad_down + sum(slab.astype(jnp.float32) for slab in after(layer_d_resid, down_parts))

    out_term = contract_rows(attended, layer_d_resid).astype(LOW)
    d_attended = contract_cols(layer_d_resid, w_out_own).astype(LOW)
    d_qkv, out_parts, mixed = attend_back(ends, qkv, d_attended, out_term, mixed)
    mixed = mixed.reshape(rows_here, block, width)
    grad_gate, grad_up = own_part(gate_term, *parts[1:3]), own_part(up_term, *parts[4:6])
    grad_out = jnp.sum(out_parts.astype(jnp.float32), axis=0)
    qkv_term = contract_rows(layer_normed, d_qkv).astype(LOW)
    qkv_term = qkv_term.reshape(4, layers, 2 * shard, 3 * owned).transpose(1, 0, 2, 3)
    qkv_term = qkv_term.reshape(layers, members * shard, 3 * owned)
    grad_low, gain_grads, *_, parts = close_layer(
        d_qkv, w_qkv, layer_x, d_resid, full_gain_attn, gain_mlp_term, qkv_term
    )
    grad_tokens = grad_low.astype(jnp.float32).reshape(rows_here, block, width)
    parts = parts.reshape(4, 2, shard, 3, 2, HD)
    parts = jnp.stack((parts[:, 0, :, :, 0], parts[:, 1, :, :, 0], parts[:, 1, :, :, 1], parts[:, 0, :, :, 1]), axis=1)
    grad_query, grad_key, grad_value = parts.transpose(3, 2, 0, 1, 4).astype(jnp.float32).reshape(3, shard, width)
    gain_grads = lax.dynamic_index_in_dim(jnp.sum(gain_grads, axis=1).reshape(2, 2, shard), lax.axis_index("x"), 1, False)
    return (
        mixed,
        grad_tokens,
        grad_query,
        grad_key,
        grad_value,
        grad_out,
        grad_gate,
        grad_up,
        grad_down,
        gain_grads[0],
        gain_grads[1],
    )


def body_any(
    tokens,
    lengths,
    cotangent,
    w_query,
    w_key,
    w_value,
    w_out,
    w_gate,
    w_up,
    w_down,
    gain_attn,
    gain_mlp,
):
    rows_here, block, width = tokens.shape
    count = rows_here * block
    scale = 1.0 / math.sqrt(HD)
    kv_place = lax.axis_index("kv")
    key_places = kv_place * block + jnp.arange(block, dtype=jnp.int32)
    attn_set = (
        lax.all_gather(w_query, ("row", "kv"), axis=0, tiled=True),
        lax.all_gather(w_key, ("row", "kv"), axis=0, tiled=True),
        lax.all_gather(w_value, ("row", "kv"), axis=0, tiled=True),
        lax.all_gather(w_out, ("row", "kv"), axis=0, tiled=True),
        lax.all_gather(gain_attn, ("row", "kv"), axis=0, tiled=True),
        lax.all_gather(gain_mlp, ("row", "kv"), axis=0, tiled=True),
    )
    full_query, full_key, full_value, full_out, full_gain_attn, full_gain_mlp = attn_set
    flat = tokens.reshape(count, width).astype(jnp.float32)
    normed_attn, inverse_attn = norm_forward(flat, full_gain_attn)
    normed_attn_low = normed_attn.astype(jnp.bfloat16)
    query_low = jnp.dot(normed_attn_low, full_query, preferred_element_type=jnp.float32).astype(
        jnp.bfloat16
    )
    key_low = jnp.dot(normed_attn_low, full_key, preferred_element_type=jnp.float32).astype(
        jnp.bfloat16
    )
    value_low = jnp.dot(normed_attn_low, full_value, preferred_element_type=jnp.float32).astype(
        jnp.bfloat16
    )
    key_heads = key_low.reshape(rows_here, block, H, HD)
    value_heads = value_low.reshape(rows_here, block, H, HD)
    segment, valid = segment_table(lengths)
    key_segment = lax.dynamic_slice_in_dim(segment, kv_place * block, block, 1)
    key_valid = lax.dynamic_slice_in_dim(valid, kv_place * block, block, 1)
    queries_all = lax.all_gather(
        query_low.reshape(rows_here, block, width), "kv", axis=1, tiled=True
    )
    which = 0
    query_rows = queries_all[which]
    query_segment = segment[which]
    sigmoid_part, allowed = score_block(
        query_rows,
        key_heads[which],
        query_segment,
        key_segment[which],
        key_valid[which],
        jnp.int32(0),
        key_places,
    )
    weight = (sigmoid_part * allowed).astype(jnp.bfloat16)
    summed = jnp.einsum(
        "hqk,khd->qhd", weight, value_heads[which], preferred_element_type=jnp.float32
    )
    pieces = [
        lax.psum_scatter(
            summed.reshape(lax.axis_size("kv") * block, width).astype(jnp.bfloat16),
            "kv",
            scatter_dimension=0,
            tiled=True,
        ).astype(jnp.float32)
    ]
    attended_low = jnp.stack(pieces).reshape(count, width).astype(jnp.bfloat16)
    resid = flat + jnp.dot(attended_low, full_out, preferred_element_type=jnp.float32)
    normed_mlp, inverse_mlp = norm_forward(resid, full_gain_mlp)
    normed_mlp_low = normed_mlp.astype(jnp.bfloat16)
    upstream_low = cotangent.reshape(count, width)
    upstream = upstream_low.astype(jnp.float32)
    slice_gate, slice_up, slice_down = (
        lax.all_gather(w_gate, "row", axis=1, tiled=True),
        lax.all_gather(w_up, "row", axis=1, tiled=True),
        lax.all_gather(w_down, "row", axis=0, tiled=True),
    )
    row_normed, row_upstream = (
        lax.all_gather(normed_mlp_low.reshape(rows_here, block, width), "kv", axis=1, tiled=True),
        lax.all_gather(cotangent, "kv", axis=1, tiled=True),
    )
    normed_rows = row_normed.reshape(rows_here * LEN, width)
    upstream_rows = row_upstream.reshape(rows_here * LEN, width)
    gate = jnp.dot(normed_rows, slice_gate, preferred_element_type=jnp.float32)
    up_part = jnp.dot(normed_rows, slice_up, preferred_element_type=jnp.float32)
    sigmoid_gate = jax.nn.sigmoid(gate)
    hidden_low = (gate * sigmoid_gate * up_part).astype(jnp.bfloat16)
    hidden_rows = hidden_low.reshape(rows_here, LEN, hidden_low.shape[1])
    which = 0
    hidden_part = hidden_rows[which]
    outputs = [
        lax.psum_scatter(
            jnp.dot(hidden_part, slice_down, preferred_element_type=jnp.float32).astype(
                jnp.bfloat16
            ),
            "kv",
            scatter_dimension=0,
            tiled=True,
        ).astype(jnp.float32)
    ]
    result = resid + jnp.stack(outputs).reshape(count, width)
    d_hidden = contract_cols(upstream_rows, slice_down)
    d_gate, d_up = gate_backward(d_hidden, gate, up_part, sigmoid_gate)
    partial_normed = contract_cols(d_gate, slice_gate) + contract_cols(d_up, slice_up)
    d_normed_mlp = (
        lax.psum_scatter(
            partial_normed.reshape(rows_here, LEN, width).astype(jnp.bfloat16),
            "kv",
            scatter_dimension=1,
            tiled=True,
        )
        .astype(jnp.float32)
        .reshape(count, width)
    )
    grad_gate, grad_up, grad_down = (
        lax.psum_scatter(
            contract_rows(normed_rows, d_gate).astype(jnp.bfloat16),
            "row",
            scatter_dimension=1,
            tiled=True,
        ).astype(jnp.float32),
        lax.psum_scatter(
            contract_rows(normed_rows, d_up).astype(jnp.bfloat16),
            "row",
            scatter_dimension=1,
            tiled=True,
        ).astype(jnp.float32),
        lax.psum_scatter(
            contract_rows(hidden_low, upstream_rows).astype(jnp.bfloat16),
            "row",
            scatter_dimension=0,
            tiled=True,
        ).astype(jnp.float32),
    )
    mixed = result.astype(jnp.bfloat16).reshape(rows_here, block, width)
    back_mlp, gain_mlp_term = norm_backward(resid, inverse_mlp, full_gain_mlp, d_normed_mlp)
    d_resid = upstream + back_mlp
    d_resid_low = d_resid.astype(jnp.bfloat16)
    d_attended = contract_cols(d_resid_low, full_out).astype(jnp.bfloat16)
    grads_all = lax.all_gather(
        d_attended.reshape(rows_here, block, width), "kv", axis=1, tiled=True
    )
    query_block = min(512, LEN)
    block_count = LEN // query_block
    which = 0

    def sweep(carry, index, which=which):
        key_total, value_total = carry
        start = index * query_block
        query_rows = lax.dynamic_slice_in_dim(queries_all[which], start, query_block, 0)
        grad_rows = lax.dynamic_slice_in_dim(grads_all[which], start, query_block, 0)
        query_segment = lax.dynamic_slice_in_dim(segment[which], start, query_block, 0)
        sigmoid_part, allowed = score_block(
            query_rows,
            key_heads[which],
            query_segment,
            key_segment[which],
            key_valid[which],
            start,
            key_places,
        )
        weight = (sigmoid_part * allowed).astype(jnp.bfloat16)
        grad_heads = grad_rows.reshape(query_block, H, HD)
        value_total = value_total + jnp.einsum(
            "hqk,qhd->khd", weight, grad_heads, preferred_element_type=jnp.float32
        )
        d_weight = jnp.einsum(
            "qhd,khd->hqk", grad_heads, value_heads[which], preferred_element_type=jnp.float32
        )
        d_score = (d_weight * sigmoid_part * (1.0 - sigmoid_part) * allowed).astype(jnp.bfloat16)
        query_part = (
            jnp.einsum(
                "hqk,khd->qhd", d_score, key_heads[which], preferred_element_type=jnp.float32
            )
            * scale
        )
        key_total = (
            key_total
            + jnp.einsum(
                "hqk,qhd->khd",
                d_score,
                query_rows.reshape(query_block, H, HD),
                preferred_element_type=jnp.float32,
            )
            * scale
        )
        return ((key_total, value_total), query_part.reshape(query_block, width))

    zeros = jnp.zeros((block, H, HD), jnp.float32)
    totals, query_parts = lax.scan(sweep, (zeros, zeros), jnp.arange(block_count, dtype=jnp.int32))
    query_terms = [query_parts.reshape(LEN, width)]
    key_grads = [totals[0].reshape(block, width)]
    value_grads = [totals[1].reshape(block, width)]
    query_local = lax.psum_scatter(
        jnp.stack(query_terms).astype(jnp.bfloat16), "kv", scatter_dimension=1, tiled=True
    ).astype(jnp.float32)
    d_query_low = query_local.reshape(count, width).astype(jnp.bfloat16)
    d_key_low = jnp.stack(key_grads).reshape(count, width).astype(jnp.bfloat16)
    d_value_low = jnp.stack(value_grads).reshape(count, width).astype(jnp.bfloat16)
    d_normed_attn = (
        contract_cols(d_query_low, full_query)
        + contract_cols(d_key_low, full_key)
        + contract_cols(d_value_low, full_value)
    )
    back_attn, gain_attn_term = norm_backward(flat, inverse_attn, full_gain_attn, d_normed_attn)
    grad_tokens = (d_resid + back_attn).reshape(rows_here, block, width)
    projected_low = jnp.concatenate((d_query_low, d_key_low, d_value_low), axis=1)
    grad_projections = lax.psum_scatter(
        contract_rows(normed_attn_low, projected_low),
        ("row", "kv"),
        scatter_dimension=0,
        tiled=True,
    )
    out_term = contract_rows(attended_low, d_resid_low)
    grad_out, grad_gain_attn, grad_gain_mlp = (
        lax.psum_scatter(out_term, ("row", "kv"), scatter_dimension=0, tiled=True),
        lax.psum_scatter(gain_attn_term, ("row", "kv"), scatter_dimension=0, tiled=True),
        lax.psum_scatter(gain_mlp_term, ("row", "kv"), scatter_dimension=0, tiled=True),
    )
    grad_query = grad_projections[:, :width]
    grad_key = grad_projections[:, width : 2 * width]
    grad_value = grad_projections[:, 2 * width :]
    return (
        mixed,
        grad_tokens,
        grad_query,
        grad_key,
        grad_value,
        grad_out,
        grad_gate,
        grad_up,
        grad_down,
        grad_gain_attn,
        grad_gain_mlp,
    )


def solution(mesh):
    rows, columns = mesh.shape["row"], mesh.shape["kv"]
    if rows == 4 and columns == 2 * rows:
        mesh = Mesh(mesh.devices.reshape(2, 2, rows, 2), ("y", "c", "z", "x"))
        row, kv, run = ("y", "c"), ("z", "x"), body_layers
    else:
        row, kv, run = "row", "kv", body_any
    both = ("y", "c", "z", "x") if run is body_layers else ("row", "kv")
    tall, wide, flat = P(both, None), P(None, both), P(both)
    tokens = P(row, kv, None)
    return jax.shard_map(
        run,
        mesh=mesh,
        in_specs=(tokens, P(row, None), tokens, tall, tall, tall, tall, wide, wide, tall, flat, flat),
        out_specs=(tokens, tokens, tall, tall, tall, tall, wide, wide, tall, flat, flat),
        check_vma=False,
    )
```

```python
import functools
import math

import jax
import jax.numpy as jnp
from jax import lax
from jax.experimental import pallas as pl
from jax.experimental.pallas import tpu as pltpu
from jax.sharding import Mesh, PartitionSpec as P

H = 16
HD = 128
LEN = 4096


EPSILON = 1e-05


def contract_rows(left, right):
    return lax.dot_general(
        left, right, (((0,), (0,)), ((), ())), preferred_element_type=jnp.float32
    )


def contract_cols(left, right):
    return lax.dot_general(
        left, right, (((1,), (1,)), ((), ())), preferred_element_type=jnp.float32
    )


def norm_forward(value, gain):
    inverse = lax.rsqrt(jnp.mean(value * value, axis=-1, keepdims=True) + EPSILON)
    return (value * inverse * gain.astype(jnp.float32), inverse)


def norm_backward(value, inverse, gain, upstream):
    scaled = upstream * gain.astype(jnp.float32)
    inner = jnp.mean(scaled * value, axis=-1, keepdims=True)
    back = inverse * scaled - value * (inverse * inverse * inverse) * inner
    gain_term = jnp.sum(upstream * value * inverse, axis=0)
    return (back, gain_term)


def segment_table(lengths):
    ends = jnp.cumsum(lengths, axis=-1)
    places = jnp.arange(LEN, dtype=jnp.int32)
    segment = jnp.sum((ends[:, None, :] <= places[None, :, None]).astype(jnp.int32), axis=-1)
    valid = places[None, :] < ends[:, -1:]
    return (segment, valid)


def score_block(
    query_rows, key_heads, query_segment, key_segment, key_valid, query_start, key_places
):
    count = query_rows.shape[0]
    query_heads = query_rows.reshape(count, H, HD)
    raw = jnp.einsum("qhd,khd->hqk", query_heads, key_heads, preferred_element_type=jnp.float32)
    scores = raw * (1.0 / math.sqrt(HD)) - math.log(LEN)
    places = query_start + jnp.arange(count, dtype=jnp.int32)
    allowed = (
        (key_places[None, :] <= places[:, None])
        & (key_segment[None, :] == query_segment[:, None])
        & key_valid[None, :]
    )
    return (jax.nn.sigmoid(scores), allowed.astype(jnp.float32)[None])


def gate_backward(d_hidden, gate, up_part, sigmoid_gate):
    d_gate = (d_hidden * up_part * sigmoid_gate * (1.0 + gate * (1.0 - sigmoid_gate))).astype(
        jnp.bfloat16
    )
    d_up = (d_hidden * gate * sigmoid_gate).astype(jnp.bfloat16)
    return (d_gate, d_up)


TILE = 512
LOW = jnp.bfloat16
VMEM_LIMIT = 60 * 1024 * 1024


def dot_nt(left, right):
    return lax.dot_general(left, right, (((1,), (1,)), ((), ())), preferred_element_type=jnp.float32)


def dot_wide(left, right):
    return jnp.dot(left, right, preferred_element_type=jnp.float32)


HALF = TILE // 2
PIECES = 4
CHUNK = 32
MESH_ID = pl.DeviceIdType.MESH


def flip(bit, by):
    return bit + by - 2 * bit * by


def spot():
    return tuple(lax.axis_index(name) for name in ("y", "c", "z", "x"))


def near():
    y, c, z, x = spot()
    return (y, c, z, 1 - x), (1 - y, c, z, x), (y, 1 - c, z, x)


def partner_of(y, c, z, x):
    return lax.rem(z, 2), z // 2, 2 * c + y, x


def place_of(y, c, x, half=None):
    first = (4 * c + 2 * y + x) * TILE
    if half is None:
        return pl.ds(pl.multiple_of(first, TILE), TILE)
    return pl.ds(pl.multiple_of(first + half * HALF, HALF), HALF)


def quarter_of(y, c, x, half, quarter):
    return pl.ds(pl.multiple_of((4 * c + 2 * y + x) * TILE + half * HALF + quarter * (HALF // 2), HALF // 2), HALF // 2)


def remote(src, dst, send, recv, peer):
    return pltpu.make_async_remote_copy(
        src_ref=src, dst_ref=dst, send_sem=send, recv_sem=recv, device_id=peer, device_id_type=MESH_ID
    )


def greet(peers):
    barrier = pltpu.get_barrier_semaphore()
    for peer in peers:
        pl.semaphore_signal(barrier, inc=1, device_id=peer, device_id_type=MESH_ID)
    pl.semaphore_wait(barrier, len(peers))


class Gather:
    def __init__(self, own, whole, send, recv):
        y, c, z, x = spot()
        across_x, across_y, core = near()

        def passed(k, at, peer):
            return remote(whole.at[at], whole.at[at], send.at[k], recv.at[k], peer)

        self.halves = []
        for half in (0, 1):
            k, at = 9 * half, place_of(y, c, x, half)
            mine = [
                remote(own(half), whole.at[at], send.at[k + m], recv.at[k + m], peer)
                for m, peer in enumerate((across_x, across_y, core))
            ]
            held_x, held_y = (y, c, 1 - x), (1 - y, c, x)
            far = (1 - y, c, 1 - x)
            self.halves.append(
                (
                    mine,
                    passed(k + 3, quarter_of(*held_x, half, 0), across_y),
                    passed(k + 4, quarter_of(*held_y, half, 1), across_x),
                    [passed(k + 5, place_of(*held_x, half), core), passed(k + 6, place_of(*held_y, half), core)],
                    [passed(k + 7 + q, quarter_of(*far, half, q), core) for q in (0, 1)],
                )
            )

    def start(self, half):
        for copy in self.halves[half][0]:
            copy.start()

    def pass_near(self, half):
        mine, over_y, over_x, from_near, from_far = self.halves[half]
        mine[0].wait_recv()
        over_y.start()
        from_near[0].start()
        mine[1].wait_recv()
        over_x.start()
        from_near[1].start()

    def pass_far(self, half):
        mine, over_y, over_x, from_near, from_far = self.halves[half]
        over_y.wait_recv()
        from_far[0].start()
        over_x.wait_recv()
        from_far[1].start()

    def finish(self):
        for mine, over_y, over_x, from_near, from_far in self.halves:
            for copy in [mine[2]] + from_near + from_far:
                copy.wait_recv()
            for copy in mine + [over_y, over_x] + from_near + from_far:
                copy.wait_send()


GATHER_COPIES = 18


class GatherWhole:
    def __init__(self, own, whole, send, recv):
        y, c, z, x = spot()
        across_x, across_y, core = near()

        def from_own(k, half, peer):
            return remote(own(half), whole.at[place_of(y, c, x, half)], send.at[k], recv.at[k], peer)

        def passed(k, at, peer):
            return remote(whole.at[at], whole.at[at], send.at[k], recv.at[k], peer)

        self.mine = [
            [from_own(0, 0, across_x), from_own(1, 0, across_y), from_own(2, 0, core)],
            [from_own(3, 1, across_x), from_own(4, 1, across_y), from_own(5, 1, core)],
        ]
        held_x = [place_of(y, c, 1 - x, half) for half in (0, 1)]
        held_y = [place_of(1 - y, c, x, half) for half in (0, 1)]
        far = [place_of(1 - y, c, 1 - x, half) for half in (0, 1)]
        self.over_y, self.over_x = passed(6, held_x[0], across_y), passed(7, held_y[1], across_x)
        self.core_x = [passed(8 + half, held_x[half], core) for half in (0, 1)]
        self.core_y = [passed(10 + half, held_y[half], core) for half in (0, 1)]
        self.core_far = [passed(12 + half, far[half], core) for half in (0, 1)]

    def start(self, half):
        for copy in self.mine[half]:
            copy.start()

    def pass_first(self):
        self.mine[0][0].wait_recv()
        self.over_y.start()
        self.core_x[0].start()
        self.mine[0][1].wait_recv()
        self.core_y[0].start()

    def pass_second(self):
        self.mine[1][1].wait_recv()
        self.over_x.start()
        self.core_y[1].start()
        self.mine[1][0].wait_recv()
        self.core_x[1].start()

    def pass_far(self):
        self.over_y.wait_recv()
        self.core_far[0].start()
        self.over_x.wait_recv()
        self.core_far[1].start()

    def finish(self):
        from_core = [self.mine[0][2], self.mine[1][2]] + self.core_x + self.core_y + self.core_far
        for copy in from_core:
            copy.wait_recv()
        for copy in self.mine[0] + self.mine[1] + [self.over_y, self.over_x] + self.core_x + self.core_y + self.core_far:
            copy.wait_send()


class Trade:
    def __init__(self, sources, dst, held, send, recv, held_recv, pass_send, detour=True):
        y, c, z, x = spot()
        self.detour = detour
        across_y = (1 - y, c, z, x)
        self.moves = z != 2 * c + y
        self.away = (y == c) & (z == 1 + y)
        self.straight = self.moves & jnp.logical_not(self.away) if detour else self.moves
        self.passes = (1 - y == c) & (z == 2 - y)
        partner = partner_of(y, c, z, x)
        comes_by = ((partner[0] == partner[1]) & (partner[2] == 1 + partner[0])).astype(jnp.int32)
        self.sender = (flip(partner[0], comes_by), partner[1], partner[2], x) if detour else partner
        self.across_y = across_y
        target = partner_of(*across_y)
        self.direct, self.keep, self.out, self.onward = [], [], [], []
        for h, source in enumerate(sources):
            self.direct.append(remote(source, dst(h, partner), send.at[h], recv.at[h], partner))
            self.keep.append(pltpu.make_async_copy(source, dst(h, (y, c, z, x)), recv.at[h]))
            self.out.append(remote(source, held.at[h], send.at[h], held_recv.at[h], across_y))
            self.onward.append(remote(held.at[h], dst(h, target), pass_send.at[h], recv.at[h], target))

    def greet(self, barrier, neighbours_greet):
        @pl.when(self.moves)
        def _():
            pl.semaphore_signal(barrier, inc=1, device_id=self.sender, device_id_type=MESH_ID)

        count = self.straight.astype(jnp.int32)
        if not self.detour:
            return count
        count = count + self.passes.astype(jnp.int32)
        if not neighbours_greet:

            @pl.when(self.passes)
            def _():
                pl.semaphore_signal(barrier, inc=1, device_id=self.across_y, device_id_type=MESH_ID)

            count = count + self.away.astype(jnp.int32)
        return count

    def start(self, h):
        @pl.when(self.straight)
        def _():
            self.direct[h].start()

        if self.detour:

            @pl.when(self.away)
            def _():
                self.out[h].start()

        @pl.when(jnp.logical_not(self.moves))
        def _():
            self.keep[h].start()

    def wait_sent(self, h):
        @pl.when(self.straight)
        def _():
            self.direct[h].wait_send()

        if self.detour:

            @pl.when(self.away)
            def _():
                self.out[h].wait_send()

    def forward(self, h):
        if self.detour:

            @pl.when(self.passes)
            def _():
                self.out[h].wait_recv()
                self.onward[h].start()

    def arrive(self, h):
        @pl.when(self.moves)
        def _():
            self.direct[h].wait_recv()

        @pl.when(jnp.logical_not(self.moves))
        def _():
            self.keep[h].wait()

    def finish(self, first=0):
        for h in range(len(self.direct)):
            if h >= first:
                self.wait_sent(h)

            if self.detour:

                @pl.when(self.passes)
                def _():
                    self.onward[h].wait_send()


def trade_scratch(pieces, rows, width):
    return [pltpu.VMEM((pieces, rows, width), LOW)] + [pltpu.SemaphoreType.DMA((pieces,)) for _ in range(4)]


class Chain:
    def __init__(self, own, slab, sems, index):
        self.own, self.slab, self.sems, self.index = own, slab, sems, index
        self.last = lax.axis_size("z") - 1

    def move(self, which, h, source, layer, to):
        y, c, z, x = spot()
        return remote(
            source, self.slab(layer), self.sems[2 * which].at[self.index, h], self.sems[2 * which + 1].at[self.index, h], (y, c, to, x)
        )

    def up(self, h):
        z = lax.axis_index("z")
        return self.move(0, h, self.own if h == 0 else self.slab(z - h), z - h, z + 1)

    def down(self, h):
        z = lax.axis_index("z")
        return self.move(1, h, self.own if h == 0 else self.slab(z + h), z + h, z - 1)

    def start(self):
        z = lax.axis_index("z")

        @pl.when(z < self.last)
        def _():
            self.up(0).start()

        @pl.when(z > 0)
        def _():
            self.down(0).start()

    def arrive(self, h):
        z = lax.axis_index("z")

        @pl.when(z - h - 1 >= 0)
        def _():
            self.move(0, h, self.slab(z - h - 1), z - h - 1, z).wait_recv()
            if h < 2:

                @pl.when(z < self.last)
                def _():
                    self.up(h + 1).start()

        @pl.when(z + h + 1 <= self.last)
        def _():
            self.move(1, h, self.slab(z + h + 1), z + h + 1, z).wait_recv()
            if h < 2:

                @pl.when(z > 0)
                def _():
                    self.down(h + 1).start()

    def finish(self):
        z = lax.axis_index("z")
        for h in range(3):

            @pl.when((z < self.last) & (z - h >= 0))
            def _():
                self.up(h).wait_send()

            @pl.when((z > 0) & (z + h <= self.last))
            def _():
                self.down(h).wait_send()


def chain_sems(count):
    return [pltpu.SemaphoreType.DMA((count, 3)) for _ in range(4)]


def greet_neighbours(peers):
    y, c, z, x = spot()
    last = lax.axis_size("z") - 1
    barrier = pltpu.get_barrier_semaphore()
    for peer in peers:
        pl.semaphore_signal(barrier, inc=1, device_id=peer, device_id_type=MESH_ID)

    @pl.when(z > 0)
    def _():
        pl.semaphore_signal(barrier, inc=1, device_id=(y, c, z - 1, x), device_id_type=MESH_ID)

    @pl.when(z < last)
    def _():
        pl.semaphore_signal(barrier, inc=1, device_id=(y, c, z + 1, x), device_id_type=MESH_ID)

    return barrier, len(peers) + (z > 0).astype(jnp.int32) + (z < last).astype(jnp.int32)


def others():
    y, c, z, x = spot()
    return [(flip(y, dy), flip(c, dc), z, flip(x, dx)) for dy in (0, 1) for dc in (0, 1) for dx in (0, 1) if dy + dc + dx]


def line_of():
    y, c, z, x = spot()
    return [(y, c, lax.rem(z + dz, 4), x) for dz in (1, 2, 3)]


class Fold:
    def __init__(self, slab, far, near_part, cross, mine, theirs, send, recv, local):
        y, c, z, x = spot()
        a, b = z // 2, lax.rem(z, 2)
        pair, middle = (y, c, 2 * a + 1 - b, x), (y, c, 2 * (1 - a) + b, x)
        self.far = remote(slab(2 * (1 - a) + 1 - b), far, send.at[0], recv.at[0], pair)
        self.near = remote(slab(2 * a + 1 - b), near_part, send.at[1], recv.at[1], pair)
        self.cross = remote(mine, cross, send.at[2], recv.at[2], middle)
        self.fetches = [
            pltpu.make_async_copy(slab(2 * (1 - a) + b), mine, local.at[0]),
            pltpu.make_async_copy(far, theirs, local.at[1]),
        ]
        self.mine, self.theirs = mine, theirs

    def start(self):
        self.far.start()
        self.fetches[0].start()

    def fold(self):
        self.far.wait_recv()
        self.fetches[1].start()
        for copy in self.fetches:
            copy.wait()
        add_rows(self.mine, 0, self.theirs, 0, self.mine.shape[0])
        self.cross.start()
        self.near.start()

    def finish(self):
        for copy in (self.near, self.cross):
            copy.wait_recv()
        for copy in (self.far, self.near, self.cross):
            copy.wait_send()


def columns_of_layer(whole):
    size = whole.shape[1] // 4
    return lambda at: whole.at[:, pl.ds(pl.multiple_of(at * size, size), size)]


def fold_peers():
    y, c, z, x = spot()
    a, b = z // 2, lax.rem(z, 2)
    return ((y, c, 2 * a + 1 - b, x), (y, c, 2 * (1 - a) + b, x))


def add_rows(total, first, term, start, count):
    def step(i, carry):
        here = pl.ds(pl.multiple_of(first + i * CHUNK, CHUNK), CHUNK)
        there = pl.ds(pl.multiple_of(start + i * CHUNK, CHUNK), CHUNK)
        total[here, :] = (total[here, :].astype(jnp.float32) + term[there, :].astype(jnp.float32)).astype(LOW)
        return carry

    lax.fori_loop(0, count // CHUNK, step, 0)


def scatter_scratch(width, parts=1):
    return [
        pltpu.VMEM((2, TILE, width), LOW),
        pltpu.VMEM((4, TILE, width), LOW),
        pltpu.VMEM((4, TILE, width), LOW),
        pltpu.VMEM((2, HALF, width), LOW),
        pltpu.VMEM((2, TILE, width), LOW),
        pltpu.SemaphoreType.DMA((parts, 10)),
        pltpu.SemaphoreType.DMA((parts, 10)),
    ]


class Scatter:
    def __init__(self, produce, staged, core_part, total, relayed, landed, send, recv, part=0, start=0, size=TILE):
        across_x, across_y, core = near()
        self.produce, self.staged, self.core_part, self.total, self.relayed = produce, staged, core_part, total, relayed
        self.start, self.size, self.half = start, size, size // 2
        send, recv = send.at[part], recv.at[part]
        rows = pl.ds(start, size)
        halves = (pl.ds(start, self.half), pl.ds(start + self.half, self.half))
        self.relay_row = start // 2
        passing = pl.ds(self.relay_row, self.half)
        self.to_core = [
            remote(staged.at[k % 2, rows], core_part.at[k, rows], send.at[k], recv.at[k], core) for k in range(4)
        ]
        self.far_x = remote(total.at[0, halves[0]], relayed.at[0, passing], send.at[4], recv.at[4], across_x)
        self.far_y = remote(total.at[0, halves[1]], relayed.at[1, passing], send.at[5], recv.at[5], across_y)
        self.to_x = [
            remote(total.at[1, at], landed.at[0, at], send.at[6 + half], recv.at[6 + half], across_x)
            for half, at in enumerate(halves)
        ]
        self.to_y = [
            remote(total.at[2, at], landed.at[1, at], send.at[8 + half], recv.at[8 + half], across_y)
            for half, at in enumerate(halves)
        ]

    def begin(self):
        y, c, z, x = spot()
        rows = pl.ds(self.start, self.size)
        for k, (to_row, to_column) in enumerate(((1 - y, 1 - x), (y, 1 - x), (1 - y, x), (y, x))):
            if k >= 2:
                self.to_core[k - 2].wait_send()
            self.produce(2 * k, to_row, 1 - c, to_column, self.staged.at[k % 2, rows])
            self.to_core[k].start()
            self.produce(2 * k + 1, to_row, c, to_column, self.total.at[k, rows])
            self.to_core[k].wait_recv()
            add_rows(self.total.at[k], self.start, self.core_part.at[k], self.start, self.size)
            if k == 0:
                self.far_x.start()
                self.far_y.start()
            if k == 1:
                self.to_x[0].start()
            if k == 2:
                self.to_y[1].start()

    def relay(self):
        self.far_y.wait_recv()
        add_rows(self.total.at[1], self.start + self.half, self.relayed.at[1], self.relay_row, self.half)
        self.to_x[1].start()
        self.far_x.wait_recv()
        add_rows(self.total.at[2], self.start, self.relayed.at[0], self.relay_row, self.half)
        self.to_y[0].start()

    def arrive(self):
        for copy in self.to_x + self.to_y:
            copy.wait_recv()

    def finish(self):
        for copy in self.to_core[2:] + [self.far_x, self.far_y] + self.to_x + self.to_y:
            copy.wait_send()


def sum_and_gather(part_of, rows_of_half, gather, beside):
    sums = [part_of(half) for half in (0, 1)]
    sums[0].begin()
    sums[0].relay()
    sums[1].begin()
    sums[0].arrive()
    rows_of_half(0)
    gather.start(0)
    beside(0)
    sums[1].relay()
    beside(1)
    sums[1].arrive()
    rows_of_half(1)
    gather.start(1)
    gather.pass_near(0)
    beside(2)
    gather.pass_near(1)
    gather.pass_far(0)
    gather.pass_far(1)
    gather.finish()
    beside(3)
    for half in (0, 1):
        sums[half].finish()


def begin_kernel(
    x_own, w_query, w_key, w_value, facts, x_whole, w_qkv, facts_whole,
    gather_send, gather_recv, w_send, w_recv, fact_send, fact_recv, local, *scratch
):
    y, c, z, x = spot()
    row = 2 * y + c
    layer = others()
    trade_parts, sems = scratch[:5], scratch[5:]
    trade = Trade(
        [x_own.at[half] for half in (0, 1)], lambda half, at: x_whole.at[place_of(at[0], at[1], at[3], half)], *trade_parts, detour=False
    )
    barrier, count = greet_neighbours(layer)
    pl.semaphore_wait(barrier, count + trade.greet(barrier, True))

    shard = w_query.shape[0]
    for half in (0, 1):
        trade.start(half)
    spread = [
        remote(facts, facts_whole.at[row, z, x], fact_send.at[k], fact_recv.at[k], peer) for k, peer in enumerate(layer)
    ]
    kept = [pltpu.make_async_copy(facts, facts_whole.at[row, z, x], local.at[6])]
    for m in range(6):
        source, slot = (w_query, w_key, w_value)[m // 2], m % 2

        def columns_of(at):
            head = 4 * (2 * at[0] + at[1]) + (3 - at[3] if slot else at[3])
            return source.at[:, pl.ds(pl.multiple_of(head * HD, HD), HD)]

        dst = w_qkv.at[row, z, pl.ds(pl.multiple_of(x * shard, shard), shard), pl.ds(m * HD, HD)]
        for k, peer in enumerate(layer):
            spread.append(remote(columns_of(peer), dst, w_send.at[m, k], w_recv.at[m, k], peer))
        kept.append(pltpu.make_async_copy(columns_of((y, c, z, x)), dst, local.at[m]))
    for copy in spread + kept:
        copy.start()

    gather = GatherWhole(lambda half: x_whole.at[place_of(y, c, x, half)], x_whole, gather_send, gather_recv)
    for half in (0, 1):
        trade.forward(half)
        trade.arrive(half)
        gather.start(half)

    for copy in kept:
        copy.wait()
    for copy in spread:
        copy.wait_recv()
    chains = [
        Chain(facts_whole.at[:, z], lambda at: facts_whole.at[:, at], sems, 0),
        Chain(w_qkv.at[:, z], lambda at: w_qkv.at[:, at], sems, 1),
    ]

    def arrive(h):
        for chain in chains:
            chain.arrive(h)

    for chain in chains:
        chain.start()
    gather.pass_first()
    arrive(0)
    gather.pass_second()
    arrive(1)
    gather.pass_far()
    arrive(2)
    gather.finish()
    trade.finish()
    for copy in spread:
        copy.wait_send()
    for chain in chains:
        chain.finish()


def anywhere():
    return pl.BlockSpec(memory_space=pl.ANY)


def in_vmem():
    return pl.BlockSpec(memory_space=pltpu.VMEM)


def dma(*shape):
    return pltpu.SemaphoreType.DMA(shape)


def remote_params(number):
    return pltpu.CompilerParams(collective_id=number, has_side_effects=True, vmem_limit_bytes=VMEM_LIMIT)


def begin(x_own, w_query, w_key, w_value, facts):
    block, width = x_own.shape
    shard = w_query.shape[0]
    x_whole, w_qkv, facts_whole = pl.pallas_call(
        begin_kernel,
        out_shape=(
            jax.ShapeDtypeStruct((8 * block, width), LOW),
            jax.ShapeDtypeStruct((4, 4, 2 * shard, 3 * width // 8), LOW),
            jax.ShapeDtypeStruct((4, 4, 2, *facts.shape), jnp.float32),
        ),
        in_specs=[in_vmem()] + [anywhere()] * 4,
        out_specs=[anywhere()] * 3,
        scratch_shapes=[
            dma(GATHER_COPIES), dma(GATHER_COPIES), dma(6, 7), dma(6, 7), dma(7), dma(7), dma(7),
            *trade_scratch(2, block // 2, width), *chain_sems(2),
        ],
        compiler_params=remote_params(1),
        cost_estimate=pl.CostEstimate(flops=0, bytes_accessed=350_000_000, transcendentals=0),
    )(x_own.reshape(2, block // 2, width), w_query, w_key, w_value, facts)
    return x_whole, w_qkv.reshape(width, 3 * width // 8), facts_whole


def summed(total, landed, here):
    parts = (total[3, here, :], landed[0, here, :], landed[1, here, :])
    return sum(part.astype(jnp.float32) for part in parts)


def over_chunks(work, half):
    def step(i, carry):
        work(pl.ds(pl.multiple_of(half * HALF + i * CHUNK, CHUNK), CHUNK))
        return carry

    lax.fori_loop(0, HALF // CHUNK, step, 0)


def own_halves(own):
    return lambda half: own.at[pl.ds(half * HALF, HALF)]


def inverse_of(value):
    return lax.rsqrt(jnp.mean(value * value, axis=-1, keepdims=True) + EPSILON)


def close_attention_kernel(attended, w_out, x_whole, gain, w_gate, w_up, resid, normed, own_gate, own_up, own, x_own, *scratch):
    scatter, (send, recv, local), sems = scratch[:7], scratch[7:10], scratch[10:]
    y, c, z, x = spot()
    fetch_x = pltpu.make_async_copy(x_whole.at[place_of(y, c, x)], x_own, local.at[0])
    fetch_x.start()
    width = w_out.shape[1]
    hidden = w_gate.shape[1]
    z = lax.axis_index("z")
    barrier, count = greet_neighbours(near())
    pl.semaphore_wait(barrier, count)

    def slab_of(whole):
        return lambda at: whole.at[:, pl.ds(pl.multiple_of(at * hidden, hidden), hidden)]

    chains, kept = [], []
    for k, (part, whole) in enumerate(((w_gate, own_gate), (w_up, own_up))):
        chains.append(Chain(part, slab_of(whole), sems, k))
        chains[k].start()
        kept.append(pltpu.make_async_copy(part, slab_of(whole)(z), local.at[1 + k]))
        kept[k].start()

    def arrive(h):
        for chain in chains:
            chain.arrive(h)

    def part_of(half):
        def produce(turn, y, c, x, out):
            at = place_of(y, c, x, half)

            def step(i, carry):
                columns = pl.ds(pl.multiple_of(i * TILE, TILE), TILE)
                out[:, columns] = dot_wide(attended[at, :], w_out[:, columns]).astype(LOW)
                return carry

            lax.fori_loop(0, width // TILE, step, 0)

        return Scatter(produce, *scatter, part=half, start=half * HALF, size=HALF)

    total, landed = scatter[2], scatter[4]

    def chunk(here):
        value = x_own[here, :].astype(jnp.float32) + summed(total, landed, here)
        resid[here, :] = value
        own[here, :] = (value * inverse_of(value) * gain[...]).astype(LOW)

    def rows_of_half(half):
        if half == 0:
            fetch_x.wait()
        over_chunks(chunk, half)

    gather = Gather(own_halves(own), normed, send, recv)
    sum_and_gather(part_of, rows_of_half, gather, lambda turn: arrive(turn - 1) if turn > 0 else None)
    keep = pltpu.make_async_copy(own, normed.at[place_of(y, c, x)], local.at[0])
    keep.start()
    for chain in chains:
        chain.finish()
    for copy in kept + [keep]:
        copy.wait()


def close_attention(attended, w_out, x_whole, gain, w_gate, w_up):
    block, width = x_whole.shape[0] // 8, x_whole.shape[1]
    hidden = w_gate.shape[1]
    return pl.pallas_call(
        close_attention_kernel,
        out_shape=(
            jax.ShapeDtypeStruct((block, width), jnp.float32),
            jax.ShapeDtypeStruct((8 * block, width), LOW),
            jax.ShapeDtypeStruct((width, 4 * hidden), LOW),
            jax.ShapeDtypeStruct((width, 4 * hidden), LOW),
        ),
        in_specs=[in_vmem(), in_vmem(), anywhere()] + [in_vmem()] * 3,
        out_specs=[in_vmem()] + [anywhere()] * 3,
        scratch_shapes=[pltpu.VMEM((block, width), LOW)] * 2
        + scatter_scratch(width, 2)
        + [dma(GATHER_COPIES), dma(GATHER_COPIES), dma(3), *chain_sems(2)],
        compiler_params=remote_params(2),
        cost_estimate=pl.CostEstimate(flops=0, bytes_accessed=450_000_000, transcendentals=0),
    )(attended, w_out, x_whole, gain, w_gate, w_up)


def norm_back(value, gain, upstream):
    inverse = inverse_of(value)
    scaled = upstream * gain
    inner = jnp.mean(scaled * value, axis=-1, keepdims=True)
    return inverse * scaled - value * (inverse * inverse * inverse) * inner, upstream * value * inverse


def fold_rows(total, terms):
    for first in range(0, CHUNK, 8):
        total[...] += terms[first : first + 8, :]


def close_mlp_kernel(
    d_gate, d_up, w_gate, w_up, resid_home, upstream_home, gain, grad_a, grad_b, d_resid, gain_term, d_resid_whole,
    far_a, near_a, cross_a, far_b, near_b, cross_b, own, blocks, *scratch
):
    scatter, (send, recv, local, fetched, fold_send, fold_recv, fold_local, mine, theirs, resid, upstream, row_sems) = scratch[:7], scratch[7:]
    rows_fetched = [
        pltpu.make_async_copy(source, target, row_sems.at[k])
        for k, (source, target) in enumerate(((resid_home, resid), (upstream_home, upstream)))
    ]
    y, c, z, x = spot()
    width = w_gate.shape[0]
    order = [
        place_of(r, k, q, half)
        for half in (0, 1)
        for r, q in ((1 - y, 1 - x), (y, 1 - x), (1 - y, x), (y, x))
        for k in (1 - c, c)
    ]

    def fetch(turn):
        slot = turn % 2
        return [
            pltpu.make_async_copy(source.at[order[turn]], blocks.at[slot, m], fetched.at[slot, m])
            for m, source in enumerate((d_gate, d_up))
        ]

    for copy in fetch(0) + rows_fetched:
        copy.start()
    greet(near() + fold_peers())
    folds = [
        Fold(columns_of_layer(grad), *refs, mine.at[k], theirs, fold_send.at[k], fold_recv.at[k], fold_local.at[k])
        for k, (grad, *refs) in enumerate(((grad_a, far_a, near_a, cross_a), (grad_b, far_b, near_b, cross_b)))
    ]
    for fold in folds:
        fold.start()

    def part_of(half):
        def produce(turn, to_y, to_c, to_x, out):
            turn = turn + 8 * half
            if turn < 15:
                for copy in fetch(turn + 1):
                    copy.start()
            for copy in fetch(turn):
                copy.wait()

            def step(i, carry):
                columns = pl.ds(pl.multiple_of(i * TILE, TILE), TILE)
                part = dot_nt(blocks[turn % 2, 0], w_gate[columns, :]) + dot_nt(blocks[turn % 2, 1], w_up[columns, :])
                out[:, columns] = part.astype(LOW)
                return carry

            lax.fori_loop(0, width // TILE, step, 0)

        return Scatter(produce, *scatter, part=half, start=half * HALF, size=HALF)

    total, landed = scatter[2], scatter[4]
    gain_term[...] = jnp.zeros_like(gain_term)

    def chunk(here):
        back, terms = norm_back(resid[here, :], gain[...], summed(total, landed, here))
        value = upstream[here, :].astype(jnp.float32) + back
        d_resid[here, :] = value
        own[here, :] = value.astype(LOW)
        fold_rows(gain_term, terms)

    def rows_of_half(half):
        if half == 0:
            for copy in rows_fetched:
                copy.wait()
        over_chunks(chunk, half)

    gather = Gather(own_halves(own), d_resid_whole, send, recv)
    sum_and_gather(part_of, rows_of_half, gather, lambda turn: folds[turn].fold() if turn < 2 else None)
    keep = pltpu.make_async_copy(own, d_resid_whole.at[place_of(y, c, x)], local.at[0])
    keep.start()
    for fold in folds:
        fold.finish()
    keep.wait()


def close_mlp(d_gate, d_up, w_gate, w_up, resid, upstream, gain, *grads):
    block, width = resid.shape
    hidden = d_gate.shape[1]
    return pl.pallas_call(
        close_mlp_kernel,
        out_shape=(
            jax.ShapeDtypeStruct((block, width), jnp.float32),
            jax.ShapeDtypeStruct((8, width), jnp.float32),
            jax.ShapeDtypeStruct((8 * block, width), LOW),
            *[jax.ShapeDtypeStruct((width, hidden // 4), LOW)] * 6,
        ),
        in_specs=[anywhere()] * 2 + [in_vmem()] * 2 + [anywhere()] * 2 + [in_vmem()] + [anywhere()] * 2,
        out_specs=[in_vmem(), in_vmem()] + [anywhere()] * 7,
        scratch_shapes=[pltpu.VMEM((block, width), LOW), pltpu.VMEM((2, 2, block // 2, hidden), LOW)]
        + scatter_scratch(width, 2)
        + [dma(GATHER_COPIES), dma(GATHER_COPIES), dma(1), dma(2, 2), dma(2, 3), dma(2, 3), dma(2, 2)]
        + [pltpu.VMEM((2, width, hidden // 4), LOW), pltpu.VMEM((width, hidden // 4), LOW)]
        + [pltpu.VMEM((block, width), jnp.float32), pltpu.VMEM((block, width), LOW), dma(2)],
        compiler_params=remote_params(3),
        cost_estimate=pl.CostEstimate(flops=0, bytes_accessed=450_000_000, transcendentals=0),
    )(d_gate, d_up, w_gate, w_up, resid, upstream, gain, *grads)


def close_layer_kernel(
    d_qkv, w_qkv, x_whole, d_resid, gain, mlp_term, grad, grad_low, gain_grads, far, near_part, cross, grad_parts, own, terms, layer_terms, part, column_terms, *scratch
):
    scatter, (send, recv, term_send, term_recv, line_send, line_recv, x_own, x_sem, *rest) = scratch[:7], scratch[7:]
    mine, theirs, fold_send, fold_recv, fold_local, part_send, part_recv = rest
    y, c, z, x = spot()
    fetch_x = pltpu.make_async_copy(x_whole.at[place_of(y, c, x)], x_own, x_sem.at[0])
    fetch_x.start()
    partner = partner_of(y, c, z, x)
    moves = z != 2 * c + y
    width = w_qkv.shape[0]
    barrier = pltpu.get_barrier_semaphore()

    @pl.when(moves)
    def _():
        pl.semaphore_signal(barrier, inc=1, device_id=partner, device_id_type=MESH_ID)

    layer = others()
    line = line_of()
    for peer in layer + line:
        pl.semaphore_signal(barrier, inc=1, device_id=peer, device_id_type=MESH_ID)
    pl.semaphore_wait(barrier, len(layer + line) + moves.astype(jnp.int32))

    size = TILE // PIECES

    def part_of(piece):
        def produce(turn, to_y, to_c, to_x, out):
            at = quarter_of(to_y, to_c, to_x, piece // 2, piece % 2)

            def step(i, carry):
                columns = pl.ds(pl.multiple_of(i * TILE, TILE), TILE)
                out[:, columns] = dot_nt(d_qkv[at, :], w_qkv[columns, :]).astype(LOW)
                return carry

            lax.fori_loop(0, width // TILE, step, 0)

        return Scatter(produce, *scatter, part=piece, start=piece * size, size=size)

    fold = Fold(lambda at: grad.at[at], far, near_part, cross, mine, theirs, fold_send, fold_recv, fold_local)
    fold.start()
    def end_fold():
        fold.finish()
        for source, target, k in ((grad.at[z], mine, 0), (near_part, theirs, 1)):
            pltpu.make_async_copy(source, target, fold_local.at[k]).start()
        for source, target, k in ((grad.at[z], mine, 0), (near_part, theirs, 1)):
            pltpu.make_async_copy(source, target, fold_local.at[k]).wait()
        add_rows(mine, 0, theirs, 0, mine.shape[0])
        last = pltpu.make_async_copy(cross, theirs, fold_local.at[1])
        last.start()
        last.wait()
        add_rows(mine, 0, theirs, 0, mine.shape[0])
        shard = mine.shape[0] // 8
        index = 4 * y + 2 * c + x
        parts = [
            remote(
                mine.at[pl.ds(pl.multiple_of((4 * peer[0] + 2 * peer[1] + peer[3]) * shard, shard), shard)],
                grad_parts.at[index],
                part_send.at[k],
                part_recv.at[k],
                peer,
            )
            for k, peer in enumerate(layer)
        ]
        kept = pltpu.make_async_copy(mine.at[pl.ds(pl.multiple_of(index * shard, shard), shard)], grad_parts.at[index], fold_local.at[0])
        for copy in parts + [kept]:
            copy.start()
        return parts + [kept]

    sums = [part_of(piece) for piece in range(PIECES)]
    sums[0].begin()
    sums[0].relay()
    sums[1].begin()
    fold.fold()
    total, landed = scatter[2], scatter[4]
    terms[1] = mlp_term[...]
    terms[0] = jnp.zeros_like(mlp_term)
    pieces = [pl.ds(piece * size, size) for piece in range(PIECES)]
    trades = [remote(own.at[at], grad_low.at[at], send.at[k], recv.at[k], partner) for k, at in enumerate(pieces)]
    keeps = [pltpu.make_async_copy(own.at[at], grad_low.at[at], recv.at[k]) for k, at in enumerate(pieces)]
    fetch_x.wait()
    to_peers = []
    for piece in range(PIECES):
        if piece == PIECES - 1:
            to_peers = end_fold()
        sums[piece].arrive()

        def step(i, carry):
            here = pl.ds(pl.multiple_of(piece * size + i * CHUNK, CHUNK), CHUNK)
            back, products = norm_back(x_own[here, :].astype(jnp.float32), gain[...], summed(total, landed, here))
            own[here, :] = (d_resid[here, :] + back).astype(LOW)
            fold_rows(terms.at[0], products)
            return carry

        lax.fori_loop(0, size // CHUNK, step, 0)

        @pl.when(moves)
        def _():
            trades[piece].start()

        @pl.when(jnp.logical_not(moves))
        def _():
            keeps[piece].start()

        if piece + 1 < PIECES:
            sums[piece + 1].relay()
        if piece + 2 < PIECES:
            sums[piece + 2].begin()

    def columns_of(row, layers):
        return pl.ds(pl.multiple_of((4 * row) * HD, HD), layers * HD)

    spread = [
        remote(terms.at[:, :, columns_of(2 * peer[0] + peer[1], 4)], layer_terms.at[k], term_send.at[k], term_recv.at[k], peer)
        for k, peer in enumerate(layer)
    ]
    for copy in spread:
        copy.start()
    for copy in spread:
        copy.wait_recv()
    part[...] = sum((layer_terms[k] for k in range(7)), terms[:, :, columns_of(2 * y + c, 4)])
    lines = [
        remote(
            part.at[:, :, pl.ds(pl.multiple_of(peer[2] * HD, HD), HD)], column_terms.at[k], line_send.at[k], line_recv.at[k], peer
        )
        for k, peer in enumerate(line)
    ]
    for copy in lines:
        copy.start()
    for copy in lines:
        copy.wait_recv()
    gain_grads[...] = sum((column_terms[k] for k in range(3)), part[:, :, pl.ds(pl.multiple_of(z * HD, HD), HD)])
    for copy in spread + lines:
        copy.wait_send()
    for part_sum in sums:
        part_sum.finish()
    for copy in to_peers:
        copy.wait()

    @pl.when(moves)
    def _():
        for copy in trades:
            copy.wait()

    @pl.when(jnp.logical_not(moves))
    def _():
        for copy in keeps:
            copy.wait()


def close_layer(d_qkv, w_qkv, x_whole, d_resid, gain, mlp_term, grad):
    block, width = d_resid.shape
    return pl.pallas_call(
        close_layer_kernel,
        out_shape=(
            jax.ShapeDtypeStruct((block, width), LOW),
            jax.ShapeDtypeStruct((2, 8, width // 16), jnp.float32),
            *[jax.ShapeDtypeStruct(grad.shape[1:], LOW)] * 3,
            jax.ShapeDtypeStruct((8, grad.shape[1] // 8, grad.shape[2]), LOW),
        ),
        in_specs=[in_vmem(), in_vmem(), anywhere()] + [in_vmem()] * 3 + [anywhere()],
        out_specs=[anywhere(), in_vmem()] + [anywhere()] * 4,
        scratch_shapes=[
            pltpu.VMEM((block, width), LOW),
            pltpu.VMEM((2, 8, width), jnp.float32),
            pltpu.VMEM((7, 2, 8, width // 4), jnp.float32),
            pltpu.VMEM((2, 8, width // 4), jnp.float32),
            pltpu.VMEM((3, 2, 8, width // 16), jnp.float32),
        ]
        + scatter_scratch(width, PIECES)
        + [dma(PIECES), dma(PIECES), dma(7), dma(7), dma(3), dma(3), pltpu.VMEM((block, width), LOW), dma(1)]
        + [pltpu.VMEM(grad.shape[1:], LOW)] * 2
        + [dma(3), dma(3), dma(2), dma(7), dma(7)],
        compiler_params=remote_params(4),
        cost_estimate=pl.CostEstimate(flops=0, bytes_accessed=350_000_000, transcendentals=0),
    )(d_qkv, w_qkv, x_whole, d_resid, gain, mlp_term, grad)


def doc_start(ends, place):
    start = jnp.zeros_like(place)
    for k in range(8):
        start = jnp.where(ends[k] <= place, ends[k], start)
    return jnp.where(place < ends[7], start, LEN)


def sigmoid_of(raw):
    return pl.reciprocal(1.0 + jnp.exp2(math.log2(LEN) - raw * (math.log2(math.e) / math.sqrt(HD))), approx=True)


def tile_at(index):
    return pl.ds(pl.multiple_of(index * TILE, TILE), TILE)


def head_of(array, rows, part, head):
    first = (part * (array.shape[1] // 3) // HD + head) * HD
    return array[rows, first : first + HD]


def attend_kernel(ends, qkv, out, total):
    i = pl.program_id(0)
    heads = qkv.shape[1] // (3 * HD)
    total[...] = jnp.zeros_like(total)
    q_place = i * TILE + lax.broadcasted_iota(jnp.int32, (TILE, 1), 0)
    q_start = doc_start(ends, q_place)

    def tile(j, diagonal):
        k_place = j * TILE + lax.broadcasted_iota(jnp.int32, (1, TILE), 1)
        allowed = k_place >= q_start
        if diagonal:
            allowed = allowed & (k_place <= q_place)
        for head in range(heads):
            raw = dot_nt(head_of(qkv, tile_at(i), 0, head), head_of(qkv, tile_at(j), 1, head))
            weight = jnp.where(allowed, sigmoid_of(raw), 0.0).astype(LOW)
            total[head] += dot_wide(weight, head_of(qkv, tile_at(j), 2, head))

    def step(j, carry):
        tile(j, False)
        return carry

    lax.fori_loop(0, i, step, 0)
    tile(i, True)
    for head in range(heads):
        out[tile_at(i), head * HD : (head + 1) * HD] = total[head].astype(LOW)


def open_mlp_kernel(normed, w_gate, w_up, upstream, gate, up, hidden, upstream_whole, send, recv, local):
    i = pl.program_id(0)
    y, c, z, x = spot()
    steps = pl.num_programs(0)
    gather = Gather(lambda half: upstream.at[pl.ds(half * HALF, HALF)], upstream_whole, send, recv)
    keep = pltpu.make_async_copy(upstream, upstream_whole.at[place_of(y, c, x)], local.at[0])

    @pl.when(i == 0)
    def _():
        greet(near())
        gather.start(0)
        gather.start(1)
        keep.start()

    def step(n, carry):
        columns = pl.ds(pl.multiple_of(n * TILE, TILE), TILE)
        gate_part, up_part = dot_wide(normed[...], w_gate[:, columns]), dot_wide(normed[...], w_up[:, columns])
        gate[:, columns] = gate_part
        up[:, columns] = up_part
        hidden[:, columns] = (gate_part * jax.nn.sigmoid(gate_part) * up_part).astype(LOW)
        return carry

    lax.fori_loop(0, w_gate.shape[1] // TILE, step, 0)

    @pl.when(i == steps - 1)
    def _():
        for half in (0, 1):
            gather.pass_near(half)
        for half in (0, 1):
            gather.pass_far(half)
        gather.finish()
        keep.wait()


def open_mlp(normed, w_gate, w_up, upstream):
    places, width = normed.shape
    hidden = w_gate.shape[1]
    rows = lambda columns: pl.BlockSpec((TILE, columns), lambda i: (i, 0))
    whole = lambda array: pl.BlockSpec(array.shape, lambda i: (0, 0))
    return pl.pallas_call(
        open_mlp_kernel,
        out_shape=(
            jax.ShapeDtypeStruct((places, hidden), jnp.float32),
            jax.ShapeDtypeStruct((places, hidden), jnp.float32),
            jax.ShapeDtypeStruct((places, hidden), LOW),
            jax.ShapeDtypeStruct((places, width), LOW),
        ),
        grid=(places // TILE,),
        in_specs=[rows(width), whole(w_gate), whole(w_up), whole(upstream)],
        out_specs=[rows(hidden), rows(hidden), rows(hidden), anywhere()],
        scratch_shapes=[dma(GATHER_COPIES), dma(GATHER_COPIES), dma(1)],
        compiler_params=remote_params(5),
        cost_estimate=pl.CostEstimate(flops=0, bytes_accessed=250_000_000, transcendentals=0),
    )(normed, w_gate, w_up, upstream)


def out_turns():
    y, c, z, x = spot()
    layers = (x, x, 3 - x, 3 - x)
    owners = [((y, c, layers[j], j % 2), (z == layers[j]) & (x == j % 2)) for j in range(4)]
    side = lax.rem((z + 1) // 2, 2)
    holders = [((y, c, j, side), (z == j) & (x == side)) for j in range(4)]
    return owners, holders


def attend_back_kernel(
    ends, qkv, grads, out_grad, mixed, out, out_parts, mixed_home, query_total, key_total, value_total, send, recv, *trade_parts
):
    j = pl.program_id(0)
    y, c, z, x = spot()
    heads = qkv.shape[1] // (3 * HD)
    shard = out_grad.shape[0] // 4
    owners, holders = out_turns()
    trade = Trade(
        [mixed.at[pl.ds(half * HALF, HALF)] for half in (0, 1)], lambda half, at: mixed_home.at[pl.ds(half * HALF, HALF)], *trade_parts
    )

    def to_owner(turn):
        return remote(out_grad.at[pl.ds(turn * shard, shard)], out_parts.at[z], send.at[turn], recv.at[z], owners[turn][0])

    def to_self(turn):
        return pltpu.make_async_copy(out_grad.at[pl.ds(turn * shard, shard)], out_parts.at[z], recv.at[z])

    @pl.when(j == 0)
    def _():
        query_total[...] = jnp.zeros_like(query_total)
        barrier = pltpu.get_barrier_semaphore()
        for peer, here in holders:

            @pl.when(jnp.logical_not(here))
            def _():
                pl.semaphore_signal(barrier, inc=1, device_id=peer, device_id_type=MESH_ID)

        pl.semaphore_wait(barrier, 4 - (x == lax.rem((z + 1) // 2, 2)).astype(jnp.int32) + trade.greet(barrier, False))
        for half in (0, 1):
            trade.start(half)
        for turn in range(4):

            @pl.when(jnp.logical_not(owners[turn][1]))
            def _():
                to_owner(turn).start()

            @pl.when(owners[turn][1])
            def _():
                to_self(turn).start()

    key_total[...] = jnp.zeros_like(key_total)
    value_total[...] = jnp.zeros_like(value_total)
    here = tile_at(j)
    k_place = j * TILE + lax.broadcasted_iota(jnp.int32, (TILE, 1), 0)
    turned = [head_of(qkv, here, 1, head).T for head in range(heads)]

    def tile(i, diagonal):
        q_place = i * TILE + lax.broadcasted_iota(jnp.int32, (1, TILE), 1)
        allowed = k_place >= doc_start(ends, q_place)
        if diagonal:
            allowed = allowed & (k_place <= q_place)
        for head in range(heads):
            query, grad = head_of(qkv, tile_at(i), 0, head), grads[tile_at(i), head * HD : (head + 1) * HD]
            sig = jnp.where(allowed, sigmoid_of(dot_nt(head_of(qkv, here, 1, head), query)), 0.0)
            value_total[head] += dot_wide(sig.astype(LOW), grad)
            d_score = (dot_nt(head_of(qkv, here, 2, head), grad) * (sig * (1.0 - sig))).astype(LOW)
            key_total[head] += dot_wide(d_score, query)
            query_total[head, :, tile_at(i)] += dot_wide(turned[head], d_score)

    def step(i, carry):
        tile(i, False)
        return carry

    tile(j, True)
    lax.fori_loop(j + 1, LEN // TILE, step, 0)
    scale = 1.0 / math.sqrt(HD)
    for head in range(heads):
        first = head * HD
        out[here, heads * HD + first : (heads + 1) * HD + first] = (key_total[head] * scale).astype(LOW)
        out[here, 2 * heads * HD + first : (2 * heads + 1) * HD + first] = value_total[head].astype(LOW)
        out[here, first : first + HD] = (query_total[head, :, here] * scale).T.astype(LOW)

    @pl.when(j == LEN // TILE - 1)
    def _():
        for turn in range(4):

            @pl.when(jnp.logical_not(owners[turn][1]))
            def _():
                to_owner(turn).wait_send()

            @pl.when(jnp.logical_not(holders[turn][1]))
            def _():
                landed = out_parts.at[turn]
                remote(landed, landed, send.at[turn], recv.at[turn], holders[turn][0]).wait_recv()

            @pl.when(owners[turn][1])
            def _():
                to_self(turn).wait()

        for half in (0, 1):
            trade.arrive(half)
        trade.finish()

    @pl.when(j == 1)
    def _():
        for half in (0, 1):
            trade.forward(half)


def back_mlp_kernel(upstream, w_down, gate, up, d_gate, d_up):
    def step(n, carry):
        columns = pl.ds(pl.multiple_of(n * TILE, TILE), TILE)
        d_hidden = dot_nt(upstream[...], w_down[columns, :])
        d_gate[:, columns], d_up[:, columns] = gate_backward(
            d_hidden, gate[:, columns], up[:, columns], jax.nn.sigmoid(gate[:, columns])
        )
        return carry

    lax.fori_loop(0, gate.shape[1] // TILE, step, 0, unroll=2)


def back_mlp(upstream, w_down, gate, up):
    places, width = upstream.shape
    hidden = gate.shape[1]
    rows = lambda size: pl.BlockSpec((TILE, size), lambda i: (i, 0))
    return pl.pallas_call(
        back_mlp_kernel,
        out_shape=(jax.ShapeDtypeStruct((places, hidden), LOW), jax.ShapeDtypeStruct((places, hidden), LOW)),
        grid=(places // TILE,),
        in_specs=[rows(width), pl.BlockSpec(w_down.shape, lambda i: (0, 0)), rows(hidden), rows(hidden)],
        out_specs=[rows(hidden), rows(hidden)],
        compiler_params=pltpu.CompilerParams(vmem_limit_bytes=VMEM_LIMIT),
        cost_estimate=pl.CostEstimate(flops=0, bytes_accessed=90_000_000, transcendentals=0),
    )(upstream, w_down, gate, up)


def attend(ends, qkv):
    places, width = qkv.shape
    heads = width // (3 * HD)
    whole = lambda columns: pl.BlockSpec((places, columns), lambda i: (0, 0))
    return pl.pallas_call(
        attend_kernel,
        out_shape=jax.ShapeDtypeStruct((places, width // 3), LOW),
        grid=(places // TILE,),
        in_specs=[pl.BlockSpec(memory_space=pltpu.SMEM), whole(width)],
        out_specs=whole(width // 3),
        scratch_shapes=[pltpu.VMEM((heads, TILE, HD), jnp.float32)],
        compiler_params=pltpu.CompilerParams(vmem_limit_bytes=VMEM_LIMIT),
        cost_estimate=pl.CostEstimate(flops=0, bytes_accessed=150_000_000, transcendentals=0),
    )(ends, qkv)


def attend_back(ends, qkv, grads, out_grad, mixed):
    places, width = qkv.shape
    heads = width // (3 * HD)
    whole = lambda columns: pl.BlockSpec((places, columns), lambda j: (0, 0))
    return pl.pallas_call(
        attend_back_kernel,
        out_shape=(
            jax.ShapeDtypeStruct((places, width), LOW),
            jax.ShapeDtypeStruct((4, out_grad.shape[0] // 4, out_grad.shape[1]), LOW),
            jax.ShapeDtypeStruct(mixed.shape, LOW),
        ),
        grid=(places // TILE,),
        in_specs=[pl.BlockSpec(memory_space=pltpu.SMEM), whole(width), whole(width // 3), anywhere(), pl.BlockSpec(mixed.shape, lambda j: (0, 0))],
        out_specs=[whole(width), anywhere(), anywhere()],
        scratch_shapes=[
            pltpu.VMEM((heads, HD, places), jnp.float32),
            pltpu.VMEM((heads, TILE, HD), jnp.float32),
            pltpu.VMEM((heads, TILE, HD), jnp.float32),
            dma(4),
            dma(4),
            *trade_scratch(2, HALF, mixed.shape[1]),
        ],
        compiler_params=remote_params(6),
        cost_estimate=pl.CostEstimate(flops=0, bytes_accessed=300_000_000, transcendentals=0),
    )(ends, qkv, grads, out_grad, mixed)


LAYER = ("y", "c", "x")
PLACES = ("c", "y", "x")
ALL = ("y", "c", "z", "x")


def trade_start(part, beside):
    y, c, z = (lax.axis_index(name) for name in ("y", "c", "z"))
    pairs = []
    for at in range(2):
        for x in range(2):
            owner = ((at * 2 + at) * 4 + 1 + at) * 2 + x
            across = (((1 - at) * 2 + at) * 4 + 1 + at) * 2 + x
            pairs.append((owner, across))
    passes = (1 - y == c) & (z == 2 - y)
    return jnp.where(passes, after(beside, lax.ppermute(part, ALL, pairs)), part)


def trade_end(started, part):
    y, c, z = (lax.axis_index(name) for name in ("y", "c", "z"))
    pairs = []
    for y_ in range(2):
        for c_ in range(2):
            for z_ in range(4):
                for x_ in range(2):
                    if z_ == 2 * c_ + y_:
                        continue
                    from_y = 1 - y_ if y_ == c_ and z_ == 1 + y_ else y_
                    owner = ((from_y * 2 + c_) * 4 + z_) * 2 + x_
                    pairs.append((owner, (((z_ % 2) * 2 + z_ // 2) * 4 + 2 * c_ + y_) * 2 + x_))
    return jnp.where(z == 2 * c + y, part, lax.ppermute(started, ALL, pairs))


def after(first, then):
    return lax.optimization_barrier((first, then))[1]


def body_layers(
    tokens, lengths, cotangent, w_query, w_key, w_value, w_out, w_gate, w_up, w_down, gain_attn, gain_mlp
):
    rows_here, block, width = tokens.shape
    members = lax.axis_size(LAYER)
    layers = lax.axis_size("z")
    shard = w_query.shape[0]
    owned = width // members
    facts = jnp.zeros((8, 2 * shard), jnp.float32)
    facts = facts.at[0, :shard].set(gain_attn.astype(jnp.float32)).at[1, :shard].set(gain_mlp.astype(jnp.float32))
    facts = facts.at[2, : lengths.shape[1]].set(lengths[0].astype(jnp.float32))
    layer_x, w_qkv, facts = begin(tokens.reshape(block, width), w_query, w_key, w_value, facts)
    full_gain_attn, full_gain_mlp = facts[:, :, :, 0, :shard].reshape(1, width), facts[:, :, :, 1, :shard].reshape(1, width)
    layer = lax.axis_index("z")
    own_lengths = facts[:, 0, 0, 2, : lengths.shape[1]].reshape(2, 2, -1)
    own_lengths = lax.dynamic_slice(own_lengths, (layer % 2, layer // 2, 0), (1, 1, own_lengths.shape[2]))[0, 0]
    ends = jnp.cumsum(own_lengths.astype(jnp.int32))
    layer_normed = norm_forward(layer_x.astype(jnp.float32), full_gain_attn)[0].astype(LOW)
    out_rows = lax.all_gather(after(facts, w_out), ("z", "x"), axis=0, tiled=True)
    qkv = dot_wide(layer_normed, w_qkv).astype(LOW)
    ready = after(facts, cotangent)
    started = trade_start(ready, qkv)
    attended = attend(ends, after(started, qkv))
    here = lax.axis_index("x")
    out_rows = after(attended, out_rows)
    w_out_own = [lax.dynamic_slice_in_dim(out_rows, head * HD, HD, 0) for head in (here, 3 - here)]
    w_out_own = jnp.concatenate(w_out_own, axis=0)
    upstream = trade_end(started, ready).reshape(block, width)
    resid, layer_mlp, own_gate, own_up = close_attention(after(upstream, attended), w_out_own, layer_x, full_gain_mlp, w_gate, w_up)

    own_down = lax.all_gather(after(resid, w_down), "z", axis=0, tiled=True)
    gate, up_part, hidden, layer_upstream = open_mlp(layer_mlp, own_gate, own_up, upstream)
    part = dot_wide(hidden, own_down).astype(LOW)
    mixed_sum = lax.psum_scatter(part, PLACES, scatter_dimension=0, tiled=True)
    down_term = contract_rows(after(part, hidden), layer_upstream).astype(LOW)
    down_rows = w_down.shape[0]
    down_parts = []
    for up in range(1, 4):
        layers_pairs = [(at, (at + up) % 4) for at in range(4)]
        slab = lax.dynamic_slice_in_dim(down_term, (layer + up) % 4 * down_rows, down_rows, 0)
        down_parts.append(lax.ppermute(slab, "z", layers_pairs))
    d_gate, d_up = back_mlp(after(down_term, layer_upstream), own_down, gate, up_part)
    gate_term, up_term = contract_rows(layer_mlp, d_gate).astype(LOW), contract_rows(layer_mlp, d_up).astype(LOW)
    d_resid, gain_mlp_term, layer_d_resid, *parts = close_mlp(
        after(mixed_sum, d_gate), d_up, own_gate, own_up, resid, upstream, full_gain_mlp, gate_term, up_term
    )

    def own_part(whole, near_part, cross):
        own = lax.dynamic_slice_in_dim(whole, layer * cross.shape[1], cross.shape[1], 1)
        return own.astype(jnp.float32) + near_part.astype(jnp.float32) + cross.astype(jnp.float32)

    mixed = (resid + after(layer_d_resid, mixed_sum).astype(jnp.float32)).astype(LOW)
    grad_down = lax.dynamic_slice_in_dim(down_term, layer * down_rows, down_rows, 0).astype(jnp.float32)
    grad_down = grad_down + sum(slab.astype(jnp.float32) for slab in after(layer_d_resid, down_parts))

    out_term = contract_rows(attended, layer_d_resid).astype(LOW)
    d_attended = contract_cols(layer_d_resid, w_out_own).astype(LOW)
    d_qkv, out_parts, mixed = attend_back(ends, qkv, d_attended, out_term, mixed)
    mixed = mixed.reshape(rows_here, block, width)
    grad_gate, grad_up = own_part(gate_term, *parts[1:3]), own_part(up_term, *parts[4:6])
    grad_out = jnp.sum(out_parts.astype(jnp.float32), axis=0)
    qkv_term = contract_rows(layer_normed, d_qkv).astype(LOW)
    qkv_term = qkv_term.reshape(4, layers, 2 * shard, 3 * owned).transpose(1, 0, 2, 3)
    qkv_term = qkv_term.reshape(layers, members * shard, 3 * owned)
    grad_low, gain_grads, *_, parts = close_layer(
        d_qkv, w_qkv, layer_x, d_resid, full_gain_attn, gain_mlp_term, qkv_term
    )
    grad_tokens = grad_low.astype(jnp.float32).reshape(rows_here, block, width)
    parts = parts.reshape(4, 2, shard, 3, 2, HD)
    parts = jnp.stack((parts[:, 0, :, :, 0], parts[:, 1, :, :, 0], parts[:, 1, :, :, 1], parts[:, 0, :, :, 1]), axis=1)
    grad_query, grad_key, grad_value = parts.transpose(3, 2, 0, 1, 4).astype(jnp.float32).reshape(3, shard, width)
    gain_grads = lax.dynamic_index_in_dim(jnp.sum(gain_grads, axis=1).reshape(2, 2, shard), lax.axis_index("x"), 1, False)
    return (
        mixed,
        grad_tokens,
        grad_query,
        grad_key,
        grad_value,
        grad_out,
        grad_gate,
        grad_up,
        grad_down,
        gain_grads[0],
        gain_grads[1],
    )


def body_any(
    tokens,
    lengths,
    cotangent,
    w_query,
    w_key,
    w_value,
    w_out,
    w_gate,
    w_up,
    w_down,
    gain_attn,
    gain_mlp,
):
    rows_here, block, width = tokens.shape
    count = rows_here * block
    scale = 1.0 / math.sqrt(HD)
    kv_place = lax.axis_index("kv")
    key_places = kv_place * block + jnp.arange(block, dtype=jnp.int32)
    attn_set = (
        lax.all_gather(w_query, ("row", "kv"), axis=0, tiled=True),
        lax.all_gather(w_key, ("row", "kv"), axis=0, tiled=True),
        lax.all_gather(w_value, ("row", "kv"), axis=0, tiled=True),
        lax.all_gather(w_out, ("row", "kv"), axis=0, tiled=True),
        lax.all_gather(gain_attn, ("row", "kv"), axis=0, tiled=True),
        lax.all_gather(gain_mlp, ("row", "kv"), axis=0, tiled=True),
    )
    full_query, full_key, full_value, full_out, full_gain_attn, full_gain_mlp = attn_set
    flat = tokens.reshape(count, width).astype(jnp.float32)
    normed_attn, inverse_attn = norm_forward(flat, full_gain_attn)
    normed_attn_low = normed_attn.astype(jnp.bfloat16)
    query_low = jnp.dot(normed_attn_low, full_query, preferred_element_type=jnp.float32).astype(
        jnp.bfloat16
    )
    key_low = jnp.dot(normed_attn_low, full_key, preferred_element_type=jnp.float32).astype(
        jnp.bfloat16
    )
    value_low = jnp.dot(normed_attn_low, full_value, preferred_element_type=jnp.float32).astype(
        jnp.bfloat16
    )
    key_heads = key_low.reshape(rows_here, block, H, HD)
    value_heads = value_low.reshape(rows_here, block, H, HD)
    segment, valid = segment_table(lengths)
    key_segment = lax.dynamic_slice_in_dim(segment, kv_place * block, block, 1)
    key_valid = lax.dynamic_slice_in_dim(valid, kv_place * block, block, 1)
    queries_all = lax.all_gather(
        query_low.reshape(rows_here, block, width), "kv", axis=1, tiled=True
    )
    which = 0
    query_rows = queries_all[which]
    query_segment = segment[which]
    sigmoid_part, allowed = score_block(
        query_rows,
        key_heads[which],
        query_segment,
        key_segment[which],
        key_valid[which],
        jnp.int32(0),
        key_places,
    )
    weight = (sigmoid_part * allowed).astype(jnp.bfloat16)
    summed = jnp.einsum(
        "hqk,khd->qhd", weight, value_heads[which], preferred_element_type=jnp.float32
    )
    pieces = [
        lax.psum_scatter(
            summed.reshape(lax.axis_size("kv") * block, width).astype(jnp.bfloat16),
            "kv",
            scatter_dimension=0,
            tiled=True,
        ).astype(jnp.float32)
    ]
    attended_low = jnp.stack(pieces).reshape(count, width).astype(jnp.bfloat16)
    resid = flat + jnp.dot(attended_low, full_out, preferred_element_type=jnp.float32)
    normed_mlp, inverse_mlp = norm_forward(resid, full_gain_mlp)
    normed_mlp_low = normed_mlp.astype(jnp.bfloat16)
    upstream_low = cotangent.reshape(count, width)
    upstream = upstream_low.astype(jnp.float32)
    slice_gate, slice_up, slice_down = (
        lax.all_gather(w_gate, "row", axis=1, tiled=True),
        lax.all_gather(w_up, "row", axis=1, tiled=True),
        lax.all_gather(w_down, "row", axis=0, tiled=True),
    )
    row_normed, row_upstream = (
        lax.all_gather(normed_mlp_low.reshape(rows_here, block, width), "kv", axis=1, tiled=True),
        lax.all_gather(cotangent, "kv", axis=1, tiled=True),
    )
    normed_rows = row_normed.reshape(rows_here * LEN, width)
    upstream_rows = row_upstream.reshape(rows_here * LEN, width)
    gate = jnp.dot(normed_rows, slice_gate, preferred_element_type=jnp.float32)
    up_part = jnp.dot(normed_rows, slice_up, preferred_element_type=jnp.float32)
    sigmoid_gate = jax.nn.sigmoid(gate)
    hidden_low = (gate * sigmoid_gate * up_part).astype(jnp.bfloat16)
    hidden_rows = hidden_low.reshape(rows_here, LEN, hidden_low.shape[1])
    which = 0
    hidden_part = hidden_rows[which]
    outputs = [
        lax.psum_scatter(
            jnp.dot(hidden_part, slice_down, preferred_element_type=jnp.float32).astype(
                jnp.bfloat16
            ),
            "kv",
            scatter_dimension=0,
            tiled=True,
        ).astype(jnp.float32)
    ]
    result = resid + jnp.stack(outputs).reshape(count, width)
    d_hidden = contract_cols(upstream_rows, slice_down)
    d_gate, d_up = gate_backward(d_hidden, gate, up_part, sigmoid_gate)
    partial_normed = contract_cols(d_gate, slice_gate) + contract_cols(d_up, slice_up)
    d_normed_mlp = (
        lax.psum_scatter(
            partial_normed.reshape(rows_here, LEN, width).astype(jnp.bfloat16),
            "kv",
            scatter_dimension=1,
            tiled=True,
        )
        .astype(jnp.float32)
        .reshape(count, width)
    )
    grad_gate, grad_up, grad_down = (
        lax.psum_scatter(
            contract_rows(normed_rows, d_gate).astype(jnp.bfloat16),
            "row",
            scatter_dimension=1,
            tiled=True,
        ).astype(jnp.float32),
        lax.psum_scatter(
            contract_rows(normed_rows, d_up).astype(jnp.bfloat16),
            "row",
            scatter_dimension=1,
            tiled=True,
        ).astype(jnp.float32),
        lax.psum_scatter(
            contract_rows(hidden_low, upstream_rows).astype(jnp.bfloat16),
            "row",
            scatter_dimension=0,
            tiled=True,
        ).astype(jnp.float32),
    )
    mixed = result.astype(jnp.bfloat16).reshape(rows_here, block, width)
    back_mlp, gain_mlp_term = norm_backward(resid, inverse_mlp, full_gain_mlp, d_normed_mlp)
    d_resid = upstream + back_mlp
    d_resid_low = d_resid.astype(jnp.bfloat16)
    d_attended = contract_cols(d_resid_low, full_out).astype(jnp.bfloat16)
    grads_all = lax.all_gather(
        d_attended.reshape(rows_here, block, width), "kv", axis=1, tiled=True
    )
    query_block = min(512, LEN)
    block_count = LEN // query_block
    which = 0

    def sweep(carry, index, which=which):
        key_total, value_total = carry
        start = index * query_block
        query_rows = lax.dynamic_slice_in_dim(queries_all[which], start, query_block, 0)
        grad_rows = lax.dynamic_slice_in_dim(grads_all[which], start, query_block, 0)
        query_segment = lax.dynamic_slice_in_dim(segment[which], start, query_block, 0)
        sigmoid_part, allowed = score_block(
            query_rows,
            key_heads[which],
            query_segment,
            key_segment[which],
            key_valid[which],
            start,
            key_places,
        )
        weight = (sigmoid_part * allowed).astype(jnp.bfloat16)
        grad_heads = grad_rows.reshape(query_block, H, HD)
        value_total = value_total + jnp.einsum(
            "hqk,qhd->khd", weight, grad_heads, preferred_element_type=jnp.float32
        )
        d_weight = jnp.einsum(
            "qhd,khd->hqk", grad_heads, value_heads[which], preferred_element_type=jnp.float32
        )
        d_score = (d_weight * sigmoid_part * (1.0 - sigmoid_part) * allowed).astype(jnp.bfloat16)
        query_part = (
            jnp.einsum(
                "hqk,khd->qhd", d_score, key_heads[which], preferred_element_type=jnp.float32
            )
            * scale
        )
        key_total = (
            key_total
            + jnp.einsum(
                "hqk,qhd->khd",
                d_score,
                query_rows.reshape(query_block, H, HD),
                preferred_element_type=jnp.float32,
            )
            * scale
        )
        return ((key_total, value_total), query_part.reshape(query_block, width))

    zeros = jnp.zeros((block, H, HD), jnp.float32)
    totals, query_parts = lax.scan(sweep, (zeros, zeros), jnp.arange(block_count, dtype=jnp.int32))
    query_terms = [query_parts.reshape(LEN, width)]
    key_grads = [totals[0].reshape(block, width)]
    value_grads = [totals[1].reshape(block, width)]
    query_local = lax.psum_scatter(
        jnp.stack(query_terms).astype(jnp.bfloat16), "kv", scatter_dimension=1, tiled=True
    ).astype(jnp.float32)
    d_query_low = query_local.reshape(count, width).astype(jnp.bfloat16)
    d_key_low = jnp.stack(key_grads).reshape(count, width).astype(jnp.bfloat16)
    d_value_low = jnp.stack(value_grads).reshape(count, width).astype(jnp.bfloat16)
    d_normed_attn = (
        contract_cols(d_query_low, full_query)
        + contract_cols(d_key_low, full_key)
        + contract_cols(d_value_low, full_value)
    )
    back_attn, gain_attn_term = norm_backward(flat, inverse_attn, full_gain_attn, d_normed_attn)
    grad_tokens = (d_resid + back_attn).reshape(rows_here, block, width)
    projected_low = jnp.concatenate((d_query_low, d_key_low, d_value_low), axis=1)
    grad_projections = lax.psum_scatter(
        contract_rows(normed_attn_low, projected_low),
        ("row", "kv"),
        scatter_dimension=0,
        tiled=True,
    )
    out_term = contract_rows(attended_low, d_resid_low)
    grad_out, grad_gain_attn, grad_gain_mlp = (
        lax.psum_scatter(out_term, ("row", "kv"), scatter_dimension=0, tiled=True),
        lax.psum_scatter(gain_attn_term, ("row", "kv"), scatter_dimension=0, tiled=True),
        lax.psum_scatter(gain_mlp_term, ("row", "kv"), scatter_dimension=0, tiled=True),
    )
    grad_query = grad_projections[:, :width]
    grad_key = grad_projections[:, width : 2 * width]
    grad_value = grad_projections[:, 2 * width :]
    return (
        mixed,
        grad_tokens,
        grad_query,
        grad_key,
        grad_value,
        grad_out,
        grad_gate,
        grad_up,
        grad_down,
        grad_gain_attn,
        grad_gain_mlp,
    )


def solution(mesh):
    rows, columns = mesh.shape["row"], mesh.shape["kv"]
    if rows == 4 and columns == 2 * rows:
        mesh = Mesh(mesh.devices.reshape(2, 2, rows, 2), ("y", "c", "z", "x"))
        row, kv, run = ("y", "c"), ("z", "x"), body_layers
    else:
        row, kv, run = "row", "kv", body_any
    both = ("y", "c", "z", "x") if run is body_layers else ("row", "kv")
    tall, wide, flat = P(both, None), P(None, both), P(both)
    tokens = P(row, kv, None)
    return jax.shard_map(
        run,
        mesh=mesh,
        in_specs=(tokens, P(row, None), tokens, tall, tall, tall, tall, wide, wide, tall, flat, flat),
        out_specs=(tokens, tokens, tall, tall, tall, tall, wide, wide, tall, flat, flat),
        check_vma=False,
    )
```

```python
import functools
import math

import jax
import jax.numpy as jnp
from jax import lax
from jax.experimental import pallas as pl
from jax.experimental.pallas import tpu as pltpu
from jax.sharding import Mesh, PartitionSpec as P

H = 16
HD = 128
LEN = 4096


EPSILON = 1e-05


def contract_rows(left, right):
    return lax.dot_general(
        left, right, (((0,), (0,)), ((), ())), preferred_element_type=jnp.float32
    )


def contract_cols(left, right):
    return lax.dot_general(
        left, right, (((1,), (1,)), ((), ())), preferred_element_type=jnp.float32
    )


def norm_forward(value, gain):
    inverse = lax.rsqrt(jnp.mean(value * value, axis=-1, keepdims=True) + EPSILON)
    return (value * inverse * gain.astype(jnp.float32), inverse)


def norm_backward(value, inverse, gain, upstream):
    scaled = upstream * gain.astype(jnp.float32)
    inner = jnp.mean(scaled * value, axis=-1, keepdims=True)
    back = inverse * scaled - value * (inverse * inverse * inverse) * inner
    gain_term = jnp.sum(upstream * value * inverse, axis=0)
    return (back, gain_term)


def segment_table(lengths):
    ends = jnp.cumsum(lengths, axis=-1)
    places = jnp.arange(LEN, dtype=jnp.int32)
    segment = jnp.sum((ends[:, None, :] <= places[None, :, None]).astype(jnp.int32), axis=-1)
    valid = places[None, :] < ends[:, -1:]
    return (segment, valid)


def score_block(
    query_rows, key_heads, query_segment, key_segment, key_valid, query_start, key_places
):
    count = query_rows.shape[0]
    query_heads = query_rows.reshape(count, H, HD)
    raw = jnp.einsum("qhd,khd->hqk", query_heads, key_heads, preferred_element_type=jnp.float32)
    scores = raw * (1.0 / math.sqrt(HD)) - math.log(LEN)
    places = query_start + jnp.arange(count, dtype=jnp.int32)
    allowed = (
        (key_places[None, :] <= places[:, None])
        & (key_segment[None, :] == query_segment[:, None])
        & key_valid[None, :]
    )
    return (jax.nn.sigmoid(scores), allowed.astype(jnp.float32)[None])


def gate_backward(d_hidden, gate, up_part, sigmoid_gate):
    d_gate = (d_hidden * up_part * sigmoid_gate * (1.0 + gate * (1.0 - sigmoid_gate))).astype(
        jnp.bfloat16
    )
    d_up = (d_hidden * gate * sigmoid_gate).astype(jnp.bfloat16)
    return (d_gate, d_up)


TILE = 512
LOW = jnp.bfloat16
VMEM_LIMIT = 60 * 1024 * 1024


def dot_nt(left, right):
    return lax.dot_general(left, right, (((1,), (1,)), ((), ())), preferred_element_type=jnp.float32)


def dot_wide(left, right):
    return jnp.dot(left, right, preferred_element_type=jnp.float32)


HALF = TILE // 2
PIECES = 4
CHUNK = 32
MESH_ID = pl.DeviceIdType.MESH


def flip(bit, by):
    return bit + by - 2 * bit * by


def spot():
    return tuple(lax.axis_index(name) for name in ("y", "c", "z", "x"))


def near():
    y, c, z, x = spot()
    return (y, c, z, 1 - x), (1 - y, c, z, x), (y, 1 - c, z, x)


def partner_of(y, c, z, x):
    return lax.rem(z, 2), z // 2, 2 * c + y, x


def place_of(y, c, x, half=None):
    first = (4 * c + 2 * y + x) * TILE
    if half is None:
        return pl.ds(pl.multiple_of(first, TILE), TILE)
    return pl.ds(pl.multiple_of(first + half * HALF, HALF), HALF)


def quarter_of(y, c, x, half, quarter):
    return pl.ds(pl.multiple_of((4 * c + 2 * y + x) * TILE + half * HALF + quarter * (HALF // 2), HALF // 2), HALF // 2)


def remote(src, dst, send, recv, peer):
    return pltpu.make_async_remote_copy(
        src_ref=src, dst_ref=dst, send_sem=send, recv_sem=recv, device_id=peer, device_id_type=MESH_ID
    )


def greet(peers):
    barrier = pltpu.get_barrier_semaphore()
    for peer in peers:
        pl.semaphore_signal(barrier, inc=1, device_id=peer, device_id_type=MESH_ID)
    pl.semaphore_wait(barrier, len(peers))


class Gather:
    def __init__(self, own, whole, send, recv):
        y, c, z, x = spot()
        across_x, across_y, core = near()

        def passed(k, at, peer):
            return remote(whole.at[at], whole.at[at], send.at[k], recv.at[k], peer)

        self.halves = []
        for half in (0, 1):
            k, at = 9 * half, place_of(y, c, x, half)
            mine = [
                remote(own(half), whole.at[at], send.at[k + m], recv.at[k + m], peer)
                for m, peer in enumerate((across_x, across_y, core))
            ]
            held_x, held_y = (y, c, 1 - x), (1 - y, c, x)
            far = (1 - y, c, 1 - x)
            self.halves.append(
                (
                    mine,
                    passed(k + 3, quarter_of(*held_x, half, 0), across_y),
                    passed(k + 4, quarter_of(*held_y, half, 1), across_x),
                    [passed(k + 5, place_of(*held_x, half), core), passed(k + 6, place_of(*held_y, half), core)],
                    [passed(k + 7 + q, quarter_of(*far, half, q), core) for q in (0, 1)],
                )
            )

    def start(self, half):
        for copy in self.halves[half][0]:
            copy.start()

    def pass_near(self, half):
        mine, over_y, over_x, from_near, from_far = self.halves[half]
        mine[0].wait_recv()
        over_y.start()
        from_near[0].start()
        mine[1].wait_recv()
        over_x.start()
        from_near[1].start()

    def pass_far(self, half):
        mine, over_y, over_x, from_near, from_far = self.halves[half]
        over_y.wait_recv()
        from_far[0].start()
        over_x.wait_recv()
        from_far[1].start()

    def finish(self):
        for mine, over_y, over_x, from_near, from_far in self.halves:
            for copy in [mine[2]] + from_near + from_far:
                copy.wait_recv()
            for copy in mine + [over_y, over_x] + from_near + from_far:
                copy.wait_send()


GATHER_COPIES = 18


class GatherWhole:
    def __init__(self, own, whole, send, recv):
        y, c, z, x = spot()
        across_x, across_y, core = near()

        def from_own(k, half, peer):
            return remote(own(half), whole.at[place_of(y, c, x, half)], send.at[k], recv.at[k], peer)

        def passed(k, at, peer):
            return remote(whole.at[at], whole.at[at], send.at[k], recv.at[k], peer)

        self.mine = [
            [from_own(0, 0, across_x), from_own(1, 0, across_y), from_own(2, 0, core)],
            [from_own(3, 1, across_x), from_own(4, 1, across_y), from_own(5, 1, core)],
        ]
        held_x = [place_of(y, c, 1 - x, half) for half in (0, 1)]
        held_y = [place_of(1 - y, c, x, half) for half in (0, 1)]
        far = [place_of(1 - y, c, 1 - x, half) for half in (0, 1)]
        self.over_y, self.over_x = passed(6, held_x[0], across_y), passed(7, held_y[1], across_x)
        self.core_x = [passed(8 + half, held_x[half], core) for half in (0, 1)]
        self.core_y = [passed(10 + half, held_y[half], core) for half in (0, 1)]
        self.core_far = [passed(12 + half, far[half], core) for half in (0, 1)]

    def start(self, half):
        for copy in self.mine[half]:
            copy.start()

    def pass_first(self):
        self.mine[0][0].wait_recv()
        self.over_y.start()
        self.core_x[0].start()
        self.mine[0][1].wait_recv()
        self.core_y[0].start()

    def pass_second(self):
        self.mine[1][1].wait_recv()
        self.over_x.start()
        self.core_y[1].start()
        self.mine[1][0].wait_recv()
        self.core_x[1].start()

    def pass_far(self):
        self.over_y.wait_recv()
        self.core_far[0].start()
        self.over_x.wait_recv()
        self.core_far[1].start()

    def finish(self):
        from_core = [self.mine[0][2], self.mine[1][2]] + self.core_x + self.core_y + self.core_far
        for copy in from_core:
            copy.wait_recv()
        for copy in self.mine[0] + self.mine[1] + [self.over_y, self.over_x] + self.core_x + self.core_y + self.core_far:
            copy.wait_send()


class Trade:
    def __init__(self, sources, dst, held, send, recv, held_recv, pass_send, detour=True):
        y, c, z, x = spot()
        self.detour = detour
        across_y = (1 - y, c, z, x)
        self.moves = z != 2 * c + y
        self.away = (y == c) & (z == 1 + y)
        self.straight = self.moves & jnp.logical_not(self.away) if detour else self.moves
        self.passes = (1 - y == c) & (z == 2 - y)
        partner = partner_of(y, c, z, x)
        comes_by = ((partner[0] == partner[1]) & (partner[2] == 1 + partner[0])).astype(jnp.int32)
        self.sender = (flip(partner[0], comes_by), partner[1], partner[2], x) if detour else partner
        self.across_y = across_y
        target = partner_of(*across_y)
        self.direct, self.keep, self.out, self.onward = [], [], [], []
        for h, source in enumerate(sources):
            self.direct.append(remote(source, dst(h, partner), send.at[h], recv.at[h], partner))
            self.keep.append(pltpu.make_async_copy(source, dst(h, (y, c, z, x)), recv.at[h]))
            self.out.append(remote(source, held.at[h], send.at[h], held_recv.at[h], across_y))
            self.onward.append(remote(held.at[h], dst(h, target), pass_send.at[h], recv.at[h], target))

    def greet(self, barrier, neighbours_greet):
        @pl.when(self.moves)
        def _():
            pl.semaphore_signal(barrier, inc=1, device_id=self.sender, device_id_type=MESH_ID)

        count = self.straight.astype(jnp.int32)
        if not self.detour:
            return count
        count = count + self.passes.astype(jnp.int32)
        if not neighbours_greet:

            @pl.when(self.passes)
            def _():
                pl.semaphore_signal(barrier, inc=1, device_id=self.across_y, device_id_type=MESH_ID)

            count = count + self.away.astype(jnp.int32)
        return count

    def start(self, h):
        @pl.when(self.straight)
        def _():
            self.direct[h].start()

        if self.detour:

            @pl.when(self.away)
            def _():
                self.out[h].start()

        @pl.when(jnp.logical_not(self.moves))
        def _():
            self.keep[h].start()

    def wait_sent(self, h):
        @pl.when(self.straight)
        def _():
            self.direct[h].wait_send()

        if self.detour:

            @pl.when(self.away)
            def _():
                self.out[h].wait_send()

    def forward(self, h):
        if self.detour:

            @pl.when(self.passes)
            def _():
                self.out[h].wait_recv()
                self.onward[h].start()

    def arrive(self, h):
        @pl.when(self.moves)
        def _():
            self.direct[h].wait_recv()

        @pl.when(jnp.logical_not(self.moves))
        def _():
            self.keep[h].wait()

    def finish(self, first=0):
        for h in range(len(self.direct)):
            if h >= first:
                self.wait_sent(h)

            if self.detour:

                @pl.when(self.passes)
                def _():
                    self.onward[h].wait_send()


def trade_scratch(pieces, rows, width):
    return [pltpu.VMEM((pieces, rows, width), LOW)] + [pltpu.SemaphoreType.DMA((pieces,)) for _ in range(4)]


class Chain:
    def __init__(self, own, slab, sems, index):
        self.own, self.slab, self.sems, self.index = own, slab, sems, index
        self.last = lax.axis_size("z") - 1

    def move(self, which, h, source, layer, to):
        y, c, z, x = spot()
        return remote(
            source, self.slab(layer), self.sems[2 * which].at[self.index, h], self.sems[2 * which + 1].at[self.index, h], (y, c, to, x)
        )

    def up(self, h):
        z = lax.axis_index("z")
        return self.move(0, h, self.own if h == 0 else self.slab(z - h), z - h, z + 1)

    def down(self, h):
        z = lax.axis_index("z")
        return self.move(1, h, self.own if h == 0 else self.slab(z + h), z + h, z - 1)

    def start(self):
        z = lax.axis_index("z")

        @pl.when(z < self.last)
        def _():
            self.up(0).start()

        @pl.when(z > 0)
        def _():
            self.down(0).start()

    def arrive(self, h):
        z = lax.axis_index("z")

        @pl.when(z - h - 1 >= 0)
        def _():
            self.move(0, h, self.slab(z - h - 1), z - h - 1, z).wait_recv()
            if h < 2:

                @pl.when(z < self.last)
                def _():
                    self.up(h + 1).start()

        @pl.when(z + h + 1 <= self.last)
        def _():
            self.move(1, h, self.slab(z + h + 1), z + h + 1, z).wait_recv()
            if h < 2:

                @pl.when(z > 0)
                def _():
                    self.down(h + 1).start()

    def finish(self):
        z = lax.axis_index("z")
        for h in range(3):

            @pl.when((z < self.last) & (z - h >= 0))
            def _():
                self.up(h).wait_send()

            @pl.when((z > 0) & (z + h <= self.last))
            def _():
                self.down(h).wait_send()


def chain_sems(count):
    return [pltpu.SemaphoreType.DMA((count, 3)) for _ in range(4)]


def greet_neighbours(peers):
    y, c, z, x = spot()
    last = lax.axis_size("z") - 1
    barrier = pltpu.get_barrier_semaphore()
    for peer in peers:
        pl.semaphore_signal(barrier, inc=1, device_id=peer, device_id_type=MESH_ID)

    @pl.when(z > 0)
    def _():
        pl.semaphore_signal(barrier, inc=1, device_id=(y, c, z - 1, x), device_id_type=MESH_ID)

    @pl.when(z < last)
    def _():
        pl.semaphore_signal(barrier, inc=1, device_id=(y, c, z + 1, x), device_id_type=MESH_ID)

    return barrier, len(peers) + (z > 0).astype(jnp.int32) + (z < last).astype(jnp.int32)


def others():
    y, c, z, x = spot()
    return [(flip(y, dy), flip(c, dc), z, flip(x, dx)) for dy in (0, 1) for dc in (0, 1) for dx in (0, 1) if dy + dc + dx]


def line_of():
    y, c, z, x = spot()
    return [(y, c, lax.rem(z + dz, 4), x) for dz in (1, 2, 3)]


class Fold:
    def __init__(self, slab, far, near_part, cross, mine, theirs, send, recv, local):
        y, c, z, x = spot()
        a, b = z // 2, lax.rem(z, 2)
        pair, middle = (y, c, 2 * a + 1 - b, x), (y, c, 2 * (1 - a) + b, x)
        self.far = remote(slab(2 * (1 - a) + 1 - b), far, send.at[0], recv.at[0], pair)
        self.near = remote(slab(2 * a + 1 - b), near_part, send.at[1], recv.at[1], pair)
        self.cross = remote(mine, cross, send.at[2], recv.at[2], middle)
        self.fetches = [
            pltpu.make_async_copy(slab(2 * (1 - a) + b), mine, local.at[0]),
            pltpu.make_async_copy(far, theirs, local.at[1]),
        ]
        self.mine, self.theirs = mine, theirs

    def start(self):
        self.far.start()
        self.fetches[0].start()

    def fold(self):
        self.far.wait_recv()
        self.fetches[1].start()
        for copy in self.fetches:
            copy.wait()
        add_rows(self.mine, 0, self.theirs, 0, self.mine.shape[0])
        self.cross.start()
        self.near.start()

    def finish(self):
        for copy in (self.near, self.cross):
            copy.wait_recv()
        for copy in (self.far, self.near, self.cross):
            copy.wait_send()


def columns_of_layer(whole):
    size = whole.shape[1] // 4
    return lambda at: whole.at[:, pl.ds(pl.multiple_of(at * size, size), size)]


def fold_peers():
    y, c, z, x = spot()
    a, b = z // 2, lax.rem(z, 2)
    return ((y, c, 2 * a + 1 - b, x), (y, c, 2 * (1 - a) + b, x))


def add_rows(total, first, term, start, count):
    def step(i, carry):
        here = pl.ds(pl.multiple_of(first + i * CHUNK, CHUNK), CHUNK)
        there = pl.ds(pl.multiple_of(start + i * CHUNK, CHUNK), CHUNK)
        total[here, :] = (total[here, :].astype(jnp.float32) + term[there, :].astype(jnp.float32)).astype(LOW)
        return carry

    lax.fori_loop(0, count // CHUNK, step, 0)


def scatter_scratch(width, parts=1):
    return [
        pltpu.VMEM((2, TILE, width), LOW),
        pltpu.VMEM((4, TILE, width), LOW),
        pltpu.VMEM((4, TILE, width), LOW),
        pltpu.VMEM((2, HALF, width), LOW),
        pltpu.VMEM((2, TILE, width), LOW),
        pltpu.SemaphoreType.DMA((parts, 10)),
        pltpu.SemaphoreType.DMA((parts, 10)),
    ]


class Scatter:
    def __init__(self, produce, staged, core_part, total, relayed, landed, send, recv, part=0, start=0, size=TILE):
        across_x, across_y, core = near()
        self.produce, self.staged, self.core_part, self.total, self.relayed = produce, staged, core_part, total, relayed
        self.start, self.size, self.half = start, size, size // 2
        send, recv = send.at[part], recv.at[part]
        rows = pl.ds(start, size)
        halves = (pl.ds(start, self.half), pl.ds(start + self.half, self.half))
        self.relay_row = start // 2
        passing = pl.ds(self.relay_row, self.half)
        self.to_core = [
            remote(staged.at[k % 2, rows], core_part.at[k, rows], send.at[k], recv.at[k], core) for k in range(4)
        ]
        self.far_x = remote(total.at[0, halves[0]], relayed.at[0, passing], send.at[4], recv.at[4], across_x)
        self.far_y = remote(total.at[0, halves[1]], relayed.at[1, passing], send.at[5], recv.at[5], across_y)
        self.to_x = [
            remote(total.at[1, at], landed.at[0, at], send.at[6 + half], recv.at[6 + half], across_x)
            for half, at in enumerate(halves)
        ]
        self.to_y = [
            remote(total.at[2, at], landed.at[1, at], send.at[8 + half], recv.at[8 + half], across_y)
            for half, at in enumerate(halves)
        ]

    def begin(self):
        y, c, z, x = spot()
        rows = pl.ds(self.start, self.size)
        for k, (to_row, to_column) in enumerate(((1 - y, 1 - x), (y, 1 - x), (1 - y, x), (y, x))):
            if k >= 2:
                self.to_core[k - 2].wait_send()
            self.produce(2 * k, to_row, 1 - c, to_column, self.staged.at[k % 2, rows])
            self.to_core[k].start()
            self.produce(2 * k + 1, to_row, c, to_column, self.total.at[k, rows])
            self.to_core[k].wait_recv()
            add_rows(self.total.at[k], self.start, self.core_part.at[k], self.start, self.size)
            if k == 0:
                self.far_x.start()
                self.far_y.start()
            if k == 1:
                self.to_x[0].start()
            if k == 2:
                self.to_y[1].start()

    def relay(self):
        self.far_y.wait_recv()
        add_rows(self.total.at[1], self.start + self.half, self.relayed.at[1], self.relay_row, self.half)
        self.to_x[1].start()
        self.far_x.wait_recv()
        add_rows(self.total.at[2], self.start, self.relayed.at[0], self.relay_row, self.half)
        self.to_y[0].start()

    def arrive(self):
        for copy in self.to_x + self.to_y:
            copy.wait_recv()

    def finish(self):
        for copy in self.to_core[2:] + [self.far_x, self.far_y] + self.to_x + self.to_y:
            copy.wait_send()


def sum_and_gather(part_of, rows_of_half, gather, beside):
    sums = [part_of(half) for half in (0, 1)]
    sums[0].begin()
    sums[0].relay()
    sums[1].begin()
    sums[0].arrive()
    rows_of_half(0)
    gather.start(0)
    beside(0)
    sums[1].relay()
    beside(1)
    sums[1].arrive()
    rows_of_half(1)
    gather.start(1)
    gather.pass_near(0)
    beside(2)
    gather.pass_near(1)
    gather.pass_far(0)
    gather.pass_far(1)
    gather.finish()
    beside(3)
    for half in (0, 1):
        sums[half].finish()


def begin_kernel(
    x_own, w_query, w_key, w_value, facts, x_whole, w_qkv, facts_whole,
    gather_send, gather_recv, w_send, w_recv, fact_send, fact_recv, local, *scratch
):
    y, c, z, x = spot()
    row = 2 * y + c
    layer = others()
    trade_parts, sems = scratch[:5], scratch[5:]
    trade = Trade(
        [x_own.at[half] for half in (0, 1)], lambda half, at: x_whole.at[place_of(at[0], at[1], at[3], half)], *trade_parts, detour=False
    )
    barrier, count = greet_neighbours(layer)
    pl.semaphore_wait(barrier, count + trade.greet(barrier, True))

    shard = w_query.shape[0]
    for half in (0, 1):
        trade.start(half)
    spread = [
        remote(facts, facts_whole.at[row, z, x], fact_send.at[k], fact_recv.at[k], peer) for k, peer in enumerate(layer)
    ]
    kept = [pltpu.make_async_copy(facts, facts_whole.at[row, z, x], local.at[6])]
    for m in range(6):
        source, slot = (w_query, w_key, w_value)[m // 2], m % 2

        def columns_of(at):
            head = 4 * (2 * at[0] + at[1]) + (3 - at[3] if slot else at[3])
            return source.at[:, pl.ds(pl.multiple_of(head * HD, HD), HD)]

        dst = w_qkv.at[row, z, pl.ds(pl.multiple_of(x * shard, shard), shard), pl.ds(m * HD, HD)]
        for k, peer in enumerate(layer):
            spread.append(remote(columns_of(peer), dst, w_send.at[m, k], w_recv.at[m, k], peer))
        kept.append(pltpu.make_async_copy(columns_of((y, c, z, x)), dst, local.at[m]))
    for copy in spread + kept:
        copy.start()

    gather = GatherWhole(lambda half: x_whole.at[place_of(y, c, x, half)], x_whole, gather_send, gather_recv)
    for half in (0, 1):
        trade.forward(half)
        trade.arrive(half)
        gather.start(half)

    for copy in kept:
        copy.wait()
    for copy in spread:
        copy.wait_recv()
    chains = [
        Chain(facts_whole.at[:, z], lambda at: facts_whole.at[:, at], sems, 0),
        Chain(w_qkv.at[:, z], lambda at: w_qkv.at[:, at], sems, 1),
    ]

    def arrive(h):
        for chain in chains:
            chain.arrive(h)

    for chain in chains:
        chain.start()
    gather.pass_first()
    arrive(0)
    gather.pass_second()
    arrive(1)
    gather.pass_far()
    arrive(2)
    gather.finish()
    trade.finish()
    for copy in spread:
        copy.wait_send()
    for chain in chains:
        chain.finish()


def anywhere():
    return pl.BlockSpec(memory_space=pl.ANY)


def in_vmem():
    return pl.BlockSpec(memory_space=pltpu.VMEM)


def dma(*shape):
    return pltpu.SemaphoreType.DMA(shape)


def remote_params(number):
    return pltpu.CompilerParams(collective_id=number, has_side_effects=True, vmem_limit_bytes=VMEM_LIMIT)


def begin(x_own, w_query, w_key, w_value, facts):
    block, width = x_own.shape
    shard = w_query.shape[0]
    x_whole, w_qkv, facts_whole = pl.pallas_call(
        begin_kernel,
        out_shape=(
            jax.ShapeDtypeStruct((8 * block, width), LOW),
            jax.ShapeDtypeStruct((4, 4, 2 * shard, 3 * width // 8), LOW),
            jax.ShapeDtypeStruct((4, 4, 2, *facts.shape), jnp.float32),
        ),
        in_specs=[in_vmem()] + [anywhere()] * 4,
        out_specs=[anywhere()] * 3,
        scratch_shapes=[
            dma(GATHER_COPIES), dma(GATHER_COPIES), dma(6, 7), dma(6, 7), dma(7), dma(7), dma(7),
            *trade_scratch(2, block // 2, width), *chain_sems(2),
        ],
        compiler_params=remote_params(1),
        cost_estimate=pl.CostEstimate(flops=0, bytes_accessed=350_000_000, transcendentals=0),
    )(x_own.reshape(2, block // 2, width), w_query, w_key, w_value, facts)
    return x_whole, w_qkv.reshape(width, 3 * width // 8), facts_whole


def summed(total, landed, here):
    parts = (total[3, here, :], landed[0, here, :], landed[1, here, :])
    return sum(part.astype(jnp.float32) for part in parts)


def over_chunks(work, half):
    def step(i, carry):
        work(pl.ds(pl.multiple_of(half * HALF + i * CHUNK, CHUNK), CHUNK))
        return carry

    lax.fori_loop(0, HALF // CHUNK, step, 0)


def own_halves(own):
    return lambda half: own.at[pl.ds(half * HALF, HALF)]


def inverse_of(value):
    return lax.rsqrt(jnp.mean(value * value, axis=-1, keepdims=True) + EPSILON)


def close_attention_kernel(attended, w_out, x_whole, gain, w_gate, w_up, resid, normed, own_gate, own_up, own, x_own, *scratch):
    scatter, (send, recv, local), sems = scratch[:7], scratch[7:10], scratch[10:]
    y, c, z, x = spot()
    fetch_x = pltpu.make_async_copy(x_whole.at[place_of(y, c, x)], x_own, local.at[0])
    fetch_x.start()
    width = w_out.shape[1]
    hidden = w_gate.shape[1]
    z = lax.axis_index("z")
    barrier, count = greet_neighbours(near())
    pl.semaphore_wait(barrier, count)

    def slab_of(whole):
        return lambda at: whole.at[:, pl.ds(pl.multiple_of(at * hidden, hidden), hidden)]

    chains, kept = [], []
    for k, (part, whole) in enumerate(((w_gate, own_gate), (w_up, own_up))):
        chains.append(Chain(part, slab_of(whole), sems, k))
        chains[k].start()
        kept.append(pltpu.make_async_copy(part, slab_of(whole)(z), local.at[1 + k]))
        kept[k].start()

    def arrive(h):
        for chain in chains:
            chain.arrive(h)

    def part_of(half):
        def produce(turn, y, c, x, out):
            at = place_of(y, c, x, half)

            def step(i, carry):
                columns = pl.ds(pl.multiple_of(i * TILE, TILE), TILE)
                out[:, columns] = dot_wide(attended[at, :], w_out[:, columns]).astype(LOW)
                return carry

            lax.fori_loop(0, width // TILE, step, 0)

        return Scatter(produce, *scatter, part=half, start=half * HALF, size=HALF)

    total, landed = scatter[2], scatter[4]

    def chunk(here):
        value = x_own[here, :].astype(jnp.float32) + summed(total, landed, here)
        resid[here, :] = value
        own[here, :] = (value * inverse_of(value) * gain[...]).astype(LOW)

    def rows_of_half(half):
        if half == 0:
            fetch_x.wait()
        over_chunks(chunk, half)

    gather = Gather(own_halves(own), normed, send, recv)
    sum_and_gather(part_of, rows_of_half, gather, lambda turn: arrive(turn - 1) if turn > 0 else None)
    keep = pltpu.make_async_copy(own, normed.at[place_of(y, c, x)], local.at[0])
    keep.start()
    for chain in chains:
        chain.finish()
    for copy in kept + [keep]:
        copy.wait()


def close_attention(attended, w_out, x_whole, gain, w_gate, w_up):
    block, width = x_whole.shape[0] // 8, x_whole.shape[1]
    hidden = w_gate.shape[1]
    return pl.pallas_call(
        close_attention_kernel,
        out_shape=(
            jax.ShapeDtypeStruct((block, width), jnp.float32),
            jax.ShapeDtypeStruct((8 * block, width), LOW),
            jax.ShapeDtypeStruct((width, 4 * hidden), LOW),
            jax.ShapeDtypeStruct((width, 4 * hidden), LOW),
        ),
        in_specs=[in_vmem(), in_vmem(), anywhere()] + [in_vmem()] * 3,
        out_specs=[in_vmem()] + [anywhere()] * 3,
        scratch_shapes=[pltpu.VMEM((block, width), LOW)] * 2
        + scatter_scratch(width, 2)
        + [dma(GATHER_COPIES), dma(GATHER_COPIES), dma(3), *chain_sems(2)],
        compiler_params=remote_params(2),
        cost_estimate=pl.CostEstimate(flops=0, bytes_accessed=450_000_000, transcendentals=0),
    )(attended, w_out, x_whole, gain, w_gate, w_up)


def norm_back(value, gain, upstream):
    inverse = inverse_of(value)
    scaled = upstream * gain
    inner = jnp.mean(scaled * value, axis=-1, keepdims=True)
    return inverse * scaled - value * (inverse * inverse * inverse) * inner, upstream * value * inverse


def fold_rows(total, terms):
    for first in range(0, CHUNK, 8):
        total[...] += terms[first : first + 8, :]


def close_mlp_kernel(
    d_gate, d_up, w_gate, w_up, resid_home, upstream_home, gain, grad_a, grad_b, d_resid, gain_term, d_resid_whole,
    far_a, near_a, cross_a, far_b, near_b, cross_b, own, blocks, *scratch
):
    scatter, (send, recv, local, fetched, fold_send, fold_recv, fold_local, mine, theirs, resid, upstream, row_sems) = scratch[:7], scratch[7:]
    rows_fetched = [
        pltpu.make_async_copy(source, target, row_sems.at[k])
        for k, (source, target) in enumerate(((resid_home, resid), (upstream_home, upstream)))
    ]
    y, c, z, x = spot()
    width = w_gate.shape[0]
    order = [
        place_of(r, k, q, half)
        for half in (0, 1)
        for r, q in ((1 - y, 1 - x), (y, 1 - x), (1 - y, x), (y, x))
        for k in (1 - c, c)
    ]

    def fetch(turn):
        slot = turn % 2
        return [
            pltpu.make_async_copy(source.at[order[turn]], blocks.at[slot, m], fetched.at[slot, m])
            for m, source in enumerate((d_gate, d_up))
        ]

    for copy in fetch(0) + rows_fetched:
        copy.start()
    greet(near() + fold_peers())
    folds = [
        Fold(columns_of_layer(grad), *refs, mine.at[k], theirs, fold_send.at[k], fold_recv.at[k], fold_local.at[k])
        for k, (grad, *refs) in enumerate(((grad_a, far_a, near_a, cross_a), (grad_b, far_b, near_b, cross_b)))
    ]
    for fold in folds:
        fold.start()

    def part_of(half):
        def produce(turn, to_y, to_c, to_x, out):
            turn = turn + 8 * half
            if turn < 15:
                for copy in fetch(turn + 1):
                    copy.start()
            for copy in fetch(turn):
                copy.wait()

            def step(i, carry):
                columns = pl.ds(pl.multiple_of(i * TILE, TILE), TILE)
                part = dot_nt(blocks[turn % 2, 0], w_gate[columns, :]) + dot_nt(blocks[turn % 2, 1], w_up[columns, :])
                out[:, columns] = part.astype(LOW)
                return carry

            lax.fori_loop(0, width // TILE, step, 0)

        return Scatter(produce, *scatter, part=half, start=half * HALF, size=HALF)

    total, landed = scatter[2], scatter[4]
    gain_term[...] = jnp.zeros_like(gain_term)

    def chunk(here):
        back, terms = norm_back(resid[here, :], gain[...], summed(total, landed, here))
        value = upstream[here, :].astype(jnp.float32) + back
        d_resid[here, :] = value
        own[here, :] = value.astype(LOW)
        fold_rows(gain_term, terms)

    def rows_of_half(half):
        if half == 0:
            for copy in rows_fetched:
                copy.wait()
        over_chunks(chunk, half)

    gather = Gather(own_halves(own), d_resid_whole, send, recv)
    sum_and_gather(part_of, rows_of_half, gather, lambda turn: folds[turn].fold() if turn < 2 else None)
    keep = pltpu.make_async_copy(own, d_resid_whole.at[place_of(y, c, x)], local.at[0])
    keep.start()
    for fold in folds:
        fold.finish()
    keep.wait()


def close_mlp(d_gate, d_up, w_gate, w_up, resid, upstream, gain, *grads):
    block, width = resid.shape
    hidden = d_gate.shape[1]
    return pl.pallas_call(
        close_mlp_kernel,
        out_shape=(
            jax.ShapeDtypeStruct((block, width), jnp.float32),
            jax.ShapeDtypeStruct((8, width), jnp.float32),
            jax.ShapeDtypeStruct((8 * block, width), LOW),
            *[jax.ShapeDtypeStruct((width, hidden // 4), LOW)] * 6,
        ),
        in_specs=[anywhere()] * 2 + [in_vmem()] * 2 + [anywhere()] * 2 + [in_vmem()] + [anywhere()] * 2,
        out_specs=[in_vmem(), in_vmem()] + [anywhere()] * 7,
        scratch_shapes=[pltpu.VMEM((block, width), LOW), pltpu.VMEM((2, 2, block // 2, hidden), LOW)]
        + scatter_scratch(width, 2)
        + [dma(GATHER_COPIES), dma(GATHER_COPIES), dma(1), dma(2, 2), dma(2, 3), dma(2, 3), dma(2, 2)]
        + [pltpu.VMEM((2, width, hidden // 4), LOW), pltpu.VMEM((width, hidden // 4), LOW)]
        + [pltpu.VMEM((block, width), jnp.float32), pltpu.VMEM((block, width), LOW), dma(2)],
        compiler_params=remote_params(3),
        cost_estimate=pl.CostEstimate(flops=0, bytes_accessed=450_000_000, transcendentals=0),
    )(d_gate, d_up, w_gate, w_up, resid, upstream, gain, *grads)


def close_layer_kernel(
    d_qkv, w_qkv, x_whole, d_resid_home, gain, mlp_term, grad, grad_low, gain_grads, far, near_part, cross, grad_parts, own, terms, layer_terms, part, column_terms, *scratch
):
    scatter, (send, recv, term_send, term_recv, line_send, line_recv, x_own, x_sem, *rest) = scratch[:7], scratch[7:]
    mine, theirs, fold_send, fold_recv, fold_local, part_send, part_recv, d_resid = rest
    fetch_d_resid = pltpu.make_async_copy(d_resid_home, d_resid, x_sem.at[1])
    fetch_d_resid.start()
    y, c, z, x = spot()
    fetch_x = pltpu.make_async_copy(x_whole.at[place_of(y, c, x)], x_own, x_sem.at[0])
    fetch_x.start()
    partner = partner_of(y, c, z, x)
    moves = z != 2 * c + y
    width = w_qkv.shape[0]
    barrier = pltpu.get_barrier_semaphore()

    @pl.when(moves)
    def _():
        pl.semaphore_signal(barrier, inc=1, device_id=partner, device_id_type=MESH_ID)

    layer = others()
    line = line_of()
    for peer in layer + line:
        pl.semaphore_signal(barrier, inc=1, device_id=peer, device_id_type=MESH_ID)
    pl.semaphore_wait(barrier, len(layer + line) + moves.astype(jnp.int32))

    size = TILE // PIECES

    def part_of(piece):
        def produce(turn, to_y, to_c, to_x, out):
            at = quarter_of(to_y, to_c, to_x, piece // 2, piece % 2)

            def step(i, carry):
                columns = pl.ds(pl.multiple_of(i * TILE, TILE), TILE)
                out[:, columns] = dot_nt(d_qkv[at, :], w_qkv[columns, :]).astype(LOW)
                return carry

            lax.fori_loop(0, width // TILE, step, 0)

        return Scatter(produce, *scatter, part=piece, start=piece * size, size=size)

    fold = Fold(lambda at: grad.at[at], far, near_part, cross, mine, theirs, fold_send, fold_recv, fold_local)
    fold.start()
    def end_fold():
        fold.finish()
        for source, target, k in ((grad.at[z], mine, 0), (near_part, theirs, 1)):
            pltpu.make_async_copy(source, target, fold_local.at[k]).start()
        for source, target, k in ((grad.at[z], mine, 0), (near_part, theirs, 1)):
            pltpu.make_async_copy(source, target, fold_local.at[k]).wait()
        add_rows(mine, 0, theirs, 0, mine.shape[0])
        last = pltpu.make_async_copy(cross, theirs, fold_local.at[1])
        last.start()
        last.wait()
        add_rows(mine, 0, theirs, 0, mine.shape[0])
        shard = mine.shape[0] // 8
        index = 4 * y + 2 * c + x
        parts = [
            remote(
                mine.at[pl.ds(pl.multiple_of((4 * peer[0] + 2 * peer[1] + peer[3]) * shard, shard), shard)],
                grad_parts.at[index],
                part_send.at[k],
                part_recv.at[k],
                peer,
            )
            for k, peer in enumerate(layer)
        ]
        kept = pltpu.make_async_copy(mine.at[pl.ds(pl.multiple_of(index * shard, shard), shard)], grad_parts.at[index], fold_local.at[0])
        for copy in parts + [kept]:
            copy.start()
        return parts + [kept]

    sums = [part_of(piece) for piece in range(PIECES)]
    sums[0].begin()
    sums[0].relay()
    sums[1].begin()
    fold.fold()
    total, landed = scatter[2], scatter[4]
    terms[1] = mlp_term[...]
    terms[0] = jnp.zeros_like(mlp_term)
    pieces = [pl.ds(piece * size, size) for piece in range(PIECES)]
    trades = [remote(own.at[at], grad_low.at[at], send.at[k], recv.at[k], partner) for k, at in enumerate(pieces)]
    keeps = [pltpu.make_async_copy(own.at[at], grad_low.at[at], recv.at[k]) for k, at in enumerate(pieces)]
    fetch_x.wait()
    fetch_d_resid.wait()
    to_peers = []
    for piece in range(PIECES):
        if piece == PIECES - 1:
            to_peers = end_fold()
        sums[piece].arrive()

        def step(i, carry):
            here = pl.ds(pl.multiple_of(piece * size + i * CHUNK, CHUNK), CHUNK)
            back, products = norm_back(x_own[here, :].astype(jnp.float32), gain[...], summed(total, landed, here))
            own[here, :] = (d_resid[here, :] + back).astype(LOW)
            fold_rows(terms.at[0], products)
            return carry

        lax.fori_loop(0, size // CHUNK, step, 0)

        @pl.when(moves)
        def _():
            trades[piece].start()

        @pl.when(jnp.logical_not(moves))
        def _():
            keeps[piece].start()

        if piece + 1 < PIECES:
            sums[piece + 1].relay()
        if piece + 2 < PIECES:
            sums[piece + 2].begin()

    def columns_of(row, layers):
        return pl.ds(pl.multiple_of((4 * row) * HD, HD), layers * HD)

    spread = [
        remote(terms.at[:, :, columns_of(2 * peer[0] + peer[1], 4)], layer_terms.at[k], term_send.at[k], term_recv.at[k], peer)
        for k, peer in enumerate(layer)
    ]
    for copy in spread:
        copy.start()
    for copy in spread:
        copy.wait_recv()
    part[...] = sum((layer_terms[k] for k in range(7)), terms[:, :, columns_of(2 * y + c, 4)])
    lines = [
        remote(
            part.at[:, :, pl.ds(pl.multiple_of(peer[2] * HD, HD), HD)], column_terms.at[k], line_send.at[k], line_recv.at[k], peer
        )
        for k, peer in enumerate(line)
    ]
    for copy in lines:
        copy.start()
    for copy in lines:
        copy.wait_recv()
    gain_grads[...] = sum((column_terms[k] for k in range(3)), part[:, :, pl.ds(pl.multiple_of(z * HD, HD), HD)])
    for copy in spread + lines:
        copy.wait_send()
    for part_sum in sums:
        part_sum.finish()
    for copy in to_peers:
        copy.wait()

    @pl.when(moves)
    def _():
        for copy in trades:
            copy.wait()

    @pl.when(jnp.logical_not(moves))
    def _():
        for copy in keeps:
            copy.wait()


def close_layer(d_qkv, w_qkv, x_whole, d_resid, gain, mlp_term, grad):
    block, width = d_resid.shape
    return pl.pallas_call(
        close_layer_kernel,
        out_shape=(
            jax.ShapeDtypeStruct((block, width), LOW),
            jax.ShapeDtypeStruct((2, 8, width // 16), jnp.float32),
            *[jax.ShapeDtypeStruct(grad.shape[1:], LOW)] * 3,
            jax.ShapeDtypeStruct((8, grad.shape[1] // 8, grad.shape[2]), LOW),
        ),
        in_specs=[in_vmem(), in_vmem(), anywhere(), anywhere(), in_vmem(), in_vmem(), anywhere()],
        out_specs=[anywhere(), in_vmem()] + [anywhere()] * 4,
        scratch_shapes=[
            pltpu.VMEM((block, width), LOW),
            pltpu.VMEM((2, 8, width), jnp.float32),
            pltpu.VMEM((7, 2, 8, width // 4), jnp.float32),
            pltpu.VMEM((2, 8, width // 4), jnp.float32),
            pltpu.VMEM((3, 2, 8, width // 16), jnp.float32),
        ]
        + scatter_scratch(width, PIECES)
        + [dma(PIECES), dma(PIECES), dma(7), dma(7), dma(3), dma(3), pltpu.VMEM((block, width), LOW), dma(2)]
        + [pltpu.VMEM(grad.shape[1:], LOW)] * 2
        + [dma(3), dma(3), dma(2), dma(7), dma(7), pltpu.VMEM((block, width), jnp.float32)],
        compiler_params=remote_params(4),
        cost_estimate=pl.CostEstimate(flops=0, bytes_accessed=350_000_000, transcendentals=0),
    )(d_qkv, w_qkv, x_whole, d_resid, gain, mlp_term, grad)


def doc_start(ends, place):
    start = jnp.zeros_like(place)
    for k in range(8):
        start = jnp.where(ends[k] <= place, ends[k], start)
    return jnp.where(place < ends[7], start, LEN)


def sigmoid_of(raw):
    return pl.reciprocal(1.0 + jnp.exp2(math.log2(LEN) - raw * (math.log2(math.e) / math.sqrt(HD))), approx=True)


def tile_at(index):
    return pl.ds(pl.multiple_of(index * TILE, TILE), TILE)


def head_of(array, rows, part, head):
    first = (part * (array.shape[1] // 3) // HD + head) * HD
    return array[rows, first : first + HD]


def attend_kernel(ends, qkv, out, total):
    i = pl.program_id(0)
    heads = qkv.shape[1] // (3 * HD)
    total[...] = jnp.zeros_like(total)
    q_place = i * TILE + lax.broadcasted_iota(jnp.int32, (TILE, 1), 0)
    q_start = doc_start(ends, q_place)

    def tile(j, diagonal):
        k_place = j * TILE + lax.broadcasted_iota(jnp.int32, (1, TILE), 1)
        allowed = k_place >= q_start
        if diagonal:
            allowed = allowed & (k_place <= q_place)
        for head in range(heads):
            raw = dot_nt(head_of(qkv, tile_at(i), 0, head), head_of(qkv, tile_at(j), 1, head))
            weight = jnp.where(allowed, sigmoid_of(raw), 0.0).astype(LOW)
            total[head] += dot_wide(weight, head_of(qkv, tile_at(j), 2, head))

    def step(j, carry):
        tile(j, False)
        return carry

    lax.fori_loop(0, i, step, 0)
    tile(i, True)
    for head in range(heads):
        out[tile_at(i), head * HD : (head + 1) * HD] = total[head].astype(LOW)


def open_mlp_kernel(normed, w_gate, w_up, upstream, gate, up, hidden, upstream_whole, send, recv, local):
    i = pl.program_id(0)
    y, c, z, x = spot()
    steps = pl.num_programs(0)
    gather = Gather(lambda half: upstream.at[pl.ds(half * HALF, HALF)], upstream_whole, send, recv)
    keep = pltpu.make_async_copy(upstream, upstream_whole.at[place_of(y, c, x)], local.at[0])

    @pl.when(i == 0)
    def _():
        greet(near())
        gather.start(0)
        gather.start(1)
        keep.start()

    def step(n, carry):
        columns = pl.ds(pl.multiple_of(n * TILE, TILE), TILE)
        gate_part, up_part = dot_wide(normed[...], w_gate[:, columns]), dot_wide(normed[...], w_up[:, columns])
        gate[:, columns] = gate_part
        up[:, columns] = up_part
        hidden[:, columns] = (gate_part * jax.nn.sigmoid(gate_part) * up_part).astype(LOW)
        return carry

    lax.fori_loop(0, w_gate.shape[1] // TILE, step, 0)

    @pl.when(i == steps - 1)
    def _():
        for half in (0, 1):
            gather.pass_near(half)
        for half in (0, 1):
            gather.pass_far(half)
        gather.finish()
        keep.wait()


def open_mlp(normed, w_gate, w_up, upstream):
    places, width = normed.shape
    hidden = w_gate.shape[1]
    rows = lambda columns: pl.BlockSpec((TILE, columns), lambda i: (i, 0))
    whole = lambda array: pl.BlockSpec(array.shape, lambda i: (0, 0))
    return pl.pallas_call(
        open_mlp_kernel,
        out_shape=(
            jax.ShapeDtypeStruct((places, hidden), jnp.float32),
            jax.ShapeDtypeStruct((places, hidden), jnp.float32),
            jax.ShapeDtypeStruct((places, hidden), LOW),
            jax.ShapeDtypeStruct((places, width), LOW),
        ),
        grid=(places // TILE,),
        in_specs=[rows(width), whole(w_gate), whole(w_up), whole(upstream)],
        out_specs=[rows(hidden), rows(hidden), rows(hidden), anywhere()],
        scratch_shapes=[dma(GATHER_COPIES), dma(GATHER_COPIES), dma(1)],
        compiler_params=remote_params(5),
        cost_estimate=pl.CostEstimate(flops=0, bytes_accessed=250_000_000, transcendentals=0),
    )(normed, w_gate, w_up, upstream)


def out_turns():
    y, c, z, x = spot()
    layers = (x, x, 3 - x, 3 - x)
    owners = [((y, c, layers[j], j % 2), (z == layers[j]) & (x == j % 2)) for j in range(4)]
    side = lax.rem((z + 1) // 2, 2)
    holders = [((y, c, j, side), (z == j) & (x == side)) for j in range(4)]
    return owners, holders


def attend_back_kernel(
    ends, qkv, grads, out_grad, mixed, out, out_parts, mixed_home, query_total, key_total, value_total, send, recv, *trade_parts
):
    j = pl.program_id(0)
    y, c, z, x = spot()
    heads = qkv.shape[1] // (3 * HD)
    shard = out_grad.shape[0] // 4
    owners, holders = out_turns()
    trade = Trade(
        [mixed.at[pl.ds(half * HALF, HALF)] for half in (0, 1)], lambda half, at: mixed_home.at[pl.ds(half * HALF, HALF)], *trade_parts
    )

    def to_owner(turn):
        return remote(out_grad.at[pl.ds(turn * shard, shard)], out_parts.at[z], send.at[turn], recv.at[z], owners[turn][0])

    def to_self(turn):
        return pltpu.make_async_copy(out_grad.at[pl.ds(turn * shard, shard)], out_parts.at[z], recv.at[z])

    @pl.when(j == 0)
    def _():
        query_total[...] = jnp.zeros_like(query_total)
        barrier = pltpu.get_barrier_semaphore()
        for peer, here in holders:

            @pl.when(jnp.logical_not(here))
            def _():
                pl.semaphore_signal(barrier, inc=1, device_id=peer, device_id_type=MESH_ID)

        pl.semaphore_wait(barrier, 4 - (x == lax.rem((z + 1) // 2, 2)).astype(jnp.int32) + trade.greet(barrier, False))
        for half in (0, 1):
            trade.start(half)
        for turn in range(4):

            @pl.when(jnp.logical_not(owners[turn][1]))
            def _():
                to_owner(turn).start()

            @pl.when(owners[turn][1])
            def _():
                to_self(turn).start()

    key_total[...] = jnp.zeros_like(key_total)
    value_total[...] = jnp.zeros_like(value_total)
    here = tile_at(j)
    k_place = j * TILE + lax.broadcasted_iota(jnp.int32, (TILE, 1), 0)
    turned = [head_of(qkv, here, 1, head).T for head in range(heads)]

    def tile(i, diagonal):
        q_place = i * TILE + lax.broadcasted_iota(jnp.int32, (1, TILE), 1)
        allowed = k_place >= doc_start(ends, q_place)
        if diagonal:
            allowed = allowed & (k_place <= q_place)
        for head in range(heads):
            query, grad = head_of(qkv, tile_at(i), 0, head), grads[tile_at(i), head * HD : (head + 1) * HD]
            sig = jnp.where(allowed, sigmoid_of(dot_nt(head_of(qkv, here, 1, head), query)), 0.0)
            value_total[head] += dot_wide(sig.astype(LOW), grad)
            d_score = (dot_nt(head_of(qkv, here, 2, head), grad) * (sig * (1.0 - sig))).astype(LOW)
            key_total[head] += dot_wide(d_score, query)
            query_total[head, :, tile_at(i)] += dot_wide(turned[head], d_score)

    def step(i, carry):
        tile(i, False)
        return carry

    tile(j, True)
    lax.fori_loop(j + 1, LEN // TILE, step, 0)
    scale = 1.0 / math.sqrt(HD)
    for head in range(heads):
        first = head * HD
        out[here, heads * HD + first : (heads + 1) * HD + first] = (key_total[head] * scale).astype(LOW)
        out[here, 2 * heads * HD + first : (2 * heads + 1) * HD + first] = value_total[head].astype(LOW)
        out[here, first : first + HD] = (query_total[head, :, here] * scale).T.astype(LOW)

    @pl.when(j == LEN // TILE - 1)
    def _():
        for turn in range(4):

            @pl.when(jnp.logical_not(owners[turn][1]))
            def _():
                to_owner(turn).wait_send()

            @pl.when(jnp.logical_not(holders[turn][1]))
            def _():
                landed = out_parts.at[turn]
                remote(landed, landed, send.at[turn], recv.at[turn], holders[turn][0]).wait_recv()

            @pl.when(owners[turn][1])
            def _():
                to_self(turn).wait()

        for half in (0, 1):
            trade.arrive(half)
        trade.finish()

    @pl.when(j == 1)
    def _():
        for half in (0, 1):
            trade.forward(half)


def back_mlp_kernel(upstream, w_down, gate, up, d_gate, d_up):
    def step(n, carry):
        columns = pl.ds(pl.multiple_of(n * TILE, TILE), TILE)
        d_hidden = dot_nt(upstream[...], w_down[columns, :])
        d_gate[:, columns], d_up[:, columns] = gate_backward(
            d_hidden, gate[:, columns], up[:, columns], jax.nn.sigmoid(gate[:, columns])
        )
        return carry

    lax.fori_loop(0, gate.shape[1] // TILE, step, 0, unroll=2)


def back_mlp(upstream, w_down, gate, up):
    places, width = upstream.shape
    hidden = gate.shape[1]
    rows = lambda size: pl.BlockSpec((TILE, size), lambda i: (i, 0))
    return pl.pallas_call(
        back_mlp_kernel,
        out_shape=(jax.ShapeDtypeStruct((places, hidden), LOW), jax.ShapeDtypeStruct((places, hidden), LOW)),
        grid=(places // TILE,),
        in_specs=[rows(width), pl.BlockSpec(w_down.shape, lambda i: (0, 0)), rows(hidden), rows(hidden)],
        out_specs=[rows(hidden), rows(hidden)],
        compiler_params=pltpu.CompilerParams(vmem_limit_bytes=VMEM_LIMIT),
        cost_estimate=pl.CostEstimate(flops=0, bytes_accessed=90_000_000, transcendentals=0),
    )(upstream, w_down, gate, up)


def attend(ends, qkv):
    places, width = qkv.shape
    heads = width // (3 * HD)
    whole = lambda columns: pl.BlockSpec((places, columns), lambda i: (0, 0))
    return pl.pallas_call(
        attend_kernel,
        out_shape=jax.ShapeDtypeStruct((places, width // 3), LOW),
        grid=(places // TILE,),
        in_specs=[pl.BlockSpec(memory_space=pltpu.SMEM), whole(width)],
        out_specs=whole(width // 3),
        scratch_shapes=[pltpu.VMEM((heads, TILE, HD), jnp.float32)],
        compiler_params=pltpu.CompilerParams(vmem_limit_bytes=VMEM_LIMIT),
        cost_estimate=pl.CostEstimate(flops=0, bytes_accessed=150_000_000, transcendentals=0),
    )(ends, qkv)


def attend_back(ends, qkv, grads, out_grad, mixed):
    places, width = qkv.shape
    heads = width // (3 * HD)
    whole = lambda columns: pl.BlockSpec((places, columns), lambda j: (0, 0))
    return pl.pallas_call(
        attend_back_kernel,
        out_shape=(
            jax.ShapeDtypeStruct((places, width), LOW),
            jax.ShapeDtypeStruct((4, out_grad.shape[0] // 4, out_grad.shape[1]), LOW),
            jax.ShapeDtypeStruct(mixed.shape, LOW),
        ),
        grid=(places // TILE,),
        in_specs=[pl.BlockSpec(memory_space=pltpu.SMEM), whole(width), whole(width // 3), anywhere(), pl.BlockSpec(mixed.shape, lambda j: (0, 0))],
        out_specs=[whole(width), anywhere(), anywhere()],
        scratch_shapes=[
            pltpu.VMEM((heads, HD, places), jnp.float32),
            pltpu.VMEM((heads, TILE, HD), jnp.float32),
            pltpu.VMEM((heads, TILE, HD), jnp.float32),
            dma(4),
            dma(4),
            *trade_scratch(2, HALF, mixed.shape[1]),
        ],
        compiler_params=remote_params(6),
        cost_estimate=pl.CostEstimate(flops=0, bytes_accessed=300_000_000, transcendentals=0),
    )(ends, qkv, grads, out_grad, mixed)


LAYER = ("y", "c", "x")
PLACES = ("c", "y", "x")
ALL = ("y", "c", "z", "x")


def trade(part):
    pairs = []
    for y in range(2):
        for c in range(2):
            for z in range(4):
                for x in range(2):
                    pairs.append((((y * 2 + c) * 4 + z) * 2 + x, (((z % 2) * 2 + z // 2) * 4 + 2 * c + y) * 2 + x))
    return lax.ppermute(part, ALL, pairs)


def after(first, then):
    return lax.optimization_barrier((first, then))[1]


def body_layers(
    tokens, lengths, cotangent, w_query, w_key, w_value, w_out, w_gate, w_up, w_down, gain_attn, gain_mlp
):
    rows_here, block, width = tokens.shape
    members = lax.axis_size(LAYER)
    layers = lax.axis_size("z")
    shard = w_query.shape[0]
    owned = width // members
    facts = jnp.zeros((8, 2 * shard), jnp.float32)
    facts = facts.at[0, :shard].set(gain_attn.astype(jnp.float32)).at[1, :shard].set(gain_mlp.astype(jnp.float32))
    facts = facts.at[2, : lengths.shape[1]].set(lengths[0].astype(jnp.float32))
    layer_x, w_qkv, facts = begin(tokens.reshape(block, width), w_query, w_key, w_value, facts)
    full_gain_attn, full_gain_mlp = facts[:, :, :, 0, :shard].reshape(1, width), facts[:, :, :, 1, :shard].reshape(1, width)
    layer = lax.axis_index("z")
    own_lengths = facts[:, 0, 0, 2, : lengths.shape[1]].reshape(2, 2, -1)
    own_lengths = lax.dynamic_slice(own_lengths, (layer % 2, layer // 2, 0), (1, 1, own_lengths.shape[2]))[0, 0]
    ends = jnp.cumsum(own_lengths.astype(jnp.int32))
    layer_normed = norm_forward(layer_x.astype(jnp.float32), full_gain_attn)[0].astype(LOW)
    here = lax.axis_index("x")
    out_rows = lax.all_gather(after(facts, w_out), ("z", "x"), axis=0, tiled=True)
    w_out_own = [lax.dynamic_slice_in_dim(out_rows, head * HD, HD, 0) for head in (here, 3 - here)]
    w_out_own = jnp.concatenate(w_out_own, axis=0)

    qkv = dot_wide(layer_normed, w_qkv).astype(LOW)
    upstream = trade(after(facts, cotangent)).reshape(block, width)
    attended = attend(ends, qkv)
    resid, layer_mlp, own_gate, own_up = close_attention(after(upstream, attended), w_out_own, layer_x, full_gain_mlp, w_gate, w_up)

    own_down = lax.all_gather(after(resid, w_down), "z", axis=0, tiled=True)
    gate, up_part, hidden, layer_upstream = open_mlp(layer_mlp, own_gate, own_up, upstream)
    part = dot_wide(hidden, own_down).astype(LOW)
    mixed_sum = lax.psum_scatter(part, PLACES, scatter_dimension=0, tiled=True)
    down_term = contract_rows(after(part, hidden), layer_upstream).astype(LOW)
    down_rows = w_down.shape[0]
    down_parts = []
    for up in range(1, 4):
        layers_pairs = [(at, (at + up) % 4) for at in range(4)]
        slab = lax.dynamic_slice_in_dim(down_term, (layer + up) % 4 * down_rows, down_rows, 0)
        down_parts.append(lax.ppermute(slab, "z", layers_pairs))
    d_gate, d_up = back_mlp(after(down_term, layer_upstream), own_down, gate, up_part)
    gate_term, up_term = contract_rows(layer_mlp, d_gate).astype(LOW), contract_rows(layer_mlp, d_up).astype(LOW)
    d_resid, gain_mlp_term, layer_d_resid, *parts = close_mlp(
        d_gate, d_up, own_gate, own_up, resid, upstream, full_gain_mlp, gate_term, up_term
    )

    def own_part(whole, near_part, cross):
        own = lax.dynamic_slice_in_dim(whole, layer * cross.shape[1], cross.shape[1], 1)
        return own.astype(jnp.float32) + near_part.astype(jnp.float32) + cross.astype(jnp.float32)

    mixed = (resid + after(layer_d_resid, mixed_sum).astype(jnp.float32)).astype(LOW)
    grad_down = lax.dynamic_slice_in_dim(down_term, layer * down_rows, down_rows, 0).astype(jnp.float32)
    grad_down = grad_down + sum(slab.astype(jnp.float32) for slab in after(layer_d_resid, down_parts))

    out_term = contract_rows(attended, layer_d_resid).astype(LOW)
    d_attended = contract_cols(layer_d_resid, w_out_own).astype(LOW)
    d_qkv, out_parts, mixed = attend_back(ends, qkv, d_attended, out_term, mixed)
    mixed = mixed.reshape(rows_here, block, width)
    grad_gate, grad_up = own_part(gate_term, *parts[1:3]), own_part(up_term, *parts[4:6])
    grad_out = jnp.sum(out_parts.astype(jnp.float32), axis=0)
    qkv_term = contract_rows(layer_normed, d_qkv).astype(LOW)
    qkv_term = qkv_term.reshape(4, layers, 2 * shard, 3 * owned).transpose(1, 0, 2, 3)
    qkv_term = qkv_term.reshape(layers, members * shard, 3 * owned)
    grad_low, gain_grads, *_, parts = close_layer(
        d_qkv, w_qkv, layer_x, d_resid, full_gain_attn, gain_mlp_term, qkv_term
    )
    grad_tokens = grad_low.astype(jnp.float32).reshape(rows_here, block, width)
    parts = parts.reshape(4, 2, shard, 3, 2, HD)
    parts = jnp.stack((parts[:, 0, :, :, 0], parts[:, 1, :, :, 0], parts[:, 1, :, :, 1], parts[:, 0, :, :, 1]), axis=1)
    grad_query, grad_key, grad_value = parts.transpose(3, 2, 0, 1, 4).astype(jnp.float32).reshape(3, shard, width)
    gain_grads = lax.dynamic_index_in_dim(jnp.sum(gain_grads, axis=1).reshape(2, 2, shard), lax.axis_index("x"), 1, False)
    return (
        mixed,
        grad_tokens,
        grad_query,
        grad_key,
        grad_value,
        grad_out,
        grad_gate,
        grad_up,
        grad_down,
        gain_grads[0],
        gain_grads[1],
    )


def body_any(
    tokens,
    lengths,
    cotangent,
    w_query,
    w_key,
    w_value,
    w_out,
    w_gate,
    w_up,
    w_down,
    gain_attn,
    gain_mlp,
):
    rows_here, block, width = tokens.shape
    count = rows_here * block
    scale = 1.0 / math.sqrt(HD)
    kv_place = lax.axis_index("kv")
    key_places = kv_place * block + jnp.arange(block, dtype=jnp.int32)
    attn_set = (
        lax.all_gather(w_query, ("row", "kv"), axis=0, tiled=True),
        lax.all_gather(w_key, ("row", "kv"), axis=0, tiled=True),
        lax.all_gather(w_value, ("row", "kv"), axis=0, tiled=True),
        lax.all_gather(w_out, ("row", "kv"), axis=0, tiled=True),
        lax.all_gather(gain_attn, ("row", "kv"), axis=0, tiled=True),
        lax.all_gather(gain_mlp, ("row", "kv"), axis=0, tiled=True),
    )
    full_query, full_key, full_value, full_out, full_gain_attn, full_gain_mlp = attn_set
    flat = tokens.reshape(count, width).astype(jnp.float32)
    normed_attn, inverse_attn = norm_forward(flat, full_gain_attn)
    normed_attn_low = normed_attn.astype(jnp.bfloat16)
    query_low = jnp.dot(normed_attn_low, full_query, preferred_element_type=jnp.float32).astype(
        jnp.bfloat16
    )
    key_low = jnp.dot(normed_attn_low, full_key, preferred_element_type=jnp.float32).astype(
        jnp.bfloat16
    )
    value_low = jnp.dot(normed_attn_low, full_value, preferred_element_type=jnp.float32).astype(
        jnp.bfloat16
    )
    key_heads = key_low.reshape(rows_here, block, H, HD)
    value_heads = value_low.reshape(rows_here, block, H, HD)
    segment, valid = segment_table(lengths)
    key_segment = lax.dynamic_slice_in_dim(segment, kv_place * block, block, 1)
    key_valid = lax.dynamic_slice_in_dim(valid, kv_place * block, block, 1)
    queries_all = lax.all_gather(
        query_low.reshape(rows_here, block, width), "kv", axis=1, tiled=True
    )
    which = 0
    query_rows = queries_all[which]
    query_segment = segment[which]
    sigmoid_part, allowed = score_block(
        query_rows,
        key_heads[which],
        query_segment,
        key_segment[which],
        key_valid[which],
        jnp.int32(0),
        key_places,
    )
    weight = (sigmoid_part * allowed).astype(jnp.bfloat16)
    summed = jnp.einsum(
        "hqk,khd->qhd", weight, value_heads[which], preferred_element_type=jnp.float32
    )
    pieces = [
        lax.psum_scatter(
            summed.reshape(lax.axis_size("kv") * block, width).astype(jnp.bfloat16),
            "kv",
            scatter_dimension=0,
            tiled=True,
        ).astype(jnp.float32)
    ]
    attended_low = jnp.stack(pieces).reshape(count, width).astype(jnp.bfloat16)
    resid = flat + jnp.dot(attended_low, full_out, preferred_element_type=jnp.float32)
    normed_mlp, inverse_mlp = norm_forward(resid, full_gain_mlp)
    normed_mlp_low = normed_mlp.astype(jnp.bfloat16)
    upstream_low = cotangent.reshape(count, width)
    upstream = upstream_low.astype(jnp.float32)
    slice_gate, slice_up, slice_down = (
        lax.all_gather(w_gate, "row", axis=1, tiled=True),
        lax.all_gather(w_up, "row", axis=1, tiled=True),
        lax.all_gather(w_down, "row", axis=0, tiled=True),
    )
    row_normed, row_upstream = (
        lax.all_gather(normed_mlp_low.reshape(rows_here, block, width), "kv", axis=1, tiled=True),
        lax.all_gather(cotangent, "kv", axis=1, tiled=True),
    )
    normed_rows = row_normed.reshape(rows_here * LEN, width)
    upstream_rows = row_upstream.reshape(rows_here * LEN, width)
    gate = jnp.dot(normed_rows, slice_gate, preferred_element_type=jnp.float32)
    up_part = jnp.dot(normed_rows, slice_up, preferred_element_type=jnp.float32)
    sigmoid_gate = jax.nn.sigmoid(gate)
    hidden_low = (gate * sigmoid_gate * up_part).astype(jnp.bfloat16)
    hidden_rows = hidden_low.reshape(rows_here, LEN, hidden_low.shape[1])
    which = 0
    hidden_part = hidden_rows[which]
    outputs = [
        lax.psum_scatter(
            jnp.dot(hidden_part, slice_down, preferred_element_type=jnp.float32).astype(
                jnp.bfloat16
            ),
            "kv",
            scatter_dimension=0,
            tiled=True,
        ).astype(jnp.float32)
    ]
    result = resid + jnp.stack(outputs).reshape(count, width)
    d_hidden = contract_cols(upstream_rows, slice_down)
    d_gate, d_up = gate_backward(d_hidden, gate, up_part, sigmoid_gate)
    partial_normed = contract_cols(d_gate, slice_gate) + contract_cols(d_up, slice_up)
    d_normed_mlp = (
        lax.psum_scatter(
            partial_normed.reshape(rows_here, LEN, width).astype(jnp.bfloat16),
            "kv",
            scatter_dimension=1,
            tiled=True,
        )
        .astype(jnp.float32)
        .reshape(count, width)
    )
    grad_gate, grad_up, grad_down = (
        lax.psum_scatter(
            contract_rows(normed_rows, d_gate).astype(jnp.bfloat16),
            "row",
            scatter_dimension=1,
            tiled=True,
        ).astype(jnp.float32),
        lax.psum_scatter(
            contract_rows(normed_rows, d_up).astype(jnp.bfloat16),
            "row",
            scatter_dimension=1,
            tiled=True,
        ).astype(jnp.float32),
        lax.psum_scatter(
            contract_rows(hidden_low, upstream_rows).astype(jnp.bfloat16),
            "row",
            scatter_dimension=0,
            tiled=True,
        ).astype(jnp.float32),
    )
    mixed = result.astype(jnp.bfloat16).reshape(rows_here, block, width)
    back_mlp, gain_mlp_term = norm_backward(resid, inverse_mlp, full_gain_mlp, d_normed_mlp)
    d_resid = upstream + back_mlp
    d_resid_low = d_resid.astype(jnp.bfloat16)
    d_attended = contract_cols(d_resid_low, full_out).astype(jnp.bfloat16)
    grads_all = lax.all_gather(
        d_attended.reshape(rows_here, block, width), "kv", axis=1, tiled=True
    )
    query_block = min(512, LEN)
    block_count = LEN // query_block
    which = 0

    def sweep(carry, index, which=which):
        key_total, value_total = carry
        start = index * query_block
        query_rows = lax.dynamic_slice_in_dim(queries_all[which], start, query_block, 0)
        grad_rows = lax.dynamic_slice_in_dim(grads_all[which], start, query_block, 0)
        query_segment = lax.dynamic_slice_in_dim(segment[which], start, query_block, 0)
        sigmoid_part, allowed = score_block(
            query_rows,
            key_heads[which],
            query_segment,
            key_segment[which],
            key_valid[which],
            start,
            key_places,
        )
        weight = (sigmoid_part * allowed).astype(jnp.bfloat16)
        grad_heads = grad_rows.reshape(query_block, H, HD)
        value_total = value_total + jnp.einsum(
            "hqk,qhd->khd", weight, grad_heads, preferred_element_type=jnp.float32
        )
        d_weight = jnp.einsum(
            "qhd,khd->hqk", grad_heads, value_heads[which], preferred_element_type=jnp.float32
        )
        d_score = (d_weight * sigmoid_part * (1.0 - sigmoid_part) * allowed).astype(jnp.bfloat16)
        query_part = (
            jnp.einsum(
                "hqk,khd->qhd", d_score, key_heads[which], preferred_element_type=jnp.float32
            )
            * scale
        )
        key_total = (
            key_total
            + jnp.einsum(
                "hqk,qhd->khd",
                d_score,
                query_rows.reshape(query_block, H, HD),
                preferred_element_type=jnp.float32,
            )
            * scale
        )
        return ((key_total, value_total), query_part.reshape(query_block, width))

    zeros = jnp.zeros((block, H, HD), jnp.float32)
    totals, query_parts = lax.scan(sweep, (zeros, zeros), jnp.arange(block_count, dtype=jnp.int32))
    query_terms = [query_parts.reshape(LEN, width)]
    key_grads = [totals[0].reshape(block, width)]
    value_grads = [totals[1].reshape(block, width)]
    query_local = lax.psum_scatter(
        jnp.stack(query_terms).astype(jnp.bfloat16), "kv", scatter_dimension=1, tiled=True
    ).astype(jnp.float32)
    d_query_low = query_local.reshape(count, width).astype(jnp.bfloat16)
    d_key_low = jnp.stack(key_grads).reshape(count, width).astype(jnp.bfloat16)
    d_value_low = jnp.stack(value_grads).reshape(count, width).astype(jnp.bfloat16)
    d_normed_attn = (
        contract_cols(d_query_low, full_query)
        + contract_cols(d_key_low, full_key)
        + contract_cols(d_value_low, full_value)
    )
    back_attn, gain_attn_term = norm_backward(flat, inverse_attn, full_gain_attn, d_normed_attn)
    grad_tokens = (d_resid + back_attn).reshape(rows_here, block, width)
    projected_low = jnp.concatenate((d_query_low, d_key_low, d_value_low), axis=1)
    grad_projections = lax.psum_scatter(
        contract_rows(normed_attn_low, projected_low),
        ("row", "kv"),
        scatter_dimension=0,
        tiled=True,
    )
    out_term = contract_rows(attended_low, d_resid_low)
    grad_out, grad_gain_attn, grad_gain_mlp = (
        lax.psum_scatter(out_term, ("row", "kv"), scatter_dimension=0, tiled=True),
        lax.psum_scatter(gain_attn_term, ("row", "kv"), scatter_dimension=0, tiled=True),
        lax.psum_scatter(gain_mlp_term, ("row", "kv"), scatter_dimension=0, tiled=True),
    )
    grad_query = grad_projections[:, :width]
    grad_key = grad_projections[:, width : 2 * width]
    grad_value = grad_projections[:, 2 * width :]
    return (
        mixed,
        grad_tokens,
        grad_query,
        grad_key,
        grad_value,
        grad_out,
        grad_gate,
        grad_up,
        grad_down,
        grad_gain_attn,
        grad_gain_mlp,
    )


def solution(mesh):
    rows, columns = mesh.shape["row"], mesh.shape["kv"]
    if rows == 4 and columns == 2 * rows:
        mesh = Mesh(mesh.devices.reshape(2, 2, rows, 2), ("y", "c", "z", "x"))
        row, kv, run = ("y", "c"), ("z", "x"), body_layers
    else:
        row, kv, run = "row", "kv", body_any
    both = ("y", "c", "z", "x") if run is body_layers else ("row", "kv")
    tall, wide, flat = P(both, None), P(None, both), P(both)
    tokens = P(row, kv, None)
    return jax.shard_map(
        run,
        mesh=mesh,
        in_specs=(tokens, P(row, None), tokens, tall, tall, tall, tall, wide, wide, tall, flat, flat),
        out_specs=(tokens, tokens, tall, tall, tall, tall, wide, wide, tall, flat, flat),
        check_vma=False,
    )
```

```python
import functools
import math

import jax
import jax.numpy as jnp
from jax import lax
from jax.experimental import pallas as pl
from jax.experimental.pallas import tpu as pltpu
from jax.sharding import Mesh, PartitionSpec as P

H = 16
HD = 128
LEN = 4096


EPSILON = 1e-05


def contract_rows(left, right):
    return lax.dot_general(
        left, right, (((0,), (0,)), ((), ())), preferred_element_type=jnp.float32
    )


def contract_cols(left, right):
    return lax.dot_general(
        left, right, (((1,), (1,)), ((), ())), preferred_element_type=jnp.float32
    )


def norm_forward(value, gain):
    inverse = lax.rsqrt(jnp.mean(value * value, axis=-1, keepdims=True) + EPSILON)
    return (value * inverse * gain.astype(jnp.float32), inverse)


def norm_backward(value, inverse, gain, upstream):
    scaled = upstream * gain.astype(jnp.float32)
    inner = jnp.mean(scaled * value, axis=-1, keepdims=True)
    back = inverse * scaled - value * (inverse * inverse * inverse) * inner
    gain_term = jnp.sum(upstream * value * inverse, axis=0)
    return (back, gain_term)


def segment_table(lengths):
    ends = jnp.cumsum(lengths, axis=-1)
    places = jnp.arange(LEN, dtype=jnp.int32)
    segment = jnp.sum((ends[:, None, :] <= places[None, :, None]).astype(jnp.int32), axis=-1)
    valid = places[None, :] < ends[:, -1:]
    return (segment, valid)


def score_block(
    query_rows, key_heads, query_segment, key_segment, key_valid, query_start, key_places
):
    count = query_rows.shape[0]
    query_heads = query_rows.reshape(count, H, HD)
    raw = jnp.einsum("qhd,khd->hqk", query_heads, key_heads, preferred_element_type=jnp.float32)
    scores = raw * (1.0 / math.sqrt(HD)) - math.log(LEN)
    places = query_start + jnp.arange(count, dtype=jnp.int32)
    allowed = (
        (key_places[None, :] <= places[:, None])
        & (key_segment[None, :] == query_segment[:, None])
        & key_valid[None, :]
    )
    return (jax.nn.sigmoid(scores), allowed.astype(jnp.float32)[None])


def gate_backward(d_hidden, gate, up_part, sigmoid_gate):
    d_gate = (d_hidden * up_part * sigmoid_gate * (1.0 + gate * (1.0 - sigmoid_gate))).astype(
        jnp.bfloat16
    )
    d_up = (d_hidden * gate * sigmoid_gate).astype(jnp.bfloat16)
    return (d_gate, d_up)


TILE = 512
LOW = jnp.bfloat16
VMEM_LIMIT = 60 * 1024 * 1024


def dot_nt(left, right):
    return lax.dot_general(left, right, (((1,), (1,)), ((), ())), preferred_element_type=jnp.float32)


def dot_wide(left, right):
    return jnp.dot(left, right, preferred_element_type=jnp.float32)


HALF = TILE // 2
PIECES = 4
CHUNK = 32
MESH_ID = pl.DeviceIdType.MESH


def flip(bit, by):
    return bit + by - 2 * bit * by


def spot():
    return tuple(lax.axis_index(name) for name in ("y", "c", "z", "x"))


def near():
    y, c, z, x = spot()
    return (y, c, z, 1 - x), (1 - y, c, z, x), (y, 1 - c, z, x)


def partner_of(y, c, z, x):
    return lax.rem(z, 2), z // 2, 2 * c + y, x


def place_of(y, c, x, half=None):
    first = (4 * c + 2 * y + x) * TILE
    if half is None:
        return pl.ds(pl.multiple_of(first, TILE), TILE)
    return pl.ds(pl.multiple_of(first + half * HALF, HALF), HALF)


def quarter_of(y, c, x, half, quarter):
    return pl.ds(pl.multiple_of((4 * c + 2 * y + x) * TILE + half * HALF + quarter * (HALF // 2), HALF // 2), HALF // 2)


def remote(src, dst, send, recv, peer):
    return pltpu.make_async_remote_copy(
        src_ref=src, dst_ref=dst, send_sem=send, recv_sem=recv, device_id=peer, device_id_type=MESH_ID
    )


def greet(peers):
    barrier = pltpu.get_barrier_semaphore()
    for peer in peers:
        pl.semaphore_signal(barrier, inc=1, device_id=peer, device_id_type=MESH_ID)
    pl.semaphore_wait(barrier, len(peers))


class Gather:
    def __init__(self, own, whole, send, recv):
        y, c, z, x = spot()
        across_x, across_y, core = near()

        def passed(k, at, peer):
            return remote(whole.at[at], whole.at[at], send.at[k], recv.at[k], peer)

        self.halves = []
        for half in (0, 1):
            k, at = 9 * half, place_of(y, c, x, half)
            mine = [
                remote(own(half), whole.at[at], send.at[k + m], recv.at[k + m], peer)
                for m, peer in enumerate((across_x, across_y, core))
            ]
            held_x, held_y = (y, c, 1 - x), (1 - y, c, x)
            far = (1 - y, c, 1 - x)
            self.halves.append(
                (
                    mine,
                    passed(k + 3, quarter_of(*held_x, half, 0), across_y),
                    passed(k + 4, quarter_of(*held_y, half, 1), across_x),
                    [passed(k + 5, place_of(*held_x, half), core), passed(k + 6, place_of(*held_y, half), core)],
                    [passed(k + 7 + q, quarter_of(*far, half, q), core) for q in (0, 1)],
                )
            )

    def start(self, half):
        for copy in self.halves[half][0]:
            copy.start()

    def pass_near(self, half):
        mine, over_y, over_x, from_near, from_far = self.halves[half]
        mine[0].wait_recv()
        over_y.start()
        from_near[0].start()
        mine[1].wait_recv()
        over_x.start()
        from_near[1].start()

    def pass_far(self, half):
        mine, over_y, over_x, from_near, from_far = self.halves[half]
        over_y.wait_recv()
        from_far[0].start()
        over_x.wait_recv()
        from_far[1].start()

    def finish(self):
        for mine, over_y, over_x, from_near, from_far in self.halves:
            for copy in [mine[2]] + from_near + from_far:
                copy.wait_recv()
            for copy in mine + [over_y, over_x] + from_near + from_far:
                copy.wait_send()


GATHER_COPIES = 18


class GatherWhole:
    def __init__(self, own, whole, send, recv):
        y, c, z, x = spot()
        across_x, across_y, core = near()

        def from_own(k, half, peer):
            return remote(own(half), whole.at[place_of(y, c, x, half)], send.at[k], recv.at[k], peer)

        def passed(k, at, peer):
            return remote(whole.at[at], whole.at[at], send.at[k], recv.at[k], peer)

        self.mine = [
            [from_own(0, 0, across_x), from_own(1, 0, across_y), from_own(2, 0, core)],
            [from_own(3, 1, across_x), from_own(4, 1, across_y), from_own(5, 1, core)],
        ]
        held_x = [place_of(y, c, 1 - x, half) for half in (0, 1)]
        held_y = [place_of(1 - y, c, x, half) for half in (0, 1)]
        far = [place_of(1 - y, c, 1 - x, half) for half in (0, 1)]
        self.over_y, self.over_x = passed(6, held_x[0], across_y), passed(7, held_y[1], across_x)
        self.core_x = [passed(8 + half, held_x[half], core) for half in (0, 1)]
        self.core_y = [passed(10 + half, held_y[half], core) for half in (0, 1)]
        self.core_far = [passed(12 + half, far[half], core) for half in (0, 1)]

    def start(self, half):
        for copy in self.mine[half]:
            copy.start()

    def pass_first(self):
        self.mine[0][0].wait_recv()
        self.over_y.start()
        self.core_x[0].start()
        self.mine[0][1].wait_recv()
        self.core_y[0].start()

    def pass_second(self):
        self.mine[1][1].wait_recv()
        self.over_x.start()
        self.core_y[1].start()
        self.mine[1][0].wait_recv()
        self.core_x[1].start()

    def pass_far(self):
        self.over_y.wait_recv()
        self.core_far[0].start()
        self.over_x.wait_recv()
        self.core_far[1].start()

    def finish(self):
        from_core = [self.mine[0][2], self.mine[1][2]] + self.core_x + self.core_y + self.core_far
        for copy in from_core:
            copy.wait_recv()
        for copy in self.mine[0] + self.mine[1] + [self.over_y, self.over_x] + self.core_x + self.core_y + self.core_far:
            copy.wait_send()


class Trade:
    def __init__(self, sources, dst, held, send, recv, held_recv, pass_send, detour=True):
        y, c, z, x = spot()
        self.detour = detour
        across_y = (1 - y, c, z, x)
        self.moves = z != 2 * c + y
        self.away = (y == c) & (z == 1 + y)
        self.straight = self.moves & jnp.logical_not(self.away) if detour else self.moves
        self.passes = (1 - y == c) & (z == 2 - y)
        partner = partner_of(y, c, z, x)
        comes_by = ((partner[0] == partner[1]) & (partner[2] == 1 + partner[0])).astype(jnp.int32)
        self.sender = (flip(partner[0], comes_by), partner[1], partner[2], x) if detour else partner
        self.across_y = across_y
        target = partner_of(*across_y)
        self.direct, self.keep, self.out, self.onward = [], [], [], []
        for h, source in enumerate(sources):
            self.direct.append(remote(source, dst(h, partner), send.at[h], recv.at[h], partner))
            self.keep.append(pltpu.make_async_copy(source, dst(h, (y, c, z, x)), recv.at[h]))
            self.out.append(remote(source, held.at[h], send.at[h], held_recv.at[h], across_y))
            self.onward.append(remote(held.at[h], dst(h, target), pass_send.at[h], recv.at[h], target))

    def greet(self, barrier, neighbours_greet):
        @pl.when(self.moves)
        def _():
            pl.semaphore_signal(barrier, inc=1, device_id=self.sender, device_id_type=MESH_ID)

        count = self.straight.astype(jnp.int32)
        if not self.detour:
            return count
        count = count + self.passes.astype(jnp.int32)
        if not neighbours_greet:

            @pl.when(self.passes)
            def _():
                pl.semaphore_signal(barrier, inc=1, device_id=self.across_y, device_id_type=MESH_ID)

            count = count + self.away.astype(jnp.int32)
        return count

    def start(self, h):
        @pl.when(self.straight)
        def _():
            self.direct[h].start()

        if self.detour:

            @pl.when(self.away)
            def _():
                self.out[h].start()

        @pl.when(jnp.logical_not(self.moves))
        def _():
            self.keep[h].start()

    def wait_sent(self, h):
        @pl.when(self.straight)
        def _():
            self.direct[h].wait_send()

        if self.detour:

            @pl.when(self.away)
            def _():
                self.out[h].wait_send()

    def forward(self, h):
        if self.detour:

            @pl.when(self.passes)
            def _():
                self.out[h].wait_recv()
                self.onward[h].start()

    def arrive(self, h):
        @pl.when(self.moves)
        def _():
            self.direct[h].wait_recv()

        @pl.when(jnp.logical_not(self.moves))
        def _():
            self.keep[h].wait()

    def finish(self, first=0):
        for h in range(len(self.direct)):
            if h >= first:
                self.wait_sent(h)

            if self.detour:

                @pl.when(self.passes)
                def _():
                    self.onward[h].wait_send()


def trade_scratch(pieces, rows, width):
    return [pltpu.VMEM((pieces, rows, width), LOW)] + [pltpu.SemaphoreType.DMA((pieces,)) for _ in range(4)]


class Chain:
    def __init__(self, own, slab, sems, index):
        self.own, self.slab, self.sems, self.index = own, slab, sems, index
        self.last = lax.axis_size("z") - 1

    def move(self, which, h, source, layer, to):
        y, c, z, x = spot()
        return remote(
            source, self.slab(layer), self.sems[2 * which].at[self.index, h], self.sems[2 * which + 1].at[self.index, h], (y, c, to, x)
        )

    def up(self, h):
        z = lax.axis_index("z")
        return self.move(0, h, self.own if h == 0 else self.slab(z - h), z - h, z + 1)

    def down(self, h):
        z = lax.axis_index("z")
        return self.move(1, h, self.own if h == 0 else self.slab(z + h), z + h, z - 1)

    def start(self):
        z = lax.axis_index("z")

        @pl.when(z < self.last)
        def _():
            self.up(0).start()

        @pl.when(z > 0)
        def _():
            self.down(0).start()

    def arrive(self, h):
        z = lax.axis_index("z")

        @pl.when(z - h - 1 >= 0)
        def _():
            self.move(0, h, self.slab(z - h - 1), z - h - 1, z).wait_recv()
            if h < 2:

                @pl.when(z < self.last)
                def _():
                    self.up(h + 1).start()

        @pl.when(z + h + 1 <= self.last)
        def _():
            self.move(1, h, self.slab(z + h + 1), z + h + 1, z).wait_recv()
            if h < 2:

                @pl.when(z > 0)
                def _():
                    self.down(h + 1).start()

    def finish(self):
        z = lax.axis_index("z")
        for h in range(3):

            @pl.when((z < self.last) & (z - h >= 0))
            def _():
                self.up(h).wait_send()

            @pl.when((z > 0) & (z + h <= self.last))
            def _():
                self.down(h).wait_send()


def chain_sems(count):
    return [pltpu.SemaphoreType.DMA((count, 3)) for _ in range(4)]


def greet_neighbours(peers):
    y, c, z, x = spot()
    last = lax.axis_size("z") - 1
    barrier = pltpu.get_barrier_semaphore()
    for peer in peers:
        pl.semaphore_signal(barrier, inc=1, device_id=peer, device_id_type=MESH_ID)

    @pl.when(z > 0)
    def _():
        pl.semaphore_signal(barrier, inc=1, device_id=(y, c, z - 1, x), device_id_type=MESH_ID)

    @pl.when(z < last)
    def _():
        pl.semaphore_signal(barrier, inc=1, device_id=(y, c, z + 1, x), device_id_type=MESH_ID)

    return barrier, len(peers) + (z > 0).astype(jnp.int32) + (z < last).astype(jnp.int32)


def others():
    y, c, z, x = spot()
    return [(flip(y, dy), flip(c, dc), z, flip(x, dx)) for dy in (0, 1) for dc in (0, 1) for dx in (0, 1) if dy + dc + dx]


def line_of():
    y, c, z, x = spot()
    return [(y, c, lax.rem(z + dz, 4), x) for dz in (1, 2, 3)]


class Fold:
    def __init__(self, slab, far, near_part, cross, mine, theirs, send, recv, local):
        y, c, z, x = spot()
        a, b = z // 2, lax.rem(z, 2)
        pair, middle = (y, c, 2 * a + 1 - b, x), (y, c, 2 * (1 - a) + b, x)
        self.far = remote(slab(2 * (1 - a) + 1 - b), far, send.at[0], recv.at[0], pair)
        self.near = remote(slab(2 * a + 1 - b), near_part, send.at[1], recv.at[1], pair)
        self.cross = remote(mine, cross, send.at[2], recv.at[2], middle)
        self.fetches = [
            pltpu.make_async_copy(slab(2 * (1 - a) + b), mine, local.at[0]),
            pltpu.make_async_copy(far, theirs, local.at[1]),
        ]
        self.mine, self.theirs = mine, theirs

    def start(self):
        self.far.start()
        self.fetches[0].start()

    def fold(self):
        self.far.wait_recv()
        self.fetches[1].start()
        for copy in self.fetches:
            copy.wait()
        add_rows(self.mine, 0, self.theirs, 0, self.mine.shape[0])
        self.cross.start()
        self.near.start()

    def finish(self):
        for copy in (self.near, self.cross):
            copy.wait_recv()
        for copy in (self.far, self.near, self.cross):
            copy.wait_send()


def columns_of_layer(whole):
    size = whole.shape[1] // 4
    return lambda at: whole.at[:, pl.ds(pl.multiple_of(at * size, size), size)]


def fold_peers():
    y, c, z, x = spot()
    a, b = z // 2, lax.rem(z, 2)
    return ((y, c, 2 * a + 1 - b, x), (y, c, 2 * (1 - a) + b, x))


def add_rows(total, first, term, start, count):
    def step(i, carry):
        here = pl.ds(pl.multiple_of(first + i * CHUNK, CHUNK), CHUNK)
        there = pl.ds(pl.multiple_of(start + i * CHUNK, CHUNK), CHUNK)
        total[here, :] = (total[here, :].astype(jnp.float32) + term[there, :].astype(jnp.float32)).astype(LOW)
        return carry

    lax.fori_loop(0, count // CHUNK, step, 0)


def scatter_scratch(width, parts=1):
    return [
        pltpu.VMEM((2, TILE, width), LOW),
        pltpu.VMEM((4, TILE, width), LOW),
        pltpu.VMEM((4, TILE, width), LOW),
        pltpu.VMEM((2, HALF, width), LOW),
        pltpu.VMEM((2, TILE, width), LOW),
        pltpu.SemaphoreType.DMA((parts, 10)),
        pltpu.SemaphoreType.DMA((parts, 10)),
    ]


class Scatter:
    def __init__(self, produce, staged, core_part, total, relayed, landed, send, recv, part=0, start=0, size=TILE):
        across_x, across_y, core = near()
        self.produce, self.staged, self.core_part, self.total, self.relayed = produce, staged, core_part, total, relayed
        self.start, self.size, self.half = start, size, size // 2
        send, recv = send.at[part], recv.at[part]
        rows = pl.ds(start, size)
        halves = (pl.ds(start, self.half), pl.ds(start + self.half, self.half))
        self.relay_row = start // 2
        passing = pl.ds(self.relay_row, self.half)
        self.to_core = [
            remote(staged.at[k % 2, rows], core_part.at[k, rows], send.at[k], recv.at[k], core) for k in range(4)
        ]
        self.far_x = remote(total.at[0, halves[0]], relayed.at[0, passing], send.at[4], recv.at[4], across_x)
        self.far_y = remote(total.at[0, halves[1]], relayed.at[1, passing], send.at[5], recv.at[5], across_y)
        self.to_x = [
            remote(total.at[1, at], landed.at[0, at], send.at[6 + half], recv.at[6 + half], across_x)
            for half, at in enumerate(halves)
        ]
        self.to_y = [
            remote(total.at[2, at], landed.at[1, at], send.at[8 + half], recv.at[8 + half], across_y)
            for half, at in enumerate(halves)
        ]

    def begin(self):
        y, c, z, x = spot()
        rows = pl.ds(self.start, self.size)
        for k, (to_row, to_column) in enumerate(((1 - y, 1 - x), (y, 1 - x), (1 - y, x), (y, x))):
            if k >= 2:
                self.to_core[k - 2].wait_send()
            self.produce(2 * k, to_row, 1 - c, to_column, self.staged.at[k % 2, rows])
            self.to_core[k].start()
            self.produce(2 * k + 1, to_row, c, to_column, self.total.at[k, rows])
            self.to_core[k].wait_recv()
            add_rows(self.total.at[k], self.start, self.core_part.at[k], self.start, self.size)
            if k == 0:
                self.far_x.start()
                self.far_y.start()
            if k == 1:
                self.to_x[0].start()
            if k == 2:
                self.to_y[1].start()

    def relay(self):
        self.far_y.wait_recv()
        add_rows(self.total.at[1], self.start + self.half, self.relayed.at[1], self.relay_row, self.half)
        self.to_x[1].start()
        self.far_x.wait_recv()
        add_rows(self.total.at[2], self.start, self.relayed.at[0], self.relay_row, self.half)
        self.to_y[0].start()

    def arrive(self):
        for copy in self.to_x + self.to_y:
            copy.wait_recv()

    def finish(self):
        for copy in self.to_core[2:] + [self.far_x, self.far_y] + self.to_x + self.to_y:
            copy.wait_send()


def sum_and_gather(part_of, rows_of_half, gather, beside):
    sums = [part_of(half) for half in (0, 1)]
    sums[0].begin()
    sums[0].relay()
    sums[1].begin()
    sums[0].arrive()
    rows_of_half(0)
    gather.start(0)
    beside(0)
    sums[1].relay()
    beside(1)
    sums[1].arrive()
    rows_of_half(1)
    gather.start(1)
    gather.pass_near(0)
    beside(2)
    gather.pass_near(1)
    gather.pass_far(0)
    gather.pass_far(1)
    gather.finish()
    beside(3)
    for half in (0, 1):
        sums[half].finish()


def begin_kernel(
    x_own, w_query, w_key, w_value, facts, x_whole, w_qkv, facts_whole,
    gather_send, gather_recv, w_send, w_recv, fact_send, fact_recv, local, *scratch
):
    y, c, z, x = spot()
    row = 2 * y + c
    layer = others()
    trade_parts, sems = scratch[:5], scratch[5:]
    trade = Trade(
        [x_own.at[half] for half in (0, 1)], lambda half, at: x_whole.at[place_of(at[0], at[1], at[3], half)], *trade_parts, detour=False
    )
    barrier, count = greet_neighbours(layer)
    pl.semaphore_wait(barrier, count + trade.greet(barrier, True))

    shard = w_query.shape[0]
    for half in (0, 1):
        trade.start(half)
    spread = [
        remote(facts, facts_whole.at[row, z, x], fact_send.at[k], fact_recv.at[k], peer) for k, peer in enumerate(layer)
    ]
    kept = [pltpu.make_async_copy(facts, facts_whole.at[row, z, x], local.at[6])]
    for m in range(6):
        source, slot = (w_query, w_key, w_value)[m // 2], m % 2

        def columns_of(at):
            head = 4 * (2 * at[0] + at[1]) + (3 - at[3] if slot else at[3])
            return source.at[:, pl.ds(pl.multiple_of(head * HD, HD), HD)]

        dst = w_qkv.at[row, z, pl.ds(pl.multiple_of(x * shard, shard), shard), pl.ds(m * HD, HD)]
        for k, peer in enumerate(layer):
            spread.append(remote(columns_of(peer), dst, w_send.at[m, k], w_recv.at[m, k], peer))
        kept.append(pltpu.make_async_copy(columns_of((y, c, z, x)), dst, local.at[m]))
    for copy in spread + kept:
        copy.start()

    gather = GatherWhole(lambda half: x_whole.at[place_of(y, c, x, half)], x_whole, gather_send, gather_recv)
    for half in (0, 1):
        trade.forward(half)
        trade.arrive(half)
        gather.start(half)

    for copy in kept:
        copy.wait()
    for copy in spread:
        copy.wait_recv()
    chains = [
        Chain(facts_whole.at[:, z], lambda at: facts_whole.at[:, at], sems, 0),
        Chain(w_qkv.at[:, z], lambda at: w_qkv.at[:, at], sems, 1),
    ]

    def arrive(h):
        for chain in chains:
            chain.arrive(h)

    for chain in chains:
        chain.start()
    gather.pass_first()
    arrive(0)
    gather.pass_second()
    arrive(1)
    gather.pass_far()
    arrive(2)
    gather.finish()
    trade.finish()
    for copy in spread:
        copy.wait_send()
    for chain in chains:
        chain.finish()


def anywhere():
    return pl.BlockSpec(memory_space=pl.ANY)


def in_vmem():
    return pl.BlockSpec(memory_space=pltpu.VMEM)


def dma(*shape):
    return pltpu.SemaphoreType.DMA(shape)


def remote_params(number):
    return pltpu.CompilerParams(collective_id=number, has_side_effects=True, vmem_limit_bytes=VMEM_LIMIT)


def begin(x_own, w_query, w_key, w_value, facts):
    block, width = x_own.shape
    shard = w_query.shape[0]
    x_whole, w_qkv, facts_whole = pl.pallas_call(
        begin_kernel,
        out_shape=(
            jax.ShapeDtypeStruct((8 * block, width), LOW),
            jax.ShapeDtypeStruct((4, 4, 2 * shard, 3 * width // 8), LOW),
            jax.ShapeDtypeStruct((4, 4, 2, *facts.shape), jnp.float32),
        ),
        in_specs=[in_vmem()] + [anywhere()] * 4,
        out_specs=[anywhere()] * 3,
        scratch_shapes=[
            dma(GATHER_COPIES), dma(GATHER_COPIES), dma(6, 7), dma(6, 7), dma(7), dma(7), dma(7),
            *trade_scratch(2, block // 2, width), *chain_sems(2),
        ],
        compiler_params=remote_params(1),
        cost_estimate=pl.CostEstimate(flops=0, bytes_accessed=350_000_000, transcendentals=0),
    )(x_own.reshape(2, block // 2, width), w_query, w_key, w_value, facts)
    return x_whole, w_qkv.reshape(width, 3 * width // 8), facts_whole


def summed(total, landed, here):
    parts = (total[3, here, :], landed[0, here, :], landed[1, here, :])
    return sum(part.astype(jnp.float32) for part in parts)


def over_chunks(work, half):
    def step(i, carry):
        work(pl.ds(pl.multiple_of(half * HALF + i * CHUNK, CHUNK), CHUNK))
        return carry

    lax.fori_loop(0, HALF // CHUNK, step, 0)


def own_halves(own):
    return lambda half: own.at[pl.ds(half * HALF, HALF)]


def inverse_of(value):
    return lax.rsqrt(jnp.mean(value * value, axis=-1, keepdims=True) + EPSILON)


def close_attention_kernel(attended, w_out, x_whole, gain, w_gate, w_up, resid, normed, own_gate, own_up, own, x_own, *scratch):
    scatter, (send, recv, local), sems = scratch[:7], scratch[7:10], scratch[10:]
    y, c, z, x = spot()
    fetch_x = pltpu.make_async_copy(x_whole.at[place_of(y, c, x)], x_own, local.at[0])
    fetch_x.start()
    width = w_out.shape[1]
    hidden = w_gate.shape[1]
    z = lax.axis_index("z")
    barrier, count = greet_neighbours(near())
    pl.semaphore_wait(barrier, count)

    def slab_of(whole):
        return lambda at: whole.at[:, pl.ds(pl.multiple_of(at * hidden, hidden), hidden)]

    chains, kept = [], []
    for k, (part, whole) in enumerate(((w_gate, own_gate), (w_up, own_up))):
        chains.append(Chain(part, slab_of(whole), sems, k))
        chains[k].start()
        kept.append(pltpu.make_async_copy(part, slab_of(whole)(z), local.at[1 + k]))
        kept[k].start()

    def arrive(h):
        for chain in chains:
            chain.arrive(h)

    def part_of(half):
        def produce(turn, y, c, x, out):
            at = place_of(y, c, x, half)

            def step(i, carry):
                columns = pl.ds(pl.multiple_of(i * TILE, TILE), TILE)
                out[:, columns] = dot_wide(attended[at, :], w_out[:, columns]).astype(LOW)
                return carry

            lax.fori_loop(0, width // TILE, step, 0)

        return Scatter(produce, *scatter, part=half, start=half * HALF, size=HALF)

    total, landed = scatter[2], scatter[4]

    def chunk(here):
        value = x_own[here, :].astype(jnp.float32) + summed(total, landed, here)
        resid[here, :] = value
        own[here, :] = (value * inverse_of(value) * gain[...]).astype(LOW)

    def rows_of_half(half):
        if half == 0:
            fetch_x.wait()
        over_chunks(chunk, half)

    gather = Gather(own_halves(own), normed, send, recv)
    sum_and_gather(part_of, rows_of_half, gather, lambda turn: arrive((0, None, 1, 2)[turn]) if turn != 1 else None)
    keep = pltpu.make_async_copy(own, normed.at[place_of(y, c, x)], local.at[0])
    keep.start()
    for chain in chains:
        chain.finish()
    for copy in kept + [keep]:
        copy.wait()


def close_attention(attended, w_out, x_whole, gain, w_gate, w_up):
    block, width = x_whole.shape[0] // 8, x_whole.shape[1]
    hidden = w_gate.shape[1]
    return pl.pallas_call(
        close_attention_kernel,
        out_shape=(
            jax.ShapeDtypeStruct((block, width), jnp.float32),
            jax.ShapeDtypeStruct((8 * block, width), LOW),
            jax.ShapeDtypeStruct((width, 4 * hidden), LOW),
            jax.ShapeDtypeStruct((width, 4 * hidden), LOW),
        ),
        in_specs=[in_vmem(), in_vmem(), anywhere()] + [in_vmem()] * 3,
        out_specs=[in_vmem()] + [anywhere()] * 3,
        scratch_shapes=[pltpu.VMEM((block, width), LOW)] * 2
        + scatter_scratch(width, 2)
        + [dma(GATHER_COPIES), dma(GATHER_COPIES), dma(3), *chain_sems(2)],
        compiler_params=remote_params(2),
        cost_estimate=pl.CostEstimate(flops=0, bytes_accessed=450_000_000, transcendentals=0),
    )(attended, w_out, x_whole, gain, w_gate, w_up)


def norm_back(value, gain, upstream):
    inverse = inverse_of(value)
    scaled = upstream * gain
    inner = jnp.mean(scaled * value, axis=-1, keepdims=True)
    return inverse * scaled - value * (inverse * inverse * inverse) * inner, upstream * value * inverse


def fold_rows(total, terms):
    for first in range(0, CHUNK, 8):
        total[...] += terms[first : first + 8, :]


def close_mlp_kernel(
    d_gate, d_up, w_gate, w_up, resid_home, upstream_home, gain, grad_a, grad_b, d_resid, gain_term, d_resid_whole,
    far_a, near_a, cross_a, far_b, near_b, cross_b, own, blocks, *scratch
):
    scatter, (send, recv, local, fetched, fold_send, fold_recv, fold_local, mine, theirs, resid, upstream, row_sems) = scratch[:7], scratch[7:]
    rows_fetched = [
        pltpu.make_async_copy(source, target, row_sems.at[k])
        for k, (source, target) in enumerate(((resid_home, resid), (upstream_home, upstream)))
    ]
    y, c, z, x = spot()
    width = w_gate.shape[0]
    order = [
        place_of(r, k, q, half)
        for half in (0, 1)
        for r, q in ((1 - y, 1 - x), (y, 1 - x), (1 - y, x), (y, x))
        for k in (1 - c, c)
    ]

    def fetch(turn):
        slot = turn % 2
        return [
            pltpu.make_async_copy(source.at[order[turn]], blocks.at[slot, m], fetched.at[slot, m])
            for m, source in enumerate((d_gate, d_up))
        ]

    for copy in fetch(0) + rows_fetched:
        copy.start()
    greet(near() + fold_peers())
    folds = [
        Fold(columns_of_layer(grad), *refs, mine.at[k], theirs, fold_send.at[k], fold_recv.at[k], fold_local.at[k])
        for k, (grad, *refs) in enumerate(((grad_a, far_a, near_a, cross_a), (grad_b, far_b, near_b, cross_b)))
    ]
    for fold in folds:
        fold.start()

    def part_of(half):
        def produce(turn, to_y, to_c, to_x, out):
            turn = turn + 8 * half
            if turn < 15:
                for copy in fetch(turn + 1):
                    copy.start()
            for copy in fetch(turn):
                copy.wait()

            def step(i, carry):
                columns = pl.ds(pl.multiple_of(i * TILE, TILE), TILE)
                part = dot_nt(blocks[turn % 2, 0], w_gate[columns, :]) + dot_nt(blocks[turn % 2, 1], w_up[columns, :])
                out[:, columns] = part.astype(LOW)
                return carry

            lax.fori_loop(0, width // TILE, step, 0)

        return Scatter(produce, *scatter, part=half, start=half * HALF, size=HALF)

    total, landed = scatter[2], scatter[4]
    gain_term[...] = jnp.zeros_like(gain_term)

    def chunk(here):
        back, terms = norm_back(resid[here, :], gain[...], summed(total, landed, here))
        value = upstream[here, :].astype(jnp.float32) + back
        d_resid[here, :] = value
        own[here, :] = value.astype(LOW)
        fold_rows(gain_term, terms)

    def rows_of_half(half):
        if half == 0:
            for copy in rows_fetched:
                copy.wait()
        over_chunks(chunk, half)

    gather = Gather(own_halves(own), d_resid_whole, send, recv)
    sum_and_gather(part_of, rows_of_half, gather, lambda turn: folds[turn].fold() if turn < 2 else None)
    keep = pltpu.make_async_copy(own, d_resid_whole.at[place_of(y, c, x)], local.at[0])
    keep.start()
    for fold in folds:
        fold.finish()
    keep.wait()


def close_mlp(d_gate, d_up, w_gate, w_up, resid, upstream, gain, *grads):
    block, width = resid.shape
    hidden = d_gate.shape[1]
    return pl.pallas_call(
        close_mlp_kernel,
        out_shape=(
            jax.ShapeDtypeStruct((block, width), jnp.float32),
            jax.ShapeDtypeStruct((8, width), jnp.float32),
            jax.ShapeDtypeStruct((8 * block, width), LOW),
            *[jax.ShapeDtypeStruct((width, hidden // 4), LOW)] * 6,
        ),
        in_specs=[anywhere()] * 2 + [in_vmem()] * 2 + [anywhere()] * 2 + [in_vmem()] + [anywhere()] * 2,
        out_specs=[in_vmem(), in_vmem()] + [anywhere()] * 7,
        scratch_shapes=[pltpu.VMEM((block, width), LOW), pltpu.VMEM((2, 2, block // 2, hidden), LOW)]
        + scatter_scratch(width, 2)
        + [dma(GATHER_COPIES), dma(GATHER_COPIES), dma(1), dma(2, 2), dma(2, 3), dma(2, 3), dma(2, 2)]
        + [pltpu.VMEM((2, width, hidden // 4), LOW), pltpu.VMEM((width, hidden // 4), LOW)]
        + [pltpu.VMEM((block, width), jnp.float32), pltpu.VMEM((block, width), LOW), dma(2)],
        compiler_params=remote_params(3),
        cost_estimate=pl.CostEstimate(flops=0, bytes_accessed=450_000_000, transcendentals=0),
    )(d_gate, d_up, w_gate, w_up, resid, upstream, gain, *grads)


def close_layer_kernel(
    d_qkv, w_qkv, x_whole, d_resid_home, gain, mlp_term, grad, grad_low, gain_grads, far, near_part, cross, grad_parts, own, terms, layer_terms, part, column_terms, *scratch
):
    scatter, (send, recv, term_send, term_recv, line_send, line_recv, x_own, x_sem, *rest) = scratch[:7], scratch[7:]
    mine, theirs, fold_send, fold_recv, fold_local, part_send, part_recv, d_resid = rest
    fetch_d_resid = pltpu.make_async_copy(d_resid_home, d_resid, x_sem.at[1])
    fetch_d_resid.start()
    y, c, z, x = spot()
    fetch_x = pltpu.make_async_copy(x_whole.at[place_of(y, c, x)], x_own, x_sem.at[0])
    fetch_x.start()
    partner = partner_of(y, c, z, x)
    moves = z != 2 * c + y
    width = w_qkv.shape[0]
    barrier = pltpu.get_barrier_semaphore()

    @pl.when(moves)
    def _():
        pl.semaphore_signal(barrier, inc=1, device_id=partner, device_id_type=MESH_ID)

    layer = others()
    line = line_of()
    for peer in layer + line:
        pl.semaphore_signal(barrier, inc=1, device_id=peer, device_id_type=MESH_ID)
    pl.semaphore_wait(barrier, len(layer + line) + moves.astype(jnp.int32))

    size = TILE // PIECES

    def part_of(piece):
        def produce(turn, to_y, to_c, to_x, out):
            at = quarter_of(to_y, to_c, to_x, piece // 2, piece % 2)

            def step(i, carry):
                columns = pl.ds(pl.multiple_of(i * TILE, TILE), TILE)
                out[:, columns] = dot_nt(d_qkv[at, :], w_qkv[columns, :]).astype(LOW)
                return carry

            lax.fori_loop(0, width // TILE, step, 0)

        return Scatter(produce, *scatter, part=piece, start=piece * size, size=size)

    fold = Fold(lambda at: grad.at[at], far, near_part, cross, mine, theirs, fold_send, fold_recv, fold_local)
    fold.start()
    def end_fold():
        fold.finish()
        for source, target, k in ((grad.at[z], mine, 0), (near_part, theirs, 1)):
            pltpu.make_async_copy(source, target, fold_local.at[k]).start()
        for source, target, k in ((grad.at[z], mine, 0), (near_part, theirs, 1)):
            pltpu.make_async_copy(source, target, fold_local.at[k]).wait()
        add_rows(mine, 0, theirs, 0, mine.shape[0])
        last = pltpu.make_async_copy(cross, theirs, fold_local.at[1])
        last.start()
        last.wait()
        add_rows(mine, 0, theirs, 0, mine.shape[0])
        shard = mine.shape[0] // 8
        index = 4 * y + 2 * c + x
        parts = [
            remote(
                mine.at[pl.ds(pl.multiple_of((4 * peer[0] + 2 * peer[1] + peer[3]) * shard, shard), shard)],
                grad_parts.at[index],
                part_send.at[k],
                part_recv.at[k],
                peer,
            )
            for k, peer in enumerate(layer)
        ]
        kept = pltpu.make_async_copy(mine.at[pl.ds(pl.multiple_of(index * shard, shard), shard)], grad_parts.at[index], fold_local.at[0])
        for copy in parts + [kept]:
            copy.start()
        return parts + [kept]

    sums = [part_of(piece) for piece in range(PIECES)]
    sums[0].begin()
    sums[0].relay()
    sums[1].begin()
    fold.fold()
    total, landed = scatter[2], scatter[4]
    terms[1] = mlp_term[...]
    terms[0] = jnp.zeros_like(mlp_term)
    pieces = [pl.ds(piece * size, size) for piece in range(PIECES)]
    trades = [remote(own.at[at], grad_low.at[at], send.at[k], recv.at[k], partner) for k, at in enumerate(pieces)]
    keeps = [pltpu.make_async_copy(own.at[at], grad_low.at[at], recv.at[k]) for k, at in enumerate(pieces)]
    fetch_x.wait()
    fetch_d_resid.wait()
    to_peers = []
    for piece in range(PIECES):
        if piece == PIECES - 1:
            to_peers = end_fold()
        sums[piece].arrive()

        def step(i, carry):
            here = pl.ds(pl.multiple_of(piece * size + i * CHUNK, CHUNK), CHUNK)
            back, products = norm_back(x_own[here, :].astype(jnp.float32), gain[...], summed(total, landed, here))
            own[here, :] = (d_resid[here, :] + back).astype(LOW)
            fold_rows(terms.at[0], products)
            return carry

        lax.fori_loop(0, size // CHUNK, step, 0)

        @pl.when(moves)
        def _():
            trades[piece].start()

        @pl.when(jnp.logical_not(moves))
        def _():
            keeps[piece].start()

        if piece + 1 < PIECES:
            sums[piece + 1].relay()
        if piece + 2 < PIECES:
            sums[piece + 2].begin()

    def columns_of(row, layers):
        return pl.ds(pl.multiple_of((4 * row) * HD, HD), layers * HD)

    spread = [
        remote(terms.at[:, :, columns_of(2 * peer[0] + peer[1], 4)], layer_terms.at[k], term_send.at[k], term_recv.at[k], peer)
        for k, peer in enumerate(layer)
    ]
    for copy in spread:
        copy.start()
    for copy in spread:
        copy.wait_recv()
    part[...] = sum((layer_terms[k] for k in range(7)), terms[:, :, columns_of(2 * y + c, 4)])
    lines = [
        remote(
            part.at[:, :, pl.ds(pl.multiple_of(peer[2] * HD, HD), HD)], column_terms.at[k], line_send.at[k], line_recv.at[k], peer
        )
        for k, peer in enumerate(line)
    ]
    for copy in lines:
        copy.start()
    for copy in lines:
        copy.wait_recv()
    gain_grads[...] = sum((column_terms[k] for k in range(3)), part[:, :, pl.ds(pl.multiple_of(z * HD, HD), HD)])
    for copy in spread + lines:
        copy.wait_send()
    for part_sum in sums:
        part_sum.finish()
    for copy in to_peers:
        copy.wait()

    @pl.when(moves)
    def _():
        for copy in trades:
            copy.wait()

    @pl.when(jnp.logical_not(moves))
    def _():
        for copy in keeps:
            copy.wait()


def close_layer(d_qkv, w_qkv, x_whole, d_resid, gain, mlp_term, grad):
    block, width = d_resid.shape
    return pl.pallas_call(
        close_layer_kernel,
        out_shape=(
            jax.ShapeDtypeStruct((block, width), LOW),
            jax.ShapeDtypeStruct((2, 8, width // 16), jnp.float32),
            *[jax.ShapeDtypeStruct(grad.shape[1:], LOW)] * 3,
            jax.ShapeDtypeStruct((8, grad.shape[1] // 8, grad.shape[2]), LOW),
        ),
        in_specs=[in_vmem(), in_vmem(), anywhere(), anywhere(), in_vmem(), in_vmem(), anywhere()],
        out_specs=[anywhere(), in_vmem()] + [anywhere()] * 4,
        scratch_shapes=[
            pltpu.VMEM((block, width), LOW),
            pltpu.VMEM((2, 8, width), jnp.float32),
            pltpu.VMEM((7, 2, 8, width // 4), jnp.float32),
            pltpu.VMEM((2, 8, width // 4), jnp.float32),
            pltpu.VMEM((3, 2, 8, width // 16), jnp.float32),
        ]
        + scatter_scratch(width, PIECES)
        + [dma(PIECES), dma(PIECES), dma(7), dma(7), dma(3), dma(3), pltpu.VMEM((block, width), LOW), dma(2)]
        + [pltpu.VMEM(grad.shape[1:], LOW)] * 2
        + [dma(3), dma(3), dma(2), dma(7), dma(7), pltpu.VMEM((block, width), jnp.float32)],
        compiler_params=remote_params(4),
        cost_estimate=pl.CostEstimate(flops=0, bytes_accessed=350_000_000, transcendentals=0),
    )(d_qkv, w_qkv, x_whole, d_resid, gain, mlp_term, grad)


def doc_start(ends, place):
    start = jnp.zeros_like(place)
    for k in range(8):
        start = jnp.where(ends[k] <= place, ends[k], start)
    return jnp.where(place < ends[7], start, LEN)


def sigmoid_of(raw):
    return pl.reciprocal(1.0 + jnp.exp2(math.log2(LEN) - raw * (math.log2(math.e) / math.sqrt(HD))), approx=True)


def tile_at(index):
    return pl.ds(pl.multiple_of(index * TILE, TILE), TILE)


def head_of(array, rows, part, head):
    first = (part * (array.shape[1] // 3) // HD + head) * HD
    return array[rows, first : first + HD]


def attend_kernel(ends, qkv, out, total):
    i = pl.program_id(0)
    heads = qkv.shape[1] // (3 * HD)
    total[...] = jnp.zeros_like(total)
    q_place = i * TILE + lax.broadcasted_iota(jnp.int32, (TILE, 1), 0)
    q_start = doc_start(ends, q_place)

    def tile(j, diagonal):
        k_place = j * TILE + lax.broadcasted_iota(jnp.int32, (1, TILE), 1)
        allowed = k_place >= q_start
        if diagonal:
            allowed = allowed & (k_place <= q_place)
        for head in range(heads):
            raw = dot_nt(head_of(qkv, tile_at(i), 0, head), head_of(qkv, tile_at(j), 1, head))
            weight = jnp.where(allowed, sigmoid_of(raw), 0.0).astype(LOW)
            total[head] += dot_wide(weight, head_of(qkv, tile_at(j), 2, head))

    def step(j, carry):
        tile(j, False)
        return carry

    lax.fori_loop(0, i, step, 0)
    tile(i, True)
    for head in range(heads):
        out[tile_at(i), head * HD : (head + 1) * HD] = total[head].astype(LOW)


def open_mlp_kernel(normed, w_gate, w_up, upstream, gate, up, hidden, upstream_whole, send, recv, local):
    i = pl.program_id(0)
    y, c, z, x = spot()
    steps = pl.num_programs(0)
    gather = Gather(lambda half: upstream.at[pl.ds(half * HALF, HALF)], upstream_whole, send, recv)
    keep = pltpu.make_async_copy(upstream, upstream_whole.at[place_of(y, c, x)], local.at[0])

    @pl.when(i == 0)
    def _():
        greet(near())
        gather.start(0)
        gather.start(1)
        keep.start()

    def step(n, carry):
        columns = pl.ds(pl.multiple_of(n * TILE, TILE), TILE)
        gate_part, up_part = dot_wide(normed[...], w_gate[:, columns]), dot_wide(normed[...], w_up[:, columns])
        gate[:, columns] = gate_part
        up[:, columns] = up_part
        hidden[:, columns] = (gate_part * jax.nn.sigmoid(gate_part) * up_part).astype(LOW)
        return carry

    lax.fori_loop(0, w_gate.shape[1] // TILE, step, 0)

    @pl.when(i == steps - 1)
    def _():
        for half in (0, 1):
            gather.pass_near(half)
        for half in (0, 1):
            gather.pass_far(half)
        gather.finish()
        keep.wait()


def open_mlp(normed, w_gate, w_up, upstream):
    places, width = normed.shape
    hidden = w_gate.shape[1]
    rows = lambda columns: pl.BlockSpec((TILE, columns), lambda i: (i, 0))
    whole = lambda array: pl.BlockSpec(array.shape, lambda i: (0, 0))
    return pl.pallas_call(
        open_mlp_kernel,
        out_shape=(
            jax.ShapeDtypeStruct((places, hidden), jnp.float32),
            jax.ShapeDtypeStruct((places, hidden), jnp.float32),
            jax.ShapeDtypeStruct((places, hidden), LOW),
            jax.ShapeDtypeStruct((places, width), LOW),
        ),
        grid=(places // TILE,),
        in_specs=[rows(width), whole(w_gate), whole(w_up), whole(upstream)],
        out_specs=[rows(hidden), rows(hidden), rows(hidden), anywhere()],
        scratch_shapes=[dma(GATHER_COPIES), dma(GATHER_COPIES), dma(1)],
        compiler_params=remote_params(5),
        cost_estimate=pl.CostEstimate(flops=0, bytes_accessed=250_000_000, transcendentals=0),
    )(normed, w_gate, w_up, upstream)


def out_turns():
    y, c, z, x = spot()
    layers = (x, x, 3 - x, 3 - x)
    owners = [((y, c, layers[j], j % 2), (z == layers[j]) & (x == j % 2)) for j in range(4)]
    side = lax.rem((z + 1) // 2, 2)
    holders = [((y, c, j, side), (z == j) & (x == side)) for j in range(4)]
    return owners, holders


def attend_back_kernel(
    ends, qkv, grads, out_grad, mixed, out, out_parts, mixed_home, query_total, key_total, value_total, send, recv, *trade_parts
):
    j = pl.program_id(0)
    y, c, z, x = spot()
    heads = qkv.shape[1] // (3 * HD)
    shard = out_grad.shape[0] // 4
    owners, holders = out_turns()
    trade = Trade(
        [mixed.at[pl.ds(half * HALF, HALF)] for half in (0, 1)], lambda half, at: mixed_home.at[pl.ds(half * HALF, HALF)], *trade_parts
    )

    def to_owner(turn):
        return remote(out_grad.at[pl.ds(turn * shard, shard)], out_parts.at[z], send.at[turn], recv.at[z], owners[turn][0])

    def to_self(turn):
        return pltpu.make_async_copy(out_grad.at[pl.ds(turn * shard, shard)], out_parts.at[z], recv.at[z])

    @pl.when(j == 0)
    def _():
        query_total[...] = jnp.zeros_like(query_total)
        barrier = pltpu.get_barrier_semaphore()
        for peer, here in holders:

            @pl.when(jnp.logical_not(here))
            def _():
                pl.semaphore_signal(barrier, inc=1, device_id=peer, device_id_type=MESH_ID)

        pl.semaphore_wait(barrier, 4 - (x == lax.rem((z + 1) // 2, 2)).astype(jnp.int32) + trade.greet(barrier, False))
        for half in (0, 1):
            trade.start(half)
        for turn in range(4):

            @pl.when(jnp.logical_not(owners[turn][1]))
            def _():
                to_owner(turn).start()

            @pl.when(owners[turn][1])
            def _():
                to_self(turn).start()

    key_total[...] = jnp.zeros_like(key_total)
    value_total[...] = jnp.zeros_like(value_total)
    here = tile_at(j)
    k_place = j * TILE + lax.broadcasted_iota(jnp.int32, (TILE, 1), 0)
    turned = [head_of(qkv, here, 1, head).T for head in range(heads)]

    def tile(i, diagonal):
        q_place = i * TILE + lax.broadcasted_iota(jnp.int32, (1, TILE), 1)
        allowed = k_place >= doc_start(ends, q_place)
        if diagonal:
            allowed = allowed & (k_place <= q_place)
        for head in range(heads):
            query, grad = head_of(qkv, tile_at(i), 0, head), grads[tile_at(i), head * HD : (head + 1) * HD]
            sig = jnp.where(allowed, sigmoid_of(dot_nt(head_of(qkv, here, 1, head), query)), 0.0)
            value_total[head] += dot_wide(sig.astype(LOW), grad)
            d_score = (dot_nt(head_of(qkv, here, 2, head), grad) * (sig * (1.0 - sig))).astype(LOW)
            key_total[head] += dot_wide(d_score, query)
            query_total[head, :, tile_at(i)] += dot_wide(turned[head], d_score)

    def step(i, carry):
        tile(i, False)
        return carry

    tile(j, True)
    lax.fori_loop(j + 1, LEN // TILE, step, 0)
    scale = 1.0 / math.sqrt(HD)
    for head in range(heads):
        first = head * HD
        out[here, heads * HD + first : (heads + 1) * HD + first] = (key_total[head] * scale).astype(LOW)
        out[here, 2 * heads * HD + first : (2 * heads + 1) * HD + first] = value_total[head].astype(LOW)
        out[here, first : first + HD] = (query_total[head, :, here] * scale).T.astype(LOW)

    @pl.when(j == LEN // TILE - 1)
    def _():
        for turn in range(4):

            @pl.when(jnp.logical_not(owners[turn][1]))
            def _():
                to_owner(turn).wait_send()

            @pl.when(jnp.logical_not(holders[turn][1]))
            def _():
                landed = out_parts.at[turn]
                remote(landed, landed, send.at[turn], recv.at[turn], holders[turn][0]).wait_recv()

            @pl.when(owners[turn][1])
            def _():
                to_self(turn).wait()

        for half in (0, 1):
            trade.arrive(half)
        trade.finish()

    @pl.when(j == 1)
    def _():
        for half in (0, 1):
            trade.forward(half)


def back_mlp_kernel(upstream, w_down, gate, up, d_gate, d_up):
    def step(n, carry):
        columns = pl.ds(pl.multiple_of(n * TILE, TILE), TILE)
        d_hidden = dot_nt(upstream[...], w_down[columns, :])
        d_gate[:, columns], d_up[:, columns] = gate_backward(
            d_hidden, gate[:, columns], up[:, columns], jax.nn.sigmoid(gate[:, columns])
        )
        return carry

    lax.fori_loop(0, gate.shape[1] // TILE, step, 0, unroll=2)


def back_mlp(upstream, w_down, gate, up):
    places, width = upstream.shape
    hidden = gate.shape[1]
    rows = lambda size: pl.BlockSpec((TILE, size), lambda i: (i, 0))
    return pl.pallas_call(
        back_mlp_kernel,
        out_shape=(jax.ShapeDtypeStruct((places, hidden), LOW), jax.ShapeDtypeStruct((places, hidden), LOW)),
        grid=(places // TILE,),
        in_specs=[rows(width), pl.BlockSpec(w_down.shape, lambda i: (0, 0)), rows(hidden), rows(hidden)],
        out_specs=[rows(hidden), rows(hidden)],
        compiler_params=pltpu.CompilerParams(vmem_limit_bytes=VMEM_LIMIT),
        cost_estimate=pl.CostEstimate(flops=0, bytes_accessed=90_000_000, transcendentals=0),
    )(upstream, w_down, gate, up)


def attend(ends, qkv):
    places, width = qkv.shape
    heads = width // (3 * HD)
    whole = lambda columns: pl.BlockSpec((places, columns), lambda i: (0, 0))
    return pl.pallas_call(
        attend_kernel,
        out_shape=jax.ShapeDtypeStruct((places, width // 3), LOW),
        grid=(places // TILE,),
        in_specs=[pl.BlockSpec(memory_space=pltpu.SMEM), whole(width)],
        out_specs=whole(width // 3),
        scratch_shapes=[pltpu.VMEM((heads, TILE, HD), jnp.float32)],
        compiler_params=pltpu.CompilerParams(vmem_limit_bytes=VMEM_LIMIT),
        cost_estimate=pl.CostEstimate(flops=0, bytes_accessed=150_000_000, transcendentals=0),
    )(ends, qkv)


def attend_back(ends, qkv, grads, out_grad, mixed):
    places, width = qkv.shape
    heads = width // (3 * HD)
    whole = lambda columns: pl.BlockSpec((places, columns), lambda j: (0, 0))
    return pl.pallas_call(
        attend_back_kernel,
        out_shape=(
            jax.ShapeDtypeStruct((places, width), LOW),
            jax.ShapeDtypeStruct((4, out_grad.shape[0] // 4, out_grad.shape[1]), LOW),
            jax.ShapeDtypeStruct(mixed.shape, LOW),
        ),
        grid=(places // TILE,),
        in_specs=[pl.BlockSpec(memory_space=pltpu.SMEM), whole(width), whole(width // 3), anywhere(), pl.BlockSpec(mixed.shape, lambda j: (0, 0))],
        out_specs=[whole(width), anywhere(), anywhere()],
        scratch_shapes=[
            pltpu.VMEM((heads, HD, places), jnp.float32),
            pltpu.VMEM((heads, TILE, HD), jnp.float32),
            pltpu.VMEM((heads, TILE, HD), jnp.float32),
            dma(4),
            dma(4),
            *trade_scratch(2, HALF, mixed.shape[1]),
        ],
        compiler_params=remote_params(6),
        cost_estimate=pl.CostEstimate(flops=0, bytes_accessed=300_000_000, transcendentals=0),
    )(ends, qkv, grads, out_grad, mixed)


LAYER = ("y", "c", "x")
PLACES = ("c", "y", "x")
ALL = ("y", "c", "z", "x")


def trade(part):
    pairs = []
    for y in range(2):
        for c in range(2):
            for z in range(4):
                for x in range(2):
                    pairs.append((((y * 2 + c) * 4 + z) * 2 + x, (((z % 2) * 2 + z // 2) * 4 + 2 * c + y) * 2 + x))
    return lax.ppermute(part, ALL, pairs)


def after(first, then):
    return lax.optimization_barrier((first, then))[1]


def body_layers(
    tokens, lengths, cotangent, w_query, w_key, w_value, w_out, w_gate, w_up, w_down, gain_attn, gain_mlp
):
    rows_here, block, width = tokens.shape
    members = lax.axis_size(LAYER)
    layers = lax.axis_size("z")
    shard = w_query.shape[0]
    owned = width // members
    facts = jnp.zeros((8, 2 * shard), jnp.float32)
    facts = facts.at[0, :shard].set(gain_attn.astype(jnp.float32)).at[1, :shard].set(gain_mlp.astype(jnp.float32))
    facts = facts.at[2, : lengths.shape[1]].set(lengths[0].astype(jnp.float32))
    layer_x, w_qkv, facts = begin(tokens.reshape(block, width), w_query, w_key, w_value, facts)
    full_gain_attn, full_gain_mlp = facts[:, :, :, 0, :shard].reshape(1, width), facts[:, :, :, 1, :shard].reshape(1, width)
    layer = lax.axis_index("z")
    own_lengths = facts[:, 0, 0, 2, : lengths.shape[1]].reshape(2, 2, -1)
    own_lengths = lax.dynamic_slice(own_lengths, (layer % 2, layer // 2, 0), (1, 1, own_lengths.shape[2]))[0, 0]
    ends = jnp.cumsum(own_lengths.astype(jnp.int32))
    layer_normed = norm_forward(layer_x.astype(jnp.float32), full_gain_attn)[0].astype(LOW)
    here = lax.axis_index("x")
    out_rows = lax.all_gather(after(facts, w_out), ("z", "x"), axis=0, tiled=True)
    w_out_own = [lax.dynamic_slice_in_dim(out_rows, head * HD, HD, 0) for head in (here, 3 - here)]
    w_out_own = jnp.concatenate(w_out_own, axis=0)

    qkv = dot_wide(layer_normed, w_qkv).astype(LOW)
    upstream = trade(after(facts, cotangent)).reshape(block, width)
    attended = attend(ends, qkv)
    resid, layer_mlp, own_gate, own_up = close_attention(after(upstream, attended), w_out_own, layer_x, full_gain_mlp, w_gate, w_up)

    own_down = lax.all_gather(after(resid, w_down), "z", axis=0, tiled=True)
    gate, up_part, hidden, layer_upstream = open_mlp(layer_mlp, own_gate, own_up, upstream)
    part = dot_wide(hidden, own_down).astype(LOW)
    mixed_sum = lax.psum_scatter(part, PLACES, scatter_dimension=0, tiled=True)
    down_term = contract_rows(after(part, hidden), layer_upstream).astype(LOW)
    down_rows = w_down.shape[0]
    down_parts = []
    for up in range(1, 4):
        layers_pairs = [(at, (at + up) % 4) for at in range(4)]
        slab = lax.dynamic_slice_in_dim(down_term, (layer + up) % 4 * down_rows, down_rows, 0)
        down_parts.append(lax.ppermute(slab, "z", layers_pairs))
    d_gate, d_up = back_mlp(after(down_term, layer_upstream), own_down, gate, up_part)
    gate_term, up_term = contract_rows(layer_mlp, d_gate).astype(LOW), contract_rows(layer_mlp, d_up).astype(LOW)
    d_resid, gain_mlp_term, layer_d_resid, *parts = close_mlp(
        d_gate, d_up, own_gate, own_up, resid, upstream, full_gain_mlp, gate_term, up_term
    )

    def own_part(whole, near_part, cross):
        own = lax.dynamic_slice_in_dim(whole, layer * cross.shape[1], cross.shape[1], 1)
        return own.astype(jnp.float32) + near_part.astype(jnp.float32) + cross.astype(jnp.float32)

    mixed = (resid + after(layer_d_resid, mixed_sum).astype(jnp.float32)).astype(LOW)
    grad_down = lax.dynamic_slice_in_dim(down_term, layer * down_rows, down_rows, 0).astype(jnp.float32)
    grad_down = grad_down + sum(slab.astype(jnp.float32) for slab in after(layer_d_resid, down_parts))

    out_term = contract_rows(attended, layer_d_resid).astype(LOW)
    d_attended = contract_cols(layer_d_resid, w_out_own).astype(LOW)
    d_qkv, out_parts, mixed = attend_back(ends, qkv, d_attended, out_term, mixed)
    mixed = mixed.reshape(rows_here, block, width)
    grad_gate, grad_up = own_part(gate_term, *parts[1:3]), own_part(up_term, *parts[4:6])
    grad_out = jnp.sum(out_parts.astype(jnp.float32), axis=0)
    qkv_term = contract_rows(layer_normed, d_qkv).astype(LOW)
    qkv_term = qkv_term.reshape(4, layers, 2 * shard, 3 * owned).transpose(1, 0, 2, 3)
    qkv_term = qkv_term.reshape(layers, members * shard, 3 * owned)
    grad_low, gain_grads, *_, parts = close_layer(
        d_qkv, w_qkv, layer_x, d_resid, full_gain_attn, gain_mlp_term, qkv_term
    )
    grad_tokens = grad_low.astype(jnp.float32).reshape(rows_here, block, width)
    parts = parts.reshape(4, 2, shard, 3, 2, HD)
    parts = jnp.stack((parts[:, 0, :, :, 0], parts[:, 1, :, :, 0], parts[:, 1, :, :, 1], parts[:, 0, :, :, 1]), axis=1)
    grad_query, grad_key, grad_value = parts.transpose(3, 2, 0, 1, 4).astype(jnp.float32).reshape(3, shard, width)
    gain_grads = lax.dynamic_index_in_dim(jnp.sum(gain_grads, axis=1).reshape(2, 2, shard), lax.axis_index("x"), 1, False)
    return (
        mixed,
        grad_tokens,
        grad_query,
        grad_key,
        grad_value,
        grad_out,
        grad_gate,
        grad_up,
        grad_down,
        gain_grads[0],
        gain_grads[1],
    )


def body_any(
    tokens,
    lengths,
    cotangent,
    w_query,
    w_key,
    w_value,
    w_out,
    w_gate,
    w_up,
    w_down,
    gain_attn,
    gain_mlp,
):
    rows_here, block, width = tokens.shape
    count = rows_here * block
    scale = 1.0 / math.sqrt(HD)
    kv_place = lax.axis_index("kv")
    key_places = kv_place * block + jnp.arange(block, dtype=jnp.int32)
    attn_set = (
        lax.all_gather(w_query, ("row", "kv"), axis=0, tiled=True),
        lax.all_gather(w_key, ("row", "kv"), axis=0, tiled=True),
        lax.all_gather(w_value, ("row", "kv"), axis=0, tiled=True),
        lax.all_gather(w_out, ("row", "kv"), axis=0, tiled=True),
        lax.all_gather(gain_attn, ("row", "kv"), axis=0, tiled=True),
        lax.all_gather(gain_mlp, ("row", "kv"), axis=0, tiled=True),
    )
    full_query, full_key, full_value, full_out, full_gain_attn, full_gain_mlp = attn_set
    flat = tokens.reshape(count, width).astype(jnp.float32)
    normed_attn, inverse_attn = norm_forward(flat, full_gain_attn)
    normed_attn_low = normed_attn.astype(jnp.bfloat16)
    query_low = jnp.dot(normed_attn_low, full_query, preferred_element_type=jnp.float32).astype(
        jnp.bfloat16
    )
    key_low = jnp.dot(normed_attn_low, full_key, preferred_element_type=jnp.float32).astype(
        jnp.bfloat16
    )
    value_low = jnp.dot(normed_attn_low, full_value, preferred_element_type=jnp.float32).astype(
        jnp.bfloat16
    )
    key_heads = key_low.reshape(rows_here, block, H, HD)
    value_heads = value_low.reshape(rows_here, block, H, HD)
    segment, valid = segment_table(lengths)
    key_segment = lax.dynamic_slice_in_dim(segment, kv_place * block, block, 1)
    key_valid = lax.dynamic_slice_in_dim(valid, kv_place * block, block, 1)
    queries_all = lax.all_gather(
        query_low.reshape(rows_here, block, width), "kv", axis=1, tiled=True
    )
    which = 0
    query_rows = queries_all[which]
    query_segment = segment[which]
    sigmoid_part, allowed = score_block(
        query_rows,
        key_heads[which],
        query_segment,
        key_segment[which],
        key_valid[which],
        jnp.int32(0),
        key_places,
    )
    weight = (sigmoid_part * allowed).astype(jnp.bfloat16)
    summed = jnp.einsum(
        "hqk,khd->qhd", weight, value_heads[which], preferred_element_type=jnp.float32
    )
    pieces = [
        lax.psum_scatter(
            summed.reshape(lax.axis_size("kv") * block, width).astype(jnp.bfloat16),
            "kv",
            scatter_dimension=0,
            tiled=True,
        ).astype(jnp.float32)
    ]
    attended_low = jnp.stack(pieces).reshape(count, width).astype(jnp.bfloat16)
    resid = flat + jnp.dot(attended_low, full_out, preferred_element_type=jnp.float32)
    normed_mlp, inverse_mlp = norm_forward(resid, full_gain_mlp)
    normed_mlp_low = normed_mlp.astype(jnp.bfloat16)
    upstream_low = cotangent.reshape(count, width)
    upstream = upstream_low.astype(jnp.float32)
    slice_gate, slice_up, slice_down = (
        lax.all_gather(w_gate, "row", axis=1, tiled=True),
        lax.all_gather(w_up, "row", axis=1, tiled=True),
        lax.all_gather(w_down, "row", axis=0, tiled=True),
    )
    row_normed, row_upstream = (
        lax.all_gather(normed_mlp_low.reshape(rows_here, block, width), "kv", axis=1, tiled=True),
        lax.all_gather(cotangent, "kv", axis=1, tiled=True),
    )
    normed_rows = row_normed.reshape(rows_here * LEN, width)
    upstream_rows = row_upstream.reshape(rows_here * LEN, width)
    gate = jnp.dot(normed_rows, slice_gate, preferred_element_type=jnp.float32)
    up_part = jnp.dot(normed_rows, slice_up, preferred_element_type=jnp.float32)
    sigmoid_gate = jax.nn.sigmoid(gate)
    hidden_low = (gate * sigmoid_gate * up_part).astype(jnp.bfloat16)
    hidden_rows = hidden_low.reshape(rows_here, LEN, hidden_low.shape[1])
    which = 0
    hidden_part = hidden_rows[which]
    outputs = [
        lax.psum_scatter(
            jnp.dot(hidden_part, slice_down, preferred_element_type=jnp.float32).astype(
                jnp.bfloat16
            ),
            "kv",
            scatter_dimension=0,
            tiled=True,
        ).astype(jnp.float32)
    ]
    result = resid + jnp.stack(outputs).reshape(count, width)
    d_hidden = contract_cols(upstream_rows, slice_down)
    d_gate, d_up = gate_backward(d_hidden, gate, up_part, sigmoid_gate)
    partial_normed = contract_cols(d_gate, slice_gate) + contract_cols(d_up, slice_up)
    d_normed_mlp = (
        lax.psum_scatter(
            partial_normed.reshape(rows_here, LEN, width).astype(jnp.bfloat16),
            "kv",
            scatter_dimension=1,
            tiled=True,
        )
        .astype(jnp.float32)
        .reshape(count, width)
    )
    grad_gate, grad_up, grad_down = (
        lax.psum_scatter(
            contract_rows(normed_rows, d_gate).astype(jnp.bfloat16),
            "row",
            scatter_dimension=1,
            tiled=True,
        ).astype(jnp.float32),
        lax.psum_scatter(
            contract_rows(normed_rows, d_up).astype(jnp.bfloat16),
            "row",
            scatter_dimension=1,
            tiled=True,
        ).astype(jnp.float32),
        lax.psum_scatter(
            contract_rows(hidden_low, upstream_rows).astype(jnp.bfloat16),
            "row",
            scatter_dimension=0,
            tiled=True,
        ).astype(jnp.float32),
    )
    mixed = result.astype(jnp.bfloat16).reshape(rows_here, block, width)
    back_mlp, gain_mlp_term = norm_backward(resid, inverse_mlp, full_gain_mlp, d_normed_mlp)
    d_resid = upstream + back_mlp
    d_resid_low = d_resid.astype(jnp.bfloat16)
    d_attended = contract_cols(d_resid_low, full_out).astype(jnp.bfloat16)
    grads_all = lax.all_gather(
        d_attended.reshape(rows_here, block, width), "kv", axis=1, tiled=True
    )
    query_block = min(512, LEN)
    block_count = LEN // query_block
    which = 0

    def sweep(carry, index, which=which):
        key_total, value_total = carry
        start = index * query_block
        query_rows = lax.dynamic_slice_in_dim(queries_all[which], start, query_block, 0)
        grad_rows = lax.dynamic_slice_in_dim(grads_all[which], start, query_block, 0)
        query_segment = lax.dynamic_slice_in_dim(segment[which], start, query_block, 0)
        sigmoid_part, allowed = score_block(
            query_rows,
            key_heads[which],
            query_segment,
            key_segment[which],
            key_valid[which],
            start,
            key_places,
        )
        weight = (sigmoid_part * allowed).astype(jnp.bfloat16)
        grad_heads = grad_rows.reshape(query_block, H, HD)
        value_total = value_total + jnp.einsum(
            "hqk,qhd->khd", weight, grad_heads, preferred_element_type=jnp.float32
        )
        d_weight = jnp.einsum(
            "qhd,khd->hqk", grad_heads, value_heads[which], preferred_element_type=jnp.float32
        )
        d_score = (d_weight * sigmoid_part * (1.0 - sigmoid_part) * allowed).astype(jnp.bfloat16)
        query_part = (
            jnp.einsum(
                "hqk,khd->qhd", d_score, key_heads[which], preferred_element_type=jnp.float32
            )
            * scale
        )
        key_total = (
            key_total
            + jnp.einsum(
                "hqk,qhd->khd",
                d_score,
                query_rows.reshape(query_block, H, HD),
                preferred_element_type=jnp.float32,
            )
            * scale
        )
        return ((key_total, value_total), query_part.reshape(query_block, width))

    zeros = jnp.zeros((block, H, HD), jnp.float32)
    totals, query_parts = lax.scan(sweep, (zeros, zeros), jnp.arange(block_count, dtype=jnp.int32))
    query_terms = [query_parts.reshape(LEN, width)]
    key_grads = [totals[0].reshape(block, width)]
    value_grads = [totals[1].reshape(block, width)]
    query_local = lax.psum_scatter(
        jnp.stack(query_terms).astype(jnp.bfloat16), "kv", scatter_dimension=1, tiled=True
    ).astype(jnp.float32)
    d_query_low = query_local.reshape(count, width).astype(jnp.bfloat16)
    d_key_low = jnp.stack(key_grads).reshape(count, width).astype(jnp.bfloat16)
    d_value_low = jnp.stack(value_grads).reshape(count, width).astype(jnp.bfloat16)
    d_normed_attn = (
        contract_cols(d_query_low, full_query)
        + contract_cols(d_key_low, full_key)
        + contract_cols(d_value_low, full_value)
    )
    back_attn, gain_attn_term = norm_backward(flat, inverse_attn, full_gain_attn, d_normed_attn)
    grad_tokens = (d_resid + back_attn).reshape(rows_here, block, width)
    projected_low = jnp.concatenate((d_query_low, d_key_low, d_value_low), axis=1)
    grad_projections = lax.psum_scatter(
        contract_rows(normed_attn_low, projected_low),
        ("row", "kv"),
        scatter_dimension=0,
        tiled=True,
    )
    out_term = contract_rows(attended_low, d_resid_low)
    grad_out, grad_gain_attn, grad_gain_mlp = (
        lax.psum_scatter(out_term, ("row", "kv"), scatter_dimension=0, tiled=True),
        lax.psum_scatter(gain_attn_term, ("row", "kv"), scatter_dimension=0, tiled=True),
        lax.psum_scatter(gain_mlp_term, ("row", "kv"), scatter_dimension=0, tiled=True),
    )
    grad_query = grad_projections[:, :width]
    grad_key = grad_projections[:, width : 2 * width]
    grad_value = grad_projections[:, 2 * width :]
    return (
        mixed,
        grad_tokens,
        grad_query,
        grad_key,
        grad_value,
        grad_out,
        grad_gate,
        grad_up,
        grad_down,
        grad_gain_attn,
        grad_gain_mlp,
    )


def solution(mesh):
    rows, columns = mesh.shape["row"], mesh.shape["kv"]
    if rows == 4 and columns == 2 * rows:
        mesh = Mesh(mesh.devices.reshape(2, 2, rows, 2), ("y", "c", "z", "x"))
        row, kv, run = ("y", "c"), ("z", "x"), body_layers
    else:
        row, kv, run = "row", "kv", body_any
    both = ("y", "c", "z", "x") if run is body_layers else ("row", "kv")
    tall, wide, flat = P(both, None), P(None, both), P(both)
    tokens = P(row, kv, None)
    return jax.shard_map(
        run,
        mesh=mesh,
        in_specs=(tokens, P(row, None), tokens, tall, tall, tall, tall, wide, wide, tall, flat, flat),
        out_specs=(tokens, tokens, tall, tall, tall, tall, wide, wide, tall, flat, flat),
        check_vma=False,
    )
```
